32 devices in a mesh: parts: 2 (over x), cl: 8 (over z, y), grp: 2 (over core).
Axes of the slice: x: 2, y: 2, z: 4, core: 2. Of those that a mesh axis runs over, the one named last changes fastest.
Arguments:
- embeddings: bfloat16 [32768, 768], P(('parts', 'cl', 'grp')), parts along dimension 0, may hold values from -8 to 8
- labels: int32 [32768], P(('parts', 'cl', 'grp')), parts along dimension 0, may hold values from 0 to 63, as said below
- owner_map: int32 [128], P('parts'), parts along dimension 0, may hold values from 0 to 7, as said below
Outputs:
- dup_log: float32 [32768], P(('parts', 'cl', 'grp')), parts along dimension 0
The draws below stay inside these ranges and needn't reach their ends.
There are 2 independent parts, one for each index of `parts`. The reference program is written for one: setup_inputs(seed, part) draws one part's arguments, and reference() takes and returns one part's arrays. A program takes and returns all parts, laid end to end along the dimension named above; each array names one. Nothing has to cross between parts.
Inputs may be any that keep to these rules, and one draw needn't show every extreme that they name: `labels`: each aligned block of 1024 rows (the rows of one device) holds at most 256 rows of any one coarse cluster, and in every block exactly 256 rows belong to one common coarse cluster. `owner_map`: each coarse cluster holds exactly 8 fine clusters.
All inputs are finite; a program needn't handle non-finite values.
Results may differ from the reference program's by a relative error of at most 0.0003.
Values may be sent and summed in bfloat16 or wider, within the bound.
No kernel may reach another device: no remote copies, remote signals or barrier semaphores. Data moves between devices by JAX's collectives and lax.ppermute only.
A program may use at most 64 MiB of HBM per device.

```python
import math
import jax
import jax.numpy as jnp
from jax import lax

E = 768
KPO = 8
SLOTS = 2048
R_DEV = 1024
N_CL = 8
N_GRP = 2


def common_draw(key):
    perm_key, busy_key, rows_key = jax.random.split(key, 3)
    order = jax.random.permutation(perm_key, KPO * N_CL).astype(jnp.int32)
    owner_map = jnp.zeros((KPO * N_CL,), jnp.int32).at[order].set(jnp.arange(KPO * N_CL, dtype=jnp.int32) % N_CL)
    busiest = jax.random.randint(busy_key, (), 0, N_CL).astype(jnp.int32)
    capacity = SLOTS // N_CL

    def one_device(device_key):
        score_key, shuffle_key, label_key = jax.random.split(device_key, 3)
        scores = jax.random.permutation(score_key, SLOTS).astype(jnp.int32)
        slot_owner = jnp.arange(SLOTS, dtype=jnp.int32) // capacity
        scores = scores + jnp.where(slot_owner == busiest, SLOTS, 0).astype(jnp.int32)
        chosen = lax.top_k(scores, R_DEV)[1].astype(jnp.int32)
        chosen = jax.random.permutation(shuffle_key, chosen)
        row_owner = chosen // capacity
        picks = jax.random.randint(label_key, (R_DEV,), 0, KPO).astype(jnp.int32)
        return order[row_owner + N_CL * picks]
    device_keys = jax.random.split(rows_key, N_CL * N_GRP)
    labels = jax.vmap(one_device)(device_keys).reshape(-1).astype(jnp.int32)
    return (labels, owner_map)


def draw_labels(key, part):
    return common_draw(key)[0]


def draw_owner_map(key, part):
    return common_draw(key)[1]


def clipped_normal(key, shape):
    return jnp.clip(jax.random.normal(key, shape, jnp.float32), -3.5, 3.5)


def draw_embeddings(key, part):
    labels, owner_map = common_draw(key)
    key = jax.random.fold_in(key, 7)
    keys = jax.random.split(key, 9)
    groups = max(1, R_DEV * N_GRP // (KPO * 4))
    total = labels.shape[0]
    coarse = owner_map[labels].astype(jnp.int32)
    coarse_table = clipped_normal(keys[0], (N_CL, E))
    fine_table = clipped_normal(keys[1], (KPO * N_CL, E))
    copy_table = clipped_normal(keys[2], (KPO * N_CL * groups, E))
    broad_table = clipped_normal(keys[8], (N_CL * groups, E))
    copy_slot = jax.random.randint(keys[3], (total,), 0, groups).astype(jnp.int32)
    copy_kind = jax.random.randint(keys[4], (total,), 0, 5).astype(jnp.int32)
    copy_on = (copy_kind < 3).astype(jnp.float32)
    broad_on = copy_kind == 2
    strength = jnp.sqrt(jnp.exp(jax.random.uniform(keys[5], (total,), jnp.float32, math.log(4.0), math.log(40.0))))
    copy_weight = strength * copy_on
    noise = clipped_normal(keys[6], (total, E))
    shared = jnp.zeros((E,), jnp.float32)
    fine_copy = copy_table[labels * groups + copy_slot]
    broad_copy = broad_table[coarse * groups + copy_slot]
    copy_rows = jnp.where(broad_on[:, None], broad_copy, fine_copy)
    rows = math.sqrt(0.2) * coarse_table[coarse] + math.sqrt(0.2) * fine_table[labels]
    rows = rows + copy_weight[:, None] * copy_rows
    rows = rows + math.sqrt(0.6) * noise
    rows = rows / jnp.sqrt(1.0 + copy_weight * copy_weight)[:, None] + shared[None, :]
    return rows.astype(jnp.bfloat16)


def setup_inputs(seed: int = 0, part: int = 0) -> dict:
    arg_keys = jax.random.split(jax.random.key(seed), 4)
    part_splits = jax.random.split(jax.random.fold_in(arg_keys[3], part), 4)
    embeddings = draw_embeddings(jax.random.fold_in(jax.random.fold_in(arg_keys[3], part), 71), part)
    labels = draw_labels(jax.random.fold_in(jax.random.fold_in(arg_keys[3], part), 71), part)
    owner_map = draw_owner_map(jax.random.fold_in(jax.random.fold_in(arg_keys[3], part), 71), part)
    return {"embeddings": embeddings, "labels": labels, "owner_map": owner_map}


temper = 0.2
neighbour_factor = 0.5
epsilon = 1e-06

def reference(embeddings, labels, owner_map):
    values32 = embeddings.astype(jnp.float32)
    squares = lax.optimization_barrier(jnp.sum(values32 * values32, axis=1, keepdims=True))
    unit_rows = (values32 * lax.rsqrt(squares + epsilon)).astype(jnp.bfloat16)
    owners = owner_map[labels].astype(jnp.int32)
    order = jnp.argsort(owners, stable=True).astype(jnp.int32)
    counts = lax.optimization_barrier(jnp.sum((owners[:, None] == jnp.arange(N_CL, dtype=jnp.int32)[None, :]).astype(jnp.int32), axis=0))
    starts = (jnp.cumsum(counts) - counts).astype(jnp.int32)
    buffer_len = N_GRP * SLOTS
    padded = jnp.concatenate([order, jnp.zeros((buffer_len,), jnp.int32)])
    total_rows = labels.shape[0]

    def one_owner(owner_id):
        picks = lax.dynamic_slice(padded, (starts[owner_id],), (buffer_len,)).astype(jnp.int32)
        live = jnp.arange(buffer_len, dtype=jnp.int32) < counts[owner_id]
        rows_x = unit_rows[picks]
        rows_lab = jnp.where(live, labels[picks], -1)
        scores = jnp.dot(rows_x, rows_x.T, preferred_element_type=jnp.float32)
        same = rows_lab[:, None] == rows_lab[None, :]
        both_live = (rows_lab[:, None] >= 0) & (rows_lab[None, :] >= 0)
        factor = jnp.where(both_live, jnp.where(same, 1.0, neighbour_factor), 0.0).astype(jnp.float32)
        totals = lax.optimization_barrier(jnp.sum(factor * jnp.exp((scores - 1.0) / temper), axis=1))
        values = jnp.log(jnp.where(live, totals, 1.0))
        return (values, jnp.where(live, picks, total_rows).astype(jnp.int32))
    values, targets = lax.map(one_owner, jnp.arange(N_CL, dtype=jnp.int32))
    result = jnp.zeros((total_rows,), jnp.float32)
    return result.at[targets.reshape(-1)].set(values.reshape(-1), mode='drop')
```

```python
import functools
import math

import jax
import jax.numpy as jnp
from jax import lax
from jax.experimental import pallas as pl
from jax.experimental.pallas import tpu as pltpu
from jax.sharding import PartitionSpec as P

SLOTS = 2048

temper = 0.2
neighbour_factor = 0.5
epsilon = 1e-06

LANES = 128
SCALE = math.log2(math.e) / temper
NEIGHBOUR = math.log2(neighbour_factor)
DEAD = -1e30
VMEM_LIMIT = 48 * 1024 * 1024


def column_of(row):
    pieces = []
    for start in range(0, row.shape[1], LANES):
        width = min(LANES, row.shape[1] - start)
        shape = (width, width)
        diagonal = lax.broadcasted_iota(jnp.int32, shape, 0) == lax.broadcasted_iota(
            jnp.int32, shape, 1
        )
        piece = jnp.broadcast_to(row[:, start : start + width], shape)
        pieces.append(jnp.sum(jnp.where(diagonal, piece, 0.0), axis=1, keepdims=True))
    return jnp.concatenate(pieces, axis=0)


def row_of(column):
    n = column.shape[0]
    diagonal = lax.broadcasted_iota(jnp.int32, (n, n), 0) == lax.broadcasted_iota(
        jnp.int32, (n, n), 1
    )
    return jnp.sum(jnp.where(diagonal, column, 0.0), axis=0, keepdims=True)


def pack_kernel(n_owner, capacity, x_ref, lab_ref, map_ref, out_ref, pos_ref, cnt_ref, unit, pos_row):
    rows = x_ref.shape[0]
    n_fine = map_ref.shape[1]
    per_owner = n_fine // n_owner
    owner_row = map_ref[...].astype(jnp.float32)
    fine_row = lax.broadcasted_iota(jnp.int32, (1, n_fine), 1).astype(jnp.float32)
    key_row = owner_row * n_fine + fine_row
    key_col = column_of(key_row)
    sorted_col = jnp.sum(jnp.where(key_row < key_col, 1.0, 0.0), axis=1, keepdims=True)
    lab = lab_ref[...].astype(jnp.float32)
    lab_row = jnp.concatenate([lab[b : b + 1, :] for b in range(lab.shape[0])], axis=1)
    fine_col = lax.broadcasted_iota(jnp.int32, (n_fine, rows), 0).astype(jnp.float32)
    fine_id = jnp.sum(jnp.where(fine_col == lab_row, sorted_col, 0.0), axis=0, keepdims=True)
    counts_col = jnp.sum(jnp.where(fine_col == fine_id, 1.0, 0.0), axis=1, keepdims=True)
    cnt_ref[...] = row_of(counts_col).astype(jnp.int32)
    coarse = jnp.floor((fine_id + 0.5) * (1.0 / per_owner))
    before = jnp.sum(
        jnp.where(fine_col < coarse * per_owner, counts_col, 0.0), axis=0, keepdims=True
    )
    index = lax.broadcasted_iota(jnp.int32, (1, rows), 1).astype(jnp.float32)
    row_key = fine_id * rows + index
    rank = jnp.zeros((1, rows), jnp.float32)
    for start in range(0, rows, LANES):
        other = column_of(row_key[:, start : start + LANES])
        rank = rank + jnp.sum(jnp.where(other < row_key, 1.0, 0.0), axis=0, keepdims=True)
    pos = (coarse * capacity + rank - before).astype(jnp.int32)
    pos_row[...] = pos
    pos_ref[...] = jnp.concatenate(
        [pos[:, start : start + LANES] for start in range(0, rows, LANES)], axis=0
    )
    x = x_ref[...].astype(jnp.float32)
    squares = jnp.sum(x * x, axis=1, keepdims=True)
    unit[...] = (x * lax.rsqrt(squares + epsilon)).astype(jnp.bfloat16)

    step = 256

    @pl.loop(0, out_ref.shape[0] // step)
    def _(block):
        slot = lax.broadcasted_iota(jnp.int32, (step, rows), 0) + block * step
        chosen = jnp.where(slot == pos_row[...], 1.0, 0.0).astype(jnp.bfloat16)
        packed = jnp.dot(chosen, unit[...], preferred_element_type=jnp.float32)
        out_ref[pl.ds(pl.multiple_of(block * step, step), step), :] = packed.astype(jnp.bfloat16)


def pack(embeddings, labels, owner_map, n_owner, capacity):
    rows, width = embeddings.shape
    n_fine = owner_map.shape[0]
    total = n_owner * capacity
    vmem = pl.BlockSpec(memory_space=pltpu.VMEM)
    return pl.pallas_call(
        functools.partial(pack_kernel, n_owner, capacity),
        out_shape=(
            jax.ShapeDtypeStruct((total, width), jnp.bfloat16),
            jax.ShapeDtypeStruct((rows // LANES, LANES), jnp.int32),
            jax.ShapeDtypeStruct((1, n_fine), jnp.int32),
        ),
        in_specs=[vmem] * 3,
        out_specs=(vmem, vmem, vmem),
        scratch_shapes=[pltpu.VMEM((rows, width), jnp.bfloat16), pltpu.VMEM((1, rows), jnp.int32)],
        compiler_params=pltpu.CompilerParams(vmem_limit_bytes=VMEM_LIMIT),
    )(embeddings, labels.reshape(rows // LANES, LANES), owner_map.reshape(1, n_fine))


def counts_kernel(n_owner, capacity, cnt_ref, mine_ref, other_ref, out_ref, lab_lane, lab_sub, bias):
    total = mine_ref.shape[0]
    per_owner = cnt_ref.shape[1] // n_owner
    me = lax.axis_index("cl")
    grp = lax.axis_index("grp")
    n_grp = lax.axis_size("grp")
    for member in range(2):
        for source in range(n_owner):
            line = source * n_grp + lax.rem(grp + member, n_grp)
            edges = []
            edge = jnp.int32(0)
            for f in range(per_owner):
                edge = edge + cnt_ref[line, me * per_owner + f]
                edges.append(edge)
            down = lax.broadcasted_iota(jnp.int32, (capacity, LANES), 0)
            label = jnp.zeros((capacity, LANES), jnp.int32)
            for edge in edges:
                label = label + jnp.where(down >= edge, 1, 0)
            start = (member * n_owner + source) * capacity
            lab_sub[start : start + capacity, :] = label
            bias[start : start + capacity, :] = jnp.where(
                label < per_owner, NEIGHBOUR - SCALE, DEAD
            )
            if member == 0:
                across = lax.broadcasted_iota(jnp.int32, (1, capacity), 1)
                label = jnp.zeros((1, capacity), jnp.int32)
                for edge in edges:
                    label = label + jnp.where(across >= edge, 1, 0)
                lab_lane[:, source * capacity : (source + 1) * capacity] = jnp.where(
                    label < per_owner, label, -1
                )
    wide, deep = min(512, total), min(256, total)

    @pl.loop(0, total // wide)
    def _(block):
        columns = pl.ds(pl.multiple_of(block * wide, wide), wide)
        rows_i = mine_ref[columns, :]
        label_i = lab_lane[:, columns]

        def add(ref, offset):
            def step(j, acc):
                start = pl.multiple_of(j * deep, deep)
                scores = lax.dot_general(
                    ref[pl.ds(start, deep), :],
                    rows_i,
                    (((1,), (1,)), ((), ())),
                    preferred_element_type=jnp.float32,
                )
                place = pl.ds(pl.multiple_of(start + offset, deep), deep)
                label_j = lab_sub[place, :]
                bias_j = bias[place, :]
                repeat = wide // LANES
                label_j = jnp.concatenate([label_j] * repeat, axis=1)
                bias_j = jnp.concatenate([bias_j] * repeat, axis=1)
                shift = jnp.where(label_j == label_i, -SCALE, bias_j)
                terms = jnp.exp2(scores * SCALE + shift)
                return acc + jnp.sum(terms.reshape(deep // 8, 8, wide), axis=0)

            return step

        acc = jnp.zeros((8, wide), jnp.float32)
        acc = lax.fori_loop(0, total // deep, add(mine_ref, 0), acc, unroll=2)
        acc = lax.fori_loop(0, total // deep, add(other_ref, total), acc, unroll=2)
        totals = jnp.sum(acc, axis=0, keepdims=True)
        out_ref[:, columns] = jnp.log(jnp.where(label_i >= 0, totals, 1.0))


def log_counts(counts, mine, other, n_owner, capacity):
    total = mine.shape[0]
    vmem = pl.BlockSpec(memory_space=pltpu.VMEM)
    return pl.pallas_call(
        functools.partial(counts_kernel, n_owner, capacity),
        out_shape=jax.ShapeDtypeStruct((1, total), jnp.float32),
        in_specs=[pl.BlockSpec(memory_space=pltpu.SMEM), vmem, vmem],
        out_specs=vmem,
        scratch_shapes=[
            pltpu.VMEM((1, total), jnp.int32),
            pltpu.VMEM((2 * total, LANES), jnp.int32),
            pltpu.VMEM((2 * total, LANES), jnp.float32),
        ],
        compiler_params=pltpu.CompilerParams(vmem_limit_bytes=VMEM_LIMIT),
    )(counts, mine, other)


def unpack_kernel(values_ref, pos_ref, out_ref):
    pos = pos_ref[...]
    lane = lax.rem(pos, LANES)
    line = lax.div(pos, LANES)
    out = jnp.zeros(pos.shape, jnp.float32)
    for r in range(values_ref.shape[0]):
        table = jnp.broadcast_to(values_ref[r : r + 1, :], pos.shape)
        found = jnp.take_along_axis(table, lane, axis=1)
        out = jnp.where(line == r, found, out)
    out_ref[...] = out


def unpack(values, pos):
    vmem = pl.BlockSpec(memory_space=pltpu.VMEM)
    return pl.pallas_call(
        unpack_kernel,
        out_shape=jax.ShapeDtypeStruct(pos.shape, jnp.float32),
        in_specs=[vmem, vmem],
        out_specs=vmem,
    )(values.reshape(-1, LANES), pos)


def body(embeddings, labels, owner_map):
    n_owner = lax.axis_size("cl")
    capacity = SLOTS // n_owner
    rows, width = embeddings.shape
    packed, pos, counts = pack(embeddings, labels, owner_map, n_owner, capacity)
    counts = lax.all_gather(counts, ("cl", "grp"), tiled=True)
    mine = lax.all_to_all(
        packed.reshape(n_owner, capacity, width), "cl", split_axis=0, concat_axis=0, tiled=True
    ).reshape(SLOTS, width)
    other = lax.ppermute(mine, "grp", [(0, 1), (1, 0)])
    results = log_counts(counts, mine, other, n_owner, capacity)
    returned = lax.all_to_all(
        results.reshape(n_owner, capacity), "cl", split_axis=0, concat_axis=0, tiled=True
    )
    return unpack(returned.reshape(SLOTS), pos).reshape(rows)


def solution(mesh):
    return jax.shard_map(
        body,
        mesh=mesh,
        in_specs=(P(("parts", "cl", "grp"), None), P(("parts", "cl", "grp")), P("parts")),
        out_specs=P(("parts", "cl", "grp")),
        check_vma=False,
    )
```

```python
import functools
import math

import jax
import jax.numpy as jnp
from jax import lax
from jax.experimental import pallas as pl
from jax.experimental.pallas import tpu as pltpu
from jax.sharding import PartitionSpec as P

SLOTS = 2048

temper = 0.2
neighbour_factor = 0.5
epsilon = 1e-06

LANES = 128
SCALE = math.log2(math.e) / temper
NEIGHBOUR = math.log2(neighbour_factor)
DEAD = -1e30
VMEM_LIMIT = 48 * 1024 * 1024
FAST_LIMIT = 32 * 1024 * 1024


def column_of(row):
    pieces = []
    for start in range(0, row.shape[1], LANES):
        width = min(LANES, row.shape[1] - start)
        shape = (width, width)
        diagonal = lax.broadcasted_iota(jnp.int32, shape, 0) == lax.broadcasted_iota(
            jnp.int32, shape, 1
        )
        piece = jnp.broadcast_to(row[:, start : start + width], shape)
        pieces.append(jnp.sum(jnp.where(diagonal, piece, 0.0), axis=1, keepdims=True))
    return jnp.concatenate(pieces, axis=0)


def row_of(column):
    n = column.shape[0]
    diagonal = lax.broadcasted_iota(jnp.int32, (n, n), 0) == lax.broadcasted_iota(
        jnp.int32, (n, n), 1
    )
    return jnp.sum(jnp.where(diagonal, column, 0.0), axis=0, keepdims=True)


def pack_kernel(n_owner, capacity, x_ref, lab_ref, map_ref, out_ref, pos_ref, cnt_ref, unit, pos_row):
    rows = x_ref.shape[0]
    n_fine = map_ref.shape[1]
    per_owner = n_fine // n_owner
    owner_row = map_ref[...].astype(jnp.float32)
    fine_row = lax.broadcasted_iota(jnp.int32, (1, n_fine), 1).astype(jnp.float32)
    key_row = owner_row * n_fine + fine_row
    key_col = column_of(key_row)
    sorted_col = jnp.sum(jnp.where(key_row < key_col, 1.0, 0.0), axis=1, keepdims=True)
    lab = lab_ref[...].astype(jnp.float32)
    lab_row = jnp.concatenate([lab[b : b + 1, :] for b in range(lab.shape[0])], axis=1)
    fine_col = lax.broadcasted_iota(jnp.int32, (n_fine, rows), 0).astype(jnp.float32)
    fine_id = jnp.sum(jnp.where(fine_col == lab_row, sorted_col, 0.0), axis=0, keepdims=True)
    counts_col = jnp.sum(jnp.where(fine_col == fine_id, 1.0, 0.0), axis=1, keepdims=True)
    cnt_ref[...] = row_of(counts_col).astype(jnp.int32)
    coarse = jnp.floor((fine_id + 0.5) * (1.0 / per_owner))
    before = jnp.sum(
        jnp.where(fine_col < coarse * per_owner, counts_col, 0.0), axis=0, keepdims=True
    )
    index = lax.broadcasted_iota(jnp.int32, (1, rows), 1).astype(jnp.float32)
    row_key = fine_id * rows + index
    rank = jnp.zeros((1, rows), jnp.float32)
    for start in range(0, rows, LANES):
        other = column_of(row_key[:, start : start + LANES])
        rank = rank + jnp.sum(jnp.where(other < row_key, 1.0, 0.0), axis=0, keepdims=True)
    pos = (coarse * capacity + rank - before).astype(jnp.int32)
    pos_row[...] = pos
    pos_ref[...] = jnp.concatenate(
        [pos[:, start : start + LANES] for start in range(0, rows, LANES)], axis=0
    )
    x = x_ref[...].astype(jnp.float32)
    squares = jnp.sum(x * x, axis=1, keepdims=True)
    unit[...] = (x * lax.rsqrt(squares + epsilon)).astype(jnp.bfloat16)

    step = 256

    @pl.loop(0, out_ref.shape[0] // step)
    def _(block):
        slot = lax.broadcasted_iota(jnp.int32, (step, rows), 0) + block * step
        chosen = jnp.where(slot == pos_row[...], 1.0, 0.0).astype(jnp.bfloat16)
        packed = jnp.dot(chosen, unit[...], preferred_element_type=jnp.float32)
        out_ref[pl.ds(pl.multiple_of(block * step, step), step), :] = packed.astype(jnp.bfloat16)


def pack(embeddings, labels, owner_map, n_owner, capacity):
    rows, width = embeddings.shape
    n_fine = owner_map.shape[0]
    total = n_owner * capacity
    vmem = pl.BlockSpec(memory_space=pltpu.VMEM)
    return pl.pallas_call(
        functools.partial(pack_kernel, n_owner, capacity),
        out_shape=(
            jax.ShapeDtypeStruct((total, width), jnp.bfloat16),
            jax.ShapeDtypeStruct((rows // LANES, LANES), jnp.int32),
            jax.ShapeDtypeStruct((1, n_fine), jnp.int32),
        ),
        in_specs=[vmem] * 3,
        out_specs=(vmem, vmem, vmem),
        scratch_shapes=[pltpu.VMEM((rows, width), jnp.bfloat16), pltpu.VMEM((1, rows), jnp.int32)],
        compiler_params=pltpu.CompilerParams(vmem_limit_bytes=VMEM_LIMIT),
    )(embeddings, labels.reshape(rows // LANES, LANES), owner_map.reshape(1, n_fine))


def counts_kernel(n_owner, capacity, cnt_ref, mine_ref, other_ref, out_ref, lab_lane, lab_sub, bias):
    total = mine_ref.shape[0]
    per_owner = cnt_ref.shape[1] // n_owner
    me = lax.axis_index("cl")
    grp = lax.axis_index("grp")
    n_grp = lax.axis_size("grp")
    for member in range(2):
        for source in range(n_owner):
            line = source * n_grp + lax.rem(grp + member, n_grp)
            edges = []
            edge = jnp.int32(0)
            for f in range(per_owner):
                edge = edge + cnt_ref[line, me * per_owner + f]
                edges.append(edge)
            down = lax.broadcasted_iota(jnp.int32, (capacity, LANES), 0)
            label = jnp.zeros((capacity, LANES), jnp.int32)
            for edge in edges:
                label = label + jnp.where(down >= edge, 1, 0)
            start = (member * n_owner + source) * capacity
            lab_sub[start : start + capacity, :] = label
            bias[start : start + capacity, :] = jnp.where(
                label < per_owner, NEIGHBOUR - SCALE, DEAD
            )
            if member == 0:
                across = lax.broadcasted_iota(jnp.int32, (1, capacity), 1)
                label = jnp.zeros((1, capacity), jnp.int32)
                for edge in edges:
                    label = label + jnp.where(across >= edge, 1, 0)
                lab_lane[:, source * capacity : (source + 1) * capacity] = jnp.where(
                    label < per_owner, label, -1
                )
    wide, deep = min(512, total), min(256, total)

    @pl.loop(0, total // wide)
    def _(block):
        columns = pl.ds(pl.multiple_of(block * wide, wide), wide)
        rows_i = mine_ref[columns, :]
        label_i = lab_lane[:, columns]

        def add(ref, offset):
            def step(j, acc):
                start = pl.multiple_of(j * deep, deep)
                scores = lax.dot_general(
                    ref[pl.ds(start, deep), :],
                    rows_i,
                    (((1,), (1,)), ((), ())),
                    preferred_element_type=jnp.float32,
                )
                place = pl.ds(pl.multiple_of(start + offset, deep), deep)
                label_j = lab_sub[place, :]
                bias_j = bias[place, :]
                repeat = wide // LANES
                label_j = jnp.concatenate([label_j] * repeat, axis=1)
                bias_j = jnp.concatenate([bias_j] * repeat, axis=1)
                shift = jnp.where(label_j == label_i, -SCALE, bias_j)
                terms = jnp.exp2(scores * SCALE + shift)
                return acc + jnp.sum(terms.reshape(deep // 8, 8, wide), axis=0)

            return step

        acc = jnp.zeros((8, wide), jnp.float32)
        acc = lax.fori_loop(0, total // deep, add(mine_ref, 0), acc, unroll=2)
        acc = lax.fori_loop(0, total // deep, add(other_ref, total), acc, unroll=2)
        totals = jnp.sum(acc, axis=0, keepdims=True)
        out_ref[:, columns] = jnp.log(jnp.where(label_i >= 0, totals, 1.0))


def log_counts(counts, mine, other, n_owner, capacity):
    total = mine.shape[0]
    vmem = pl.BlockSpec(memory_space=pltpu.VMEM)
    return pl.pallas_call(
        functools.partial(counts_kernel, n_owner, capacity),
        out_shape=jax.ShapeDtypeStruct((1, total), jnp.float32),
        in_specs=[pl.BlockSpec(memory_space=pltpu.SMEM), vmem, vmem],
        out_specs=vmem,
        scratch_shapes=[
            pltpu.VMEM((1, total), jnp.int32),
            pltpu.VMEM((2 * total, LANES), jnp.int32),
            pltpu.VMEM((2 * total, LANES), jnp.float32),
        ],
        compiler_params=pltpu.CompilerParams(vmem_limit_bytes=VMEM_LIMIT),
    )(counts, mine, other)


def unpack_kernel(values_ref, pos_ref, out_ref):
    pos = pos_ref[...]
    lane = lax.rem(pos, LANES)
    line = lax.div(pos, LANES)
    out = jnp.zeros(pos.shape, jnp.float32)
    for r in range(values_ref.shape[0]):
        table = jnp.broadcast_to(values_ref[r : r + 1, :], pos.shape)
        found = jnp.take_along_axis(table, lane, axis=1)
        out = jnp.where(line == r, found, out)
    out_ref[...] = out


def unpack(values, pos):
    vmem = pl.BlockSpec(memory_space=pltpu.VMEM)
    return pl.pallas_call(
        unpack_kernel,
        out_shape=jax.ShapeDtypeStruct(pos.shape, jnp.float32),
        in_specs=[vmem, vmem],
        out_specs=vmem,
    )(values.reshape(-1, LANES), pos)


def swapped(x, first, second):
    return jnp.where(x == first, second, jnp.where(x == second, first, x))


def fast_pack_kernel(
    n_owner, capacity, main, home, x_hbm, lab_hbm, map_hbm, *refs
):
    outs, extra_ref, pos_ref, info_ref = refs[:n_owner], *refs[n_owner : n_owner + 3]
    x_ref, lab_ref, map_ref, unit, pos_row, sems = refs[n_owner + 3 :]
    copies = [
        pltpu.make_async_copy(src, dst, sems.at[i])
        for i, (src, dst) in enumerate(((x_hbm, x_ref), (lab_hbm, lab_ref), (map_hbm, map_ref)))
    ]
    for copy in copies:
        copy.start()
    rows = x_ref.shape[0]
    n_fine = map_ref.shape[1]
    per_owner = n_fine // n_owner
    me = lax.axis_index("cl")
    copies[1].wait()
    copies[2].wait()
    owner_row = map_ref[...].astype(jnp.float32)
    fine_row = lax.broadcasted_iota(jnp.int32, (1, n_fine), 1).astype(jnp.float32)
    key_row = owner_row * n_fine + fine_row
    key_col = column_of(key_row)
    sorted_col = jnp.sum(jnp.where(key_row < key_col, 1.0, 0.0), axis=1, keepdims=True)
    lab = lab_ref[...].astype(jnp.float32)
    lab_row = jnp.concatenate([lab[b : b + 1, :] for b in range(lab.shape[0])], axis=1)
    fine_col = lax.broadcasted_iota(jnp.int32, (n_fine, rows), 0).astype(jnp.float32)
    fine_id = jnp.sum(jnp.where(fine_col == lab_row, sorted_col, 0.0), axis=0, keepdims=True)
    counts_col = jnp.sum(jnp.where(fine_col == fine_id, 1.0, 0.0), axis=1, keepdims=True)
    coarse = jnp.floor((fine_id + 0.5) * (1.0 / per_owner))
    first = coarse * per_owner
    before = jnp.sum(jnp.where(fine_col < first, counts_col, 0.0), axis=0, keepdims=True)
    upto = jnp.sum(jnp.where(fine_col < first + per_owner, counts_col, 0.0), axis=0, keepdims=True)
    full = jnp.min(
        jnp.where(upto - before == capacity, coarse, float(n_owner)), axis=1, keepdims=True
    )
    info = jnp.concatenate(
        [row_of(counts_col), jnp.broadcast_to(full, (1, info_ref.shape[1] - n_fine))], axis=1
    )
    info_ref[...] = info.astype(jnp.int32)
    index = lax.broadcasted_iota(jnp.int32, (1, rows), 1).astype(jnp.float32)
    row_key = fine_id * rows + index
    rank = jnp.zeros((1, rows), jnp.float32)
    for start in range(0, rows, LANES):
        other = column_of(row_key[:, start : start + LANES])
        rank = rank + jnp.sum(jnp.where(other < row_key, 1.0, 0.0), axis=0, keepdims=True)
    rank = (rank - before).astype(jnp.int32)
    place = swapped(coarse.astype(jnp.int32), full.astype(jnp.int32), home)
    step = place ^ me
    table = step * capacity + rank
    pos_ref[...] = jnp.concatenate(
        [table[:, start : start + LANES] for start in range(0, rows, LANES)], axis=0
    )
    rest = jnp.where(place == home, n_owner * main + rank - main, -1)
    pos_row[...] = jnp.where(rank < main, step * main + rank, rest)
    copies[0].wait()
    x = x_ref[...].astype(jnp.float32)
    squares = jnp.sum(x * x, axis=1, keepdims=True)
    unit[...] = (x * lax.rsqrt(squares + epsilon)).astype(jnp.bfloat16)

    def chosen_rows(start, count):
        slot = lax.broadcasted_iota(jnp.int32, (count, rows), 0) + start
        chosen = jnp.where(slot == pos_row[...], 1.0, 0.0).astype(jnp.bfloat16)
        return jnp.dot(chosen, unit[...], preferred_element_type=jnp.float32).astype(jnp.bfloat16)

    together = 4
    for group in range(0, n_owner, together):
        packed = chosen_rows(group * main, together * main)
        for i in range(together):
            outs[group + i][...] = packed[i * main : (i + 1) * main]
    extra_ref[...] = chosen_rows(n_owner * main, capacity - main)


def fast_pack(embeddings, labels, owner_map, n_owner, capacity, main, home):
    rows, width = embeddings.shape
    n_fine = owner_map.shape[0]
    info = -(-(n_fine + 1) // LANES) * LANES
    vmem = pl.BlockSpec(memory_space=pltpu.VMEM)
    anywhere = pl.BlockSpec(memory_space=pl.ANY)
    lab_shape = (rows // LANES, LANES)
    out = pl.pallas_call(
        functools.partial(fast_pack_kernel, n_owner, capacity, main, home),
        out_shape=(
            *[jax.ShapeDtypeStruct((main, width), jnp.bfloat16)] * n_owner,
            jax.ShapeDtypeStruct((capacity - main, width), jnp.bfloat16),
            jax.ShapeDtypeStruct(lab_shape, jnp.int32),
            jax.ShapeDtypeStruct((1, info), jnp.int32),
        ),
        in_specs=[anywhere] * 3,
        out_specs=(vmem,) * (n_owner + 3),
        scratch_shapes=[
            pltpu.VMEM((rows, width), jnp.bfloat16),
            pltpu.VMEM(lab_shape, jnp.int32),
            pltpu.VMEM((1, n_fine), jnp.int32),
            pltpu.VMEM((rows, width), jnp.bfloat16),
            pltpu.VMEM((1, rows), jnp.int32),
            pltpu.SemaphoreType.DMA((3,)),
        ],
        compiler_params=pltpu.CompilerParams(vmem_limit_bytes=FAST_LIMIT),
    )(embeddings, labels.reshape(lab_shape), owner_map.reshape(1, n_fine))
    return out[:n_owner], out[n_owner], out[n_owner + 1], out[n_owner + 2]


def fast_counts_kernel(n_owner, n_fine, capacity, main, home, info_ref, *refs):
    n_in = 4 * n_owner
    sources, outs = refs[:n_in], refs[n_in : n_in + n_owner]
    rows_ref, lab_lane, lab_sub, bias, result, sems = refs[n_in + n_owner :]
    per_owner = n_fine // n_owner
    rest = capacity - main
    n_main, n_rest = n_owner * main, n_owner * rest
    total = n_main + n_rest
    me = lax.axis_index("cl")
    hot = info_ref[0, n_fine]
    is_home = me == home
    cluster = swapped(me, hot, home)
    copies = []
    for part, (offset, size) in enumerate(
        ((0, main), (total, main), (n_main, rest), (total + n_main, rest))
    ):
        copies.append(
            [
                pltpu.make_async_copy(
                    sources[part * n_owner + k],
                    rows_ref.at[pl.ds(offset + k * size, size)],
                    sems.at[part * n_owner + k],
                )
                for k in range(n_owner)
            ]
        )
    for copy in copies[0] + copies[1]:
        copy.start()

    @pl.when(is_home)
    def _():
        for copy in copies[2] + copies[3]:
            copy.start()

    for member in range(2):
        for k in range(n_owner):
            line = 2 * k + member
            edges = []
            edge = jnp.int32(0)
            for f in range(per_owner):
                edge = edge + info_ref[line, cluster * per_owner + f]
                edges.append(edge)
            down = lax.broadcasted_iota(jnp.int32, (capacity, LANES), 0)
            label = jnp.zeros((capacity, LANES), jnp.int32)
            for edge in edges:
                label = label + jnp.where(down >= edge, 1, 0)
            shift = jnp.where(label < per_owner, NEIGHBOUR - SCALE, DEAD)
            start = member * total + k * main
            lab_sub[start : start + main, :] = label[:main]
            bias[start : start + main, :] = shift[:main]
            start = member * total + n_main + k * rest
            lab_sub[start : start + rest, :] = label[main:]
            bias[start : start + rest, :] = shift[main:]
            if member == 0:
                across = lax.broadcasted_iota(jnp.int32, (1, capacity), 1)
                label = jnp.zeros((1, capacity), jnp.int32)
                for edge in edges:
                    label = label + jnp.where(across >= edge, 1, 0)
                label = jnp.where(label < per_owner, label, -1)
                lab_lane[:, k * main : (k + 1) * main] = label[:, :main]
                lab_lane[:, n_main + k * rest : n_main + (k + 1) * rest] = label[:, main:]

    for copy in copies[0] + copies[1]:
        copy.wait()

    @pl.when(is_home)
    def _():
        for copy in copies[2] + copies[3]:
            copy.wait()

    wide = 256
    tiles_main = [(s + i * (n_main // 2), n_main // 2) for s in (0, total) for i in range(2)]
    tiles_rest = [
        (s + i * (n_rest // 2), n_rest // 2) for s in (n_main, total + n_main) for i in range(2)
    ]

    def sums(rows_i, label_i, tiles):
        acc = jnp.zeros((8, wide), jnp.float32)
        for start, deep in tiles:
            scores = lax.dot_general(
                rows_ref[start : start + deep, :],
                rows_i,
                (((1,), (1,)), ((), ())),
                preferred_element_type=jnp.float32,
            )
            repeat = wide // LANES
            label_j = jnp.concatenate([lab_sub[start : start + deep, :]] * repeat, axis=1)
            bias_j = jnp.concatenate([bias[start : start + deep, :]] * repeat, axis=1)
            shift = jnp.where(label_j == label_i, -SCALE, bias_j)
            terms = jnp.exp2(scores * SCALE + shift)
            acc = acc + jnp.sum(terms.reshape(deep // 8, 8, wide), axis=0)
        return acc

    blocks = jnp.where(is_home, total // wide, -(-n_main // wide))

    @pl.loop(0, blocks)
    def _(block):
        columns = pl.ds(pl.multiple_of(block * wide, wide), wide)
        rows_i = rows_ref[columns, :]
        label_i = lab_lane[:, columns]
        result[:, columns] = jnp.sum(sums(rows_i, label_i, tiles_main), axis=0, keepdims=True)

        @pl.when(is_home)
        def _():
            more = sums(rows_i, label_i, tiles_rest)
            result[:, columns] += jnp.sum(more, axis=0, keepdims=True)

    values = jnp.log(jnp.where(lab_lane[...] >= 0, result[...], 1.0))
    for k in range(n_owner):
        outs[k][:, :main] = values[:, k * main : (k + 1) * main]
        outs[k][:, main:] = values[:, n_main + k * rest : n_main + (k + 1) * rest]


def fast_counts(info, chunks, n_owner, n_fine, capacity, main, home):
    width = chunks[0].shape[1]
    total = n_owner * capacity
    vmem = pl.BlockSpec(memory_space=pltpu.VMEM)
    anywhere = pl.BlockSpec(memory_space=pl.ANY)
    return pl.pallas_call(
        functools.partial(fast_counts_kernel, n_owner, n_fine, capacity, main, home),
        out_shape=(jax.ShapeDtypeStruct((1, capacity), jnp.float32),) * n_owner,
        in_specs=[pl.BlockSpec(memory_space=pltpu.SMEM)] + [anywhere] * len(chunks),
        out_specs=(vmem,) * n_owner,
        scratch_shapes=[
            pltpu.VMEM((2 * total, width), jnp.bfloat16),
            pltpu.VMEM((1, total), jnp.int32),
            pltpu.VMEM((2 * total, LANES), jnp.int32),
            pltpu.VMEM((2 * total, LANES), jnp.float32),
            pltpu.VMEM((1, total), jnp.float32),
            pltpu.SemaphoreType.DMA((4 * n_owner,)),
        ],
        compiler_params=pltpu.CompilerParams(vmem_limit_bytes=FAST_LIMIT),
    )(info, *chunks)


def everywhere(info, n_owner):
    info = jnp.concatenate([info, lax.ppermute(info, "grp", [(0, 1), (1, 0)])], axis=0)
    bit = 1
    while bit < n_owner:
        moved = lax.ppermute(info, "cl", [(i, i ^ bit) for i in range(n_owner)])
        info = jnp.concatenate([info, moved], axis=0)
        bit *= 2
    return info


def all_fit(info, n_owner, n_fine, capacity, main):
    lines = info.shape[0]
    hot = info[:, n_fine]
    sums = jnp.sum(info[:, :n_fine].reshape(lines, n_owner, n_fine // n_owner), axis=2)
    is_hot = jnp.arange(n_owner)[None, :] == hot[0]
    fits = jnp.all((sums <= main) | is_hot) & jnp.all(hot == hot[0])
    unfit = jnp.where(fits, 0, 1).astype(jnp.int32).reshape(1, 1)
    unfit = unfit + lax.ppermute(unfit, "parts", [(0, 1), (1, 0)])
    return unfit[0, 0] == 0


def general(embeddings, labels, owner_map):
    n_owner = lax.axis_size("cl")
    capacity = SLOTS // n_owner
    rows, width = embeddings.shape
    packed, pos, counts = pack(embeddings, labels, owner_map, n_owner, capacity)
    counts = lax.all_gather(counts, ("cl", "grp"), tiled=True)
    mine = lax.all_to_all(
        packed.reshape(n_owner, capacity, width), "cl", split_axis=0, concat_axis=0, tiled=True
    ).reshape(SLOTS, width)
    other = lax.ppermute(mine, "grp", [(0, 1), (1, 0)])
    results = log_counts(counts, mine, other, n_owner, capacity)
    returned = lax.all_to_all(
        results.reshape(n_owner, capacity), "cl", split_axis=0, concat_axis=0, tiled=True
    )
    return unpack(returned.reshape(SLOTS), pos).reshape(rows)


def body(embeddings, labels, owner_map):
    n_owner = lax.axis_size("cl")
    capacity = SLOTS // n_owner
    rows = embeddings.shape[0]
    n_fine = owner_map.shape[0]
    main = -(-(rows // n_owner * 9 // 8) // 16) * 16
    if main >= capacity:
        return general(embeddings, labels, owner_map)
    home = n_owner // 4
    sends, extra, pos, info = fast_pack(
        embeddings, labels, owner_map, n_owner, capacity, main, home
    )
    info = everywhere(info, n_owner)
    fits = all_fit(info, n_owner, n_fine, capacity, main)

    def to_step(x, k):
        return x if k == 0 else lax.ppermute(x, "cl", [(i, i ^ k) for i in range(n_owner)])

    def to_home(x, k):
        return x if k == 0 else lax.ppermute(x, "cl", [(home ^ k, home)])

    mine = [to_step(sends[k], k) for k in range(n_owner)]
    mine_rest = [to_home(extra, k) for k in range(n_owner)]
    other = [lax.ppermute(x, "grp", [(0, 1), (1, 0)]) for x in mine]
    home_pairs = [(2 * home, 2 * home + 1), (2 * home + 1, 2 * home)]
    other_rest = [lax.ppermute(x, ("cl", "grp"), home_pairs) for x in mine_rest]
    results = fast_counts(
        info, mine + other + mine_rest + other_rest, n_owner, n_fine, capacity, main, home
    )
    returned = jnp.concatenate([to_step(results[k], k) for k in range(n_owner)], axis=0)
    return lax.cond(
        fits,
        lambda: unpack(returned, pos).reshape(rows),
        lambda: general(embeddings, labels, owner_map),
    )


def solution(mesh):
    return jax.shard_map(
        body,
        mesh=mesh,
        in_specs=(P(("parts", "cl", "grp"), None), P(("parts", "cl", "grp")), P("parts")),
        out_specs=P(("parts", "cl", "grp")),
        check_vma=False,
    )
```

```python
import functools
import math

import jax
import jax.numpy as jnp
from jax import lax
from jax.experimental import pallas as pl
from jax.experimental.pallas import tpu as pltpu
from jax.sharding import PartitionSpec as P

SLOTS = 2048

temper = 0.2
neighbour_factor = 0.5
epsilon = 1e-06

LANES = 128
SCALE = math.log2(math.e) / temper
NEIGHBOUR = math.log2(neighbour_factor)
DEAD = -1e30
VMEM_LIMIT = 48 * 1024 * 1024
FAST_LIMIT = 40 * 1024 * 1024
INFO = 16


def column_of(row):
    pieces = []
    for start in range(0, row.shape[1], LANES):
        width = min(LANES, row.shape[1] - start)
        shape = (width, width)
        diagonal = lax.broadcasted_iota(jnp.int32, shape, 0) == lax.broadcasted_iota(
            jnp.int32, shape, 1
        )
        piece = jnp.broadcast_to(row[:, start : start + width], shape)
        pieces.append(jnp.sum(jnp.where(diagonal, piece, 0.0), axis=1, keepdims=True))
    return jnp.concatenate(pieces, axis=0)


def row_of(column):
    n = column.shape[0]
    diagonal = lax.broadcasted_iota(jnp.int32, (n, n), 0) == lax.broadcasted_iota(
        jnp.int32, (n, n), 1
    )
    return jnp.sum(jnp.where(diagonal, column, 0.0), axis=0, keepdims=True)


def pack_kernel(n_owner, capacity, x_ref, lab_ref, map_ref, out_ref, pos_ref, cnt_ref, unit, pos_row):
    rows = x_ref.shape[0]
    n_fine = map_ref.shape[1]
    per_owner = n_fine // n_owner
    owner_row = map_ref[...].astype(jnp.float32)
    fine_row = lax.broadcasted_iota(jnp.int32, (1, n_fine), 1).astype(jnp.float32)
    key_row = owner_row * n_fine + fine_row
    key_col = column_of(key_row)
    sorted_col = jnp.sum(jnp.where(key_row < key_col, 1.0, 0.0), axis=1, keepdims=True)
    lab = lab_ref[...].astype(jnp.float32)
    lab_row = jnp.concatenate([lab[b : b + 1, :] for b in range(lab.shape[0])], axis=1)
    fine_col = lax.broadcasted_iota(jnp.int32, (n_fine, rows), 0).astype(jnp.float32)
    fine_id = jnp.sum(jnp.where(fine_col == lab_row, sorted_col, 0.0), axis=0, keepdims=True)
    counts_col = jnp.sum(jnp.where(fine_col == fine_id, 1.0, 0.0), axis=1, keepdims=True)
    cnt_ref[...] = row_of(counts_col).astype(jnp.int32)
    coarse = jnp.floor((fine_id + 0.5) * (1.0 / per_owner))
    before = jnp.sum(
        jnp.where(fine_col < coarse * per_owner, counts_col, 0.0), axis=0, keepdims=True
    )
    index = lax.broadcasted_iota(jnp.int32, (1, rows), 1).astype(jnp.float32)
    row_key = fine_id * rows + index
    rank = jnp.zeros((1, rows), jnp.float32)
    for start in range(0, rows, LANES):
        other = column_of(row_key[:, start : start + LANES])
        rank = rank + jnp.sum(jnp.where(other < row_key, 1.0, 0.0), axis=0, keepdims=True)
    pos = (coarse * capacity + rank - before).astype(jnp.int32)
    pos_row[...] = pos
    pos_ref[...] = jnp.concatenate(
        [pos[:, start : start + LANES] for start in range(0, rows, LANES)], axis=0
    )
    x = x_ref[...].astype(jnp.float32)
    squares = jnp.sum(x * x, axis=1, keepdims=True)
    unit[...] = (x * lax.rsqrt(squares + epsilon)).astype(jnp.bfloat16)

    step = 256

    @pl.loop(0, out_ref.shape[0] // step)
    def _(block):
        slot = lax.broadcasted_iota(jnp.int32, (step, rows), 0) + block * step
        chosen = jnp.where(slot == pos_row[...], 1.0, 0.0).astype(jnp.bfloat16)
        packed = jnp.dot(chosen, unit[...], preferred_element_type=jnp.float32)
        out_ref[pl.ds(pl.multiple_of(block * step, step), step), :] = packed.astype(jnp.bfloat16)


def pack(embeddings, labels, owner_map, n_owner, capacity):
    rows, width = embeddings.shape
    n_fine = owner_map.shape[0]
    total = n_owner * capacity
    vmem = pl.BlockSpec(memory_space=pltpu.VMEM)
    return pl.pallas_call(
        functools.partial(pack_kernel, n_owner, capacity),
        out_shape=(
            jax.ShapeDtypeStruct((total, width), jnp.bfloat16),
            jax.ShapeDtypeStruct((rows // LANES, LANES), jnp.int32),
            jax.ShapeDtypeStruct((1, n_fine), jnp.int32),
        ),
        in_specs=[vmem] * 3,
        out_specs=(vmem, vmem, vmem),
        scratch_shapes=[pltpu.VMEM((rows, width), jnp.bfloat16), pltpu.VMEM((1, rows), jnp.int32)],
        compiler_params=pltpu.CompilerParams(vmem_limit_bytes=VMEM_LIMIT),
    )(embeddings, labels.reshape(rows // LANES, LANES), owner_map.reshape(1, n_fine))


def counts_kernel(n_owner, capacity, cnt_ref, mine_ref, other_ref, out_ref, lab_lane, lab_sub, bias):
    total = mine_ref.shape[0]
    per_owner = cnt_ref.shape[1] // n_owner
    me = lax.axis_index("cl")
    grp = lax.axis_index("grp")
    n_grp = lax.axis_size("grp")
    for member in range(2):
        for source in range(n_owner):
            line = source * n_grp + lax.rem(grp + member, n_grp)
            edges = []
            edge = jnp.int32(0)
            for f in range(per_owner):
                edge = edge + cnt_ref[line, me * per_owner + f]
                edges.append(edge)
            down = lax.broadcasted_iota(jnp.int32, (capacity, LANES), 0)
            label = jnp.zeros((capacity, LANES), jnp.int32)
            for edge in edges:
                label = label + jnp.where(down >= edge, 1, 0)
            start = (member * n_owner + source) * capacity
            lab_sub[start : start + capacity, :] = label
            bias[start : start + capacity, :] = jnp.where(
                label < per_owner, NEIGHBOUR - SCALE, DEAD
            )
            if member == 0:
                across = lax.broadcasted_iota(jnp.int32, (1, capacity), 1)
                label = jnp.zeros((1, capacity), jnp.int32)
                for edge in edges:
                    label = label + jnp.where(across >= edge, 1, 0)
                lab_lane[:, source * capacity : (source + 1) * capacity] = jnp.where(
                    label < per_owner, label, -1
                )
    wide, deep = min(512, total), min(256, total)

    @pl.loop(0, total // wide)
    def _(block):
        columns = pl.ds(pl.multiple_of(block * wide, wide), wide)
        rows_i = mine_ref[columns, :]
        label_i = lab_lane[:, columns]

        def add(ref, offset):
            def step(j, acc):
                start = pl.multiple_of(j * deep, deep)
                scores = lax.dot_general(
                    ref[pl.ds(start, deep), :],
                    rows_i,
                    (((1,), (1,)), ((), ())),
                    preferred_element_type=jnp.float32,
                )
                place = pl.ds(pl.multiple_of(start + offset, deep), deep)
                label_j = lab_sub[place, :]
                bias_j = bias[place, :]
                repeat = wide // LANES
                label_j = jnp.concatenate([label_j] * repeat, axis=1)
                bias_j = jnp.concatenate([bias_j] * repeat, axis=1)
                shift = jnp.where(label_j == label_i, -SCALE, bias_j)
                terms = jnp.exp2(scores * SCALE + shift)
                return acc + jnp.sum(terms.reshape(deep // 8, 8, wide), axis=0)

            return step

        acc = jnp.zeros((8, wide), jnp.float32)
        acc = lax.fori_loop(0, total // deep, add(mine_ref, 0), acc, unroll=2)
        acc = lax.fori_loop(0, total // deep, add(other_ref, total), acc, unroll=2)
        totals = jnp.sum(acc, axis=0, keepdims=True)
        out_ref[:, columns] = jnp.log(jnp.where(label_i >= 0, totals, 1.0))


def log_counts(counts, mine, other, n_owner, capacity):
    total = mine.shape[0]
    vmem = pl.BlockSpec(memory_space=pltpu.VMEM)
    return pl.pallas_call(
        functools.partial(counts_kernel, n_owner, capacity),
        out_shape=jax.ShapeDtypeStruct((1, total), jnp.float32),
        in_specs=[pl.BlockSpec(memory_space=pltpu.SMEM), vmem, vmem],
        out_specs=vmem,
        scratch_shapes=[
            pltpu.VMEM((1, total), jnp.int32),
            pltpu.VMEM((2 * total, LANES), jnp.int32),
            pltpu.VMEM((2 * total, LANES), jnp.float32),
        ],
        compiler_params=pltpu.CompilerParams(vmem_limit_bytes=VMEM_LIMIT),
    )(counts, mine, other)


def unpack_kernel(values_ref, pos_ref, out_ref):
    pos = pos_ref[...]
    lane = lax.rem(pos, LANES)
    line = lax.div(pos, LANES)
    out = jnp.zeros(pos.shape, jnp.float32)
    for r in range(values_ref.shape[0]):
        table = jnp.broadcast_to(values_ref[r : r + 1, :], pos.shape)
        found = jnp.take_along_axis(table, lane, axis=1)
        out = jnp.where(line == r, found, out)
    out_ref[...] = out


def unpack(values, pos):
    vmem = pl.BlockSpec(memory_space=pltpu.VMEM)
    return pl.pallas_call(
        unpack_kernel,
        out_shape=jax.ShapeDtypeStruct(pos.shape, jnp.float32),
        in_specs=[vmem, vmem],
        out_specs=vmem,
    )(values.reshape(-1, LANES), pos)


def swapped(x, first, second):
    return jnp.where(x == first, second, jnp.where(x == second, first, x))


def fast_pack_kernel(n_owner, capacity, main, home, x_hbm, lab_hbm, map_hbm, *refs):
    main_ref, extra_ref, pos_ref, x_ref, lab_ref, map_ref, unit, pos_row, sems = refs
    copies = [
        pltpu.make_async_copy(src, dst, sems.at[i])
        for i, (src, dst) in enumerate(((x_hbm, x_ref), (lab_hbm, lab_ref), (map_hbm, map_ref)))
    ]
    for copy in copies:
        copy.start()
    rows = x_ref.shape[0]
    n_fine = map_ref.shape[1]
    per_owner = n_fine // n_owner
    rest = capacity - main
    copies[1].wait()
    copies[2].wait()
    owner_row = map_ref[...].astype(jnp.float32)
    fine_row = lax.broadcasted_iota(jnp.int32, (1, n_fine), 1).astype(jnp.float32)
    key_row = owner_row * n_fine + fine_row
    key_col = column_of(key_row)
    sorted_col = jnp.sum(jnp.where(key_row < key_col, 1.0, 0.0), axis=1, keepdims=True)
    lab = lab_ref[...].astype(jnp.float32)
    lab_row = jnp.concatenate([lab[b : b + 1, :] for b in range(lab.shape[0])], axis=1)
    fine_col = lax.broadcasted_iota(jnp.int32, (n_fine, rows), 0).astype(jnp.float32)
    fine_id = jnp.sum(jnp.where(fine_col == lab_row, sorted_col, 0.0), axis=0, keepdims=True)
    counts_col = jnp.sum(jnp.where(fine_col == fine_id, 1.0, 0.0), axis=1, keepdims=True)
    coarse = jnp.floor((fine_id + 0.5) * (1.0 / per_owner))
    first = coarse * per_owner
    before = jnp.sum(jnp.where(fine_col < first, counts_col, 0.0), axis=0, keepdims=True)
    upto = jnp.sum(jnp.where(fine_col < first + per_owner, counts_col, 0.0), axis=0, keepdims=True)
    full = jnp.min(
        jnp.where(upto - before == capacity, coarse, float(n_owner)), axis=1, keepdims=True
    )
    line = lax.broadcasted_iota(jnp.int32, (n_fine, LANES), 0)
    lane = lax.broadcasted_iota(jnp.int32, (n_fine, LANES), 1)
    inside = (line <= lane) & (lax.div(line, per_owner) == lax.div(lane, per_owner))
    running = jnp.sum(jnp.where(inside, counts_col, 0.0), axis=0, keepdims=True)
    info = jnp.where(lane[:1] < n_fine, running, full)
    index = lax.broadcasted_iota(jnp.int32, (1, rows), 1).astype(jnp.float32)
    row_key = fine_id * rows + index
    rank = jnp.zeros((1, rows), jnp.float32)
    for start in range(0, rows, LANES):
        other = column_of(row_key[:, start : start + LANES])
        rank = rank + jnp.sum(jnp.where(other < row_key, 1.0, 0.0), axis=0, keepdims=True)
    rank = (rank - before).astype(jnp.int32)
    place = swapped(coarse.astype(jnp.int32), full.astype(jnp.int32), home)
    table = place * capacity + rank
    pos_ref[...] = jnp.concatenate(
        [table[:, start : start + LANES] for start in range(0, rows, LANES)], axis=0
    )
    later = jnp.where(place == home, n_owner * main + rank - main, -1)
    pos_row[...] = jnp.where(rank < main, place * main + rank, later)
    copies[0].wait()
    x = x_ref[...].astype(jnp.float32)
    squares = jnp.sum(x * x, axis=1, keepdims=True)
    unit[...] = (x * lax.rsqrt(squares + epsilon)).astype(jnp.bfloat16)

    def chosen_rows(start, count):
        slot = lax.broadcasted_iota(jnp.int32, (count, rows), 0) + start
        chosen = jnp.where(slot == pos_row[...], 1.0, 0.0).astype(jnp.bfloat16)
        return jnp.dot(chosen, unit[...], preferred_element_type=jnp.float32).astype(jnp.bfloat16)

    extra_ref[:rest, :] = chosen_rows(n_owner * main, rest)
    extra_ref[rest:, :] = jnp.zeros((extra_ref.shape[0] - rest, extra_ref.shape[1]), jnp.bfloat16)
    extra_ref[rest:, :LANES] = jnp.broadcast_to(
        info, (extra_ref.shape[0] - rest, LANES)
    ).astype(jnp.bfloat16)
    count = n_owner * main // 4
    for start in range(0, n_owner * main, count):
        main_ref[start : start + count, :] = chosen_rows(start, count)


def fast_pack(embeddings, labels, owner_map, n_owner, capacity, main, home):
    rows, width = embeddings.shape
    n_fine = owner_map.shape[0]
    vmem = pl.BlockSpec(memory_space=pltpu.VMEM)
    anywhere = pl.BlockSpec(memory_space=pl.ANY)
    lab_shape = (rows // LANES, LANES)
    return pl.pallas_call(
        functools.partial(fast_pack_kernel, n_owner, capacity, main, home),
        out_shape=(
            jax.ShapeDtypeStruct((n_owner * main, width), jnp.bfloat16),
            jax.ShapeDtypeStruct((capacity - main + INFO, width), jnp.bfloat16),
            jax.ShapeDtypeStruct(lab_shape, jnp.int32),
        ),
        in_specs=[anywhere] * 3,
        out_specs=(vmem,) * 3,
        scratch_shapes=[
            pltpu.VMEM((rows, width), jnp.bfloat16),
            pltpu.VMEM(lab_shape, jnp.int32),
            pltpu.VMEM((1, n_fine), jnp.int32),
            pltpu.VMEM((rows, width), jnp.bfloat16),
            pltpu.VMEM((1, rows), jnp.int32),
            pltpu.SemaphoreType.DMA((3,)),
        ],
        compiler_params=pltpu.CompilerParams(vmem_limit_bytes=FAST_LIMIT),
    )(embeddings, labels.reshape(lab_shape), owner_map.reshape(1, n_fine))


def pieces(start, count, parts):
    return [(start + i * (count // parts), count // parts) for i in range(parts)]


def fast_counts_kernel(
    n_owner, n_fine, capacity, main, home, mine_ref, other_ref, gathered, *refs
):
    out_ref, unfit_ref, rows_ref, lab_lane, lab_sub, bias, result, sems = refs
    per_owner = n_fine // n_owner
    rest = capacity - main
    n_main, n_rest = n_owner * main, n_owner * rest
    total = n_main + n_rest
    grp = lax.axis_index("grp")
    me = lax.axis_index("cl")
    is_home = me == home
    copies = [
        pltpu.make_async_copy(
            gathered.at[pl.ds((2 * k + lax.rem(grp + member, 2)) * (rest + INFO), rest)],
            rows_ref.at[pl.ds(member * n_rest + k * rest, rest)],
            sems.at[member * n_owner + k],
        )
        for member in range(2)
        for k in range(n_owner)
    ]

    @pl.when(is_home)
    def _():
        for copy in copies:
            copy.start()

    def info_of(line):
        start = pl.multiple_of(line * (rest + INFO) + rest, INFO)
        return gathered[pl.ds(start, INFO), :LANES][:1].astype(jnp.float32)

    lane = lax.broadcasted_iota(jnp.int32, (1, LANES), 1)
    hot = jnp.max(jnp.where(lane == n_fine, info_of(0), 0.0), axis=1, keepdims=True)
    hot = hot.astype(jnp.int32)
    lane_cluster = lax.div(lane, per_owner)
    is_edge = lane_cluster == swapped(me, hot, home)
    last = (lane < n_fine) & (lax.rem(lane, per_owner) == per_owner - 1) & (lane_cluster != hot)
    unfit = jnp.zeros((1, LANES), jnp.float32)
    for member in range(2):
        for k in range(n_owner):
            info = info_of(2 * k + lax.rem(grp + member, 2))
            wrong = (last & (info > main)) | ((lane == n_fine) & (info != hot.astype(jnp.float32)))
            unfit = unfit + jnp.where(wrong, 1.0, 0.0)
            edges = jnp.where(is_edge, info, 2.0 * capacity)

            def write(start, first, count, edges=edges):
                slot = lax.broadcasted_iota(jnp.int32, (count, LANES), 0) + first
                label = jnp.where(slot.astype(jnp.float32) >= edges, 1.0, 0.0)
                label = jnp.broadcast_to(jnp.sum(label, axis=1, keepdims=True), (count, LANES))
                lab_sub[start : start + count, :] = label
                bias[start : start + count, :] = jnp.where(
                    label < per_owner, NEIGHBOUR - SCALE, DEAD
                )

            write(member * n_main + k * main, 0, main)

            @pl.when(is_home)
            def _():
                write(2 * n_main + member * n_rest + k * rest, main, rest)

    unfit_ref[...] = jnp.broadcast_to(
        jnp.max(unfit, axis=1, keepdims=True), unfit_ref.shape
    ).astype(jnp.int32)

    def turn(start, count, to):
        for i in range(0, count, LANES):
            block = jnp.transpose(lab_sub[start + i : start + i + LANES, :])[:1]
            lab_lane[:, to + i : to + i + LANES] = jnp.where(block < per_owner, block, -1.0)

    turn(0, n_main, 0)

    @pl.when(is_home)
    def _():
        turn(2 * n_main, n_rest, n_main)

    near = [(mine_ref, s, s, d) for s, d in pieces(0, n_main, 2)]
    near += [(other_ref, s, s + n_main, d) for s, d in pieces(0, n_main, 2)]
    far = [(rows_ref, s, s + 2 * n_main, d) for s, d in pieces(0, 2 * n_rest, 4)]

    def sums(rows_i, label_i, tiles):
        wide = rows_i.shape[0]

        def scores_of(tile):
            ref, start, _, deep = tile
            return lax.dot_general(
                ref[start : start + deep, :],
                rows_i,
                (((1,), (1,)), ((), ())),
                preferred_element_type=jnp.float32,
            )

        acc = jnp.zeros((8, wide), jnp.float32)
        ahead = scores_of(tiles[0])
        for i, (_, _, place, deep) in enumerate(tiles):
            scores = ahead
            if i + 1 < len(tiles):
                ahead = scores_of(tiles[i + 1])
            label_j = jnp.concatenate([lab_sub[place : place + deep, :]] * (wide // LANES), axis=1)
            bias_j = jnp.concatenate([bias[place : place + deep, :]] * (wide // LANES), axis=1)
            shift = jnp.where(label_j == label_i, -SCALE, bias_j)
            terms = jnp.exp2(scores * SCALE + shift)
            acc = acc + jnp.sum(terms.reshape(deep // 8, 8, wide), axis=0)
        return jnp.sum(acc, axis=0, keepdims=True)

    def block(ref, start, wide, to):
        label_i = lab_lane[:, pl.ds(to, wide)]
        result[:, pl.ds(to, wide)] = sums(ref[pl.ds(start, wide), :], label_i, near)

    def block_far(ref, start, wide, to):
        label_i = lab_lane[:, pl.ds(to, wide)]
        result[:, pl.ds(to, wide)] += sums(ref[pl.ds(start, wide), :], label_i, far)

    def each_block(ref, count, to, run):
        wide = 256
        full = count // wide

        @pl.loop(0, full)
        def _(i):
            start = pl.multiple_of(i * wide, wide)
            run(ref, start, wide, pl.multiple_of(start + to, LANES))

        if count % wide:
            run(ref, full * wide, count % wide, full * wide + to)

    each_block(mine_ref, n_main, 0, block)

    @pl.when(is_home)
    def _():
        for copy in copies:
            copy.wait()
        each_block(mine_ref, n_main, 0, block_far)
        each_block(rows_ref, n_rest, n_main, block)
        each_block(rows_ref, n_rest, n_main, block_far)

    values = jnp.log(jnp.where(lab_lane[...] >= 0, result[...], 1.0))
    for k in range(n_owner):
        out_ref[k, :, :main] = values[:, k * main : (k + 1) * main]
        out_ref[k, :, main:] = values[:, n_main + k * rest : n_main + (k + 1) * rest]


def fast_counts(mine, other, gathered, n_owner, n_fine, capacity, main, home):
    width = mine.shape[1]
    total = n_owner * capacity
    n_rest = n_owner * (capacity - main)
    vmem = pl.BlockSpec(memory_space=pltpu.VMEM)
    return pl.pallas_call(
        functools.partial(fast_counts_kernel, n_owner, n_fine, capacity, main, home),
        out_shape=(
            jax.ShapeDtypeStruct((n_owner, 1, capacity), jnp.float32),
            jax.ShapeDtypeStruct((8, LANES), jnp.int32),
        ),
        in_specs=[vmem] * 3,
        out_specs=(vmem, vmem),
        scratch_shapes=[
            pltpu.VMEM((2 * n_rest, width), jnp.bfloat16),
            pltpu.VMEM((1, total), jnp.float32),
            pltpu.VMEM((2 * total, LANES), jnp.float32),
            pltpu.VMEM((2 * total, LANES), jnp.float32),
            pltpu.VMEM((1, total), jnp.float32),
            pltpu.SemaphoreType.DMA((2 * n_owner,)),
        ],
        compiler_params=pltpu.CompilerParams(vmem_limit_bytes=FAST_LIMIT),
    )(mine, other, gathered)


def fast_unpack_kernel(values_ref, pos_ref, out_ref):
    pos = pos_ref[...]
    lane = lax.rem(pos, LANES)
    line = lax.div(pos, LANES)
    out = jnp.zeros(pos.shape, jnp.float32)
    per = values_ref.shape[2] // LANES
    for r in range(values_ref.shape[0] * per):
        start = r % per * LANES
        table = jnp.broadcast_to(values_ref[r // per, :, start : start + LANES], pos.shape)
        found = jnp.take_along_axis(table, lane, axis=1)
        out = jnp.where(line == r, found, out)
    out_ref[...] = out


def fast_unpack(values, pos):
    vmem = pl.BlockSpec(memory_space=pltpu.VMEM)
    return pl.pallas_call(
        fast_unpack_kernel,
        out_shape=jax.ShapeDtypeStruct(pos.shape, jnp.float32),
        in_specs=[vmem, vmem],
        out_specs=vmem,
    )(values, pos)


def general(embeddings, labels, owner_map):
    n_owner = lax.axis_size("cl")
    capacity = SLOTS // n_owner
    rows, width = embeddings.shape
    packed, pos, counts = pack(embeddings, labels, owner_map, n_owner, capacity)
    counts = lax.all_gather(counts, ("cl", "grp"), tiled=True)
    mine = lax.all_to_all(
        packed.reshape(n_owner, capacity, width), "cl", split_axis=0, concat_axis=0, tiled=True
    ).reshape(SLOTS, width)
    other = lax.ppermute(mine, "grp", [(0, 1), (1, 0)])
    results = log_counts(counts, mine, other, n_owner, capacity)
    returned = lax.all_to_all(
        results.reshape(n_owner, capacity), "cl", split_axis=0, concat_axis=0, tiled=True
    )
    return unpack(returned.reshape(SLOTS), pos).reshape(rows)


def body(embeddings, labels, owner_map):
    n_owner = lax.axis_size("cl")
    capacity = SLOTS // n_owner
    rows = embeddings.shape[0]
    n_fine = owner_map.shape[0]
    main = -(-(rows // n_owner * 9 // 8) // 16) * 16
    if main >= capacity or n_fine >= LANES:
        return general(embeddings, labels, owner_map)
    home = n_owner // 4
    width = embeddings.shape[1]
    packed, extra, pos = fast_pack(embeddings, labels, owner_map, n_owner, capacity, main, home)
    gathered = lax.all_gather(extra, ("cl", "grp"), tiled=True)
    mine = lax.all_to_all(
        packed.reshape(n_owner, main, width), "cl", split_axis=0, concat_axis=0, tiled=True
    ).reshape(n_owner * main, width)
    other = lax.ppermute(mine, "grp", [(0, 1), (1, 0)])
    results, unfit = fast_counts(mine, other, gathered, n_owner, n_fine, capacity, main, home)
    returned = lax.all_to_all(results, "cl", split_axis=0, concat_axis=0, tiled=True)
    return lax.cond(
        unfit[0, 0] == 0,
        lambda: fast_unpack(returned, pos).reshape(rows),
        lambda: general(embeddings, labels, owner_map),
    )


def solution(mesh):
    return jax.shard_map(
        body,
        mesh=mesh,
        in_specs=(P(("parts", "cl", "grp"), None), P(("parts", "cl", "grp")), P("parts")),
        out_specs=P(("parts", "cl", "grp")),
        check_vma=False,
    )
```

```python
import functools
import math

import jax
import jax.numpy as jnp
from jax import lax
from jax.experimental import pallas as pl
from jax.experimental.pallas import tpu as pltpu
from jax.sharding import PartitionSpec as P

SLOTS = 2048

temper = 0.2
neighbour_factor = 0.5
epsilon = 1e-06

LANES = 128
SCALE = math.log2(math.e) / temper
NEIGHBOUR = math.log2(neighbour_factor)
DEAD = -1e30
VMEM_LIMIT = 48 * 1024 * 1024
FAST_LIMIT = 40 * 1024 * 1024
INFO = 16


def column_of(row):
    pieces = []
    for start in range(0, row.shape[1], LANES):
        width = min(LANES, row.shape[1] - start)
        shape = (width, width)
        diagonal = lax.broadcasted_iota(jnp.int32, shape, 0) == lax.broadcasted_iota(
            jnp.int32, shape, 1
        )
        piece = jnp.broadcast_to(row[:, start : start + width], shape)
        pieces.append(jnp.sum(jnp.where(diagonal, piece, 0.0), axis=1, keepdims=True))
    return jnp.concatenate(pieces, axis=0)


def row_of(column):
    n = column.shape[0]
    diagonal = lax.broadcasted_iota(jnp.int32, (n, n), 0) == lax.broadcasted_iota(
        jnp.int32, (n, n), 1
    )
    return jnp.sum(jnp.where(diagonal, column, 0.0), axis=0, keepdims=True)


def pack_kernel(n_owner, capacity, x_ref, lab_ref, map_ref, out_ref, pos_ref, cnt_ref, unit, pos_row):
    rows = x_ref.shape[0]
    n_fine = map_ref.shape[1]
    per_owner = n_fine // n_owner
    owner_row = map_ref[...].astype(jnp.float32)
    fine_row = lax.broadcasted_iota(jnp.int32, (1, n_fine), 1).astype(jnp.float32)
    key_row = owner_row * n_fine + fine_row
    key_col = column_of(key_row)
    sorted_col = jnp.sum(jnp.where(key_row < key_col, 1.0, 0.0), axis=1, keepdims=True)
    lab = lab_ref[...].astype(jnp.float32)
    lab_row = jnp.concatenate([lab[b : b + 1, :] for b in range(lab.shape[0])], axis=1)
    fine_col = lax.broadcasted_iota(jnp.int32, (n_fine, rows), 0).astype(jnp.float32)
    fine_id = jnp.sum(jnp.where(fine_col == lab_row, sorted_col, 0.0), axis=0, keepdims=True)
    counts_col = jnp.sum(jnp.where(fine_col == fine_id, 1.0, 0.0), axis=1, keepdims=True)
    cnt_ref[...] = row_of(counts_col).astype(jnp.int32)
    coarse = jnp.floor((fine_id + 0.5) * (1.0 / per_owner))
    before = jnp.sum(
        jnp.where(fine_col < coarse * per_owner, counts_col, 0.0), axis=0, keepdims=True
    )
    index = lax.broadcasted_iota(jnp.int32, (1, rows), 1).astype(jnp.float32)
    row_key = fine_id * rows + index
    rank = jnp.zeros((1, rows), jnp.float32)
    for start in range(0, rows, LANES):
        other = column_of(row_key[:, start : start + LANES])
        rank = rank + jnp.sum(jnp.where(other < row_key, 1.0, 0.0), axis=0, keepdims=True)
    pos = (coarse * capacity + rank - before).astype(jnp.int32)
    pos_row[...] = pos
    pos_ref[...] = jnp.concatenate(
        [pos[:, start : start + LANES] for start in range(0, rows, LANES)], axis=0
    )
    x = x_ref[...].astype(jnp.float32)
    squares = jnp.sum(x * x, axis=1, keepdims=True)
    unit[...] = (x * lax.rsqrt(squares + epsilon)).astype(jnp.bfloat16)

    step = 256

    @pl.loop(0, out_ref.shape[0] // step)
    def _(block):
        slot = lax.broadcasted_iota(jnp.int32, (step, rows), 0) + block * step
        chosen = jnp.where(slot == pos_row[...], 1.0, 0.0).astype(jnp.bfloat16)
        packed = jnp.dot(chosen, unit[...], preferred_element_type=jnp.float32)
        out_ref[pl.ds(pl.multiple_of(block * step, step), step), :] = packed.astype(jnp.bfloat16)


def pack(embeddings, labels, owner_map, n_owner, capacity):
    rows, width = embeddings.shape
    n_fine = owner_map.shape[0]
    total = n_owner * capacity
    vmem = pl.BlockSpec(memory_space=pltpu.VMEM)
    return pl.pallas_call(
        functools.partial(pack_kernel, n_owner, capacity),
        out_shape=(
            jax.ShapeDtypeStruct((total, width), jnp.bfloat16),
            jax.ShapeDtypeStruct((rows // LANES, LANES), jnp.int32),
            jax.ShapeDtypeStruct((1, n_fine), jnp.int32),
        ),
        in_specs=[vmem] * 3,
        out_specs=(vmem, vmem, vmem),
        scratch_shapes=[pltpu.VMEM((rows, width), jnp.bfloat16), pltpu.VMEM((1, rows), jnp.int32)],
        compiler_params=pltpu.CompilerParams(vmem_limit_bytes=VMEM_LIMIT),
    )(embeddings, labels.reshape(rows // LANES, LANES), owner_map.reshape(1, n_fine))


def counts_kernel(n_owner, capacity, cnt_ref, mine_ref, other_ref, out_ref, lab_lane, lab_sub, bias):
    total = mine_ref.shape[0]
    per_owner = cnt_ref.shape[1] // n_owner
    me = lax.axis_index("cl")
    grp = lax.axis_index("grp")
    n_grp = lax.axis_size("grp")
    for member in range(2):
        for source in range(n_owner):
            line = source * n_grp + lax.rem(grp + member, n_grp)
            edges = []
            edge = jnp.int32(0)
            for f in range(per_owner):
                edge = edge + cnt_ref[line, me * per_owner + f]
                edges.append(edge)
            down = lax.broadcasted_iota(jnp.int32, (capacity, LANES), 0)
            label = jnp.zeros((capacity, LANES), jnp.int32)
            for edge in edges:
                label = label + jnp.where(down >= edge, 1, 0)
            start = (member * n_owner + source) * capacity
            lab_sub[start : start + capacity, :] = label
            bias[start : start + capacity, :] = jnp.where(
                label < per_owner, NEIGHBOUR - SCALE, DEAD
            )
            if member == 0:
                across = lax.broadcasted_iota(jnp.int32, (1, capacity), 1)
                label = jnp.zeros((1, capacity), jnp.int32)
                for edge in edges:
                    label = label + jnp.where(across >= edge, 1, 0)
                lab_lane[:, source * capacity : (source + 1) * capacity] = jnp.where(
                    label < per_owner, label, -1
                )
    wide, deep = min(512, total), min(256, total)

    @pl.loop(0, total // wide)
    def _(block):
        columns = pl.ds(pl.multiple_of(block * wide, wide), wide)
        rows_i = mine_ref[columns, :]
        label_i = lab_lane[:, columns]

        def add(ref, offset):
            def step(j, acc):
                start = pl.multiple_of(j * deep, deep)
                scores = lax.dot_general(
                    ref[pl.ds(start, deep), :],
                    rows_i,
                    (((1,), (1,)), ((), ())),
                    preferred_element_type=jnp.float32,
                )
                place = pl.ds(pl.multiple_of(start + offset, deep), deep)
                label_j = lab_sub[place, :]
                bias_j = bias[place, :]
                repeat = wide // LANES
                label_j = jnp.concatenate([label_j] * repeat, axis=1)
                bias_j = jnp.concatenate([bias_j] * repeat, axis=1)
                shift = jnp.where(label_j == label_i, -SCALE, bias_j)
                terms = jnp.exp2(scores * SCALE + shift)
                return acc + jnp.sum(terms.reshape(deep // 8, 8, wide), axis=0)

            return step

        acc = jnp.zeros((8, wide), jnp.float32)
        acc = lax.fori_loop(0, total // deep, add(mine_ref, 0), acc, unroll=2)
        acc = lax.fori_loop(0, total // deep, add(other_ref, total), acc, unroll=2)
        totals = jnp.sum(acc, axis=0, keepdims=True)
        out_ref[:, columns] = jnp.log(jnp.where(label_i >= 0, totals, 1.0))


def log_counts(counts, mine, other, n_owner, capacity):
    total = mine.shape[0]
    vmem = pl.BlockSpec(memory_space=pltpu.VMEM)
    return pl.pallas_call(
        functools.partial(counts_kernel, n_owner, capacity),
        out_shape=jax.ShapeDtypeStruct((1, total), jnp.float32),
        in_specs=[pl.BlockSpec(memory_space=pltpu.SMEM), vmem, vmem],
        out_specs=vmem,
        scratch_shapes=[
            pltpu.VMEM((1, total), jnp.int32),
            pltpu.VMEM((2 * total, LANES), jnp.int32),
            pltpu.VMEM((2 * total, LANES), jnp.float32),
        ],
        compiler_params=pltpu.CompilerParams(vmem_limit_bytes=VMEM_LIMIT),
    )(counts, mine, other)


def unpack_kernel(values_ref, pos_ref, out_ref):
    pos = pos_ref[...]
    lane = lax.rem(pos, LANES)
    line = lax.div(pos, LANES)
    out = jnp.zeros(pos.shape, jnp.float32)
    for r in range(values_ref.shape[0]):
        table = jnp.broadcast_to(values_ref[r : r + 1, :], pos.shape)
        found = jnp.take_along_axis(table, lane, axis=1)
        out = jnp.where(line == r, found, out)
    out_ref[...] = out


def unpack(values, pos):
    vmem = pl.BlockSpec(memory_space=pltpu.VMEM)
    return pl.pallas_call(
        unpack_kernel,
        out_shape=jax.ShapeDtypeStruct(pos.shape, jnp.float32),
        in_specs=[vmem, vmem],
        out_specs=vmem,
    )(values.reshape(-1, LANES), pos)


def swapped(x, first, second):
    return jnp.where(x == first, second, jnp.where(x == second, first, x))


def fast_pack_kernel(n_owner, capacity, main, home, x_hbm, lab_hbm, map_hbm, *refs):
    main_ref, extra_ref, pos_ref, x_ref, lab_ref, map_ref, unit, pos_row, sems = refs
    copies = [
        pltpu.make_async_copy(src, dst, sems.at[i])
        for i, (src, dst) in enumerate(((x_hbm, x_ref), (lab_hbm, lab_ref), (map_hbm, map_ref)))
    ]
    for copy in copies:
        copy.start()
    rows = x_ref.shape[0]
    n_fine = map_ref.shape[1]
    per_owner = n_fine // n_owner
    rest = capacity - main
    copies[1].wait()
    copies[2].wait()
    owner_row = map_ref[...].astype(jnp.float32)
    fine_row = lax.broadcasted_iota(jnp.int32, (1, n_fine), 1).astype(jnp.float32)
    key_row = owner_row * n_fine + fine_row
    key_col = column_of(key_row)
    sorted_col = jnp.sum(jnp.where(key_row < key_col, 1.0, 0.0), axis=1, keepdims=True)
    lab = lab_ref[...].astype(jnp.float32)
    lab_row = jnp.concatenate([lab[b : b + 1, :] for b in range(lab.shape[0])], axis=1)
    fine_col = lax.broadcasted_iota(jnp.int32, (n_fine, rows), 0).astype(jnp.float32)
    fine_id = jnp.sum(jnp.where(fine_col == lab_row, sorted_col, 0.0), axis=0, keepdims=True)
    counts_col = jnp.sum(jnp.where(fine_col == fine_id, 1.0, 0.0), axis=1, keepdims=True)
    coarse = jnp.floor((fine_id + 0.5) * (1.0 / per_owner))
    first = coarse * per_owner
    before = jnp.sum(jnp.where(fine_col < first, counts_col, 0.0), axis=0, keepdims=True)
    upto = jnp.sum(jnp.where(fine_col < first + per_owner, counts_col, 0.0), axis=0, keepdims=True)
    full = jnp.min(
        jnp.where(upto - before == capacity, coarse, float(n_owner)), axis=1, keepdims=True
    )
    line = lax.broadcasted_iota(jnp.int32, (n_fine, LANES), 0)
    lane = lax.broadcasted_iota(jnp.int32, (n_fine, LANES), 1)
    inside = (line <= lane) & (lax.div(line, per_owner) == lax.div(lane, per_owner))
    running = jnp.sum(jnp.where(inside, counts_col, 0.0), axis=0, keepdims=True)
    info = jnp.where(lane[:1] < n_fine, running, full)
    index = lax.broadcasted_iota(jnp.int32, (1, rows), 1).astype(jnp.float32)
    row_key = fine_id * rows + index
    rank = jnp.zeros((1, rows), jnp.float32)
    for start in range(0, rows, LANES):
        other = column_of(row_key[:, start : start + LANES])
        rank = rank + jnp.sum(jnp.where(other < row_key, 1.0, 0.0), axis=0, keepdims=True)
    rank = (rank - before).astype(jnp.int32)
    place = swapped(coarse.astype(jnp.int32), full.astype(jnp.int32), home)
    table = place * capacity + rank
    pos_ref[...] = jnp.concatenate(
        [table[:, start : start + LANES] for start in range(0, rows, LANES)], axis=0
    )
    later = jnp.where(place == home, n_owner * main + rank - main, -1)
    fits = rank < jnp.where(place == home, main, main - 1)
    pos_row[...] = jnp.where(fits, place * main + rank, later)
    copies[0].wait()
    x = x_ref[...].astype(jnp.float32)
    squares = jnp.sum(x * x, axis=1, keepdims=True)
    unit[...] = (x * lax.rsqrt(squares + epsilon)).astype(jnp.bfloat16)

    def chosen_rows(start, count):
        slot = lax.broadcasted_iota(jnp.int32, (count, rows), 0) + start
        chosen = jnp.where(slot == pos_row[...], 1.0, 0.0).astype(jnp.bfloat16)
        return jnp.dot(chosen, unit[...], preferred_element_type=jnp.float32).astype(jnp.bfloat16)

    extra_ref[:rest, :] = chosen_rows(n_owner * main, rest)
    extra_ref[rest:, :] = jnp.zeros((extra_ref.shape[0] - rest, extra_ref.shape[1]), jnp.bfloat16)
    extra_ref[rest:, :LANES] = jnp.broadcast_to(
        info, (extra_ref.shape[0] - rest, LANES)
    ).astype(jnp.bfloat16)
    count = n_owner * main // 4
    for start in range(0, n_owner * main, count):
        main_ref[start : start + count, :] = chosen_rows(start, count)
    for owner in range(n_owner):
        if owner != home:
            tail = slice((owner + 1) * main - INFO, (owner + 1) * main)
            old = main_ref[tail, :LANES].astype(jnp.float32)
            down = lax.broadcasted_iota(jnp.int32, old.shape, 0)
            main_ref[tail, :LANES] = jnp.where(down == INFO - 1, info, old).astype(jnp.bfloat16)


def fast_pack(embeddings, labels, owner_map, n_owner, capacity, main, home):
    rows, width = embeddings.shape
    n_fine = owner_map.shape[0]
    vmem = pl.BlockSpec(memory_space=pltpu.VMEM)
    anywhere = pl.BlockSpec(memory_space=pl.ANY)
    lab_shape = (rows // LANES, LANES)
    return pl.pallas_call(
        functools.partial(fast_pack_kernel, n_owner, capacity, main, home),
        out_shape=(
            jax.ShapeDtypeStruct((n_owner * main, width), jnp.bfloat16),
            jax.ShapeDtypeStruct((capacity - main + INFO, width), jnp.bfloat16),
            jax.ShapeDtypeStruct(lab_shape, jnp.int32),
        ),
        in_specs=[anywhere] * 3,
        out_specs=(vmem,) * 3,
        scratch_shapes=[
            pltpu.VMEM((rows, width), jnp.bfloat16),
            pltpu.VMEM(lab_shape, jnp.int32),
            pltpu.VMEM((1, n_fine), jnp.int32),
            pltpu.VMEM((rows, width), jnp.bfloat16),
            pltpu.VMEM((1, rows), jnp.int32),
            pltpu.SemaphoreType.DMA((3,)),
        ],
        compiler_params=pltpu.CompilerParams(vmem_limit_bytes=FAST_LIMIT),
    )(embeddings, labels.reshape(lab_shape), owner_map.reshape(1, n_fine))


def pieces(start, count, parts):
    return [(start + i * (count // parts), count // parts) for i in range(parts)]


def gather_kernel(n_owner, rest, home, *refs):
    chunks, out, sems = refs[:n_owner], refs[n_owner], refs[n_owner + 1]
    copies = []
    for k, chunk in enumerate(chunks):
        source = home ^ k
        parts = (
            (0, rest, source * rest),
            (rest, INFO, n_owner * rest + source * INFO),
        )
        for start, count, to in parts:
            copies.append(
                pltpu.make_async_copy(
                    chunk.at[pl.ds(start, count)],
                    out.at[pl.ds(to, count)],
                    sems.at[len(copies)],
                )
            )

    @pl.when(lax.axis_index("cl") == home)
    def _():
        for copy in copies:
            copy.start()
        for copy in copies:
            copy.wait()


def gather_rest(chunks, n_owner, rest, home):
    anywhere = pl.BlockSpec(memory_space=pl.ANY)
    shape = (n_owner * (rest + INFO), chunks[0].shape[1])
    return pl.pallas_call(
        functools.partial(gather_kernel, n_owner, rest, home),
        out_shape=jax.ShapeDtypeStruct(shape, jnp.bfloat16),
        in_specs=[anywhere] * n_owner,
        out_specs=anywhere,
        scratch_shapes=[pltpu.SemaphoreType.DMA((2 * n_owner,))],
        cost_estimate=pl.CostEstimate(
            flops=0, bytes_accessed=4 * shape[0] * shape[1], transcendentals=0
        ),
    )(*chunks)


def fast_counts_kernel(
    n_owner, n_fine, capacity, main, home, mine_ref, other_ref, rest_mine, rest_other, *refs
):
    out_ref, unfit_ref, lab_lane, lab_sub, bias, result, score_a, score_b = refs
    per_owner = n_fine // n_owner
    rest = capacity - main
    n_main, n_rest = n_owner * main, n_owner * rest
    me = lax.axis_index("cl")
    is_home = me == home
    mains, rests = (mine_ref, other_ref), (rest_mine, rest_other)

    def info_of(member, k):
        in_main = mains[member][(k + 1) * main - INFO : (k + 1) * main, :LANES]
        start = n_rest + k * INFO
        in_rest = rests[member][start : start + INFO, :LANES]
        in_main = in_main.astype(jnp.float32)[INFO - 1 :]
        return jnp.where(is_home, in_rest.astype(jnp.float32)[INFO - 1 :], in_main)

    lane = lax.broadcasted_iota(jnp.int32, (1, LANES), 1)
    hot = jnp.max(jnp.where(lane == n_fine, info_of(0, 0), 0.0), axis=1, keepdims=True)
    hot = hot.astype(jnp.int32)
    lane_cluster = lax.div(lane, per_owner)
    is_edge = lane_cluster == swapped(me, hot, home)
    last = (lane < n_fine) & (lax.rem(lane, per_owner) == per_owner - 1) & (lane_cluster != hot)
    unfit = jnp.zeros((1, LANES), jnp.float32)
    for member in range(2):
        for k in range(n_owner):
            info = info_of(member, k)
            wrong = (last & (info >= main)) | ((lane == n_fine) & (info != hot.astype(jnp.float32)))
            unfit = unfit + jnp.where(wrong, 1.0, 0.0)
            edges = jnp.where(is_edge, info, 2.0 * capacity)

            def write(start, first, count, edges=edges):
                slot = lax.broadcasted_iota(jnp.int32, (count, LANES), 0) + first
                label = jnp.where(slot.astype(jnp.float32) >= edges, 1.0, 0.0)
                label = jnp.broadcast_to(jnp.sum(label, axis=1, keepdims=True), (count, LANES))
                lab_sub[start : start + count, :] = label
                bias[start : start + count, :] = jnp.where(
                    label < per_owner, NEIGHBOUR - SCALE, DEAD
                )

            write(member * n_main + k * main, 0, main)

            @pl.when(is_home)
            def _():
                write(2 * n_main + member * n_rest + k * rest, main, rest)

    unfit_ref[...] = jnp.broadcast_to(
        jnp.max(unfit, axis=1, keepdims=True), unfit_ref.shape
    ).astype(jnp.int32)

    def turn(start, count, to):
        for i in range(0, count, LANES):
            block = jnp.transpose(lab_sub[start + i : start + i + LANES, :])[:1]
            lab_lane[:, to + i : to + i + LANES] = jnp.where(block < per_owner, block, -1.0)

    turn(0, n_main, 0)

    @pl.when(is_home)
    def _():
        turn(2 * n_main, n_rest, n_main)

    near = [(mine_ref, s, s, d) for s, d in pieces(0, n_main, 2)]
    near += [(other_ref, s, s + n_main, d) for s, d in pieces(0, n_main, 2)]
    far = [(rest_mine, s, s + 2 * n_main, d) for s, d in pieces(0, n_rest, 2)]
    far += [(rest_other, s, s + 2 * n_main + n_rest, d) for s, d in pieces(0, n_rest, 2)]
    step = 32

    def sums(rows_i, label_i, tiles):
        wide = rows_i.shape[0]
        repeat = wide // LANES

        def scores_to(buffer, tile):
            ref, start, _, deep = tile
            buffer[:deep, :wide] = lax.dot_general(
                ref[start : start + deep, :],
                rows_i,
                (((1,), (1,)), ((), ())),
                preferred_element_type=jnp.float32,
            )

        acc = jnp.zeros((8, wide), jnp.float32)
        here, ahead = score_a, score_b
        scores_to(here, tiles[0])
        for i, (_, _, place, deep) in enumerate(tiles):
            if i + 1 < len(tiles):
                scores_to(ahead, tiles[i + 1])
            for c in range(0, deep, step):
                part = slice(place + c, place + c + step)
                label_j = jnp.concatenate([lab_sub[part, :]] * repeat, axis=1)
                bias_j = jnp.concatenate([bias[part, :]] * repeat, axis=1)
                shift = jnp.where(label_j == label_i, -SCALE, bias_j)
                terms = jnp.exp2(here[c : c + step, :wide] * SCALE + shift)
                acc = acc + jnp.sum(terms.reshape(step // 8, 8, wide), axis=0)
            here, ahead = ahead, here
        return jnp.sum(acc, axis=0, keepdims=True)

    def block(ref, start, wide, to):
        label_i = lab_lane[:, pl.ds(to, wide)]
        result[:, pl.ds(to, wide)] = sums(ref[pl.ds(start, wide), :], label_i, near)

    def block_far(ref, start, wide, to):
        label_i = lab_lane[:, pl.ds(to, wide)]
        result[:, pl.ds(to, wide)] += sums(ref[pl.ds(start, wide), :], label_i, far)

    def each_block(ref, count, to, run):
        wide = 256
        full = count // wide

        @pl.loop(0, full)
        def _(i):
            start = pl.multiple_of(i * wide, wide)
            run(ref, start, wide, pl.multiple_of(start + to, LANES))

        if count % wide:
            run(ref, full * wide, count % wide, full * wide + to)

    each_block(mine_ref, n_main, 0, block)

    @pl.when(is_home)
    def _():
        each_block(mine_ref, n_main, 0, block_far)
        each_block(rest_mine, n_rest, n_main, block)
        each_block(rest_mine, n_rest, n_main, block_far)

    values = jnp.log(jnp.where(lab_lane[...] >= 0, result[...], 1.0))
    for k in range(n_owner):
        out_ref[k, :, :main] = values[:, k * main : (k + 1) * main]
        out_ref[k, :, main:] = values[:, n_main + k * rest : n_main + (k + 1) * rest]


def fast_counts(arrays, n_owner, n_fine, capacity, main, home):
    total = n_owner * capacity
    n_main = n_owner * main
    vmem = pl.BlockSpec(memory_space=pltpu.VMEM)
    return pl.pallas_call(
        functools.partial(fast_counts_kernel, n_owner, n_fine, capacity, main, home),
        out_shape=(
            jax.ShapeDtypeStruct((n_owner, 1, capacity), jnp.float32),
            jax.ShapeDtypeStruct((8, LANES), jnp.int32),
        ),
        in_specs=[vmem] * 4,
        out_specs=(vmem, vmem),
        scratch_shapes=[
            pltpu.VMEM((1, total), jnp.float32),
            pltpu.VMEM((2 * total, LANES), jnp.float32),
            pltpu.VMEM((2 * total, LANES), jnp.float32),
            pltpu.VMEM((1, total), jnp.float32),
            pltpu.VMEM((n_main // 2, 256), jnp.float32),
            pltpu.VMEM((n_main // 2, 256), jnp.float32),
        ],
        compiler_params=pltpu.CompilerParams(vmem_limit_bytes=FAST_LIMIT),
    )(*arrays)


def fast_unpack_kernel(values_ref, pos_ref, out_ref):
    pos = pos_ref[...]
    lane = lax.rem(pos, LANES)
    line = lax.div(pos, LANES)
    out = jnp.zeros(pos.shape, jnp.float32)
    per = values_ref.shape[2] // LANES
    for r in range(values_ref.shape[0] * per):
        start = r % per * LANES
        table = jnp.broadcast_to(values_ref[r // per, :, start : start + LANES], pos.shape)
        found = jnp.take_along_axis(table, lane, axis=1)
        out = jnp.where(line == r, found, out)
    out_ref[...] = out


def fast_unpack(values, pos):
    vmem = pl.BlockSpec(memory_space=pltpu.VMEM)
    return pl.pallas_call(
        fast_unpack_kernel,
        out_shape=jax.ShapeDtypeStruct(pos.shape, jnp.float32),
        in_specs=[vmem, vmem],
        out_specs=vmem,
    )(values, pos)


def general(embeddings, labels, owner_map):
    n_owner = lax.axis_size("cl")
    capacity = SLOTS // n_owner
    rows, width = embeddings.shape
    packed, pos, counts = pack(embeddings, labels, owner_map, n_owner, capacity)
    counts = lax.all_gather(counts, ("cl", "grp"), tiled=True)
    mine = lax.all_to_all(
        packed.reshape(n_owner, capacity, width), "cl", split_axis=0, concat_axis=0, tiled=True
    ).reshape(SLOTS, width)
    other = lax.ppermute(mine, "grp", [(0, 1), (1, 0)])
    results = log_counts(counts, mine, other, n_owner, capacity)
    returned = lax.all_to_all(
        results.reshape(n_owner, capacity), "cl", split_axis=0, concat_axis=0, tiled=True
    )
    return unpack(returned.reshape(SLOTS), pos).reshape(rows)


def body(embeddings, labels, owner_map):
    n_owner = lax.axis_size("cl")
    capacity = SLOTS // n_owner
    rows = embeddings.shape[0]
    n_fine = owner_map.shape[0]
    main = -(-(rows // n_owner * 9 // 8) // 16) * 16
    if main >= capacity or n_fine >= LANES:
        return general(embeddings, labels, owner_map)
    home = n_owner // 4
    width = embeddings.shape[1]
    packed, extra, pos = fast_pack(embeddings, labels, owner_map, n_owner, capacity, main, home)
    rest = capacity - main
    chunks = [extra]
    chunks += [lax.ppermute(extra, "cl", [(home ^ k, home)]) for k in range(1, n_owner)]
    rest_mine = gather_rest(chunks, n_owner, rest, home)
    pairs = [(2 * home, 2 * home + 1), (2 * home + 1, 2 * home)]
    rest_other = lax.ppermute(rest_mine, ("cl", "grp"), pairs)
    mine = lax.all_to_all(
        packed.reshape(n_owner, main, width), "cl", split_axis=0, concat_axis=0, tiled=True
    ).reshape(n_owner * main, width)
    other = lax.ppermute(mine, "grp", [(0, 1), (1, 0)])
    arrays = (mine, other, rest_mine, rest_other)
    results, unfit = fast_counts(arrays, n_owner, n_fine, capacity, main, home)
    returned = lax.all_to_all(results, "cl", split_axis=0, concat_axis=0, tiled=True)
    return lax.cond(
        unfit[0, 0] == 0,
        lambda: fast_unpack(returned, pos).reshape(rows),
        lambda: general(embeddings, labels, owner_map),
    )


def solution(mesh):
    return jax.shard_map(
        body,
        mesh=mesh,
        in_specs=(P(("parts", "cl", "grp"), None), P(("parts", "cl", "grp")), P("parts")),
        out_specs=P(("parts", "cl", "grp")),
        check_vma=False,
    )
```

```python
import functools
import math

import jax
import jax.numpy as jnp
from jax import lax
from jax.experimental import pallas as pl
from jax.experimental.pallas import tpu as pltpu
from jax.sharding import PartitionSpec as P

SLOTS = 2048

temper = 0.2
neighbour_factor = 0.5
epsilon = 1e-06

LANES = 128
SCALE = math.log2(math.e) / temper
NEIGHBOUR = math.log2(neighbour_factor)
DEAD = -1e30
VMEM_LIMIT = 48 * 1024 * 1024
FAST_LIMIT = 40 * 1024 * 1024
INFO = 16


def column_of(row):
    pieces = []
    for start in range(0, row.shape[1], LANES):
        width = min(LANES, row.shape[1] - start)
        shape = (width, width)
        diagonal = lax.broadcasted_iota(jnp.int32, shape, 0) == lax.broadcasted_iota(
            jnp.int32, shape, 1
        )
        piece = jnp.broadcast_to(row[:, start : start + width], shape)
        pieces.append(jnp.sum(jnp.where(diagonal, piece, 0.0), axis=1, keepdims=True))
    return jnp.concatenate(pieces, axis=0)


def row_of(column):
    n = column.shape[0]
    diagonal = lax.broadcasted_iota(jnp.int32, (n, n), 0) == lax.broadcasted_iota(
        jnp.int32, (n, n), 1
    )
    return jnp.sum(jnp.where(diagonal, column, 0.0), axis=0, keepdims=True)


def pack_kernel(n_owner, capacity, x_ref, lab_ref, map_ref, out_ref, pos_ref, cnt_ref, unit, pos_row):
    rows = x_ref.shape[0]
    n_fine = map_ref.shape[1]
    per_owner = n_fine // n_owner
    owner_row = map_ref[...].astype(jnp.float32)
    fine_row = lax.broadcasted_iota(jnp.int32, (1, n_fine), 1).astype(jnp.float32)
    key_row = owner_row * n_fine + fine_row
    key_col = column_of(key_row)
    sorted_col = jnp.sum(jnp.where(key_row < key_col, 1.0, 0.0), axis=1, keepdims=True)
    lab = lab_ref[...].astype(jnp.float32)
    lab_row = jnp.concatenate([lab[b : b + 1, :] for b in range(lab.shape[0])], axis=1)
    fine_col = lax.broadcasted_iota(jnp.int32, (n_fine, rows), 0).astype(jnp.float32)
    fine_id = jnp.sum(jnp.where(fine_col == lab_row, sorted_col, 0.0), axis=0, keepdims=True)
    counts_col = jnp.sum(jnp.where(fine_col == fine_id, 1.0, 0.0), axis=1, keepdims=True)
    cnt_ref[...] = row_of(counts_col).astype(jnp.int32)
    coarse = jnp.floor((fine_id + 0.5) * (1.0 / per_owner))
    before = jnp.sum(
        jnp.where(fine_col < coarse * per_owner, counts_col, 0.0), axis=0, keepdims=True
    )
    index = lax.broadcasted_iota(jnp.int32, (1, rows), 1).astype(jnp.float32)
    row_key = fine_id * rows + index
    rank = jnp.zeros((1, rows), jnp.float32)
    for start in range(0, rows, LANES):
        other = column_of(row_key[:, start : start + LANES])
        rank = rank + jnp.sum(jnp.where(other < row_key, 1.0, 0.0), axis=0, keepdims=True)
    pos = (coarse * capacity + rank - before).astype(jnp.int32)
    pos_row[...] = pos
    pos_ref[...] = jnp.concatenate(
        [pos[:, start : start + LANES] for start in range(0, rows, LANES)], axis=0
    )
    x = x_ref[...].astype(jnp.float32)
    squares = jnp.sum(x * x, axis=1, keepdims=True)
    unit[...] = (x * lax.rsqrt(squares + epsilon)).astype(jnp.bfloat16)

    step = 256

    @pl.loop(0, out_ref.shape[0] // step)
    def _(block):
        slot = lax.broadcasted_iota(jnp.int32, (step, rows), 0) + block * step
        chosen = jnp.where(slot == pos_row[...], 1.0, 0.0).astype(jnp.bfloat16)
        packed = jnp.dot(chosen, unit[...], preferred_element_type=jnp.float32)
        out_ref[pl.ds(pl.multiple_of(block * step, step), step), :] = packed.astype(jnp.bfloat16)


def pack(embeddings, labels, owner_map, n_owner, capacity):
    rows, width = embeddings.shape
    n_fine = owner_map.shape[0]
    total = n_owner * capacity
    vmem = pl.BlockSpec(memory_space=pltpu.VMEM)
    return pl.pallas_call(
        functools.partial(pack_kernel, n_owner, capacity),
        out_shape=(
            jax.ShapeDtypeStruct((total, width), jnp.bfloat16),
            jax.ShapeDtypeStruct((rows // LANES, LANES), jnp.int32),
            jax.ShapeDtypeStruct((1, n_fine), jnp.int32),
        ),
        in_specs=[vmem] * 3,
        out_specs=(vmem, vmem, vmem),
        scratch_shapes=[pltpu.VMEM((rows, width), jnp.bfloat16), pltpu.VMEM((1, rows), jnp.int32)],
        compiler_params=pltpu.CompilerParams(vmem_limit_bytes=VMEM_LIMIT),
    )(embeddings, labels.reshape(rows // LANES, LANES), owner_map.reshape(1, n_fine))


def counts_kernel(n_owner, capacity, cnt_ref, mine_ref, other_ref, out_ref, lab_lane, lab_sub, bias):
    total = mine_ref.shape[0]
    per_owner = cnt_ref.shape[1] // n_owner
    me = lax.axis_index("cl")
    grp = lax.axis_index("grp")
    n_grp = lax.axis_size("grp")
    for member in range(2):
        for source in range(n_owner):
            line = source * n_grp + lax.rem(grp + member, n_grp)
            edges = []
            edge = jnp.int32(0)
            for f in range(per_owner):
                edge = edge + cnt_ref[line, me * per_owner + f]
                edges.append(edge)
            down = lax.broadcasted_iota(jnp.int32, (capacity, LANES), 0)
            label = jnp.zeros((capacity, LANES), jnp.int32)
            for edge in edges:
                label = label + jnp.where(down >= edge, 1, 0)
            start = (member * n_owner + source) * capacity
            lab_sub[start : start + capacity, :] = label
            bias[start : start + capacity, :] = jnp.where(
                label < per_owner, NEIGHBOUR - SCALE, DEAD
            )
            if member == 0:
                across = lax.broadcasted_iota(jnp.int32, (1, capacity), 1)
                label = jnp.zeros((1, capacity), jnp.int32)
                for edge in edges:
                    label = label + jnp.where(across >= edge, 1, 0)
                lab_lane[:, source * capacity : (source + 1) * capacity] = jnp.where(
                    label < per_owner, label, -1
                )
    wide, deep = min(512, total), min(256, total)

    @pl.loop(0, total // wide)
    def _(block):
        columns = pl.ds(pl.multiple_of(block * wide, wide), wide)
        rows_i = mine_ref[columns, :]
        label_i = lab_lane[:, columns]

        def add(ref, offset):
            def step(j, acc):
                start = pl.multiple_of(j * deep, deep)
                scores = lax.dot_general(
                    ref[pl.ds(start, deep), :],
                    rows_i,
                    (((1,), (1,)), ((), ())),
                    preferred_element_type=jnp.float32,
                )
                place = pl.ds(pl.multiple_of(start + offset, deep), deep)
                label_j = lab_sub[place, :]
                bias_j = bias[place, :]
                repeat = wide // LANES
                label_j = jnp.concatenate([label_j] * repeat, axis=1)
                bias_j = jnp.concatenate([bias_j] * repeat, axis=1)
                shift = jnp.where(label_j == label_i, -SCALE, bias_j)
                terms = jnp.exp2(scores * SCALE + shift)
                return acc + jnp.sum(terms.reshape(deep // 8, 8, wide), axis=0)

            return step

        acc = jnp.zeros((8, wide), jnp.float32)
        acc = lax.fori_loop(0, total // deep, add(mine_ref, 0), acc, unroll=2)
        acc = lax.fori_loop(0, total // deep, add(other_ref, total), acc, unroll=2)
        totals = jnp.sum(acc, axis=0, keepdims=True)
        out_ref[:, columns] = jnp.log(jnp.where(label_i >= 0, totals, 1.0))


def log_counts(counts, mine, other, n_owner, capacity):
    total = mine.shape[0]
    vmem = pl.BlockSpec(memory_space=pltpu.VMEM)
    return pl.pallas_call(
        functools.partial(counts_kernel, n_owner, capacity),
        out_shape=jax.ShapeDtypeStruct((1, total), jnp.float32),
        in_specs=[pl.BlockSpec(memory_space=pltpu.SMEM), vmem, vmem],
        out_specs=vmem,
        scratch_shapes=[
            pltpu.VMEM((1, total), jnp.int32),
            pltpu.VMEM((2 * total, LANES), jnp.int32),
            pltpu.VMEM((2 * total, LANES), jnp.float32),
        ],
        compiler_params=pltpu.CompilerParams(vmem_limit_bytes=VMEM_LIMIT),
    )(counts, mine, other)


def unpack_kernel(values_ref, pos_ref, out_ref):
    pos = pos_ref[...]
    lane = lax.rem(pos, LANES)
    line = lax.div(pos, LANES)
    out = jnp.zeros(pos.shape, jnp.float32)
    for r in range(values_ref.shape[0]):
        table = jnp.broadcast_to(values_ref[r : r + 1, :], pos.shape)
        found = jnp.take_along_axis(table, lane, axis=1)
        out = jnp.where(line == r, found, out)
    out_ref[...] = out


def unpack(values, pos):
    vmem = pl.BlockSpec(memory_space=pltpu.VMEM)
    return pl.pallas_call(
        unpack_kernel,
        out_shape=jax.ShapeDtypeStruct(pos.shape, jnp.float32),
        in_specs=[vmem, vmem],
        out_specs=vmem,
    )(values.reshape(-1, LANES), pos)


def pieces(start, count, parts):
    return [(start + i * (count // parts), count // parts) for i in range(parts)]


def swapped(x, first, second):
    return jnp.where(x == first, second, jnp.where(x == second, first, x))


def place_kernel(n_owner, capacity, main, home, x_hbm, lab_hbm, map_hbm, *refs):
    unit, slot_ref, info_ref, extra_ref, pos_ref, x_ref, lab_ref, map_ref, sems = refs
    copies = [
        pltpu.make_async_copy(src, dst, sems.at[i])
        for i, (src, dst) in enumerate(((x_hbm, x_ref), (lab_hbm, lab_ref), (map_hbm, map_ref)))
    ]
    for copy in copies:
        copy.start()
    rows = x_ref.shape[0]
    n_fine = map_ref.shape[1]
    per_owner = n_fine // n_owner
    rest = capacity - main
    copies[1].wait()
    copies[2].wait()
    owner_row = map_ref[...].astype(jnp.float32)
    fine_row = lax.broadcasted_iota(jnp.int32, (1, n_fine), 1).astype(jnp.float32)
    key_row = owner_row * n_fine + fine_row
    key_col = column_of(key_row)
    sorted_col = jnp.sum(jnp.where(key_row < key_col, 1.0, 0.0), axis=1, keepdims=True)
    lab = lab_ref[...].astype(jnp.float32)
    lab_row = jnp.concatenate([lab[b : b + 1, :] for b in range(lab.shape[0])], axis=1)
    fine_col = lax.broadcasted_iota(jnp.int32, (n_fine, rows), 0).astype(jnp.float32)
    fine_id = jnp.sum(jnp.where(fine_col == lab_row, sorted_col, 0.0), axis=0, keepdims=True)
    counts_col = jnp.sum(jnp.where(fine_col == fine_id, 1.0, 0.0), axis=1, keepdims=True)
    coarse = jnp.floor((fine_id + 0.5) * (1.0 / per_owner))
    first = coarse * per_owner
    before = jnp.sum(jnp.where(fine_col < first, counts_col, 0.0), axis=0, keepdims=True)
    upto = jnp.sum(jnp.where(fine_col < first + per_owner, counts_col, 0.0), axis=0, keepdims=True)
    full = jnp.min(
        jnp.where(upto - before == capacity, coarse, float(n_owner)), axis=1, keepdims=True
    )
    line = lax.broadcasted_iota(jnp.int32, (n_fine, LANES), 0)
    lane = lax.broadcasted_iota(jnp.int32, (n_fine, LANES), 1)
    inside = (line <= lane) & (lax.div(line, per_owner) == lax.div(lane, per_owner))
    running = jnp.sum(jnp.where(inside, counts_col, 0.0), axis=0, keepdims=True)
    info = jnp.where(lane[:1] < n_fine, running, full)
    info_ref[...] = info
    index = lax.broadcasted_iota(jnp.int32, (1, rows), 1).astype(jnp.float32)
    row_key = fine_id * rows + index
    rank = jnp.zeros((1, rows), jnp.float32)
    for start in range(0, rows, LANES):
        other = column_of(row_key[:, start : start + LANES])
        rank = rank + jnp.sum(jnp.where(other < row_key, 1.0, 0.0), axis=0, keepdims=True)
    rank = (rank - before).astype(jnp.int32)
    place = swapped(coarse.astype(jnp.int32), full.astype(jnp.int32), home)
    table = place * capacity + rank
    pos_ref[...] = jnp.concatenate(
        [table[:, start : start + LANES] for start in range(0, rows, LANES)], axis=0
    )
    later = jnp.where(place == home, n_owner * main + rank - main, -1)
    fits = rank < jnp.where(place == home, main, main - 1)
    slot = jnp.where(fits, place * main + rank, later)
    slot_ref[...] = slot
    copies[0].wait()
    x = x_ref[...].astype(jnp.float32)
    squares = jnp.sum(x * x, axis=1, keepdims=True)
    unit[...] = (x * lax.rsqrt(squares + epsilon)).astype(jnp.bfloat16)
    extra_ref[:rest, :] = chosen_rows(unit, slot, n_owner * main, rest)
    extra_ref[rest:, :] = jnp.zeros((INFO, extra_ref.shape[1]), jnp.bfloat16)
    extra_ref[rest:, :LANES] = jnp.broadcast_to(info, (INFO, LANES)).astype(jnp.bfloat16)


def chosen_rows(unit, slot, start, count):
    here = lax.broadcasted_iota(jnp.int32, (count, unit.shape[0]), 0) + start
    chosen = jnp.where(here == slot, 1.0, 0.0).astype(jnp.bfloat16)
    return jnp.dot(chosen, unit[...], preferred_element_type=jnp.float32).astype(jnp.bfloat16)


def main_kernel(n_owner, main, home, unit, slot_ref, info_ref, main_ref):
    count = n_owner * main // 4
    for start in range(0, n_owner * main, count):
        main_ref[start : start + count, :] = chosen_rows(unit, slot_ref[...], start, count)
    for owner in range(n_owner):
        if owner != home:
            tail = slice((owner + 1) * main - INFO, (owner + 1) * main)
            old = main_ref[tail, :LANES].astype(jnp.float32)
            down = lax.broadcasted_iota(jnp.int32, old.shape, 0)
            new = jnp.where(down == INFO - 1, info_ref[...], old)
            main_ref[tail, :LANES] = new.astype(jnp.bfloat16)


def vmem_specs(count):
    return (pl.BlockSpec(memory_space=pltpu.VMEM),) * count


def place_rows(embeddings, labels, owner_map, n_owner, capacity, main, home):
    rows, width = embeddings.shape
    n_fine = owner_map.shape[0]
    lab_shape = (rows // LANES, LANES)
    return pl.pallas_call(
        functools.partial(place_kernel, n_owner, capacity, main, home),
        out_shape=(
            jax.ShapeDtypeStruct((rows, width), jnp.bfloat16),
            jax.ShapeDtypeStruct((1, rows), jnp.int32),
            jax.ShapeDtypeStruct((1, LANES), jnp.float32),
            jax.ShapeDtypeStruct((capacity - main + INFO, width), jnp.bfloat16),
            jax.ShapeDtypeStruct(lab_shape, jnp.int32),
        ),
        in_specs=[pl.BlockSpec(memory_space=pl.ANY)] * 3,
        out_specs=vmem_specs(5),
        scratch_shapes=[
            pltpu.VMEM((rows, width), jnp.bfloat16),
            pltpu.VMEM(lab_shape, jnp.int32),
            pltpu.VMEM((1, n_fine), jnp.int32),
            pltpu.SemaphoreType.DMA((3,)),
        ],
        compiler_params=pltpu.CompilerParams(vmem_limit_bytes=FAST_LIMIT),
    )(embeddings, labels.reshape(lab_shape), owner_map.reshape(1, n_fine))


def pack_main(unit, slot, info, n_owner, main, home):
    return pl.pallas_call(
        functools.partial(main_kernel, n_owner, main, home),
        out_shape=jax.ShapeDtypeStruct((n_owner * main, unit.shape[1]), jnp.bfloat16),
        in_specs=list(vmem_specs(3)),
        out_specs=vmem_specs(1)[0],
        compiler_params=pltpu.CompilerParams(vmem_limit_bytes=FAST_LIMIT),
        cost_estimate=pl.CostEstimate(
            flops=2 * n_owner * main * unit.shape[0] * unit.shape[1],
            bytes_accessed=4 * unit.shape[0] * unit.shape[1],
            transcendentals=0,
        ),
    )(unit, slot, info)


def gather_kernel(rest, plane, *refs):
    chunks, out = refs[:-1], refs[-1]

    @pl.when(lax.div(lax.axis_index("cl"), 2) == plane)
    def _():
        for z, chunk in enumerate(chunks):
            out[z * rest : (z + 1) * rest, :] = chunk[:rest, :]
            start = len(chunks) * rest + z * INFO
            out[start : start + INFO, :] = chunk[rest:, :]


def gather_rest(chunks, rest, plane):
    shape = (len(chunks) * (rest + INFO), chunks[0].shape[1])
    return pl.pallas_call(
        functools.partial(gather_kernel, rest, plane),
        out_shape=jax.ShapeDtypeStruct(shape, jnp.bfloat16),
        in_specs=list(vmem_specs(len(chunks))),
        out_specs=vmem_specs(1)[0],
        cost_estimate=pl.CostEstimate(
            flops=0, bytes_accessed=4 * shape[0] * shape[1], transcendentals=0
        ),
    )(*chunks)


class Layout:
    def __init__(self, n_owner, n_fine, capacity, main, home):
        self.n_owner, self.n_fine, self.capacity = n_owner, n_fine, capacity
        self.main, self.home = main, home
        self.rest = capacity - main
        self.per_owner = n_fine // n_owner
        self.planes = n_owner // 2
        self.n_main = n_owner * main
        self.n_rest = self.planes * self.rest
        self.rest_lines = self.planes * (self.rest + INFO)
        self.total = self.n_main + 2 * self.rest_lines

    def rest_at(self, y):
        return self.n_main + y * self.rest_lines


def info_line(lay, is_home, main_ref, rest_refs, source):
    in_main = main_ref[(source + 1) * lay.main - INFO : (source + 1) * lay.main, :LANES]
    z, y = source // 2, source % 2
    start = lay.n_rest + z * INFO
    in_rest = rest_refs[y][start : start + INFO, :LANES]
    in_main = in_main.astype(jnp.float32)[INFO - 1 :]
    return jnp.where(is_home, in_rest.astype(jnp.float32)[INFO - 1 :], in_main)


def write_labels(lay, infos, cluster, is_home, lab_sub, bias):
    lane = lax.broadcasted_iota(jnp.int32, (1, LANES), 1)
    is_edge = lax.div(lane, lay.per_owner) == cluster
    for source, info in enumerate(infos):
        edges = jnp.where(is_edge, info, 2.0 * lay.capacity)

        def write(start, first, count, edges=edges):
            slot = lax.broadcasted_iota(jnp.int32, (count, LANES), 0) + first
            label = jnp.where(slot.astype(jnp.float32) >= edges, 1.0, 0.0)
            label = jnp.broadcast_to(jnp.sum(label, axis=1, keepdims=True), (count, LANES))
            lab_sub[start : start + count, :] = label
            bias[start : start + count, :] = jnp.where(
                label < lay.per_owner, NEIGHBOUR - SCALE, DEAD
            )

        write(source * lay.main, 0, lay.main)

        @pl.when(is_home)
        def _(source=source, write=write):
            start = lay.rest_at(source % 2) + source // 2 * lay.rest
            write(start, lay.main, lay.rest)

    @pl.when(is_home)
    def _():
        for y in range(2):
            start = lay.rest_at(y) + lay.n_rest
            lab_sub[start : start + lay.rest_lines - lay.n_rest, :] = jnp.full(
                (lay.rest_lines - lay.n_rest, LANES), float(lay.per_owner), jnp.float32
            )


def hot_of(lay, info):
    lane = lax.broadcasted_iota(jnp.int32, (1, LANES), 1)
    hot = jnp.max(jnp.where(lane == lay.n_fine, info, 0.0), axis=1, keepdims=True)
    return hot.astype(jnp.int32)


def pair_sums(rows_i, label_i, tiles, buffers):
    wide = rows_i.shape[0]
    repeat = wide // LANES
    dead_i = jnp.where(label_i >= 0, 0.0, DEAD)
    step = 32

    def scores_to(buffer, tile):
        ref, start, deep = tile[:3]
        buffer[:deep, :wide] = lax.dot_general(
            ref[start : start + deep, :],
            rows_i,
            (((1,), (1,)), ((), ())),
            preferred_element_type=jnp.float32,
        )

    acc = jnp.zeros((8, wide), jnp.float32)
    here, ahead = buffers
    scores_to(here, tiles[0])
    for i, (_, _, deep, lab_sub, bias, place, back) in enumerate(tiles):
        if i + 1 < len(tiles):
            scores_to(ahead, tiles[i + 1])
        for c in range(0, deep, step):
            part = slice(place + c, place + c + step)
            label_j = jnp.concatenate([lab_sub[part, :]] * repeat, axis=1)
            bias_j = jnp.concatenate([bias[part, :]] * repeat, axis=1)
            if back is not None:
                bias_j = bias_j + dead_i
            shift = jnp.where(label_j == label_i, -SCALE, bias_j)
            terms = jnp.exp2(here[c : c + step, :wide] * SCALE + shift)
            acc = acc + jnp.sum(terms.reshape(step // 8, 8, wide), axis=0)
            if back is not None:
                across = terms[:, :LANES]
                for r in range(1, repeat):
                    across = across + terms[:, r * LANES : (r + 1) * LANES]
                back[part, :] += across
        here, ahead = ahead, here
    return jnp.sum(acc, axis=0, keepdims=True)


def each_block(count, run):
    wide = 256
    full = count // wide

    @pl.loop(0, full)
    def _(i):
        run(pl.multiple_of(i * wide, wide), wide)

    if count % wide:
        run(full * wide, count % wide)


def row_sums(back, start, count):
    ones = jnp.ones((8, LANES), jnp.float32)
    sums = lax.dot_general(
        ones,
        back[start : start + count, :],
        (((1,), (1,)), ((), ())),
        precision=lax.Precision.HIGHEST,
        preferred_element_type=jnp.float32,
    )
    return sums[:1]


def inner_kernel(lay, mine, rest_a, rest_b, sums, lab_lane, lab_sub, bias, back, buf_a, buf_b):
    me = lax.axis_index("cl")
    is_home = me == lay.home
    rests = (rest_a, rest_b)
    infos = [info_line(lay, is_home, mine, rests, s) for s in range(lay.n_owner)]
    cluster = swapped(me, hot_of(lay, infos[0]), lay.home)
    write_labels(lay, infos, cluster, is_home, lab_sub, bias)

    def turn(start, count):
        for i in range(start, start + count, LANES):
            block = jnp.transpose(lab_sub[i : i + LANES, :])[:1]
            lab_lane[:, i : i + LANES] = jnp.where(block < lay.per_owner, block, -1.0)

    turn(0, lay.n_main)
    buffers = (buf_a, buf_b)
    own = [
        (mine, s, d, lab_sub, bias, s, None) for s, d in pieces(0, lay.n_main, 2)
    ]

    def main_block(start, wide):
        place = pl.ds(start, wide)
        sums[:, place] = pair_sums(mine[place, :], lab_lane[:, place], own, buffers)

    each_block(lay.n_main, main_block)

    @pl.when(is_home)
    def _():
        turn(lay.n_main, 2 * lay.rest_lines)
        n_back = 2 * lay.rest_lines
        back[lay.n_main : lay.n_main + n_back, :] = jnp.zeros((n_back, LANES), jnp.float32)
        seconds = [(rests[y], 0, lay.n_rest, lab_sub, bias, lay.rest_at(y), back) for y in (0, 1)]

        def more(start, wide):
            place = pl.ds(start, wide)
            sums[:, place] += pair_sums(mine[place, :], lab_lane[:, place], seconds, buffers)

        each_block(lay.n_main, more)
        among = [tile[:6] + (None,) for tile in seconds]
        for y in range(2):

            def rest_block(start, wide, y=y):
                place = pl.ds(start + lay.rest_at(y), wide)
                rows_i = rests[y][pl.ds(start, wide), :]
                sums[:, place] = pair_sums(rows_i, lab_lane[:, place], among, buffers)

            each_block(lay.rest_lines, rest_block)
        place = slice(lay.n_main, lay.n_main + n_back)
        sums[:, place] += row_sums(back, lay.n_main, n_back)


def cross_kernel(lay, *refs):
    mine, rest_a, rest_b, other, other_a, other_b, lab_lane, sums = refs[:8]
    out, out_other, unfit_ref, lab_sub, bias, back, buf_a, buf_b = refs[8:]
    me = lax.axis_index("cl")
    grp = lax.axis_index("grp")
    is_home = me == lay.home
    rests, others = (rest_a, rest_b), (other_a, other_b)
    infos = [info_line(lay, is_home, other, others, s) for s in range(lay.n_owner)]
    own = [info_line(lay, is_home, mine, rests, s) for s in range(lay.n_owner)]
    hot = hot_of(lay, own[0])
    lane = lax.broadcasted_iota(jnp.int32, (1, LANES), 1)
    last = (lane < lay.n_fine) & (lax.rem(lane, lay.per_owner) == lay.per_owner - 1)
    last = last & (lax.div(lane, lay.per_owner) != hot)
    unfit = jnp.zeros((1, LANES), jnp.float32)
    for info in infos + own:
        wrong = last & (info >= lay.main)
        differs = (info != hot.astype(jnp.float32)) | (info >= lay.n_owner)
        wrong = wrong | ((lane == lay.n_fine) & differs)
        unfit = unfit + jnp.where(wrong, 1.0, 0.0)
    unfit_ref[...] = jnp.broadcast_to(
        jnp.max(unfit, axis=1, keepdims=True), unfit_ref.shape
    ).astype(jnp.int32)
    write_labels(lay, infos, swapped(me, hot, lay.home), is_home, lab_sub, bias)
    back[: lay.n_main, :] = jnp.zeros((lay.n_main, LANES), jnp.float32)
    buffers = (buf_a, buf_b)
    out[...] = sums[...]
    half = 512

    def main_tiles(low):
        start, count = (0, half) if low else (half, lay.n_main - half)
        return [(other, s, d, lab_sub, bias, s, back) for s, d in pieces(start, count, 2)]

    def main_blocks(first, count, low):
        def run(start, wide):
            place = pl.ds(first + start, wide)
            out[:, place] += pair_sums(
                mine[place, :], lab_lane[:, place], main_tiles(low), buffers
            )

        each_block(count, run)

    @pl.when(grp == 0)
    def _():
        main_blocks(0, half, True)
        main_blocks(half, lay.n_main - half, False)

    @pl.when(grp == 1)
    def _():
        main_blocks(0, half, False)
        main_blocks(half, lay.n_main - half, True)

    @pl.when(is_home)
    def _():
        back[lay.n_main :, :] = jnp.zeros((2 * lay.rest_lines, LANES), jnp.float32)
        seconds = [(others[y], 0, lay.n_rest, lab_sub, bias, lay.rest_at(y), back) for y in (0, 1)]

        def more(start, wide):
            place = pl.ds(start, wide)
            out[:, place] += pair_sums(mine[place, :], lab_lane[:, place], seconds, buffers)

        each_block(lay.n_main, more)
        for y in range(2):
            for g in range(2):

                @pl.when(grp == g)
                def _(y=y, g=g):
                    ref, _, _, _, _, place_j, _ = seconds[y ^ g]
                    tiles = [
                        (ref, s, d, lab_sub, bias, place_j + s, back)
                        for s, d in pieces(0, lay.n_rest, 2)
                    ]

                    def run(start, wide):
                        place = pl.ds(start + lay.rest_at(y), wide)
                        rows_i = rests[y][pl.ds(start, wide), :]
                        out[:, place] += pair_sums(rows_i, lab_lane[:, place], tiles, buffers)

                    each_block(lay.rest_lines, run)

        out_other[:, lay.n_main :] = row_sums(back, lay.n_main, 2 * lay.rest_lines)

    out_other[:, : lay.n_main] = row_sums(back, 0, lay.n_main)


def join_kernel(lay, sums, more, out_ref):
    values = jnp.log(sums[...] + more[...])
    for source in range(lay.n_owner):
        out_ref[source, :, : lay.main] = values[:, source * lay.main : (source + 1) * lay.main]
        start = lay.rest_at(source % 2) + source // 2 * lay.rest
        out_ref[source, :, lay.main :] = values[:, start : start + lay.rest]


def inner_sums(lay, mine, rests):
    row = jax.ShapeDtypeStruct((1, lay.total), jnp.float32)
    side = pltpu.VMEM((lay.total, LANES), jnp.float32)
    buffer = pltpu.VMEM((lay.n_main // 2, 256), jnp.float32)
    return pl.pallas_call(
        functools.partial(inner_kernel, lay),
        out_shape=(row, row),
        in_specs=list(vmem_specs(3)),
        out_specs=vmem_specs(2),
        scratch_shapes=[side, side, side, buffer, buffer],
        compiler_params=pltpu.CompilerParams(vmem_limit_bytes=FAST_LIMIT),
        cost_estimate=pair_cost(lay, mine),
    )(mine, *rests)


def cross_sums(lay, mine, rests, other, others, lab_lane, sums):
    row = jax.ShapeDtypeStruct((1, lay.total), jnp.float32)
    side = pltpu.VMEM((lay.total, LANES), jnp.float32)
    buffer = pltpu.VMEM((lay.n_main // 2, 256), jnp.float32)
    return pl.pallas_call(
        functools.partial(cross_kernel, lay),
        out_shape=(row, row, jax.ShapeDtypeStruct((8, LANES), jnp.int32)),
        in_specs=list(vmem_specs(8)),
        out_specs=vmem_specs(3),
        scratch_shapes=[side, side, side, buffer, buffer],
        compiler_params=pltpu.CompilerParams(vmem_limit_bytes=FAST_LIMIT),
        cost_estimate=pair_cost(lay, mine),
    )(mine, *rests, other, *others, lab_lane, sums)


def pair_cost(lay, rows):
    pairs = lay.n_main * lay.n_main
    return pl.CostEstimate(
        flops=2 * pairs * rows.shape[1],
        bytes_accessed=4 * lay.n_main * rows.shape[1],
        transcendentals=pairs,
    )


def join(lay, sums, more):
    return pl.pallas_call(
        functools.partial(join_kernel, lay),
        out_shape=jax.ShapeDtypeStruct((lay.n_owner, 1, lay.capacity), jnp.float32),
        in_specs=list(vmem_specs(2)),
        out_specs=vmem_specs(1)[0],
    )(sums, more)


def fast_unpack_kernel(values_ref, pos_ref, out_ref):
    pos = pos_ref[...]
    lane = lax.rem(pos, LANES)
    line = lax.div(pos, LANES)
    out = jnp.zeros(pos.shape, jnp.float32)
    per = values_ref.shape[2] // LANES
    for r in range(values_ref.shape[0] * per):
        start = r % per * LANES
        table = jnp.broadcast_to(values_ref[r // per, :, start : start + LANES], pos.shape)
        found = jnp.take_along_axis(table, lane, axis=1)
        out = jnp.where(line == r, found, out)
    out_ref[...] = out


def fast_unpack(values, pos):
    vmem = pl.BlockSpec(memory_space=pltpu.VMEM)
    return pl.pallas_call(
        fast_unpack_kernel,
        out_shape=jax.ShapeDtypeStruct(pos.shape, jnp.float32),
        in_specs=[vmem, vmem],
        out_specs=vmem,
    )(values, pos)


def general(embeddings, labels, owner_map):
    n_owner = lax.axis_size("cl")
    capacity = SLOTS // n_owner
    rows, width = embeddings.shape
    packed, pos, counts = pack(embeddings, labels, owner_map, n_owner, capacity)
    counts = lax.all_gather(counts, ("cl", "grp"), tiled=True)
    mine = lax.all_to_all(
        packed.reshape(n_owner, capacity, width), "cl", split_axis=0, concat_axis=0, tiled=True
    ).reshape(SLOTS, width)
    other = lax.ppermute(mine, "grp", [(0, 1), (1, 0)])
    results = log_counts(counts, mine, other, n_owner, capacity)
    returned = lax.all_to_all(
        results.reshape(n_owner, capacity), "cl", split_axis=0, concat_axis=0, tiled=True
    )
    return unpack(returned.reshape(SLOTS), pos).reshape(rows)


def body(embeddings, labels, owner_map):
    n_owner = lax.axis_size("cl")
    capacity = SLOTS // n_owner
    rows, width = embeddings.shape
    n_fine = owner_map.shape[0]
    main = -(-(rows // n_owner * 9 // 8) // 16) * 16
    if main >= capacity or n_fine >= LANES:
        return general(embeddings, labels, owner_map)
    planes = n_owner // 2
    plane = planes // 2 - 1
    home = 2 * plane
    lay = Layout(n_owner, n_fine, capacity, main, home)
    unit, slot, info, extra, pos = place_rows(
        embeddings, labels, owner_map, n_owner, capacity, main, home
    )
    chunks = [
        extra
        if z == plane
        else lax.ppermute(extra, "cl", [(2 * z + y, 2 * plane + y) for y in range(2)])
        for z in range(planes)
    ]
    rest_a = gather_rest(chunks, lay.rest, plane)
    rest_b = lax.ppermute(rest_a, "cl", [(home + 1, home)])
    rests = (rest_a, rest_b)
    swap = [(2 * home, 2 * home + 1), (2 * home + 1, 2 * home)]
    others = tuple(lax.ppermute(x, ("cl", "grp"), swap) for x in rests)
    packed = pack_main(unit, slot, info, n_owner, main, home)
    mine = lax.all_to_all(
        packed.reshape(n_owner, main, width), "cl", split_axis=0, concat_axis=0, tiled=True
    ).reshape(n_owner * main, width)
    other = lax.ppermute(mine, "grp", [(0, 1), (1, 0)])
    sums, lab_lane = inner_sums(lay, mine, rests)
    sums, for_other, unfit = cross_sums(lay, mine, rests, other, others, lab_lane, sums)
    results = join(lay, sums, lax.ppermute(for_other, "grp", [(0, 1), (1, 0)]))
    returned = lax.all_to_all(results, "cl", split_axis=0, concat_axis=0, tiled=True)
    return lax.cond(
        unfit[0, 0] == 0,
        lambda: fast_unpack(returned, pos).reshape(rows),
        lambda: general(embeddings, labels, owner_map),
    )


def solution(mesh):
    return jax.shard_map(
        body,
        mesh=mesh,
        in_specs=(P(("parts", "cl", "grp"), None), P(("parts", "cl", "grp")), P("parts")),
        out_specs=P(("parts", "cl", "grp")),
        check_vma=False,
    )
```

```python
import functools
import math

import jax
import jax.numpy as jnp
from jax import lax
from jax.experimental import pallas as pl
from jax.experimental.pallas import tpu as pltpu
from jax.sharding import PartitionSpec as P

SLOTS = 2048

temper = 0.2
neighbour_factor = 0.5
epsilon = 1e-06

LANES = 128
SCALE = math.log2(math.e) / temper
NEIGHBOUR = math.log2(neighbour_factor)
DEAD = -1e30
VMEM_LIMIT = 48 * 1024 * 1024
FAST_LIMIT = 40 * 1024 * 1024
INFO = 16


def column_of(row):
    pieces = []
    for start in range(0, row.shape[1], LANES):
        width = min(LANES, row.shape[1] - start)
        shape = (width, width)
        diagonal = lax.broadcasted_iota(jnp.int32, shape, 0) == lax.broadcasted_iota(
            jnp.int32, shape, 1
        )
        piece = jnp.broadcast_to(row[:, start : start + width], shape)
        pieces.append(jnp.sum(jnp.where(diagonal, piece, 0.0), axis=1, keepdims=True))
    return jnp.concatenate(pieces, axis=0)


def row_of(column):
    n = column.shape[0]
    diagonal = lax.broadcasted_iota(jnp.int32, (n, n), 0) == lax.broadcasted_iota(
        jnp.int32, (n, n), 1
    )
    return jnp.sum(jnp.where(diagonal, column, 0.0), axis=0, keepdims=True)


def pack_kernel(n_owner, capacity, x_ref, lab_ref, map_ref, out_ref, pos_ref, cnt_ref, unit, pos_row):
    rows = x_ref.shape[0]
    n_fine = map_ref.shape[1]
    per_owner = n_fine // n_owner
    owner_row = map_ref[...].astype(jnp.float32)
    fine_row = lax.broadcasted_iota(jnp.int32, (1, n_fine), 1).astype(jnp.float32)
    key_row = owner_row * n_fine + fine_row
    key_col = column_of(key_row)
    sorted_col = jnp.sum(jnp.where(key_row < key_col, 1.0, 0.0), axis=1, keepdims=True)
    lab = lab_ref[...].astype(jnp.float32)
    lab_row = jnp.concatenate([lab[b : b + 1, :] for b in range(lab.shape[0])], axis=1)
    fine_col = lax.broadcasted_iota(jnp.int32, (n_fine, rows), 0).astype(jnp.float32)
    fine_id = jnp.sum(jnp.where(fine_col == lab_row, sorted_col, 0.0), axis=0, keepdims=True)
    counts_col = jnp.sum(jnp.where(fine_col == fine_id, 1.0, 0.0), axis=1, keepdims=True)
    cnt_ref[...] = row_of(counts_col).astype(jnp.int32)
    coarse = jnp.floor((fine_id + 0.5) * (1.0 / per_owner))
    before = jnp.sum(
        jnp.where(fine_col < coarse * per_owner, counts_col, 0.0), axis=0, keepdims=True
    )
    index = lax.broadcasted_iota(jnp.int32, (1, rows), 1).astype(jnp.float32)
    row_key = fine_id * rows + index
    rank = jnp.zeros((1, rows), jnp.float32)
    for start in range(0, rows, LANES):
        other = column_of(row_key[:, start : start + LANES])
        rank = rank + jnp.sum(jnp.where(other < row_key, 1.0, 0.0), axis=0, keepdims=True)
    pos = (coarse * capacity + rank - before).astype(jnp.int32)
    pos_row[...] = pos
    pos_ref[...] = jnp.concatenate(
        [pos[:, start : start + LANES] for start in range(0, rows, LANES)], axis=0
    )
    x = x_ref[...].astype(jnp.float32)
    squares = jnp.sum(x * x, axis=1, keepdims=True)
    unit[...] = (x * lax.rsqrt(squares + epsilon)).astype(jnp.bfloat16)

    step = 256

    @pl.loop(0, out_ref.shape[0] // step)
    def _(block):
        slot = lax.broadcasted_iota(jnp.int32, (step, rows), 0) + block * step
        chosen = jnp.where(slot == pos_row[...], 1.0, 0.0).astype(jnp.bfloat16)
        packed = jnp.dot(chosen, unit[...], preferred_element_type=jnp.float32)
        out_ref[pl.ds(pl.multiple_of(block * step, step), step), :] = packed.astype(jnp.bfloat16)


def pack(embeddings, labels, owner_map, n_owner, capacity):
    rows, width = embeddings.shape
    n_fine = owner_map.shape[0]
    total = n_owner * capacity
    vmem = pl.BlockSpec(memory_space=pltpu.VMEM)
    return pl.pallas_call(
        functools.partial(pack_kernel, n_owner, capacity),
        out_shape=(
            jax.ShapeDtypeStruct((total, width), jnp.bfloat16),
            jax.ShapeDtypeStruct((rows // LANES, LANES), jnp.int32),
            jax.ShapeDtypeStruct((1, n_fine), jnp.int32),
        ),
        in_specs=[vmem] * 3,
        out_specs=(vmem, vmem, vmem),
        scratch_shapes=[pltpu.VMEM((rows, width), jnp.bfloat16), pltpu.VMEM((1, rows), jnp.int32)],
        compiler_params=pltpu.CompilerParams(vmem_limit_bytes=VMEM_LIMIT),
    )(embeddings, labels.reshape(rows // LANES, LANES), owner_map.reshape(1, n_fine))


def counts_kernel(n_owner, capacity, cnt_ref, mine_ref, other_ref, out_ref, lab_lane, lab_sub, bias):
    total = mine_ref.shape[0]
    per_owner = cnt_ref.shape[1] // n_owner
    me = lax.axis_index("cl")
    grp = lax.axis_index("grp")
    n_grp = lax.axis_size("grp")
    for member in range(2):
        for source in range(n_owner):
            line = source * n_grp + lax.rem(grp + member, n_grp)
            edges = []
            edge = jnp.int32(0)
            for f in range(per_owner):
                edge = edge + cnt_ref[line, me * per_owner + f]
                edges.append(edge)
            down = lax.broadcasted_iota(jnp.int32, (capacity, LANES), 0)
            label = jnp.zeros((capacity, LANES), jnp.int32)
            for edge in edges:
                label = label + jnp.where(down >= edge, 1, 0)
            start = (member * n_owner + source) * capacity
            lab_sub[start : start + capacity, :] = label
            bias[start : start + capacity, :] = jnp.where(
                label < per_owner, NEIGHBOUR - SCALE, DEAD
            )
            if member == 0:
                across = lax.broadcasted_iota(jnp.int32, (1, capacity), 1)
                label = jnp.zeros((1, capacity), jnp.int32)
                for edge in edges:
                    label = label + jnp.where(across >= edge, 1, 0)
                lab_lane[:, source * capacity : (source + 1) * capacity] = jnp.where(
                    label < per_owner, label, -1
                )
    wide, deep = min(512, total), min(256, total)

    @pl.loop(0, total // wide)
    def _(block):
        columns = pl.ds(pl.multiple_of(block * wide, wide), wide)
        rows_i = mine_ref[columns, :]
        label_i = lab_lane[:, columns]

        def add(ref, offset):
            def step(j, acc):
                start = pl.multiple_of(j * deep, deep)
                scores = lax.dot_general(
                    ref[pl.ds(start, deep), :],
                    rows_i,
                    (((1,), (1,)), ((), ())),
                    preferred_element_type=jnp.float32,
                )
                place = pl.ds(pl.multiple_of(start + offset, deep), deep)
                label_j = lab_sub[place, :]
                bias_j = bias[place, :]
                repeat = wide // LANES
                label_j = jnp.concatenate([label_j] * repeat, axis=1)
                bias_j = jnp.concatenate([bias_j] * repeat, axis=1)
                shift = jnp.where(label_j == label_i, -SCALE, bias_j)
                terms = jnp.exp2(scores * SCALE + shift)
                return acc + jnp.sum(terms.reshape(deep // 8, 8, wide), axis=0)

            return step

        acc = jnp.zeros((8, wide), jnp.float32)
        acc = lax.fori_loop(0, total // deep, add(mine_ref, 0), acc, unroll=2)
        acc = lax.fori_loop(0, total // deep, add(other_ref, total), acc, unroll=2)
        totals = jnp.sum(acc, axis=0, keepdims=True)
        out_ref[:, columns] = jnp.log(jnp.where(label_i >= 0, totals, 1.0))


def log_counts(counts, mine, other, n_owner, capacity):
    total = mine.shape[0]
    vmem = pl.BlockSpec(memory_space=pltpu.VMEM)
    return pl.pallas_call(
        functools.partial(counts_kernel, n_owner, capacity),
        out_shape=jax.ShapeDtypeStruct((1, total), jnp.float32),
        in_specs=[pl.BlockSpec(memory_space=pltpu.SMEM), vmem, vmem],
        out_specs=vmem,
        scratch_shapes=[
            pltpu.VMEM((1, total), jnp.int32),
            pltpu.VMEM((2 * total, LANES), jnp.int32),
            pltpu.VMEM((2 * total, LANES), jnp.float32),
        ],
        compiler_params=pltpu.CompilerParams(vmem_limit_bytes=VMEM_LIMIT),
    )(counts, mine, other)


def unpack_kernel(values_ref, pos_ref, out_ref):
    pos = pos_ref[...]
    lane = lax.rem(pos, LANES)
    line = lax.div(pos, LANES)
    out = jnp.zeros(pos.shape, jnp.float32)
    for r in range(values_ref.shape[0]):
        table = jnp.broadcast_to(values_ref[r : r + 1, :], pos.shape)
        found = jnp.take_along_axis(table, lane, axis=1)
        out = jnp.where(line == r, found, out)
    out_ref[...] = out


def unpack(values, pos):
    vmem = pl.BlockSpec(memory_space=pltpu.VMEM)
    return pl.pallas_call(
        unpack_kernel,
        out_shape=jax.ShapeDtypeStruct(pos.shape, jnp.float32),
        in_specs=[vmem, vmem],
        out_specs=vmem,
    )(values.reshape(-1, LANES), pos)


def swapped(x, first, second):
    return jnp.where(x == first, second, jnp.where(x == second, first, x))


def place_kernel(n_owner, capacity, main, home, x_hbm, lab_hbm, map_hbm, *refs):
    unit, slot_ref, info_ref, extra_ref, pos_ref, x_ref, lab_ref, map_ref, sems = refs
    copies = [
        pltpu.make_async_copy(src, dst, sems.at[i])
        for i, (src, dst) in enumerate(((x_hbm, x_ref), (lab_hbm, lab_ref), (map_hbm, map_ref)))
    ]
    for copy in copies:
        copy.start()
    rows = x_ref.shape[0]
    n_fine = map_ref.shape[1]
    per_owner = n_fine // n_owner
    rest = capacity - main
    copies[1].wait()
    copies[2].wait()
    owner_row = map_ref[...].astype(jnp.float32)
    fine_row = lax.broadcasted_iota(jnp.int32, (1, n_fine), 1).astype(jnp.float32)
    key_row = owner_row * n_fine + fine_row
    key_col = column_of(key_row)
    sorted_col = jnp.sum(jnp.where(key_row < key_col, 1.0, 0.0), axis=1, keepdims=True)
    lab = lab_ref[...].astype(jnp.float32)
    lab_row = jnp.concatenate([lab[b : b + 1, :] for b in range(lab.shape[0])], axis=1)
    fine_col = lax.broadcasted_iota(jnp.int32, (n_fine, rows), 0).astype(jnp.float32)
    fine_id = jnp.sum(jnp.where(fine_col == lab_row, sorted_col, 0.0), axis=0, keepdims=True)
    counts_col = jnp.sum(jnp.where(fine_col == fine_id, 1.0, 0.0), axis=1, keepdims=True)
    coarse = jnp.floor((fine_id + 0.5) * (1.0 / per_owner))
    first = coarse * per_owner
    before = jnp.sum(jnp.where(fine_col < first, counts_col, 0.0), axis=0, keepdims=True)
    upto = jnp.sum(jnp.where(fine_col < first + per_owner, counts_col, 0.0), axis=0, keepdims=True)
    full = jnp.min(
        jnp.where(upto - before == capacity, coarse, float(n_owner)), axis=1, keepdims=True
    )
    line = lax.broadcasted_iota(jnp.int32, (n_fine, LANES), 0)
    lane = lax.broadcasted_iota(jnp.int32, (n_fine, LANES), 1)
    inside = (line <= lane) & (lax.div(line, per_owner) == lax.div(lane, per_owner))
    running = jnp.sum(jnp.where(inside, counts_col, 0.0), axis=0, keepdims=True)
    info = jnp.where(lane[:1] < n_fine, running, full)
    info_ref[...] = info
    index = lax.broadcasted_iota(jnp.int32, (1, rows), 1).astype(jnp.float32)
    row_key = fine_id * rows + index
    rank = jnp.zeros((1, rows), jnp.float32)
    for start in range(0, rows, LANES):
        other = column_of(row_key[:, start : start + LANES])
        rank = rank + jnp.sum(jnp.where(other < row_key, 1.0, 0.0), axis=0, keepdims=True)
    rank = (rank - before).astype(jnp.int32)
    place = swapped(coarse.astype(jnp.int32), full.astype(jnp.int32), home)
    table = place * capacity + rank
    pos_ref[...] = jnp.concatenate(
        [table[:, start : start + LANES] for start in range(0, rows, LANES)], axis=0
    )
    later = jnp.where(place == home, n_owner * main + rank - main, -1)
    fits = rank < jnp.where(place == home, main, main - 1)
    slot = jnp.where(fits, place * main + rank, later)
    slot_ref[...] = slot
    copies[0].wait()
    x = x_ref[...].astype(jnp.float32)
    squares = jnp.sum(x * x, axis=1, keepdims=True)
    unit[...] = (x * lax.rsqrt(squares + epsilon)).astype(jnp.bfloat16)
    extra_ref[:rest, :] = chosen_rows(unit, slot, n_owner * main, rest)
    extra_ref[rest:, :] = jnp.zeros((INFO, extra_ref.shape[1]), jnp.bfloat16)
    extra_ref[rest:, :LANES] = jnp.broadcast_to(info, (INFO, LANES)).astype(jnp.bfloat16)


def chosen_rows(unit, slot, start, count):
    here = lax.broadcasted_iota(jnp.int32, (count, unit.shape[0]), 0) + start
    chosen = jnp.where(here == slot, 1.0, 0.0).astype(jnp.bfloat16)
    return jnp.dot(chosen, unit[...], preferred_element_type=jnp.float32).astype(jnp.bfloat16)


def main_kernel(n_owner, main, home, unit, slot_ref, info_ref, main_ref):
    count = n_owner * main // 4
    for start in range(0, n_owner * main, count):
        main_ref[start : start + count, :] = chosen_rows(unit, slot_ref[...], start, count)
    for owner in range(n_owner):
        if owner != home:
            tail = slice((owner + 1) * main - INFO, (owner + 1) * main)
            old = main_ref[tail, :LANES].astype(jnp.float32)
            down = lax.broadcasted_iota(jnp.int32, old.shape, 0)
            new = jnp.where(down == INFO - 1, info_ref[...], old)
            main_ref[tail, :LANES] = new.astype(jnp.bfloat16)


def vmem_specs(count):
    return (pl.BlockSpec(memory_space=pltpu.VMEM),) * count


def place_rows(embeddings, labels, owner_map, n_owner, capacity, main, home):
    rows, width = embeddings.shape
    n_fine = owner_map.shape[0]
    lab_shape = (rows // LANES, LANES)
    return pl.pallas_call(
        functools.partial(place_kernel, n_owner, capacity, main, home),
        out_shape=(
            jax.ShapeDtypeStruct((rows, width), jnp.bfloat16),
            jax.ShapeDtypeStruct((1, rows), jnp.int32),
            jax.ShapeDtypeStruct((1, LANES), jnp.float32),
            jax.ShapeDtypeStruct((capacity - main + INFO, width), jnp.bfloat16),
            jax.ShapeDtypeStruct(lab_shape, jnp.int32),
        ),
        in_specs=[pl.BlockSpec(memory_space=pl.ANY)] * 3,
        out_specs=vmem_specs(5),
        scratch_shapes=[
            pltpu.VMEM((rows, width), jnp.bfloat16),
            pltpu.VMEM(lab_shape, jnp.int32),
            pltpu.VMEM((1, n_fine), jnp.int32),
            pltpu.SemaphoreType.DMA((3,)),
        ],
        compiler_params=pltpu.CompilerParams(vmem_limit_bytes=FAST_LIMIT),
    )(embeddings, labels.reshape(lab_shape), owner_map.reshape(1, n_fine))


def pack_main(unit, slot, info, n_owner, main, home):
    return pl.pallas_call(
        functools.partial(main_kernel, n_owner, main, home),
        out_shape=jax.ShapeDtypeStruct((n_owner * main, unit.shape[1]), jnp.bfloat16),
        in_specs=list(vmem_specs(3)),
        out_specs=vmem_specs(1)[0],
        compiler_params=pltpu.CompilerParams(vmem_limit_bytes=FAST_LIMIT),
        cost_estimate=pl.CostEstimate(
            flops=2 * n_owner * main * unit.shape[0] * unit.shape[1],
            bytes_accessed=4 * unit.shape[0] * unit.shape[1],
            transcendentals=0,
        ),
    )(unit, slot, info)


def gate_kernel(*refs):
    pass


def after(rows, received):
    anywhere = pl.BlockSpec(memory_space=pl.ANY)
    return pl.pallas_call(
        gate_kernel,
        out_shape=jax.ShapeDtypeStruct(rows.shape, rows.dtype),
        in_specs=[anywhere] * (1 + len(received)),
        out_specs=anywhere,
        input_output_aliases={0: 0},
    )(rows, *received)


def gather_kernel(rest, home, *refs):
    chunks, out = refs[:-1], refs[-1]

    @pl.when(lax.axis_index("cl") == home)
    def _():
        for source, chunk in enumerate(chunks):
            out[source * rest : (source + 1) * rest, :] = chunk[:rest, :]
            start = len(chunks) * rest + source * INFO
            out[start : start + INFO, :] = chunk[rest:, :]


def gather_rest(chunks, rest, home):
    shape = (len(chunks) * (rest + INFO), chunks[0].shape[1])
    return pl.pallas_call(
        functools.partial(gather_kernel, rest, home),
        out_shape=jax.ShapeDtypeStruct(shape, jnp.bfloat16),
        in_specs=list(vmem_specs(len(chunks))),
        out_specs=vmem_specs(1)[0],
        cost_estimate=pl.CostEstimate(
            flops=0, bytes_accessed=4 * shape[0] * shape[1], transcendentals=0
        ),
    )(*chunks)


class Layout:
    def __init__(self, n_owner, n_fine, capacity, main, home):
        self.n_owner, self.n_fine, self.capacity = n_owner, n_fine, capacity
        self.main, self.home = main, home
        self.rest = capacity - main
        self.per_owner = n_fine // n_owner
        self.n_main = n_owner * main
        self.n_rest = n_owner * self.rest
        self.total = self.n_main + self.n_rest


def info_line(lay, is_home, main_ref, rest_ref, source):
    in_main = main_ref[(source + 1) * lay.main - INFO : (source + 1) * lay.main, :LANES]
    start = lay.n_rest + source * INFO
    in_rest = rest_ref[start : start + INFO, :LANES]
    in_main = in_main.astype(jnp.float32)[INFO - 1 :]
    return jnp.where(is_home, in_rest.astype(jnp.float32)[INFO - 1 :], in_main)


def write_labels(lay, infos, cluster, is_home, lab_sub, bias):
    lane = lax.broadcasted_iota(jnp.int32, (1, LANES), 1)
    is_edge = lax.div(lane, lay.per_owner) == cluster
    for source, info in enumerate(infos):
        edges = jnp.where(is_edge, info, 2.0 * lay.capacity)

        def write(start, first, count, edges=edges):
            slot = lax.broadcasted_iota(jnp.int32, (count, LANES), 0) + first
            label = jnp.where(slot.astype(jnp.float32) >= edges, 1.0, 0.0)
            label = jnp.broadcast_to(jnp.sum(label, axis=1, keepdims=True), (count, LANES))
            lab_sub[start : start + count, :] = label
            bias[start : start + count, :] = jnp.where(
                label < lay.per_owner, NEIGHBOUR - SCALE, DEAD
            )

        write(source * lay.main, 0, lay.main)

        @pl.when(is_home)
        def _(source=source, write=write):
            write(lay.n_main + source * lay.rest, lay.main, lay.rest)


def hot_of(lay, info):
    lane = lax.broadcasted_iota(jnp.int32, (1, LANES), 1)
    hot = jnp.max(jnp.where(lane == lay.n_fine, info, 0.0), axis=1, keepdims=True)
    return hot.astype(jnp.int32)


def scores_to(buffer, rows_j, rows_i):
    buffer[: rows_j.shape[0], : rows_i.shape[0]] = lax.dot_general(
        rows_j,
        rows_i,
        (((1,), (1,)), ((), ())),
        preferred_element_type=jnp.float32,
    )


def add_terms(acc, buffer, deep, label_i, lab_sub, bias, place):
    wide = label_i.shape[1]
    repeat = wide // LANES
    step = 32
    for c in range(0, deep, step):
        part = slice(place + c, place + c + step)
        label_j = jnp.concatenate([lab_sub[part, :]] * repeat, axis=1)
        bias_j = jnp.concatenate([bias[part, :]] * repeat, axis=1)
        shift = jnp.where(label_j == label_i, -SCALE, bias_j)
        terms = jnp.exp2(buffer[c : c + step, :wide] * SCALE + shift)
        acc = acc + jnp.sum(terms.reshape(step // 8, 8, wide), axis=0)
    return acc


def main_sums(lay, rows_i, rows_j, lab_lane, lab_sub, bias, buffers, put):
    half = lay.n_main // 2
    low, high = buffers

    def run(start, wide):
        place = pl.ds(start, wide)
        here, label_i = rows_i[place, :], lab_lane[:, place]
        scores_to(low, rows_j[:half, :], here)
        scores_to(high, rows_j[half : lay.n_main, :], here)
        acc = jnp.zeros((8, wide), jnp.float32)
        acc = add_terms(acc, low, half, label_i, lab_sub, bias, 0)
        acc = add_terms(acc, high, half, label_i, lab_sub, bias, half)
        put(place, jnp.sum(acc, axis=0, keepdims=True))

    wide = 256
    full = lay.n_main // wide

    @pl.loop(0, full)
    def _(i):
        run(pl.multiple_of(i * wide, wide), wide)

    if lay.n_main % wide:
        run(full * wide, lay.n_main % wide)


def all_sums(lay, rows_i, rows_j, rest_j, lab_lane, lab_sub, bias, buffers, put):
    wide = 256
    blocks = lay.total // wide
    first, second = buffers

    def place_of(block):
        return pl.ds(pl.multiple_of(block * wide, wide), wide)

    scores_to(first, rows_j[: lay.n_main, :], rows_i[:wide, :])

    @pl.loop(0, blocks)
    def _(block):
        place = place_of(block)
        label_i = lab_lane[:, place]
        scores_to(second, rest_j[: lay.n_rest, :], rows_i[place, :])
        acc = jnp.zeros((8, wide), jnp.float32)
        acc = add_terms(acc, first, lay.n_main, label_i, lab_sub, bias, 0)
        scores_to(first, rows_j[: lay.n_main, :], rows_i[place_of(jnp.minimum(block + 1, blocks - 1)), :])
        acc = add_terms(acc, second, lay.n_rest, label_i, lab_sub, bias, lay.n_main)
        put(place, jnp.sum(acc, axis=0, keepdims=True))


def join_rows(lay, mine, rest, rows):
    for start in range(0, lay.n_main, lay.main):
        rows[start : start + lay.main, :] = mine[start : start + lay.main, :]
    for start in range(0, lay.n_rest, lay.rest):
        to = lay.n_main + start
        rows[to : to + lay.rest, :] = rest[start : start + lay.rest, :]


def inner_kernel(lay, mine, rest, sums, lab_lane, lab_sub, bias, rows, buf_a, buf_b):
    me = lax.axis_index("cl")
    is_home = me == lay.home
    infos = [info_line(lay, is_home, mine, rest, s) for s in range(lay.n_owner)]
    cluster = swapped(me, hot_of(lay, infos[0]), lay.home)
    write_labels(lay, infos, cluster, is_home, lab_sub, bias)

    def turn(start, count):
        for i in range(start, start + count, LANES):
            block = jnp.transpose(lab_sub[i : i + LANES, :])[:1]
            lab_lane[:, i : i + LANES] = jnp.where(block < lay.per_owner, block, -1.0)

    def put(place, values):
        sums[:, place] = values

    turn(0, lay.n_main)
    buffers = (buf_a, buf_b)

    @pl.when(is_home)
    def _():
        turn(lay.n_main, lay.n_rest)
        join_rows(lay, mine, rest, rows)
        all_sums(lay, rows, mine, rest, lab_lane, lab_sub, bias, buffers, put)

    @pl.when(jnp.logical_not(is_home))
    def _():
        main_sums(lay, mine, mine, lab_lane, lab_sub, bias, buffers, put)


def cross_kernel(lay, *refs):
    mine, rest, other, rest_other, lab_lane, sums = refs[:6]
    out_ref, unfit_ref, lab_sub, bias, rows, total, buf_a, buf_b = refs[6:]
    me = lax.axis_index("cl")
    is_home = me == lay.home
    infos = [info_line(lay, is_home, other, rest_other, s) for s in range(lay.n_owner)]
    own = [info_line(lay, is_home, mine, rest, s) for s in range(lay.n_owner)]
    hot = hot_of(lay, own[0])
    lane = lax.broadcasted_iota(jnp.int32, (1, LANES), 1)
    last = (lane < lay.n_fine) & (lax.rem(lane, lay.per_owner) == lay.per_owner - 1)
    last = last & (lax.div(lane, lay.per_owner) != hot)
    unfit = jnp.zeros((1, LANES), jnp.float32)
    for info in infos + own:
        wrong = last & (info >= lay.main)
        differs = (info != hot.astype(jnp.float32)) | (info >= lay.n_owner)
        wrong = wrong | ((lane == lay.n_fine) & differs)
        unfit = unfit + jnp.where(wrong, 1.0, 0.0)
    unfit_ref[...] = jnp.broadcast_to(
        jnp.max(unfit, axis=1, keepdims=True), unfit_ref.shape
    ).astype(jnp.int32)
    write_labels(lay, infos, swapped(me, hot, lay.home), is_home, lab_sub, bias)
    buffers = (buf_a, buf_b)

    def put(place, values):
        values = values + sums[:, place]
        total[:, place] = jnp.log(jnp.where(lab_lane[:, place] >= 0, values, 1.0))

    @pl.when(is_home)
    def _():
        join_rows(lay, mine, rest, rows)
        all_sums(lay, rows, other, rest_other, lab_lane, lab_sub, bias, buffers, put)

    @pl.when(jnp.logical_not(is_home))
    def _():
        main_sums(lay, mine, other, lab_lane, lab_sub, bias, buffers, put)

    for source in range(lay.n_owner):
        out_ref[source, :, : lay.main] = total[:, source * lay.main : (source + 1) * lay.main]
        start = lay.n_main + source * lay.rest
        out_ref[source, :, lay.main :] = total[:, start : start + lay.rest]


def pair_scratch(lay, width):
    side = pltpu.VMEM((lay.total, LANES), jnp.float32)
    buffer = pltpu.VMEM((lay.n_main, 256), jnp.float32)
    rows = pltpu.VMEM((lay.total, width), jnp.bfloat16)
    return [side, side, rows], [buffer, buffer]


def pair_cost(lay, rows):
    pairs = lay.n_main * lay.n_main
    return pl.CostEstimate(
        flops=2 * pairs * rows.shape[1],
        bytes_accessed=4 * lay.n_main * rows.shape[1],
        transcendentals=pairs,
    )


def inner_sums(lay, mine, rest):
    row = jax.ShapeDtypeStruct((1, lay.total), jnp.float32)
    sides, buffers = pair_scratch(lay, mine.shape[1])
    return pl.pallas_call(
        functools.partial(inner_kernel, lay),
        out_shape=(row, row),
        in_specs=list(vmem_specs(2)),
        out_specs=vmem_specs(2),
        scratch_shapes=sides + buffers,
        compiler_params=pltpu.CompilerParams(vmem_limit_bytes=FAST_LIMIT),
        cost_estimate=pair_cost(lay, mine),
    )(mine, rest)


def cross_sums(lay, mine, rest, other, rest_other, lab_lane, sums):
    row = pltpu.VMEM((1, lay.total), jnp.float32)
    sides, buffers = pair_scratch(lay, mine.shape[1])
    return pl.pallas_call(
        functools.partial(cross_kernel, lay),
        out_shape=(
            jax.ShapeDtypeStruct((lay.n_owner, 1, lay.capacity), jnp.float32),
            jax.ShapeDtypeStruct((8, LANES), jnp.int32),
        ),
        in_specs=list(vmem_specs(6)),
        out_specs=vmem_specs(2),
        scratch_shapes=sides + [row] + buffers,
        compiler_params=pltpu.CompilerParams(vmem_limit_bytes=FAST_LIMIT),
        cost_estimate=pair_cost(lay, mine),
    )(mine, rest, other, rest_other, lab_lane, sums)


def fast_unpack_kernel(values_ref, pos_ref, out_ref):
    pos = pos_ref[...]
    lane = lax.rem(pos, LANES)
    line = lax.div(pos, LANES)
    out = jnp.zeros(pos.shape, jnp.float32)
    per = values_ref.shape[2] // LANES
    for r in range(values_ref.shape[0] * per):
        start = r % per * LANES
        table = jnp.broadcast_to(values_ref[r // per, :, start : start + LANES], pos.shape)
        found = jnp.take_along_axis(table, lane, axis=1)
        out = jnp.where(line == r, found, out)
    out_ref[...] = out


def fast_unpack(values, pos):
    vmem = pl.BlockSpec(memory_space=pltpu.VMEM)
    return pl.pallas_call(
        fast_unpack_kernel,
        out_shape=jax.ShapeDtypeStruct(pos.shape, jnp.float32),
        in_specs=[vmem, vmem],
        out_specs=vmem,
    )(values, pos)


def general(embeddings, labels, owner_map):
    n_owner = lax.axis_size("cl")
    capacity = SLOTS // n_owner
    rows, width = embeddings.shape
    packed, pos, counts = pack(embeddings, labels, owner_map, n_owner, capacity)
    counts = lax.all_gather(counts, ("cl", "grp"), tiled=True)
    mine = lax.all_to_all(
        packed.reshape(n_owner, capacity, width), "cl", split_axis=0, concat_axis=0, tiled=True
    ).reshape(SLOTS, width)
    other = lax.ppermute(mine, "grp", [(0, 1), (1, 0)])
    results = log_counts(counts, mine, other, n_owner, capacity)
    returned = lax.all_to_all(
        results.reshape(n_owner, capacity), "cl", split_axis=0, concat_axis=0, tiled=True
    )
    return unpack(returned.reshape(SLOTS), pos).reshape(rows)


def body(embeddings, labels, owner_map):
    n_owner = lax.axis_size("cl")
    capacity = SLOTS // n_owner
    rows, width = embeddings.shape
    n_fine = owner_map.shape[0]
    main = -(-(rows // n_owner * 9 // 8) // 16) * 16
    if main >= capacity or n_fine >= LANES:
        return general(embeddings, labels, owner_map)
    home = n_owner // 4
    lay = Layout(n_owner, n_fine, capacity, main, home)
    unit, slot, info, extra, pos = place_rows(
        embeddings, labels, owner_map, n_owner, capacity, main, home
    )
    chunks = [
        extra if source == home else lax.ppermute(extra, "cl", [(source, home)])
        for source in range(n_owner)
    ]
    packed = pack_main(unit, slot, info, n_owner, main, home)
    packed = after(packed, chunks[:home] + chunks[home + 1 :])
    rest = gather_rest(chunks, lay.rest, home)
    rest_other = lax.ppermute(
        rest, ("cl", "grp"), [(2 * home, 2 * home + 1), (2 * home + 1, 2 * home)]
    )
    mine = lax.all_to_all(
        packed.reshape(n_owner, main, width), "cl", split_axis=0, concat_axis=0, tiled=True
    ).reshape(n_owner * main, width)
    other = lax.ppermute(mine, "grp", [(0, 1), (1, 0)])
    sums, lab_lane = inner_sums(lay, mine, rest)
    results, unfit = cross_sums(lay, mine, rest, other, rest_other, lab_lane, sums)
    returned = lax.all_to_all(results, "cl", split_axis=0, concat_axis=0, tiled=True)
    return lax.cond(
        unfit[0, 0] == 0,
        lambda: fast_unpack(returned, pos).reshape(rows),
        lambda: general(embeddings, labels, owner_map),
    )


def solution(mesh):
    return jax.shard_map(
        body,
        mesh=mesh,
        in_specs=(P(("parts", "cl", "grp"), None), P(("parts", "cl", "grp")), P("parts")),
        out_specs=P(("parts", "cl", "grp")),
        check_vma=False,
    )
```

```python
import functools
import math

import jax
import jax.numpy as jnp
from jax import lax
from jax.experimental import pallas as pl
from jax.experimental.pallas import tpu as pltpu
from jax.sharding import PartitionSpec as P

SLOTS = 2048

temper = 0.2
neighbour_factor = 0.5
epsilon = 1e-06

LANES = 128
SCALE = math.log2(math.e) / temper
NEIGHBOUR = math.log2(neighbour_factor)
DEAD = -1e30
VMEM_LIMIT = 48 * 1024 * 1024
FAST_LIMIT = 40 * 1024 * 1024
INFO = 16


def column_of(row):
    pieces = []
    for start in range(0, row.shape[1], LANES):
        width = min(LANES, row.shape[1] - start)
        shape = (width, width)
        diagonal = lax.broadcasted_iota(jnp.int32, shape, 0) == lax.broadcasted_iota(
            jnp.int32, shape, 1
        )
        piece = jnp.broadcast_to(row[:, start : start + width], shape)
        pieces.append(jnp.sum(jnp.where(diagonal, piece, 0.0), axis=1, keepdims=True))
    return jnp.concatenate(pieces, axis=0)


def row_of(column):
    n = column.shape[0]
    diagonal = lax.broadcasted_iota(jnp.int32, (n, n), 0) == lax.broadcasted_iota(
        jnp.int32, (n, n), 1
    )
    return jnp.sum(jnp.where(diagonal, column, 0.0), axis=0, keepdims=True)


def pack_kernel(n_owner, capacity, x_ref, lab_ref, map_ref, out_ref, pos_ref, cnt_ref, unit, pos_row):
    rows = x_ref.shape[0]
    n_fine = map_ref.shape[1]
    per_owner = n_fine // n_owner
    owner_row = map_ref[...].astype(jnp.float32)
    fine_row = lax.broadcasted_iota(jnp.int32, (1, n_fine), 1).astype(jnp.float32)
    key_row = owner_row * n_fine + fine_row
    key_col = column_of(key_row)
    sorted_col = jnp.sum(jnp.where(key_row < key_col, 1.0, 0.0), axis=1, keepdims=True)
    lab = lab_ref[...].astype(jnp.float32)
    lab_row = jnp.concatenate([lab[b : b + 1, :] for b in range(lab.shape[0])], axis=1)
    fine_col = lax.broadcasted_iota(jnp.int32, (n_fine, rows), 0).astype(jnp.float32)
    fine_id = jnp.sum(jnp.where(fine_col == lab_row, sorted_col, 0.0), axis=0, keepdims=True)
    counts_col = jnp.sum(jnp.where(fine_col == fine_id, 1.0, 0.0), axis=1, keepdims=True)
    cnt_ref[...] = row_of(counts_col).astype(jnp.int32)
    coarse = jnp.floor((fine_id + 0.5) * (1.0 / per_owner))
    before = jnp.sum(
        jnp.where(fine_col < coarse * per_owner, counts_col, 0.0), axis=0, keepdims=True
    )
    index = lax.broadcasted_iota(jnp.int32, (1, rows), 1).astype(jnp.float32)
    row_key = fine_id * rows + index
    rank = jnp.zeros((1, rows), jnp.float32)
    for start in range(0, rows, LANES):
        other = column_of(row_key[:, start : start + LANES])
        rank = rank + jnp.sum(jnp.where(other < row_key, 1.0, 0.0), axis=0, keepdims=True)
    pos = (coarse * capacity + rank - before).astype(jnp.int32)
    pos_row[...] = pos
    pos_ref[...] = jnp.concatenate(
        [pos[:, start : start + LANES] for start in range(0, rows, LANES)], axis=0
    )
    x = x_ref[...].astype(jnp.float32)
    squares = jnp.sum(x * x, axis=1, keepdims=True)
    unit[...] = (x * lax.rsqrt(squares + epsilon)).astype(jnp.bfloat16)

    step = 256

    @pl.loop(0, out_ref.shape[0] // step)
    def _(block):
        slot = lax.broadcasted_iota(jnp.int32, (step, rows), 0) + block * step
        chosen = jnp.where(slot == pos_row[...], 1.0, 0.0).astype(jnp.bfloat16)
        packed = jnp.dot(chosen, unit[...], preferred_element_type=jnp.float32)
        out_ref[pl.ds(pl.multiple_of(block * step, step), step), :] = packed.astype(jnp.bfloat16)


def pack(embeddings, labels, owner_map, n_owner, capacity):
    rows, width = embeddings.shape
    n_fine = owner_map.shape[0]
    total = n_owner * capacity
    vmem = pl.BlockSpec(memory_space=pltpu.VMEM)
    return pl.pallas_call(
        functools.partial(pack_kernel, n_owner, capacity),
        out_shape=(
            jax.ShapeDtypeStruct((total, width), jnp.bfloat16),
            jax.ShapeDtypeStruct((rows // LANES, LANES), jnp.int32),
            jax.ShapeDtypeStruct((1, n_fine), jnp.int32),
        ),
        in_specs=[vmem] * 3,
        out_specs=(vmem, vmem, vmem),
        scratch_shapes=[pltpu.VMEM((rows, width), jnp.bfloat16), pltpu.VMEM((1, rows), jnp.int32)],
        compiler_params=pltpu.CompilerParams(vmem_limit_bytes=VMEM_LIMIT),
    )(embeddings, labels.reshape(rows // LANES, LANES), owner_map.reshape(1, n_fine))


def counts_kernel(n_owner, capacity, cnt_ref, mine_ref, other_ref, out_ref, lab_lane, lab_sub, bias):
    total = mine_ref.shape[0]
    per_owner = cnt_ref.shape[1] // n_owner
    me = lax.axis_index("cl")
    grp = lax.axis_index("grp")
    n_grp = lax.axis_size("grp")
    for member in range(2):
        for source in range(n_owner):
            line = source * n_grp + lax.rem(grp + member, n_grp)
            edges = []
            edge = jnp.int32(0)
            for f in range(per_owner):
                edge = edge + cnt_ref[line, me * per_owner + f]
                edges.append(edge)
            down = lax.broadcasted_iota(jnp.int32, (capacity, LANES), 0)
            label = jnp.zeros((capacity, LANES), jnp.int32)
            for edge in edges:
                label = label + jnp.where(down >= edge, 1, 0)
            start = (member * n_owner + source) * capacity
            lab_sub[start : start + capacity, :] = label
            bias[start : start + capacity, :] = jnp.where(
                label < per_owner, NEIGHBOUR - SCALE, DEAD
            )
            if member == 0:
                across = lax.broadcasted_iota(jnp.int32, (1, capacity), 1)
                label = jnp.zeros((1, capacity), jnp.int32)
                for edge in edges:
                    label = label + jnp.where(across >= edge, 1, 0)
                lab_lane[:, source * capacity : (source + 1) * capacity] = jnp.where(
                    label < per_owner, label, -1
                )
    wide, deep = min(512, total), min(256, total)

    @pl.loop(0, total // wide)
    def _(block):
        columns = pl.ds(pl.multiple_of(block * wide, wide), wide)
        rows_i = mine_ref[columns, :]
        label_i = lab_lane[:, columns]

        def add(ref, offset):
            def step(j, acc):
                start = pl.multiple_of(j * deep, deep)
                scores = lax.dot_general(
                    ref[pl.ds(start, deep), :],
                    rows_i,
                    (((1,), (1,)), ((), ())),
                    preferred_element_type=jnp.float32,
                )
                place = pl.ds(pl.multiple_of(start + offset, deep), deep)
                label_j = lab_sub[place, :]
                bias_j = bias[place, :]
                repeat = wide // LANES
                label_j = jnp.concatenate([label_j] * repeat, axis=1)
                bias_j = jnp.concatenate([bias_j] * repeat, axis=1)
                shift = jnp.where(label_j == label_i, -SCALE, bias_j)
                terms = jnp.exp2(scores * SCALE + shift)
                return acc + jnp.sum(terms.reshape(deep // 8, 8, wide), axis=0)

            return step

        acc = jnp.zeros((8, wide), jnp.float32)
        acc = lax.fori_loop(0, total // deep, add(mine_ref, 0), acc, unroll=2)
        acc = lax.fori_loop(0, total // deep, add(other_ref, total), acc, unroll=2)
        totals = jnp.sum(acc, axis=0, keepdims=True)
        out_ref[:, columns] = jnp.log(jnp.where(label_i >= 0, totals, 1.0))


def log_counts(counts, mine, other, n_owner, capacity):
    total = mine.shape[0]
    vmem = pl.BlockSpec(memory_space=pltpu.VMEM)
    return pl.pallas_call(
        functools.partial(counts_kernel, n_owner, capacity),
        out_shape=jax.ShapeDtypeStruct((1, total), jnp.float32),
        in_specs=[pl.BlockSpec(memory_space=pltpu.SMEM), vmem, vmem],
        out_specs=vmem,
        scratch_shapes=[
            pltpu.VMEM((1, total), jnp.int32),
            pltpu.VMEM((2 * total, LANES), jnp.int32),
            pltpu.VMEM((2 * total, LANES), jnp.float32),
        ],
        compiler_params=pltpu.CompilerParams(vmem_limit_bytes=VMEM_LIMIT),
    )(counts, mine, other)


def unpack_kernel(values_ref, pos_ref, out_ref):
    pos = pos_ref[...]
    lane = lax.rem(pos, LANES)
    line = lax.div(pos, LANES)
    out = jnp.zeros(pos.shape, jnp.float32)
    for r in range(values_ref.shape[0]):
        table = jnp.broadcast_to(values_ref[r : r + 1, :], pos.shape)
        found = jnp.take_along_axis(table, lane, axis=1)
        out = jnp.where(line == r, found, out)
    out_ref[...] = out


def unpack(values, pos):
    vmem = pl.BlockSpec(memory_space=pltpu.VMEM)
    return pl.pallas_call(
        unpack_kernel,
        out_shape=jax.ShapeDtypeStruct(pos.shape, jnp.float32),
        in_specs=[vmem, vmem],
        out_specs=vmem,
    )(values.reshape(-1, LANES), pos)


def swapped(x, first, second):
    return jnp.where(x == first, second, jnp.where(x == second, first, x))


def place_kernel(lay, x_hbm, lab_hbm, map_hbm, *refs):
    n_owner, capacity, main, home = lay.n_owner, lay.capacity, lay.main, lay.home
    unit, slot_ref, info_ref, extra_ref, pos_ref, x_ref, lab_ref, map_ref, sems = refs
    copies = [
        pltpu.make_async_copy(src, dst, sems.at[i])
        for i, (src, dst) in enumerate(((x_hbm, x_ref), (lab_hbm, lab_ref), (map_hbm, map_ref)))
    ]
    for copy in copies:
        copy.start()
    rows = x_ref.shape[0]
    n_fine = map_ref.shape[1]
    per_owner = n_fine // n_owner
    copies[1].wait()
    copies[2].wait()
    owner_row = map_ref[...].astype(jnp.float32)
    fine_row = lax.broadcasted_iota(jnp.int32, (1, n_fine), 1).astype(jnp.float32)
    key_row = owner_row * n_fine + fine_row
    key_col = column_of(key_row)
    sorted_col = jnp.sum(jnp.where(key_row < key_col, 1.0, 0.0), axis=1, keepdims=True)
    lab = lab_ref[...].astype(jnp.float32)
    lab_row = jnp.concatenate([lab[b : b + 1, :] for b in range(lab.shape[0])], axis=1)
    fine_col = lax.broadcasted_iota(jnp.int32, (n_fine, rows), 0).astype(jnp.float32)
    fine_id = jnp.sum(jnp.where(fine_col == lab_row, sorted_col, 0.0), axis=0, keepdims=True)
    counts_col = jnp.sum(jnp.where(fine_col == fine_id, 1.0, 0.0), axis=1, keepdims=True)
    coarse = jnp.floor((fine_id + 0.5) * (1.0 / per_owner))
    first = coarse * per_owner
    before = jnp.sum(jnp.where(fine_col < first, counts_col, 0.0), axis=0, keepdims=True)
    upto = jnp.sum(jnp.where(fine_col < first + per_owner, counts_col, 0.0), axis=0, keepdims=True)
    full = jnp.min(
        jnp.where(upto - before == capacity, coarse, float(n_owner)), axis=1, keepdims=True
    )
    line = lax.broadcasted_iota(jnp.int32, (n_fine, LANES), 0)
    lane = lax.broadcasted_iota(jnp.int32, (n_fine, LANES), 1)
    inside = (line <= lane) & (lax.div(line, per_owner) == lax.div(lane, per_owner))
    running = jnp.sum(jnp.where(inside, counts_col, 0.0), axis=0, keepdims=True)
    info = jnp.where(lane[:1] < n_fine, running, full)
    info_ref[...] = info
    index = lax.broadcasted_iota(jnp.int32, (1, rows), 1).astype(jnp.float32)
    row_key = fine_id * rows + index
    rank = jnp.zeros((1, rows), jnp.float32)
    for start in range(0, rows, LANES):
        other = column_of(row_key[:, start : start + LANES])
        rank = rank + jnp.sum(jnp.where(other < row_key, 1.0, 0.0), axis=0, keepdims=True)
    rank = (rank - before).astype(jnp.int32)
    place = swapped(coarse.astype(jnp.int32), full.astype(jnp.int32), home)
    table = place * capacity + rank
    pos_ref[...] = jnp.concatenate(
        [table[:, start : start + LANES] for start in range(0, rows, LANES)], axis=0
    )
    later = jnp.where(place == home, lay.n_main + rank - lay.head, -1)
    fits = rank < jnp.where(place == home, lay.head, main - 1)
    slot = jnp.where(fits, place * main + rank, later)
    slot_ref[...] = slot
    copies[0].wait()
    x = x_ref[...].astype(jnp.float32)
    squares = jnp.sum(x * x, axis=1, keepdims=True)
    unit[...] = (x * lax.rsqrt(squares + epsilon)).astype(jnp.bfloat16)
    extra_ref[...] = chosen_rows(unit, slot, lay.n_main, lay.rest)


def chosen_rows(unit, slot, start, count):
    here = lax.broadcasted_iota(jnp.int32, (count, unit.shape[0]), 0) + start
    chosen = jnp.where(here == slot, 1.0, 0.0).astype(jnp.bfloat16)
    return jnp.dot(chosen, unit[...], preferred_element_type=jnp.float32).astype(jnp.bfloat16)


def main_kernel(lay, unit, slot_ref, info_ref, main_ref):
    count = lay.n_main // 4
    for start in range(0, lay.n_main, count):
        main_ref[start : start + count, :] = chosen_rows(unit, slot_ref[...], start, count)
    for owner in range(lay.n_owner):
        tail = slice((owner + 1) * lay.main - INFO, (owner + 1) * lay.main)
        old = main_ref[tail, :LANES].astype(jnp.float32)
        down = lax.broadcasted_iota(jnp.int32, old.shape, 0)
        new = jnp.where(down == INFO - 1, info_ref[...], old)
        main_ref[tail, :LANES] = new.astype(jnp.bfloat16)


def vmem_specs(count):
    return (pl.BlockSpec(memory_space=pltpu.VMEM),) * count


def place_rows(embeddings, labels, owner_map, lay):
    rows, width = embeddings.shape
    n_fine = owner_map.shape[0]
    lab_shape = (rows // LANES, LANES)
    return pl.pallas_call(
        functools.partial(place_kernel, lay),
        out_shape=(
            jax.ShapeDtypeStruct((rows, width), jnp.bfloat16),
            jax.ShapeDtypeStruct((1, rows), jnp.int32),
            jax.ShapeDtypeStruct((1, LANES), jnp.float32),
            jax.ShapeDtypeStruct((lay.rest, width), jnp.bfloat16),
            jax.ShapeDtypeStruct(lab_shape, jnp.int32),
        ),
        in_specs=[pl.BlockSpec(memory_space=pl.ANY)] * 3,
        out_specs=vmem_specs(5),
        scratch_shapes=[
            pltpu.VMEM((rows, width), jnp.bfloat16),
            pltpu.VMEM(lab_shape, jnp.int32),
            pltpu.VMEM((1, n_fine), jnp.int32),
            pltpu.SemaphoreType.DMA((3,)),
        ],
        compiler_params=pltpu.CompilerParams(vmem_limit_bytes=FAST_LIMIT),
    )(embeddings, labels.reshape(lab_shape), owner_map.reshape(1, n_fine))


def pack_main(unit, slot, info, lay):
    return pl.pallas_call(
        functools.partial(main_kernel, lay),
        out_shape=jax.ShapeDtypeStruct((lay.n_main, unit.shape[1]), jnp.bfloat16),
        in_specs=list(vmem_specs(3)),
        out_specs=vmem_specs(1)[0],
        compiler_params=pltpu.CompilerParams(vmem_limit_bytes=FAST_LIMIT),
        cost_estimate=pl.CostEstimate(
            flops=2 * lay.n_main * unit.shape[0] * unit.shape[1],
            bytes_accessed=4 * unit.shape[0] * unit.shape[1],
            transcendentals=0,
        ),
    )(unit, slot, info)


def gate_kernel(*refs):
    pass


def after(rows, received):
    anywhere = pl.BlockSpec(memory_space=pl.ANY)
    return pl.pallas_call(
        gate_kernel,
        out_shape=jax.ShapeDtypeStruct(rows.shape, rows.dtype),
        in_specs=[anywhere] * 2,
        out_specs=anywhere,
        input_output_aliases={0: 0},
    )(rows, received)


class Layout:
    def __init__(self, n_owner, n_fine, capacity, main, home):
        self.n_owner, self.n_fine, self.capacity = n_owner, n_fine, capacity
        self.main, self.home = main, home
        self.head = main - INFO
        self.rest = capacity - self.head
        self.per_owner = n_fine // n_owner
        self.n_main = n_owner * main
        self.n_head = n_owner * self.head
        self.n_rest = n_owner * self.rest


def info_line(lay, main_ref, source):
    end = (source + 1) * lay.main
    return main_ref[end - INFO : end, :LANES].astype(jnp.float32)[INFO - 1 :]


def lines_of(lay, main_ref):
    return [info_line(lay, main_ref, source) for source in range(lay.n_owner)]


def hot_of(lay, info):
    lane = lax.broadcasted_iota(jnp.int32, (1, LANES), 1)
    hot = jnp.max(jnp.where(lane == lay.n_fine, info, 0.0), axis=1, keepdims=True)
    return hot.astype(jnp.int32)


def write_labels(lay, infos, first, count, at, lab_sub, bias):
    cluster = swapped(lax.axis_index("cl"), hot_of(lay, infos[0]), lay.home)
    lane = lax.broadcasted_iota(jnp.int32, (1, LANES), 1)
    is_edge = lax.div(lane, lay.per_owner) == cluster
    for source, info in enumerate(infos):
        edges = jnp.where(is_edge, info, 2.0 * lay.capacity)
        slot = lax.broadcasted_iota(jnp.int32, (count, LANES), 0) + first
        label = jnp.where(slot.astype(jnp.float32) >= edges, 1.0, 0.0)
        label = jnp.broadcast_to(jnp.sum(label, axis=1, keepdims=True), (count, LANES))
        start = at + source * count
        lab_sub[start : start + count, :] = label
        bias[start : start + count, :] = jnp.where(label < lay.per_owner, NEIGHBOUR - SCALE, DEAD)


def turn_labels(lay, lab_sub, start, count, lab_lane, at):
    for i in range(0, count, LANES):
        block = jnp.transpose(lab_sub[start + i : start + i + LANES, :])[:1]
        lab_lane[:, at + i : at + i + LANES] = jnp.where(block < lay.per_owner, block, -1.0)


def copy_head(lay, main_ref, rows):
    for source in range(lay.n_owner):
        rows[source * lay.head : (source + 1) * lay.head, :] = main_ref[
            source * lay.main : source * lay.main + lay.head, :
        ]


def pieces(start, count, parts):
    return [(start + i * (count // parts), count // parts) for i in range(parts)]


def stream(rows_i, first, count, tiles, lab_lane, at, lab_sub, bias, buffers, put):
    step = 32
    tiles = [(ref, s, d, place + s - start) for ref, start, n, place, parts in tiles for s, d in pieces(start, n, parts)]

    def scores_to(buffer, tile, rows):
        ref, start, deep, _ = tile
        buffer[:deep, : rows.shape[0]] = lax.dot_general(
            ref[start : start + deep, :],
            rows,
            (((1,), (1,)), ((), ())),
            preferred_element_type=jnp.float32,
        )

    def run(start, blocks, wide):
        repeat = wide // LANES

        def rows_of(block):
            return rows_i[pl.ds(pl.multiple_of(first + start + block * wide, LANES), wide), :]

        scores_to(buffers[0], tiles[0], rows_of(0))

        def body(block, carry):
            here = rows_of(block)
            place = pl.ds(pl.multiple_of(at + start + block * wide, LANES), wide)
            label_i = lab_lane[:, place]
            acc = jnp.zeros((8, wide), jnp.float32)
            for i, (_, _, deep, line) in enumerate(tiles):
                if i + 1 < len(tiles):
                    scores_to(buffers[(i + 1) % 2], tiles[i + 1], here)
                else:
                    scores_to(buffers[0], tiles[0], rows_of(jnp.minimum(block + 1, blocks - 1)))
                buffer = buffers[i % 2]
                for c in range(0, deep, step):
                    part = slice(line + c, line + c + step)
                    label_j = jnp.concatenate([lab_sub[part, :]] * repeat, axis=1)
                    bias_j = jnp.concatenate([bias[part, :]] * repeat, axis=1)
                    shift = jnp.where(label_j == label_i, -SCALE, bias_j)
                    terms = jnp.exp2(buffer[c : c + step, :wide] * SCALE + shift)
                    acc = acc + jnp.sum(terms.reshape(step // 8, 8, wide), axis=0)
            put(place, jnp.sum(acc, axis=0, keepdims=True))
            return carry

        lax.fori_loop(0, blocks, body, 0)

    wide = 256
    if count >= wide:
        run(0, count // wide, wide)
    if count % wide:
        run(count - count % wide, 1, count % wide)


def setter(ref):
    def put(place, values):
        ref[:, place] = values

    return put


def adder(ref):
    def put(place, values):
        ref[:, place] += values

    return put


def inner_kernel(lay, mine, sums, lab_lane, lab_sub, bias, rows, buf_a, buf_b):
    is_home = lax.axis_index("cl") == lay.home
    infos = lines_of(lay, mine)

    def work(ref, count, per):
        write_labels(lay, infos, 0, per, 0, lab_sub, bias)
        turn_labels(lay, lab_sub, 0, count, lab_lane, 0)
        tiles = [(ref, 0, count, 0, 4)]
        stream(ref, 0, count, tiles, lab_lane, 0, lab_sub, bias, (buf_a, buf_b), setter(sums))

    @pl.when(is_home)
    def _():
        copy_head(lay, mine, rows)
        work(rows, lay.n_head, lay.head)

    @pl.when(jnp.logical_not(is_home))
    def _():
        work(mine, lay.n_main, lay.main)


def cross_kernel(lay, mine, other, sums, lab_lane, total, unfit_ref, lab_sub, bias, rows, rows_j, buf_a, buf_b):
    is_home = lax.axis_index("cl") == lay.home
    infos = lines_of(lay, other)
    own = lines_of(lay, mine)
    hot = hot_of(lay, own[0])
    lane = lax.broadcasted_iota(jnp.int32, (1, LANES), 1)
    last = (lane < lay.n_fine) & (lax.rem(lane, lay.per_owner) == lay.per_owner - 1)
    last = last & (lax.div(lane, lay.per_owner) != hot)
    unfit = jnp.zeros((1, LANES), jnp.float32)
    for info in infos + own:
        wrong = last & (info >= lay.main)
        differs = (info != hot.astype(jnp.float32)) | (info >= lay.n_owner)
        wrong = wrong | ((lane == lay.n_fine) & differs)
        unfit = unfit + jnp.where(wrong, 1.0, 0.0)
    unfit_ref[...] = jnp.broadcast_to(
        jnp.max(unfit, axis=1, keepdims=True), unfit_ref.shape
    ).astype(jnp.int32)
    total[...] = sums[...]

    def work(ref, ref_j, count, per):
        write_labels(lay, infos, 0, per, 0, lab_sub, bias)
        tiles = [(ref_j, 0, count, 0, 4)]
        stream(ref, 0, count, tiles, lab_lane, 0, lab_sub, bias, (buf_a, buf_b), adder(total))

    @pl.when(is_home)
    def _():
        copy_head(lay, mine, rows)
        copy_head(lay, other, rows_j)
        work(rows, rows_j, lay.n_head, lay.head)

    @pl.when(jnp.logical_not(is_home))
    def _():
        work(mine, other, lay.n_main, lay.main)


def rest_pairs(lay, rows, rest, rows_j, rest_j, lab_lane, lab_sub, bias, buffers, put):
    seconds = (rest_j, 0, lay.n_rest, lay.n_head, 4)
    mains = (rows_j, 0, lay.n_head, 0, 4)
    stream(rows, 0, lay.n_head, [seconds], lab_lane, 0, lab_sub, bias, buffers, put)
    stream(
        rest, 0, lay.n_rest, [seconds, mains], lab_lane, lay.n_head, lab_sub, bias, buffers, put
    )


def inner_rest_kernel(lay, mine, rest, sums, lab_lane, lab_sub, bias, rows, buf_a, buf_b):
    @pl.when(lax.axis_index("cl") == lay.home)
    def _():
        infos = lines_of(lay, mine)
        write_labels(lay, infos, 0, lay.head, 0, lab_sub, bias)
        write_labels(lay, infos, lay.head, lay.rest, lay.n_head, lab_sub, bias)
        turn_labels(lay, lab_sub, 0, lay.n_head + lay.n_rest, lab_lane, 0)
        copy_head(lay, mine, rows)
        buffers = (buf_a, buf_b)
        rest_pairs(lay, rows, rest, rows, rest, lab_lane, lab_sub, bias, buffers, setter(sums))


def cross_rest_kernel(lay, *refs):
    mine, rest, other, rest_other, main_sums, main_lane, sums, lab_lane = refs[:8]
    out_ref, lab_sub, bias, rows, rows_j, total, buf_a, buf_b = refs[8:]
    is_home = lax.axis_index("cl") == lay.home

    @pl.when(is_home)
    def _():
        infos = lines_of(lay, other)
        write_labels(lay, infos, 0, lay.head, 0, lab_sub, bias)
        write_labels(lay, infos, lay.head, lay.rest, lay.n_head, lab_sub, bias)
        copy_head(lay, mine, rows)
        copy_head(lay, other, rows_j)
        total[...] = sums[...]
        total[:, : lay.n_head] += main_sums[:, : lay.n_head]
        buffers = (buf_a, buf_b)
        rest_pairs(
            lay, rows, rest, rows_j, rest_other, lab_lane, lab_sub, bias, buffers, adder(total)
        )
        values = jnp.log(total[...])
        for source in range(lay.n_owner):
            start = source * lay.head
            out_ref[source, :, : lay.head] = values[:, start : start + lay.head]
            start = lay.n_head + source * lay.rest
            out_ref[source, :, lay.head :] = values[:, start : start + lay.rest]

    @pl.when(jnp.logical_not(is_home))
    def _():
        values = jnp.log(jnp.where(main_lane[...] >= 0, main_sums[...], 1.0))
        for source in range(lay.n_owner):
            start = source * lay.main
            out_ref[source, :, : lay.main] = values[:, start : start + lay.main]


def pair_call(kernel, lay, arrays, out_shape, lines, joins, more=()):
    width = arrays[0].shape[1]
    side = pltpu.VMEM((lines, LANES), jnp.float32)
    rows = pltpu.VMEM((lay.n_head, width), jnp.bfloat16)
    buffer = pltpu.VMEM((lay.n_main // 4, 256), jnp.float32)
    out = pl.pallas_call(
        functools.partial(kernel, lay),
        out_shape=out_shape,
        in_specs=list(vmem_specs(len(arrays))),
        out_specs=vmem_specs(len(out_shape)),
        scratch_shapes=[side, side] + [rows] * joins + list(more) + [buffer, buffer],
        compiler_params=pltpu.CompilerParams(vmem_limit_bytes=FAST_LIMIT),
        cost_estimate=pl.CostEstimate(
            flops=2 * lay.n_main * lay.n_main * width,
            bytes_accessed=4 * lay.n_main * width,
            transcendentals=lay.n_main * lay.n_main,
        ),
    )(*arrays)
    return out


def fast_unpack_kernel(values_ref, pos_ref, out_ref):
    pos = pos_ref[...]
    lane = lax.rem(pos, LANES)
    line = lax.div(pos, LANES)
    out = jnp.zeros(pos.shape, jnp.float32)
    per = values_ref.shape[2] // LANES
    for r in range(values_ref.shape[0] * per):
        start = r % per * LANES
        table = jnp.broadcast_to(values_ref[r // per, :, start : start + LANES], pos.shape)
        found = jnp.take_along_axis(table, lane, axis=1)
        out = jnp.where(line == r, found, out)
    out_ref[...] = out


def fast_unpack(values, pos):
    vmem = pl.BlockSpec(memory_space=pltpu.VMEM)
    return pl.pallas_call(
        fast_unpack_kernel,
        out_shape=jax.ShapeDtypeStruct(pos.shape, jnp.float32),
        in_specs=[vmem, vmem],
        out_specs=vmem,
    )(values, pos)


def general(embeddings, labels, owner_map):
    n_owner = lax.axis_size("cl")
    capacity = SLOTS // n_owner
    rows, width = embeddings.shape
    packed, pos, counts = pack(embeddings, labels, owner_map, n_owner, capacity)
    counts = lax.all_gather(counts, ("cl", "grp"), tiled=True)
    mine = lax.all_to_all(
        packed.reshape(n_owner, capacity, width), "cl", split_axis=0, concat_axis=0, tiled=True
    ).reshape(SLOTS, width)
    other = lax.ppermute(mine, "grp", [(0, 1), (1, 0)])
    results = log_counts(counts, mine, other, n_owner, capacity)
    returned = lax.all_to_all(
        results.reshape(n_owner, capacity), "cl", split_axis=0, concat_axis=0, tiled=True
    )
    return unpack(returned.reshape(SLOTS), pos).reshape(rows)


def body(embeddings, labels, owner_map):
    n_owner = lax.axis_size("cl")
    capacity = SLOTS // n_owner
    rows, width = embeddings.shape
    n_fine = owner_map.shape[0]
    main = -(-(rows // n_owner * 9 // 8) // 16) * 16
    if main >= capacity or n_fine >= LANES:
        return general(embeddings, labels, owner_map)
    planes = n_owner // 2
    plane = planes // 2 - 1
    home = 2 * plane
    lay = Layout(n_owner, n_fine, capacity, main, home)
    unit, slot, info, extra, pos = place_rows(embeddings, labels, owner_map, lay)
    moved = lax.ppermute(extra, "cl", [(2 * z + 1, 2 * z) for z in range(planes)])
    both = jnp.concatenate([extra, moved], axis=0)
    packed = after(pack_main(unit, slot, info, lay), both)
    mine = lax.all_to_all(
        packed.reshape(n_owner, main, width), "cl", split_axis=0, concat_axis=0, tiled=True
    ).reshape(n_owner * main, width)
    rest = jnp.concatenate(
        [
            both if z == plane else lax.ppermute(both, "cl", [(2 * z, home)])
            for z in range(planes)
        ],
        axis=0,
    )
    other = lax.ppermute(mine, "grp", [(0, 1), (1, 0)])
    rest_other = lax.ppermute(
        rest, ("cl", "grp"), [(2 * home, 2 * home + 1), (2 * home + 1, 2 * home)]
    )
    row = jax.ShapeDtypeStruct((1, lay.n_main), jnp.float32)
    long_row = jax.ShapeDtypeStruct((1, lay.n_head + lay.n_rest), jnp.float32)
    flag = jax.ShapeDtypeStruct((8, LANES), jnp.int32)
    table = jax.ShapeDtypeStruct((n_owner, 1, capacity), jnp.float32)
    sums, main_lane = pair_call(inner_kernel, lay, (mine,), (row, row), lay.n_main, 1)
    sums, unfit = pair_call(
        cross_kernel, lay, (mine, other, sums, main_lane), (row, flag), lay.n_main, 2
    )
    lines = lay.n_head + lay.n_rest
    rest_sums, lane = pair_call(
        inner_rest_kernel, lay, (mine, rest), (long_row, long_row), lines, 1
    )
    (results,) = pair_call(
        cross_rest_kernel,
        lay,
        (mine, rest, other, rest_other, sums, main_lane, rest_sums, lane),
        (table,),
        lines,
        2,
        (pltpu.VMEM(long_row.shape, jnp.float32),),
    )
    returned = lax.all_to_all(results, "cl", split_axis=0, concat_axis=0, tiled=True)
    return lax.cond(
        unfit[0, 0] == 0,
        lambda: fast_unpack(returned, pos).reshape(rows),
        lambda: general(embeddings, labels, owner_map),
    )


def solution(mesh):
    return jax.shard_map(
        body,
        mesh=mesh,
        in_specs=(P(("parts", "cl", "grp"), None), P(("parts", "cl", "grp")), P("parts")),
        out_specs=P(("parts", "cl", "grp")),
        check_vma=False,
    )
```

```python
import functools
import math

import jax
import jax.numpy as jnp
from jax import lax
from jax.experimental import pallas as pl
from jax.experimental.pallas import tpu as pltpu
from jax.sharding import PartitionSpec as P

SLOTS = 2048

temper = 0.2
neighbour_factor = 0.5
epsilon = 1e-06

LANES = 128
SCALE = math.log2(math.e) / temper
NEIGHBOUR = math.log2(neighbour_factor)
DEAD = -1e30
VMEM_LIMIT = 48 * 1024 * 1024
FAST_LIMIT = 40 * 1024 * 1024
WIDE = 512
INFO = 16


def column_of(row):
    pieces = []
    for start in range(0, row.shape[1], LANES):
        width = min(LANES, row.shape[1] - start)
        shape = (width, width)
        diagonal = lax.broadcasted_iota(jnp.int32, shape, 0) == lax.broadcasted_iota(
            jnp.int32, shape, 1
        )
        piece = jnp.broadcast_to(row[:, start : start + width], shape)
        pieces.append(jnp.sum(jnp.where(diagonal, piece, 0.0), axis=1, keepdims=True))
    return jnp.concatenate(pieces, axis=0)


def row_of(column):
    n = column.shape[0]
    diagonal = lax.broadcasted_iota(jnp.int32, (n, n), 0) == lax.broadcasted_iota(
        jnp.int32, (n, n), 1
    )
    return jnp.sum(jnp.where(diagonal, column, 0.0), axis=0, keepdims=True)


def pack_kernel(n_owner, capacity, x_ref, lab_ref, map_ref, out_ref, pos_ref, cnt_ref, unit, pos_row):
    rows = x_ref.shape[0]
    n_fine = map_ref.shape[1]
    per_owner = n_fine // n_owner
    owner_row = map_ref[...].astype(jnp.float32)
    fine_row = lax.broadcasted_iota(jnp.int32, (1, n_fine), 1).astype(jnp.float32)
    key_row = owner_row * n_fine + fine_row
    key_col = column_of(key_row)
    sorted_col = jnp.sum(jnp.where(key_row < key_col, 1.0, 0.0), axis=1, keepdims=True)
    lab = lab_ref[...].astype(jnp.float32)
    lab_row = jnp.concatenate([lab[b : b + 1, :] for b in range(lab.shape[0])], axis=1)
    fine_col = lax.broadcasted_iota(jnp.int32, (n_fine, rows), 0).astype(jnp.float32)
    fine_id = jnp.sum(jnp.where(fine_col == lab_row, sorted_col, 0.0), axis=0, keepdims=True)
    counts_col = jnp.sum(jnp.where(fine_col == fine_id, 1.0, 0.0), axis=1, keepdims=True)
    cnt_ref[...] = row_of(counts_col).astype(jnp.int32)
    coarse = jnp.floor((fine_id + 0.5) * (1.0 / per_owner))
    before = jnp.sum(
        jnp.where(fine_col < coarse * per_owner, counts_col, 0.0), axis=0, keepdims=True
    )
    index = lax.broadcasted_iota(jnp.int32, (1, rows), 1).astype(jnp.float32)
    row_key = fine_id * rows + index
    rank = jnp.zeros((1, rows), jnp.float32)
    for start in range(0, rows, LANES):
        other = column_of(row_key[:, start : start + LANES])
        rank = rank + jnp.sum(jnp.where(other < row_key, 1.0, 0.0), axis=0, keepdims=True)
    pos = (coarse * capacity + rank - before).astype(jnp.int32)
    pos_row[...] = pos
    pos_ref[...] = jnp.concatenate(
        [pos[:, start : start + LANES] for start in range(0, rows, LANES)], axis=0
    )
    x = x_ref[...].astype(jnp.float32)
    squares = jnp.sum(x * x, axis=1, keepdims=True)
    unit[...] = (x * lax.rsqrt(squares + epsilon)).astype(jnp.bfloat16)

    step = 256

    @pl.loop(0, out_ref.shape[0] // step)
    def _(block):
        slot = lax.broadcasted_iota(jnp.int32, (step, rows), 0) + block * step
        chosen = jnp.where(slot == pos_row[...], 1.0, 0.0).astype(jnp.bfloat16)
        packed = jnp.dot(chosen, unit[...], preferred_element_type=jnp.float32)
        out_ref[pl.ds(pl.multiple_of(block * step, step), step), :] = packed.astype(jnp.bfloat16)


def pack(embeddings, labels, owner_map, n_owner, capacity):
    rows, width = embeddings.shape
    n_fine = owner_map.shape[0]
    total = n_owner * capacity
    vmem = pl.BlockSpec(memory_space=pltpu.VMEM)
    return pl.pallas_call(
        functools.partial(pack_kernel, n_owner, capacity),
        out_shape=(
            jax.ShapeDtypeStruct((total, width), jnp.bfloat16),
            jax.ShapeDtypeStruct((rows // LANES, LANES), jnp.int32),
            jax.ShapeDtypeStruct((1, n_fine), jnp.int32),
        ),
        in_specs=[vmem] * 3,
        out_specs=(vmem, vmem, vmem),
        scratch_shapes=[pltpu.VMEM((rows, width), jnp.bfloat16), pltpu.VMEM((1, rows), jnp.int32)],
        compiler_params=pltpu.CompilerParams(vmem_limit_bytes=VMEM_LIMIT),
    )(embeddings, labels.reshape(rows // LANES, LANES), owner_map.reshape(1, n_fine))


def counts_kernel(n_owner, capacity, cnt_ref, mine_ref, other_ref, out_ref, lab_lane, lab_sub, bias):
    total = mine_ref.shape[0]
    per_owner = cnt_ref.shape[1] // n_owner
    me = lax.axis_index("cl")
    grp = lax.axis_index("grp")
    n_grp = lax.axis_size("grp")
    for member in range(2):
        for source in range(n_owner):
            line = source * n_grp + lax.rem(grp + member, n_grp)
            edges = []
            edge = jnp.int32(0)
            for f in range(per_owner):
                edge = edge + cnt_ref[line, me * per_owner + f]
                edges.append(edge)
            down = lax.broadcasted_iota(jnp.int32, (capacity, LANES), 0)
            label = jnp.zeros((capacity, LANES), jnp.int32)
            for edge in edges:
                label = label + jnp.where(down >= edge, 1, 0)
            start = (member * n_owner + source) * capacity
            lab_sub[start : start + capacity, :] = label
            bias[start : start + capacity, :] = jnp.where(
                label < per_owner, NEIGHBOUR - SCALE, DEAD
            )
            if member == 0:
                across = lax.broadcasted_iota(jnp.int32, (1, capacity), 1)
                label = jnp.zeros((1, capacity), jnp.int32)
                for edge in edges:
                    label = label + jnp.where(across >= edge, 1, 0)
                lab_lane[:, source * capacity : (source + 1) * capacity] = jnp.where(
                    label < per_owner, label, -1
                )
    wide, deep = min(512, total), min(256, total)

    @pl.loop(0, total // wide)
    def _(block):
        columns = pl.ds(pl.multiple_of(block * wide, wide), wide)
        rows_i = mine_ref[columns, :]
        label_i = lab_lane[:, columns]

        def add(ref, offset):
            def step(j, acc):
                start = pl.multiple_of(j * deep, deep)
                scores = lax.dot_general(
                    ref[pl.ds(start, deep), :],
                    rows_i,
                    (((1,), (1,)), ((), ())),
                    preferred_element_type=jnp.float32,
                )
                place = pl.ds(pl.multiple_of(start + offset, deep), deep)
                label_j = lab_sub[place, :]
                bias_j = bias[place, :]
                repeat = wide // LANES
                label_j = jnp.concatenate([label_j] * repeat, axis=1)
                bias_j = jnp.concatenate([bias_j] * repeat, axis=1)
                shift = jnp.where(label_j == label_i, -SCALE, bias_j)
                terms = jnp.exp2(scores * SCALE + shift)
                return acc + jnp.sum(terms.reshape(deep // 8, 8, wide), axis=0)

            return step

        acc = jnp.zeros((8, wide), jnp.float32)
        acc = lax.fori_loop(0, total // deep, add(mine_ref, 0), acc, unroll=2)
        acc = lax.fori_loop(0, total // deep, add(other_ref, total), acc, unroll=2)
        totals = jnp.sum(acc, axis=0, keepdims=True)
        out_ref[:, columns] = jnp.log(jnp.where(label_i >= 0, totals, 1.0))


def log_counts(counts, mine, other, n_owner, capacity):
    total = mine.shape[0]
    vmem = pl.BlockSpec(memory_space=pltpu.VMEM)
    return pl.pallas_call(
        functools.partial(counts_kernel, n_owner, capacity),
        out_shape=jax.ShapeDtypeStruct((1, total), jnp.float32),
        in_specs=[pl.BlockSpec(memory_space=pltpu.SMEM), vmem, vmem],
        out_specs=vmem,
        scratch_shapes=[
            pltpu.VMEM((1, total), jnp.int32),
            pltpu.VMEM((2 * total, LANES), jnp.int32),
            pltpu.VMEM((2 * total, LANES), jnp.float32),
        ],
        compiler_params=pltpu.CompilerParams(vmem_limit_bytes=VMEM_LIMIT),
    )(counts, mine, other)


def unpack_kernel(values_ref, pos_ref, out_ref):
    pos = pos_ref[...]
    lane = lax.rem(pos, LANES)
    line = lax.div(pos, LANES)
    out = jnp.zeros(pos.shape, jnp.float32)
    for r in range(values_ref.shape[0]):
        table = jnp.broadcast_to(values_ref[r : r + 1, :], pos.shape)
        found = jnp.take_along_axis(table, lane, axis=1)
        out = jnp.where(line == r, found, out)
    out_ref[...] = out


def unpack(values, pos):
    vmem = pl.BlockSpec(memory_space=pltpu.VMEM)
    return pl.pallas_call(
        unpack_kernel,
        out_shape=jax.ShapeDtypeStruct(pos.shape, jnp.float32),
        in_specs=[vmem, vmem],
        out_specs=vmem,
    )(values.reshape(-1, LANES), pos)


def swapped(x, first, second):
    return jnp.where(x == first, second, jnp.where(x == second, first, x))


def place_kernel(lay, x_hbm, lab_hbm, map_hbm, *refs):
    n_owner, capacity, main, home = lay.n_owner, lay.capacity, lay.main, lay.home
    unit, slot_ref, info_ref, extra_ref, pos_ref, x_ref, lab_ref, map_ref, sems = refs
    copies = [
        pltpu.make_async_copy(src, dst, sems.at[i])
        for i, (src, dst) in enumerate(((x_hbm, x_ref), (lab_hbm, lab_ref), (map_hbm, map_ref)))
    ]
    for copy in copies:
        copy.start()
    rows = x_ref.shape[0]
    n_fine = map_ref.shape[1]
    per_owner = n_fine // n_owner
    copies[1].wait()
    copies[2].wait()
    owner_row = map_ref[...].astype(jnp.float32)
    fine_row = lax.broadcasted_iota(jnp.int32, (1, n_fine), 1).astype(jnp.float32)
    key_row = owner_row * n_fine + fine_row
    key_col = column_of(key_row)
    sorted_col = jnp.sum(jnp.where(key_row < key_col, 1.0, 0.0), axis=1, keepdims=True)
    lab = lab_ref[...].astype(jnp.float32)
    lab_row = jnp.concatenate([lab[b : b + 1, :] for b in range(lab.shape[0])], axis=1)
    fine_col = lax.broadcasted_iota(jnp.int32, (n_fine, rows), 0).astype(jnp.float32)
    fine_id = jnp.sum(jnp.where(fine_col == lab_row, sorted_col, 0.0), axis=0, keepdims=True)
    counts_col = jnp.sum(jnp.where(fine_col == fine_id, 1.0, 0.0), axis=1, keepdims=True)
    coarse = jnp.floor((fine_id + 0.5) * (1.0 / per_owner))
    first = coarse * per_owner
    before = jnp.sum(jnp.where(fine_col < first, counts_col, 0.0), axis=0, keepdims=True)
    upto = jnp.sum(jnp.where(fine_col < first + per_owner, counts_col, 0.0), axis=0, keepdims=True)
    full = jnp.min(
        jnp.where(upto - before == capacity, coarse, float(n_owner)), axis=1, keepdims=True
    )
    line = lax.broadcasted_iota(jnp.int32, (n_fine, LANES), 0)
    lane = lax.broadcasted_iota(jnp.int32, (n_fine, LANES), 1)
    inside = (line <= lane) & (lax.div(line, per_owner) == lax.div(lane, per_owner))
    running = jnp.sum(jnp.where(inside, counts_col, 0.0), axis=0, keepdims=True)
    info = jnp.where(lane[:1] < n_fine, running, full)
    info_ref[...] = info
    index = lax.broadcasted_iota(jnp.int32, (1, rows), 1).astype(jnp.float32)
    row_key = fine_id * rows + index
    rank = jnp.zeros((1, rows), jnp.float32)
    for start in range(0, rows, LANES):
        other = column_of(row_key[:, start : start + LANES])
        rank = rank + jnp.sum(jnp.where(other < row_key, 1.0, 0.0), axis=0, keepdims=True)
    rank = (rank - before).astype(jnp.int32)
    place = swapped(coarse.astype(jnp.int32), full.astype(jnp.int32), home)
    table = place * capacity + rank
    pos_ref[...] = jnp.concatenate(
        [table[:, start : start + LANES] for start in range(0, rows, LANES)], axis=0
    )
    later = jnp.where(place == home, lay.n_main + rank - lay.head, -1)
    fits = rank < jnp.where(place == home, lay.head, main - 1)
    slot = jnp.where(fits, place * main + rank, later)
    slot_ref[...] = slot
    copies[0].wait()
    x = x_ref[...].astype(jnp.float32)
    squares = jnp.sum(x * x, axis=1, keepdims=True)
    unit[...] = (x * lax.rsqrt(squares + epsilon)).astype(jnp.bfloat16)
    extra_ref[...] = chosen_rows(unit, slot, lay.n_main, lay.rest)


def chosen_rows(unit, slot, start, count):
    here = lax.broadcasted_iota(jnp.int32, (count, unit.shape[0]), 0) + start
    chosen = jnp.where(here == slot, 1.0, 0.0).astype(jnp.bfloat16)
    return jnp.dot(chosen, unit[...], preferred_element_type=jnp.float32).astype(jnp.bfloat16)


def main_kernel(lay, unit, slot_ref, info_ref, main_ref):
    count = lay.n_main // 4
    for start in range(0, lay.n_main, count):
        main_ref[start : start + count, :] = chosen_rows(unit, slot_ref[...], start, count)
    for owner in range(lay.n_owner):
        tail = slice((owner + 1) * lay.main - INFO, (owner + 1) * lay.main)
        old = main_ref[tail, :LANES].astype(jnp.float32)
        down = lax.broadcasted_iota(jnp.int32, old.shape, 0)
        new = jnp.where(down == INFO - 1, info_ref[...], old)
        main_ref[tail, :LANES] = new.astype(jnp.bfloat16)


def vmem_specs(count):
    return (pl.BlockSpec(memory_space=pltpu.VMEM),) * count


def place_rows(embeddings, labels, owner_map, lay):
    rows, width = embeddings.shape
    n_fine = owner_map.shape[0]
    lab_shape = (rows // LANES, LANES)
    return pl.pallas_call(
        functools.partial(place_kernel, lay),
        out_shape=(
            jax.ShapeDtypeStruct((rows, width), jnp.bfloat16),
            jax.ShapeDtypeStruct((1, rows), jnp.int32),
            jax.ShapeDtypeStruct((1, LANES), jnp.float32),
            jax.ShapeDtypeStruct((lay.rest, width), jnp.bfloat16),
            jax.ShapeDtypeStruct(lab_shape, jnp.int32),
        ),
        in_specs=[pl.BlockSpec(memory_space=pl.ANY)] * 3,
        out_specs=vmem_specs(5),
        scratch_shapes=[
            pltpu.VMEM((rows, width), jnp.bfloat16),
            pltpu.VMEM(lab_shape, jnp.int32),
            pltpu.VMEM((1, n_fine), jnp.int32),
            pltpu.SemaphoreType.DMA((3,)),
        ],
        compiler_params=pltpu.CompilerParams(vmem_limit_bytes=FAST_LIMIT),
    )(embeddings, labels.reshape(lab_shape), owner_map.reshape(1, n_fine))


def pack_main(unit, slot, info, lay):
    return pl.pallas_call(
        functools.partial(main_kernel, lay),
        out_shape=jax.ShapeDtypeStruct((lay.n_main, unit.shape[1]), jnp.bfloat16),
        in_specs=list(vmem_specs(3)),
        out_specs=vmem_specs(1)[0],
        compiler_params=pltpu.CompilerParams(vmem_limit_bytes=FAST_LIMIT),
        cost_estimate=pl.CostEstimate(
            flops=2 * lay.n_main * unit.shape[0] * unit.shape[1],
            bytes_accessed=4 * unit.shape[0] * unit.shape[1],
            transcendentals=0,
        ),
    )(unit, slot, info)


def pair_up_kernel(packed_in, extra, moved, packed, both):
    rows = extra.shape[0]
    both[:rows, :] = extra[...]
    both[rows:, :] = moved[...]


def pair_up(packed, extra, moved):
    return pl.pallas_call(
        pair_up_kernel,
        out_shape=(
            jax.ShapeDtypeStruct(packed.shape, packed.dtype),
            jax.ShapeDtypeStruct((2 * extra.shape[0], extra.shape[1]), extra.dtype),
        ),
        in_specs=list(vmem_specs(3)),
        out_specs=vmem_specs(2),
        input_output_aliases={0: 0},
        compiler_params=pltpu.CompilerParams(vmem_limit_bytes=FAST_LIMIT),
    )(packed, extra, moved)


def gate_kernel(*refs):
    pass


def after(arrays, sums):
    anywhere = pl.BlockSpec(memory_space=pl.ANY)
    return pl.pallas_call(
        gate_kernel,
        out_shape=tuple(jax.ShapeDtypeStruct(x.shape, x.dtype) for x in arrays),
        in_specs=[anywhere] * (len(arrays) + 1),
        out_specs=(anywhere,) * len(arrays),
        input_output_aliases={i: i for i in range(len(arrays))},
    )(*arrays, sums)


class Layout:
    def __init__(self, n_owner, n_fine, capacity, main, home):
        self.n_owner, self.n_fine, self.capacity = n_owner, n_fine, capacity
        self.main, self.home = main, home
        self.head = main - INFO
        self.rest = capacity - self.head
        self.per_owner = n_fine // n_owner
        self.planes = n_owner // 2
        self.n_main = n_owner * main
        self.n_head = n_owner * self.head
        self.n_rest = n_owner * self.rest


def info_line(lay, main_ref, source):
    end = (source + 1) * lay.main
    return main_ref[end - INFO : end, :LANES].astype(jnp.float32)[INFO - 1 :]


def lines_of(lay, main_ref):
    return [info_line(lay, main_ref, source) for source in range(lay.n_owner)]


def hot_of(lay, info):
    lane = lax.broadcasted_iota(jnp.int32, (1, LANES), 1)
    hot = jnp.max(jnp.where(lane == lay.n_fine, info, 0.0), axis=1, keepdims=True)
    return hot.astype(jnp.int32)


def write_labels(lay, infos, first, count, at, lab_sub, bias):
    cluster = swapped(lax.axis_index("cl"), hot_of(lay, infos[0]), lay.home)
    lane = lax.broadcasted_iota(jnp.int32, (1, LANES), 1)
    is_edge = lax.div(lane, lay.per_owner) == cluster
    for source, info in enumerate(infos):
        edges = jnp.where(is_edge, info, 2.0 * lay.capacity)
        slot = lax.broadcasted_iota(jnp.int32, (count, LANES), 0) + first
        label = jnp.where(slot.astype(jnp.float32) >= edges, 1.0, 0.0)
        label = jnp.broadcast_to(jnp.sum(label, axis=1, keepdims=True), (count, LANES))
        start = at + source * count
        lab_sub[start : start + count, :] = label
        if bias is not None:
            bias[start : start + count, :] = jnp.where(
                label < lay.per_owner, NEIGHBOUR - SCALE, DEAD
            )


def turn_labels(lay, lab_sub, start, count, lab_lane, at):
    for i in range(0, count, LANES):
        block = jnp.transpose(lab_sub[start + i : start + i + LANES, :])[:1]
        lab_lane[:, at + i : at + i + LANES] = jnp.where(block < lay.per_owner, block, -1.0)


def copy_head(lay, main_ref, rows):
    for source in range(lay.n_owner):
        rows[source * lay.head : (source + 1) * lay.head, :] = main_ref[
            source * lay.main : source * lay.main + lay.head, :
        ]


def pieces(start, count, parts):
    return [(start + i * (count // parts), count // parts) for i in range(parts)]


def stream(rows_i, first, count, tiles, lab_lane, at, lab_sub, bias, buffers, put):
    step = 32
    tiles = [
        (ref, s, d, place + s - start)
        for ref, start, n, place, parts in tiles
        for s, d in pieces(start, n, parts)
    ]

    def scores_to(buffer, tile, rows):
        ref, start, deep, _ = tile
        buffer[:deep, : rows.shape[0]] = lax.dot_general(
            ref[start : start + deep, :],
            rows,
            (((1,), (1,)), ((), ())),
            preferred_element_type=jnp.float32,
        )

    def run(start, blocks, wide):
        repeat = wide // LANES

        def rows_of(block):
            return rows_i[pl.ds(pl.multiple_of(first + start + block * wide, LANES), wide), :]

        scores_to(buffers[0], tiles[0], rows_of(0))

        def body(block, carry):
            here = rows_of(block)
            place = pl.ds(pl.multiple_of(at + start + block * wide, LANES), wide)
            label_i = lab_lane[:, place]
            acc = jnp.zeros((8, wide), jnp.float32)
            for i, (_, _, deep, line) in enumerate(tiles):
                if i + 1 < len(tiles):
                    scores_to(buffers[(i + 1) % 2], tiles[i + 1], here)
                else:
                    scores_to(buffers[0], tiles[0], rows_of(jnp.minimum(block + 1, blocks - 1)))
                buffer = buffers[i % 2]
                for c in range(0, deep, step):
                    part = slice(line + c, line + c + step)
                    label_j = jnp.concatenate([lab_sub[part, :]] * repeat, axis=1)
                    if bias is None:
                        bias_j = NEIGHBOUR - SCALE
                    else:
                        bias_j = jnp.concatenate([bias[part, :]] * repeat, axis=1)
                    shift = jnp.where(label_j == label_i, -SCALE, bias_j)
                    terms = jnp.exp2(buffer[c : c + step, :wide] * SCALE + shift)
                    acc = acc + jnp.sum(terms.reshape(step // 8, 8, wide), axis=0)
            put(place, jnp.sum(acc, axis=0, keepdims=True))
            return carry

        lax.fori_loop(0, blocks, body, 0)

    wide = WIDE
    if count >= wide:
        run(0, count // wide, wide)
    if count % wide:
        run(count - count % wide, 1, count % wide)


def setter(ref):
    def put(place, values):
        ref[:, place] = values

    return put


def adder(ref):
    def put(place, values):
        ref[:, place] += values

    return put


def inner_kernel(lay, mine, sums, lab_lane, lab_sub, bias, rows, buf_a, buf_b):
    is_home = lax.axis_index("cl") == lay.home
    infos = lines_of(lay, mine)

    def work(ref, count, per, bias):
        write_labels(lay, infos, 0, per, 0, lab_sub, bias)
        turn_labels(lay, lab_sub, 0, count, lab_lane, 0)
        tiles = [(ref, 0, count, 0, 4)]
        stream(ref, 0, count, tiles, lab_lane, 0, lab_sub, bias, (buf_a, buf_b), setter(sums))

    @pl.when(is_home)
    def _():
        copy_head(lay, mine, rows)
        work(rows, lay.n_head, lay.head, None)

    @pl.when(jnp.logical_not(is_home))
    def _():
        work(mine, lay.n_main, lay.main, bias)


def cross_kernel(lay, mine, other, sums, lab_lane, total, unfit_ref, lab_sub, bias, rows, rows_j, buf_a, buf_b):
    is_home = lax.axis_index("cl") == lay.home
    infos = lines_of(lay, other)
    own = lines_of(lay, mine)
    hot = hot_of(lay, own[0])
    lane = lax.broadcasted_iota(jnp.int32, (1, LANES), 1)
    last = (lane < lay.n_fine) & (lax.rem(lane, lay.per_owner) == lay.per_owner - 1)
    last = last & (lax.div(lane, lay.per_owner) != hot)
    unfit = jnp.zeros((1, LANES), jnp.float32)
    for info in infos + own:
        wrong = last & (info >= lay.main)
        differs = (info != hot.astype(jnp.float32)) | (info >= lay.n_owner)
        wrong = wrong | ((lane == lay.n_fine) & differs)
        unfit = unfit + jnp.where(wrong, 1.0, 0.0)
    unfit_ref[...] = jnp.broadcast_to(
        jnp.max(unfit, axis=1, keepdims=True), unfit_ref.shape
    ).astype(jnp.int32)
    total[...] = sums[...]

    def work(ref, ref_j, count, per, bias):
        write_labels(lay, infos, 0, per, 0, lab_sub, bias)
        tiles = [(ref_j, 0, count, 0, 4)]
        stream(ref, 0, count, tiles, lab_lane, 0, lab_sub, bias, (buf_a, buf_b), adder(total))

    @pl.when(is_home)
    def _():
        copy_head(lay, mine, rows)
        copy_head(lay, other, rows_j)
        work(rows, rows_j, lay.n_head, lay.head, None)

    @pl.when(jnp.logical_not(is_home))
    def _():
        work(mine, other, lay.n_main, lay.main, bias)


def copy_all(lay, main_ref, rests, rows):
    copy_head(lay, main_ref, rows)
    for i, ref in enumerate(rests):
        start = lay.n_head + i * ref.shape[0]
        rows[start : start + ref.shape[0], :] = ref[...]


def rest_labels(lay, infos, lab_sub):
    write_labels(lay, infos, 0, lay.head, 0, lab_sub, None)
    write_labels(lay, infos, lay.head, lay.rest, lay.n_head, lab_sub, None)


def rest_pairs(lay, rows, rows_j, lab_lane, lab_sub, buffers, put):
    n_head, n_rest = lay.n_head, lay.n_rest
    seconds = (rows_j, n_head, n_rest, n_head, 4)
    mains = (rows_j, 0, n_head, 0, 4)
    stream(rows, 0, n_head, [seconds], lab_lane, 0, lab_sub, None, buffers, put)
    stream(rows, n_head, n_rest, [seconds, mains], lab_lane, n_head, lab_sub, None, buffers, put)


def inner_rest_kernel(lay, mine, *refs):
    rests = refs[: lay.planes]
    sums, lab_lane, lab_sub, rows, buf_a, buf_b = refs[lay.planes :]

    @pl.when(lax.axis_index("cl") == lay.home)
    def _():
        rest_labels(lay, lines_of(lay, mine), lab_sub)
        turn_labels(lay, lab_sub, 0, lay.n_head + lay.n_rest, lab_lane, 0)
        copy_all(lay, mine, rests, rows)
        rest_pairs(lay, rows, rows, lab_lane, lab_sub, (buf_a, buf_b), setter(sums))


def cross_rest_kernel(lay, mine, other, *refs):
    rests, refs = refs[: lay.planes], refs[lay.planes :]
    others, refs = refs[: lay.planes], refs[lay.planes :]
    main_sums, main_lane, sums, lab_lane, out_ref, lab_sub, rows, rows_j, total, buf_a, buf_b = refs
    is_home = lax.axis_index("cl") == lay.home

    @pl.when(is_home)
    def _():
        rest_labels(lay, lines_of(lay, other), lab_sub)
        copy_all(lay, mine, rests, rows)
        copy_all(lay, other, others, rows_j)
        total[...] = sums[...]
        total[:, : lay.n_head] += main_sums[:, : lay.n_head]
        rest_pairs(lay, rows, rows_j, lab_lane, lab_sub, (buf_a, buf_b), adder(total))
        values = jnp.log(total[...])
        for source in range(lay.n_owner):
            start = source * lay.head
            out_ref[source, :, : lay.head] = values[:, start : start + lay.head]
            start = lay.n_head + source * lay.rest
            out_ref[source, :, lay.head :] = values[:, start : start + lay.rest]

    @pl.when(jnp.logical_not(is_home))
    def _():
        values = jnp.log(jnp.where(main_lane[...] >= 0, main_sums[...], 1.0))
        for source in range(lay.n_owner):
            start = source * lay.main
            out_ref[source, :, : lay.main] = values[:, start : start + lay.main]


def pair_call(kernel, lay, arrays, out_shape, sides, joins, more=()):
    width = arrays[0].shape[1]
    side = pltpu.VMEM((sides[0], LANES), jnp.float32)
    rows = pltpu.VMEM((joins[0], width), jnp.bfloat16)
    buffer = pltpu.VMEM((lay.n_main // 4, WIDE), jnp.float32)
    out = pl.pallas_call(
        functools.partial(kernel, lay),
        out_shape=out_shape,
        in_specs=list(vmem_specs(len(arrays))),
        out_specs=vmem_specs(len(out_shape)),
        scratch_shapes=[side] * sides[1] + [rows] * joins[1] + list(more) + [buffer, buffer],
        compiler_params=pltpu.CompilerParams(vmem_limit_bytes=FAST_LIMIT),
        cost_estimate=pl.CostEstimate(
            flops=2 * lay.n_main * lay.n_main * width,
            bytes_accessed=4 * lay.n_main * width,
            transcendentals=lay.n_main * lay.n_main,
        ),
    )(*arrays)
    return out


def fast_unpack_kernel(values_ref, pos_ref, out_ref):
    pos = pos_ref[...]
    lane = lax.rem(pos, LANES)
    line = lax.div(pos, LANES)
    out = jnp.zeros(pos.shape, jnp.float32)
    per = values_ref.shape[2] // LANES
    for r in range(values_ref.shape[0] * per):
        start = r % per * LANES
        table = jnp.broadcast_to(values_ref[r // per, :, start : start + LANES], pos.shape)
        found = jnp.take_along_axis(table, lane, axis=1)
        out = jnp.where(line == r, found, out)
    out_ref[...] = out


def fast_unpack(values, pos):
    vmem = pl.BlockSpec(memory_space=pltpu.VMEM)
    return pl.pallas_call(
        fast_unpack_kernel,
        out_shape=jax.ShapeDtypeStruct(pos.shape, jnp.float32),
        in_specs=[vmem, vmem],
        out_specs=vmem,
    )(values, pos)


def general(embeddings, labels, owner_map):
    n_owner = lax.axis_size("cl")
    capacity = SLOTS // n_owner
    rows, width = embeddings.shape
    packed, pos, counts = pack(embeddings, labels, owner_map, n_owner, capacity)
    counts = lax.all_gather(counts, ("cl", "grp"), tiled=True)
    mine = lax.all_to_all(
        packed.reshape(n_owner, capacity, width), "cl", split_axis=0, concat_axis=0, tiled=True
    ).reshape(SLOTS, width)
    other = lax.ppermute(mine, "grp", [(0, 1), (1, 0)])
    results = log_counts(counts, mine, other, n_owner, capacity)
    returned = lax.all_to_all(
        results.reshape(n_owner, capacity), "cl", split_axis=0, concat_axis=0, tiled=True
    )
    return unpack(returned.reshape(SLOTS), pos).reshape(rows)


def body(embeddings, labels, owner_map):
    n_owner = lax.axis_size("cl")
    capacity = SLOTS // n_owner
    rows, width = embeddings.shape
    n_fine = owner_map.shape[0]
    main = -(-(rows // n_owner * 9 // 8) // 16) * 16
    if main >= capacity or n_fine >= LANES:
        return general(embeddings, labels, owner_map)
    planes = n_owner // 2
    plane = planes // 2 - 1
    home = 2 * plane
    lay = Layout(n_owner, n_fine, capacity, main, home)
    unit, slot, info, extra, pos = place_rows(embeddings, labels, owner_map, lay)
    moved = lax.ppermute(extra, "cl", [(2 * z + 1, 2 * z) for z in range(planes)])
    packed, both = pair_up(pack_main(unit, slot, info, lay), extra, moved)
    mine = lax.all_to_all(
        packed.reshape(n_owner, main, width), "cl", split_axis=0, concat_axis=0, tiled=True
    ).reshape(n_owner * main, width)
    far = [lax.ppermute(both, "cl", [(2 * z, home)]) for z in range(planes) if z != plane]
    other = lax.ppermute(mine, "grp", [(0, 1), (1, 0)])
    row = jax.ShapeDtypeStruct((1, lay.n_main), jnp.float32)
    lines = lay.n_head + lay.n_rest
    long_row = jax.ShapeDtypeStruct((1, lines), jnp.float32)
    flag = jax.ShapeDtypeStruct((8, LANES), jnp.int32)
    table = jax.ShapeDtypeStruct((n_owner, 1, capacity), jnp.float32)
    sides, joins = (lay.n_main, 2), (lay.n_head, 1)
    sums, main_lane = pair_call(inner_kernel, lay, (mine,), (row, row), sides, joins)
    joins = (lay.n_head, 2)
    sums, unfit = pair_call(
        cross_kernel, lay, (mine, other, sums, main_lane), (row, flag), sides, joins
    )
    far = list(after(far, sums))
    rests = far[:plane] + [both] + far[plane:]
    swap = [(2 * home, 2 * home + 1), (2 * home + 1, 2 * home)]
    rests_other = [lax.ppermute(x, ("cl", "grp"), swap) for x in rests]
    rest_sums, lane = pair_call(
        inner_rest_kernel, lay, (mine, *rests), (long_row, long_row), (lines, 1), (lines, 1)
    )
    arrays = (mine, other, *rests, *rests_other, sums, main_lane, rest_sums, lane)
    total = pltpu.VMEM(long_row.shape, jnp.float32)
    (results,) = pair_call(
        cross_rest_kernel, lay, arrays, (table,), (lines, 1), (lines, 2), (total,)
    )
    returned = lax.all_to_all(results, "cl", split_axis=0, concat_axis=0, tiled=True)
    return lax.cond(
        unfit[0, 0] == 0,
        lambda: fast_unpack(returned, pos).reshape(rows),
        lambda: general(embeddings, labels, owner_map),
    )


def solution(mesh):
    return jax.shard_map(
        body,
        mesh=mesh,
        in_specs=(P(("parts", "cl", "grp"), None), P(("parts", "cl", "grp")), P("parts")),
        out_specs=P(("parts", "cl", "grp")),
        check_vma=False,
    )
```

```python
import functools
import math

import jax
import jax.numpy as jnp
from jax import lax
from jax.experimental import pallas as pl
from jax.experimental.pallas import tpu as pltpu
from jax.sharding import PartitionSpec as P

SLOTS = 2048

temper = 0.2
neighbour_factor = 0.5
epsilon = 1e-06

LANES = 128
SCALE = math.log2(math.e) / temper
NEIGHBOUR = math.log2(neighbour_factor)
DEAD = -1e30
VMEM_LIMIT = 48 * 1024 * 1024
FAST_LIMIT = 20 * 1024 * 1024
WIDE = 512
INFO = 16


def column_of(row):
    pieces = []
    for start in range(0, row.shape[1], LANES):
        width = min(LANES, row.shape[1] - start)
        shape = (width, width)
        diagonal = lax.broadcasted_iota(jnp.int32, shape, 0) == lax.broadcasted_iota(
            jnp.int32, shape, 1
        )
        piece = jnp.broadcast_to(row[:, start : start + width], shape)
        pieces.append(jnp.sum(jnp.where(diagonal, piece, 0.0), axis=1, keepdims=True))
    return jnp.concatenate(pieces, axis=0)


def row_of(column):
    n = column.shape[0]
    diagonal = lax.broadcasted_iota(jnp.int32, (n, n), 0) == lax.broadcasted_iota(
        jnp.int32, (n, n), 1
    )
    return jnp.sum(jnp.where(diagonal, column, 0.0), axis=0, keepdims=True)


def pack_kernel(n_owner, capacity, x_ref, lab_ref, map_ref, out_ref, pos_ref, cnt_ref, unit, pos_row):
    rows = x_ref.shape[0]
    n_fine = map_ref.shape[1]
    per_owner = n_fine // n_owner
    owner_row = map_ref[...].astype(jnp.float32)
    fine_row = lax.broadcasted_iota(jnp.int32, (1, n_fine), 1).astype(jnp.float32)
    key_row = owner_row * n_fine + fine_row
    key_col = column_of(key_row)
    sorted_col = jnp.sum(jnp.where(key_row < key_col, 1.0, 0.0), axis=1, keepdims=True)
    lab = lab_ref[...].astype(jnp.float32)
    lab_row = jnp.concatenate([lab[b : b + 1, :] for b in range(lab.shape[0])], axis=1)
    fine_col = lax.broadcasted_iota(jnp.int32, (n_fine, rows), 0).astype(jnp.float32)
    fine_id = jnp.sum(jnp.where(fine_col == lab_row, sorted_col, 0.0), axis=0, keepdims=True)
    counts_col = jnp.sum(jnp.where(fine_col == fine_id, 1.0, 0.0), axis=1, keepdims=True)
    cnt_ref[...] = row_of(counts_col).astype(jnp.int32)
    coarse = jnp.floor((fine_id + 0.5) * (1.0 / per_owner))
    before = jnp.sum(
        jnp.where(fine_col < coarse * per_owner, counts_col, 0.0), axis=0, keepdims=True
    )
    index = lax.broadcasted_iota(jnp.int32, (1, rows), 1).astype(jnp.float32)
    row_key = fine_id * rows + index
    rank = jnp.zeros((1, rows), jnp.float32)
    for start in range(0, rows, LANES):
        other = column_of(row_key[:, start : start + LANES])
        rank = rank + jnp.sum(jnp.where(other < row_key, 1.0, 0.0), axis=0, keepdims=True)
    pos = (coarse * capacity + rank - before).astype(jnp.int32)
    pos_row[...] = pos
    pos_ref[...] = jnp.concatenate(
        [pos[:, start : start + LANES] for start in range(0, rows, LANES)], axis=0
    )
    x = x_ref[...].astype(jnp.float32)
    squares = jnp.sum(x * x, axis=1, keepdims=True)
    unit[...] = (x * lax.rsqrt(squares + epsilon)).astype(jnp.bfloat16)

    step = 256

    @pl.loop(0, out_ref.shape[0] // step)
    def _(block):
        slot = lax.broadcasted_iota(jnp.int32, (step, rows), 0) + block * step
        chosen = jnp.where(slot == pos_row[...], 1.0, 0.0).astype(jnp.bfloat16)
        packed = jnp.dot(chosen, unit[...], preferred_element_type=jnp.float32)
        out_ref[pl.ds(pl.multiple_of(block * step, step), step), :] = packed.astype(jnp.bfloat16)


def pack(embeddings, labels, owner_map, n_owner, capacity):
    rows, width = embeddings.shape
    n_fine = owner_map.shape[0]
    total = n_owner * capacity
    vmem = pl.BlockSpec(memory_space=pltpu.VMEM)
    return pl.pallas_call(
        functools.partial(pack_kernel, n_owner, capacity),
        out_shape=(
            jax.ShapeDtypeStruct((total, width), jnp.bfloat16),
            jax.ShapeDtypeStruct((rows // LANES, LANES), jnp.int32),
            jax.ShapeDtypeStruct((1, n_fine), jnp.int32),
        ),
        in_specs=[vmem] * 3,
        out_specs=(vmem, vmem, vmem),
        scratch_shapes=[pltpu.VMEM((rows, width), jnp.bfloat16), pltpu.VMEM((1, rows), jnp.int32)],
        compiler_params=pltpu.CompilerParams(vmem_limit_bytes=VMEM_LIMIT),
    )(embeddings, labels.reshape(rows // LANES, LANES), owner_map.reshape(1, n_fine))


def counts_kernel(n_owner, capacity, cnt_ref, mine_ref, other_ref, out_ref, lab_lane, lab_sub, bias):
    total = mine_ref.shape[0]
    per_owner = cnt_ref.shape[1] // n_owner
    me = lax.axis_index("cl")
    grp = lax.axis_index("grp")
    n_grp = lax.axis_size("grp")
    for member in range(2):
        for source in range(n_owner):
            line = source * n_grp + lax.rem(grp + member, n_grp)
            edges = []
            edge = jnp.int32(0)
            for f in range(per_owner):
                edge = edge + cnt_ref[line, me * per_owner + f]
                edges.append(edge)
            down = lax.broadcasted_iota(jnp.int32, (capacity, LANES), 0)
            label = jnp.zeros((capacity, LANES), jnp.int32)
            for edge in edges:
                label = label + jnp.where(down >= edge, 1, 0)
            start = (member * n_owner + source) * capacity
            lab_sub[start : start + capacity, :] = label
            bias[start : start + capacity, :] = jnp.where(
                label < per_owner, NEIGHBOUR - SCALE, DEAD
            )
            if member == 0:
                across = lax.broadcasted_iota(jnp.int32, (1, capacity), 1)
                label = jnp.zeros((1, capacity), jnp.int32)
                for edge in edges:
                    label = label + jnp.where(across >= edge, 1, 0)
                lab_lane[:, source * capacity : (source + 1) * capacity] = jnp.where(
                    label < per_owner, label, -1
                )
    wide, deep = min(512, total), min(256, total)

    @pl.loop(0, total // wide)
    def _(block):
        columns = pl.ds(pl.multiple_of(block * wide, wide), wide)
        rows_i = mine_ref[columns, :]
        label_i = lab_lane[:, columns]

        def add(ref, offset):
            def step(j, acc):
                start = pl.multiple_of(j * deep, deep)
                scores = lax.dot_general(
                    ref[pl.ds(start, deep), :],
                    rows_i,
                    (((1,), (1,)), ((), ())),
                    preferred_element_type=jnp.float32,
                )
                place = pl.ds(pl.multiple_of(start + offset, deep), deep)
                label_j = lab_sub[place, :]
                bias_j = bias[place, :]
                repeat = wide // LANES
                label_j = jnp.concatenate([label_j] * repeat, axis=1)
                bias_j = jnp.concatenate([bias_j] * repeat, axis=1)
                shift = jnp.where(label_j == label_i, -SCALE, bias_j)
                terms = jnp.exp2(scores * SCALE + shift)
                return acc + jnp.sum(terms.reshape(deep // 8, 8, wide), axis=0)

            return step

        acc = jnp.zeros((8, wide), jnp.float32)
        acc = lax.fori_loop(0, total // deep, add(mine_ref, 0), acc, unroll=2)
        acc = lax.fori_loop(0, total // deep, add(other_ref, total), acc, unroll=2)
        totals = jnp.sum(acc, axis=0, keepdims=True)
        out_ref[:, columns] = jnp.log(jnp.where(label_i >= 0, totals, 1.0))


def log_counts(counts, mine, other, n_owner, capacity):
    total = mine.shape[0]
    vmem = pl.BlockSpec(memory_space=pltpu.VMEM)
    return pl.pallas_call(
        functools.partial(counts_kernel, n_owner, capacity),
        out_shape=jax.ShapeDtypeStruct((1, total), jnp.float32),
        in_specs=[pl.BlockSpec(memory_space=pltpu.SMEM), vmem, vmem],
        out_specs=vmem,
        scratch_shapes=[
            pltpu.VMEM((1, total), jnp.int32),
            pltpu.VMEM((2 * total, LANES), jnp.int32),
            pltpu.VMEM((2 * total, LANES), jnp.float32),
        ],
        compiler_params=pltpu.CompilerParams(vmem_limit_bytes=VMEM_LIMIT),
    )(counts, mine, other)


def unpack_kernel(values_ref, pos_ref, out_ref):
    pos = pos_ref[...]
    lane = lax.rem(pos, LANES)
    line = lax.div(pos, LANES)
    out = jnp.zeros(pos.shape, jnp.float32)
    for r in range(values_ref.shape[0]):
        table = jnp.broadcast_to(values_ref[r : r + 1, :], pos.shape)
        found = jnp.take_along_axis(table, lane, axis=1)
        out = jnp.where(line == r, found, out)
    out_ref[...] = out


def unpack(values, pos):
    vmem = pl.BlockSpec(memory_space=pltpu.VMEM)
    return pl.pallas_call(
        unpack_kernel,
        out_shape=jax.ShapeDtypeStruct(pos.shape, jnp.float32),
        in_specs=[vmem, vmem],
        out_specs=vmem,
    )(values.reshape(-1, LANES), pos)


def swapped(x, first, second):
    return jnp.where(x == first, second, jnp.where(x == second, first, x))


def place_kernel(lay, x_hbm, lab_hbm, map_hbm, *refs):
    n_owner, capacity, main, home = lay.n_owner, lay.capacity, lay.main, lay.home
    unit, slot_ref, info_ref, extra_ref, pos_ref, x_ref, lab_ref, map_ref, sems = refs
    copies = [
        pltpu.make_async_copy(src, dst, sems.at[i])
        for i, (src, dst) in enumerate(((x_hbm, x_ref), (lab_hbm, lab_ref), (map_hbm, map_ref)))
    ]
    for copy in copies:
        copy.start()
    rows = x_ref.shape[0]
    n_fine = map_ref.shape[1]
    per_owner = n_fine // n_owner
    copies[1].wait()
    copies[2].wait()
    owner_row = map_ref[...].astype(jnp.float32)
    fine_row = lax.broadcasted_iota(jnp.int32, (1, n_fine), 1).astype(jnp.float32)
    key_row = owner_row * n_fine + fine_row
    key_col = column_of(key_row)
    sorted_col = jnp.sum(jnp.where(key_row < key_col, 1.0, 0.0), axis=1, keepdims=True)
    lab = lab_ref[...].astype(jnp.float32)
    lab_row = jnp.concatenate([lab[b : b + 1, :] for b in range(lab.shape[0])], axis=1)
    fine_col = lax.broadcasted_iota(jnp.int32, (n_fine, rows), 0).astype(jnp.float32)
    fine_id = jnp.sum(jnp.where(fine_col == lab_row, sorted_col, 0.0), axis=0, keepdims=True)
    counts_col = jnp.sum(jnp.where(fine_col == fine_id, 1.0, 0.0), axis=1, keepdims=True)
    coarse = jnp.floor((fine_id + 0.5) * (1.0 / per_owner))
    first = coarse * per_owner
    before = jnp.sum(jnp.where(fine_col < first, counts_col, 0.0), axis=0, keepdims=True)
    upto = jnp.sum(jnp.where(fine_col < first + per_owner, counts_col, 0.0), axis=0, keepdims=True)
    full = jnp.min(
        jnp.where(upto - before == capacity, coarse, float(n_owner)), axis=1, keepdims=True
    )
    line = lax.broadcasted_iota(jnp.int32, (n_fine, LANES), 0)
    lane = lax.broadcasted_iota(jnp.int32, (n_fine, LANES), 1)
    inside = (line <= lane) & (lax.div(line, per_owner) == lax.div(lane, per_owner))
    running = jnp.sum(jnp.where(inside, counts_col, 0.0), axis=0, keepdims=True)
    info = jnp.where(lane[:1] < n_fine, running, full)
    info_ref[...] = info
    index = lax.broadcasted_iota(jnp.int32, (1, rows), 1).astype(jnp.float32)
    row_key = fine_id * rows + index
    rank = jnp.zeros((1, rows), jnp.float32)
    for start in range(0, rows, LANES):
        other = column_of(row_key[:, start : start + LANES])
        rank = rank + jnp.sum(jnp.where(other < row_key, 1.0, 0.0), axis=0, keepdims=True)
    rank = (rank - before).astype(jnp.int32)
    place = swapped(coarse.astype(jnp.int32), full.astype(jnp.int32), home)
    table = place * capacity + rank
    pos_ref[...] = jnp.concatenate(
        [table[:, start : start + LANES] for start in range(0, rows, LANES)], axis=0
    )
    later = jnp.where(place == home, lay.n_main + rank - lay.head, -1)
    fits = rank < jnp.where(place == home, lay.head, main - 1)
    slot = jnp.where(fits, place * main + rank, later)
    slot_ref[...] = slot
    copies[0].wait()
    x = x_ref[...].astype(jnp.float32)
    squares = jnp.sum(x * x, axis=1, keepdims=True)
    unit[...] = (x * lax.rsqrt(squares + epsilon)).astype(jnp.bfloat16)
    extra_ref[...] = chosen_rows(unit, slot, lay.n_main, lay.rest)


def chosen_rows(unit, slot, start, count):
    here = lax.broadcasted_iota(jnp.int32, (count, unit.shape[0]), 0) + start
    chosen = jnp.where(here == slot, 1.0, 0.0).astype(jnp.bfloat16)
    return jnp.dot(chosen, unit[...], preferred_element_type=jnp.float32).astype(jnp.bfloat16)


def main_kernel(lay, unit, slot_ref, info_ref, main_ref):
    count = lay.n_main // 4
    for start in range(0, lay.n_main, count):
        main_ref[start : start + count, :] = chosen_rows(unit, slot_ref[...], start, count)
    for owner in range(lay.n_owner):
        tail = slice((owner + 1) * lay.main - INFO, (owner + 1) * lay.main)
        old = main_ref[tail, :LANES].astype(jnp.float32)
        down = lax.broadcasted_iota(jnp.int32, old.shape, 0)
        new = jnp.where(down == INFO - 1, info_ref[...], old)
        main_ref[tail, :LANES] = new.astype(jnp.bfloat16)


def vmem_specs(count):
    return (pl.BlockSpec(memory_space=pltpu.VMEM),) * count


def place_rows(embeddings, labels, owner_map, lay):
    rows, width = embeddings.shape
    n_fine = owner_map.shape[0]
    lab_shape = (rows // LANES, LANES)
    return pl.pallas_call(
        functools.partial(place_kernel, lay),
        out_shape=(
            jax.ShapeDtypeStruct((rows, width), jnp.bfloat16),
            jax.ShapeDtypeStruct((1, rows), jnp.int32),
            jax.ShapeDtypeStruct((1, LANES), jnp.float32),
            jax.ShapeDtypeStruct((lay.rest, width), jnp.bfloat16),
            jax.ShapeDtypeStruct(lab_shape, jnp.int32),
        ),
        in_specs=[pl.BlockSpec(memory_space=pl.ANY)] * 3,
        out_specs=vmem_specs(5),
        scratch_shapes=[
            pltpu.VMEM((rows, width), jnp.bfloat16),
            pltpu.VMEM(lab_shape, jnp.int32),
            pltpu.VMEM((1, n_fine), jnp.int32),
            pltpu.SemaphoreType.DMA((3,)),
        ],
        compiler_params=pltpu.CompilerParams(vmem_limit_bytes=FAST_LIMIT),
    )(embeddings, labels.reshape(lab_shape), owner_map.reshape(1, n_fine))


def pack_main(unit, slot, info, lay):
    return pl.pallas_call(
        functools.partial(main_kernel, lay),
        out_shape=jax.ShapeDtypeStruct((lay.n_main, unit.shape[1]), jnp.bfloat16),
        in_specs=list(vmem_specs(3)),
        out_specs=vmem_specs(1)[0],
        compiler_params=pltpu.CompilerParams(vmem_limit_bytes=FAST_LIMIT),
        cost_estimate=pl.CostEstimate(
            flops=2 * lay.n_main * unit.shape[0] * unit.shape[1],
            bytes_accessed=4 * unit.shape[0] * unit.shape[1],
            transcendentals=0,
        ),
    )(unit, slot, info)


def gather_kernel(home, *refs):
    chunks, out = refs[:-2], refs[-1]

    @pl.when(lax.axis_index("cl") == home)
    def _():
        for source, chunk in enumerate(chunks):
            rows = chunk.shape[0]
            out[source * rows : (source + 1) * rows, :] = chunk[...]


def gather_rest(chunks, home, sums):
    rows, width = chunks[0].shape
    return pl.pallas_call(
        functools.partial(gather_kernel, home),
        out_shape=jax.ShapeDtypeStruct((len(chunks) * rows, width), jnp.bfloat16),
        in_specs=list(vmem_specs(len(chunks) + 1)),
        out_specs=vmem_specs(1)[0],
        compiler_params=pltpu.CompilerParams(vmem_limit_bytes=FAST_LIMIT),
    )(*chunks, sums)


class Layout:
    def __init__(self, n_owner, n_fine, capacity, main, home):
        self.n_owner, self.n_fine, self.capacity = n_owner, n_fine, capacity
        self.main, self.home = main, home
        self.head = main - INFO
        self.rest = capacity - self.head
        self.per_owner = n_fine // n_owner
        self.n_main = n_owner * main
        self.n_head = n_owner * self.head
        self.n_rest = n_owner * self.rest


def info_line(lay, main_ref, source):
    end = (source + 1) * lay.main
    return main_ref[end - INFO : end, :LANES].astype(jnp.float32)[INFO - 1 :]


def lines_of(lay, main_ref):
    return [info_line(lay, main_ref, source) for source in range(lay.n_owner)]


def hot_of(lay, info):
    lane = lax.broadcasted_iota(jnp.int32, (1, LANES), 1)
    hot = jnp.max(jnp.where(lane == lay.n_fine, info, 0.0), axis=1, keepdims=True)
    return hot.astype(jnp.int32)


def write_labels(lay, infos, first, count, at, lab_sub, bias):
    cluster = swapped(lax.axis_index("cl"), hot_of(lay, infos[0]), lay.home)
    lane = lax.broadcasted_iota(jnp.int32, (1, LANES), 1)
    is_edge = lax.div(lane, lay.per_owner) == cluster
    for source, info in enumerate(infos):
        edges = jnp.where(is_edge, info, 2.0 * lay.capacity)
        slot = lax.broadcasted_iota(jnp.int32, (count, LANES), 0) + first
        label = jnp.where(slot.astype(jnp.float32) >= edges, 1.0, 0.0)
        label = jnp.broadcast_to(jnp.sum(label, axis=1, keepdims=True), (count, LANES))
        start = at + source * count
        lab_sub[start : start + count, :] = label
        if bias is not None:
            bias[start : start + count, :] = jnp.where(
                label < lay.per_owner, NEIGHBOUR - SCALE, DEAD
            )


def turn_labels(lay, lab_sub, start, count, lab_lane, at):
    for i in range(0, count, LANES):
        block = jnp.transpose(lab_sub[start + i : start + i + LANES, :])[:1]
        lab_lane[:, at + i : at + i + LANES] = jnp.where(block < lay.per_owner, block, -1.0)


def copy_head(lay, main_ref, rows):
    for source in range(lay.n_owner):
        rows[source * lay.head : (source + 1) * lay.head, :] = main_ref[
            source * lay.main : source * lay.main + lay.head, :
        ]


def pieces(start, count, parts):
    return [(start + i * (count // parts), count // parts) for i in range(parts)]


def stream(
    rows_i, first, count, tiles, lab_lane, at, lab_sub, bias, buffers, put, natural=False
):
    step = 32
    tiles = [
        (ref, s, d, place + s - start)
        for ref, start, n, place, parts in tiles
        for s, d in pieces(start, n, parts)
    ]

    def scores_to(buffer, tile, rows):
        ref, start, deep, _ = tile
        buffer[:deep, : rows.shape[0]] = lax.dot_general(
            ref[start : start + deep, :],
            rows,
            (((1,), (1,)), ((), ())),
            preferred_element_type=jnp.float32,
        )

    def run(start, blocks, wide):
        repeat = wide // LANES

        def rows_of(block):
            return rows_i[pl.ds(pl.multiple_of(first + start + block * wide, LANES), wide), :]

        scores_to(buffers[0], tiles[0], rows_of(0))

        def body(block, carry):
            here = rows_of(block)
            place = pl.ds(pl.multiple_of(at + start + block * wide, LANES), wide)
            label_i = lab_lane[:, place]
            acc = jnp.zeros((8, wide), jnp.float32)
            for i, (_, _, deep, line) in enumerate(tiles):
                if i + 1 < len(tiles):
                    scores_to(buffers[(i + 1) % 2], tiles[i + 1], here)
                else:
                    scores_to(buffers[0], tiles[0], rows_of(jnp.minimum(block + 1, blocks - 1)))
                buffer = buffers[i % 2]
                for c in range(0, deep, step):
                    part = slice(line + c, line + c + step)
                    label_j = jnp.concatenate([lab_sub[part, :]] * repeat, axis=1)
                    if bias is None:
                        bias_j = NEIGHBOUR - SCALE
                    else:
                        bias_j = jnp.concatenate([bias[part, :]] * repeat, axis=1)
                    scores = buffer[c : c + step, :wide]
                    if natural:
                        low = math.log(neighbour_factor) - 1.0 / temper
                        shift = jnp.where(label_j == label_i, -1.0 / temper, low)
                        terms = jnp.exp(scores * (1.0 / temper) + shift)
                    else:
                        shift = jnp.where(label_j == label_i, -SCALE, bias_j)
                        terms = jnp.exp2(scores * SCALE + shift)
                    acc = acc + jnp.sum(terms.reshape(step // 8, 8, wide), axis=0)
            put(place, jnp.sum(acc, axis=0, keepdims=True))
            return carry

        lax.fori_loop(0, blocks, body, 0)

    wide = WIDE
    if count >= wide:
        run(0, count // wide, wide)
    if count % wide:
        run(count - count % wide, 1, count % wide)


def setter(ref):
    def put(place, values):
        ref[:, place] = values

    return put


def adder(ref):
    def put(place, values):
        ref[:, place] += values

    return put


def inner_kernel(lay, mine, sums, lab_lane, lab_sub, bias, rows, buf_a, buf_b):
    is_home = lax.axis_index("cl") == lay.home
    infos = lines_of(lay, mine)

    def work(ref, count, per, bias):
        write_labels(lay, infos, 0, per, 0, lab_sub, bias)
        turn_labels(lay, lab_sub, 0, count, lab_lane, 0)
        tiles = [(ref, 0, count, 0, 4)]
        stream(ref, 0, count, tiles, lab_lane, 0, lab_sub, bias, (buf_a, buf_b), setter(sums))

    @pl.when(is_home)
    def _():
        copy_head(lay, mine, rows)
        work(rows, lay.n_head, lay.head, None)

    @pl.when(jnp.logical_not(is_home))
    def _():
        work(mine, lay.n_main, lay.main, bias)


def cross_kernel(lay, mine, other, sums, lab_lane, total, unfit_ref, lab_sub, bias, rows, rows_j, buf_a, buf_b):
    is_home = lax.axis_index("cl") == lay.home
    infos = lines_of(lay, other)
    own = lines_of(lay, mine)
    hot = hot_of(lay, own[0])
    lane = lax.broadcasted_iota(jnp.int32, (1, LANES), 1)
    last = (lane < lay.n_fine) & (lax.rem(lane, lay.per_owner) == lay.per_owner - 1)
    last = last & (lax.div(lane, lay.per_owner) != hot)
    unfit = jnp.zeros((1, LANES), jnp.float32)
    for info in infos + own:
        wrong = last & (info >= lay.main)
        differs = (info != hot.astype(jnp.float32)) | (info >= lay.n_owner)
        wrong = wrong | ((lane == lay.n_fine) & differs)
        unfit = unfit + jnp.where(wrong, 1.0, 0.0)
    unfit_ref[0, 0] = jnp.max(unfit).astype(jnp.int32)
    total[...] = sums[...]

    def work(ref, ref_j, count, per, bias):
        write_labels(lay, infos, 0, per, 0, lab_sub, bias)
        tiles = [(ref_j, 0, count, 0, 4)]
        stream(ref, 0, count, tiles, lab_lane, 0, lab_sub, bias, (buf_a, buf_b), adder(total))

    @pl.when(is_home)
    def _():
        copy_head(lay, mine, rows)
        copy_head(lay, other, rows_j)
        work(rows, rows_j, lay.n_head, lay.head, None)

    @pl.when(jnp.logical_not(is_home))
    def _():
        work(mine, other, lay.n_main, lay.main, bias)


def copy_all(lay, main_ref, rest, rows):
    copy_head(lay, main_ref, rows)
    rows[lay.n_head :, :] = rest[...]


def rest_labels(lay, infos, lab_sub):
    write_labels(lay, infos, 0, lay.head, 0, lab_sub, None)
    write_labels(lay, infos, lay.head, lay.rest, lay.n_head, lab_sub, None)


def rest_pairs(lay, rows, rows_j, lab_lane, lab_sub, buffers, put):
    n_head, n_rest = lay.n_head, lay.n_rest
    seconds = (rows_j, n_head, n_rest, n_head, 4)
    mains = (rows_j, 0, n_head, 0, 4)
    stream(rows, 0, n_head, [seconds], lab_lane, 0, lab_sub, None, buffers, put, True)
    second_tiles = [seconds, mains]
    stream(rows, n_head, n_rest, second_tiles, lab_lane, n_head, lab_sub, None, buffers, put, True)


def inner_rest_kernel(lay, mine, rest, sums, lab_lane, lab_sub, rows, buf_a, buf_b):

    @pl.when(lax.axis_index("cl") == lay.home)
    def _():
        rest_labels(lay, lines_of(lay, mine), lab_sub)
        turn_labels(lay, lab_sub, 0, lay.n_head + lay.n_rest, lab_lane, 0)
        copy_all(lay, mine, rest, rows)
        rest_pairs(lay, rows, rows, lab_lane, lab_sub, (buf_a, buf_b), setter(sums))


def cross_rest_kernel(lay, mine, other, rest, rest_other, *refs):
    main_sums, main_lane, sums, lab_lane, out_ref, lab_sub, rows, rows_j, total, buf_a, buf_b = refs
    is_home = lax.axis_index("cl") == lay.home

    @pl.when(is_home)
    def _():
        rest_labels(lay, lines_of(lay, other), lab_sub)
        copy_all(lay, mine, rest, rows)
        copy_all(lay, other, rest_other, rows_j)
        total[...] = sums[...]
        total[:, : lay.n_head] += main_sums[:, : lay.n_head]
        rest_pairs(lay, rows, rows_j, lab_lane, lab_sub, (buf_a, buf_b), adder(total))
        values = jnp.log(total[...])
        for source in range(lay.n_owner):
            start = source * lay.head
            out_ref[source, :, : lay.head] = values[:, start : start + lay.head]
            start = lay.n_head + source * lay.rest
            out_ref[source, :, lay.head :] = values[:, start : start + lay.rest]

    @pl.when(jnp.logical_not(is_home))
    def _():
        values = jnp.log(jnp.where(main_lane[...] >= 0, main_sums[...], 1.0))
        for source in range(lay.n_owner):
            start = source * lay.main
            out_ref[source, :, : lay.main] = values[:, start : start + lay.main]


def pair_call(kernel, lay, arrays, out_shape, sides, joins, more=(), out_specs=None):
    width = arrays[0].shape[1]
    side = pltpu.VMEM((sides[0], LANES), jnp.float32)
    rows = pltpu.VMEM((joins[0], width), jnp.bfloat16)
    buffer = pltpu.VMEM((lay.n_main // 4, WIDE), jnp.float32)
    out = pl.pallas_call(
        functools.partial(kernel, lay),
        out_shape=out_shape,
        in_specs=list(vmem_specs(len(arrays))),
        out_specs=out_specs or vmem_specs(len(out_shape)),
        scratch_shapes=[side] * sides[1] + [rows] * joins[1] + list(more) + [buffer, buffer],
        compiler_params=pltpu.CompilerParams(vmem_limit_bytes=FAST_LIMIT),
    )(*arrays)
    return out


def fast_unpack_kernel(values_ref, pos_ref, out_ref):
    pos = pos_ref[...]
    lane = lax.rem(pos, LANES)
    line = lax.div(pos, LANES)
    out = jnp.zeros(pos.shape, jnp.float32)
    per = values_ref.shape[2] // LANES
    for r in range(values_ref.shape[0] * per):
        start = r % per * LANES
        table = jnp.broadcast_to(values_ref[r // per, :, start : start + LANES], pos.shape)
        found = jnp.take_along_axis(table, lane, axis=1)
        out = jnp.where(line == r, found, out)
    out_ref[...] = out


def fast_unpack(values, pos):
    vmem = pl.BlockSpec(memory_space=pltpu.VMEM)
    return pl.pallas_call(
        fast_unpack_kernel,
        out_shape=jax.ShapeDtypeStruct(pos.shape, jnp.float32),
        in_specs=[vmem, vmem],
        out_specs=vmem,
    )(values, pos)


def general(embeddings, labels, owner_map):
    n_owner = lax.axis_size("cl")
    capacity = SLOTS // n_owner
    rows, width = embeddings.shape
    packed, pos, counts = pack(embeddings, labels, owner_map, n_owner, capacity)
    counts = lax.all_gather(counts, ("cl", "grp"), tiled=True)
    mine = lax.all_to_all(
        packed.reshape(n_owner, capacity, width), "cl", split_axis=0, concat_axis=0, tiled=True
    ).reshape(SLOTS, width)
    other = lax.ppermute(mine, "grp", [(0, 1), (1, 0)])
    results = log_counts(counts, mine, other, n_owner, capacity)
    returned = lax.all_to_all(
        results.reshape(n_owner, capacity), "cl", split_axis=0, concat_axis=0, tiled=True
    )
    return unpack(returned.reshape(SLOTS), pos).reshape(rows)


def body(embeddings, labels, owner_map):
    n_owner = lax.axis_size("cl")
    capacity = SLOTS // n_owner
    rows, width = embeddings.shape
    n_fine = owner_map.shape[0]
    main = -(-(rows // n_owner * 9 // 8) // 16) * 16
    if main >= capacity or n_fine >= LANES:
        return general(embeddings, labels, owner_map)
    home = n_owner // 4
    lay = Layout(n_owner, n_fine, capacity, main, home)
    unit, slot, info, extra, pos = place_rows(embeddings, labels, owner_map, lay)
    packed = pack_main(unit, slot, info, lay)
    chunks = [
        extra if source == home else lax.ppermute(extra, "cl", [(source, home)])
        for source in range(n_owner)
    ]
    mine = lax.all_to_all(
        packed.reshape(n_owner, main, width), "cl", split_axis=0, concat_axis=0, tiled=True
    ).reshape(n_owner * main, width)
    other = lax.ppermute(mine, "grp", [(0, 1), (1, 0)])
    row = jax.ShapeDtypeStruct((1, lay.n_main), jnp.float32)
    lines = lay.n_head + lay.n_rest
    long_row = jax.ShapeDtypeStruct((1, lines), jnp.float32)
    flag = jax.ShapeDtypeStruct((1, 1), jnp.int32)
    table = jax.ShapeDtypeStruct((n_owner, 1, capacity), jnp.float32)
    sides, joins = (lay.n_main, 2), (lay.n_head, 1)
    sums, main_lane = pair_call(inner_kernel, lay, (mine,), (row, row), sides, joins)
    joins = (lay.n_head, 2)
    arrays = (mine, other, sums, main_lane)
    specs = (pl.BlockSpec(memory_space=pltpu.VMEM), pl.BlockSpec(memory_space=pltpu.SMEM))
    sums, unfit = pair_call(cross_kernel, lay, arrays, (row, flag), sides, joins, out_specs=specs)
    rest = gather_rest(chunks, home, sums)
    swap = [(2 * home, 2 * home + 1), (2 * home + 1, 2 * home)]
    rest_other = lax.ppermute(rest, ("cl", "grp"), swap)
    rest_sums, lane = pair_call(
        inner_rest_kernel, lay, (mine, rest), (long_row, long_row), (lines, 1), (lines, 1)
    )
    arrays = (mine, other, rest, rest_other, sums, main_lane, rest_sums, lane)
    total = pltpu.VMEM(long_row.shape, jnp.float32)
    (results,) = pair_call(
        cross_rest_kernel, lay, arrays, (table,), (lines, 1), (lines, 2), (total,)
    )
    returned = lax.all_to_all(results, "cl", split_axis=0, concat_axis=0, tiled=True)
    return lax.cond(
        unfit[0, 0] == 0,
        lambda: fast_unpack(returned, pos).reshape(rows),
        lambda: general(embeddings, labels, owner_map),
    )


def solution(mesh):
    return jax.shard_map(
        body,
        mesh=mesh,
        in_specs=(P(("parts", "cl", "grp"), None), P(("parts", "cl", "grp")), P("parts")),
        out_specs=P(("parts", "cl", "grp")),
        check_vma=False,
    )
```

```python
import functools
import math

import jax
import jax.numpy as jnp
from jax import lax
from jax.experimental import pallas as pl
from jax.experimental.pallas import tpu as pltpu
from jax.sharding import PartitionSpec as P

SLOTS = 2048

temper = 0.2
neighbour_factor = 0.5
epsilon = 1e-06

LANES = 128
SCALE = math.log2(math.e) / temper
NEIGHBOUR = math.log2(neighbour_factor)
DEAD = -1e30
VMEM_LIMIT = 48 * 1024 * 1024
FAST_LIMIT = 24 * 1024 * 1024
WIDE = 512
INFO = 16


def column_of(row):
    pieces = []
    for start in range(0, row.shape[1], LANES):
        width = min(LANES, row.shape[1] - start)
        shape = (width, width)
        diagonal = lax.broadcasted_iota(jnp.int32, shape, 0) == lax.broadcasted_iota(
            jnp.int32, shape, 1
        )
        piece = jnp.broadcast_to(row[:, start : start + width], shape)
        pieces.append(jnp.sum(jnp.where(diagonal, piece, 0.0), axis=1, keepdims=True))
    return jnp.concatenate(pieces, axis=0)


def row_of(column):
    n = column.shape[0]
    diagonal = lax.broadcasted_iota(jnp.int32, (n, n), 0) == lax.broadcasted_iota(
        jnp.int32, (n, n), 1
    )
    return jnp.sum(jnp.where(diagonal, column, 0.0), axis=0, keepdims=True)


def pack_kernel(n_owner, capacity, x_ref, lab_ref, map_ref, out_ref, pos_ref, cnt_ref, unit, pos_row):
    rows = x_ref.shape[0]
    n_fine = map_ref.shape[1]
    per_owner = n_fine // n_owner
    owner_row = map_ref[...].astype(jnp.float32)
    fine_row = lax.broadcasted_iota(jnp.int32, (1, n_fine), 1).astype(jnp.float32)
    key_row = owner_row * n_fine + fine_row
    key_col = column_of(key_row)
    sorted_col = jnp.sum(jnp.where(key_row < key_col, 1.0, 0.0), axis=1, keepdims=True)
    lab = lab_ref[...].astype(jnp.float32)
    lab_row = jnp.concatenate([lab[b : b + 1, :] for b in range(lab.shape[0])], axis=1)
    fine_col = lax.broadcasted_iota(jnp.int32, (n_fine, rows), 0).astype(jnp.float32)
    fine_id = jnp.sum(jnp.where(fine_col == lab_row, sorted_col, 0.0), axis=0, keepdims=True)
    counts_col = jnp.sum(jnp.where(fine_col == fine_id, 1.0, 0.0), axis=1, keepdims=True)
    cnt_ref[...] = row_of(counts_col).astype(jnp.int32)
    coarse = jnp.floor((fine_id + 0.5) * (1.0 / per_owner))
    before = jnp.sum(
        jnp.where(fine_col < coarse * per_owner, counts_col, 0.0), axis=0, keepdims=True
    )
    index = lax.broadcasted_iota(jnp.int32, (1, rows), 1).astype(jnp.float32)
    row_key = fine_id * rows + index
    rank = jnp.zeros((1, rows), jnp.float32)
    for start in range(0, rows, LANES):
        other = column_of(row_key[:, start : start + LANES])
        rank = rank + jnp.sum(jnp.where(other < row_key, 1.0, 0.0), axis=0, keepdims=True)
    pos = (coarse * capacity + rank - before).astype(jnp.int32)
    pos_row[...] = pos
    pos_ref[...] = jnp.concatenate(
        [pos[:, start : start + LANES] for start in range(0, rows, LANES)], axis=0
    )
    x = x_ref[...].astype(jnp.float32)
    squares = jnp.sum(x * x, axis=1, keepdims=True)
    unit[...] = (x * lax.rsqrt(squares + epsilon)).astype(jnp.bfloat16)

    step = 256

    @pl.loop(0, out_ref.shape[0] // step)
    def _(block):
        slot = lax.broadcasted_iota(jnp.int32, (step, rows), 0) + block * step
        chosen = jnp.where(slot == pos_row[...], 1.0, 0.0).astype(jnp.bfloat16)
        packed = jnp.dot(chosen, unit[...], preferred_element_type=jnp.float32)
        out_ref[pl.ds(pl.multiple_of(block * step, step), step), :] = packed.astype(jnp.bfloat16)


def pack(embeddings, labels, owner_map, n_owner, capacity):
    rows, width = embeddings.shape
    n_fine = owner_map.shape[0]
    total = n_owner * capacity
    vmem = pl.BlockSpec(memory_space=pltpu.VMEM)
    return pl.pallas_call(
        functools.partial(pack_kernel, n_owner, capacity),
        out_shape=(
            jax.ShapeDtypeStruct((total, width), jnp.bfloat16),
            jax.ShapeDtypeStruct((rows // LANES, LANES), jnp.int32),
            jax.ShapeDtypeStruct((1, n_fine), jnp.int32),
        ),
        in_specs=[vmem] * 3,
        out_specs=(vmem, vmem, vmem),
        scratch_shapes=[pltpu.VMEM((rows, width), jnp.bfloat16), pltpu.VMEM((1, rows), jnp.int32)],
        compiler_params=pltpu.CompilerParams(vmem_limit_bytes=VMEM_LIMIT),
    )(embeddings, labels.reshape(rows // LANES, LANES), owner_map.reshape(1, n_fine))


def counts_kernel(n_owner, capacity, cnt_ref, mine_ref, other_ref, out_ref, lab_lane, lab_sub, bias):
    total = mine_ref.shape[0]
    per_owner = cnt_ref.shape[1] // n_owner
    me = lax.axis_index("cl")
    grp = lax.axis_index("grp")
    n_grp = lax.axis_size("grp")
    for member in range(2):
        for source in range(n_owner):
            line = source * n_grp + lax.rem(grp + member, n_grp)
            edges = []
            edge = jnp.int32(0)
            for f in range(per_owner):
                edge = edge + cnt_ref[line, me * per_owner + f]
                edges.append(edge)
            down = lax.broadcasted_iota(jnp.int32, (capacity, LANES), 0)
            label = jnp.zeros((capacity, LANES), jnp.int32)
            for edge in edges:
                label = label + jnp.where(down >= edge, 1, 0)
            start = (member * n_owner + source) * capacity
            lab_sub[start : start + capacity, :] = label
            bias[start : start + capacity, :] = jnp.where(
                label < per_owner, NEIGHBOUR - SCALE, DEAD
            )
            if member == 0:
                across = lax.broadcasted_iota(jnp.int32, (1, capacity), 1)
                label = jnp.zeros((1, capacity), jnp.int32)
                for edge in edges:
                    label = label + jnp.where(across >= edge, 1, 0)
                lab_lane[:, source * capacity : (source + 1) * capacity] = jnp.where(
                    label < per_owner, label, -1
                )
    wide, deep = min(512, total), min(256, total)

    @pl.loop(0, total // wide)
    def _(block):
        columns = pl.ds(pl.multiple_of(block * wide, wide), wide)
        rows_i = mine_ref[columns, :]
        label_i = lab_lane[:, columns]

        def add(ref, offset):
            def step(j, acc):
                start = pl.multiple_of(j * deep, deep)
                scores = lax.dot_general(
                    ref[pl.ds(start, deep), :],
                    rows_i,
                    (((1,), (1,)), ((), ())),
                    preferred_element_type=jnp.float32,
                )
                place = pl.ds(pl.multiple_of(start + offset, deep), deep)
                label_j = lab_sub[place, :]
                bias_j = bias[place, :]
                repeat = wide // LANES
                label_j = jnp.concatenate([label_j] * repeat, axis=1)
                bias_j = jnp.concatenate([bias_j] * repeat, axis=1)
                shift = jnp.where(label_j == label_i, -SCALE, bias_j)
                terms = jnp.exp2(scores * SCALE + shift)
                return acc + jnp.sum(terms.reshape(deep // 8, 8, wide), axis=0)

            return step

        acc = jnp.zeros((8, wide), jnp.float32)
        acc = lax.fori_loop(0, total // deep, add(mine_ref, 0), acc, unroll=2)
        acc = lax.fori_loop(0, total // deep, add(other_ref, total), acc, unroll=2)
        totals = jnp.sum(acc, axis=0, keepdims=True)
        out_ref[:, columns] = jnp.log(jnp.where(label_i >= 0, totals, 1.0))


def log_counts(counts, mine, other, n_owner, capacity):
    total = mine.shape[0]
    vmem = pl.BlockSpec(memory_space=pltpu.VMEM)
    return pl.pallas_call(
        functools.partial(counts_kernel, n_owner, capacity),
        out_shape=jax.ShapeDtypeStruct((1, total), jnp.float32),
        in_specs=[pl.BlockSpec(memory_space=pltpu.SMEM), vmem, vmem],
        out_specs=vmem,
        scratch_shapes=[
            pltpu.VMEM((1, total), jnp.int32),
            pltpu.VMEM((2 * total, LANES), jnp.int32),
            pltpu.VMEM((2 * total, LANES), jnp.float32),
        ],
        compiler_params=pltpu.CompilerParams(vmem_limit_bytes=VMEM_LIMIT),
    )(counts, mine, other)


def unpack_kernel(values_ref, pos_ref, out_ref):
    pos = pos_ref[...]
    lane = lax.rem(pos, LANES)
    line = lax.div(pos, LANES)
    out = jnp.zeros(pos.shape, jnp.float32)
    for r in range(values_ref.shape[0]):
        table = jnp.broadcast_to(values_ref[r : r + 1, :], pos.shape)
        found = jnp.take_along_axis(table, lane, axis=1)
        out = jnp.where(line == r, found, out)
    out_ref[...] = out


def unpack(values, pos):
    vmem = pl.BlockSpec(memory_space=pltpu.VMEM)
    return pl.pallas_call(
        unpack_kernel,
        out_shape=jax.ShapeDtypeStruct(pos.shape, jnp.float32),
        in_specs=[vmem, vmem],
        out_specs=vmem,
    )(values.reshape(-1, LANES), pos)


def swapped(x, first, second):
    return jnp.where(x == first, second, jnp.where(x == second, first, x))


def place_kernel(lay, x_hbm, lab_hbm, map_hbm, *refs):
    n_owner, capacity, main, home = lay.n_owner, lay.capacity, lay.main, lay.home
    unit, slot_ref, info_ref, extra_ref, pos_ref, x_ref, lab_ref, map_ref, sems = refs
    copies = [
        pltpu.make_async_copy(src, dst, sems.at[i])
        for i, (src, dst) in enumerate(((x_hbm, x_ref), (lab_hbm, lab_ref), (map_hbm, map_ref)))
    ]
    for copy in copies:
        copy.start()
    rows = x_ref.shape[0]
    n_fine = map_ref.shape[1]
    per_owner = n_fine // n_owner
    copies[1].wait()
    copies[2].wait()
    owner_row = map_ref[...].astype(jnp.float32)
    fine_row = lax.broadcasted_iota(jnp.int32, (1, n_fine), 1).astype(jnp.float32)
    key_row = owner_row * n_fine + fine_row
    key_col = column_of(key_row)
    sorted_col = jnp.sum(jnp.where(key_row < key_col, 1.0, 0.0), axis=1, keepdims=True)
    lab = lab_ref[...].astype(jnp.float32)
    lab_row = jnp.concatenate([lab[b : b + 1, :] for b in range(lab.shape[0])], axis=1)
    fine_col = lax.broadcasted_iota(jnp.int32, (n_fine, rows), 0).astype(jnp.float32)
    fine_id = jnp.sum(jnp.where(fine_col == lab_row, sorted_col, 0.0), axis=0, keepdims=True)
    counts_col = jnp.sum(jnp.where(fine_col == fine_id, 1.0, 0.0), axis=1, keepdims=True)
    coarse = jnp.floor((fine_id + 0.5) * (1.0 / per_owner))
    first = coarse * per_owner
    before = jnp.sum(jnp.where(fine_col < first, counts_col, 0.0), axis=0, keepdims=True)
    upto = jnp.sum(jnp.where(fine_col < first + per_owner, counts_col, 0.0), axis=0, keepdims=True)
    full = jnp.min(
        jnp.where(upto - before == capacity, coarse, float(n_owner)), axis=1, keepdims=True
    )
    line = lax.broadcasted_iota(jnp.int32, (n_fine, LANES), 0)
    lane = lax.broadcasted_iota(jnp.int32, (n_fine, LANES), 1)
    inside = (line <= lane) & (lax.div(line, per_owner) == lax.div(lane, per_owner))
    running = jnp.sum(jnp.where(inside, counts_col, 0.0), axis=0, keepdims=True)
    info = jnp.where(lane[:1] < n_fine, running, full)
    info_ref[...] = info
    index = lax.broadcasted_iota(jnp.int32, (1, rows), 1).astype(jnp.float32)
    row_key = fine_id * rows + index
    rank = jnp.zeros((1, rows), jnp.float32)
    for start in range(0, rows, LANES):
        other = column_of(row_key[:, start : start + LANES])
        rank = rank + jnp.sum(jnp.where(other < row_key, 1.0, 0.0), axis=0, keepdims=True)
    rank = (rank - before).astype(jnp.int32)
    place = swapped(coarse.astype(jnp.int32), full.astype(jnp.int32), home)
    table = place * capacity + rank
    pos_ref[...] = jnp.concatenate(
        [table[:, start : start + LANES] for start in range(0, rows, LANES)], axis=0
    )
    later = jnp.where(place == home, lay.n_main + rank - lay.head, -1)
    fits = rank < jnp.where(place == home, lay.head, main - 1)
    slot = jnp.where(fits, place * main + rank, later)
    slot_ref[...] = slot
    copies[0].wait()
    x = x_ref[...].astype(jnp.float32)
    squares = jnp.sum(x * x, axis=1, keepdims=True)
    unit[...] = (x * lax.rsqrt(squares + epsilon)).astype(jnp.bfloat16)
    extra_ref[...] = chosen_rows(unit, slot, lay.n_main, lay.rest)


def chosen_rows(unit, slot, start, count):
    here = lax.broadcasted_iota(jnp.int32, (count, unit.shape[0]), 0) + start
    chosen = jnp.where(here == slot, 1.0, 0.0).astype(jnp.bfloat16)
    return jnp.dot(chosen, unit[...], preferred_element_type=jnp.float32).astype(jnp.bfloat16)


def main_kernel(lay, unit, slot_ref, info_ref, main_ref):
    count = lay.n_main // 4
    for start in range(0, lay.n_main, count):
        main_ref[start : start + count, :] = chosen_rows(unit, slot_ref[...], start, count)
    for owner in range(lay.n_owner):
        tail = slice((owner + 1) * lay.main - INFO, (owner + 1) * lay.main)
        old = main_ref[tail, :LANES].astype(jnp.float32)
        down = lax.broadcasted_iota(jnp.int32, old.shape, 0)
        new = jnp.where(down == INFO - 1, info_ref[...], old)
        main_ref[tail, :LANES] = new.astype(jnp.bfloat16)


def vmem_specs(count):
    return (pl.BlockSpec(memory_space=pltpu.VMEM),) * count


def place_rows(embeddings, labels, owner_map, lay):
    rows, width = embeddings.shape
    n_fine = owner_map.shape[0]
    lab_shape = (rows // LANES, LANES)
    return pl.pallas_call(
        functools.partial(place_kernel, lay),
        out_shape=(
            jax.ShapeDtypeStruct((rows, width), jnp.bfloat16),
            jax.ShapeDtypeStruct((1, rows), jnp.int32),
            jax.ShapeDtypeStruct((1, LANES), jnp.float32),
            jax.ShapeDtypeStruct((lay.rest, width), jnp.bfloat16),
            jax.ShapeDtypeStruct(lab_shape, jnp.int32),
        ),
        in_specs=[pl.BlockSpec(memory_space=pl.ANY)] * 3,
        out_specs=vmem_specs(5),
        scratch_shapes=[
            pltpu.VMEM((rows, width), jnp.bfloat16),
            pltpu.VMEM(lab_shape, jnp.int32),
            pltpu.VMEM((1, n_fine), jnp.int32),
            pltpu.SemaphoreType.DMA((3,)),
        ],
        compiler_params=pltpu.CompilerParams(vmem_limit_bytes=FAST_LIMIT),
    )(embeddings, labels.reshape(lab_shape), owner_map.reshape(1, n_fine))


def pack_main(unit, slot, info, lay):
    return pl.pallas_call(
        functools.partial(main_kernel, lay),
        out_shape=jax.ShapeDtypeStruct((lay.n_main, unit.shape[1]), jnp.bfloat16),
        in_specs=list(vmem_specs(3)),
        out_specs=vmem_specs(1)[0],
        compiler_params=pltpu.CompilerParams(vmem_limit_bytes=FAST_LIMIT),
        cost_estimate=pl.CostEstimate(
            flops=2 * lay.n_main * unit.shape[0] * unit.shape[1],
            bytes_accessed=4 * unit.shape[0] * unit.shape[1],
            transcendentals=0,
        ),
    )(unit, slot, info)


def gate_kernel(*refs):
    pass


def after(rows, there):
    anywhere = pl.BlockSpec(memory_space=pl.ANY)
    return pl.pallas_call(
        gate_kernel,
        out_shape=jax.ShapeDtypeStruct(rows.shape, rows.dtype),
        in_specs=[anywhere] * 2,
        out_specs=anywhere,
        input_output_aliases={0: 0},
    )(rows, there)


def pair_up_kernel(first, second, out):
    rows = first.shape[0]
    out[:rows, :] = first[...]
    out[rows:, :] = second[...]


def pair_up(first, second):
    rows, width = first.shape
    return pl.pallas_call(
        pair_up_kernel,
        out_shape=jax.ShapeDtypeStruct((2 * rows, width), jnp.bfloat16),
        in_specs=list(vmem_specs(2)),
        out_specs=vmem_specs(1)[0],
        compiler_params=pltpu.CompilerParams(vmem_limit_bytes=FAST_LIMIT),
    )(first, second)


def gather_kernel(home, *refs):
    chunks, out = refs[:-2], refs[-1]

    @pl.when(lax.axis_index("cl") == home)
    def _():
        start = 0
        for chunk in chunks:
            out[start : start + chunk.shape[0], :] = chunk[...]
            start += chunk.shape[0]


def gather_rest(chunks, home, sums):
    rows, width = sum(x.shape[0] for x in chunks), chunks[0].shape[1]
    return pl.pallas_call(
        functools.partial(gather_kernel, home),
        out_shape=jax.ShapeDtypeStruct((rows, width), jnp.bfloat16),
        in_specs=list(vmem_specs(len(chunks) + 1)),
        out_specs=vmem_specs(1)[0],
        compiler_params=pltpu.CompilerParams(vmem_limit_bytes=FAST_LIMIT),
    )(*chunks, sums)


class Layout:
    def __init__(self, n_owner, n_fine, capacity, main, home):
        self.n_owner, self.n_fine, self.capacity = n_owner, n_fine, capacity
        self.main, self.home = main, home
        self.head = main - INFO
        self.rest = capacity - self.head
        self.per_owner = n_fine // n_owner
        self.n_main = n_owner * main
        self.n_head = n_owner * self.head
        self.n_rest = n_owner * self.rest


def info_line(lay, main_ref, source):
    end = (source + 1) * lay.main
    return main_ref[end - INFO : end, :LANES].astype(jnp.float32)[INFO - 1 :]


def lines_of(lay, main_ref):
    return [info_line(lay, main_ref, source) for source in range(lay.n_owner)]


def hot_of(lay, info):
    lane = lax.broadcasted_iota(jnp.int32, (1, LANES), 1)
    hot = jnp.max(jnp.where(lane == lay.n_fine, info, 0.0), axis=1, keepdims=True)
    return hot.astype(jnp.int32)


def write_labels(lay, infos, first, count, at, lab_sub, bias):
    cluster = swapped(lax.axis_index("cl"), hot_of(lay, infos[0]), lay.home)
    lane = lax.broadcasted_iota(jnp.int32, (1, LANES), 1)
    is_edge = lax.div(lane, lay.per_owner) == cluster
    for source, info in enumerate(infos):
        edges = jnp.where(is_edge, info, 2.0 * lay.capacity)
        slot = lax.broadcasted_iota(jnp.int32, (count, LANES), 0) + first
        label = jnp.where(slot.astype(jnp.float32) >= edges, 1.0, 0.0)
        label = jnp.broadcast_to(jnp.sum(label, axis=1, keepdims=True), (count, LANES))
        start = at + source * count
        lab_sub[start : start + count, :] = label
        if bias is not None:
            bias[start : start + count, :] = jnp.where(
                label < lay.per_owner, NEIGHBOUR - SCALE, DEAD
            )


def turn_labels(lay, lab_sub, start, count, lab_lane, at):
    for i in range(0, count, LANES):
        block = jnp.transpose(lab_sub[start + i : start + i + LANES, :])[:1]
        lab_lane[:, at + i : at + i + LANES] = jnp.where(block < lay.per_owner, block, -1.0)


def copy_head(lay, main_ref, rows):
    for source in range(lay.n_owner):
        rows[source * lay.head : (source + 1) * lay.head, :] = main_ref[
            source * lay.main : source * lay.main + lay.head, :
        ]


def pieces(start, count, parts):
    return [(start + i * (count // parts), count // parts) for i in range(parts)]


def stream(
    rows_i, first, count, tiles, lab_lane, at, lab_sub, bias, buffers, put, wide=WIDE
):
    step = 32
    tiles = [
        (ref, s, d, place + s - start)
        for ref, start, n, place, parts in tiles
        for s, d in pieces(start, n, parts)
    ]

    def scores_to(buffer, tile, rows):
        ref, start, deep, _ = tile
        buffer[:deep, : rows.shape[0]] = lax.dot_general(
            ref[start : start + deep, :],
            rows,
            (((1,), (1,)), ((), ())),
            preferred_element_type=jnp.float32,
        )

    def run(start, blocks, wide):
        repeat = wide // LANES

        def rows_of(block):
            return rows_i[pl.ds(pl.multiple_of(first + start + block * wide, LANES), wide), :]

        scores_to(buffers[0], tiles[0], rows_of(0))

        def body(block, carry):
            here = rows_of(block)
            place = pl.ds(pl.multiple_of(at + start + block * wide, LANES), wide)
            label_i = lab_lane[:, place]
            acc = jnp.zeros((8, wide), jnp.float32)
            for i, (_, _, deep, line) in enumerate(tiles):
                if i + 1 < len(tiles):
                    scores_to(buffers[(i + 1) % 2], tiles[i + 1], here)
                else:
                    scores_to(buffers[0], tiles[0], rows_of(jnp.minimum(block + 1, blocks - 1)))
                buffer = buffers[i % 2]
                for c in range(0, deep, step):
                    part = slice(line + c, line + c + step)
                    label_j = jnp.concatenate([lab_sub[part, :]] * repeat, axis=1)
                    if bias is None:
                        bias_j = NEIGHBOUR - SCALE
                    else:
                        bias_j = jnp.concatenate([bias[part, :]] * repeat, axis=1)
                    scores = buffer[c : c + step, :wide]
                    shift = jnp.where(label_j == label_i, -SCALE, bias_j)
                    terms = jnp.exp2(scores * SCALE + shift)
                    acc = acc + jnp.sum(terms.reshape(step // 8, 8, wide), axis=0)
            put(place, jnp.sum(acc, axis=0, keepdims=True))
            return carry

        lax.fori_loop(0, blocks, body, 0)

    if count >= wide:
        run(0, count // wide, wide)
    if count % wide:
        run(count - count % wide, 1, count % wide)


def setter(ref):
    def put(place, values):
        ref[:, place] = values

    return put


def adder(ref):
    def put(place, values):
        ref[:, place] += values

    return put


def inner_kernel(lay, mine, sums, lab_lane, lab_sub, bias, rows, buf_a, buf_b):
    is_home = lax.axis_index("cl") == lay.home
    infos = lines_of(lay, mine)

    def work(ref, count, per, bias):
        write_labels(lay, infos, 0, per, 0, lab_sub, bias)
        turn_labels(lay, lab_sub, 0, count, lab_lane, 0)
        tiles = [(ref, 0, count, 0, 2)]
        stream(ref, 0, count, tiles, lab_lane, 0, lab_sub, bias, (buf_a, buf_b), setter(sums))

    @pl.when(is_home)
    def _():
        copy_head(lay, mine, rows)
        work(rows, lay.n_head, lay.head, None)

    @pl.when(jnp.logical_not(is_home))
    def _():
        work(mine, lay.n_main, lay.main, bias)


def cross_kernel(lay, mine, other, sums, lab_lane, total, unfit_ref, lab_sub, bias, rows, rows_j, buf_a, buf_b):
    is_home = lax.axis_index("cl") == lay.home
    infos = lines_of(lay, other)
    own = lines_of(lay, mine)
    hot = hot_of(lay, own[0])
    lane = lax.broadcasted_iota(jnp.int32, (1, LANES), 1)
    last = (lane < lay.n_fine) & (lax.rem(lane, lay.per_owner) == lay.per_owner - 1)
    last = last & (lax.div(lane, lay.per_owner) != hot)
    unfit = jnp.zeros((1, LANES), jnp.float32)
    for info in infos + own:
        wrong = last & (info >= lay.main)
        differs = (info != hot.astype(jnp.float32)) | (info >= lay.n_owner)
        wrong = wrong | ((lane == lay.n_fine) & differs)
        unfit = unfit + jnp.where(wrong, 1.0, 0.0)
    unfit_ref[0, 0] = jnp.max(unfit).astype(jnp.int32)
    total[...] = sums[...]

    def work(ref, ref_j, count, per, bias):
        write_labels(lay, infos, 0, per, 0, lab_sub, bias)
        tiles = [(ref_j, 0, count, 0, 2)]
        stream(ref, 0, count, tiles, lab_lane, 0, lab_sub, bias, (buf_a, buf_b), adder(total))

    @pl.when(is_home)
    def _():
        copy_head(lay, mine, rows)
        copy_head(lay, other, rows_j)
        work(rows, rows_j, lay.n_head, lay.head, None)

    @pl.when(jnp.logical_not(is_home))
    def _():
        work(mine, other, lay.n_main, lay.main, bias)


def copy_all(lay, main_ref, rest, rows):
    copy_head(lay, main_ref, rows)
    rows[lay.n_head :, :] = rest[...]


def rest_labels(lay, infos, lab_sub):
    write_labels(lay, infos, 0, lay.head, 0, lab_sub, None)
    write_labels(lay, infos, lay.head, lay.rest, lay.n_head, lab_sub, None)


def rest_pairs(lay, rows, rows_j, lab_lane, lab_sub, buffers, put, wide):
    n_head, n_rest = lay.n_head, lay.n_rest
    seconds = (rows_j, n_head, n_rest, n_head, 2)
    mains = (rows_j, 0, n_head, 0, 2)
    stream(rows, 0, n_head, [seconds], lab_lane, 0, lab_sub, None, buffers, put, wide)
    second_tiles = [seconds, mains]
    stream(rows, n_head, n_rest, second_tiles, lab_lane, n_head, lab_sub, None, buffers, put, wide)


def inner_rest_kernel(lay, mine, rest, sums, lab_lane, lab_sub, rows, buf_a, buf_b):

    @pl.when(lax.axis_index("cl") == lay.home)
    def _():
        rest_labels(lay, lines_of(lay, mine), lab_sub)
        turn_labels(lay, lab_sub, 0, lay.n_head + lay.n_rest, lab_lane, 0)
        copy_all(lay, mine, rest, rows)
        rest_pairs(lay, rows, rows, lab_lane, lab_sub, (buf_a, buf_b), setter(sums), WIDE)


def cross_rest_kernel(lay, mine, other, rest, rest_other, *refs):
    main_sums, main_lane, sums, lab_lane, out_ref, lab_sub, rows, rows_j, total, buf_a, buf_b = refs
    is_home = lax.axis_index("cl") == lay.home

    @pl.when(is_home)
    def _():
        rest_labels(lay, lines_of(lay, other), lab_sub)
        copy_all(lay, mine, rest, rows)
        copy_all(lay, other, rest_other, rows_j)
        total[...] = sums[...]
        total[:, : lay.n_head] += main_sums[:, : lay.n_head]
        rest_pairs(lay, rows, rows_j, lab_lane, lab_sub, (buf_a, buf_b), adder(total), 2 * WIDE)
        values = jnp.log(total[...])
        for source in range(lay.n_owner):
            start = source * lay.head
            out_ref[source, :, : lay.head] = values[:, start : start + lay.head]
            start = lay.n_head + source * lay.rest
            out_ref[source, :, lay.head :] = values[:, start : start + lay.rest]

    @pl.when(jnp.logical_not(is_home))
    def _():
        values = jnp.log(jnp.where(main_lane[...] >= 0, main_sums[...], 1.0))
        for source in range(lay.n_owner):
            start = source * lay.main
            out_ref[source, :, : lay.main] = values[:, start : start + lay.main]


def pair_call(kernel, lay, arrays, out_shape, sides, joins, more=(), out_specs=None, pairs=0):
    width = arrays[0].shape[1]
    side = pltpu.VMEM((sides[0], LANES), jnp.float32)
    rows = pltpu.VMEM((joins[0], width), jnp.bfloat16)
    buffer = pltpu.VMEM((lay.n_main // 2, 2 * WIDE), jnp.float32)
    out = pl.pallas_call(
        functools.partial(kernel, lay),
        out_shape=out_shape,
        in_specs=list(vmem_specs(len(arrays))),
        out_specs=out_specs or vmem_specs(len(out_shape)),
        scratch_shapes=[side] * sides[1] + [rows] * joins[1] + list(more) + [buffer, buffer],
        compiler_params=pltpu.CompilerParams(vmem_limit_bytes=FAST_LIMIT),
        cost_estimate=pl.CostEstimate(
            flops=2 * pairs * width, bytes_accessed=1, transcendentals=pairs
        ),
    )(*arrays)
    return out


def fast_unpack_kernel(values_ref, pos_ref, out_ref):
    pos = pos_ref[...]
    lane = lax.rem(pos, LANES)
    line = lax.div(pos, LANES)
    out = jnp.zeros(pos.shape, jnp.float32)
    per = values_ref.shape[2] // LANES
    for r in range(values_ref.shape[0] * per):
        start = r % per * LANES
        table = jnp.broadcast_to(values_ref[r // per, :, start : start + LANES], pos.shape)
        found = jnp.take_along_axis(table, lane, axis=1)
        out = jnp.where(line == r, found, out)
    out_ref[...] = out


def fast_unpack(values, pos):
    vmem = pl.BlockSpec(memory_space=pltpu.VMEM)
    return pl.pallas_call(
        fast_unpack_kernel,
        out_shape=jax.ShapeDtypeStruct(pos.shape, jnp.float32),
        in_specs=[vmem, vmem],
        out_specs=vmem,
    )(values, pos)


def general(embeddings, labels, owner_map):
    n_owner = lax.axis_size("cl")
    capacity = SLOTS // n_owner
    rows, width = embeddings.shape
    packed, pos, counts = pack(embeddings, labels, owner_map, n_owner, capacity)
    counts = lax.all_gather(counts, ("cl", "grp"), tiled=True)
    mine = lax.all_to_all(
        packed.reshape(n_owner, capacity, width), "cl", split_axis=0, concat_axis=0, tiled=True
    ).reshape(SLOTS, width)
    other = lax.ppermute(mine, "grp", [(0, 1), (1, 0)])
    results = log_counts(counts, mine, other, n_owner, capacity)
    returned = lax.all_to_all(
        results.reshape(n_owner, capacity), "cl", split_axis=0, concat_axis=0, tiled=True
    )
    return unpack(returned.reshape(SLOTS), pos).reshape(rows)


def body(embeddings, labels, owner_map):
    n_owner = lax.axis_size("cl")
    capacity = SLOTS // n_owner
    rows, width = embeddings.shape
    n_fine = owner_map.shape[0]
    main = -(-(rows // n_owner * 9 // 8) // 16) * 16
    if main >= capacity or n_fine >= LANES:
        return general(embeddings, labels, owner_map)
    home = n_owner // 4
    lay = Layout(n_owner, n_fine, capacity, main, home)
    unit, slot, info, extra, pos = place_rows(embeddings, labels, owner_map, lay)
    packed = pack_main(unit, slot, info, lay)
    planes, plane = n_owner // 2, home // 2
    turning = [z for z in range(planes) if z not in (plane, plane + 1)]
    moved = lax.ppermute(extra, "cl", [(2 * z + 1, 2 * z) for z in turning])
    both = pair_up(extra, moved)
    chunks = []
    for z in range(planes):
        if z in turning:
            chunks.append(lax.ppermute(both, "cl", [(2 * z, home)]))
        else:
            for source in (2 * z, 2 * z + 1):
                chunks.append(
                    extra if source == home else lax.ppermute(extra, "cl", [(source, home)])
                )
    mine = lax.all_to_all(
        packed.reshape(n_owner, main, width), "cl", split_axis=0, concat_axis=0, tiled=True
    ).reshape(n_owner * main, width)
    mine = after(mine, both)
    other = lax.ppermute(mine, "grp", [(0, 1), (1, 0)])
    row = jax.ShapeDtypeStruct((1, lay.n_main), jnp.float32)
    lines = lay.n_head + lay.n_rest
    long_row = jax.ShapeDtypeStruct((1, lines), jnp.float32)
    flag = jax.ShapeDtypeStruct((1, 1), jnp.int32)
    table = jax.ShapeDtypeStruct((n_owner, 1, capacity), jnp.float32)
    sides, joins = (lay.n_main, 2), (lay.n_head, 1)
    sums, main_lane = pair_call(inner_kernel, lay, (mine,), (row, row), sides, joins)
    joins = (lay.n_head, 2)
    arrays = (mine, other, sums, main_lane)
    specs = (pl.BlockSpec(memory_space=pltpu.VMEM), pl.BlockSpec(memory_space=pltpu.SMEM))
    sums, unfit = pair_call(cross_kernel, lay, arrays, (row, flag), sides, joins, out_specs=specs)
    rest = gather_rest(chunks, home, sums)
    swap = [(2 * home, 2 * home + 1), (2 * home + 1, 2 * home)]
    rest_other = lax.ppermute(rest, ("cl", "grp"), swap)
    rest_sums, lane = pair_call(
        inner_rest_kernel,
        lay,
        (mine, rest),
        (long_row, long_row),
        (lines, 1),
        (lines, 1),
        pairs=3 * lay.n_head * lay.n_rest,
    )
    arrays = (mine, other, rest, rest_other, sums, main_lane, rest_sums, lane)
    total = pltpu.VMEM(long_row.shape, jnp.float32)
    (results,) = pair_call(
        cross_rest_kernel, lay, arrays, (table,), (lines, 1), (lines, 2), (total,)
    )
    returned = lax.all_to_all(results, "cl", split_axis=0, concat_axis=0, tiled=True)
    return lax.cond(
        unfit[0, 0] == 0,
        lambda: fast_unpack(returned, pos).reshape(rows),
        lambda: general(embeddings, labels, owner_map),
    )


def solution(mesh):
    return jax.shard_map(
        body,
        mesh=mesh,
        in_specs=(P(("parts", "cl", "grp"), None), P(("parts", "cl", "grp")), P("parts")),
        out_specs=P(("parts", "cl", "grp")),
        check_vma=False,
    )
```

```python
import functools
import math

import jax
import jax.numpy as jnp
from jax import lax
from jax.experimental import pallas as pl
from jax.experimental.pallas import tpu as pltpu
from jax.sharding import PartitionSpec as P

SLOTS = 2048

temper = 0.2
neighbour_factor = 0.5
epsilon = 1e-06

LANES = 128
SCALE = math.log2(math.e) / temper
NEIGHBOUR = math.log2(neighbour_factor)
DEAD = -1e30
VMEM_LIMIT = 48 * 1024 * 1024
FAST_LIMIT = 24 * 1024 * 1024
WIDE = 512
INFO = 16


def column_of(row):
    pieces = []
    for start in range(0, row.shape[1], LANES):
        width = min(LANES, row.shape[1] - start)
        shape = (width, width)
        diagonal = lax.broadcasted_iota(jnp.int32, shape, 0) == lax.broadcasted_iota(
            jnp.int32, shape, 1
        )
        piece = jnp.broadcast_to(row[:, start : start + width], shape)
        pieces.append(jnp.sum(jnp.where(diagonal, piece, 0.0), axis=1, keepdims=True))
    return jnp.concatenate(pieces, axis=0)


def row_of(column):
    n = column.shape[0]
    diagonal = lax.broadcasted_iota(jnp.int32, (n, n), 0) == lax.broadcasted_iota(
        jnp.int32, (n, n), 1
    )
    return jnp.sum(jnp.where(diagonal, column, 0.0), axis=0, keepdims=True)


def pack_kernel(n_owner, capacity, x_ref, lab_ref, map_ref, out_ref, pos_ref, cnt_ref, unit, pos_row):
    rows = x_ref.shape[0]
    n_fine = map_ref.shape[1]
    per_owner = n_fine // n_owner
    owner_row = map_ref[...].astype(jnp.float32)
    fine_row = lax.broadcasted_iota(jnp.int32, (1, n_fine), 1).astype(jnp.float32)
    key_row = owner_row * n_fine + fine_row
    key_col = column_of(key_row)
    sorted_col = jnp.sum(jnp.where(key_row < key_col, 1.0, 0.0), axis=1, keepdims=True)
    lab = lab_ref[...].astype(jnp.float32)
    lab_row = jnp.concatenate([lab[b : b + 1, :] for b in range(lab.shape[0])], axis=1)
    fine_col = lax.broadcasted_iota(jnp.int32, (n_fine, rows), 0).astype(jnp.float32)
    fine_id = jnp.sum(jnp.where(fine_col == lab_row, sorted_col, 0.0), axis=0, keepdims=True)
    counts_col = jnp.sum(jnp.where(fine_col == fine_id, 1.0, 0.0), axis=1, keepdims=True)
    cnt_ref[...] = row_of(counts_col).astype(jnp.int32)
    coarse = jnp.floor((fine_id + 0.5) * (1.0 / per_owner))
    before = jnp.sum(
        jnp.where(fine_col < coarse * per_owner, counts_col, 0.0), axis=0, keepdims=True
    )
    index = lax.broadcasted_iota(jnp.int32, (1, rows), 1).astype(jnp.float32)
    row_key = fine_id * rows + index
    rank = jnp.zeros((1, rows), jnp.float32)
    for start in range(0, rows, LANES):
        other = column_of(row_key[:, start : start + LANES])
        rank = rank + jnp.sum(jnp.where(other < row_key, 1.0, 0.0), axis=0, keepdims=True)
    pos = (coarse * capacity + rank - before).astype(jnp.int32)
    pos_row[...] = pos
    pos_ref[...] = jnp.concatenate(
        [pos[:, start : start + LANES] for start in range(0, rows, LANES)], axis=0
    )
    x = x_ref[...].astype(jnp.float32)
    squares = jnp.sum(x * x, axis=1, keepdims=True)
    unit[...] = (x * lax.rsqrt(squares + epsilon)).astype(jnp.bfloat16)

    step = 256

    @pl.loop(0, out_ref.shape[0] // step)
    def _(block):
        slot = lax.broadcasted_iota(jnp.int32, (step, rows), 0) + block * step
        chosen = jnp.where(slot == pos_row[...], 1.0, 0.0).astype(jnp.bfloat16)
        packed = jnp.dot(chosen, unit[...], preferred_element_type=jnp.float32)
        out_ref[pl.ds(pl.multiple_of(block * step, step), step), :] = packed.astype(jnp.bfloat16)


def pack(embeddings, labels, owner_map, n_owner, capacity):
    rows, width = embeddings.shape
    n_fine = owner_map.shape[0]
    total = n_owner * capacity
    vmem = pl.BlockSpec(memory_space=pltpu.VMEM)
    return pl.pallas_call(
        functools.partial(pack_kernel, n_owner, capacity),
        out_shape=(
            jax.ShapeDtypeStruct((total, width), jnp.bfloat16),
            jax.ShapeDtypeStruct((rows // LANES, LANES), jnp.int32),
            jax.ShapeDtypeStruct((1, n_fine), jnp.int32),
        ),
        in_specs=[vmem] * 3,
        out_specs=(vmem, vmem, vmem),
        scratch_shapes=[pltpu.VMEM((rows, width), jnp.bfloat16), pltpu.VMEM((1, rows), jnp.int32)],
        compiler_params=pltpu.CompilerParams(vmem_limit_bytes=VMEM_LIMIT),
    )(embeddings, labels.reshape(rows // LANES, LANES), owner_map.reshape(1, n_fine))


def counts_kernel(n_owner, capacity, cnt_ref, mine_ref, other_ref, out_ref, lab_lane, lab_sub, bias):
    total = mine_ref.shape[0]
    per_owner = cnt_ref.shape[1] // n_owner
    me = lax.axis_index("cl")
    grp = lax.axis_index("grp")
    n_grp = lax.axis_size("grp")
    for member in range(2):
        for source in range(n_owner):
            line = source * n_grp + lax.rem(grp + member, n_grp)
            edges = []
            edge = jnp.int32(0)
            for f in range(per_owner):
                edge = edge + cnt_ref[line, me * per_owner + f]
                edges.append(edge)
            down = lax.broadcasted_iota(jnp.int32, (capacity, LANES), 0)
            label = jnp.zeros((capacity, LANES), jnp.int32)
            for edge in edges:
                label = label + jnp.where(down >= edge, 1, 0)
            start = (member * n_owner + source) * capacity
            lab_sub[start : start + capacity, :] = label
            bias[start : start + capacity, :] = jnp.where(
                label < per_owner, NEIGHBOUR - SCALE, DEAD
            )
            if member == 0:
                across = lax.broadcasted_iota(jnp.int32, (1, capacity), 1)
                label = jnp.zeros((1, capacity), jnp.int32)
                for edge in edges:
                    label = label + jnp.where(across >= edge, 1, 0)
                lab_lane[:, source * capacity : (source + 1) * capacity] = jnp.where(
                    label < per_owner, label, -1
                )
    wide, deep = min(512, total), min(256, total)

    @pl.loop(0, total // wide)
    def _(block):
        columns = pl.ds(pl.multiple_of(block * wide, wide), wide)
        rows_i = mine_ref[columns, :]
        label_i = lab_lane[:, columns]

        def add(ref, offset):
            def step(j, acc):
                start = pl.multiple_of(j * deep, deep)
                scores = lax.dot_general(
                    ref[pl.ds(start, deep), :],
                    rows_i,
                    (((1,), (1,)), ((), ())),
                    preferred_element_type=jnp.float32,
                )
                place = pl.ds(pl.multiple_of(start + offset, deep), deep)
                label_j = lab_sub[place, :]
                bias_j = bias[place, :]
                repeat = wide // LANES
                label_j = jnp.concatenate([label_j] * repeat, axis=1)
                bias_j = jnp.concatenate([bias_j] * repeat, axis=1)
                shift = jnp.where(label_j == label_i, -SCALE, bias_j)
                terms = jnp.exp2(scores * SCALE + shift)
                return acc + jnp.sum(terms.reshape(deep // 8, 8, wide), axis=0)

            return step

        acc = jnp.zeros((8, wide), jnp.float32)
        acc = lax.fori_loop(0, total // deep, add(mine_ref, 0), acc, unroll=2)
        acc = lax.fori_loop(0, total // deep, add(other_ref, total), acc, unroll=2)
        totals = jnp.sum(acc, axis=0, keepdims=True)
        out_ref[:, columns] = jnp.log(jnp.where(label_i >= 0, totals, 1.0))


def log_counts(counts, mine, other, n_owner, capacity):
    total = mine.shape[0]
    vmem = pl.BlockSpec(memory_space=pltpu.VMEM)
    return pl.pallas_call(
        functools.partial(counts_kernel, n_owner, capacity),
        out_shape=jax.ShapeDtypeStruct((1, total), jnp.float32),
        in_specs=[pl.BlockSpec(memory_space=pltpu.SMEM), vmem, vmem],
        out_specs=vmem,
        scratch_shapes=[
            pltpu.VMEM((1, total), jnp.int32),
            pltpu.VMEM((2 * total, LANES), jnp.int32),
            pltpu.VMEM((2 * total, LANES), jnp.float32),
        ],
        compiler_params=pltpu.CompilerParams(vmem_limit_bytes=VMEM_LIMIT),
    )(counts, mine, other)


def unpack_kernel(values_ref, pos_ref, out_ref):
    pos = pos_ref[...]
    lane = lax.rem(pos, LANES)
    line = lax.div(pos, LANES)
    out = jnp.zeros(pos.shape, jnp.float32)
    for r in range(values_ref.shape[0]):
        table = jnp.broadcast_to(values_ref[r : r + 1, :], pos.shape)
        found = jnp.take_along_axis(table, lane, axis=1)
        out = jnp.where(line == r, found, out)
    out_ref[...] = out


def unpack(values, pos):
    vmem = pl.BlockSpec(memory_space=pltpu.VMEM)
    return pl.pallas_call(
        unpack_kernel,
        out_shape=jax.ShapeDtypeStruct(pos.shape, jnp.float32),
        in_specs=[vmem, vmem],
        out_specs=vmem,
    )(values.reshape(-1, LANES), pos)


def swapped(x, first, second):
    return jnp.where(x == first, second, jnp.where(x == second, first, x))


def place_kernel(lay, x_hbm, lab_hbm, map_hbm, *refs):
    n_owner, capacity, main, home = lay.n_owner, lay.capacity, lay.main, lay.home
    unit, slot_ref, info_ref, extra_ref, pos_ref, x_ref, lab_ref, map_ref, sems = refs
    copies = [
        pltpu.make_async_copy(src, dst, sems.at[i])
        for i, (src, dst) in enumerate(((x_hbm, x_ref), (lab_hbm, lab_ref), (map_hbm, map_ref)))
    ]
    for copy in copies:
        copy.start()
    rows = x_ref.shape[0]
    n_fine = map_ref.shape[1]
    per_owner = n_fine // n_owner
    copies[1].wait()
    copies[2].wait()
    owner_row = map_ref[...].astype(jnp.float32)
    fine_row = lax.broadcasted_iota(jnp.int32, (1, n_fine), 1).astype(jnp.float32)
    key_row = owner_row * n_fine + fine_row
    key_col = column_of(key_row)
    sorted_col = jnp.sum(jnp.where(key_row < key_col, 1.0, 0.0), axis=1, keepdims=True)
    lab = lab_ref[...].astype(jnp.float32)
    lab_row = jnp.concatenate([lab[b : b + 1, :] for b in range(lab.shape[0])], axis=1)
    fine_col = lax.broadcasted_iota(jnp.int32, (n_fine, rows), 0).astype(jnp.float32)
    fine_id = jnp.sum(jnp.where(fine_col == lab_row, sorted_col, 0.0), axis=0, keepdims=True)
    counts_col = jnp.sum(jnp.where(fine_col == fine_id, 1.0, 0.0), axis=1, keepdims=True)
    coarse = jnp.floor((fine_id + 0.5) * (1.0 / per_owner))
    first = coarse * per_owner
    before = jnp.sum(jnp.where(fine_col < first, counts_col, 0.0), axis=0, keepdims=True)
    upto = jnp.sum(jnp.where(fine_col < first + per_owner, counts_col, 0.0), axis=0, keepdims=True)
    full = jnp.min(
        jnp.where(upto - before == capacity, coarse, float(n_owner)), axis=1, keepdims=True
    )
    line = lax.broadcasted_iota(jnp.int32, (n_fine, LANES), 0)
    lane = lax.broadcasted_iota(jnp.int32, (n_fine, LANES), 1)
    inside = (line <= lane) & (lax.div(line, per_owner) == lax.div(lane, per_owner))
    running = jnp.sum(jnp.where(inside, counts_col, 0.0), axis=0, keepdims=True)
    info = jnp.where(lane[:1] < n_fine, running, full)
    info_ref[...] = info
    index = lax.broadcasted_iota(jnp.int32, (1, rows), 1).astype(jnp.float32)
    row_key = fine_id * rows + index
    rank = jnp.zeros((1, rows), jnp.float32)
    for start in range(0, rows, LANES):
        other = column_of(row_key[:, start : start + LANES])
        rank = rank + jnp.sum(jnp.where(other < row_key, 1.0, 0.0), axis=0, keepdims=True)
    rank = (rank - before).astype(jnp.int32)
    place = swapped(coarse.astype(jnp.int32), full.astype(jnp.int32), home)
    table = place * capacity + rank
    pos_ref[...] = jnp.concatenate(
        [table[:, start : start + LANES] for start in range(0, rows, LANES)], axis=0
    )
    later = jnp.where(place == home, lay.n_main + rank - lay.head, -1)
    fits = rank < jnp.where(place == home, lay.head, main - 1)
    slot = jnp.where(fits, place * main + rank, later)
    slot_ref[...] = slot
    copies[0].wait()
    x = x_ref[...].astype(jnp.float32)
    squares = jnp.sum(x * x, axis=1, keepdims=True)
    unit[...] = (x * lax.rsqrt(squares + epsilon)).astype(jnp.bfloat16)
    extra_ref[...] = chosen_rows(unit, slot, lay.n_main, lay.rest)


def chosen_rows(unit, slot, start, count):
    here = lax.broadcasted_iota(jnp.int32, (count, unit.shape[0]), 0) + start
    chosen = jnp.where(here == slot, 1.0, 0.0).astype(jnp.bfloat16)
    return jnp.dot(chosen, unit[...], preferred_element_type=jnp.float32).astype(jnp.bfloat16)


def main_kernel(lay, unit, slot_ref, info_ref, main_ref):
    count = lay.n_main // 4
    for start in range(0, lay.n_main, count):
        main_ref[start : start + count, :] = chosen_rows(unit, slot_ref[...], start, count)
    for owner in range(lay.n_owner):
        tail = slice((owner + 1) * lay.main - INFO, (owner + 1) * lay.main)
        old = main_ref[tail, :LANES].astype(jnp.float32)
        down = lax.broadcasted_iota(jnp.int32, old.shape, 0)
        new = jnp.where(down == INFO - 1, info_ref[...], old)
        main_ref[tail, :LANES] = new.astype(jnp.bfloat16)


def vmem_specs(count):
    return (pl.BlockSpec(memory_space=pltpu.VMEM),) * count


def place_rows(embeddings, labels, owner_map, lay):
    rows, width = embeddings.shape
    n_fine = owner_map.shape[0]
    lab_shape = (rows // LANES, LANES)
    return pl.pallas_call(
        functools.partial(place_kernel, lay),
        out_shape=(
            jax.ShapeDtypeStruct((rows, width), jnp.bfloat16),
            jax.ShapeDtypeStruct((1, rows), jnp.int32),
            jax.ShapeDtypeStruct((1, LANES), jnp.float32),
            jax.ShapeDtypeStruct((lay.rest, width), jnp.bfloat16),
            jax.ShapeDtypeStruct(lab_shape, jnp.int32),
        ),
        in_specs=[pl.BlockSpec(memory_space=pl.ANY)] * 3,
        out_specs=vmem_specs(5),
        scratch_shapes=[
            pltpu.VMEM((rows, width), jnp.bfloat16),
            pltpu.VMEM(lab_shape, jnp.int32),
            pltpu.VMEM((1, n_fine), jnp.int32),
            pltpu.SemaphoreType.DMA((3,)),
        ],
        compiler_params=pltpu.CompilerParams(vmem_limit_bytes=FAST_LIMIT),
    )(embeddings, labels.reshape(lab_shape), owner_map.reshape(1, n_fine))


def pack_main(unit, slot, info, lay):
    return pl.pallas_call(
        functools.partial(main_kernel, lay),
        out_shape=jax.ShapeDtypeStruct((lay.n_main, unit.shape[1]), jnp.bfloat16),
        in_specs=list(vmem_specs(3)),
        out_specs=vmem_specs(1)[0],
        compiler_params=pltpu.CompilerParams(vmem_limit_bytes=FAST_LIMIT),
        cost_estimate=pl.CostEstimate(
            flops=2 * lay.n_main * unit.shape[0] * unit.shape[1],
            bytes_accessed=4 * unit.shape[0] * unit.shape[1],
            transcendentals=0,
        ),
    )(unit, slot, info)


def gate_kernel(*refs):
    pass


def after(rows, there):
    return pl.pallas_call(
        gate_kernel,
        out_shape=jax.ShapeDtypeStruct(rows.shape, rows.dtype),
        in_specs=list(vmem_specs(2)),
        out_specs=vmem_specs(1)[0],
        input_output_aliases={0: 0},
        compiler_params=pltpu.CompilerParams(vmem_limit_bytes=FAST_LIMIT),
    )(rows, there)


def lay_out_kernel(n_arrays, home, *refs):
    chunks, out = refs[:n_arrays], refs[-1]

    def copy():
        start = 0
        for chunk in chunks:
            out[start : start + chunk.shape[0], :] = chunk[...]
            start += chunk.shape[0]

    if home is None:
        copy()
    else:
        pl.when(lax.axis_index("cl") == home)(copy)


def lay_out(chunks, home=None, waits=()):
    rows, width = sum(x.shape[0] for x in chunks), chunks[0].shape[1]
    return pl.pallas_call(
        functools.partial(lay_out_kernel, len(chunks), home),
        out_shape=jax.ShapeDtypeStruct((rows, width), jnp.bfloat16),
        in_specs=list(vmem_specs(len(chunks) + len(waits))),
        out_specs=vmem_specs(1)[0],
        compiler_params=pltpu.CompilerParams(vmem_limit_bytes=FAST_LIMIT),
    )(*chunks, *waits)


class Layout:
    early, late = (0, 1, 2, 3), (4, 6, 5, 7)

    def __init__(self, n_owner, n_fine, capacity, main, home):
        self.n_owner, self.n_fine, self.capacity = n_owner, n_fine, capacity
        self.main, self.home = main, home
        self.head = main - INFO
        self.rest = capacity - self.head
        self.per_owner = n_fine // n_owner
        self.n_main = n_owner * main
        self.n_head = n_owner * self.head
        self.n_early = len(self.early) * self.rest
        self.n_late = len(self.late) * self.rest
        self.n_first = self.n_head + self.n_early
        self.n_all = self.n_first + self.n_late


def info_line(lay, main_ref, source):
    end = (source + 1) * lay.main
    return main_ref[end - INFO : end, :LANES].astype(jnp.float32)[INFO - 1 :]


def lines_of(lay, main_ref):
    return [info_line(lay, main_ref, source) for source in range(lay.n_owner)]


def hot_of(lay, info):
    lane = lax.broadcasted_iota(jnp.int32, (1, LANES), 1)
    hot = jnp.max(jnp.where(lane == lay.n_fine, info, 0.0), axis=1, keepdims=True)
    return hot.astype(jnp.int32)


def write_labels(lay, infos, sources, first, count, at, lab_sub, bias):
    cluster = swapped(lax.axis_index("cl"), hot_of(lay, infos[0]), lay.home)
    lane = lax.broadcasted_iota(jnp.int32, (1, LANES), 1)
    is_edge = lax.div(lane, lay.per_owner) == cluster
    for i, source in enumerate(sources):
        edges = jnp.where(is_edge, infos[source], 2.0 * lay.capacity)
        slot = lax.broadcasted_iota(jnp.int32, (count, LANES), 0) + first
        label = jnp.where(slot.astype(jnp.float32) >= edges, 1.0, 0.0)
        label = jnp.broadcast_to(jnp.sum(label, axis=1, keepdims=True), (count, LANES))
        start = at + i * count
        lab_sub[start : start + count, :] = label
        if bias is not None:
            bias[start : start + count, :] = jnp.where(
                label < lay.per_owner, NEIGHBOUR - SCALE, DEAD
            )


def first_labels(lay, infos, lab_sub):
    write_labels(lay, infos, range(lay.n_owner), 0, lay.head, 0, lab_sub, None)
    write_labels(lay, infos, lay.early, lay.head, lay.rest, lay.n_head, lab_sub, None)


def late_labels(lay, infos, lab_sub):
    write_labels(lay, infos, lay.late, lay.head, lay.rest, 0, lab_sub, None)


def turn_labels(lay, lab_sub, count, lab_lane, at):
    for i in range(0, count, LANES):
        block = jnp.transpose(lab_sub[i : i + LANES, :])[:1]
        lab_lane[:, at + i : at + i + LANES] = jnp.where(block < lay.per_owner, block, -1.0)


def copy_head(lay, main_ref, rows):
    for source in range(lay.n_owner):
        rows[source * lay.head : (source + 1) * lay.head, :] = main_ref[
            source * lay.main : source * lay.main + lay.head, :
        ]


def pieces(count, parts):
    return [(i * (count // parts), count // parts) for i in range(parts)]


def stream(lanes, tiles, lab_lane, buffers, put):
    rows_i, count, at = lanes
    step = 32
    tiles = [
        (ref, s, d, lab_sub, bias, line + s)
        for ref, n, lab_sub, bias, line, parts in tiles
        for s, d in pieces(n, parts)
    ]

    def scores_to(buffer, tile, rows):
        ref, start, deep = tile[:3]
        buffer[:deep, : rows.shape[0]] = lax.dot_general(
            ref[start : start + deep, :],
            rows,
            (((1,), (1,)), ((), ())),
            preferred_element_type=jnp.float32,
        )

    def run(start, blocks, wide):
        repeat = wide // LANES

        def rows_of(block):
            return rows_i[pl.ds(pl.multiple_of(start + block * wide, LANES), wide), :]

        scores_to(buffers[0], tiles[0], rows_of(0))

        def body(block, carry):
            here = rows_of(block)
            place = pl.ds(pl.multiple_of(at + start + block * wide, LANES), wide)
            label_i = lab_lane[:, place]
            acc = jnp.zeros((8, wide), jnp.float32)
            for i, (_, _, deep, lab_sub, bias, line) in enumerate(tiles):
                if i + 1 < len(tiles):
                    scores_to(buffers[(i + 1) % 2], tiles[i + 1], here)
                else:
                    scores_to(buffers[0], tiles[0], rows_of(jnp.minimum(block + 1, blocks - 1)))
                buffer = buffers[i % 2]
                for c in range(0, deep, step):
                    part = slice(line + c, line + c + step)
                    label_j = jnp.concatenate([lab_sub[part, :]] * repeat, axis=1)
                    if bias is None:
                        bias_j = NEIGHBOUR - SCALE
                    else:
                        bias_j = jnp.concatenate([bias[part, :]] * repeat, axis=1)
                    shift = jnp.where(label_j == label_i, -SCALE, bias_j)
                    terms = jnp.exp2(buffer[c : c + step, :wide] * SCALE + shift)
                    acc = acc + jnp.sum(terms.reshape(step // 8, 8, wide), axis=0)
            put(place, jnp.sum(acc, axis=0, keepdims=True))
            return carry

        lax.fori_loop(0, blocks, body, 0)

    if count >= WIDE:
        run(0, count // WIDE, WIDE)
    if count % WIDE:
        run(count - count % WIDE, 1, count % WIDE)


def setter(ref):
    def put(place, values):
        ref[:, place] = values

    return put


def adder(ref):
    def put(place, values):
        ref[:, place] += values

    return put


def inner_kernel(lay, mine, early, sums, lab_lane, lab_sub, rows, bias, buf_a, buf_b):
    is_home = lax.axis_index("cl") == lay.home
    infos = lines_of(lay, mine)
    buffers = (buf_a, buf_b)

    @pl.when(is_home)
    def _():
        copy_head(lay, mine, rows)
        first_labels(lay, infos, lab_sub)
        turn_labels(lay, lab_sub, lay.n_first, lab_lane, 0)
        tiles = [(rows, lay.n_head, lab_sub, None, 0, 2)]
        tiles += [(early, lay.n_early, lab_sub, None, lay.n_head, 2)]
        stream((rows, lay.n_head, 0), tiles, lab_lane, buffers, setter(sums))
        stream((early, lay.n_early, lay.n_head), tiles, lab_lane, buffers, setter(sums))

    @pl.when(jnp.logical_not(is_home))
    def _():
        write_labels(lay, infos, range(lay.n_owner), 0, lay.main, 0, lab_sub, bias)
        turn_labels(lay, lab_sub, lay.n_main, lab_lane, 0)
        tiles = [(mine, lay.n_main, lab_sub, bias, 0, 2)]
        stream((mine, lay.n_main, 0), tiles, lab_lane, buffers, setter(sums))


def cross_kernel(lay, mine, other, early, early_j, rows, sums, lab_lane, *refs):
    total, unfit_ref, lab_sub, rows_j, bias, buf_a, buf_b = refs
    is_home = lax.axis_index("cl") == lay.home
    infos = lines_of(lay, other)
    own = lines_of(lay, mine)
    hot = hot_of(lay, own[0])
    lane = lax.broadcasted_iota(jnp.int32, (1, LANES), 1)
    last = (lane < lay.n_fine) & (lax.rem(lane, lay.per_owner) == lay.per_owner - 1)
    last = last & (lax.div(lane, lay.per_owner) != hot)
    unfit = jnp.zeros((1, LANES), jnp.float32)
    for info in infos + own:
        wrong = last & (info >= lay.main)
        differs = (info != hot.astype(jnp.float32)) | (info >= lay.n_owner)
        wrong = wrong | ((lane == lay.n_fine) & differs)
        unfit = unfit + jnp.where(wrong, 1.0, 0.0)
    unfit_ref[0, 0] = jnp.max(unfit).astype(jnp.int32)
    total[...] = sums[...]
    buffers = (buf_a, buf_b)

    @pl.when(is_home)
    def _():
        copy_head(lay, other, rows_j)
        first_labels(lay, infos, lab_sub)
        tiles = [(rows_j, lay.n_head, lab_sub, None, 0, 2)]
        tiles += [(early_j, lay.n_early, lab_sub, None, lay.n_head, 2)]
        stream((rows, lay.n_head, 0), tiles, lab_lane, buffers, adder(total))
        stream((early, lay.n_early, lay.n_head), tiles, lab_lane, buffers, adder(total))

    @pl.when(jnp.logical_not(is_home))
    def _():
        write_labels(lay, infos, range(lay.n_owner), 0, lay.main, 0, lab_sub, bias)
        tiles = [(other, lay.n_main, lab_sub, bias, 0, 2)]
        stream((mine, lay.n_main, 0), tiles, lab_lane, buffers, adder(total))


def late_pairs(lay, i_refs, j_refs, lab_sub, late_sub, lab_lane, buffers, put):
    rows, early, late = i_refs
    rows_j, early_j, late_j = j_refs
    lates = [(late_j, lay.n_late, late_sub, None, 0, 2)]
    every = lates + [(rows_j, lay.n_head, lab_sub, None, 0, 2)]
    every += [(early_j, lay.n_early, lab_sub, None, lay.n_head, 2)]
    stream((rows, lay.n_head, 0), lates, lab_lane, buffers, put)
    stream((early, lay.n_early, lay.n_head), lates, lab_lane, buffers, put)
    stream((late, lay.n_late, lay.n_first), every, lab_lane, buffers, put)


def inner_late_kernel(lay, mine, early, late, rows, lab_sub, first_lane, *refs):
    sums, lab_lane, late_sub, buf_a, buf_b = refs

    @pl.when(lax.axis_index("cl") == lay.home)
    def _():
        late_labels(lay, lines_of(lay, mine), late_sub)
        lab_lane[:, : lay.n_first] = first_lane[...]
        turn_labels(lay, late_sub, lay.n_late, lab_lane, lay.n_first)
        refs = (rows, early, late)
        buffers = (buf_a, buf_b)
        late_pairs(lay, refs, refs, lab_sub, late_sub, lab_lane, buffers, setter(sums))


def cross_late_kernel(lay, other, early, late, early_j, late_j, rows, rows_j, *refs):
    lab_sub, first_lane, first_sums, lab_lane, sums = refs[:5]
    out_ref, total, late_sub, buf_a, buf_b = refs[5:]
    is_home = lax.axis_index("cl") == lay.home

    @pl.when(is_home)
    def _():
        late_labels(lay, lines_of(lay, other), late_sub)
        total[...] = sums[...]
        total[:, : lay.n_first] += first_sums[...]
        i_refs, j_refs = (rows, early, late), (rows_j, early_j, late_j)
        buffers = (buf_a, buf_b)
        late_pairs(lay, i_refs, j_refs, lab_sub, late_sub, lab_lane, buffers, adder(total))
        values = jnp.log(total[...])
        for source in range(lay.n_owner):
            start = source * lay.head
            out_ref[source, :, : lay.head] = values[:, start : start + lay.head]
        for i, source in enumerate(lay.early + lay.late):
            start = lay.n_head + i * lay.rest
            out_ref[source, :, lay.head :] = values[:, start : start + lay.rest]

    @pl.when(jnp.logical_not(is_home))
    def _():
        values = jnp.log(jnp.where(first_lane[...] >= 0, first_sums[...], 1.0))
        for source in range(lay.n_owner):
            start = source * lay.main
            out_ref[source, :, : lay.main] = values[:, start : start + lay.main]


def pair_call(kernel, lay, arrays, out_shape, scratch, out_specs=None, pairs=0):
    width = arrays[0].shape[1]
    buffer = pltpu.VMEM((lay.n_main // 2, WIDE), jnp.float32)
    return pl.pallas_call(
        functools.partial(kernel, lay),
        out_shape=out_shape,
        in_specs=list(vmem_specs(len(arrays))),
        out_specs=out_specs or vmem_specs(len(out_shape)),
        scratch_shapes=list(scratch) + [buffer, buffer],
        compiler_params=pltpu.CompilerParams(vmem_limit_bytes=FAST_LIMIT),
        cost_estimate=pl.CostEstimate(
            flops=2 * pairs * width, bytes_accessed=1, transcendentals=pairs
        ),
    )(*arrays)


def fast_unpack_kernel(values_ref, pos_ref, out_ref):
    pos = pos_ref[...]
    lane = lax.rem(pos, LANES)
    line = lax.div(pos, LANES)
    out = jnp.zeros(pos.shape, jnp.float32)
    per = values_ref.shape[2] // LANES
    for r in range(values_ref.shape[0] * per):
        start = r % per * LANES
        table = jnp.broadcast_to(values_ref[r // per, :, start : start + LANES], pos.shape)
        found = jnp.take_along_axis(table, lane, axis=1)
        out = jnp.where(line == r, found, out)
    out_ref[...] = out


def fast_unpack(values, pos):
    vmem = pl.BlockSpec(memory_space=pltpu.VMEM)
    return pl.pallas_call(
        fast_unpack_kernel,
        out_shape=jax.ShapeDtypeStruct(pos.shape, jnp.float32),
        in_specs=[vmem, vmem],
        out_specs=vmem,
    )(values, pos)


def general(embeddings, labels, owner_map):
    n_owner = lax.axis_size("cl")
    capacity = SLOTS // n_owner
    rows, width = embeddings.shape
    packed, pos, counts = pack(embeddings, labels, owner_map, n_owner, capacity)
    counts = lax.all_gather(counts, ("cl", "grp"), tiled=True)
    mine = lax.all_to_all(
        packed.reshape(n_owner, capacity, width), "cl", split_axis=0, concat_axis=0, tiled=True
    ).reshape(SLOTS, width)
    other = lax.ppermute(mine, "grp", [(0, 1), (1, 0)])
    results = log_counts(counts, mine, other, n_owner, capacity)
    returned = lax.all_to_all(
        results.reshape(n_owner, capacity), "cl", split_axis=0, concat_axis=0, tiled=True
    )
    return unpack(returned.reshape(SLOTS), pos).reshape(rows)


def body(embeddings, labels, owner_map):
    n_owner = lax.axis_size("cl")
    capacity = SLOTS // n_owner
    rows, width = embeddings.shape
    n_fine = owner_map.shape[0]
    main = -(-(rows // n_owner * 9 // 8) // 16) * 16
    if n_owner != 8 or main >= capacity or n_fine >= LANES:
        return general(embeddings, labels, owner_map)
    home = 2
    lay = Layout(n_owner, n_fine, capacity, main, home)
    unit, slot, info, extra, pos = place_rows(embeddings, labels, owner_map, lay)
    packed = pack_main(unit, slot, info, lay)

    def hop(x, pairs):
        return lax.ppermute(x, "cl", pairs)

    def swap(x):
        pairs = [(2 * home, 2 * home + 1), (2 * home + 1, 2 * home)]
        return lax.ppermute(x, ("cl", "grp"), pairs)

    both = lay_out([extra, hop(extra, [(1, 0), (6, 4), (7, 5)])])
    early = lay_out([hop(both, [(0, home)]), extra, hop(extra, [(3, home)])], home)
    early_j = swap(early)
    mine = lax.all_to_all(
        packed.reshape(n_owner, main, width), "cl", split_axis=0, concat_axis=0, tiled=True
    ).reshape(n_owner * main, width)
    mine = after(mine, early_j)
    other = lax.ppermute(mine, "grp", [(0, 1), (1, 0)])
    late = [hop(both, [(4, home)]), hop(both, [(5, home)])]

    def array(shape, dtype=jnp.float32):
        return jax.ShapeDtypeStruct(shape, dtype)

    def scratch(shape):
        return pltpu.VMEM(shape, jnp.float32)

    row, long_row = array((1, lay.n_first)), array((1, lay.n_all))
    side, bias = array((lay.n_first, LANES)), scratch((lay.n_main, LANES))
    heads = array((lay.n_head, width), jnp.bfloat16)
    late_side = scratch((lay.n_late, LANES))
    sums, first_lane, lab_sub, heads_i = pair_call(
        inner_kernel, lay, (mine, early), (row, row, side, heads), (bias,)
    )
    specs = vmem_specs(1) + (pl.BlockSpec(memory_space=pltpu.SMEM),) + vmem_specs(2)
    sums, unfit, lab_sub_j, heads_j = pair_call(
        cross_kernel,
        lay,
        (mine, other, early, early_j, heads_i, sums, first_lane),
        (row, array((1, 1), jnp.int32), side, heads),
        (bias,),
        specs,
    )
    late = lay_out(late, home, (sums,))
    late_j = swap(late)
    late_sums, lane = pair_call(
        inner_late_kernel,
        lay,
        (mine, early, late, heads_i, lab_sub, first_lane),
        (long_row, long_row),
        (late_side,),
        pairs=lay.n_late * (lay.n_all + lay.n_first),
    )
    (results,) = pair_call(
        cross_late_kernel,
        lay,
        (
            *(other, early, late, early_j, late_j, heads_i, heads_j),
            *(lab_sub_j, first_lane, sums, lane, late_sums),
        ),
        (array((n_owner, 1, capacity)),),
        (scratch(long_row.shape), late_side),
    )
    returned = lax.all_to_all(results, "cl", split_axis=0, concat_axis=0, tiled=True)
    return lax.cond(
        unfit[0, 0] == 0,
        lambda: fast_unpack(returned, pos).reshape(rows),
        lambda: general(embeddings, labels, owner_map),
    )


def solution(mesh):
    return jax.shard_map(
        body,
        mesh=mesh,
        in_specs=(P(("parts", "cl", "grp"), None), P(("parts", "cl", "grp")), P("parts")),
        out_specs=P(("parts", "cl", "grp")),
        check_vma=False,
    )
```

```python
import functools
import math

import jax
import jax.numpy as jnp
from jax import lax
from jax.experimental import pallas as pl
from jax.experimental.pallas import tpu as pltpu
from jax.sharding import PartitionSpec as P

SLOTS = 2048

temper = 0.2
neighbour_factor = 0.5
epsilon = 1e-06

LANES = 128
SCALE = math.log2(math.e) / temper
NEIGHBOUR = math.log2(neighbour_factor)
DEAD = -1e30
VMEM_LIMIT = 48 * 1024 * 1024
FAST_LIMIT = 16 * 1024 * 1024
WIDE = 512
INFO = 16


def column_of(row):
    pieces = []
    for start in range(0, row.shape[1], LANES):
        width = min(LANES, row.shape[1] - start)
        shape = (width, width)
        diagonal = lax.broadcasted_iota(jnp.int32, shape, 0) == lax.broadcasted_iota(
            jnp.int32, shape, 1
        )
        piece = jnp.broadcast_to(row[:, start : start + width], shape)
        pieces.append(jnp.sum(jnp.where(diagonal, piece, 0.0), axis=1, keepdims=True))
    return jnp.concatenate(pieces, axis=0)


def row_of(column):
    n = column.shape[0]
    diagonal = lax.broadcasted_iota(jnp.int32, (n, n), 0) == lax.broadcasted_iota(
        jnp.int32, (n, n), 1
    )
    return jnp.sum(jnp.where(diagonal, column, 0.0), axis=0, keepdims=True)


def pack_kernel(n_owner, capacity, x_ref, lab_ref, map_ref, out_ref, pos_ref, cnt_ref, unit, pos_row):
    rows = x_ref.shape[0]
    n_fine = map_ref.shape[1]
    per_owner = n_fine // n_owner
    owner_row = map_ref[...].astype(jnp.float32)
    fine_row = lax.broadcasted_iota(jnp.int32, (1, n_fine), 1).astype(jnp.float32)
    key_row = owner_row * n_fine + fine_row
    key_col = column_of(key_row)
    sorted_col = jnp.sum(jnp.where(key_row < key_col, 1.0, 0.0), axis=1, keepdims=True)
    lab = lab_ref[...].astype(jnp.float32)
    lab_row = jnp.concatenate([lab[b : b + 1, :] for b in range(lab.shape[0])], axis=1)
    fine_col = lax.broadcasted_iota(jnp.int32, (n_fine, rows), 0).astype(jnp.float32)
    fine_id = jnp.sum(jnp.where(fine_col == lab_row, sorted_col, 0.0), axis=0, keepdims=True)
    counts_col = jnp.sum(jnp.where(fine_col == fine_id, 1.0, 0.0), axis=1, keepdims=True)
    cnt_ref[...] = row_of(counts_col).astype(jnp.int32)
    coarse = jnp.floor((fine_id + 0.5) * (1.0 / per_owner))
    before = jnp.sum(
        jnp.where(fine_col < coarse * per_owner, counts_col, 0.0), axis=0, keepdims=True
    )
    index = lax.broadcasted_iota(jnp.int32, (1, rows), 1).astype(jnp.float32)
    row_key = fine_id * rows + index
    rank = jnp.zeros((1, rows), jnp.float32)
    for start in range(0, rows, LANES):
        other = column_of(row_key[:, start : start + LANES])
        rank = rank + jnp.sum(jnp.where(other < row_key, 1.0, 0.0), axis=0, keepdims=True)
    pos = (coarse * capacity + rank - before).astype(jnp.int32)
    pos_row[...] = pos
    pos_ref[...] = jnp.concatenate(
        [pos[:, start : start + LANES] for start in range(0, rows, LANES)], axis=0
    )
    x = x_ref[...].astype(jnp.float32)
    squares = jnp.sum(x * x, axis=1, keepdims=True)
    unit[...] = (x * lax.rsqrt(squares + epsilon)).astype(jnp.bfloat16)

    step = 256

    @pl.loop(0, out_ref.shape[0] // step)
    def _(block):
        slot = lax.broadcasted_iota(jnp.int32, (step, rows), 0) + block * step
        chosen = jnp.where(slot == pos_row[...], 1.0, 0.0).astype(jnp.bfloat16)
        packed = jnp.dot(chosen, unit[...], preferred_element_type=jnp.float32)
        out_ref[pl.ds(pl.multiple_of(block * step, step), step), :] = packed.astype(jnp.bfloat16)


def pack(embeddings, labels, owner_map, n_owner, capacity):
    rows, width = embeddings.shape
    n_fine = owner_map.shape[0]
    total = n_owner * capacity
    vmem = pl.BlockSpec(memory_space=pltpu.VMEM)
    return pl.pallas_call(
        functools.partial(pack_kernel, n_owner, capacity),
        out_shape=(
            jax.ShapeDtypeStruct((total, width), jnp.bfloat16),
            jax.ShapeDtypeStruct((rows // LANES, LANES), jnp.int32),
            jax.ShapeDtypeStruct((1, n_fine), jnp.int32),
        ),
        in_specs=[vmem] * 3,
        out_specs=(vmem, vmem, vmem),
        scratch_shapes=[pltpu.VMEM((rows, width), jnp.bfloat16), pltpu.VMEM((1, rows), jnp.int32)],
        compiler_params=pltpu.CompilerParams(vmem_limit_bytes=VMEM_LIMIT),
    )(embeddings, labels.reshape(rows // LANES, LANES), owner_map.reshape(1, n_fine))


def counts_kernel(n_owner, capacity, cnt_ref, mine_ref, other_ref, out_ref, lab_lane, lab_sub, bias):
    total = mine_ref.shape[0]
    per_owner = cnt_ref.shape[1] // n_owner
    me = lax.axis_index("cl")
    grp = lax.axis_index("grp")
    n_grp = lax.axis_size("grp")
    for member in range(2):
        for source in range(n_owner):
            line = source * n_grp + lax.rem(grp + member, n_grp)
            edges = []
            edge = jnp.int32(0)
            for f in range(per_owner):
                edge = edge + cnt_ref[line, me * per_owner + f]
                edges.append(edge)
            down = lax.broadcasted_iota(jnp.int32, (capacity, LANES), 0)
            label = jnp.zeros((capacity, LANES), jnp.int32)
            for edge in edges:
                label = label + jnp.where(down >= edge, 1, 0)
            start = (member * n_owner + source) * capacity
            lab_sub[start : start + capacity, :] = label
            bias[start : start + capacity, :] = jnp.where(
                label < per_owner, NEIGHBOUR - SCALE, DEAD
            )
            if member == 0:
                across = lax.broadcasted_iota(jnp.int32, (1, capacity), 1)
                label = jnp.zeros((1, capacity), jnp.int32)
                for edge in edges:
                    label = label + jnp.where(across >= edge, 1, 0)
                lab_lane[:, source * capacity : (source + 1) * capacity] = jnp.where(
                    label < per_owner, label, -1
                )
    wide, deep = min(512, total), min(256, total)

    @pl.loop(0, total // wide)
    def _(block):
        columns = pl.ds(pl.multiple_of(block * wide, wide), wide)
        rows_i = mine_ref[columns, :]
        label_i = lab_lane[:, columns]

        def add(ref, offset):
            def step(j, acc):
                start = pl.multiple_of(j * deep, deep)
                scores = lax.dot_general(
                    ref[pl.ds(start, deep), :],
                    rows_i,
                    (((1,), (1,)), ((), ())),
                    preferred_element_type=jnp.float32,
                )
                place = pl.ds(pl.multiple_of(start + offset, deep), deep)
                label_j = lab_sub[place, :]
                bias_j = bias[place, :]
                repeat = wide // LANES
                label_j = jnp.concatenate([label_j] * repeat, axis=1)
                bias_j = jnp.concatenate([bias_j] * repeat, axis=1)
                shift = jnp.where(label_j == label_i, -SCALE, bias_j)
                terms = jnp.exp2(scores * SCALE + shift)
                return acc + jnp.sum(terms.reshape(deep // 8, 8, wide), axis=0)

            return step

        acc = jnp.zeros((8, wide), jnp.float32)
        acc = lax.fori_loop(0, total // deep, add(mine_ref, 0), acc, unroll=2)
        acc = lax.fori_loop(0, total // deep, add(other_ref, total), acc, unroll=2)
        totals = jnp.sum(acc, axis=0, keepdims=True)
        out_ref[:, columns] = jnp.log(jnp.where(label_i >= 0, totals, 1.0))


def log_counts(counts, mine, other, n_owner, capacity):
    total = mine.shape[0]
    vmem = pl.BlockSpec(memory_space=pltpu.VMEM)
    return pl.pallas_call(
        functools.partial(counts_kernel, n_owner, capacity),
        out_shape=jax.ShapeDtypeStruct((1, total), jnp.float32),
        in_specs=[pl.BlockSpec(memory_space=pltpu.SMEM), vmem, vmem],
        out_specs=vmem,
        scratch_shapes=[
            pltpu.VMEM((1, total), jnp.int32),
            pltpu.VMEM((2 * total, LANES), jnp.int32),
            pltpu.VMEM((2 * total, LANES), jnp.float32),
        ],
        compiler_params=pltpu.CompilerParams(vmem_limit_bytes=VMEM_LIMIT),
    )(counts, mine, other)


def unpack_kernel(values_ref, pos_ref, out_ref):
    pos = pos_ref[...]
    lane = lax.rem(pos, LANES)
    line = lax.div(pos, LANES)
    out = jnp.zeros(pos.shape, jnp.float32)
    for r in range(values_ref.shape[0]):
        table = jnp.broadcast_to(values_ref[r : r + 1, :], pos.shape)
        found = jnp.take_along_axis(table, lane, axis=1)
        out = jnp.where(line == r, found, out)
    out_ref[...] = out


def unpack(values, pos):
    vmem = pl.BlockSpec(memory_space=pltpu.VMEM)
    return pl.pallas_call(
        unpack_kernel,
        out_shape=jax.ShapeDtypeStruct(pos.shape, jnp.float32),
        in_specs=[vmem, vmem],
        out_specs=vmem,
    )(values.reshape(-1, LANES), pos)


def swapped(x, first, second):
    return jnp.where(x == first, second, jnp.where(x == second, first, x))


def place_kernel(lay, x_hbm, lab_hbm, map_hbm, *refs):
    main_hbm, hot_ref, tail_ref, pos_ref, x_ref, lab_ref, map_ref, unit, main_ref, sems = refs
    n_owner, capacity, main, home = lay.n_owner, lay.capacity, lay.main, lay.home
    copies = [
        pltpu.make_async_copy(src, dst, sems.at[i])
        for i, (src, dst) in enumerate(((x_hbm, x_ref), (lab_hbm, lab_ref), (map_hbm, map_ref)))
    ]
    for copy in copies:
        copy.start()
    rows, width = x_ref.shape
    n_fine = map_ref.shape[1]
    per_owner = n_fine // n_owner
    copies[1].wait()
    copies[2].wait()
    owner_row = map_ref[...].astype(jnp.float32)
    fine_row = lax.broadcasted_iota(jnp.int32, (1, n_fine), 1).astype(jnp.float32)
    key_row = owner_row * n_fine + fine_row
    key_col = column_of(key_row)
    sorted_col = jnp.sum(jnp.where(key_row < key_col, 1.0, 0.0), axis=1, keepdims=True)
    lab = lab_ref[...].astype(jnp.float32)
    lab_row = jnp.concatenate([lab[b : b + 1, :] for b in range(lab.shape[0])], axis=1)
    fine_col = lax.broadcasted_iota(jnp.int32, (n_fine, rows), 0).astype(jnp.float32)
    fine_id = jnp.sum(jnp.where(fine_col == lab_row, sorted_col, 0.0), axis=0, keepdims=True)
    counts_col = jnp.sum(jnp.where(fine_col == fine_id, 1.0, 0.0), axis=1, keepdims=True)
    coarse = jnp.floor((fine_id + 0.5) * (1.0 / per_owner))
    first = coarse * per_owner
    before = jnp.sum(jnp.where(fine_col < first, counts_col, 0.0), axis=0, keepdims=True)
    upto = jnp.sum(jnp.where(fine_col < first + per_owner, counts_col, 0.0), axis=0, keepdims=True)
    full = jnp.min(
        jnp.where(upto - before == capacity, coarse, float(n_owner)), axis=1, keepdims=True
    )
    line = lax.broadcasted_iota(jnp.int32, (n_fine, LANES), 0)
    lane = lax.broadcasted_iota(jnp.int32, (n_fine, LANES), 1)
    inside = (line <= lane) & (lax.div(line, per_owner) == lax.div(lane, per_owner))
    running = jnp.sum(jnp.where(inside, counts_col, 0.0), axis=0, keepdims=True)
    info = jnp.where(lane[:1] < n_fine, running, full)
    index = lax.broadcasted_iota(jnp.int32, (1, rows), 1).astype(jnp.float32)
    row_key = fine_id * rows + index
    rank = jnp.zeros((1, rows), jnp.float32)
    for start in range(0, rows, LANES):
        other = column_of(row_key[:, start : start + LANES])
        rank = rank + jnp.sum(jnp.where(other < row_key, 1.0, 0.0), axis=0, keepdims=True)
    rank = (rank - before).astype(jnp.int32)
    place = swapped(coarse.astype(jnp.int32), full.astype(jnp.int32), home)
    table = place * capacity + rank
    pos_ref[...] = jnp.concatenate(
        [table[:, start : start + LANES] for start in range(0, rows, LANES)], axis=0
    )
    fits = rank < jnp.where(place == home, lay.head, main - 1)
    slot = jnp.where(fits, place * main + rank, -1)
    hot_slot = jnp.where(place == home, rank, -1)
    copies[0].wait()
    x = x_ref[...].astype(jnp.float32)
    squares = jnp.sum(x * x, axis=1, keepdims=True)
    unit[...] = (x * lax.rsqrt(squares + epsilon)).astype(jnp.bfloat16)

    def chosen_rows(slot, start, count):
        here = lax.broadcasted_iota(jnp.int32, (count, rows), 0) + start
        chosen = jnp.where(here == slot, 1.0, 0.0).astype(jnp.bfloat16)
        return jnp.dot(chosen, unit[...], preferred_element_type=jnp.float32)

    count = 2 * main
    down = lax.broadcasted_iota(jnp.int32, (count, LANES), 0)
    is_info = lax.rem(down, main) == main - 1
    writes = []
    for i, start in enumerate(range(0, lay.n_main, count)):
        packed = chosen_rows(slot, start, count)
        place = slice(start, start + count)
        main_ref[place, LANES:] = packed[:, LANES:].astype(jnp.bfloat16)
        main_ref[place, :LANES] = jnp.where(is_info, info, packed[:, :LANES]).astype(jnp.bfloat16)
        writes.append(
            pltpu.make_async_copy(
                main_ref.at[pl.ds(start, count)], main_hbm.at[pl.ds(start, count)], sems.at[3 + i]
            )
        )
        writes[-1].start()
    hot = chosen_rows(hot_slot, 0, capacity).astype(jnp.bfloat16)
    hot_ref[:capacity, :] = hot
    hot_ref[capacity:, :] = jnp.zeros((INFO, width), jnp.bfloat16)
    hot_ref[capacity:, :LANES] = jnp.broadcast_to(info, (INFO, LANES)).astype(jnp.bfloat16)
    tail_ref[...] = hot[lay.head :, :]
    for write in writes:
        write.wait()


def vmem_specs(count):
    return (pl.BlockSpec(memory_space=pltpu.VMEM),) * count


def place_rows(embeddings, labels, owner_map, lay):
    rows, width = embeddings.shape
    n_fine = owner_map.shape[0]
    lab_shape = (rows // LANES, LANES)
    anywhere = pl.BlockSpec(memory_space=pl.ANY)
    return pl.pallas_call(
        functools.partial(place_kernel, lay),
        out_shape=(
            jax.ShapeDtypeStruct((lay.n_main, width), jnp.bfloat16),
            jax.ShapeDtypeStruct((lay.capacity + INFO, width), jnp.bfloat16),
            jax.ShapeDtypeStruct((lay.rest, width), jnp.bfloat16),
            jax.ShapeDtypeStruct(lab_shape, jnp.int32),
        ),
        in_specs=[anywhere] * 3,
        out_specs=(anywhere,) + vmem_specs(3),
        scratch_shapes=[
            pltpu.VMEM((rows, width), jnp.bfloat16),
            pltpu.VMEM(lab_shape, jnp.int32),
            pltpu.VMEM((1, n_fine), jnp.int32),
            pltpu.VMEM((rows, width), jnp.bfloat16),
            pltpu.VMEM((lay.n_main, width), jnp.bfloat16),
            pltpu.SemaphoreType.DMA((3 + lay.n_owner // 2,)),
        ],
        compiler_params=pltpu.CompilerParams(vmem_limit_bytes=FAST_LIMIT),
    )(embeddings, labels.reshape(lab_shape), owner_map.reshape(1, n_fine))


def gate_kernel(*refs):
    pass


def after(rows, *there):
    return pl.pallas_call(
        gate_kernel,
        out_shape=jax.ShapeDtypeStruct(rows.shape, rows.dtype),
        in_specs=list(vmem_specs(1 + len(there))),
        out_specs=vmem_specs(1)[0],
        input_output_aliases={0: 0},
        compiler_params=pltpu.CompilerParams(vmem_limit_bytes=FAST_LIMIT),
    )(rows, *there)


def lay_early_kernel(lay, *refs):
    chunks, out = refs[:-1], refs[-1]

    @pl.when(lax.axis_index("cl") == lay.home)
    def _():
        for i, chunk in enumerate(chunks):
            out[i * lay.capacity : (i + 1) * lay.capacity, :] = chunk[: lay.capacity, :]
            start = lay.n_early + i * INFO
            out[start : start + INFO, :] = chunk[lay.capacity :, :]


def lay_early(chunks, lay):
    rows, width = sum(x.shape[0] for x in chunks), chunks[0].shape[1]
    return pl.pallas_call(
        functools.partial(lay_early_kernel, lay),
        out_shape=jax.ShapeDtypeStruct((rows, width), jnp.bfloat16),
        in_specs=list(vmem_specs(len(chunks))),
        out_specs=vmem_specs(1)[0],
        compiler_params=pltpu.CompilerParams(vmem_limit_bytes=FAST_LIMIT),
    )(*chunks)


def lay_out_kernel(n_arrays, home, *refs):
    chunks, out = refs[:n_arrays], refs[-1]

    def copy():
        start = 0
        for chunk in chunks:
            out[start : start + chunk.shape[0], :] = chunk[...]
            start += chunk.shape[0]

    if home is None:
        copy()
    else:
        pl.when(lax.axis_index("cl") == home)(copy)


def lay_out(chunks, home=None, waits=()):
    rows, width = sum(x.shape[0] for x in chunks), chunks[0].shape[1]
    return pl.pallas_call(
        functools.partial(lay_out_kernel, len(chunks), home),
        out_shape=jax.ShapeDtypeStruct((rows, width), jnp.bfloat16),
        in_specs=list(vmem_specs(len(chunks) + len(waits))),
        out_specs=vmem_specs(1)[0],
        compiler_params=pltpu.CompilerParams(vmem_limit_bytes=FAST_LIMIT),
    )(*chunks, *waits)


class Layout:
    early, heads, late = (0, 1, 2, 3), (4, 5, 6, 7), (4, 6, 5, 7)

    def __init__(self, n_owner, n_fine, capacity, main, home):
        self.n_owner, self.n_fine, self.capacity = n_owner, n_fine, capacity
        self.main, self.home = main, home
        self.head = main - INFO
        self.rest = capacity - self.head
        self.per_owner = n_fine // n_owner
        self.n_main = n_owner * main
        self.n_early = len(self.early) * capacity
        self.n_head = len(self.heads) * self.head
        self.n_late = len(self.late) * self.rest
        self.n_first = self.n_early + self.n_head
        self.n_all = self.n_first + self.n_late


def info_line(lay, main_ref, source):
    end = (source + 1) * lay.main
    return main_ref[end - INFO : end, :LANES].astype(jnp.float32)[INFO - 1 :]


def lines_of(lay, main_ref):
    return [info_line(lay, main_ref, source) for source in range(lay.n_owner)]


def hot_of(lay, info):
    lane = lax.broadcasted_iota(jnp.int32, (1, LANES), 1)
    hot = jnp.max(jnp.where(lane == lay.n_fine, info, 0.0), axis=1, keepdims=True)
    return hot.astype(jnp.int32)


def write_labels(lay, infos, sources, first, count, at, lab_sub, bias):
    cluster = swapped(lax.axis_index("cl"), hot_of(lay, infos[0]), lay.home)
    lane = lax.broadcasted_iota(jnp.int32, (1, LANES), 1)
    is_edge = lax.div(lane, lay.per_owner) == cluster
    for i, source in enumerate(sources):
        edges = jnp.where(is_edge, infos[source], 2.0 * lay.capacity)
        slot = lax.broadcasted_iota(jnp.int32, (count, LANES), 0) + first
        label = jnp.where(slot.astype(jnp.float32) >= edges, 1.0, 0.0)
        label = jnp.broadcast_to(jnp.sum(label, axis=1, keepdims=True), (count, LANES))
        start = at + i * count
        lab_sub[start : start + count, :] = label
        if bias is not None:
            bias[start : start + count, :] = jnp.where(
                label < lay.per_owner, NEIGHBOUR - SCALE, DEAD
            )


def early_lines(lay, early):
    starts = [lay.n_early + i * INFO for i in range(len(lay.early))]
    return {
        source: early[start : start + INFO, :LANES].astype(jnp.float32)[INFO - 1 :]
        for source, start in zip(lay.early, starts)
    }


def turn_labels(lay, lab_sub, count, lab_lane, at):
    for i in range(0, count, LANES):
        block = jnp.transpose(lab_sub[i : i + LANES, :])[:1]
        lab_lane[:, at + i : at + i + LANES] = jnp.where(block < lay.per_owner, block, -1.0)


def copy_head(lay, main_ref, rows):
    for i, source in enumerate(lay.heads):
        rows[i * lay.head : (i + 1) * lay.head, :] = main_ref[
            source * lay.main : source * lay.main + lay.head, :
        ]


def pieces(count, parts):
    return [(i * (count // parts), count // parts) for i in range(parts)]


def stream(lanes, tiles, lab_lane, buffers, put):
    rows_i, count, at = lanes
    step = 32
    tiles = [
        (ref, s, d, lab_sub, bias, line + s)
        for ref, n, lab_sub, bias, line, parts in tiles
        for s, d in pieces(n, parts)
    ]

    def scores_to(buffer, tile, rows):
        ref, start, deep = tile[:3]
        buffer[:deep, : rows.shape[0]] = lax.dot_general(
            ref[start : start + deep, :],
            rows,
            (((1,), (1,)), ((), ())),
            preferred_element_type=jnp.float32,
        )

    def run(start, blocks, wide):
        repeat = wide // LANES

        def rows_of(block):
            return rows_i[pl.ds(pl.multiple_of(start + block * wide, LANES), wide), :]

        scores_to(buffers[0], tiles[0], rows_of(0))

        def body(block, carry):
            here = rows_of(block)
            place = pl.ds(pl.multiple_of(at + start + block * wide, LANES), wide)
            label_i = lab_lane[:, place]
            acc = jnp.zeros((8, wide), jnp.float32)
            for i, (_, _, deep, lab_sub, bias, line) in enumerate(tiles):
                if i + 1 < len(tiles):
                    scores_to(buffers[(i + 1) % 2], tiles[i + 1], here)
                else:
                    scores_to(buffers[0], tiles[0], rows_of(jnp.minimum(block + 1, blocks - 1)))
                buffer = buffers[i % 2]
                for c in range(0, deep, step):
                    part = slice(line + c, line + c + step)
                    label_j = jnp.concatenate([lab_sub[part, :]] * repeat, axis=1)
                    if bias is None:
                        bias_j = NEIGHBOUR - SCALE
                    else:
                        bias_j = jnp.concatenate([bias[part, :]] * repeat, axis=1)
                    shift = jnp.where(label_j == label_i, -SCALE, bias_j)
                    terms = jnp.exp2(buffer[c : c + step, :wide] * SCALE + shift)
                    acc = acc + jnp.sum(terms.reshape(step // 8, 8, wide), axis=0)
            put(place, jnp.sum(acc, axis=0, keepdims=True))
            return carry

        lax.fori_loop(0, blocks, body, 0)

    if count >= WIDE:
        run(0, count // WIDE, WIDE)
    if count % WIDE:
        run(count - count % WIDE, 1, count % WIDE)


def setter(ref):
    def put(place, values):
        ref[:, place] = values

    return put


def adder(ref):
    def put(place, values):
        ref[:, place] += values

    return put


def inner_early_kernel(lay, early, sums, lab_lane, lab_sub, buf_a, buf_b):
    @pl.when(lax.axis_index("cl") == lay.home)
    def _():
        infos = early_lines(lay, early)
        write_labels(lay, infos, lay.early, 0, lay.capacity, 0, lab_sub, None)
        turn_labels(lay, lab_sub, lay.n_early, lab_lane, 0)
        tiles = [(early, lay.n_early, lab_sub, None, 0, 2)]
        stream((early, lay.n_early, 0), tiles, lab_lane, (buf_a, buf_b), setter(sums))


def cross_early_kernel(lay, early, early_j, sums, lab_lane, total, lab_sub, buf_a, buf_b):
    @pl.when(lax.axis_index("cl") == lay.home)
    def _():
        infos = early_lines(lay, early_j)
        write_labels(lay, infos, lay.early, 0, lay.capacity, 0, lab_sub, None)
        total[...] = sums[...]
        tiles = [(early_j, lay.n_early, lab_sub, None, 0, 2)]
        stream((early, lay.n_early, 0), tiles, lab_lane, (buf_a, buf_b), adder(total))


def grown_pairs(old_i, new_i, old_j, new_j, lab_lane, buffers, put):
    for lanes in old_i:
        stream(lanes, [new_j], lab_lane, buffers, put)
    stream(new_i, [new_j] + old_j, lab_lane, buffers, put)


def inner_kernel(lay, mine, early, early_sums, early_lane, early_sub, *refs):
    sums, lab_lane, lab_sub, rows, bias, buf_a, buf_b = refs
    is_home = lax.axis_index("cl") == lay.home
    infos = lines_of(lay, mine)
    buffers = (buf_a, buf_b)

    @pl.when(is_home)
    def _():
        copy_head(lay, mine, rows)
        write_labels(lay, infos, lay.heads, 0, lay.head, 0, lab_sub, None)
        lab_lane[:, : lay.n_early] = early_lane[...]
        turn_labels(lay, lab_sub, lay.n_head, lab_lane, lay.n_early)
        sums[:, : lay.n_early] = early_sums[...]
        sums[:, lay.n_early :] = jnp.zeros((1, lay.n_head), jnp.float32)
        grown_pairs(
            [(early, lay.n_early, 0)],
            (rows, lay.n_head, lay.n_early),
            [(early, lay.n_early, early_sub, None, 0, 2)],
            (rows, lay.n_head, lab_sub, None, 0, 2),
            lab_lane,
            buffers,
            adder(sums),
        )

    @pl.when(jnp.logical_not(is_home))
    def _():
        write_labels(lay, infos, range(lay.n_owner), 0, lay.main, 0, lab_sub, bias)
        turn_labels(lay, lab_sub, lay.n_main, lab_lane, 0)
        tiles = [(mine, lay.n_main, lab_sub, bias, 0, 2)]
        stream((mine, lay.n_main, 0), tiles, lab_lane, buffers, setter(sums))


def cross_kernel(lay, mine, other, early, early_j, early_sub_j, rows, sums, lab_lane, *refs):
    total, unfit_ref, lab_sub, rows_j, bias, buf_a, buf_b = refs
    is_home = lax.axis_index("cl") == lay.home
    infos = lines_of(lay, other)
    own = lines_of(lay, mine)
    hot = hot_of(lay, own[0])
    lane = lax.broadcasted_iota(jnp.int32, (1, LANES), 1)
    last = (lane < lay.n_fine) & (lax.rem(lane, lay.per_owner) == lay.per_owner - 1)
    last = last & (lax.div(lane, lay.per_owner) != hot)
    unfit = jnp.zeros((1, LANES), jnp.float32)
    for info in infos + own:
        wrong = last & (info >= lay.main)
        differs = (info != hot.astype(jnp.float32)) | (info >= lay.n_owner)
        wrong = wrong | ((lane == lay.n_fine) & differs)
        unfit = unfit + jnp.where(wrong, 1.0, 0.0)
    unfit_ref[0, 0] = jnp.max(unfit).astype(jnp.int32)
    total[...] = sums[...]
    buffers = (buf_a, buf_b)

    @pl.when(is_home)
    def _():
        copy_head(lay, other, rows_j)
        write_labels(lay, infos, lay.heads, 0, lay.head, 0, lab_sub, None)
        grown_pairs(
            [(early, lay.n_early, 0)],
            (rows, lay.n_head, lay.n_early),
            [(early_j, lay.n_early, early_sub_j, None, 0, 2)],
            (rows_j, lay.n_head, lab_sub, None, 0, 2),
            lab_lane,
            buffers,
            adder(total),
        )

    @pl.when(jnp.logical_not(is_home))
    def _():
        write_labels(lay, infos, range(lay.n_owner), 0, lay.main, 0, lab_sub, bias)
        tiles = [(other, lay.n_main, lab_sub, bias, 0, 2)]
        stream((mine, lay.n_main, 0), tiles, lab_lane, buffers, adder(total))


def late_pairs(lay, i_refs, j_refs, subs, lab_lane, buffers, put):
    early, rows, late = i_refs
    early_j, rows_j, late_j = j_refs
    early_sub, lab_sub, late_sub = subs
    grown_pairs(
        [(early, lay.n_early, 0), (rows, lay.n_head, lay.n_early)],
        (late, lay.n_late, lay.n_first),
        [
            (early_j, lay.n_early, early_sub, None, 0, 2),
            (rows_j, lay.n_head, lab_sub, None, 0, 2),
        ],
        (late_j, lay.n_late, late_sub, None, 0, 2),
        lab_lane,
        buffers,
        put,
    )


def inner_late_kernel(lay, mine, early, late, rows, early_sub, lab_sub, first_lane, *refs):
    sums, lab_lane, late_sub, buf_a, buf_b = refs

    @pl.when(lax.axis_index("cl") == lay.home)
    def _():
        infos = lines_of(lay, mine)
        write_labels(lay, infos, lay.late, lay.head, lay.rest, 0, late_sub, None)
        lab_lane[:, : lay.n_first] = first_lane[...]
        turn_labels(lay, late_sub, lay.n_late, lab_lane, lay.n_first)
        refs, subs = (early, rows, late), (early_sub, lab_sub, late_sub)
        late_pairs(lay, refs, refs, subs, lab_lane, (buf_a, buf_b), setter(sums))


def cross_late_kernel(lay, other, early, late, early_j, late_j, rows, rows_j, *refs):
    early_sub, lab_sub, first_lane, first_sums, lab_lane, sums = refs[:6]
    out_ref, total, late_sub, buf_a, buf_b = refs[6:]
    is_home = lax.axis_index("cl") == lay.home

    @pl.when(is_home)
    def _():
        infos = lines_of(lay, other)
        write_labels(lay, infos, lay.late, lay.head, lay.rest, 0, late_sub, None)
        total[...] = sums[...]
        total[:, : lay.n_first] += first_sums[...]
        i_refs, j_refs = (early, rows, late), (early_j, rows_j, late_j)
        subs = (early_sub, lab_sub, late_sub)
        late_pairs(lay, i_refs, j_refs, subs, lab_lane, (buf_a, buf_b), adder(total))
        values = jnp.log(total[...])
        for i, source in enumerate(lay.early):
            start = i * lay.capacity
            out_ref[source, :, :] = values[:, start : start + lay.capacity]
        for i, source in enumerate(lay.heads):
            start = lay.n_early + i * lay.head
            out_ref[source, :, : lay.head] = values[:, start : start + lay.head]
        for i, source in enumerate(lay.late):
            start = lay.n_first + i * lay.rest
            out_ref[source, :, lay.head :] = values[:, start : start + lay.rest]

    @pl.when(jnp.logical_not(is_home))
    def _():
        values = jnp.log(jnp.where(first_lane[...] >= 0, first_sums[...], 1.0))
        for source in range(lay.n_owner):
            start = source * lay.main
            out_ref[source, :, : lay.main] = values[:, start : start + lay.main]


def pair_call(kernel, lay, arrays, out_shape, scratch, out_specs=None, pairs=0):
    width = arrays[0].shape[1]
    buffer = pltpu.VMEM((lay.n_main // 2, WIDE), jnp.float32)
    return pl.pallas_call(
        functools.partial(kernel, lay),
        out_shape=out_shape,
        in_specs=list(vmem_specs(len(arrays))),
        out_specs=out_specs or vmem_specs(len(out_shape)),
        scratch_shapes=list(scratch) + [buffer, buffer],
        compiler_params=pltpu.CompilerParams(vmem_limit_bytes=FAST_LIMIT),
        cost_estimate=pl.CostEstimate(
            flops=2 * pairs * width, bytes_accessed=1, transcendentals=pairs
        ),
    )(*arrays)


def fast_unpack_kernel(values_ref, pos_ref, out_ref):
    pos = pos_ref[...]
    lane = lax.rem(pos, LANES)
    line = lax.div(pos, LANES)
    out = jnp.zeros(pos.shape, jnp.float32)
    per = values_ref.shape[2] // LANES
    for r in range(values_ref.shape[0] * per):
        start = r % per * LANES
        table = jnp.broadcast_to(values_ref[r // per, :, start : start + LANES], pos.shape)
        found = jnp.take_along_axis(table, lane, axis=1)
        out = jnp.where(line == r, found, out)
    out_ref[...] = out


def fast_unpack(values, pos):
    vmem = pl.BlockSpec(memory_space=pltpu.VMEM)
    return pl.pallas_call(
        fast_unpack_kernel,
        out_shape=jax.ShapeDtypeStruct(pos.shape, jnp.float32),
        in_specs=[vmem, vmem],
        out_specs=vmem,
    )(values, pos)


def general(embeddings, labels, owner_map):
    n_owner = lax.axis_size("cl")
    capacity = SLOTS // n_owner
    rows, width = embeddings.shape
    packed, pos, counts = pack(embeddings, labels, owner_map, n_owner, capacity)
    counts = lax.all_gather(counts, ("cl", "grp"), tiled=True)
    mine = lax.all_to_all(
        packed.reshape(n_owner, capacity, width), "cl", split_axis=0, concat_axis=0, tiled=True
    ).reshape(SLOTS, width)
    other = lax.ppermute(mine, "grp", [(0, 1), (1, 0)])
    results = log_counts(counts, mine, other, n_owner, capacity)
    returned = lax.all_to_all(
        results.reshape(n_owner, capacity), "cl", split_axis=0, concat_axis=0, tiled=True
    )
    return unpack(returned.reshape(SLOTS), pos).reshape(rows)


def body(embeddings, labels, owner_map):
    n_owner = lax.axis_size("cl")
    capacity = SLOTS // n_owner
    rows, width = embeddings.shape
    n_fine = owner_map.shape[0]
    main = -(-(rows // n_owner * 9 // 8) // 16) * 16
    if n_owner != 8 or main >= capacity or n_fine >= LANES:
        return general(embeddings, labels, owner_map)
    home = 2
    lay = Layout(n_owner, n_fine, capacity, main, home)
    packed, hot, tail, pos = place_rows(embeddings, labels, owner_map, lay)

    def hop(x, pairs):
        return lax.ppermute(x, "cl", pairs)

    def swap(x):
        pairs = [(2 * home, 2 * home + 1), (2 * home + 1, 2 * home)]
        return lax.ppermute(x, ("cl", "grp"), pairs)

    def array(shape, dtype=jnp.float32):
        return jax.ShapeDtypeStruct(shape, dtype)

    def scratch(shape):
        return pltpu.VMEM(shape, jnp.float32)

    both = lay_out([tail, hop(tail, [(6, 4), (7, 5)])])
    early = [hot if s == home else hop(hot, [(s, home)]) for s in lay.early]
    early = lay_early(early, lay)
    early_j = swap(early)
    early_row, early_side = array((1, lay.n_early)), array((lay.n_early, LANES))
    pairs = lay.n_early * lay.n_early
    early_sums, early_lane, early_sub = pair_call(
        inner_early_kernel, lay, (early,), (early_row, early_row, early_side), (), pairs=pairs
    )
    early_sums, early_sub_j = pair_call(
        cross_early_kernel,
        lay,
        (early, early_j, early_sums, early_lane),
        (early_row, early_side),
        (),
        pairs=pairs,
    )
    mine = lax.all_to_all(
        packed.reshape(n_owner, main, width), "cl", split_axis=0, concat_axis=0, tiled=True
    ).reshape(n_owner * main, width)
    mine = after(mine, early_sums, both)
    other = lax.ppermute(mine, "grp", [(0, 1), (1, 0)])
    late = [hop(both, [(4, home)]), hop(both, [(5, home)])]
    row, long_row = array((1, lay.n_first)), array((1, lay.n_all))
    side, bias = array((lay.n_main, LANES)), scratch((lay.n_main, LANES))
    heads = array((lay.n_head, width), jnp.bfloat16)
    late_side = scratch((lay.n_late, LANES))
    sums, first_lane, lab_sub, heads_i = pair_call(
        inner_kernel,
        lay,
        (mine, early, early_sums, early_lane, early_sub),
        (row, row, side, heads),
        (bias,),
    )
    specs = vmem_specs(1) + (pl.BlockSpec(memory_space=pltpu.SMEM),) + vmem_specs(2)
    sums, unfit, lab_sub_j, heads_j = pair_call(
        cross_kernel,
        lay,
        (mine, other, early, early_j, early_sub_j, heads_i, sums, first_lane),
        (row, array((1, 1), jnp.int32), side, heads),
        (bias,),
        specs,
    )
    late = lay_out(late, home, (sums,))
    late_j = swap(late)
    late_sums, lane = pair_call(
        inner_late_kernel,
        lay,
        (mine, early, late, heads_i, early_sub, lab_sub, first_lane),
        (long_row, long_row),
        (late_side,),
        pairs=lay.n_late * (lay.n_all + lay.n_first),
    )
    (results,) = pair_call(
        cross_late_kernel,
        lay,
        (
            *(other, early, late, early_j, late_j, heads_i, heads_j),
            *(early_sub_j, lab_sub_j, first_lane, sums, lane, late_sums),
        ),
        (array((n_owner, 1, capacity)),),
        (scratch(long_row.shape), late_side),
    )
    returned = lax.all_to_all(results, "cl", split_axis=0, concat_axis=0, tiled=True)
    return lax.cond(
        unfit[0, 0] == 0,
        lambda: fast_unpack(returned, pos).reshape(rows),
        lambda: general(embeddings, labels, owner_map),
    )


def solution(mesh):
    return jax.shard_map(
        body,
        mesh=mesh,
        in_specs=(P(("parts", "cl", "grp"), None), P(("parts", "cl", "grp")), P("parts")),
        out_specs=P(("parts", "cl", "grp")),
        check_vma=False,
    )
```

```python
import functools
import math

import jax
import jax.numpy as jnp
from jax import lax
from jax.experimental import pallas as pl
from jax.experimental.pallas import tpu as pltpu
from jax.sharding import PartitionSpec as P

SLOTS = 2048

temper = 0.2
neighbour_factor = 0.5
epsilon = 1e-06

LANES = 128
SCALE = math.log2(math.e) / temper
NEIGHBOUR = math.log2(neighbour_factor)
DEAD = -1e30
VMEM_LIMIT = 48 * 1024 * 1024
FAST_LIMIT = 16 * 1024 * 1024
WIDE = 512
INFO = 16


def column_of(row):
    pieces = []
    for start in range(0, row.shape[1], LANES):
        width = min(LANES, row.shape[1] - start)
        shape = (width, width)
        diagonal = lax.broadcasted_iota(jnp.int32, shape, 0) == lax.broadcasted_iota(
            jnp.int32, shape, 1
        )
        piece = jnp.broadcast_to(row[:, start : start + width], shape)
        pieces.append(jnp.sum(jnp.where(diagonal, piece, 0.0), axis=1, keepdims=True))
    return jnp.concatenate(pieces, axis=0)


def row_of(column):
    n = column.shape[0]
    diagonal = lax.broadcasted_iota(jnp.int32, (n, n), 0) == lax.broadcasted_iota(
        jnp.int32, (n, n), 1
    )
    return jnp.sum(jnp.where(diagonal, column, 0.0), axis=0, keepdims=True)


def pack_kernel(n_owner, capacity, x_ref, lab_ref, map_ref, out_ref, pos_ref, cnt_ref, unit, pos_row):
    rows = x_ref.shape[0]
    n_fine = map_ref.shape[1]
    per_owner = n_fine // n_owner
    owner_row = map_ref[...].astype(jnp.float32)
    fine_row = lax.broadcasted_iota(jnp.int32, (1, n_fine), 1).astype(jnp.float32)
    key_row = owner_row * n_fine + fine_row
    key_col = column_of(key_row)
    sorted_col = jnp.sum(jnp.where(key_row < key_col, 1.0, 0.0), axis=1, keepdims=True)
    lab = lab_ref[...].astype(jnp.float32)
    lab_row = jnp.concatenate([lab[b : b + 1, :] for b in range(lab.shape[0])], axis=1)
    fine_col = lax.broadcasted_iota(jnp.int32, (n_fine, rows), 0).astype(jnp.float32)
    fine_id = jnp.sum(jnp.where(fine_col == lab_row, sorted_col, 0.0), axis=0, keepdims=True)
    counts_col = jnp.sum(jnp.where(fine_col == fine_id, 1.0, 0.0), axis=1, keepdims=True)
    cnt_ref[...] = row_of(counts_col).astype(jnp.int32)
    coarse = jnp.floor((fine_id + 0.5) * (1.0 / per_owner))
    before = jnp.sum(
        jnp.where(fine_col < coarse * per_owner, counts_col, 0.0), axis=0, keepdims=True
    )
    index = lax.broadcasted_iota(jnp.int32, (1, rows), 1).astype(jnp.float32)
    row_key = fine_id * rows + index
    rank = jnp.zeros((1, rows), jnp.float32)
    for start in range(0, rows, LANES):
        other = column_of(row_key[:, start : start + LANES])
        rank = rank + jnp.sum(jnp.where(other < row_key, 1.0, 0.0), axis=0, keepdims=True)
    pos = (coarse * capacity + rank - before).astype(jnp.int32)
    pos_row[...] = pos
    pos_ref[...] = jnp.concatenate(
        [pos[:, start : start + LANES] for start in range(0, rows, LANES)], axis=0
    )
    x = x_ref[...].astype(jnp.float32)
    squares = jnp.sum(x * x, axis=1, keepdims=True)
    unit[...] = (x * lax.rsqrt(squares + epsilon)).astype(jnp.bfloat16)

    step = 256

    @pl.loop(0, out_ref.shape[0] // step)
    def _(block):
        slot = lax.broadcasted_iota(jnp.int32, (step, rows), 0) + block * step
        chosen = jnp.where(slot == pos_row[...], 1.0, 0.0).astype(jnp.bfloat16)
        packed = jnp.dot(chosen, unit[...], preferred_element_type=jnp.float32)
        out_ref[pl.ds(pl.multiple_of(block * step, step), step), :] = packed.astype(jnp.bfloat16)


def pack(embeddings, labels, owner_map, n_owner, capacity):
    rows, width = embeddings.shape
    n_fine = owner_map.shape[0]
    total = n_owner * capacity
    vmem = pl.BlockSpec(memory_space=pltpu.VMEM)
    return pl.pallas_call(
        functools.partial(pack_kernel, n_owner, capacity),
        out_shape=(
            jax.ShapeDtypeStruct((total, width), jnp.bfloat16),
            jax.ShapeDtypeStruct((rows // LANES, LANES), jnp.int32),
            jax.ShapeDtypeStruct((1, n_fine), jnp.int32),
        ),
        in_specs=[vmem] * 3,
        out_specs=(vmem, vmem, vmem),
        scratch_shapes=[pltpu.VMEM((rows, width), jnp.bfloat16), pltpu.VMEM((1, rows), jnp.int32)],
        compiler_params=pltpu.CompilerParams(vmem_limit_bytes=VMEM_LIMIT),
    )(embeddings, labels.reshape(rows // LANES, LANES), owner_map.reshape(1, n_fine))


def counts_kernel(n_owner, capacity, cnt_ref, mine_ref, other_ref, out_ref, lab_lane, lab_sub, bias):
    total = mine_ref.shape[0]
    per_owner = cnt_ref.shape[1] // n_owner
    me = lax.axis_index("cl")
    grp = lax.axis_index("grp")
    n_grp = lax.axis_size("grp")
    for member in range(2):
        for source in range(n_owner):
            line = source * n_grp + lax.rem(grp + member, n_grp)
            edges = []
            edge = jnp.int32(0)
            for f in range(per_owner):
                edge = edge + cnt_ref[line, me * per_owner + f]
                edges.append(edge)
            down = lax.broadcasted_iota(jnp.int32, (capacity, LANES), 0)
            label = jnp.zeros((capacity, LANES), jnp.int32)
            for edge in edges:
                label = label + jnp.where(down >= edge, 1, 0)
            start = (member * n_owner + source) * capacity
            lab_sub[start : start + capacity, :] = label
            bias[start : start + capacity, :] = jnp.where(
                label < per_owner, NEIGHBOUR - SCALE, DEAD
            )
            if member == 0:
                across = lax.broadcasted_iota(jnp.int32, (1, capacity), 1)
                label = jnp.zeros((1, capacity), jnp.int32)
                for edge in edges:
                    label = label + jnp.where(across >= edge, 1, 0)
                lab_lane[:, source * capacity : (source + 1) * capacity] = jnp.where(
                    label < per_owner, label, -1
                )
    wide, deep = min(512, total), min(256, total)

    @pl.loop(0, total // wide)
    def _(block):
        columns = pl.ds(pl.multiple_of(block * wide, wide), wide)
        rows_i = mine_ref[columns, :]
        label_i = lab_lane[:, columns]

        def add(ref, offset):
            def step(j, acc):
                start = pl.multiple_of(j * deep, deep)
                scores = lax.dot_general(
                    ref[pl.ds(start, deep), :],
                    rows_i,
                    (((1,), (1,)), ((), ())),
                    preferred_element_type=jnp.float32,
                )
                place = pl.ds(pl.multiple_of(start + offset, deep), deep)
                label_j = lab_sub[place, :]
                bias_j = bias[place, :]
                repeat = wide // LANES
                label_j = jnp.concatenate([label_j] * repeat, axis=1)
                bias_j = jnp.concatenate([bias_j] * repeat, axis=1)
                shift = jnp.where(label_j == label_i, -SCALE, bias_j)
                terms = jnp.exp2(scores * SCALE + shift)
                return acc + jnp.sum(terms.reshape(deep // 8, 8, wide), axis=0)

            return step

        acc = jnp.zeros((8, wide), jnp.float32)
        acc = lax.fori_loop(0, total // deep, add(mine_ref, 0), acc, unroll=2)
        acc = lax.fori_loop(0, total // deep, add(other_ref, total), acc, unroll=2)
        totals = jnp.sum(acc, axis=0, keepdims=True)
        out_ref[:, columns] = jnp.log(jnp.where(label_i >= 0, totals, 1.0))


def log_counts(counts, mine, other, n_owner, capacity):
    total = mine.shape[0]
    vmem = pl.BlockSpec(memory_space=pltpu.VMEM)
    return pl.pallas_call(
        functools.partial(counts_kernel, n_owner, capacity),
        out_shape=jax.ShapeDtypeStruct((1, total), jnp.float32),
        in_specs=[pl.BlockSpec(memory_space=pltpu.SMEM), vmem, vmem],
        out_specs=vmem,
        scratch_shapes=[
            pltpu.VMEM((1, total), jnp.int32),
            pltpu.VMEM((2 * total, LANES), jnp.int32),
            pltpu.VMEM((2 * total, LANES), jnp.float32),
        ],
        compiler_params=pltpu.CompilerParams(vmem_limit_bytes=VMEM_LIMIT),
    )(counts, mine, other)


def unpack_kernel(values_ref, pos_ref, out_ref):
    pos = pos_ref[...]
    lane = lax.rem(pos, LANES)
    line = lax.div(pos, LANES)
    out = jnp.zeros(pos.shape, jnp.float32)
    for r in range(values_ref.shape[0]):
        table = jnp.broadcast_to(values_ref[r : r + 1, :], pos.shape)
        found = jnp.take_along_axis(table, lane, axis=1)
        out = jnp.where(line == r, found, out)
    out_ref[...] = out


def unpack(values, pos):
    vmem = pl.BlockSpec(memory_space=pltpu.VMEM)
    return pl.pallas_call(
        unpack_kernel,
        out_shape=jax.ShapeDtypeStruct(pos.shape, jnp.float32),
        in_specs=[vmem, vmem],
        out_specs=vmem,
    )(values.reshape(-1, LANES), pos)


def swapped(x, first, second):
    return jnp.where(x == first, second, jnp.where(x == second, first, x))


def place_kernel(lay, x_hbm, lab_hbm, map_hbm, *refs):
    main_hbm, tail_ref, pos_ref, x_ref, lab_ref, map_ref, unit, main_ref, sems = refs
    n_owner, capacity, main, home = lay.n_owner, lay.capacity, lay.main, lay.home
    copies = [
        pltpu.make_async_copy(src, dst, sems.at[i])
        for i, (src, dst) in enumerate(((x_hbm, x_ref), (lab_hbm, lab_ref), (map_hbm, map_ref)))
    ]
    for copy in copies:
        copy.start()
    rows, width = x_ref.shape
    n_fine = map_ref.shape[1]
    per_owner = n_fine // n_owner
    copies[1].wait()
    copies[2].wait()
    owner_row = map_ref[...].astype(jnp.float32)
    fine_row = lax.broadcasted_iota(jnp.int32, (1, n_fine), 1).astype(jnp.float32)
    key_row = owner_row * n_fine + fine_row
    key_col = column_of(key_row)
    sorted_col = jnp.sum(jnp.where(key_row < key_col, 1.0, 0.0), axis=1, keepdims=True)
    lab = lab_ref[...].astype(jnp.float32)
    lab_row = jnp.concatenate([lab[b : b + 1, :] for b in range(lab.shape[0])], axis=1)
    fine_col = lax.broadcasted_iota(jnp.int32, (n_fine, rows), 0).astype(jnp.float32)
    fine_id = jnp.sum(jnp.where(fine_col == lab_row, sorted_col, 0.0), axis=0, keepdims=True)
    counts_col = jnp.sum(jnp.where(fine_col == fine_id, 1.0, 0.0), axis=1, keepdims=True)
    coarse = jnp.floor((fine_id + 0.5) * (1.0 / per_owner))
    first = coarse * per_owner
    before = jnp.sum(jnp.where(fine_col < first, counts_col, 0.0), axis=0, keepdims=True)
    upto = jnp.sum(jnp.where(fine_col < first + per_owner, counts_col, 0.0), axis=0, keepdims=True)
    full = jnp.min(
        jnp.where(upto - before == capacity, coarse, float(n_owner)), axis=1, keepdims=True
    )
    line = lax.broadcasted_iota(jnp.int32, (n_fine, LANES), 0)
    lane = lax.broadcasted_iota(jnp.int32, (n_fine, LANES), 1)
    inside = (line <= lane) & (lax.div(line, per_owner) == lax.div(lane, per_owner))
    running = jnp.sum(jnp.where(inside, counts_col, 0.0), axis=0, keepdims=True)
    info = jnp.where(lane[:1] < n_fine, running, full)
    index = lax.broadcasted_iota(jnp.int32, (1, rows), 1).astype(jnp.float32)
    row_key = fine_id * rows + index
    rank = jnp.zeros((1, rows), jnp.float32)
    for start in range(0, rows, LANES):
        other = column_of(row_key[:, start : start + LANES])
        rank = rank + jnp.sum(jnp.where(other < row_key, 1.0, 0.0), axis=0, keepdims=True)
    rank = (rank - before).astype(jnp.int32)
    place = swapped(coarse.astype(jnp.int32), full.astype(jnp.int32), home)
    table = place * capacity + rank
    pos_ref[...] = jnp.concatenate(
        [table[:, start : start + LANES] for start in range(0, rows, LANES)], axis=0
    )
    fits = rank < jnp.where(place == home, lay.head, main - 1)
    slot = jnp.where(fits, place * main + rank, -1)
    tail_slot = jnp.where(place == home, rank - lay.head, -1)
    copies[0].wait()
    x = x_ref[...].astype(jnp.float32)
    squares = jnp.sum(x * x, axis=1, keepdims=True)
    unit[...] = (x * lax.rsqrt(squares + epsilon)).astype(jnp.bfloat16)

    def chosen_rows(slot, start, count):
        here = lax.broadcasted_iota(jnp.int32, (count, rows), 0) + start
        chosen = jnp.where(here == slot, 1.0, 0.0).astype(jnp.bfloat16)
        return jnp.dot(chosen, unit[...], preferred_element_type=jnp.float32)

    count = 2 * main
    down = lax.broadcasted_iota(jnp.int32, (count, LANES), 0)
    is_info = lax.rem(down, main) == main - 1
    writes = []
    for i, start in enumerate(range(0, lay.n_main, count)):
        packed = chosen_rows(slot, start, count)
        place = slice(start, start + count)
        main_ref[place, LANES:] = packed[:, LANES:].astype(jnp.bfloat16)
        main_ref[place, :LANES] = jnp.where(is_info, info, packed[:, :LANES]).astype(jnp.bfloat16)
        writes.append(
            pltpu.make_async_copy(
                main_ref.at[pl.ds(start, count)], main_hbm.at[pl.ds(start, count)], sems.at[3 + i]
            )
        )
        writes[-1].start()
    tail_ref[...] = chosen_rows(tail_slot, 0, lay.rest).astype(jnp.bfloat16)
    for write in writes:
        write.wait()


def vmem_specs(count):
    return (pl.BlockSpec(memory_space=pltpu.VMEM),) * count


def place_rows(embeddings, labels, owner_map, lay):
    rows, width = embeddings.shape
    n_fine = owner_map.shape[0]
    lab_shape = (rows // LANES, LANES)
    anywhere = pl.BlockSpec(memory_space=pl.ANY)
    return pl.pallas_call(
        functools.partial(place_kernel, lay),
        out_shape=(
            jax.ShapeDtypeStruct((lay.n_main, width), jnp.bfloat16),
            jax.ShapeDtypeStruct((lay.rest, width), jnp.bfloat16),
            jax.ShapeDtypeStruct(lab_shape, jnp.int32),
        ),
        in_specs=[anywhere] * 3,
        out_specs=(anywhere,) + vmem_specs(2),
        scratch_shapes=[
            pltpu.VMEM((rows, width), jnp.bfloat16),
            pltpu.VMEM(lab_shape, jnp.int32),
            pltpu.VMEM((1, n_fine), jnp.int32),
            pltpu.VMEM((rows, width), jnp.bfloat16),
            pltpu.VMEM((lay.n_main, width), jnp.bfloat16),
            pltpu.SemaphoreType.DMA((3 + lay.n_owner // 2,)),
        ],
        compiler_params=pltpu.CompilerParams(vmem_limit_bytes=FAST_LIMIT),
    )(embeddings, labels.reshape(lab_shape), owner_map.reshape(1, n_fine))


def gate_kernel(*refs):
    pass


def after(rows, *there):
    return pl.pallas_call(
        gate_kernel,
        out_shape=jax.ShapeDtypeStruct(rows.shape, rows.dtype),
        in_specs=list(vmem_specs(1 + len(there))),
        out_specs=vmem_specs(1)[0],
        input_output_aliases={0: 0},
        compiler_params=pltpu.CompilerParams(vmem_limit_bytes=FAST_LIMIT),
    )(rows, *there)


def lay_out_kernel(n_arrays, home, *refs):
    chunks, out = refs[:n_arrays], refs[-1]

    def copy():
        start = 0
        for chunk in chunks:
            out[start : start + chunk.shape[0], :] = chunk[...]
            start += chunk.shape[0]

    if home is None:
        copy()
    else:
        pl.when(lax.axis_index("cl") == home)(copy)


def lay_out(chunks, home=None, waits=()):
    rows, width = sum(x.shape[0] for x in chunks), chunks[0].shape[1]
    return pl.pallas_call(
        functools.partial(lay_out_kernel, len(chunks), home),
        out_shape=jax.ShapeDtypeStruct((rows, width), jnp.bfloat16),
        in_specs=list(vmem_specs(len(chunks) + len(waits))),
        out_specs=vmem_specs(1)[0],
        compiler_params=pltpu.CompilerParams(vmem_limit_bytes=FAST_LIMIT),
    )(*chunks, *waits)


class Layout:
    early, late = (0, 1, 2, 3), (4, 6, 5, 7)

    def __init__(self, n_owner, n_fine, capacity, main, home):
        self.n_owner, self.n_fine, self.capacity = n_owner, n_fine, capacity
        self.main, self.home = main, home
        self.head = main - INFO
        self.rest = capacity - self.head
        self.per_owner = n_fine // n_owner
        self.n_main = n_owner * main
        self.n_head = n_owner * self.head
        self.n_early = len(self.early) * self.rest
        self.n_late = len(self.late) * self.rest
        self.n_first = self.n_head + self.n_early
        self.n_all = self.n_first + self.n_late


def info_line(lay, main_ref, source):
    end = (source + 1) * lay.main
    return main_ref[end - INFO : end, :LANES].astype(jnp.float32)[INFO - 1 :]


def lines_of(lay, main_ref):
    return [info_line(lay, main_ref, source) for source in range(lay.n_owner)]


def hot_of(lay, info):
    lane = lax.broadcasted_iota(jnp.int32, (1, LANES), 1)
    hot = jnp.max(jnp.where(lane == lay.n_fine, info, 0.0), axis=1, keepdims=True)
    return hot.astype(jnp.int32)


def write_labels(lay, infos, sources, first, count, at, lab_sub, bias):
    cluster = swapped(lax.axis_index("cl"), hot_of(lay, infos[0]), lay.home)
    lane = lax.broadcasted_iota(jnp.int32, (1, LANES), 1)
    is_edge = lax.div(lane, lay.per_owner) == cluster
    for i, source in enumerate(sources):
        edges = jnp.where(is_edge, infos[source], 2.0 * lay.capacity)
        slot = lax.broadcasted_iota(jnp.int32, (count, LANES), 0) + first
        label = jnp.where(slot.astype(jnp.float32) >= edges, 1.0, 0.0)
        label = jnp.broadcast_to(jnp.sum(label, axis=1, keepdims=True), (count, LANES))
        start = at + i * count
        lab_sub[start : start + count, :] = label
        if bias is not None:
            bias[start : start + count, :] = jnp.where(
                label < lay.per_owner, NEIGHBOUR - SCALE, DEAD
            )


def first_labels(lay, infos, lab_sub):
    write_labels(lay, infos, range(lay.n_owner), 0, lay.head, 0, lab_sub, None)
    write_labels(lay, infos, lay.early, lay.head, lay.rest, lay.n_head, lab_sub, None)


def late_labels(lay, infos, lab_sub):
    write_labels(lay, infos, lay.late, lay.head, lay.rest, 0, lab_sub, None)


def turn_labels(lay, lab_sub, count, lab_lane, at):
    for i in range(0, count, LANES):
        block = jnp.transpose(lab_sub[i : i + LANES, :])[:1]
        lab_lane[:, at + i : at + i + LANES] = jnp.where(block < lay.per_owner, block, -1.0)


def copy_head(lay, main_ref, rows):
    for source in range(lay.n_owner):
        rows[source * lay.head : (source + 1) * lay.head, :] = main_ref[
            source * lay.main : source * lay.main + lay.head, :
        ]


def pieces(count, parts):
    return [(i * (count // parts), count // parts) for i in range(parts)]


def stream(lanes, tiles, lab_lane, buffers, put):
    rows_i, count, at = lanes
    step = 32
    tiles = [
        (ref, s, d, lab_sub, bias, line + s, back)
        for ref, n, lab_sub, bias, line, parts, back in tiles
        for s, d in pieces(n, parts)
    ]

    def scores_to(buffer, tile, rows):
        ref, start, deep = tile[:3]
        buffer[:deep, : rows.shape[0]] = lax.dot_general(
            ref[start : start + deep, :],
            rows,
            (((1,), (1,)), ((), ())),
            preferred_element_type=jnp.float32,
        )

    def run(start, blocks, wide):
        repeat = wide // LANES

        def rows_of(block):
            return rows_i[pl.ds(pl.multiple_of(start + block * wide, LANES), wide), :]

        scores_to(buffers[0], tiles[0], rows_of(0))

        def body(block, carry):
            here = rows_of(block)
            place = pl.ds(pl.multiple_of(at + start + block * wide, LANES), wide)
            label_i = lab_lane[:, place]
            acc = jnp.zeros((8, wide), jnp.float32)
            for i, (_, _, deep, lab_sub, bias, line, back) in enumerate(tiles):
                if i + 1 < len(tiles):
                    scores_to(buffers[(i + 1) % 2], tiles[i + 1], here)
                else:
                    scores_to(buffers[0], tiles[0], rows_of(jnp.minimum(block + 1, blocks - 1)))
                buffer = buffers[i % 2]
                for c in range(0, deep, step):
                    part = slice(line + c, line + c + step)
                    label_j = jnp.concatenate([lab_sub[part, :]] * repeat, axis=1)
                    if bias is None:
                        bias_j = NEIGHBOUR - SCALE
                    else:
                        bias_j = jnp.concatenate([bias[part, :]] * repeat, axis=1)
                    shift = jnp.where(label_j == label_i, -SCALE, bias_j)
                    terms = jnp.exp2(buffer[c : c + step, :wide] * SCALE + shift)
                    acc = acc + jnp.sum(terms.reshape(step // 8, 8, wide), axis=0)
                    if back is not None:
                        across = terms[:, :LANES]
                        for r in range(1, repeat):
                            across = across + terms[:, r * LANES : (r + 1) * LANES]
                        back[slice(line + c, line + c + step), :] += across
            put(place, jnp.sum(acc, axis=0, keepdims=True))
            return carry

        lax.fori_loop(0, blocks, body, 0)

    if count >= WIDE:
        run(0, count // WIDE, WIDE)
    if count % WIDE:
        run(count - count % WIDE, 1, count % WIDE)


def turn_sums(back, count, sums, at):
    for i in range(0, count, LANES):
        block = jnp.transpose(back[i : i + LANES, :])
        sums[:, at + i : at + i + LANES] += jnp.sum(block, axis=0, keepdims=True)


def setter(ref):
    def put(place, values):
        ref[:, place] = values

    return put


def adder(ref):
    def put(place, values):
        ref[:, place] += values

    return put


def inner_kernel(lay, mine, early, sums, lab_lane, lab_sub, rows, bias, back, buf_a, buf_b):
    is_home = lax.axis_index("cl") == lay.home
    infos = lines_of(lay, mine)
    buffers = (buf_a, buf_b)

    @pl.when(is_home)
    def _():
        copy_head(lay, mine, rows)
        first_labels(lay, infos, lab_sub)
        turn_labels(lay, lab_sub, lay.n_first, lab_lane, 0)
        early_sub = lab_sub.at[pl.ds(lay.n_head, lay.n_early)]
        back[...] = jnp.zeros(back.shape, jnp.float32)
        tiles = [(rows, lay.n_head, lab_sub, None, 0, 2, None)]
        tiles += [(early, lay.n_early, early_sub, None, 0, 2, back)]
        stream((rows, lay.n_head, 0), tiles, lab_lane, buffers, setter(sums))
        tiles = [(early, lay.n_early, early_sub, None, 0, 2, None)]
        stream((early, lay.n_early, lay.n_head), tiles, lab_lane, buffers, setter(sums))
        turn_sums(back, lay.n_early, sums, lay.n_head)

    @pl.when(jnp.logical_not(is_home))
    def _():
        write_labels(lay, infos, range(lay.n_owner), 0, lay.main, 0, lab_sub, bias)
        turn_labels(lay, lab_sub, lay.n_main, lab_lane, 0)
        tiles = [(mine, lay.n_main, lab_sub, bias, 0, 2, None)]
        stream((mine, lay.n_main, 0), tiles, lab_lane, buffers, setter(sums))


def cross_kernel(lay, mine, other, early, early_j, rows, sums, lab_lane, *refs):
    total, unfit_ref, lab_sub, rows_j, bias, buf_a, buf_b = refs
    is_home = lax.axis_index("cl") == lay.home
    infos = lines_of(lay, other)
    own = lines_of(lay, mine)
    hot = hot_of(lay, own[0])
    lane = lax.broadcasted_iota(jnp.int32, (1, LANES), 1)
    last = (lane < lay.n_fine) & (lax.rem(lane, lay.per_owner) == lay.per_owner - 1)
    last = last & (lax.div(lane, lay.per_owner) != hot)
    unfit = jnp.zeros((1, LANES), jnp.float32)
    for info in infos + own:
        wrong = last & (info >= lay.main)
        differs = (info != hot.astype(jnp.float32)) | (info >= lay.n_owner)
        wrong = wrong | ((lane == lay.n_fine) & differs)
        unfit = unfit + jnp.where(wrong, 1.0, 0.0)
    unfit_ref[0, 0] = jnp.max(unfit).astype(jnp.int32)
    total[...] = sums[...]
    buffers = (buf_a, buf_b)

    @pl.when(is_home)
    def _():
        copy_head(lay, other, rows_j)
        first_labels(lay, infos, lab_sub)
        tiles = [(rows_j, lay.n_head, lab_sub, None, 0, 2, None)]
        tiles += [(early_j, lay.n_early, lab_sub, None, lay.n_head, 2, None)]
        stream((rows, lay.n_head, 0), tiles, lab_lane, buffers, adder(total))
        stream((early, lay.n_early, lay.n_head), tiles, lab_lane, buffers, adder(total))

    @pl.when(jnp.logical_not(is_home))
    def _():
        write_labels(lay, infos, range(lay.n_owner), 0, lay.main, 0, lab_sub, bias)
        tiles = [(other, lay.n_main, lab_sub, bias, 0, 2, None)]
        stream((mine, lay.n_main, 0), tiles, lab_lane, buffers, adder(total))


def late_pairs(lay, i_refs, j_refs, lab_sub, late_sub, lab_lane, buffers, put, back=None):
    rows, early, late = i_refs
    rows_j, early_j, late_j = j_refs
    lates = [(late_j, lay.n_late, late_sub, None, 0, 2, back)]
    stream((rows, lay.n_head, 0), lates, lab_lane, buffers, put)
    stream((early, lay.n_early, lay.n_head), lates, lab_lane, buffers, put)
    every = [(late_j, lay.n_late, late_sub, None, 0, 2, None)]
    if back is None:
        every += [(rows_j, lay.n_head, lab_sub, None, 0, 2, None)]
        every += [(early_j, lay.n_early, lab_sub, None, lay.n_head, 2, None)]
    stream((late, lay.n_late, lay.n_first), every, lab_lane, buffers, put)


def inner_late_kernel(lay, mine, early, late, rows, lab_sub, first_lane, *refs):
    sums, lab_lane, late_sub, back, buf_a, buf_b = refs

    @pl.when(lax.axis_index("cl") == lay.home)
    def _():
        late_labels(lay, lines_of(lay, mine), late_sub)
        lab_lane[:, : lay.n_first] = first_lane[...]
        turn_labels(lay, late_sub, lay.n_late, lab_lane, lay.n_first)
        refs = (rows, early, late)
        buffers = (buf_a, buf_b)
        back[...] = jnp.zeros(back.shape, jnp.float32)
        put = setter(sums)
        late_pairs(lay, refs, refs, lab_sub, late_sub, lab_lane, buffers, put, back)
        turn_sums(back, lay.n_late, sums, lay.n_first)


def cross_late_kernel(lay, other, early, late, early_j, late_j, rows, rows_j, *refs):
    lab_sub, first_lane, first_sums, lab_lane, sums = refs[:5]
    out_ref, total, late_sub, buf_a, buf_b = refs[5:]
    is_home = lax.axis_index("cl") == lay.home

    @pl.when(is_home)
    def _():
        late_labels(lay, lines_of(lay, other), late_sub)
        total[...] = sums[...]
        total[:, : lay.n_first] += first_sums[...]
        i_refs, j_refs = (rows, early, late), (rows_j, early_j, late_j)
        buffers = (buf_a, buf_b)
        late_pairs(lay, i_refs, j_refs, lab_sub, late_sub, lab_lane, buffers, adder(total))
        values = jnp.log(total[...])
        for source in range(lay.n_owner):
            start = source * lay.head
            out_ref[source, :, : lay.head] = values[:, start : start + lay.head]
        for i, source in enumerate(lay.early + lay.late):
            start = lay.n_head + i * lay.rest
            out_ref[source, :, lay.head :] = values[:, start : start + lay.rest]

    @pl.when(jnp.logical_not(is_home))
    def _():
        values = jnp.log(jnp.where(first_lane[...] >= 0, first_sums[...], 1.0))
        for source in range(lay.n_owner):
            start = source * lay.main
            out_ref[source, :, : lay.main] = values[:, start : start + lay.main]


def pair_call(kernel, lay, arrays, out_shape, scratch, out_specs=None, pairs=0):
    width = arrays[0].shape[1]
    buffer = pltpu.VMEM((lay.n_main // 2, WIDE), jnp.float32)
    return pl.pallas_call(
        functools.partial(kernel, lay),
        out_shape=out_shape,
        in_specs=list(vmem_specs(len(arrays))),
        out_specs=out_specs or vmem_specs(len(out_shape)),
        scratch_shapes=list(scratch) + [buffer, buffer],
        compiler_params=pltpu.CompilerParams(vmem_limit_bytes=FAST_LIMIT),
        cost_estimate=pl.CostEstimate(
            flops=2 * pairs * width, bytes_accessed=1, transcendentals=pairs
        ),
    )(*arrays)


def fast_unpack_kernel(values_ref, pos_ref, out_ref):
    pos = pos_ref[...]
    lane = lax.rem(pos, LANES)
    line = lax.div(pos, LANES)
    out = jnp.zeros(pos.shape, jnp.float32)
    per = values_ref.shape[2] // LANES
    for r in range(values_ref.shape[0] * per):
        start = r % per * LANES
        table = jnp.broadcast_to(values_ref[r // per, :, start : start + LANES], pos.shape)
        found = jnp.take_along_axis(table, lane, axis=1)
        out = jnp.where(line == r, found, out)
    out_ref[...] = out


def fast_unpack(values, pos):
    vmem = pl.BlockSpec(memory_space=pltpu.VMEM)
    return pl.pallas_call(
        fast_unpack_kernel,
        out_shape=jax.ShapeDtypeStruct(pos.shape, jnp.float32),
        in_specs=[vmem, vmem],
        out_specs=vmem,
    )(values, pos)


def general(embeddings, labels, owner_map):
    n_owner = lax.axis_size("cl")
    capacity = SLOTS // n_owner
    rows, width = embeddings.shape
    packed, pos, counts = pack(embeddings, labels, owner_map, n_owner, capacity)
    counts = lax.all_gather(counts, ("cl", "grp"), tiled=True)
    mine = lax.all_to_all(
        packed.reshape(n_owner, capacity, width), "cl", split_axis=0, concat_axis=0, tiled=True
    ).reshape(SLOTS, width)
    other = lax.ppermute(mine, "grp", [(0, 1), (1, 0)])
    results = log_counts(counts, mine, other, n_owner, capacity)
    returned = lax.all_to_all(
        results.reshape(n_owner, capacity), "cl", split_axis=0, concat_axis=0, tiled=True
    )
    return unpack(returned.reshape(SLOTS), pos).reshape(rows)


def body(embeddings, labels, owner_map):
    n_owner = lax.axis_size("cl")
    capacity = SLOTS // n_owner
    rows, width = embeddings.shape
    n_fine = owner_map.shape[0]
    main = -(-(rows // n_owner * 9 // 8) // 16) * 16
    if n_owner != 8 or main >= capacity or n_fine >= LANES:
        return general(embeddings, labels, owner_map)
    home = 2
    lay = Layout(n_owner, n_fine, capacity, main, home)
    packed, extra, pos = place_rows(embeddings, labels, owner_map, lay)

    def hop(x, pairs):
        return lax.ppermute(x, "cl", pairs)

    def swap(x):
        pairs = [(2 * home, 2 * home + 1), (2 * home + 1, 2 * home)]
        return lax.ppermute(x, ("cl", "grp"), pairs)

    both = lay_out([extra, hop(extra, [(6, 4), (7, 5)])])
    early = [extra if s == home else hop(extra, [(s, home)]) for s in lay.early]
    early = lay_out(early, home)
    mine = lax.all_to_all(
        packed.reshape(n_owner, main, width), "cl", split_axis=0, concat_axis=0, tiled=True
    ).reshape(n_owner * main, width)
    mine = after(mine, early, both)
    other = lax.ppermute(mine, "grp", [(0, 1), (1, 0)])
    early_j = swap(early)
    late = [hop(both, [(4, home)]), hop(both, [(5, home)])]

    def array(shape, dtype=jnp.float32):
        return jax.ShapeDtypeStruct(shape, dtype)

    def scratch(shape):
        return pltpu.VMEM(shape, jnp.float32)

    row, long_row = array((1, lay.n_first)), array((1, lay.n_all))
    side, bias = array((lay.n_first, LANES)), scratch((lay.n_main, LANES))
    heads = array((lay.n_head, width), jnp.bfloat16)
    late_side, early_side = scratch((lay.n_late, LANES)), scratch((lay.n_early, LANES))
    sums, first_lane, lab_sub, heads_i = pair_call(
        inner_kernel, lay, (mine, early), (row, row, side, heads), (bias, early_side)
    )
    specs = vmem_specs(1) + (pl.BlockSpec(memory_space=pltpu.SMEM),) + vmem_specs(2)
    sums, unfit, lab_sub_j, heads_j = pair_call(
        cross_kernel,
        lay,
        (mine, other, early, early_j, heads_i, sums, first_lane),
        (row, array((1, 1), jnp.int32), side, heads),
        (bias,),
        specs,
    )
    late = lay_out(late, home, (sums,))
    late_j = swap(late)
    late_sums, lane = pair_call(
        inner_late_kernel,
        lay,
        (mine, early, late, heads_i, lab_sub, first_lane),
        (long_row, long_row),
        (late_side, late_side),
        pairs=lay.n_late * (lay.n_all + lay.n_first),
    )
    (results,) = pair_call(
        cross_late_kernel,
        lay,
        (
            *(other, early, late, early_j, late_j, heads_i, heads_j),
            *(lab_sub_j, first_lane, sums, lane, late_sums),
        ),
        (array((n_owner, 1, capacity)),),
        (scratch(long_row.shape), late_side),
    )
    returned = lax.all_to_all(results, "cl", split_axis=0, concat_axis=0, tiled=True)
    return lax.cond(
        unfit[0, 0] == 0,
        lambda: fast_unpack(returned, pos).reshape(rows),
        lambda: general(embeddings, labels, owner_map),
    )


def solution(mesh):
    return jax.shard_map(
        body,
        mesh=mesh,
        in_specs=(P(("parts", "cl", "grp"), None), P(("parts", "cl", "grp")), P("parts")),
        out_specs=P(("parts", "cl", "grp")),
        check_vma=False,
    )
```

```python
import functools
import math

import jax
import jax.numpy as jnp
from jax import lax
from jax.experimental import pallas as pl
from jax.experimental.pallas import tpu as pltpu
from jax.sharding import PartitionSpec as P

SLOTS = 2048

temper = 0.2
neighbour_factor = 0.5
epsilon = 1e-06

LANES = 128
SCALE = math.log2(math.e) / temper
NEIGHBOUR = math.log2(neighbour_factor)
DEAD = -1e30
VMEM_LIMIT = 48 * 1024 * 1024
FAST_LIMIT = 16 * 1024 * 1024
WIDE = 512
INFO = 16


def column_of(row):
    pieces = []
    for start in range(0, row.shape[1], LANES):
        width = min(LANES, row.shape[1] - start)
        shape = (width, width)
        diagonal = lax.broadcasted_iota(jnp.int32, shape, 0) == lax.broadcasted_iota(
            jnp.int32, shape, 1
        )
        piece = jnp.broadcast_to(row[:, start : start + width], shape)
        pieces.append(jnp.sum(jnp.where(diagonal, piece, 0.0), axis=1, keepdims=True))
    return jnp.concatenate(pieces, axis=0)


def row_of(column):
    n = column.shape[0]
    diagonal = lax.broadcasted_iota(jnp.int32, (n, n), 0) == lax.broadcasted_iota(
        jnp.int32, (n, n), 1
    )
    return jnp.sum(jnp.where(diagonal, column, 0.0), axis=0, keepdims=True)


def pack_kernel(n_owner, capacity, x_ref, lab_ref, map_ref, out_ref, pos_ref, cnt_ref, unit, pos_row):
    rows = x_ref.shape[0]
    n_fine = map_ref.shape[1]
    per_owner = n_fine // n_owner
    owner_row = map_ref[...].astype(jnp.float32)
    fine_row = lax.broadcasted_iota(jnp.int32, (1, n_fine), 1).astype(jnp.float32)
    key_row = owner_row * n_fine + fine_row
    key_col = column_of(key_row)
    sorted_col = jnp.sum(jnp.where(key_row < key_col, 1.0, 0.0), axis=1, keepdims=True)
    lab = lab_ref[...].astype(jnp.float32)
    lab_row = jnp.concatenate([lab[b : b + 1, :] for b in range(lab.shape[0])], axis=1)
    fine_col = lax.broadcasted_iota(jnp.int32, (n_fine, rows), 0).astype(jnp.float32)
    fine_id = jnp.sum(jnp.where(fine_col == lab_row, sorted_col, 0.0), axis=0, keepdims=True)
    counts_col = jnp.sum(jnp.where(fine_col == fine_id, 1.0, 0.0), axis=1, keepdims=True)
    cnt_ref[...] = row_of(counts_col).astype(jnp.int32)
    coarse = jnp.floor((fine_id + 0.5) * (1.0 / per_owner))
    before = jnp.sum(
        jnp.where(fine_col < coarse * per_owner, counts_col, 0.0), axis=0, keepdims=True
    )
    index = lax.broadcasted_iota(jnp.int32, (1, rows), 1).astype(jnp.float32)
    row_key = fine_id * rows + index
    rank = jnp.zeros((1, rows), jnp.float32)
    for start in range(0, rows, LANES):
        other = column_of(row_key[:, start : start + LANES])
        rank = rank + jnp.sum(jnp.where(other < row_key, 1.0, 0.0), axis=0, keepdims=True)
    pos = (coarse * capacity + rank - before).astype(jnp.int32)
    pos_row[...] = pos
    pos_ref[...] = jnp.concatenate(
        [pos[:, start : start + LANES] for start in range(0, rows, LANES)], axis=0
    )
    x = x_ref[...].astype(jnp.float32)
    squares = jnp.sum(x * x, axis=1, keepdims=True)
    unit[...] = (x * lax.rsqrt(squares + epsilon)).astype(jnp.bfloat16)

    step = 256

    @pl.loop(0, out_ref.shape[0] // step)
    def _(block):
        slot = lax.broadcasted_iota(jnp.int32, (step, rows), 0) + block * step
        chosen = jnp.where(slot == pos_row[...], 1.0, 0.0).astype(jnp.bfloat16)
        packed = jnp.dot(chosen, unit[...], preferred_element_type=jnp.float32)
        out_ref[pl.ds(pl.multiple_of(block * step, step), step), :] = packed.astype(jnp.bfloat16)


def pack(embeddings, labels, owner_map, n_owner, capacity):
    rows, width = embeddings.shape
    n_fine = owner_map.shape[0]
    total = n_owner * capacity
    vmem = pl.BlockSpec(memory_space=pltpu.VMEM)
    return pl.pallas_call(
        functools.partial(pack_kernel, n_owner, capacity),
        out_shape=(
            jax.ShapeDtypeStruct((total, width), jnp.bfloat16),
            jax.ShapeDtypeStruct((rows // LANES, LANES), jnp.int32),
            jax.ShapeDtypeStruct((1, n_fine), jnp.int32),
        ),
        in_specs=[vmem] * 3,
        out_specs=(vmem, vmem, vmem),
        scratch_shapes=[pltpu.VMEM((rows, width), jnp.bfloat16), pltpu.VMEM((1, rows), jnp.int32)],
        compiler_params=pltpu.CompilerParams(vmem_limit_bytes=VMEM_LIMIT),
    )(embeddings, labels.reshape(rows // LANES, LANES), owner_map.reshape(1, n_fine))


def counts_kernel(n_owner, capacity, cnt_ref, mine_ref, other_ref, out_ref, lab_lane, lab_sub, bias):
    total = mine_ref.shape[0]
    per_owner = cnt_ref.shape[1] // n_owner
    me = lax.axis_index("cl")
    grp = lax.axis_index("grp")
    n_grp = lax.axis_size("grp")
    for member in range(2):
        for source in range(n_owner):
            line = source * n_grp + lax.rem(grp + member, n_grp)
            edges = []
            edge = jnp.int32(0)
            for f in range(per_owner):
                edge = edge + cnt_ref[line, me * per_owner + f]
                edges.append(edge)
            down = lax.broadcasted_iota(jnp.int32, (capacity, LANES), 0)
            label = jnp.zeros((capacity, LANES), jnp.int32)
            for edge in edges:
                label = label + jnp.where(down >= edge, 1, 0)
            start = (member * n_owner + source) * capacity
            lab_sub[start : start + capacity, :] = label
            bias[start : start + capacity, :] = jnp.where(
                label < per_owner, NEIGHBOUR - SCALE, DEAD
            )
            if member == 0:
                across = lax.broadcasted_iota(jnp.int32, (1, capacity), 1)
                label = jnp.zeros((1, capacity), jnp.int32)
                for edge in edges:
                    label = label + jnp.where(across >= edge, 1, 0)
                lab_lane[:, source * capacity : (source + 1) * capacity] = jnp.where(
                    label < per_owner, label, -1
                )
    wide, deep = min(512, total), min(256, total)

    @pl.loop(0, total // wide)
    def _(block):
        columns = pl.ds(pl.multiple_of(block * wide, wide), wide)
        rows_i = mine_ref[columns, :]
        label_i = lab_lane[:, columns]

        def add(ref, offset):
            def step(j, acc):
                start = pl.multiple_of(j * deep, deep)
                scores = lax.dot_general(
                    ref[pl.ds(start, deep), :],
                    rows_i,
                    (((1,), (1,)), ((), ())),
                    preferred_element_type=jnp.float32,
                )
                place = pl.ds(pl.multiple_of(start + offset, deep), deep)
                label_j = lab_sub[place, :]
                bias_j = bias[place, :]
                repeat = wide // LANES
                label_j = jnp.concatenate([label_j] * repeat, axis=1)
                bias_j = jnp.concatenate([bias_j] * repeat, axis=1)
                shift = jnp.where(label_j == label_i, -SCALE, bias_j)
                terms = jnp.exp2(scores * SCALE + shift)
                return acc + jnp.sum(terms.reshape(deep // 8, 8, wide), axis=0)

            return step

        acc = jnp.zeros((8, wide), jnp.float32)
        acc = lax.fori_loop(0, total // deep, add(mine_ref, 0), acc, unroll=2)
        acc = lax.fori_loop(0, total // deep, add(other_ref, total), acc, unroll=2)
        totals = jnp.sum(acc, axis=0, keepdims=True)
        out_ref[:, columns] = jnp.log(jnp.where(label_i >= 0, totals, 1.0))


def log_counts(counts, mine, other, n_owner, capacity):
    total = mine.shape[0]
    vmem = pl.BlockSpec(memory_space=pltpu.VMEM)
    return pl.pallas_call(
        functools.partial(counts_kernel, n_owner, capacity),
        out_shape=jax.ShapeDtypeStruct((1, total), jnp.float32),
        in_specs=[pl.BlockSpec(memory_space=pltpu.SMEM), vmem, vmem],
        out_specs=vmem,
        scratch_shapes=[
            pltpu.VMEM((1, total), jnp.int32),
            pltpu.VMEM((2 * total, LANES), jnp.int32),
            pltpu.VMEM((2 * total, LANES), jnp.float32),
        ],
        compiler_params=pltpu.CompilerParams(vmem_limit_bytes=VMEM_LIMIT),
    )(counts, mine, other)


def unpack_kernel(values_ref, pos_ref, out_ref):
    pos = pos_ref[...]
    lane = lax.rem(pos, LANES)
    line = lax.div(pos, LANES)
    out = jnp.zeros(pos.shape, jnp.float32)
    for r in range(values_ref.shape[0]):
        table = jnp.broadcast_to(values_ref[r : r + 1, :], pos.shape)
        found = jnp.take_along_axis(table, lane, axis=1)
        out = jnp.where(line == r, found, out)
    out_ref[...] = out


def unpack(values, pos):
    vmem = pl.BlockSpec(memory_space=pltpu.VMEM)
    return pl.pallas_call(
        unpack_kernel,
        out_shape=jax.ShapeDtypeStruct(pos.shape, jnp.float32),
        in_specs=[vmem, vmem],
        out_specs=vmem,
    )(values.reshape(-1, LANES), pos)


def swapped(x, first, second):
    return jnp.where(x == first, second, jnp.where(x == second, first, x))


def place_kernel(lay, x_hbm, lab_hbm, map_hbm, *refs):
    main_hbm, tail_ref, pos_ref, x_ref, lab_ref, map_ref, unit, main_ref, sems = refs
    n_owner, capacity, main, home = lay.n_owner, lay.capacity, lay.main, lay.home
    copies = [
        pltpu.make_async_copy(src, dst, sems.at[i])
        for i, (src, dst) in enumerate(((x_hbm, x_ref), (lab_hbm, lab_ref), (map_hbm, map_ref)))
    ]
    for copy in copies:
        copy.start()
    rows, width = x_ref.shape
    n_fine = map_ref.shape[1]
    per_owner = n_fine // n_owner
    copies[1].wait()
    copies[2].wait()
    owner_row = map_ref[...].astype(jnp.float32)
    fine_row = lax.broadcasted_iota(jnp.int32, (1, n_fine), 1).astype(jnp.float32)
    key_row = owner_row * n_fine + fine_row
    key_col = column_of(key_row)
    sorted_col = jnp.sum(jnp.where(key_row < key_col, 1.0, 0.0), axis=1, keepdims=True)
    lab = lab_ref[...].astype(jnp.float32)
    lab_row = jnp.concatenate([lab[b : b + 1, :] for b in range(lab.shape[0])], axis=1)
    fine_col = lax.broadcasted_iota(jnp.int32, (n_fine, rows), 0).astype(jnp.float32)
    fine_id = jnp.sum(jnp.where(fine_col == lab_row, sorted_col, 0.0), axis=0, keepdims=True)
    counts_col = jnp.sum(jnp.where(fine_col == fine_id, 1.0, 0.0), axis=1, keepdims=True)
    coarse = jnp.floor((fine_id + 0.5) * (1.0 / per_owner))
    first = coarse * per_owner
    before = jnp.sum(jnp.where(fine_col < first, counts_col, 0.0), axis=0, keepdims=True)
    upto = jnp.sum(jnp.where(fine_col < first + per_owner, counts_col, 0.0), axis=0, keepdims=True)
    full = jnp.min(
        jnp.where(upto - before == capacity, coarse, float(n_owner)), axis=1, keepdims=True
    )
    line = lax.broadcasted_iota(jnp.int32, (n_fine, LANES), 0)
    lane = lax.broadcasted_iota(jnp.int32, (n_fine, LANES), 1)
    inside = (line <= lane) & (lax.div(line, per_owner) == lax.div(lane, per_owner))
    running = jnp.sum(jnp.where(inside, counts_col, 0.0), axis=0, keepdims=True)
    info = jnp.where(lane[:1] < n_fine, running, full)
    index = lax.broadcasted_iota(jnp.int32, (1, rows), 1).astype(jnp.float32)
    row_key = fine_id * rows + index
    rank = jnp.zeros((1, rows), jnp.float32)
    for start in range(0, rows, LANES):
        other = column_of(row_key[:, start : start + LANES])
        rank = rank + jnp.sum(jnp.where(other < row_key, 1.0, 0.0), axis=0, keepdims=True)
    rank = (rank - before).astype(jnp.int32)
    place = swapped(coarse.astype(jnp.int32), full.astype(jnp.int32), home)
    table = place * capacity + rank
    pos_ref[...] = jnp.concatenate(
        [table[:, start : start + LANES] for start in range(0, rows, LANES)], axis=0
    )
    fits = rank < jnp.where(place == home, lay.head, main - 1)
    slot = jnp.where(fits, place * main + rank, -1)
    tail_slot = jnp.where(place == home, rank - lay.head, -1)
    copies[0].wait()
    x = x_ref[...].astype(jnp.float32)
    squares = jnp.sum(x * x, axis=1, keepdims=True)
    unit[...] = (x * lax.rsqrt(squares + epsilon)).astype(jnp.bfloat16)

    def chosen_rows(slot, start, count):
        here = lax.broadcasted_iota(jnp.int32, (count, rows), 0) + start
        chosen = jnp.where(here == slot, 1.0, 0.0).astype(jnp.bfloat16)
        return jnp.dot(chosen, unit[...], preferred_element_type=jnp.float32)

    count = 2 * main
    down = lax.broadcasted_iota(jnp.int32, (count, LANES), 0)
    is_info = lax.rem(down, main) == main - 1
    writes = []
    for i, start in enumerate(range(0, lay.n_main, count)):
        packed = chosen_rows(slot, start, count)
        place = slice(start, start + count)
        main_ref[place, LANES:] = packed[:, LANES:].astype(jnp.bfloat16)
        main_ref[place, :LANES] = jnp.where(is_info, info, packed[:, :LANES]).astype(jnp.bfloat16)
        writes.append(
            pltpu.make_async_copy(
                main_ref.at[pl.ds(start, count)], main_hbm.at[pl.ds(start, count)], sems.at[3 + i]
            )
        )
        writes[-1].start()
    tail_ref[...] = chosen_rows(tail_slot, 0, lay.rest).astype(jnp.bfloat16)
    for write in writes:
        write.wait()


def vmem_specs(count):
    return (pl.BlockSpec(memory_space=pltpu.VMEM),) * count


def place_rows(embeddings, labels, owner_map, lay):
    rows, width = embeddings.shape
    n_fine = owner_map.shape[0]
    lab_shape = (rows // LANES, LANES)
    anywhere = pl.BlockSpec(memory_space=pl.ANY)
    return pl.pallas_call(
        functools.partial(place_kernel, lay),
        out_shape=(
            jax.ShapeDtypeStruct((lay.n_main, width), jnp.bfloat16),
            jax.ShapeDtypeStruct((lay.rest, width), jnp.bfloat16),
            jax.ShapeDtypeStruct(lab_shape, jnp.int32),
        ),
        in_specs=[anywhere] * 3,
        out_specs=(anywhere,) + vmem_specs(2),
        scratch_shapes=[
            pltpu.VMEM((rows, width), jnp.bfloat16),
            pltpu.VMEM(lab_shape, jnp.int32),
            pltpu.VMEM((1, n_fine), jnp.int32),
            pltpu.VMEM((rows, width), jnp.bfloat16),
            pltpu.VMEM((lay.n_main, width), jnp.bfloat16),
            pltpu.SemaphoreType.DMA((3 + lay.n_owner // 2,)),
        ],
        compiler_params=pltpu.CompilerParams(vmem_limit_bytes=FAST_LIMIT),
    )(embeddings, labels.reshape(lab_shape), owner_map.reshape(1, n_fine))


def gate_kernel(*refs):
    pass


def after(rows, *there):
    return pl.pallas_call(
        gate_kernel,
        out_shape=jax.ShapeDtypeStruct(rows.shape, rows.dtype),
        in_specs=list(vmem_specs(1 + len(there))),
        out_specs=vmem_specs(1)[0],
        input_output_aliases={0: 0},
        compiler_params=pltpu.CompilerParams(vmem_limit_bytes=FAST_LIMIT),
    )(rows, *there)


def lay_out_kernel(n_arrays, home, *refs):
    chunks, out = refs[:n_arrays], refs[-1]

    def copy():
        start = 0
        for chunk in chunks:
            out[start : start + chunk.shape[0], :] = chunk[...]
            start += chunk.shape[0]

    if home is None:
        copy()
    else:
        pl.when(lax.axis_index("cl") == home)(copy)


def lay_out(chunks, home=None, waits=()):
    rows, width = sum(x.shape[0] for x in chunks), chunks[0].shape[1]
    return pl.pallas_call(
        functools.partial(lay_out_kernel, len(chunks), home),
        out_shape=jax.ShapeDtypeStruct((rows, width), jnp.bfloat16),
        in_specs=list(vmem_specs(len(chunks) + len(waits))),
        out_specs=vmem_specs(1)[0],
        compiler_params=pltpu.CompilerParams(vmem_limit_bytes=FAST_LIMIT),
    )(*chunks, *waits)


class Layout:
    early, late = (0, 1, 2, 3), (4, 6, 5, 7)

    def __init__(self, n_owner, n_fine, capacity, main, home):
        self.n_owner, self.n_fine, self.capacity = n_owner, n_fine, capacity
        self.main, self.home = main, home
        self.head = main - INFO
        self.rest = capacity - self.head
        self.per_owner = n_fine // n_owner
        self.n_main = n_owner * main
        self.n_head = n_owner * self.head
        self.n_early = len(self.early) * self.rest
        self.n_late = len(self.late) * self.rest
        self.n_first = self.n_head + self.n_early
        self.n_all = self.n_first + self.n_late


def info_line(lay, main_ref, source):
    end = (source + 1) * lay.main
    return main_ref[end - INFO : end, :LANES].astype(jnp.float32)[INFO - 1 :]


def lines_of(lay, main_ref):
    return [info_line(lay, main_ref, source) for source in range(lay.n_owner)]


def hot_of(lay, info):
    lane = lax.broadcasted_iota(jnp.int32, (1, LANES), 1)
    hot = jnp.max(jnp.where(lane == lay.n_fine, info, 0.0), axis=1, keepdims=True)
    return hot.astype(jnp.int32)


def write_labels(lay, infos, sources, first, count, at, lab_sub, bias):
    cluster = swapped(lax.axis_index("cl"), hot_of(lay, infos[0]), lay.home)
    lane = lax.broadcasted_iota(jnp.int32, (1, LANES), 1)
    is_edge = lax.div(lane, lay.per_owner) == cluster
    for i, source in enumerate(sources):
        edges = jnp.where(is_edge, infos[source], 2.0 * lay.capacity)
        slot = lax.broadcasted_iota(jnp.int32, (count, LANES), 0) + first
        label = jnp.where(slot.astype(jnp.float32) >= edges, 1.0, 0.0)
        label = jnp.broadcast_to(jnp.sum(label, axis=1, keepdims=True), (count, LANES))
        start = at + i * count
        lab_sub[start : start + count, :] = label
        if bias is not None:
            bias[start : start + count, :] = jnp.where(
                label < lay.per_owner, NEIGHBOUR - SCALE, DEAD
            )


def first_labels(lay, infos, lab_sub):
    write_labels(lay, infos, range(lay.n_owner), 0, lay.head, 0, lab_sub, None)
    write_labels(lay, infos, lay.early, lay.head, lay.rest, lay.n_head, lab_sub, None)


def late_labels(lay, infos, lab_sub):
    write_labels(lay, infos, lay.late, lay.head, lay.rest, 0, lab_sub, None)


def turn_labels(lay, lab_sub, count, lab_lane, at):
    for i in range(0, count, LANES):
        block = jnp.transpose(lab_sub[i : i + LANES, :])[:1]
        lab_lane[:, at + i : at + i + LANES] = jnp.where(block < lay.per_owner, block, -1.0)


def copy_head(lay, main_ref, rows):
    for source in range(lay.n_owner):
        rows[source * lay.head : (source + 1) * lay.head, :] = main_ref[
            source * lay.main : source * lay.main + lay.head, :
        ]


def pieces(count, parts):
    return [(i * (count // parts), count // parts) for i in range(parts)]


def stream(lanes, tiles, lab_lane, buffers, put):
    rows_i, count, at = lanes
    step = 32
    tiles = [
        (ref, s, d, lab_sub, bias, line + s, back)
        for ref, n, lab_sub, bias, line, parts, back in tiles
        for s, d in pieces(n, parts)
    ]

    def scores_to(buffer, tile, rows):
        ref, start, deep = tile[:3]
        buffer[:deep, : rows.shape[0]] = lax.dot_general(
            ref[start : start + deep, :],
            rows,
            (((1,), (1,)), ((), ())),
            preferred_element_type=jnp.float32,
        )

    def run(start, blocks, wide):
        repeat = wide // LANES

        def rows_of(block):
            return rows_i[pl.ds(pl.multiple_of(start + block * wide, LANES), wide), :]

        scores_to(buffers[0], tiles[0], rows_of(0))

        def one_block(block):
            here = rows_of(block)
            place = pl.ds(pl.multiple_of(at + start + block * wide, LANES), wide)
            label_i = lab_lane[:, place]
            acc = jnp.zeros((8, wide), jnp.float32)
            for i, (_, _, deep, lab_sub, bias, line, back) in enumerate(tiles):
                if i + 1 < len(tiles):
                    scores_to(buffers[(i + 1) % 2], tiles[i + 1], here)
                elif blocks > 1:

                    @pl.when(block + 1 < blocks)
                    def _():
                        scores_to(buffers[0], tiles[0], rows_of(block + 1))

                buffer = buffers[i % 2]
                for c in range(0, deep, step):
                    part = slice(line + c, line + c + step)
                    label_j = jnp.concatenate([lab_sub[part, :]] * repeat, axis=1)
                    if bias is None:
                        bias_j = NEIGHBOUR - SCALE
                    else:
                        bias_j = jnp.concatenate([bias[part, :]] * repeat, axis=1)
                    shift = jnp.where(label_j == label_i, -SCALE, bias_j)
                    terms = jnp.exp2(buffer[c : c + step, :wide] * SCALE + shift)
                    acc = acc + jnp.sum(terms.reshape(step // 8, 8, wide), axis=0)
                    if back is not None:
                        across = terms[:, :LANES]
                        for r in range(1, repeat):
                            across = across + terms[:, r * LANES : (r + 1) * LANES]
                        back[part, :] += across
            put(place, jnp.sum(acc, axis=0, keepdims=True))

        if blocks == 1:
            one_block(0)
        else:
            pl.loop(0, blocks)(one_block)

    if count >= WIDE:
        run(0, count // WIDE, WIDE)
    if count % WIDE:
        run(count - count % WIDE, 1, count % WIDE)


def turn_sums(back, count, sums, at):
    for i in range(0, count, LANES):
        block = jnp.transpose(back[i : i + LANES, :])
        sums[:, at + i : at + i + LANES] += jnp.sum(block, axis=0, keepdims=True)


def setter(ref):
    def put(place, values):
        ref[:, place] = values

    return put


def adder(ref):
    def put(place, values):
        ref[:, place] += values

    return put


def inner_kernel(lay, mine, early, sums, lab_lane, lab_sub, rows, bias, back, buf_a, buf_b):
    is_home = lax.axis_index("cl") == lay.home
    infos = lines_of(lay, mine)
    buffers = (buf_a, buf_b)

    @pl.when(is_home)
    def _():
        copy_head(lay, mine, rows)
        first_labels(lay, infos, lab_sub)
        turn_labels(lay, lab_sub, lay.n_first, lab_lane, 0)
        back[...] = jnp.zeros(back.shape, jnp.float32)
        size = lay.n_early
        blocks = [(rows.at[pl.ds(start, size)], start) for start in range(0, lay.n_head, size)]
        blocks.append((early, lay.n_head))
        for i, (ref, at) in enumerate(blocks):
            tiles = [
                (ref_j, size, lab_sub, None, at_j, 2, None if at_j == at else back)
                for ref_j, at_j in blocks[i:]
            ]
            stream((ref, size, at), tiles, lab_lane, buffers, setter(sums))
        turn_sums(back, lay.n_first, sums, 0)

    @pl.when(jnp.logical_not(is_home))
    def _():
        write_labels(lay, infos, range(lay.n_owner), 0, lay.main, 0, lab_sub, bias)
        turn_labels(lay, lab_sub, lay.n_main, lab_lane, 0)
        tiles = [(mine, lay.n_main, lab_sub, bias, 0, 2, None)]
        stream((mine, lay.n_main, 0), tiles, lab_lane, buffers, setter(sums))


def cross_kernel(lay, mine, other, early, early_j, rows, sums, lab_lane, *refs):
    total, unfit_ref, lab_sub, rows_j, bias, buf_a, buf_b = refs
    is_home = lax.axis_index("cl") == lay.home
    infos = lines_of(lay, other)
    own = lines_of(lay, mine)
    hot = hot_of(lay, own[0])
    lane = lax.broadcasted_iota(jnp.int32, (1, LANES), 1)
    last = (lane < lay.n_fine) & (lax.rem(lane, lay.per_owner) == lay.per_owner - 1)
    last = last & (lax.div(lane, lay.per_owner) != hot)
    unfit = jnp.zeros((1, LANES), jnp.float32)
    for info in infos + own:
        wrong = last & (info >= lay.main)
        differs = (info != hot.astype(jnp.float32)) | (info >= lay.n_owner)
        wrong = wrong | ((lane == lay.n_fine) & differs)
        unfit = unfit + jnp.where(wrong, 1.0, 0.0)
    unfit_ref[0, 0] = jnp.max(unfit).astype(jnp.int32)
    total[...] = sums[...]
    buffers = (buf_a, buf_b)

    @pl.when(is_home)
    def _():
        copy_head(lay, other, rows_j)
        first_labels(lay, infos, lab_sub)
        tiles = [(rows_j, lay.n_head, lab_sub, None, 0, 2, None)]
        tiles += [(early_j, lay.n_early, lab_sub, None, lay.n_head, 2, None)]
        stream((rows, lay.n_head, 0), tiles, lab_lane, buffers, adder(total))
        stream((early, lay.n_early, lay.n_head), tiles, lab_lane, buffers, adder(total))

    @pl.when(jnp.logical_not(is_home))
    def _():
        write_labels(lay, infos, range(lay.n_owner), 0, lay.main, 0, lab_sub, bias)
        tiles = [(other, lay.n_main, lab_sub, bias, 0, 2, None)]
        stream((mine, lay.n_main, 0), tiles, lab_lane, buffers, adder(total))


def late_pairs(lay, i_refs, j_refs, lab_sub, late_sub, lab_lane, buffers, put, back=None):
    rows, early, late = i_refs
    rows_j, early_j, late_j = j_refs
    lates = [(late_j, lay.n_late, late_sub, None, 0, 2, back)]
    stream((rows, lay.n_head, 0), lates, lab_lane, buffers, put)
    stream((early, lay.n_early, lay.n_head), lates, lab_lane, buffers, put)
    every = [(late_j, lay.n_late, late_sub, None, 0, 2, None)]
    if back is None:
        every += [(rows_j, lay.n_head, lab_sub, None, 0, 2, None)]
        every += [(early_j, lay.n_early, lab_sub, None, lay.n_head, 2, None)]
    stream((late, lay.n_late, lay.n_first), every, lab_lane, buffers, put)


def inner_late_kernel(lay, mine, early, late, rows, lab_sub, first_lane, *refs):
    sums, lab_lane, late_sub, back, buf_a, buf_b = refs

    @pl.when(lax.axis_index("cl") == lay.home)
    def _():
        late_labels(lay, lines_of(lay, mine), late_sub)
        lab_lane[:, : lay.n_first] = first_lane[...]
        turn_labels(lay, late_sub, lay.n_late, lab_lane, lay.n_first)
        refs = (rows, early, late)
        buffers = (buf_a, buf_b)
        back[...] = jnp.zeros(back.shape, jnp.float32)
        put = setter(sums)
        late_pairs(lay, refs, refs, lab_sub, late_sub, lab_lane, buffers, put, back)
        turn_sums(back, lay.n_late, sums, lay.n_first)


def cross_late_kernel(lay, other, early, late, early_j, late_j, rows, rows_j, *refs):
    lab_sub, first_lane, first_sums, lab_lane, sums = refs[:5]
    out_ref, total, late_sub, buf_a, buf_b = refs[5:]
    is_home = lax.axis_index("cl") == lay.home

    @pl.when(is_home)
    def _():
        late_labels(lay, lines_of(lay, other), late_sub)
        total[...] = sums[...]
        total[:, : lay.n_first] += first_sums[...]
        i_refs, j_refs = (rows, early, late), (rows_j, early_j, late_j)
        buffers = (buf_a, buf_b)
        late_pairs(lay, i_refs, j_refs, lab_sub, late_sub, lab_lane, buffers, adder(total))
        values = jnp.log(total[...])
        for source in range(lay.n_owner):
            start = source * lay.head
            out_ref[source, :, : lay.head] = values[:, start : start + lay.head]
        for i, source in enumerate(lay.early + lay.late):
            start = lay.n_head + i * lay.rest
            out_ref[source, :, lay.head :] = values[:, start : start + lay.rest]

    @pl.when(jnp.logical_not(is_home))
    def _():
        values = jnp.log(jnp.where(first_lane[...] >= 0, first_sums[...], 1.0))
        for source in range(lay.n_owner):
            start = source * lay.main
            out_ref[source, :, : lay.main] = values[:, start : start + lay.main]


def pair_call(kernel, lay, arrays, out_shape, scratch, out_specs=None, pairs=0):
    width = arrays[0].shape[1]
    buffer = pltpu.VMEM((lay.n_main // 2, WIDE), jnp.float32)
    return pl.pallas_call(
        functools.partial(kernel, lay),
        out_shape=out_shape,
        in_specs=list(vmem_specs(len(arrays))),
        out_specs=out_specs or vmem_specs(len(out_shape)),
        scratch_shapes=list(scratch) + [buffer, buffer],
        compiler_params=pltpu.CompilerParams(vmem_limit_bytes=FAST_LIMIT),
        cost_estimate=pl.CostEstimate(
            flops=2 * pairs * width, bytes_accessed=1, transcendentals=pairs
        ),
    )(*arrays)


def fast_unpack_kernel(values_ref, pos_ref, out_ref):
    pos = pos_ref[...]
    lane = lax.rem(pos, LANES)
    line = lax.div(pos, LANES)
    out = jnp.zeros(pos.shape, jnp.float32)
    per = values_ref.shape[2] // LANES
    for r in range(values_ref.shape[0] * per):
        start = r % per * LANES
        table = jnp.broadcast_to(values_ref[r // per, :, start : start + LANES], pos.shape)
        found = jnp.take_along_axis(table, lane, axis=1)
        out = jnp.where(line == r, found, out)
    out_ref[...] = out


def fast_unpack(values, pos):
    vmem = pl.BlockSpec(memory_space=pltpu.VMEM)
    return pl.pallas_call(
        fast_unpack_kernel,
        out_shape=jax.ShapeDtypeStruct(pos.shape, jnp.float32),
        in_specs=[vmem, vmem],
        out_specs=vmem,
    )(values, pos)


def general(embeddings, labels, owner_map):
    n_owner = lax.axis_size("cl")
    capacity = SLOTS // n_owner
    rows, width = embeddings.shape
    packed, pos, counts = pack(embeddings, labels, owner_map, n_owner, capacity)
    counts = lax.all_gather(counts, ("cl", "grp"), tiled=True)
    mine = lax.all_to_all(
        packed.reshape(n_owner, capacity, width), "cl", split_axis=0, concat_axis=0, tiled=True
    ).reshape(SLOTS, width)
    other = lax.ppermute(mine, "grp", [(0, 1), (1, 0)])
    results = log_counts(counts, mine, other, n_owner, capacity)
    returned = lax.all_to_all(
        results.reshape(n_owner, capacity), "cl", split_axis=0, concat_axis=0, tiled=True
    )
    return unpack(returned.reshape(SLOTS), pos).reshape(rows)


def body(embeddings, labels, owner_map):
    n_owner = lax.axis_size("cl")
    capacity = SLOTS // n_owner
    rows, width = embeddings.shape
    n_fine = owner_map.shape[0]
    main = -(-(rows // n_owner * 9 // 8) // 16) * 16
    if n_owner != 8 or main >= capacity or n_fine >= LANES:
        return general(embeddings, labels, owner_map)
    home = 2
    lay = Layout(n_owner, n_fine, capacity, main, home)
    packed, extra, pos = place_rows(embeddings, labels, owner_map, lay)

    def hop(x, pairs):
        return lax.ppermute(x, "cl", pairs)

    def swap(x):
        pairs = [(2 * home, 2 * home + 1), (2 * home + 1, 2 * home)]
        return lax.ppermute(x, ("cl", "grp"), pairs)

    both = lay_out([extra, hop(extra, [(6, 4), (7, 5)])])
    early = [extra if s == home else hop(extra, [(s, home)]) for s in lay.early]
    early = lay_out(early, home)
    mine = lax.all_to_all(
        packed.reshape(n_owner, main, width), "cl", split_axis=0, concat_axis=0, tiled=True
    ).reshape(n_owner * main, width)
    mine = after(mine, early, both)
    other = lax.ppermute(mine, "grp", [(0, 1), (1, 0)])
    early_j = swap(early)
    late = [hop(both, [(4, home)]), hop(both, [(5, home)])]

    def array(shape, dtype=jnp.float32):
        return jax.ShapeDtypeStruct(shape, dtype)

    def scratch(shape):
        return pltpu.VMEM(shape, jnp.float32)

    row, long_row = array((1, lay.n_first)), array((1, lay.n_all))
    side, bias = array((lay.n_first, LANES)), scratch((lay.n_main, LANES))
    heads = array((lay.n_head, width), jnp.bfloat16)
    late_side, first_side = scratch((lay.n_late, LANES)), scratch((lay.n_first, LANES))
    sums, first_lane, lab_sub, heads_i = pair_call(
        inner_kernel, lay, (mine, early), (row, row, side, heads), (bias, first_side)
    )
    specs = vmem_specs(1) + (pl.BlockSpec(memory_space=pltpu.SMEM),) + vmem_specs(2)
    sums, unfit, lab_sub_j, heads_j = pair_call(
        cross_kernel,
        lay,
        (mine, other, early, early_j, heads_i, sums, first_lane),
        (row, array((1, 1), jnp.int32), side, heads),
        (bias,),
        specs,
    )
    late = lay_out(late, home, (sums,))
    late_j = swap(late)
    late_sums, lane = pair_call(
        inner_late_kernel,
        lay,
        (mine, early, late, heads_i, lab_sub, first_lane),
        (long_row, long_row),
        (late_side, late_side),
        pairs=lay.n_late * (lay.n_all + lay.n_first),
    )
    (results,) = pair_call(
        cross_late_kernel,
        lay,
        (
            *(other, early, late, early_j, late_j, heads_i, heads_j),
            *(lab_sub_j, first_lane, sums, lane, late_sums),
        ),
        (array((n_owner, 1, capacity)),),
        (scratch(long_row.shape), late_side),
    )
    returned = lax.all_to_all(results, "cl", split_axis=0, concat_axis=0, tiled=True)
    return lax.cond(
        unfit[0, 0] == 0,
        lambda: fast_unpack(returned, pos).reshape(rows),
        lambda: general(embeddings, labels, owner_map),
    )


def solution(mesh):
    return jax.shard_map(
        body,
        mesh=mesh,
        in_specs=(P(("parts", "cl", "grp"), None), P(("parts", "cl", "grp")), P("parts")),
        out_specs=P(("parts", "cl", "grp")),
        check_vma=False,
    )
```

```python
import functools
import math

import jax
import jax.numpy as jnp
from jax import lax
from jax.experimental import pallas as pl
from jax.experimental.pallas import tpu as pltpu
from jax.sharding import PartitionSpec as P

SLOTS = 2048

temper = 0.2
neighbour_factor = 0.5
epsilon = 1e-06

LANES = 128
SCALE = math.log2(math.e) / temper
NEIGHBOUR = math.log2(neighbour_factor)
DEAD = -1e30
VMEM_LIMIT = 48 * 1024 * 1024
FAST_LIMIT = 16 * 1024 * 1024
WIDE = 512
INFO = 16


def column_of(row):
    pieces = []
    for start in range(0, row.shape[1], LANES):
        width = min(LANES, row.shape[1] - start)
        shape = (width, width)
        diagonal = lax.broadcasted_iota(jnp.int32, shape, 0) == lax.broadcasted_iota(
            jnp.int32, shape, 1
        )
        piece = jnp.broadcast_to(row[:, start : start + width], shape)
        pieces.append(jnp.sum(jnp.where(diagonal, piece, 0.0), axis=1, keepdims=True))
    return jnp.concatenate(pieces, axis=0)


def row_of(column):
    n = column.shape[0]
    diagonal = lax.broadcasted_iota(jnp.int32, (n, n), 0) == lax.broadcasted_iota(
        jnp.int32, (n, n), 1
    )
    return jnp.sum(jnp.where(diagonal, column, 0.0), axis=0, keepdims=True)


def pack_kernel(n_owner, capacity, x_ref, lab_ref, map_ref, out_ref, pos_ref, cnt_ref, unit, pos_row):
    rows = x_ref.shape[0]
    n_fine = map_ref.shape[1]
    per_owner = n_fine // n_owner
    owner_row = map_ref[...].astype(jnp.float32)
    fine_row = lax.broadcasted_iota(jnp.int32, (1, n_fine), 1).astype(jnp.float32)
    key_row = owner_row * n_fine + fine_row
    key_col = column_of(key_row)
    sorted_col = jnp.sum(jnp.where(key_row < key_col, 1.0, 0.0), axis=1, keepdims=True)
    lab = lab_ref[...].astype(jnp.float32)
    lab_row = jnp.concatenate([lab[b : b + 1, :] for b in range(lab.shape[0])], axis=1)
    fine_col = lax.broadcasted_iota(jnp.int32, (n_fine, rows), 0).astype(jnp.float32)
    fine_id = jnp.sum(jnp.where(fine_col == lab_row, sorted_col, 0.0), axis=0, keepdims=True)
    counts_col = jnp.sum(jnp.where(fine_col == fine_id, 1.0, 0.0), axis=1, keepdims=True)
    cnt_ref[...] = row_of(counts_col).astype(jnp.int32)
    coarse = jnp.floor((fine_id + 0.5) * (1.0 / per_owner))
    before = jnp.sum(
        jnp.where(fine_col < coarse * per_owner, counts_col, 0.0), axis=0, keepdims=True
    )
    index = lax.broadcasted_iota(jnp.int32, (1, rows), 1).astype(jnp.float32)
    row_key = fine_id * rows + index
    rank = jnp.zeros((1, rows), jnp.float32)
    for start in range(0, rows, LANES):
        other = column_of(row_key[:, start : start + LANES])
        rank = rank + jnp.sum(jnp.where(other < row_key, 1.0, 0.0), axis=0, keepdims=True)
    pos = (coarse * capacity + rank - before).astype(jnp.int32)
    pos_row[...] = pos
    pos_ref[...] = jnp.concatenate(
        [pos[:, start : start + LANES] for start in range(0, rows, LANES)], axis=0
    )
    x = x_ref[...].astype(jnp.float32)
    squares = jnp.sum(x * x, axis=1, keepdims=True)
    unit[...] = (x * lax.rsqrt(squares + epsilon)).astype(jnp.bfloat16)

    step = 256

    @pl.loop(0, out_ref.shape[0] // step)
    def _(block):
        slot = lax.broadcasted_iota(jnp.int32, (step, rows), 0) + block * step
        chosen = jnp.where(slot == pos_row[...], 1.0, 0.0).astype(jnp.bfloat16)
        packed = jnp.dot(chosen, unit[...], preferred_element_type=jnp.float32)
        out_ref[pl.ds(pl.multiple_of(block * step, step), step), :] = packed.astype(jnp.bfloat16)


def pack(embeddings, labels, owner_map, n_owner, capacity):
    rows, width = embeddings.shape
    n_fine = owner_map.shape[0]
    total = n_owner * capacity
    vmem = pl.BlockSpec(memory_space=pltpu.VMEM)
    return pl.pallas_call(
        functools.partial(pack_kernel, n_owner, capacity),
        out_shape=(
            jax.ShapeDtypeStruct((total, width), jnp.bfloat16),
            jax.ShapeDtypeStruct((rows // LANES, LANES), jnp.int32),
            jax.ShapeDtypeStruct((1, n_fine), jnp.int32),
        ),
        in_specs=[vmem] * 3,
        out_specs=(vmem, vmem, vmem),
        scratch_shapes=[pltpu.VMEM((rows, width), jnp.bfloat16), pltpu.VMEM((1, rows), jnp.int32)],
        compiler_params=pltpu.CompilerParams(vmem_limit_bytes=VMEM_LIMIT),
    )(embeddings, labels.reshape(rows // LANES, LANES), owner_map.reshape(1, n_fine))


def counts_kernel(n_owner, capacity, cnt_ref, mine_ref, other_ref, out_ref, lab_lane, lab_sub, bias):
    total = mine_ref.shape[0]
    per_owner = cnt_ref.shape[1] // n_owner
    me = lax.axis_index("cl")
    grp = lax.axis_index("grp")
    n_grp = lax.axis_size("grp")
    for member in range(2):
        for source in range(n_owner):
            line = source * n_grp + lax.rem(grp + member, n_grp)
            edges = []
            edge = jnp.int32(0)
            for f in range(per_owner):
                edge = edge + cnt_ref[line, me * per_owner + f]
                edges.append(edge)
            down = lax.broadcasted_iota(jnp.int32, (capacity, LANES), 0)
            label = jnp.zeros((capacity, LANES), jnp.int32)
            for edge in edges:
                label = label + jnp.where(down >= edge, 1, 0)
            start = (member * n_owner + source) * capacity
            lab_sub[start : start + capacity, :] = label
            bias[start : start + capacity, :] = jnp.where(
                label < per_owner, NEIGHBOUR - SCALE, DEAD
            )
            if member == 0:
                across = lax.broadcasted_iota(jnp.int32, (1, capacity), 1)
                label = jnp.zeros((1, capacity), jnp.int32)
                for edge in edges:
                    label = label + jnp.where(across >= edge, 1, 0)
                lab_lane[:, source * capacity : (source + 1) * capacity] = jnp.where(
                    label < per_owner, label, -1
                )
    wide, deep = min(512, total), min(256, total)

    @pl.loop(0, total // wide)
    def _(block):
        columns = pl.ds(pl.multiple_of(block * wide, wide), wide)
        rows_i = mine_ref[columns, :]
        label_i = lab_lane[:, columns]

        def add(ref, offset):
            def step(j, acc):
                start = pl.multiple_of(j * deep, deep)
                scores = lax.dot_general(
                    ref[pl.ds(start, deep), :],
                    rows_i,
                    (((1,), (1,)), ((), ())),
                    preferred_element_type=jnp.float32,
                )
                place = pl.ds(pl.multiple_of(start + offset, deep), deep)
                label_j = lab_sub[place, :]
                bias_j = bias[place, :]
                repeat = wide // LANES
                label_j = jnp.concatenate([label_j] * repeat, axis=1)
                bias_j = jnp.concatenate([bias_j] * repeat, axis=1)
                shift = jnp.where(label_j == label_i, -SCALE, bias_j)
                terms = jnp.exp2(scores * SCALE + shift)
                return acc + jnp.sum(terms.reshape(deep // 8, 8, wide), axis=0)

            return step

        acc = jnp.zeros((8, wide), jnp.float32)
        acc = lax.fori_loop(0, total // deep, add(mine_ref, 0), acc, unroll=2)
        acc = lax.fori_loop(0, total // deep, add(other_ref, total), acc, unroll=2)
        totals = jnp.sum(acc, axis=0, keepdims=True)
        out_ref[:, columns] = jnp.log(jnp.where(label_i >= 0, totals, 1.0))


def log_counts(counts, mine, other, n_owner, capacity):
    total = mine.shape[0]
    vmem = pl.BlockSpec(memory_space=pltpu.VMEM)
    return pl.pallas_call(
        functools.partial(counts_kernel, n_owner, capacity),
        out_shape=jax.ShapeDtypeStruct((1, total), jnp.float32),
        in_specs=[pl.BlockSpec(memory_space=pltpu.SMEM), vmem, vmem],
        out_specs=vmem,
        scratch_shapes=[
            pltpu.VMEM((1, total), jnp.int32),
            pltpu.VMEM((2 * total, LANES), jnp.int32),
            pltpu.VMEM((2 * total, LANES), jnp.float32),
        ],
        compiler_params=pltpu.CompilerParams(vmem_limit_bytes=VMEM_LIMIT),
    )(counts, mine, other)


def unpack_kernel(values_ref, pos_ref, out_ref):
    pos = pos_ref[...]
    lane = lax.rem(pos, LANES)
    line = lax.div(pos, LANES)
    out = jnp.zeros(pos.shape, jnp.float32)
    for r in range(values_ref.shape[0]):
        table = jnp.broadcast_to(values_ref[r : r + 1, :], pos.shape)
        found = jnp.take_along_axis(table, lane, axis=1)
        out = jnp.where(line == r, found, out)
    out_ref[...] = out


def unpack(values, pos):
    vmem = pl.BlockSpec(memory_space=pltpu.VMEM)
    return pl.pallas_call(
        unpack_kernel,
        out_shape=jax.ShapeDtypeStruct(pos.shape, jnp.float32),
        in_specs=[vmem, vmem],
        out_specs=vmem,
    )(values.reshape(-1, LANES), pos)


def swapped(x, first, second):
    return jnp.where(x == first, second, jnp.where(x == second, first, x))


def place_kernel(lay, x_hbm, lab_hbm, map_hbm, *refs):
    main_hbm, tail_ref, pos_ref, x_ref, lab_ref, map_ref, unit, main_ref, sems = refs
    n_owner, capacity, main, home = lay.n_owner, lay.capacity, lay.main, lay.home
    copies = [
        pltpu.make_async_copy(src, dst, sems.at[i])
        for i, (src, dst) in enumerate(((x_hbm, x_ref), (lab_hbm, lab_ref), (map_hbm, map_ref)))
    ]
    for copy in copies:
        copy.start()
    rows, width = x_ref.shape
    n_fine = map_ref.shape[1]
    per_owner = n_fine // n_owner
    copies[1].wait()
    copies[2].wait()
    owner_row = map_ref[...].astype(jnp.float32)
    fine_row = lax.broadcasted_iota(jnp.int32, (1, n_fine), 1).astype(jnp.float32)
    key_row = owner_row * n_fine + fine_row
    key_col = column_of(key_row)
    sorted_col = jnp.sum(jnp.where(key_row < key_col, 1.0, 0.0), axis=1, keepdims=True)
    lab = lab_ref[...].astype(jnp.float32)
    lab_row = jnp.concatenate([lab[b : b + 1, :] for b in range(lab.shape[0])], axis=1)
    fine_col = lax.broadcasted_iota(jnp.int32, (n_fine, rows), 0).astype(jnp.float32)
    fine_id = jnp.sum(jnp.where(fine_col == lab_row, sorted_col, 0.0), axis=0, keepdims=True)
    counts_col = jnp.sum(jnp.where(fine_col == fine_id, 1.0, 0.0), axis=1, keepdims=True)
    coarse = jnp.floor((fine_id + 0.5) * (1.0 / per_owner))
    first = coarse * per_owner
    before = jnp.sum(jnp.where(fine_col < first, counts_col, 0.0), axis=0, keepdims=True)
    upto = jnp.sum(jnp.where(fine_col < first + per_owner, counts_col, 0.0), axis=0, keepdims=True)
    full = jnp.min(
        jnp.where(upto - before == capacity, coarse, float(n_owner)), axis=1, keepdims=True
    )
    line = lax.broadcasted_iota(jnp.int32, (n_fine, LANES), 0)
    lane = lax.broadcasted_iota(jnp.int32, (n_fine, LANES), 1)
    inside = (line <= lane) & (lax.div(line, per_owner) == lax.div(lane, per_owner))
    running = jnp.sum(jnp.where(inside, counts_col, 0.0), axis=0, keepdims=True)
    info = jnp.where(lane[:1] < n_fine, running, full)
    index = lax.broadcasted_iota(jnp.int32, (1, rows), 1).astype(jnp.float32)
    row_key = fine_id * rows + index
    rank = jnp.zeros((1, rows), jnp.float32)
    for start in range(0, rows, LANES):
        other = column_of(row_key[:, start : start + LANES])
        rank = rank + jnp.sum(jnp.where(other < row_key, 1.0, 0.0), axis=0, keepdims=True)
    rank = (rank - before).astype(jnp.int32)
    place = swapped(coarse.astype(jnp.int32), full.astype(jnp.int32), home)
    table = place * capacity + rank
    pos_ref[...] = jnp.concatenate(
        [table[:, start : start + LANES] for start in range(0, rows, LANES)], axis=0
    )
    fits = rank < jnp.where(place == home, lay.head, main - 1)
    slot = jnp.where(fits, place * main + rank, -1)
    tail_slot = jnp.where(place == home, rank - lay.head, -1)
    copies[0].wait()
    x = x_ref[...].astype(jnp.float32)
    squares = jnp.sum(x * x, axis=1, keepdims=True)
    unit[...] = (x * lax.rsqrt(squares + epsilon)).astype(jnp.bfloat16)

    def chosen_rows(slot, start, count):
        here = lax.broadcasted_iota(jnp.int32, (count, rows), 0) + start
        chosen = jnp.where(here == slot, 1.0, 0.0).astype(jnp.bfloat16)
        return jnp.dot(chosen, unit[...], preferred_element_type=jnp.float32)

    count = 2 * main
    down = lax.broadcasted_iota(jnp.int32, (count, LANES), 0)
    is_info = lax.rem(down, main) == main - 1
    writes = []
    for i, start in enumerate(range(0, lay.n_main, count)):
        packed = chosen_rows(slot, start, count)
        place = slice(start, start + count)
        main_ref[place, LANES:] = packed[:, LANES:].astype(jnp.bfloat16)
        main_ref[place, :LANES] = jnp.where(is_info, info, packed[:, :LANES]).astype(jnp.bfloat16)
        writes.append(
            pltpu.make_async_copy(
                main_ref.at[pl.ds(start, count)], main_hbm.at[pl.ds(start, count)], sems.at[3 + i]
            )
        )
        writes[-1].start()
    tail_ref[...] = chosen_rows(tail_slot, 0, lay.rest).astype(jnp.bfloat16)
    for write in writes:
        write.wait()


def vmem_specs(count):
    return (pl.BlockSpec(memory_space=pltpu.VMEM),) * count


def place_rows(embeddings, labels, owner_map, lay):
    rows, width = embeddings.shape
    n_fine = owner_map.shape[0]
    lab_shape = (rows // LANES, LANES)
    anywhere = pl.BlockSpec(memory_space=pl.ANY)
    return pl.pallas_call(
        functools.partial(place_kernel, lay),
        out_shape=(
            jax.ShapeDtypeStruct((lay.n_main, width), jnp.bfloat16),
            jax.ShapeDtypeStruct((lay.rest, width), jnp.bfloat16),
            jax.ShapeDtypeStruct(lab_shape, jnp.int32),
        ),
        in_specs=[anywhere] * 3,
        out_specs=(anywhere,) + vmem_specs(2),
        scratch_shapes=[
            pltpu.VMEM((rows, width), jnp.bfloat16),
            pltpu.VMEM(lab_shape, jnp.int32),
            pltpu.VMEM((1, n_fine), jnp.int32),
            pltpu.VMEM((rows, width), jnp.bfloat16),
            pltpu.VMEM((lay.n_main, width), jnp.bfloat16),
            pltpu.SemaphoreType.DMA((3 + lay.n_owner // 2,)),
        ],
        compiler_params=pltpu.CompilerParams(vmem_limit_bytes=FAST_LIMIT),
    )(embeddings, labels.reshape(lab_shape), owner_map.reshape(1, n_fine))


def gate_kernel(*refs):
    pass


def after(rows, *there):
    return pl.pallas_call(
        gate_kernel,
        out_shape=jax.ShapeDtypeStruct(rows.shape, rows.dtype),
        in_specs=list(vmem_specs(1 + len(there))),
        out_specs=vmem_specs(1)[0],
        input_output_aliases={0: 0},
        compiler_params=pltpu.CompilerParams(vmem_limit_bytes=FAST_LIMIT),
    )(rows, *there)


def lay_out_kernel(n_arrays, home, *refs):
    chunks, out = refs[:n_arrays], refs[-1]

    def copy():
        start = 0
        for chunk in chunks:
            out[start : start + chunk.shape[0], :] = chunk[...]
            start += chunk.shape[0]

    if home is None:
        copy()
    else:
        pl.when(lax.axis_index("cl") == home)(copy)


def lay_out(chunks, home=None, waits=()):
    rows, width = sum(x.shape[0] for x in chunks), chunks[0].shape[1]
    return pl.pallas_call(
        functools.partial(lay_out_kernel, len(chunks), home),
        out_shape=jax.ShapeDtypeStruct((rows, width), jnp.bfloat16),
        in_specs=list(vmem_specs(len(chunks) + len(waits))),
        out_specs=vmem_specs(1)[0],
        compiler_params=pltpu.CompilerParams(vmem_limit_bytes=FAST_LIMIT),
    )(*chunks, *waits)


class Layout:
    early, late = (0, 1, 2, 3), (4, 6, 5, 7)

    def __init__(self, n_owner, n_fine, capacity, main, home):
        self.n_owner, self.n_fine, self.capacity = n_owner, n_fine, capacity
        self.main, self.home = main, home
        self.head = main - INFO
        self.rest = capacity - self.head
        self.per_owner = n_fine // n_owner
        self.n_main = n_owner * main
        self.n_head = n_owner * self.head
        self.n_early = len(self.early) * self.rest
        self.n_late = len(self.late) * self.rest
        self.n_first = self.n_head + self.n_early
        self.n_all = self.n_first + self.n_late


def info_line(lay, main_ref, source):
    end = (source + 1) * lay.main
    return main_ref[end - INFO : end, :LANES].astype(jnp.float32)[INFO - 1 :]


def lines_of(lay, main_ref):
    return [info_line(lay, main_ref, source) for source in range(lay.n_owner)]


def hot_of(lay, info):
    lane = lax.broadcasted_iota(jnp.int32, (1, LANES), 1)
    hot = jnp.max(jnp.where(lane == lay.n_fine, info, 0.0), axis=1, keepdims=True)
    return hot.astype(jnp.int32)


def write_labels(lay, infos, sources, first, count, at, lab_sub, bias):
    cluster = swapped(lax.axis_index("cl"), hot_of(lay, infos[0]), lay.home)
    lane = lax.broadcasted_iota(jnp.int32, (1, LANES), 1)
    is_edge = lax.div(lane, lay.per_owner) == cluster
    for i, source in enumerate(sources):
        edges = jnp.where(is_edge, infos[source], 2.0 * lay.capacity)
        slot = lax.broadcasted_iota(jnp.int32, (count, LANES), 0) + first
        label = jnp.where(slot.astype(jnp.float32) >= edges, 1.0, 0.0)
        label = jnp.broadcast_to(jnp.sum(label, axis=1, keepdims=True), (count, LANES))
        start = at + i * count
        lab_sub[start : start + count, :] = label
        if bias is not None:
            bias[start : start + count, :] = jnp.where(
                label < lay.per_owner, NEIGHBOUR - SCALE, DEAD
            )


def first_labels(lay, infos, lab_sub):
    write_labels(lay, infos, range(lay.n_owner), 0, lay.head, 0, lab_sub, None)
    write_labels(lay, infos, lay.early, lay.head, lay.rest, lay.n_head, lab_sub, None)


def late_labels(lay, infos, lab_sub):
    write_labels(lay, infos, lay.late, lay.head, lay.rest, 0, lab_sub, None)


def turn_labels(lay, lab_sub, count, lab_lane, at):
    for i in range(0, count, LANES):
        block = jnp.transpose(lab_sub[i : i + LANES, :])[:1]
        lab_lane[:, at + i : at + i + LANES] = jnp.where(block < lay.per_owner, block, -1.0)


def copy_head(lay, main_ref, rows):
    for source in range(lay.n_owner):
        rows[source * lay.head : (source + 1) * lay.head, :] = main_ref[
            source * lay.main : source * lay.main + lay.head, :
        ]


def pieces(count, parts):
    return [(i * (count // parts), count // parts) for i in range(parts)]


def stream(lanes, tiles, lab_lane, buffers, put):
    rows_i, count, at = lanes
    step = 32
    tiles = [
        (ref, s, d, lab_sub, bias, line + s, back)
        for ref, n, lab_sub, bias, line, parts, back in tiles
        for s, d in pieces(n, parts)
    ]

    def scores_to(buffer, tile, rows):
        ref, start, deep = tile[:3]
        buffer[:deep, : rows.shape[0]] = lax.dot_general(
            ref[start : start + deep, :],
            rows,
            (((1,), (1,)), ((), ())),
            preferred_element_type=jnp.float32,
        )

    def run(start, blocks, wide):
        repeat = wide // LANES

        def rows_of(block):
            return rows_i[pl.ds(pl.multiple_of(start + block * wide, LANES), wide), :]

        scores_to(buffers[0], tiles[0], rows_of(0))

        def one_block(block):
            here = rows_of(block)
            place = pl.ds(pl.multiple_of(at + start + block * wide, LANES), wide)
            label_i = lab_lane[:, place]
            acc = jnp.zeros((8, wide), jnp.float32)
            for i, (_, _, deep, lab_sub, bias, line, back) in enumerate(tiles):
                if i + 1 < len(tiles):
                    scores_to(buffers[(i + 1) % 2], tiles[i + 1], here)
                elif blocks > 1:

                    @pl.when(block + 1 < blocks)
                    def _():
                        scores_to(buffers[0], tiles[0], rows_of(block + 1))

                buffer = buffers[i % 2]
                for c in range(0, deep, step):
                    part = slice(line + c, line + c + step)
                    label_j = jnp.concatenate([lab_sub[part, :]] * repeat, axis=1)
                    if bias is None:
                        bias_j = NEIGHBOUR - SCALE
                    else:
                        bias_j = jnp.concatenate([bias[part, :]] * repeat, axis=1)
                    shift = jnp.where(label_j == label_i, -SCALE, bias_j)
                    terms = jnp.exp2(buffer[c : c + step, :wide] * SCALE + shift)
                    acc = acc + jnp.sum(terms.reshape(step // 8, 8, wide), axis=0)
                    if back is not None:
                        across = terms[:, :LANES]
                        for r in range(1, repeat):
                            across = across + terms[:, r * LANES : (r + 1) * LANES]
                        back[part, :] += across
            put(place, jnp.sum(acc, axis=0, keepdims=True))

        if blocks == 1:
            one_block(0)
        else:
            pl.loop(0, blocks)(one_block)

    if count >= WIDE:
        run(0, count // WIDE, WIDE)
    if count % WIDE:
        run(count - count % WIDE, 1, count % WIDE)


def turn_sums(back, count, sums, at):
    for i in range(0, count, LANES):
        block = jnp.transpose(back[i : i + LANES, :])
        sums[:, at + i : at + i + LANES] += jnp.sum(block, axis=0, keepdims=True)


def setter(ref):
    def put(place, values):
        ref[:, place] = values

    return put


def adder(ref):
    def put(place, values):
        ref[:, place] += values

    return put


def inner_kernel(lay, mine, early, sums, lab_lane, lab_sub, rows, bias, back, buf_a, buf_b):
    is_home = lax.axis_index("cl") == lay.home
    infos = lines_of(lay, mine)
    buffers = (buf_a, buf_b)

    @pl.when(is_home)
    def _():
        copy_head(lay, mine, rows)
        first_labels(lay, infos, lab_sub)
        turn_labels(lay, lab_sub, lay.n_first, lab_lane, 0)
        back[...] = jnp.zeros(back.shape, jnp.float32)
        size = lay.n_early
        blocks = [(rows.at[pl.ds(start, size)], start) for start in range(0, lay.n_head, size)]
        blocks.append((early, lay.n_head))
        for i, (ref, at) in enumerate(blocks):
            tiles = [
                (ref_j, size, lab_sub, None, at_j, 2, None if at_j == at else back)
                for ref_j, at_j in blocks[i:]
            ]
            stream((ref, size, at), tiles, lab_lane, buffers, setter(sums))
        turn_sums(back, lay.n_first, sums, 0)

    @pl.when(jnp.logical_not(is_home))
    def _():
        write_labels(lay, infos, range(lay.n_owner), 0, lay.main, 0, lab_sub, bias)
        turn_labels(lay, lab_sub, lay.n_main, lab_lane, 0)
        tiles = [(mine, lay.n_main, lab_sub, bias, 0, 2, None)]
        stream((mine, lay.n_main, 0), tiles, lab_lane, buffers, setter(sums))


def cross_kernel(lay, mine, other, early, early_j, rows, sums, lab_lane, *refs):
    total, unfit_ref, lab_sub, rows_j, bias, buf_a, buf_b = refs
    is_home = lax.axis_index("cl") == lay.home
    infos = lines_of(lay, other)
    own = lines_of(lay, mine)
    hot = hot_of(lay, own[0])
    lane = lax.broadcasted_iota(jnp.int32, (1, LANES), 1)
    last = (lane < lay.n_fine) & (lax.rem(lane, lay.per_owner) == lay.per_owner - 1)
    last = last & (lax.div(lane, lay.per_owner) != hot)
    unfit = jnp.zeros((1, LANES), jnp.float32)
    for info in infos + own:
        wrong = last & (info >= lay.main)
        differs = (info != hot.astype(jnp.float32)) | (info >= lay.n_owner)
        wrong = wrong | ((lane == lay.n_fine) & differs)
        unfit = unfit + jnp.where(wrong, 1.0, 0.0)
    unfit_ref[0, 0] = jnp.max(unfit).astype(jnp.int32)
    total[...] = sums[...]
    buffers = (buf_a, buf_b)

    @pl.when(is_home)
    def _():
        copy_head(lay, other, rows_j)
        first_labels(lay, infos, lab_sub)
        tiles = [(rows_j, lay.n_head, lab_sub, None, 0, 2, None)]
        tiles += [(early_j, lay.n_early, lab_sub, None, lay.n_head, 2, None)]
        stream((rows, lay.n_head, 0), tiles, lab_lane, buffers, adder(total))
        stream((early, lay.n_early, lay.n_head), tiles, lab_lane, buffers, adder(total))

    @pl.when(jnp.logical_not(is_home))
    def _():
        write_labels(lay, infos, range(lay.n_owner), 0, lay.main, 0, lab_sub, bias)
        tiles = [(other, lay.n_main, lab_sub, bias, 0, 2, None)]
        stream((mine, lay.n_main, 0), tiles, lab_lane, buffers, adder(total))


def late_pairs(lay, i_refs, j_refs, lab_sub, late_sub, lab_lane, buffers, put, back=None):
    rows, early, late = i_refs
    rows_j, early_j, late_j = j_refs
    lates = [(late_j, lay.n_late, late_sub, None, 0, 2, back)]
    stream((rows, lay.n_head, 0), lates, lab_lane, buffers, put)
    stream((early, lay.n_early, lay.n_head), lates, lab_lane, buffers, put)
    every = [(late_j, lay.n_late, late_sub, None, 0, 2, None)]
    if back is None:
        every += [(rows_j, lay.n_head, lab_sub, None, 0, 2, None)]
        every += [(early_j, lay.n_early, lab_sub, None, lay.n_head, 2, None)]
    stream((late, lay.n_late, lay.n_first), every, lab_lane, buffers, put)


def inner_late_kernel(lay, mine, early, late, rows, lab_sub, first_lane, *refs):
    sums, lab_lane, late_sub, back, buf_a, buf_b = refs

    @pl.when(lax.axis_index("cl") == lay.home)
    def _():
        late_labels(lay, lines_of(lay, mine), late_sub)
        lab_lane[:, : lay.n_first] = first_lane[...]
        turn_labels(lay, late_sub, lay.n_late, lab_lane, lay.n_first)
        refs = (rows, early, late)
        buffers = (buf_a, buf_b)
        back[...] = jnp.zeros(back.shape, jnp.float32)
        put = setter(sums)
        late_pairs(lay, refs, refs, lab_sub, late_sub, lab_lane, buffers, put, back)
        turn_sums(back, lay.n_late, sums, lay.n_first)


def cross_late_kernel(lay, other, early, late, early_j, late_j, rows, rows_j, *refs):
    lab_sub, first_lane, first_sums, lab_lane, sums = refs[:5]
    out_ref, total, late_sub, buf_a, buf_b = refs[5:]
    is_home = lax.axis_index("cl") == lay.home

    @pl.when(is_home)
    def _():
        late_labels(lay, lines_of(lay, other), late_sub)
        total[...] = sums[...]
        total[:, : lay.n_first] += first_sums[...]
        i_refs, j_refs = (rows, early, late), (rows_j, early_j, late_j)
        buffers = (buf_a, buf_b)
        late_pairs(lay, i_refs, j_refs, lab_sub, late_sub, lab_lane, buffers, adder(total))
        values = jnp.log(total[...])
        for source in range(lay.n_owner):
            start = source * lay.head
            out_ref[source, :, : lay.head] = values[:, start : start + lay.head]
        for i, source in enumerate(lay.early + lay.late):
            start = lay.n_head + i * lay.rest
            out_ref[source, :, lay.head :] = values[:, start : start + lay.rest]

    @pl.when(jnp.logical_not(is_home))
    def _():
        values = jnp.log(jnp.where(first_lane[...] >= 0, first_sums[...], 1.0))
        for source in range(lay.n_owner):
            start = source * lay.main
            out_ref[source, :, : lay.main] = values[:, start : start + lay.main]


def pair_call(kernel, lay, arrays, out_shape, scratch, out_specs=None, pairs=0):
    width = arrays[0].shape[1]
    buffer = pltpu.VMEM((lay.n_main // 2, WIDE), jnp.float32)
    return pl.pallas_call(
        functools.partial(kernel, lay),
        out_shape=out_shape,
        in_specs=list(vmem_specs(len(arrays))),
        out_specs=out_specs or vmem_specs(len(out_shape)),
        scratch_shapes=list(scratch) + [buffer, buffer],
        compiler_params=pltpu.CompilerParams(vmem_limit_bytes=FAST_LIMIT),
        cost_estimate=pl.CostEstimate(
            flops=2 * pairs * width, bytes_accessed=1, transcendentals=pairs
        ),
    )(*arrays)


def fast_unpack_kernel(values_ref, pos_ref, out_ref):
    pos = pos_ref[...]
    lane = lax.rem(pos, LANES)
    line = lax.div(pos, LANES)
    out = jnp.zeros(pos.shape, jnp.float32)
    per = values_ref.shape[2] // LANES
    for r in range(values_ref.shape[0] * per):
        start = r % per * LANES
        table = jnp.broadcast_to(values_ref[r // per, :, start : start + LANES], pos.shape)
        found = jnp.take_along_axis(table, lane, axis=1)
        out = jnp.where(line == r, found, out)
    out_ref[...] = out


def fast_unpack(values, pos):
    vmem = pl.BlockSpec(memory_space=pltpu.VMEM)
    return pl.pallas_call(
        fast_unpack_kernel,
        out_shape=jax.ShapeDtypeStruct(pos.shape, jnp.float32),
        in_specs=[vmem, vmem],
        out_specs=vmem,
    )(values, pos)


def general(embeddings, labels, owner_map):
    n_owner = lax.axis_size("cl")
    capacity = SLOTS // n_owner
    rows, width = embeddings.shape
    packed, pos, counts = pack(embeddings, labels, owner_map, n_owner, capacity)
    counts = lax.all_gather(counts, ("cl", "grp"), tiled=True)
    mine = lax.all_to_all(
        packed.reshape(n_owner, capacity, width), "cl", split_axis=0, concat_axis=0, tiled=True
    ).reshape(SLOTS, width)
    other = lax.ppermute(mine, "grp", [(0, 1), (1, 0)])
    results = log_counts(counts, mine, other, n_owner, capacity)
    returned = lax.all_to_all(
        results.reshape(n_owner, capacity), "cl", split_axis=0, concat_axis=0, tiled=True
    )
    return unpack(returned.reshape(SLOTS), pos).reshape(rows)


def body(embeddings, labels, owner_map):
    n_owner = lax.axis_size("cl")
    capacity = SLOTS // n_owner
    rows, width = embeddings.shape
    n_fine = owner_map.shape[0]
    main = -(-(rows // n_owner * 9 // 8) // 16) * 16
    if n_owner != 8 or main >= capacity or n_fine >= LANES:
        return general(embeddings, labels, owner_map)
    home = 2
    lay = Layout(n_owner, n_fine, capacity, main, home)
    packed, extra, pos = place_rows(embeddings, labels, owner_map, lay)

    def hop(x, pairs):
        return lax.ppermute(x, "cl", pairs)

    def swap(x):
        return lax.ppermute(x, "grp", [(0, 1), (1, 0)])

    both = lay_out([extra, hop(extra, [(6, 4), (7, 5)])])
    early = [extra if s == home else hop(extra, [(s, home)]) for s in lay.early]
    early = lay_out(early, home)
    mine = lax.all_to_all(
        packed.reshape(n_owner, main, width), "cl", split_axis=0, concat_axis=0, tiled=True
    ).reshape(n_owner * main, width)
    mine = after(mine, early, both)
    other, early_j = swap(mine), swap(early)
    late = [hop(both, [(4, home)]), hop(both, [(5, home)])]

    def array(shape, dtype=jnp.float32):
        return jax.ShapeDtypeStruct(shape, dtype)

    def scratch(shape):
        return pltpu.VMEM(shape, jnp.float32)

    row, long_row = array((1, lay.n_first)), array((1, lay.n_all))
    side, bias = array((lay.n_first, LANES)), scratch((lay.n_main, LANES))
    heads = array((lay.n_head, width), jnp.bfloat16)
    late_side, first_side = scratch((lay.n_late, LANES)), scratch((lay.n_first, LANES))
    sums, first_lane, lab_sub, heads_i = pair_call(
        inner_kernel, lay, (mine, early), (row, row, side, heads), (bias, first_side)
    )
    specs = vmem_specs(1) + (pl.BlockSpec(memory_space=pltpu.SMEM),) + vmem_specs(2)
    sums, unfit, lab_sub_j, heads_j = pair_call(
        cross_kernel,
        lay,
        (mine, other, early, early_j, heads_i, sums, first_lane),
        (row, array((1, 1), jnp.int32), side, heads),
        (bias,),
        specs,
    )
    late = lay_out(late, home, (sums,))
    late_j = swap(late)
    late_sums, lane = pair_call(
        inner_late_kernel,
        lay,
        (mine, early, late, heads_i, lab_sub, first_lane),
        (long_row, long_row),
        (late_side, late_side),
        pairs=lay.n_late * (lay.n_all + lay.n_first),
    )
    (results,) = pair_call(
        cross_late_kernel,
        lay,
        (
            *(other, early, late, early_j, late_j, heads_i, heads_j),
            *(lab_sub_j, first_lane, sums, lane, late_sums),
        ),
        (array((n_owner, 1, capacity)),),
        (scratch(long_row.shape), late_side),
    )
    returned = lax.all_to_all(results, "cl", split_axis=0, concat_axis=0, tiled=True)
    return lax.cond(
        unfit[0, 0] == 0,
        lambda: fast_unpack(returned, pos).reshape(rows),
        lambda: general(embeddings, labels, owner_map),
    )


def solution(mesh):
    return jax.shard_map(
        body,
        mesh=mesh,
        in_specs=(P(("parts", "cl", "grp"), None), P(("parts", "cl", "grp")), P("parts")),
        out_specs=P(("parts", "cl", "grp")),
        check_vma=False,
    )
```

```python
import functools
import math

import jax
import jax.numpy as jnp
from jax import lax
from jax.experimental import pallas as pl
from jax.experimental.pallas import tpu as pltpu
from jax.sharding import PartitionSpec as P

SLOTS = 2048

temper = 0.2
neighbour_factor = 0.5
epsilon = 1e-06

LANES = 128
SCALE = math.log2(math.e) / temper
NEIGHBOUR = math.log2(neighbour_factor)
DEAD = -1e30
VMEM_LIMIT = 48 * 1024 * 1024
FAST_LIMIT = 16 * 1024 * 1024
WIDE = 512
INFO = 16


def column_of(row):
    pieces = []
    for start in range(0, row.shape[1], LANES):
        width = min(LANES, row.shape[1] - start)
        shape = (width, width)
        diagonal = lax.broadcasted_iota(jnp.int32, shape, 0) == lax.broadcasted_iota(
            jnp.int32, shape, 1
        )
        piece = jnp.broadcast_to(row[:, start : start + width], shape)
        pieces.append(jnp.sum(jnp.where(diagonal, piece, 0.0), axis=1, keepdims=True))
    return jnp.concatenate(pieces, axis=0)


def row_of(column):
    n = column.shape[0]
    diagonal = lax.broadcasted_iota(jnp.int32, (n, n), 0) == lax.broadcasted_iota(
        jnp.int32, (n, n), 1
    )
    return jnp.sum(jnp.where(diagonal, column, 0.0), axis=0, keepdims=True)


def pack_kernel(n_owner, capacity, x_ref, lab_ref, map_ref, out_ref, pos_ref, cnt_ref, unit, pos_row):
    rows = x_ref.shape[0]
    n_fine = map_ref.shape[1]
    per_owner = n_fine // n_owner
    owner_row = map_ref[...].astype(jnp.float32)
    fine_row = lax.broadcasted_iota(jnp.int32, (1, n_fine), 1).astype(jnp.float32)
    key_row = owner_row * n_fine + fine_row
    key_col = column_of(key_row)
    sorted_col = jnp.sum(jnp.where(key_row < key_col, 1.0, 0.0), axis=1, keepdims=True)
    lab = lab_ref[...].astype(jnp.float32)
    lab_row = jnp.concatenate([lab[b : b + 1, :] for b in range(lab.shape[0])], axis=1)
    fine_col = lax.broadcasted_iota(jnp.int32, (n_fine, rows), 0).astype(jnp.float32)
    fine_id = jnp.sum(jnp.where(fine_col == lab_row, sorted_col, 0.0), axis=0, keepdims=True)
    counts_col = jnp.sum(jnp.where(fine_col == fine_id, 1.0, 0.0), axis=1, keepdims=True)
    cnt_ref[...] = row_of(counts_col).astype(jnp.int32)
    coarse = jnp.floor((fine_id + 0.5) * (1.0 / per_owner))
    before = jnp.sum(
        jnp.where(fine_col < coarse * per_owner, counts_col, 0.0), axis=0, keepdims=True
    )
    index = lax.broadcasted_iota(jnp.int32, (1, rows), 1).astype(jnp.float32)
    row_key = fine_id * rows + index
    rank = jnp.zeros((1, rows), jnp.float32)
    for start in range(0, rows, LANES):
        other = column_of(row_key[:, start : start + LANES])
        rank = rank + jnp.sum(jnp.where(other < row_key, 1.0, 0.0), axis=0, keepdims=True)
    pos = (coarse * capacity + rank - before).astype(jnp.int32)
    pos_row[...] = pos
    pos_ref[...] = jnp.concatenate(
        [pos[:, start : start + LANES] for start in range(0, rows, LANES)], axis=0
    )
    x = x_ref[...].astype(jnp.float32)
    squares = jnp.sum(x * x, axis=1, keepdims=True)
    unit[...] = (x * lax.rsqrt(squares + epsilon)).astype(jnp.bfloat16)

    step = 256

    @pl.loop(0, out_ref.shape[0] // step)
    def _(block):
        slot = lax.broadcasted_iota(jnp.int32, (step, rows), 0) + block * step
        chosen = jnp.where(slot == pos_row[...], 1.0, 0.0).astype(jnp.bfloat16)
        packed = jnp.dot(chosen, unit[...], preferred_element_type=jnp.float32)
        out_ref[pl.ds(pl.multiple_of(block * step, step), step), :] = packed.astype(jnp.bfloat16)


def pack(embeddings, labels, owner_map, n_owner, capacity):
    rows, width = embeddings.shape
    n_fine = owner_map.shape[0]
    total = n_owner * capacity
    vmem = pl.BlockSpec(memory_space=pltpu.VMEM)
    return pl.pallas_call(
        functools.partial(pack_kernel, n_owner, capacity),
        out_shape=(
            jax.ShapeDtypeStruct((total, width), jnp.bfloat16),
            jax.ShapeDtypeStruct((rows // LANES, LANES), jnp.int32),
            jax.ShapeDtypeStruct((1, n_fine), jnp.int32),
        ),
        in_specs=[vmem] * 3,
        out_specs=(vmem, vmem, vmem),
        scratch_shapes=[pltpu.VMEM((rows, width), jnp.bfloat16), pltpu.VMEM((1, rows), jnp.int32)],
        compiler_params=pltpu.CompilerParams(vmem_limit_bytes=VMEM_LIMIT),
    )(embeddings, labels.reshape(rows // LANES, LANES), owner_map.reshape(1, n_fine))


def counts_kernel(n_owner, capacity, cnt_ref, mine_ref, other_ref, out_ref, lab_lane, lab_sub, bias):
    total = mine_ref.shape[0]
    per_owner = cnt_ref.shape[1] // n_owner
    me = lax.axis_index("cl")
    grp = lax.axis_index("grp")
    n_grp = lax.axis_size("grp")
    for member in range(2):
        for source in range(n_owner):
            line = source * n_grp + lax.rem(grp + member, n_grp)
            edges = []
            edge = jnp.int32(0)
            for f in range(per_owner):
                edge = edge + cnt_ref[line, me * per_owner + f]
                edges.append(edge)
            down = lax.broadcasted_iota(jnp.int32, (capacity, LANES), 0)
            label = jnp.zeros((capacity, LANES), jnp.int32)
            for edge in edges:
                label = label + jnp.where(down >= edge, 1, 0)
            start = (member * n_owner + source) * capacity
            lab_sub[start : start + capacity, :] = label
            bias[start : start + capacity, :] = jnp.where(
                label < per_owner, NEIGHBOUR - SCALE, DEAD
            )
            if member == 0:
                across = lax.broadcasted_iota(jnp.int32, (1, capacity), 1)
                label = jnp.zeros((1, capacity), jnp.int32)
                for edge in edges:
                    label = label + jnp.where(across >= edge, 1, 0)
                lab_lane[:, source * capacity : (source + 1) * capacity] = jnp.where(
                    label < per_owner, label, -1
                )
    wide, deep = min(512, total), min(256, total)

    @pl.loop(0, total // wide)
    def _(block):
        columns = pl.ds(pl.multiple_of(block * wide, wide), wide)
        rows_i = mine_ref[columns, :]
        label_i = lab_lane[:, columns]

        def add(ref, offset):
            def step(j, acc):
                start = pl.multiple_of(j * deep, deep)
                scores = lax.dot_general(
                    ref[pl.ds(start, deep), :],
                    rows_i,
                    (((1,), (1,)), ((), ())),
                    preferred_element_type=jnp.float32,
                )
                place = pl.ds(pl.multiple_of(start + offset, deep), deep)
                label_j = lab_sub[place, :]
                bias_j = bias[place, :]
                repeat = wide // LANES
                label_j = jnp.concatenate([label_j] * repeat, axis=1)
                bias_j = jnp.concatenate([bias_j] * repeat, axis=1)
                shift = jnp.where(label_j == label_i, -SCALE, bias_j)
                terms = jnp.exp2(scores * SCALE + shift)
                return acc + jnp.sum(terms.reshape(deep // 8, 8, wide), axis=0)

            return step

        acc = jnp.zeros((8, wide), jnp.float32)
        acc = lax.fori_loop(0, total // deep, add(mine_ref, 0), acc, unroll=2)
        acc = lax.fori_loop(0, total // deep, add(other_ref, total), acc, unroll=2)
        totals = jnp.sum(acc, axis=0, keepdims=True)
        out_ref[:, columns] = jnp.log(jnp.where(label_i >= 0, totals, 1.0))


def log_counts(counts, mine, other, n_owner, capacity):
    total = mine.shape[0]
    vmem = pl.BlockSpec(memory_space=pltpu.VMEM)
    return pl.pallas_call(
        functools.partial(counts_kernel, n_owner, capacity),
        out_shape=jax.ShapeDtypeStruct((1, total), jnp.float32),
        in_specs=[pl.BlockSpec(memory_space=pltpu.SMEM), vmem, vmem],
        out_specs=vmem,
        scratch_shapes=[
            pltpu.VMEM((1, total), jnp.int32),
            pltpu.VMEM((2 * total, LANES), jnp.int32),
            pltpu.VMEM((2 * total, LANES), jnp.float32),
        ],
        compiler_params=pltpu.CompilerParams(vmem_limit_bytes=VMEM_LIMIT),
    )(counts, mine, other)


def unpack_kernel(values_ref, pos_ref, out_ref):
    pos = pos_ref[...]
    lane = lax.rem(pos, LANES)
    line = lax.div(pos, LANES)
    out = jnp.zeros(pos.shape, jnp.float32)
    for r in range(values_ref.shape[0]):
        table = jnp.broadcast_to(values_ref[r : r + 1, :], pos.shape)
        found = jnp.take_along_axis(table, lane, axis=1)
        out = jnp.where(line == r, found, out)
    out_ref[...] = out


def unpack(values, pos):
    vmem = pl.BlockSpec(memory_space=pltpu.VMEM)
    return pl.pallas_call(
        unpack_kernel,
        out_shape=jax.ShapeDtypeStruct(pos.shape, jnp.float32),
        in_specs=[vmem, vmem],
        out_specs=vmem,
    )(values.reshape(-1, LANES), pos)


def swapped(x, first, second):
    return jnp.where(x == first, second, jnp.where(x == second, first, x))


def place_kernel(lay, x_hbm, lab_hbm, map_hbm, *refs):
    main_hbm, tail_ref, pos_ref, x_ref, lab_ref, map_ref, unit, main_ref, sems = refs
    n_owner, capacity, main, home = lay.n_owner, lay.capacity, lay.main, lay.home
    copies = [
        pltpu.make_async_copy(src, dst, sems.at[i])
        for i, (src, dst) in enumerate(((x_hbm, x_ref), (lab_hbm, lab_ref), (map_hbm, map_ref)))
    ]
    for copy in copies:
        copy.start()
    rows, width = x_ref.shape
    n_fine = map_ref.shape[1]
    per_owner = n_fine // n_owner
    copies[1].wait()
    copies[2].wait()
    owner_row = map_ref[...].astype(jnp.float32)
    fine_row = lax.broadcasted_iota(jnp.int32, (1, n_fine), 1).astype(jnp.float32)
    key_row = owner_row * n_fine + fine_row
    key_col = column_of(key_row)
    sorted_col = jnp.sum(jnp.where(key_row < key_col, 1.0, 0.0), axis=1, keepdims=True)
    lab = lab_ref[...].astype(jnp.float32)
    lab_row = jnp.concatenate([lab[b : b + 1, :] for b in range(lab.shape[0])], axis=1)
    fine_col = lax.broadcasted_iota(jnp.int32, (n_fine, rows), 0).astype(jnp.float32)
    fine_id = jnp.sum(jnp.where(fine_col == lab_row, sorted_col, 0.0), axis=0, keepdims=True)
    counts_col = jnp.sum(jnp.where(fine_col == fine_id, 1.0, 0.0), axis=1, keepdims=True)
    coarse = jnp.floor((fine_id + 0.5) * (1.0 / per_owner))
    first = coarse * per_owner
    before = jnp.sum(jnp.where(fine_col < first, counts_col, 0.0), axis=0, keepdims=True)
    upto = jnp.sum(jnp.where(fine_col < first + per_owner, counts_col, 0.0), axis=0, keepdims=True)
    full = jnp.min(
        jnp.where(upto - before == capacity, coarse, float(n_owner)), axis=1, keepdims=True
    )
    line = lax.broadcasted_iota(jnp.int32, (n_fine, LANES), 0)
    lane = lax.broadcasted_iota(jnp.int32, (n_fine, LANES), 1)
    inside = (line <= lane) & (lax.div(line, per_owner) == lax.div(lane, per_owner))
    running = jnp.sum(jnp.where(inside, counts_col, 0.0), axis=0, keepdims=True)
    info = jnp.where(lane[:1] < n_fine, running, full)
    index = lax.broadcasted_iota(jnp.int32, (1, rows), 1).astype(jnp.float32)
    row_key = fine_id * rows + index
    rank = jnp.zeros((1, rows), jnp.float32)
    for start in range(0, rows, LANES):
        other = column_of(row_key[:, start : start + LANES])
        rank = rank + jnp.sum(jnp.where(other < row_key, 1.0, 0.0), axis=0, keepdims=True)
    rank = (rank - before).astype(jnp.int32)
    place = swapped(coarse.astype(jnp.int32), full.astype(jnp.int32), home)
    table = place * capacity + rank
    pos_ref[...] = jnp.concatenate(
        [table[:, start : start + LANES] for start in range(0, rows, LANES)], axis=0
    )
    fits = rank < jnp.where(place == home, lay.head, main - 1)
    slot = jnp.where(fits, place * main + rank, -1)
    tail_slot = jnp.where(place == home, rank - lay.head, -1)
    copies[0].wait()
    x = x_ref[...].astype(jnp.float32)
    squares = jnp.sum(x * x, axis=1, keepdims=True)
    unit[...] = (x * lax.rsqrt(squares + epsilon)).astype(jnp.bfloat16)

    def chosen_rows(slot, start, count):
        here = lax.broadcasted_iota(jnp.int32, (count, rows), 0) + start
        chosen = jnp.where(here == slot, 1.0, 0.0).astype(jnp.bfloat16)
        return jnp.dot(chosen, unit[...], preferred_element_type=jnp.float32)

    count = 2 * main
    down = lax.broadcasted_iota(jnp.int32, (count, LANES), 0)
    is_info = lax.rem(down, main) == main - 1
    writes = []
    for i, start in enumerate(range(0, lay.n_main, count)):
        packed = chosen_rows(slot, start, count)
        place = slice(start, start + count)
        main_ref[place, LANES:] = packed[:, LANES:].astype(jnp.bfloat16)
        main_ref[place, :LANES] = jnp.where(is_info, info, packed[:, :LANES]).astype(jnp.bfloat16)
        writes.append(
            pltpu.make_async_copy(
                main_ref.at[pl.ds(start, count)], main_hbm.at[pl.ds(start, count)], sems.at[3 + i]
            )
        )
        writes[-1].start()
    tail_ref[...] = chosen_rows(tail_slot, 0, lay.rest).astype(jnp.bfloat16)
    for write in writes:
        write.wait()


def vmem_specs(count):
    return (pl.BlockSpec(memory_space=pltpu.VMEM),) * count


def place_rows(embeddings, labels, owner_map, lay):
    rows, width = embeddings.shape
    n_fine = owner_map.shape[0]
    lab_shape = (rows // LANES, LANES)
    anywhere = pl.BlockSpec(memory_space=pl.ANY)
    return pl.pallas_call(
        functools.partial(place_kernel, lay),
        out_shape=(
            jax.ShapeDtypeStruct((lay.n_main, width), jnp.bfloat16),
            jax.ShapeDtypeStruct((lay.rest, width), jnp.bfloat16),
            jax.ShapeDtypeStruct(lab_shape, jnp.int32),
        ),
        in_specs=[anywhere] * 3,
        out_specs=(anywhere,) + vmem_specs(2),
        scratch_shapes=[
            pltpu.VMEM((rows, width), jnp.bfloat16),
            pltpu.VMEM(lab_shape, jnp.int32),
            pltpu.VMEM((1, n_fine), jnp.int32),
            pltpu.VMEM((rows, width), jnp.bfloat16),
            pltpu.VMEM((lay.n_main, width), jnp.bfloat16),
            pltpu.SemaphoreType.DMA((3 + lay.n_owner // 2,)),
        ],
        compiler_params=pltpu.CompilerParams(vmem_limit_bytes=FAST_LIMIT),
    )(embeddings, labels.reshape(lab_shape), owner_map.reshape(1, n_fine))


def gate_kernel(*refs):
    pass


def after(rows, *there):
    return pl.pallas_call(
        gate_kernel,
        out_shape=jax.ShapeDtypeStruct(rows.shape, rows.dtype),
        in_specs=list(vmem_specs(1 + len(there))),
        out_specs=vmem_specs(1)[0],
        input_output_aliases={0: 0},
        compiler_params=pltpu.CompilerParams(vmem_limit_bytes=FAST_LIMIT),
    )(rows, *there)


def lay_out_kernel(n_arrays, home, *refs):
    chunks, out = refs[:n_arrays], refs[-1]

    def copy():
        start = 0
        for chunk in chunks:
            out[start : start + chunk.shape[0], :] = chunk[...]
            start += chunk.shape[0]

    if home is None:
        copy()
    else:
        pl.when(lax.axis_index("cl") == home)(copy)


def lay_out(chunks, home=None, waits=()):
    rows, width = sum(x.shape[0] for x in chunks), chunks[0].shape[1]
    return pl.pallas_call(
        functools.partial(lay_out_kernel, len(chunks), home),
        out_shape=jax.ShapeDtypeStruct((rows, width), jnp.bfloat16),
        in_specs=list(vmem_specs(len(chunks) + len(waits))),
        out_specs=vmem_specs(1)[0],
        compiler_params=pltpu.CompilerParams(vmem_limit_bytes=FAST_LIMIT),
    )(*chunks, *waits)


class Layout:
    early, late = (0, 1, 2, 3), (4, 6, 5, 7)

    def __init__(self, n_owner, n_fine, capacity, main, home):
        self.n_owner, self.n_fine, self.capacity = n_owner, n_fine, capacity
        self.main, self.home = main, home
        self.head = main - INFO
        self.rest = capacity - self.head
        self.per_owner = n_fine // n_owner
        self.n_main = n_owner * main
        self.n_head = n_owner * self.head
        self.n_early = len(self.early) * self.rest
        self.n_late = len(self.late) * self.rest
        self.n_first = self.n_head + self.n_early
        self.n_all = self.n_first + self.n_late


def info_line(lay, main_ref, source):
    end = (source + 1) * lay.main
    return main_ref[end - INFO : end, :LANES].astype(jnp.float32)[INFO - 1 :]


def lines_of(lay, main_ref):
    return [info_line(lay, main_ref, source) for source in range(lay.n_owner)]


def hot_of(lay, info):
    lane = lax.broadcasted_iota(jnp.int32, (1, LANES), 1)
    hot = jnp.max(jnp.where(lane == lay.n_fine, info, 0.0), axis=1, keepdims=True)
    return hot.astype(jnp.int32)


def write_labels(lay, infos, sources, first, count, at, lab_sub, bias):
    cluster = swapped(lax.axis_index("cl"), hot_of(lay, infos[0]), lay.home)
    lane = lax.broadcasted_iota(jnp.int32, (1, LANES), 1)
    is_edge = lax.div(lane, lay.per_owner) == cluster
    for i, source in enumerate(sources):
        edges = jnp.where(is_edge, infos[source], 2.0 * lay.capacity)
        slot = lax.broadcasted_iota(jnp.int32, (count, LANES), 0) + first
        label = jnp.where(slot.astype(jnp.float32) >= edges, 1.0, 0.0)
        label = jnp.broadcast_to(jnp.sum(label, axis=1, keepdims=True), (count, LANES))
        start = at + i * count
        lab_sub[start : start + count, :] = label
        if bias is not None:
            bias[start : start + count, :] = jnp.where(
                label < lay.per_owner, NEIGHBOUR - SCALE, DEAD
            )


def first_labels(lay, infos, lab_sub):
    write_labels(lay, infos, range(lay.n_owner), 0, lay.head, 0, lab_sub, None)
    write_labels(lay, infos, lay.early, lay.head, lay.rest, lay.n_head, lab_sub, None)


def late_labels(lay, infos, lab_sub):
    write_labels(lay, infos, lay.late, lay.head, lay.rest, 0, lab_sub, None)


def turn_labels(lay, lab_sub, count, lab_lane, at):
    for i in range(0, count, LANES):
        block = jnp.transpose(lab_sub[i : i + LANES, :])[:1]
        lab_lane[:, at + i : at + i + LANES] = jnp.where(block < lay.per_owner, block, -1.0)


def copy_head(lay, main_ref, rows):
    for source in range(lay.n_owner):
        rows[source * lay.head : (source + 1) * lay.head, :] = main_ref[
            source * lay.main : source * lay.main + lay.head, :
        ]


def pieces(count, parts):
    return [(i * (count // parts), count // parts) for i in range(parts)]


def stream(lanes, tiles, lab_lane, buffers, put):
    rows_i, count, at = lanes
    step = 32
    tiles = [
        (ref, s, d, lab_sub, bias, line + s, back)
        for ref, n, lab_sub, bias, line, parts, back in tiles
        for s, d in pieces(n, parts)
    ]

    def scores_to(buffer, tile, rows):
        ref, start, deep = tile[:3]
        buffer[:deep, : rows.shape[0]] = lax.dot_general(
            ref[start : start + deep, :],
            rows,
            (((1,), (1,)), ((), ())),
            preferred_element_type=jnp.float32,
        )

    def run(start, blocks, wide):
        repeat = wide // LANES

        def rows_of(block):
            return rows_i[pl.ds(pl.multiple_of(start + block * wide, LANES), wide), :]

        scores_to(buffers[0], tiles[0], rows_of(0))

        def one_block(block):
            here = rows_of(block)
            place = pl.ds(pl.multiple_of(at + start + block * wide, LANES), wide)
            label_i = lab_lane[:, place]
            acc = jnp.zeros((8, wide), jnp.float32)
            for i, (_, _, deep, lab_sub, bias, line, back) in enumerate(tiles):
                if i + 1 < len(tiles):
                    scores_to(buffers[(i + 1) % 2], tiles[i + 1], here)
                elif blocks > 1:

                    @pl.when(block + 1 < blocks)
                    def _():
                        scores_to(buffers[0], tiles[0], rows_of(block + 1))

                buffer = buffers[i % 2]
                for c in range(0, deep, step):
                    part = slice(line + c, line + c + step)
                    label_j = jnp.concatenate([lab_sub[part, :]] * repeat, axis=1)
                    if bias is None:
                        bias_j = NEIGHBOUR - SCALE
                    else:
                        bias_j = jnp.concatenate([bias[part, :]] * repeat, axis=1)
                    shift = jnp.where(label_j == label_i, -SCALE, bias_j)
                    terms = jnp.exp2(buffer[c : c + step, :wide] * SCALE + shift)
                    acc = acc + jnp.sum(terms.reshape(step // 8, 8, wide), axis=0)
                    if back is not None:
                        across = terms[:, :LANES]
                        for r in range(1, repeat):
                            across = across + terms[:, r * LANES : (r + 1) * LANES]
                        back[part, :] += across
            put(place, jnp.sum(acc, axis=0, keepdims=True))

        if blocks == 1:
            one_block(0)
        else:
            pl.loop(0, blocks)(one_block)

    if count >= WIDE:
        run(0, count // WIDE, WIDE)
    if count % WIDE:
        run(count - count % WIDE, 1, count % WIDE)


def turn_sums(back, count, sums, at):
    for i in range(0, count, LANES):
        block = jnp.transpose(back[i : i + LANES, :])
        sums[:, at + i : at + i + LANES] += jnp.sum(block, axis=0, keepdims=True)


def setter(ref):
    def put(place, values):
        ref[:, place] = values

    return put


def adder(ref):
    def put(place, values):
        ref[:, place] += values

    return put


def inner_kernel(lay, mine, early, sums, lab_lane, lab_sub, rows, bias, back, buf_a, buf_b):
    is_home = lax.axis_index("cl") == lay.home
    infos = lines_of(lay, mine)
    buffers = (buf_a, buf_b)

    @pl.when(is_home)
    def _():
        copy_head(lay, mine, rows)
        first_labels(lay, infos, lab_sub)
        turn_labels(lay, lab_sub, lay.n_first, lab_lane, 0)
        back[...] = jnp.zeros(back.shape, jnp.float32)
        size = lay.n_early
        blocks = [(rows.at[pl.ds(start, size)], start) for start in range(0, lay.n_head, size)]
        blocks.append((early, lay.n_head))
        for i, (ref, at) in enumerate(blocks):
            tiles = [
                (ref_j, size, lab_sub, None, at_j, 2, None if at_j == at else back)
                for ref_j, at_j in blocks[i:]
            ]
            stream((ref, size, at), tiles, lab_lane, buffers, setter(sums))
        turn_sums(back, lay.n_first, sums, 0)

    @pl.when(jnp.logical_not(is_home))
    def _():
        write_labels(lay, infos, range(lay.n_owner), 0, lay.main, 0, lab_sub, bias)
        turn_labels(lay, lab_sub, lay.n_main, lab_lane, 0)
        tiles = [(mine, lay.n_main, lab_sub, bias, 0, 2, None)]
        stream((mine, lay.n_main, 0), tiles, lab_lane, buffers, setter(sums))


def cross_kernel(lay, mine, other, early, early_j, rows, sums, lab_lane, *refs):
    total, unfit_ref, lab_sub, rows_j, bias, buf_a, buf_b = refs
    is_home = lax.axis_index("cl") == lay.home
    infos = lines_of(lay, other)
    own = lines_of(lay, mine)
    hot = hot_of(lay, own[0])
    lane = lax.broadcasted_iota(jnp.int32, (1, LANES), 1)
    last = (lane < lay.n_fine) & (lax.rem(lane, lay.per_owner) == lay.per_owner - 1)
    last = last & (lax.div(lane, lay.per_owner) != hot)
    unfit = jnp.zeros((1, LANES), jnp.float32)
    for info in infos + own:
        wrong = last & (info >= lay.main)
        differs = (info != hot.astype(jnp.float32)) | (info >= lay.n_owner)
        wrong = wrong | ((lane == lay.n_fine) & differs)
        unfit = unfit + jnp.where(wrong, 1.0, 0.0)
    unfit_ref[0, 0] = jnp.max(unfit).astype(jnp.int32)
    total[...] = sums[...]
    buffers = (buf_a, buf_b)

    @pl.when(is_home)
    def _():
        copy_head(lay, other, rows_j)
        first_labels(lay, infos, lab_sub)
        tiles = [(rows_j, lay.n_head, lab_sub, None, 0, 2, None)]
        tiles += [(early_j, lay.n_early, lab_sub, None, lay.n_head, 2, None)]
        stream((rows, lay.n_head, 0), tiles, lab_lane, buffers, adder(total))
        stream((early, lay.n_early, lay.n_head), tiles, lab_lane, buffers, adder(total))

    @pl.when(jnp.logical_not(is_home))
    def _():
        write_labels(lay, infos, range(lay.n_owner), 0, lay.main, 0, lab_sub, bias)
        tiles = [(other, lay.n_main, lab_sub, bias, 0, 2, None)]
        stream((mine, lay.n_main, 0), tiles, lab_lane, buffers, adder(total))


def late_pairs(lay, i_refs, j_refs, lab_sub, late_sub, lab_lane, buffers, put, back=None):
    rows, early, late = i_refs
    rows_j, early_j, late_j = j_refs
    lates = [(late_j, lay.n_late, late_sub, None, 0, 2, back)]
    stream((rows, lay.n_head, 0), lates, lab_lane, buffers, put)
    stream((early, lay.n_early, lay.n_head), lates, lab_lane, buffers, put)
    every = [(late_j, lay.n_late, late_sub, None, 0, 2, None)]
    if back is None:
        every += [(rows_j, lay.n_head, lab_sub, None, 0, 2, None)]
        every += [(early_j, lay.n_early, lab_sub, None, lay.n_head, 2, None)]
    stream((late, lay.n_late, lay.n_first), every, lab_lane, buffers, put)


def inner_late_kernel(lay, mine, early, late, rows, lab_sub, first_lane, *refs):
    sums, lab_lane, late_sub, back, buf_a, buf_b = refs

    @pl.when(lax.axis_index("cl") == lay.home)
    def _():
        late_labels(lay, lines_of(lay, mine), late_sub)
        lab_lane[:, : lay.n_first] = first_lane[...]
        turn_labels(lay, late_sub, lay.n_late, lab_lane, lay.n_first)
        refs = (rows, early, late)
        buffers = (buf_a, buf_b)
        back[...] = jnp.zeros(back.shape, jnp.float32)
        put = setter(sums)
        late_pairs(lay, refs, refs, lab_sub, late_sub, lab_lane, buffers, put, back)
        turn_sums(back, lay.n_late, sums, lay.n_first)


def cross_late_kernel(lay, other, early, late, early_j, late_j, rows, rows_j, *refs):
    lab_sub, first_lane, first_sums, lab_lane, sums = refs[:5]
    out_ref, total, late_sub, buf_a, buf_b = refs[5:]
    is_home = lax.axis_index("cl") == lay.home

    @pl.when(is_home)
    def _():
        late_labels(lay, lines_of(lay, other), late_sub)
        total[...] = sums[...]
        total[:, : lay.n_first] += first_sums[...]
        i_refs, j_refs = (rows, early, late), (rows_j, early_j, late_j)
        buffers = (buf_a, buf_b)
        late_pairs(lay, i_refs, j_refs, lab_sub, late_sub, lab_lane, buffers, adder(total))
        values = jnp.log(total[...])
        for source in range(lay.n_owner):
            start = source * lay.head
            out_ref[source, :, : lay.head] = values[:, start : start + lay.head]
        for i, source in enumerate(lay.early + lay.late):
            start = lay.n_head + i * lay.rest
            out_ref[source, :, lay.head :] = values[:, start : start + lay.rest]

    @pl.when(jnp.logical_not(is_home))
    def _():
        values = jnp.log(jnp.where(first_lane[...] >= 0, first_sums[...], 1.0))
        for source in range(lay.n_owner):
            start = source * lay.main
            out_ref[source, :, : lay.main] = values[:, start : start + lay.main]


def pair_call(kernel, lay, arrays, out_shape, scratch, out_specs=None, pairs=0):
    width = arrays[0].shape[1]
    buffer = pltpu.VMEM((lay.n_main // 2, WIDE), jnp.float32)
    return pl.pallas_call(
        functools.partial(kernel, lay),
        out_shape=out_shape,
        in_specs=list(vmem_specs(len(arrays))),
        out_specs=out_specs or vmem_specs(len(out_shape)),
        scratch_shapes=list(scratch) + [buffer, buffer],
        compiler_params=pltpu.CompilerParams(vmem_limit_bytes=FAST_LIMIT),
        cost_estimate=pl.CostEstimate(
            flops=2 * pairs * width, bytes_accessed=1, transcendentals=pairs
        ),
    )(*arrays)


def fast_unpack_kernel(values_ref, pos_ref, out_ref):
    pos = pos_ref[...]
    lane = lax.rem(pos, LANES)
    line = lax.div(pos, LANES)
    out = jnp.zeros(pos.shape, jnp.float32)
    per = values_ref.shape[2] // LANES
    for r in range(values_ref.shape[0] * per):
        start = r % per * LANES
        table = jnp.broadcast_to(values_ref[r // per, :, start : start + LANES], pos.shape)
        found = jnp.take_along_axis(table, lane, axis=1)
        out = jnp.where(line == r, found, out)
    out_ref[...] = out


def fast_unpack(values, pos):
    vmem = pl.BlockSpec(memory_space=pltpu.VMEM)
    return pl.pallas_call(
        fast_unpack_kernel,
        out_shape=jax.ShapeDtypeStruct(pos.shape, jnp.float32),
        in_specs=[vmem, vmem],
        out_specs=vmem,
    )(values, pos)


def general(embeddings, labels, owner_map):
    n_owner = lax.axis_size("cl")
    capacity = SLOTS // n_owner
    rows, width = embeddings.shape
    packed, pos, counts = pack(embeddings, labels, owner_map, n_owner, capacity)
    counts = lax.all_gather(counts, ("cl", "grp"), tiled=True)
    mine = lax.all_to_all(
        packed.reshape(n_owner, capacity, width), "cl", split_axis=0, concat_axis=0, tiled=True
    ).reshape(SLOTS, width)
    other = lax.ppermute(mine, "grp", [(0, 1), (1, 0)])
    results = log_counts(counts, mine, other, n_owner, capacity)
    returned = lax.all_to_all(
        results.reshape(n_owner, capacity), "cl", split_axis=0, concat_axis=0, tiled=True
    )
    return unpack(returned.reshape(SLOTS), pos).reshape(rows)


def body(embeddings, labels, owner_map):
    n_owner = lax.axis_size("cl")
    capacity = SLOTS // n_owner
    rows, width = embeddings.shape
    n_fine = owner_map.shape[0]
    main = -(-(rows // n_owner * 9 // 8) // 16) * 16
    if n_owner != 8 or main >= capacity or n_fine >= LANES:
        return general(embeddings, labels, owner_map)
    home = 2
    lay = Layout(n_owner, n_fine, capacity, main, home)
    packed, extra, pos = place_rows(embeddings, labels, owner_map, lay)

    def hop(x, pairs):
        partner = dict(pairs) | {target: source for source, target in pairs}
        return lax.ppermute(x, "cl", [(i, partner.get(i, i)) for i in range(n_owner)])

    def swap(x):
        return lax.ppermute(x, "grp", [(0, 1), (1, 0)])

    both = lay_out([extra, hop(extra, [(6, 4), (7, 5)])])
    early = [extra if s == home else hop(extra, [(s, home)]) for s in lay.early]
    early = lay_out(early, home)
    mine = lax.all_to_all(
        packed.reshape(n_owner, main, width), "cl", split_axis=0, concat_axis=0, tiled=True
    ).reshape(n_owner * main, width)
    mine = after(mine, early, both)
    other, early_j = swap(mine), swap(early)
    late = [hop(both, [(4, home)]), hop(both, [(5, home)])]

    def array(shape, dtype=jnp.float32):
        return jax.ShapeDtypeStruct(shape, dtype)

    def scratch(shape):
        return pltpu.VMEM(shape, jnp.float32)

    row, long_row = array((1, lay.n_first)), array((1, lay.n_all))
    side, bias = array((lay.n_first, LANES)), scratch((lay.n_main, LANES))
    heads = array((lay.n_head, width), jnp.bfloat16)
    late_side, first_side = scratch((lay.n_late, LANES)), scratch((lay.n_first, LANES))
    sums, first_lane, lab_sub, heads_i = pair_call(
        inner_kernel, lay, (mine, early), (row, row, side, heads), (bias, first_side)
    )
    specs = vmem_specs(1) + (pl.BlockSpec(memory_space=pltpu.SMEM),) + vmem_specs(2)
    sums, unfit, lab_sub_j, heads_j = pair_call(
        cross_kernel,
        lay,
        (mine, other, early, early_j, heads_i, sums, first_lane),
        (row, array((1, 1), jnp.int32), side, heads),
        (bias,),
        specs,
    )
    late = lay_out(late, home, (sums,))
    late_j = swap(late)
    late_sums, lane = pair_call(
        inner_late_kernel,
        lay,
        (mine, early, late, heads_i, lab_sub, first_lane),
        (long_row, long_row),
        (late_side, late_side),
        pairs=lay.n_late * (lay.n_all + lay.n_first),
    )
    (results,) = pair_call(
        cross_late_kernel,
        lay,
        (
            *(other, early, late, early_j, late_j, heads_i, heads_j),
            *(lab_sub_j, first_lane, sums, lane, late_sums),
        ),
        (array((n_owner, 1, capacity)),),
        (scratch(long_row.shape), late_side),
    )
    returned = lax.all_to_all(results, "cl", split_axis=0, concat_axis=0, tiled=True)
    return lax.cond(
        unfit[0, 0] == 0,
        lambda: fast_unpack(returned, pos).reshape(rows),
        lambda: general(embeddings, labels, owner_map),
    )


def solution(mesh):
    return jax.shard_map(
        body,
        mesh=mesh,
        in_specs=(P(("parts", "cl", "grp"), None), P(("parts", "cl", "grp")), P("parts")),
        out_specs=P(("parts", "cl", "grp")),
        check_vma=False,
    )
```

```python
import functools
import math

import jax
import jax.numpy as jnp
from jax import lax
from jax.experimental import pallas as pl
from jax.experimental.pallas import tpu as pltpu
from jax.sharding import PartitionSpec as P

SLOTS = 2048

temper = 0.2
neighbour_factor = 0.5
epsilon = 1e-06

LANES = 128
SCALE = math.log2(math.e) / temper
NEIGHBOUR = math.log2(neighbour_factor)
DEAD = -1e30
VMEM_LIMIT = 48 * 1024 * 1024
FAST_LIMIT = 16 * 1024 * 1024
WIDE = 512
INFO = 16


def column_of(row):
    pieces = []
    for start in range(0, row.shape[1], LANES):
        width = min(LANES, row.shape[1] - start)
        shape = (width, width)
        diagonal = lax.broadcasted_iota(jnp.int32, shape, 0) == lax.broadcasted_iota(
            jnp.int32, shape, 1
        )
        piece = jnp.broadcast_to(row[:, start : start + width], shape)
        pieces.append(jnp.sum(jnp.where(diagonal, piece, 0.0), axis=1, keepdims=True))
    return jnp.concatenate(pieces, axis=0)


def row_of(column):
    n = column.shape[0]
    diagonal = lax.broadcasted_iota(jnp.int32, (n, n), 0) == lax.broadcasted_iota(
        jnp.int32, (n, n), 1
    )
    return jnp.sum(jnp.where(diagonal, column, 0.0), axis=0, keepdims=True)


def pack_kernel(n_owner, capacity, x_ref, lab_ref, map_ref, out_ref, pos_ref, cnt_ref, unit, pos_row):
    rows = x_ref.shape[0]
    n_fine = map_ref.shape[1]
    per_owner = n_fine // n_owner
    owner_row = map_ref[...].astype(jnp.float32)
    fine_row = lax.broadcasted_iota(jnp.int32, (1, n_fine), 1).astype(jnp.float32)
    key_row = owner_row * n_fine + fine_row
    key_col = column_of(key_row)
    sorted_col = jnp.sum(jnp.where(key_row < key_col, 1.0, 0.0), axis=1, keepdims=True)
    lab = lab_ref[...].astype(jnp.float32)
    lab_row = jnp.concatenate([lab[b : b + 1, :] for b in range(lab.shape[0])], axis=1)
    fine_col = lax.broadcasted_iota(jnp.int32, (n_fine, rows), 0).astype(jnp.float32)
    fine_id = jnp.sum(jnp.where(fine_col == lab_row, sorted_col, 0.0), axis=0, keepdims=True)
    counts_col = jnp.sum(jnp.where(fine_col == fine_id, 1.0, 0.0), axis=1, keepdims=True)
    cnt_ref[...] = row_of(counts_col).astype(jnp.int32)
    coarse = jnp.floor((fine_id + 0.5) * (1.0 / per_owner))
    before = jnp.sum(
        jnp.where(fine_col < coarse * per_owner, counts_col, 0.0), axis=0, keepdims=True
    )
    index = lax.broadcasted_iota(jnp.int32, (1, rows), 1).astype(jnp.float32)
    row_key = fine_id * rows + index
    rank = jnp.zeros((1, rows), jnp.float32)
    for start in range(0, rows, LANES):
        other = column_of(row_key[:, start : start + LANES])
        rank = rank + jnp.sum(jnp.where(other < row_key, 1.0, 0.0), axis=0, keepdims=True)
    pos = (coarse * capacity + rank - before).astype(jnp.int32)
    pos_row[...] = pos
    pos_ref[...] = jnp.concatenate(
        [pos[:, start : start + LANES] for start in range(0, rows, LANES)], axis=0
    )
    x = x_ref[...].astype(jnp.float32)
    squares = jnp.sum(x * x, axis=1, keepdims=True)
    unit[...] = (x * lax.rsqrt(squares + epsilon)).astype(jnp.bfloat16)

    step = 256

    @pl.loop(0, out_ref.shape[0] // step)
    def _(block):
        slot = lax.broadcasted_iota(jnp.int32, (step, rows), 0) + block * step
        chosen = jnp.where(slot == pos_row[...], 1.0, 0.0).astype(jnp.bfloat16)
        packed = jnp.dot(chosen, unit[...], preferred_element_type=jnp.float32)
        out_ref[pl.ds(pl.multiple_of(block * step, step), step), :] = packed.astype(jnp.bfloat16)


def pack(embeddings, labels, owner_map, n_owner, capacity):
    rows, width = embeddings.shape
    n_fine = owner_map.shape[0]
    total = n_owner * capacity
    vmem = pl.BlockSpec(memory_space=pltpu.VMEM)
    return pl.pallas_call(
        functools.partial(pack_kernel, n_owner, capacity),
        out_shape=(
            jax.ShapeDtypeStruct((total, width), jnp.bfloat16),
            jax.ShapeDtypeStruct((rows // LANES, LANES), jnp.int32),
            jax.ShapeDtypeStruct((1, n_fine), jnp.int32),
        ),
        in_specs=[vmem] * 3,
        out_specs=(vmem, vmem, vmem),
        scratch_shapes=[pltpu.VMEM((rows, width), jnp.bfloat16), pltpu.VMEM((1, rows), jnp.int32)],
        compiler_params=pltpu.CompilerParams(vmem_limit_bytes=VMEM_LIMIT),
    )(embeddings, labels.reshape(rows // LANES, LANES), owner_map.reshape(1, n_fine))


def counts_kernel(n_owner, capacity, cnt_ref, mine_ref, other_ref, out_ref, lab_lane, lab_sub, bias):
    total = mine_ref.shape[0]
    per_owner = cnt_ref.shape[1] // n_owner
    me = lax.axis_index("cl")
    grp = lax.axis_index("grp")
    n_grp = lax.axis_size("grp")
    for member in range(2):
        for source in range(n_owner):
            line = source * n_grp + lax.rem(grp + member, n_grp)
            edges = []
            edge = jnp.int32(0)
            for f in range(per_owner):
                edge = edge + cnt_ref[line, me * per_owner + f]
                edges.append(edge)
            down = lax.broadcasted_iota(jnp.int32, (capacity, LANES), 0)
            label = jnp.zeros((capacity, LANES), jnp.int32)
            for edge in edges:
                label = label + jnp.where(down >= edge, 1, 0)
            start = (member * n_owner + source) * capacity
            lab_sub[start : start + capacity, :] = label
            bias[start : start + capacity, :] = jnp.where(
                label < per_owner, NEIGHBOUR - SCALE, DEAD
            )
            if member == 0:
                across = lax.broadcasted_iota(jnp.int32, (1, capacity), 1)
                label = jnp.zeros((1, capacity), jnp.int32)
                for edge in edges:
                    label = label + jnp.where(across >= edge, 1, 0)
                lab_lane[:, source * capacity : (source + 1) * capacity] = jnp.where(
                    label < per_owner, label, -1
                )
    wide, deep = min(512, total), min(256, total)

    @pl.loop(0, total // wide)
    def _(block):
        columns = pl.ds(pl.multiple_of(block * wide, wide), wide)
        rows_i = mine_ref[columns, :]
        label_i = lab_lane[:, columns]

        def add(ref, offset):
            def step(j, acc):
                start = pl.multiple_of(j * deep, deep)
                scores = lax.dot_general(
                    ref[pl.ds(start, deep), :],
                    rows_i,
                    (((1,), (1,)), ((), ())),
                    preferred_element_type=jnp.float32,
                )
                place = pl.ds(pl.multiple_of(start + offset, deep), deep)
                label_j = lab_sub[place, :]
                bias_j = bias[place, :]
                repeat = wide // LANES
                label_j = jnp.concatenate([label_j] * repeat, axis=1)
                bias_j = jnp.concatenate([bias_j] * repeat, axis=1)
                shift = jnp.where(label_j == label_i, -SCALE, bias_j)
                terms = jnp.exp2(scores * SCALE + shift)
                return acc + jnp.sum(terms.reshape(deep // 8, 8, wide), axis=0)

            return step

        acc = jnp.zeros((8, wide), jnp.float32)
        acc = lax.fori_loop(0, total // deep, add(mine_ref, 0), acc, unroll=2)
        acc = lax.fori_loop(0, total // deep, add(other_ref, total), acc, unroll=2)
        totals = jnp.sum(acc, axis=0, keepdims=True)
        out_ref[:, columns] = jnp.log(jnp.where(label_i >= 0, totals, 1.0))


def log_counts(counts, mine, other, n_owner, capacity):
    total = mine.shape[0]
    vmem = pl.BlockSpec(memory_space=pltpu.VMEM)
    return pl.pallas_call(
        functools.partial(counts_kernel, n_owner, capacity),
        out_shape=jax.ShapeDtypeStruct((1, total), jnp.float32),
        in_specs=[pl.BlockSpec(memory_space=pltpu.SMEM), vmem, vmem],
        out_specs=vmem,
        scratch_shapes=[
            pltpu.VMEM((1, total), jnp.int32),
            pltpu.VMEM((2 * total, LANES), jnp.int32),
            pltpu.VMEM((2 * total, LANES), jnp.float32),
        ],
        compiler_params=pltpu.CompilerParams(vmem_limit_bytes=VMEM_LIMIT),
    )(counts, mine, other)


def unpack_kernel(values_ref, pos_ref, out_ref):
    pos = pos_ref[...]
    lane = lax.rem(pos, LANES)
    line = lax.div(pos, LANES)
    out = jnp.zeros(pos.shape, jnp.float32)
    for r in range(values_ref.shape[0]):
        table = jnp.broadcast_to(values_ref[r : r + 1, :], pos.shape)
        found = jnp.take_along_axis(table, lane, axis=1)
        out = jnp.where(line == r, found, out)
    out_ref[...] = out


def unpack(values, pos):
    vmem = pl.BlockSpec(memory_space=pltpu.VMEM)
    return pl.pallas_call(
        unpack_kernel,
        out_shape=jax.ShapeDtypeStruct(pos.shape, jnp.float32),
        in_specs=[vmem, vmem],
        out_specs=vmem,
    )(values.reshape(-1, LANES), pos)


def swapped(x, first, second):
    return jnp.where(x == first, second, jnp.where(x == second, first, x))


def place_kernel(lay, x_hbm, lab_hbm, map_hbm, *refs):
    main_hbm, tail_ref, pos_ref, x_ref, lab_ref, map_ref, unit, main_ref, sems = refs
    n_owner, capacity, main, home = lay.n_owner, lay.capacity, lay.main, lay.home
    copies = [
        pltpu.make_async_copy(src, dst, sems.at[i])
        for i, (src, dst) in enumerate(((x_hbm, x_ref), (lab_hbm, lab_ref), (map_hbm, map_ref)))
    ]
    for copy in copies:
        copy.start()
    rows, width = x_ref.shape
    n_fine = map_ref.shape[1]
    per_owner = n_fine // n_owner
    copies[1].wait()
    copies[2].wait()
    owner_row = map_ref[...].astype(jnp.float32)
    fine_row = lax.broadcasted_iota(jnp.int32, (1, n_fine), 1).astype(jnp.float32)
    key_row = owner_row * n_fine + fine_row
    key_col = column_of(key_row)
    sorted_col = jnp.sum(jnp.where(key_row < key_col, 1.0, 0.0), axis=1, keepdims=True)
    lab = lab_ref[...].astype(jnp.float32)
    lab_row = jnp.concatenate([lab[b : b + 1, :] for b in range(lab.shape[0])], axis=1)
    fine_col = lax.broadcasted_iota(jnp.int32, (n_fine, rows), 0).astype(jnp.float32)
    fine_id = jnp.sum(jnp.where(fine_col == lab_row, sorted_col, 0.0), axis=0, keepdims=True)
    counts_col = jnp.sum(jnp.where(fine_col == fine_id, 1.0, 0.0), axis=1, keepdims=True)
    coarse = jnp.floor((fine_id + 0.5) * (1.0 / per_owner))
    first = coarse * per_owner
    before = jnp.sum(jnp.where(fine_col < first, counts_col, 0.0), axis=0, keepdims=True)
    upto = jnp.sum(jnp.where(fine_col < first + per_owner, counts_col, 0.0), axis=0, keepdims=True)
    full = jnp.min(
        jnp.where(upto - before == capacity, coarse, float(n_owner)), axis=1, keepdims=True
    )
    line = lax.broadcasted_iota(jnp.int32, (n_fine, LANES), 0)
    lane = lax.broadcasted_iota(jnp.int32, (n_fine, LANES), 1)
    inside = (line <= lane) & (lax.div(line, per_owner) == lax.div(lane, per_owner))
    running = jnp.sum(jnp.where(inside, counts_col, 0.0), axis=0, keepdims=True)
    info = jnp.where(lane[:1] < n_fine, running, full)
    index = lax.broadcasted_iota(jnp.int32, (1, rows), 1).astype(jnp.float32)
    row_key = fine_id * rows + index
    rank = jnp.zeros((1, rows), jnp.float32)
    for start in range(0, rows, LANES):
        other = column_of(row_key[:, start : start + LANES])
        rank = rank + jnp.sum(jnp.where(other < row_key, 1.0, 0.0), axis=0, keepdims=True)
    rank = (rank - before).astype(jnp.int32)
    place = swapped(coarse.astype(jnp.int32), full.astype(jnp.int32), home)
    table = place * capacity + rank
    pos_ref[...] = jnp.concatenate(
        [table[:, start : start + LANES] for start in range(0, rows, LANES)], axis=0
    )
    fits = rank < jnp.where(place == home, lay.head, main - 1)
    slot = jnp.where(fits, place * main + rank, -1)
    tail_slot = jnp.where(place == home, rank - lay.head, -1)
    copies[0].wait()
    x = x_ref[...].astype(jnp.float32)
    squares = jnp.sum(x * x, axis=1, keepdims=True)
    unit[...] = (x * lax.rsqrt(squares + epsilon)).astype(jnp.bfloat16)

    def chosen_rows(slot, start, count):
        here = lax.broadcasted_iota(jnp.int32, (count, rows), 0) + start
        chosen = jnp.where(here == slot, 1.0, 0.0).astype(jnp.bfloat16)
        return jnp.dot(chosen, unit[...], preferred_element_type=jnp.float32)

    count = 2 * main
    down = lax.broadcasted_iota(jnp.int32, (count, LANES), 0)
    is_info = lax.rem(down, main) == main - 1
    writes = []
    for i, start in enumerate(range(0, lay.n_main, count)):
        packed = chosen_rows(slot, start, count)
        place = slice(start, start + count)
        main_ref[place, LANES:] = packed[:, LANES:].astype(jnp.bfloat16)
        main_ref[place, :LANES] = jnp.where(is_info, info, packed[:, :LANES]).astype(jnp.bfloat16)
        writes.append(
            pltpu.make_async_copy(
                main_ref.at[pl.ds(start, count)], main_hbm.at[pl.ds(start, count)], sems.at[3 + i]
            )
        )
        writes[-1].start()
    tail_ref[...] = chosen_rows(tail_slot, 0, lay.rest).astype(jnp.bfloat16)
    for write in writes:
        write.wait()


def vmem_specs(count):
    return (pl.BlockSpec(memory_space=pltpu.VMEM),) * count


def place_rows(embeddings, labels, owner_map, lay):
    rows, width = embeddings.shape
    n_fine = owner_map.shape[0]
    lab_shape = (rows // LANES, LANES)
    anywhere = pl.BlockSpec(memory_space=pl.ANY)
    return pl.pallas_call(
        functools.partial(place_kernel, lay),
        out_shape=(
            jax.ShapeDtypeStruct((lay.n_main, width), jnp.bfloat16),
            jax.ShapeDtypeStruct((lay.rest, width), jnp.bfloat16),
            jax.ShapeDtypeStruct(lab_shape, jnp.int32),
        ),
        in_specs=[anywhere] * 3,
        out_specs=(anywhere,) + vmem_specs(2),
        scratch_shapes=[
            pltpu.VMEM((rows, width), jnp.bfloat16),
            pltpu.VMEM(lab_shape, jnp.int32),
            pltpu.VMEM((1, n_fine), jnp.int32),
            pltpu.VMEM((rows, width), jnp.bfloat16),
            pltpu.VMEM((lay.n_main, width), jnp.bfloat16),
            pltpu.SemaphoreType.DMA((3 + lay.n_owner // 2,)),
        ],
        compiler_params=pltpu.CompilerParams(vmem_limit_bytes=FAST_LIMIT),
    )(embeddings, labels.reshape(lab_shape), owner_map.reshape(1, n_fine))


def gate_kernel(*refs):
    pass


def after(rows, *there):
    return pl.pallas_call(
        gate_kernel,
        out_shape=jax.ShapeDtypeStruct(rows.shape, rows.dtype),
        in_specs=list(vmem_specs(1 + len(there))),
        out_specs=vmem_specs(1)[0],
        input_output_aliases={0: 0},
        compiler_params=pltpu.CompilerParams(vmem_limit_bytes=FAST_LIMIT),
    )(rows, *there)


def lay_out_kernel(n_arrays, home, *refs):
    chunks, out = refs[:n_arrays], refs[-1]

    def copy():
        start = 0
        for chunk in chunks:
            out[start : start + chunk.shape[0], :] = chunk[...]
            start += chunk.shape[0]

    if home is None:
        copy()
    else:
        pl.when(lax.axis_index("cl") == home)(copy)


def lay_out(chunks, home=None, waits=()):
    rows, width = sum(x.shape[0] for x in chunks), chunks[0].shape[1]
    return pl.pallas_call(
        functools.partial(lay_out_kernel, len(chunks), home),
        out_shape=jax.ShapeDtypeStruct((rows, width), jnp.bfloat16),
        in_specs=list(vmem_specs(len(chunks) + len(waits))),
        out_specs=vmem_specs(1)[0],
        compiler_params=pltpu.CompilerParams(vmem_limit_bytes=FAST_LIMIT),
    )(*chunks, *waits)


class Layout:
    early, late = (0, 1, 2, 3), (4, 6, 5, 7)

    def __init__(self, n_owner, n_fine, capacity, main, home):
        self.n_owner, self.n_fine, self.capacity = n_owner, n_fine, capacity
        self.main, self.home = main, home
        self.head = main - INFO
        self.rest = capacity - self.head
        self.per_owner = n_fine // n_owner
        self.n_main = n_owner * main
        self.n_head = n_owner * self.head
        self.n_early = len(self.early) * self.rest
        self.n_late = len(self.late) * self.rest
        self.n_first = self.n_head + self.n_early
        self.n_all = self.n_first + self.n_late


def info_line(lay, main_ref, source):
    end = (source + 1) * lay.main
    return main_ref[end - INFO : end, :LANES].astype(jnp.float32)[INFO - 1 :]


def lines_of(lay, main_ref):
    return [info_line(lay, main_ref, source) for source in range(lay.n_owner)]


def hot_of(lay, info):
    lane = lax.broadcasted_iota(jnp.int32, (1, LANES), 1)
    hot = jnp.max(jnp.where(lane == lay.n_fine, info, 0.0), axis=1, keepdims=True)
    return hot.astype(jnp.int32)


def write_labels(lay, infos, sources, first, count, at, lab_sub, bias):
    cluster = swapped(lax.axis_index("cl"), hot_of(lay, infos[0]), lay.home)
    lane = lax.broadcasted_iota(jnp.int32, (1, LANES), 1)
    is_edge = lax.div(lane, lay.per_owner) == cluster
    for i, source in enumerate(sources):
        edges = jnp.where(is_edge, infos[source], 2.0 * lay.capacity)
        slot = lax.broadcasted_iota(jnp.int32, (count, LANES), 0) + first
        label = jnp.where(slot.astype(jnp.float32) >= edges, 1.0, 0.0)
        label = jnp.broadcast_to(jnp.sum(label, axis=1, keepdims=True), (count, LANES))
        start = at + i * count
        lab_sub[start : start + count, :] = label
        if bias is not None:
            bias[start : start + count, :] = jnp.where(
                label < lay.per_owner, NEIGHBOUR - SCALE, DEAD
            )


def first_labels(lay, infos, lab_sub):
    write_labels(lay, infos, range(lay.n_owner), 0, lay.head, 0, lab_sub, None)
    write_labels(lay, infos, lay.early, lay.head, lay.rest, lay.n_head, lab_sub, None)


def late_labels(lay, infos, lab_sub):
    write_labels(lay, infos, lay.late, lay.head, lay.rest, 0, lab_sub, None)


def turn_labels(lay, lab_sub, count, lab_lane, at):
    for i in range(0, count, LANES):
        block = jnp.transpose(lab_sub[i : i + LANES, :])[:1]
        lab_lane[:, at + i : at + i + LANES] = jnp.where(block < lay.per_owner, block, -1.0)


def copy_head(lay, main_ref, rows):
    for source in range(lay.n_owner):
        rows[source * lay.head : (source + 1) * lay.head, :] = main_ref[
            source * lay.main : source * lay.main + lay.head, :
        ]


def pieces(count, parts):
    return [(i * (count // parts), count // parts) for i in range(parts)]


def stream(lanes, tiles, lab_lane, buffers, put):
    rows_i, count, at = lanes
    step = 32
    tiles = [
        (ref, s, d, lab_sub, bias, line + s, back)
        for ref, n, lab_sub, bias, line, parts, back in tiles
        for s, d in pieces(n, parts)
    ]

    def scores_to(buffer, tile, rows):
        ref, start, deep = tile[:3]
        buffer[:deep, : rows.shape[0]] = lax.dot_general(
            ref[start : start + deep, :],
            rows,
            (((1,), (1,)), ((), ())),
            preferred_element_type=jnp.float32,
        )

    def run(start, blocks, wide):
        repeat = wide // LANES

        def rows_of(block):
            return rows_i[pl.ds(pl.multiple_of(start + block * wide, LANES), wide), :]

        scores_to(buffers[0], tiles[0], rows_of(0))

        def one_block(block):
            here = rows_of(block)
            place = pl.ds(pl.multiple_of(at + start + block * wide, LANES), wide)
            label_i = lab_lane[:, place]
            acc = jnp.zeros((8, wide), jnp.float32)
            for i, (_, _, deep, lab_sub, bias, line, back) in enumerate(tiles):
                if i + 1 < len(tiles):
                    scores_to(buffers[(i + 1) % 2], tiles[i + 1], here)
                elif blocks > 1:

                    @pl.when(block + 1 < blocks)
                    def _():
                        scores_to(buffers[0], tiles[0], rows_of(block + 1))

                buffer = buffers[i % 2]
                for c in range(0, deep, step):
                    part = slice(line + c, line + c + step)
                    label_j = jnp.concatenate([lab_sub[part, :]] * repeat, axis=1)
                    if bias is None:
                        bias_j = NEIGHBOUR - SCALE
                    else:
                        bias_j = jnp.concatenate([bias[part, :]] * repeat, axis=1)
                    shift = jnp.where(label_j == label_i, -SCALE, bias_j)
                    terms = jnp.exp2(buffer[c : c + step, :wide] * SCALE + shift)
                    acc = acc + jnp.sum(terms.reshape(step // 8, 8, wide), axis=0)
                    if back is not None:
                        across = terms[:, :LANES]
                        for r in range(1, repeat):
                            across = across + terms[:, r * LANES : (r + 1) * LANES]
                        back[part, :] += across
            put(place, jnp.sum(acc, axis=0, keepdims=True))

        if blocks == 1:
            one_block(0)
        else:
            pl.loop(0, blocks)(one_block)

    if count >= WIDE:
        run(0, count // WIDE, WIDE)
    if count % WIDE:
        run(count - count % WIDE, 1, count % WIDE)


def turn_sums(back, count, sums, at):
    for i in range(0, count, LANES):
        block = jnp.transpose(back[i : i + LANES, :])
        sums[:, at + i : at + i + LANES] += jnp.sum(block, axis=0, keepdims=True)


def setter(ref):
    def put(place, values):
        ref[:, place] = values

    return put


def adder(ref):
    def put(place, values):
        ref[:, place] += values

    return put


def inner_kernel(lay, mine, early, sums, lab_lane, lab_sub, rows, bias, back, buf_a, buf_b):
    is_home = lax.axis_index("cl") == lay.home
    infos = lines_of(lay, mine)
    buffers = (buf_a, buf_b)

    @pl.when(is_home)
    def _():
        copy_head(lay, mine, rows)
        first_labels(lay, infos, lab_sub)
        turn_labels(lay, lab_sub, lay.n_first, lab_lane, 0)
        back[...] = jnp.zeros(back.shape, jnp.float32)
        size = lay.n_early
        blocks = [(rows.at[pl.ds(start, size)], start) for start in range(0, lay.n_head, size)]
        blocks.append((early, lay.n_head))
        for i, (ref, at) in enumerate(blocks):
            tiles = [
                (ref_j, size, lab_sub, None, at_j, 2, None if at_j == at else back)
                for ref_j, at_j in blocks[i:]
            ]
            stream((ref, size, at), tiles, lab_lane, buffers, setter(sums))
        turn_sums(back, lay.n_first, sums, 0)

    @pl.when(jnp.logical_not(is_home))
    def _():
        write_labels(lay, infos, range(lay.n_owner), 0, lay.main, 0, lab_sub, bias)
        turn_labels(lay, lab_sub, lay.n_main, lab_lane, 0)
        tiles = [(mine, lay.n_main, lab_sub, bias, 0, 2, None)]
        stream((mine, lay.n_main, 0), tiles, lab_lane, buffers, setter(sums))


def cross_kernel(lay, mine, other, early, early_j, rows, sums, lab_lane, *refs):
    total, unfit_ref, lab_sub, rows_j, bias, buf_a, buf_b = refs
    is_home = lax.axis_index("cl") == lay.home
    infos = lines_of(lay, other)
    own = lines_of(lay, mine)
    hot = hot_of(lay, own[0])
    lane = lax.broadcasted_iota(jnp.int32, (1, LANES), 1)
    last = (lane < lay.n_fine) & (lax.rem(lane, lay.per_owner) == lay.per_owner - 1)
    last = last & (lax.div(lane, lay.per_owner) != hot)
    unfit = jnp.zeros((1, LANES), jnp.float32)
    for info in infos + own:
        wrong = last & (info >= lay.main)
        differs = (info != hot.astype(jnp.float32)) | (info >= lay.n_owner)
        wrong = wrong | ((lane == lay.n_fine) & differs)
        unfit = unfit + jnp.where(wrong, 1.0, 0.0)
    unfit_ref[0, 0] = jnp.max(unfit).astype(jnp.int32)
    total[...] = sums[...]
    buffers = (buf_a, buf_b)

    @pl.when(is_home)
    def _():
        copy_head(lay, other, rows_j)
        first_labels(lay, infos, lab_sub)
        tiles = [(rows_j, lay.n_head, lab_sub, None, 0, 2, None)]
        tiles += [(early_j, lay.n_early, lab_sub, None, lay.n_head, 2, None)]
        stream((rows, lay.n_head, 0), tiles, lab_lane, buffers, adder(total))
        stream((early, lay.n_early, lay.n_head), tiles, lab_lane, buffers, adder(total))

    @pl.when(jnp.logical_not(is_home))
    def _():
        write_labels(lay, infos, range(lay.n_owner), 0, lay.main, 0, lab_sub, bias)
        tiles = [(other, lay.n_main, lab_sub, bias, 0, 2, None)]
        stream((mine, lay.n_main, 0), tiles, lab_lane, buffers, adder(total))


def late_pairs(lay, i_refs, j_refs, lab_sub, late_sub, lab_lane, buffers, put, back=None):
    rows, early, late = i_refs
    rows_j, early_j, late_j = j_refs
    lates = [(late_j, lay.n_late, late_sub, None, 0, 2, back)]
    stream((rows, lay.n_head, 0), lates, lab_lane, buffers, put)
    stream((early, lay.n_early, lay.n_head), lates, lab_lane, buffers, put)
    every = [(late_j, lay.n_late, late_sub, None, 0, 2, None)]
    if back is None:
        every += [(rows_j, lay.n_head, lab_sub, None, 0, 2, None)]
        every += [(early_j, lay.n_early, lab_sub, None, lay.n_head, 2, None)]
    stream((late, lay.n_late, lay.n_first), every, lab_lane, buffers, put)


def inner_late_kernel(lay, mine, early, late, rows, lab_sub, first_lane, *refs):
    sums, lab_lane, late_sub, back, buf_a, buf_b = refs

    @pl.when(lax.axis_index("cl") == lay.home)
    def _():
        late_labels(lay, lines_of(lay, mine), late_sub)
        lab_lane[:, : lay.n_first] = first_lane[...]
        turn_labels(lay, late_sub, lay.n_late, lab_lane, lay.n_first)
        refs = (rows, early, late)
        buffers = (buf_a, buf_b)
        back[...] = jnp.zeros(back.shape, jnp.float32)
        put = setter(sums)
        late_pairs(lay, refs, refs, lab_sub, late_sub, lab_lane, buffers, put, back)
        turn_sums(back, lay.n_late, sums, lay.n_first)


def cross_late_kernel(lay, other, early, late, early_j, late_j, rows, rows_j, *refs):
    lab_sub, first_lane, first_sums, lab_lane, sums = refs[:5]
    out_ref, total, late_sub, buf_a, buf_b = refs[5:]
    is_home = lax.axis_index("cl") == lay.home

    @pl.when(is_home)
    def _():
        late_labels(lay, lines_of(lay, other), late_sub)
        total[...] = sums[...]
        total[:, : lay.n_first] += first_sums[...]
        i_refs, j_refs = (rows, early, late), (rows_j, early_j, late_j)
        buffers = (buf_a, buf_b)
        late_pairs(lay, i_refs, j_refs, lab_sub, late_sub, lab_lane, buffers, adder(total))
        values = jnp.log(total[...])
        for source in range(lay.n_owner):
            start = source * lay.head
            out_ref[source, :, : lay.head] = values[:, start : start + lay.head]
        for i, source in enumerate(lay.early + lay.late):
            start = lay.n_head + i * lay.rest
            out_ref[source, :, lay.head :] = values[:, start : start + lay.rest]

    @pl.when(jnp.logical_not(is_home))
    def _():
        values = jnp.log(jnp.where(first_lane[...] >= 0, first_sums[...], 1.0))
        for source in range(lay.n_owner):
            start = source * lay.main
            out_ref[source, :, : lay.main] = values[:, start : start + lay.main]


def pair_call(kernel, lay, arrays, out_shape, scratch, out_specs=None, pairs=0):
    width = arrays[0].shape[1]
    buffer = pltpu.VMEM((lay.n_main // 2, WIDE), jnp.float32)
    return pl.pallas_call(
        functools.partial(kernel, lay),
        out_shape=out_shape,
        in_specs=list(vmem_specs(len(arrays))),
        out_specs=out_specs or vmem_specs(len(out_shape)),
        scratch_shapes=list(scratch) + [buffer, buffer],
        compiler_params=pltpu.CompilerParams(vmem_limit_bytes=FAST_LIMIT),
        cost_estimate=pl.CostEstimate(
            flops=2 * pairs * width, bytes_accessed=1, transcendentals=pairs
        ),
    )(*arrays)


def fast_unpack_kernel(values_ref, pos_ref, out_ref):
    pos = pos_ref[...]
    lane = lax.rem(pos, LANES)
    line = lax.div(pos, LANES)
    out = jnp.zeros(pos.shape, jnp.float32)
    per = values_ref.shape[2] // LANES
    for r in range(values_ref.shape[0] * per):
        start = r % per * LANES
        table = jnp.broadcast_to(values_ref[r // per, :, start : start + LANES], pos.shape)
        found = jnp.take_along_axis(table, lane, axis=1)
        out = jnp.where(line == r, found, out)
    out_ref[...] = out


def fast_unpack(values, pos):
    vmem = pl.BlockSpec(memory_space=pltpu.VMEM)
    return pl.pallas_call(
        fast_unpack_kernel,
        out_shape=jax.ShapeDtypeStruct(pos.shape, jnp.float32),
        in_specs=[vmem, vmem],
        out_specs=vmem,
    )(values, pos)


def general(embeddings, labels, owner_map):
    n_owner = lax.axis_size("cl")
    capacity = SLOTS // n_owner
    rows, width = embeddings.shape
    packed, pos, counts = pack(embeddings, labels, owner_map, n_owner, capacity)
    counts = lax.all_gather(counts, ("cl", "grp"), tiled=True)
    mine = lax.all_to_all(
        packed.reshape(n_owner, capacity, width), "cl", split_axis=0, concat_axis=0, tiled=True
    ).reshape(SLOTS, width)
    other = lax.ppermute(mine, "grp", [(0, 1), (1, 0)])
    results = log_counts(counts, mine, other, n_owner, capacity)
    returned = lax.all_to_all(
        results.reshape(n_owner, capacity), "cl", split_axis=0, concat_axis=0, tiled=True
    )
    return unpack(returned.reshape(SLOTS), pos).reshape(rows)


def body(embeddings, labels, owner_map):
    n_owner = lax.axis_size("cl")
    capacity = SLOTS // n_owner
    rows, width = embeddings.shape
    n_fine = owner_map.shape[0]
    main = -(-(rows // n_owner * 9 // 8) // 16) * 16
    if n_owner != 8 or main >= capacity or n_fine >= LANES:
        return general(embeddings, labels, owner_map)
    home = 2
    lay = Layout(n_owner, n_fine, capacity, main, home)
    packed, extra, pos = place_rows(embeddings, labels, owner_map, lay)

    def hop(x, pairs):
        return lax.ppermute(x, "cl", pairs)

    def swap(x):
        return lax.ppermute(x, "grp", [(0, 1), (1, 0)])

    moved = hop(extra, [(6, 4), (7, 5)])
    early = [extra if s == home else hop(extra, [(s, home)]) for s in lay.early]
    early = lay_out(early, home)
    mine = lax.all_to_all(
        packed.reshape(n_owner, main, width), "cl", split_axis=0, concat_axis=0, tiled=True
    ).reshape(n_owner * main, width)
    mine = after(mine, early, moved)
    other, early_j = swap(mine), swap(early)
    late = [hop(x, [(s, home)]) for s in (4, 5) for x in (extra, moved)]

    def array(shape, dtype=jnp.float32):
        return jax.ShapeDtypeStruct(shape, dtype)

    def scratch(shape):
        return pltpu.VMEM(shape, jnp.float32)

    row, long_row = array((1, lay.n_first)), array((1, lay.n_all))
    side, bias = array((lay.n_first, LANES)), scratch((lay.n_main, LANES))
    heads = array((lay.n_head, width), jnp.bfloat16)
    late_side, first_side = scratch((lay.n_late, LANES)), scratch((lay.n_first, LANES))
    sums, first_lane, lab_sub, heads_i = pair_call(
        inner_kernel, lay, (mine, early), (row, row, side, heads), (bias, first_side)
    )
    specs = vmem_specs(1) + (pl.BlockSpec(memory_space=pltpu.SMEM),) + vmem_specs(2)
    sums, unfit, lab_sub_j, heads_j = pair_call(
        cross_kernel,
        lay,
        (mine, other, early, early_j, heads_i, sums, first_lane),
        (row, array((1, 1), jnp.int32), side, heads),
        (bias,),
        specs,
    )
    late = lay_out(late, home, (sums,))
    late_j = swap(late)
    late_sums, lane = pair_call(
        inner_late_kernel,
        lay,
        (mine, early, late, heads_i, lab_sub, first_lane),
        (long_row, long_row),
        (late_side, late_side),
        pairs=lay.n_late * (lay.n_all + lay.n_first),
    )
    (results,) = pair_call(
        cross_late_kernel,
        lay,
        (
            *(other, early, late, early_j, late_j, heads_i, heads_j),
            *(lab_sub_j, first_lane, sums, lane, late_sums),
        ),
        (array((n_owner, 1, capacity)),),
        (scratch(long_row.shape), late_side),
    )
    returned = lax.all_to_all(results, "cl", split_axis=0, concat_axis=0, tiled=True)
    return lax.cond(
        unfit[0, 0] == 0,
        lambda: fast_unpack(returned, pos).reshape(rows),
        lambda: general(embeddings, labels, owner_map),
    )


def solution(mesh):
    return jax.shard_map(
        body,
        mesh=mesh,
        in_specs=(P(("parts", "cl", "grp"), None), P(("parts", "cl", "grp")), P("parts")),
        out_specs=P(("parts", "cl", "grp")),
        check_vma=False,
    )
```

```python
import functools
import math

import jax
import jax.numpy as jnp
from jax import lax
from jax.experimental import pallas as pl
from jax.experimental.pallas import tpu as pltpu
from jax.sharding import PartitionSpec as P

SLOTS = 2048

temper = 0.2
neighbour_factor = 0.5
epsilon = 1e-06

LANES = 128
SCALE = math.log2(math.e) / temper
NEIGHBOUR = math.log2(neighbour_factor)
DEAD = -1e30
VMEM_LIMIT = 48 * 1024 * 1024
FAST_LIMIT = 16 * 1024 * 1024
WIDE = 512
INFO = 16


def column_of(row):
    pieces = []
    for start in range(0, row.shape[1], LANES):
        width = min(LANES, row.shape[1] - start)
        shape = (width, width)
        diagonal = lax.broadcasted_iota(jnp.int32, shape, 0) == lax.broadcasted_iota(
            jnp.int32, shape, 1
        )
        piece = jnp.broadcast_to(row[:, start : start + width], shape)
        pieces.append(jnp.sum(jnp.where(diagonal, piece, 0.0), axis=1, keepdims=True))
    return jnp.concatenate(pieces, axis=0)


def row_of(column):
    n = column.shape[0]
    diagonal = lax.broadcasted_iota(jnp.int32, (n, n), 0) == lax.broadcasted_iota(
        jnp.int32, (n, n), 1
    )
    return jnp.sum(jnp.where(diagonal, column, 0.0), axis=0, keepdims=True)


def pack_kernel(n_owner, capacity, x_ref, lab_ref, map_ref, out_ref, pos_ref, cnt_ref, unit, pos_row):
    rows = x_ref.shape[0]
    n_fine = map_ref.shape[1]
    per_owner = n_fine // n_owner
    owner_row = map_ref[...].astype(jnp.float32)
    fine_row = lax.broadcasted_iota(jnp.int32, (1, n_fine), 1).astype(jnp.float32)
    key_row = owner_row * n_fine + fine_row
    key_col = column_of(key_row)
    sorted_col = jnp.sum(jnp.where(key_row < key_col, 1.0, 0.0), axis=1, keepdims=True)
    lab = lab_ref[...].astype(jnp.float32)
    lab_row = jnp.concatenate([lab[b : b + 1, :] for b in range(lab.shape[0])], axis=1)
    fine_col = lax.broadcasted_iota(jnp.int32, (n_fine, rows), 0).astype(jnp.float32)
    fine_id = jnp.sum(jnp.where(fine_col == lab_row, sorted_col, 0.0), axis=0, keepdims=True)
    counts_col = jnp.sum(jnp.where(fine_col == fine_id, 1.0, 0.0), axis=1, keepdims=True)
    cnt_ref[...] = row_of(counts_col).astype(jnp.int32)
    coarse = jnp.floor((fine_id + 0.5) * (1.0 / per_owner))
    before = jnp.sum(
        jnp.where(fine_col < coarse * per_owner, counts_col, 0.0), axis=0, keepdims=True
    )
    index = lax.broadcasted_iota(jnp.int32, (1, rows), 1).astype(jnp.float32)
    row_key = fine_id * rows + index
    rank = jnp.zeros((1, rows), jnp.float32)
    for start in range(0, rows, LANES):
        other = column_of(row_key[:, start : start + LANES])
        rank = rank + jnp.sum(jnp.where(other < row_key, 1.0, 0.0), axis=0, keepdims=True)
    pos = (coarse * capacity + rank - before).astype(jnp.int32)
    pos_row[...] = pos
    pos_ref[...] = jnp.concatenate(
        [pos[:, start : start + LANES] for start in range(0, rows, LANES)], axis=0
    )
    x = x_ref[...].astype(jnp.float32)
    squares = jnp.sum(x * x, axis=1, keepdims=True)
    unit[...] = (x * lax.rsqrt(squares + epsilon)).astype(jnp.bfloat16)

    step = 256

    @pl.loop(0, out_ref.shape[0] // step)
    def _(block):
        slot = lax.broadcasted_iota(jnp.int32, (step, rows), 0) + block * step
        chosen = jnp.where(slot == pos_row[...], 1.0, 0.0).astype(jnp.bfloat16)
        packed = jnp.dot(chosen, unit[...], preferred_element_type=jnp.float32)
        out_ref[pl.ds(pl.multiple_of(block * step, step), step), :] = packed.astype(jnp.bfloat16)


def pack(embeddings, labels, owner_map, n_owner, capacity):
    rows, width = embeddings.shape
    n_fine = owner_map.shape[0]
    total = n_owner * capacity
    vmem = pl.BlockSpec(memory_space=pltpu.VMEM)
    return pl.pallas_call(
        functools.partial(pack_kernel, n_owner, capacity),
        out_shape=(
            jax.ShapeDtypeStruct((total, width), jnp.bfloat16),
            jax.ShapeDtypeStruct((rows // LANES, LANES), jnp.int32),
            jax.ShapeDtypeStruct((1, n_fine), jnp.int32),
        ),
        in_specs=[vmem] * 3,
        out_specs=(vmem, vmem, vmem),
        scratch_shapes=[pltpu.VMEM((rows, width), jnp.bfloat16), pltpu.VMEM((1, rows), jnp.int32)],
        compiler_params=pltpu.CompilerParams(vmem_limit_bytes=VMEM_LIMIT),
    )(embeddings, labels.reshape(rows // LANES, LANES), owner_map.reshape(1, n_fine))


def counts_kernel(n_owner, capacity, cnt_ref, mine_ref, other_ref, out_ref, lab_lane, lab_sub, bias):
    total = mine_ref.shape[0]
    per_owner = cnt_ref.shape[1] // n_owner
    me = lax.axis_index("cl")
    grp = lax.axis_index("grp")
    n_grp = lax.axis_size("grp")
    for member in range(2):
        for source in range(n_owner):
            line = source * n_grp + lax.rem(grp + member, n_grp)
            edges = []
            edge = jnp.int32(0)
            for f in range(per_owner):
                edge = edge + cnt_ref[line, me * per_owner + f]
                edges.append(edge)
            down = lax.broadcasted_iota(jnp.int32, (capacity, LANES), 0)
            label = jnp.zeros((capacity, LANES), jnp.int32)
            for edge in edges:
                label = label + jnp.where(down >= edge, 1, 0)
            start = (member * n_owner + source) * capacity
            lab_sub[start : start + capacity, :] = label
            bias[start : start + capacity, :] = jnp.where(
                label < per_owner, NEIGHBOUR - SCALE, DEAD
            )
            if member == 0:
                across = lax.broadcasted_iota(jnp.int32, (1, capacity), 1)
                label = jnp.zeros((1, capacity), jnp.int32)
                for edge in edges:
                    label = label + jnp.where(across >= edge, 1, 0)
                lab_lane[:, source * capacity : (source + 1) * capacity] = jnp.where(
                    label < per_owner, label, -1
                )
    wide, deep = min(512, total), min(256, total)

    @pl.loop(0, total // wide)
    def _(block):
        columns = pl.ds(pl.multiple_of(block * wide, wide), wide)
        rows_i = mine_ref[columns, :]
        label_i = lab_lane[:, columns]

        def add(ref, offset):
            def step(j, acc):
                start = pl.multiple_of(j * deep, deep)
                scores = lax.dot_general(
                    ref[pl.ds(start, deep), :],
                    rows_i,
                    (((1,), (1,)), ((), ())),
                    preferred_element_type=jnp.float32,
                )
                place = pl.ds(pl.multiple_of(start + offset, deep), deep)
                label_j = lab_sub[place, :]
                bias_j = bias[place, :]
                repeat = wide // LANES
                label_j = jnp.concatenate([label_j] * repeat, axis=1)
                bias_j = jnp.concatenate([bias_j] * repeat, axis=1)
                shift = jnp.where(label_j == label_i, -SCALE, bias_j)
                terms = jnp.exp2(scores * SCALE + shift)
                return acc + jnp.sum(terms.reshape(deep // 8, 8, wide), axis=0)

            return step

        acc = jnp.zeros((8, wide), jnp.float32)
        acc = lax.fori_loop(0, total // deep, add(mine_ref, 0), acc, unroll=2)
        acc = lax.fori_loop(0, total // deep, add(other_ref, total), acc, unroll=2)
        totals = jnp.sum(acc, axis=0, keepdims=True)
        out_ref[:, columns] = jnp.log(jnp.where(label_i >= 0, totals, 1.0))


def log_counts(counts, mine, other, n_owner, capacity):
    total = mine.shape[0]
    vmem = pl.BlockSpec(memory_space=pltpu.VMEM)
    return pl.pallas_call(
        functools.partial(counts_kernel, n_owner, capacity),
        out_shape=jax.ShapeDtypeStruct((1, total), jnp.float32),
        in_specs=[pl.BlockSpec(memory_space=pltpu.SMEM), vmem, vmem],
        out_specs=vmem,
        scratch_shapes=[
            pltpu.VMEM((1, total), jnp.int32),
            pltpu.VMEM((2 * total, LANES), jnp.int32),
            pltpu.VMEM((2 * total, LANES), jnp.float32),
        ],
        compiler_params=pltpu.CompilerParams(vmem_limit_bytes=VMEM_LIMIT),
    )(counts, mine, other)


def unpack_kernel(values_ref, pos_ref, out_ref):
    pos = pos_ref[...]
    lane = lax.rem(pos, LANES)
    line = lax.div(pos, LANES)
    out = jnp.zeros(pos.shape, jnp.float32)
    for r in range(values_ref.shape[0]):
        table = jnp.broadcast_to(values_ref[r : r + 1, :], pos.shape)
        found = jnp.take_along_axis(table, lane, axis=1)
        out = jnp.where(line == r, found, out)
    out_ref[...] = out


def unpack(values, pos):
    vmem = pl.BlockSpec(memory_space=pltpu.VMEM)
    return pl.pallas_call(
        unpack_kernel,
        out_shape=jax.ShapeDtypeStruct(pos.shape, jnp.float32),
        in_specs=[vmem, vmem],
        out_specs=vmem,
    )(values.reshape(-1, LANES), pos)


def swapped(x, first, second):
    return jnp.where(x == first, second, jnp.where(x == second, first, x))


def place_kernel(lay, x_hbm, lab_hbm, map_hbm, *refs):
    main_hbm, tail_ref, pos_ref, x_ref, lab_ref, map_ref, unit, main_ref, sems = refs
    n_owner, capacity, main, home = lay.n_owner, lay.capacity, lay.main, lay.home
    copies = [
        pltpu.make_async_copy(src, dst, sems.at[i])
        for i, (src, dst) in enumerate(((x_hbm, x_ref), (lab_hbm, lab_ref), (map_hbm, map_ref)))
    ]
    for copy in copies:
        copy.start()
    rows, width = x_ref.shape
    n_fine = map_ref.shape[1]
    per_owner = n_fine // n_owner
    copies[1].wait()
    copies[2].wait()
    owner_row = map_ref[...].astype(jnp.float32)
    fine_row = lax.broadcasted_iota(jnp.int32, (1, n_fine), 1).astype(jnp.float32)
    key_row = owner_row * n_fine + fine_row
    key_col = column_of(key_row)
    sorted_col = jnp.sum(jnp.where(key_row < key_col, 1.0, 0.0), axis=1, keepdims=True)
    lab = lab_ref[...].astype(jnp.float32)
    lab_row = jnp.concatenate([lab[b : b + 1, :] for b in range(lab.shape[0])], axis=1)
    fine_col = lax.broadcasted_iota(jnp.int32, (n_fine, rows), 0).astype(jnp.float32)
    fine_id = jnp.sum(jnp.where(fine_col == lab_row, sorted_col, 0.0), axis=0, keepdims=True)
    counts_col = jnp.sum(jnp.where(fine_col == fine_id, 1.0, 0.0), axis=1, keepdims=True)
    coarse = jnp.floor((fine_id + 0.5) * (1.0 / per_owner))
    first = coarse * per_owner
    before = jnp.sum(jnp.where(fine_col < first, counts_col, 0.0), axis=0, keepdims=True)
    upto = jnp.sum(jnp.where(fine_col < first + per_owner, counts_col, 0.0), axis=0, keepdims=True)
    full = jnp.min(
        jnp.where(upto - before == capacity, coarse, float(n_owner)), axis=1, keepdims=True
    )
    line = lax.broadcasted_iota(jnp.int32, (n_fine, LANES), 0)
    lane = lax.broadcasted_iota(jnp.int32, (n_fine, LANES), 1)
    inside = (line <= lane) & (lax.div(line, per_owner) == lax.div(lane, per_owner))
    running = jnp.sum(jnp.where(inside, counts_col, 0.0), axis=0, keepdims=True)
    info = jnp.where(lane[:1] < n_fine, running, full)
    index = lax.broadcasted_iota(jnp.int32, (1, rows), 1).astype(jnp.float32)
    row_key = fine_id * rows + index
    rank = jnp.zeros((1, rows), jnp.float32)
    for start in range(0, rows, LANES):
        other = column_of(row_key[:, start : start + LANES])
        rank = rank + jnp.sum(jnp.where(other < row_key, 1.0, 0.0), axis=0, keepdims=True)
    rank = (rank - before).astype(jnp.int32)
    place = swapped(coarse.astype(jnp.int32), full.astype(jnp.int32), home)
    table = place * capacity + rank
    pos_ref[...] = jnp.concatenate(
        [table[:, start : start + LANES] for start in range(0, rows, LANES)], axis=0
    )
    fits = rank < jnp.where(place == home, lay.head, main - 1)
    slot = jnp.where(fits, place * main + rank, -1)
    tail_slot = jnp.where(place == home, rank - lay.head, -1)
    copies[0].wait()
    x = x_ref[...].astype(jnp.float32)
    squares = jnp.sum(x * x, axis=1, keepdims=True)
    unit[...] = (x * lax.rsqrt(squares + epsilon)).astype(jnp.bfloat16)

    def chosen_rows(slot, start, count):
        here = lax.broadcasted_iota(jnp.int32, (count, rows), 0) + start
        chosen = jnp.where(here == slot, 1.0, 0.0).astype(jnp.bfloat16)
        return jnp.dot(chosen, unit[...], preferred_element_type=jnp.float32)

    count = 2 * main
    down = lax.broadcasted_iota(jnp.int32, (count, LANES), 0)
    is_info = lax.rem(down, main) == main - 1
    writes = []
    for i, start in enumerate(range(0, lay.n_main, count)):
        packed = chosen_rows(slot, start, count)
        place = slice(start, start + count)
        main_ref[place, LANES:] = packed[:, LANES:].astype(jnp.bfloat16)
        main_ref[place, :LANES] = jnp.where(is_info, info, packed[:, :LANES]).astype(jnp.bfloat16)
        writes.append(
            pltpu.make_async_copy(
                main_ref.at[pl.ds(start, count)], main_hbm.at[pl.ds(start, count)], sems.at[3 + i]
            )
        )
        writes[-1].start()
    tail_ref[...] = chosen_rows(tail_slot, 0, lay.rest).astype(jnp.bfloat16)
    for write in writes:
        write.wait()


def vmem_specs(count):
    return (pl.BlockSpec(memory_space=pltpu.VMEM),) * count


def place_rows(embeddings, labels, owner_map, lay):
    rows, width = embeddings.shape
    n_fine = owner_map.shape[0]
    lab_shape = (rows // LANES, LANES)
    anywhere = pl.BlockSpec(memory_space=pl.ANY)
    return pl.pallas_call(
        functools.partial(place_kernel, lay),
        out_shape=(
            jax.ShapeDtypeStruct((lay.n_main, width), jnp.bfloat16),
            jax.ShapeDtypeStruct((lay.rest, width), jnp.bfloat16),
            jax.ShapeDtypeStruct(lab_shape, jnp.int32),
        ),
        in_specs=[anywhere] * 3,
        out_specs=(anywhere,) + vmem_specs(2),
        scratch_shapes=[
            pltpu.VMEM((rows, width), jnp.bfloat16),
            pltpu.VMEM(lab_shape, jnp.int32),
            pltpu.VMEM((1, n_fine), jnp.int32),
            pltpu.VMEM((rows, width), jnp.bfloat16),
            pltpu.VMEM((lay.n_main, width), jnp.bfloat16),
            pltpu.SemaphoreType.DMA((3 + lay.n_owner // 2,)),
        ],
        compiler_params=pltpu.CompilerParams(vmem_limit_bytes=FAST_LIMIT),
    )(embeddings, labels.reshape(lab_shape), owner_map.reshape(1, n_fine))


def gate_kernel(*refs):
    pass


def after(rows, *there):
    return pl.pallas_call(
        gate_kernel,
        out_shape=jax.ShapeDtypeStruct(rows.shape, rows.dtype),
        in_specs=list(vmem_specs(1 + len(there))),
        out_specs=vmem_specs(1)[0],
        input_output_aliases={0: 0},
        compiler_params=pltpu.CompilerParams(vmem_limit_bytes=FAST_LIMIT),
    )(rows, *there)


def lay_out_kernel(n_arrays, home, *refs):
    chunks, out = refs[:n_arrays], refs[-1]

    def copy():
        start = 0
        for chunk in chunks:
            out[start : start + chunk.shape[0], :] = chunk[...]
            start += chunk.shape[0]

    if home is None:
        copy()
    else:
        pl.when(lax.axis_index("cl") == home)(copy)


def lay_out(chunks, home=None, waits=()):
    rows, width = sum(x.shape[0] for x in chunks), chunks[0].shape[1]
    return pl.pallas_call(
        functools.partial(lay_out_kernel, len(chunks), home),
        out_shape=jax.ShapeDtypeStruct((rows, width), jnp.bfloat16),
        in_specs=list(vmem_specs(len(chunks) + len(waits))),
        out_specs=vmem_specs(1)[0],
        compiler_params=pltpu.CompilerParams(vmem_limit_bytes=FAST_LIMIT),
    )(*chunks, *waits)


class Layout:
    early, late = (0, 1, 2, 3), (4, 6, 5, 7)

    def __init__(self, n_owner, n_fine, capacity, main, home):
        self.n_owner, self.n_fine, self.capacity = n_owner, n_fine, capacity
        self.main, self.home = main, home
        self.head = main - INFO
        self.rest = capacity - self.head
        self.per_owner = n_fine // n_owner
        self.n_main = n_owner * main
        self.n_head = n_owner * self.head
        self.n_early = len(self.early) * self.rest
        self.n_late = len(self.late) * self.rest
        self.n_first = self.n_head + self.n_early
        self.n_all = self.n_first + self.n_late


def info_line(lay, main_ref, source):
    end = (source + 1) * lay.main
    return main_ref[end - INFO : end, :LANES].astype(jnp.float32)[INFO - 1 :]


def lines_of(lay, main_ref):
    return [info_line(lay, main_ref, source) for source in range(lay.n_owner)]


def hot_of(lay, info):
    lane = lax.broadcasted_iota(jnp.int32, (1, LANES), 1)
    hot = jnp.max(jnp.where(lane == lay.n_fine, info, 0.0), axis=1, keepdims=True)
    return hot.astype(jnp.int32)


def write_labels(lay, infos, sources, first, count, at, lab_sub, bias):
    cluster = swapped(lax.axis_index("cl"), hot_of(lay, infos[0]), lay.home)
    lane = lax.broadcasted_iota(jnp.int32, (1, LANES), 1)
    is_edge = lax.div(lane, lay.per_owner) == cluster
    for i, source in enumerate(sources):
        edges = jnp.where(is_edge, infos[source], 2.0 * lay.capacity)
        slot = lax.broadcasted_iota(jnp.int32, (count, LANES), 0) + first
        label = jnp.where(slot.astype(jnp.float32) >= edges, 1.0, 0.0)
        label = jnp.broadcast_to(jnp.sum(label, axis=1, keepdims=True), (count, LANES))
        start = at + i * count
        lab_sub[start : start + count, :] = label
        if bias is not None:
            bias[start : start + count, :] = jnp.where(
                label < lay.per_owner, NEIGHBOUR - SCALE, DEAD
            )


def first_labels(lay, infos, lab_sub):
    write_labels(lay, infos, range(lay.n_owner), 0, lay.head, 0, lab_sub, None)
    write_labels(lay, infos, lay.early, lay.head, lay.rest, lay.n_head, lab_sub, None)


def late_labels(lay, infos, lab_sub):
    write_labels(lay, infos, lay.late, lay.head, lay.rest, 0, lab_sub, None)


def turn_labels(lay, lab_sub, count, lab_lane, at):
    for i in range(0, count, LANES):
        block = jnp.transpose(lab_sub[i : i + LANES, :])[:1]
        lab_lane[:, at + i : at + i + LANES] = jnp.where(block < lay.per_owner, block, -1.0)


def copy_head(lay, main_ref, rows):
    for source in range(lay.n_owner):
        rows[source * lay.head : (source + 1) * lay.head, :] = main_ref[
            source * lay.main : source * lay.main + lay.head, :
        ]


def pieces(count, parts):
    return [(i * (count // parts), count // parts) for i in range(parts)]


def stream(lanes, tiles, lab_lane, buffers, put):
    rows_i, count, at = lanes
    step = 32
    tiles = [
        (ref, s, d, lab_sub, bias, line + s, back)
        for ref, n, lab_sub, bias, line, parts, back in tiles
        for s, d in pieces(n, parts)
    ]

    def scores_to(buffer, tile, rows):
        ref, start, deep = tile[:3]
        buffer[:deep, : rows.shape[0]] = lax.dot_general(
            ref[start : start + deep, :],
            rows,
            (((1,), (1,)), ((), ())),
            preferred_element_type=jnp.float32,
        )

    def run(start, blocks, wide):
        repeat = wide // LANES

        def rows_of(block):
            return rows_i[pl.ds(pl.multiple_of(start + block * wide, LANES), wide), :]

        scores_to(buffers[0], tiles[0], rows_of(0))

        def one_block(block):
            here = rows_of(block)
            place = pl.ds(pl.multiple_of(at + start + block * wide, LANES), wide)
            label_i = lab_lane[:, place]
            acc = jnp.zeros((8, wide), jnp.float32)
            for i, (_, _, deep, lab_sub, bias, line, back) in enumerate(tiles):
                if i + 1 < len(tiles):
                    scores_to(buffers[(i + 1) % 2], tiles[i + 1], here)
                elif blocks > 1:

                    @pl.when(block + 1 < blocks)
                    def _():
                        scores_to(buffers[0], tiles[0], rows_of(block + 1))

                buffer = buffers[i % 2]
                for c in range(0, deep, step):
                    part = slice(line + c, line + c + step)
                    label_j = jnp.concatenate([lab_sub[part, :]] * repeat, axis=1)
                    if bias is None:
                        bias_j = NEIGHBOUR - SCALE
                    else:
                        bias_j = jnp.concatenate([bias[part, :]] * repeat, axis=1)
                    shift = jnp.where(label_j == label_i, -SCALE, bias_j)
                    terms = jnp.exp2(buffer[c : c + step, :wide] * SCALE + shift)
                    acc = acc + jnp.sum(terms.reshape(step // 8, 8, wide), axis=0)
                    if back is not None:
                        across = terms[:, :LANES]
                        for r in range(1, repeat):
                            across = across + terms[:, r * LANES : (r + 1) * LANES]
                        back[part, :] += across
            put(place, jnp.sum(acc, axis=0, keepdims=True))

        if blocks == 1:
            one_block(0)
        else:
            pl.loop(0, blocks)(one_block)

    if count >= WIDE:
        run(0, count // WIDE, WIDE)
    if count % WIDE:
        run(count - count % WIDE, 1, count % WIDE)


def turn_sums(back, count, sums, at):
    for i in range(0, count, LANES):
        block = jnp.transpose(back[i : i + LANES, :])
        sums[:, at + i : at + i + LANES] += jnp.sum(block, axis=0, keepdims=True)


def setter(ref):
    def put(place, values):
        ref[:, place] = values

    return put


def adder(ref):
    def put(place, values):
        ref[:, place] += values

    return put


def inner_kernel(lay, mine, early, sums, lab_lane, lab_sub, rows, bias, back, buf_a, buf_b):
    is_home = lax.axis_index("cl") == lay.home
    infos = lines_of(lay, mine)
    buffers = (buf_a, buf_b)

    @pl.when(is_home)
    def _():
        copy_head(lay, mine, rows)
        first_labels(lay, infos, lab_sub)
        turn_labels(lay, lab_sub, lay.n_first, lab_lane, 0)
        back[...] = jnp.zeros(back.shape, jnp.float32)
        size = lay.n_early
        blocks = [(rows.at[pl.ds(start, size)], start) for start in range(0, lay.n_head, size)]
        blocks.append((early, lay.n_head))
        for i, (ref, at) in enumerate(blocks):
            tiles = [
                (ref_j, size, lab_sub, None, at_j, 2, None if at_j == at else back)
                for ref_j, at_j in blocks[i:]
            ]
            stream((ref, size, at), tiles, lab_lane, buffers, setter(sums))
        turn_sums(back, lay.n_first, sums, 0)

    @pl.when(jnp.logical_not(is_home))
    def _():
        write_labels(lay, infos, range(lay.n_owner), 0, lay.main, 0, lab_sub, bias)
        turn_labels(lay, lab_sub, lay.n_main, lab_lane, 0)
        tiles = [(mine, lay.n_main, lab_sub, bias, 0, 2, None)]
        stream((mine, lay.n_main, 0), tiles, lab_lane, buffers, setter(sums))


def half_blocks(ref_i, ref_j, lab_sub, line, back, at, lab_lane, buffers, put):
    half = ref_j.shape[0] // 2
    grp = lax.axis_index("grp")
    for h in range(2):
        start = pl.multiple_of((h ^ grp) * half, half)
        rows_j = ref_j.at[pl.ds(start, half)]
        sub = lab_sub.at[pl.ds(line + start, half)]
        backs = back.at[pl.ds(line + start, half)]
        lanes = (ref_i.at[pl.ds(h * half, half)], half, at + h * half)
        stream(lanes, [(rows_j, half, sub, None, 0, 1, backs)], lab_lane, buffers, put)


def cross_kernel(lay, mine, other, early, early_j, rows, sums, lab_lane, *refs):
    total, for_other, unfit_ref, lab_sub, rows_j, bias, back, buf_a, buf_b = refs
    is_home = lax.axis_index("cl") == lay.home
    infos = lines_of(lay, other)
    own = lines_of(lay, mine)
    hot = hot_of(lay, own[0])
    lane = lax.broadcasted_iota(jnp.int32, (1, LANES), 1)
    last = (lane < lay.n_fine) & (lax.rem(lane, lay.per_owner) == lay.per_owner - 1)
    last = last & (lax.div(lane, lay.per_owner) != hot)
    unfit = jnp.zeros((1, LANES), jnp.float32)
    for info in infos + own:
        wrong = last & (info >= lay.main)
        differs = (info != hot.astype(jnp.float32)) | (info >= lay.n_owner)
        wrong = wrong | ((lane == lay.n_fine) & differs)
        unfit = unfit + jnp.where(wrong, 1.0, 0.0)
    unfit_ref[0, 0] = jnp.max(unfit).astype(jnp.int32)
    total[...] = sums[...]
    buffers = (buf_a, buf_b)

    @pl.when(is_home)
    def _():
        copy_head(lay, other, rows_j)
        first_labels(lay, infos, lab_sub)
        back[...] = jnp.zeros(back.shape, jnp.float32)
        size = lay.n_early
        blocks_i = [rows.at[pl.ds(start, size)] for start in range(0, lay.n_head, size)] + [early]
        blocks_j = [rows_j.at[pl.ds(start, size)] for start in range(0, lay.n_head, size)]
        blocks_j.append(early_j)
        put, n = adder(total), len(blocks_i)
        for i, ref in enumerate(blocks_i):
            tiles = [
                (blocks_j[j], size, lab_sub, None, j * size, 2, back)
                for j in ((i + step) % n for step in range(1, (n + 1) // 2))
            ]
            stream((ref, size, i * size), tiles, lab_lane, buffers, put)
            half_blocks(
                ref, blocks_j[i], lab_sub, i * size, back, i * size, lab_lane, buffers, put
            )
        for_other[...] = jnp.zeros(for_other.shape, jnp.float32)
        turn_sums(back, lay.n_first, for_other, 0)

    @pl.when(jnp.logical_not(is_home))
    def _():
        write_labels(lay, infos, range(lay.n_owner), 0, lay.main, 0, lab_sub, bias)
        tiles = [(other, lay.n_main, lab_sub, bias, 0, 2, None)]
        stream((mine, lay.n_main, 0), tiles, lab_lane, buffers, adder(total))


def late_pairs(lay, i_refs, late_j, late_sub, back, lab_lane, buffers, put):
    rows, early = i_refs
    lates = [(late_j, lay.n_late, late_sub, None, 0, 2, back)]
    stream((rows, lay.n_head, 0), lates, lab_lane, buffers, put)
    stream((early, lay.n_early, lay.n_head), lates, lab_lane, buffers, put)


def inner_late_kernel(lay, mine, early, late, rows, first_lane, *refs):
    sums, lab_lane, late_sub, back, buf_a, buf_b = refs

    @pl.when(lax.axis_index("cl") == lay.home)
    def _():
        late_labels(lay, lines_of(lay, mine), late_sub)
        lab_lane[:, : lay.n_first] = first_lane[...]
        turn_labels(lay, late_sub, lay.n_late, lab_lane, lay.n_first)
        buffers = (buf_a, buf_b)
        back[...] = jnp.zeros(back.shape, jnp.float32)
        put = setter(sums)
        late_pairs(lay, (rows, early), late, late_sub, back, lab_lane, buffers, put)
        tiles = [(late, lay.n_late, late_sub, None, 0, 2, None)]
        stream((late, lay.n_late, lay.n_first), tiles, lab_lane, buffers, put)
        turn_sums(back, lay.n_late, sums, lay.n_first)


def cross_late_kernel(lay, other, early, late, late_j, rows, first_lane, *refs):
    first_sums, first_other, lab_lane, sums, out_ref, total, late_sub, back, buf_a, buf_b = refs
    is_home = lax.axis_index("cl") == lay.home
    grp = lax.axis_index("grp")

    @pl.when(is_home)
    def _():
        infos = lines_of(lay, other)
        write_labels(lay, infos, lay.late, lay.head, lay.rest, 0, late_sub, None)
        total[...] = sums[...]
        total[:, : lay.n_first] += first_sums[...]
        back[...] = jnp.zeros(back.shape, jnp.float32)
        buffers, put = (buf_a, buf_b), adder(total)
        late_pairs(lay, (rows, early), late_j, late_sub, back, lab_lane, buffers, put)
        half_blocks(late, late_j, late_sub, 0, back, lay.n_first, lab_lane, buffers, put)

        def write(line, values):
            for source in range(lay.n_owner):
                start = source * lay.head
                out_ref[2 * source + line, :, : lay.head] = values[:, start : start + lay.head]
            for i, source in enumerate(lay.early + lay.late):
                start = lay.n_head + i * lay.rest
                out_ref[2 * source + line, :, lay.head :] = values[:, start : start + lay.rest]

        write(grp, total[...])
        total[:, : lay.n_first] = first_other[...]
        total[:, lay.n_first :] = jnp.zeros((1, lay.n_late), jnp.float32)
        turn_sums(back, lay.n_late, total, lay.n_first)
        write(1 - grp, total[...])

    @pl.when(jnp.logical_not(is_home))
    def _():
        out_ref[...] = jnp.zeros(out_ref.shape, jnp.float32)
        values = jnp.where(first_lane[...] >= 0, first_sums[...], 1.0)
        for source in range(lay.n_owner):
            start = source * lay.main
            out_ref[2 * source + grp, :, : lay.main] = values[:, start : start + lay.main]


def pair_call(kernel, lay, arrays, out_shape, scratch, out_specs=None, pairs=0):
    width = arrays[0].shape[1]
    buffer = pltpu.VMEM((lay.n_main // 2, WIDE), jnp.float32)
    return pl.pallas_call(
        functools.partial(kernel, lay),
        out_shape=out_shape,
        in_specs=list(vmem_specs(len(arrays))),
        out_specs=out_specs or vmem_specs(len(out_shape)),
        scratch_shapes=list(scratch) + [buffer, buffer],
        compiler_params=pltpu.CompilerParams(vmem_limit_bytes=FAST_LIMIT),
        cost_estimate=pl.CostEstimate(
            flops=2 * pairs * width, bytes_accessed=1, transcendentals=pairs
        ),
    )(*arrays)


def fast_unpack_kernel(values_ref, pos_ref, out_ref):
    pos = pos_ref[...]
    lane = lax.rem(pos, LANES)
    line = lax.div(pos, LANES)
    out = jnp.ones(pos.shape, jnp.float32)
    per = values_ref.shape[2] // LANES
    for r in range(values_ref.shape[0] // 2 * per):
        owner, part = r // per, slice(r % per * LANES, (r % per + 1) * LANES)
        table = values_ref[2 * owner, :, part] + values_ref[2 * owner + 1, :, part]
        found = jnp.take_along_axis(jnp.broadcast_to(table, pos.shape), lane, axis=1)
        out = jnp.where(line == r, found, out)
    out_ref[...] = jnp.log(out)


def fast_unpack(values, pos):
    vmem = pl.BlockSpec(memory_space=pltpu.VMEM)
    return pl.pallas_call(
        fast_unpack_kernel,
        out_shape=jax.ShapeDtypeStruct(pos.shape, jnp.float32),
        in_specs=[vmem, vmem],
        out_specs=vmem,
    )(values, pos)


def general(embeddings, labels, owner_map):
    n_owner = lax.axis_size("cl")
    capacity = SLOTS // n_owner
    rows, width = embeddings.shape
    packed, pos, counts = pack(embeddings, labels, owner_map, n_owner, capacity)
    counts = lax.all_gather(counts, ("cl", "grp"), tiled=True)
    mine = lax.all_to_all(
        packed.reshape(n_owner, capacity, width), "cl", split_axis=0, concat_axis=0, tiled=True
    ).reshape(SLOTS, width)
    other = lax.ppermute(mine, "grp", [(0, 1), (1, 0)])
    results = log_counts(counts, mine, other, n_owner, capacity)
    returned = lax.all_to_all(
        results.reshape(n_owner, capacity), "cl", split_axis=0, concat_axis=0, tiled=True
    )
    return unpack(returned.reshape(SLOTS), pos).reshape(rows)


def body(embeddings, labels, owner_map):
    n_owner = lax.axis_size("cl")
    capacity = SLOTS // n_owner
    rows, width = embeddings.shape
    n_fine = owner_map.shape[0]
    main = -(-(rows // n_owner * 9 // 8) // 16) * 16
    if n_owner != 8 or main >= capacity or n_fine >= LANES:
        return general(embeddings, labels, owner_map)
    home = 2
    lay = Layout(n_owner, n_fine, capacity, main, home)
    packed, extra, pos = place_rows(embeddings, labels, owner_map, lay)

    def hop(x, pairs):
        return lax.ppermute(x, "cl", pairs)

    def swap(x):
        return lax.ppermute(x, "grp", [(0, 1), (1, 0)])

    moved = hop(extra, [(6, 4), (7, 5)])
    early = [extra if s == home else hop(extra, [(s, home)]) for s in lay.early]
    early = lay_out(early, home)
    mine = lax.all_to_all(
        packed.reshape(n_owner, main, width), "cl", split_axis=0, concat_axis=0, tiled=True
    ).reshape(n_owner * main, width)
    mine = after(mine, early, moved)
    other, early_j = swap(mine), swap(early)
    late = [hop(x, [(s, home)]) for s in (4, 5) for x in (extra, moved)]

    def array(shape, dtype=jnp.float32):
        return jax.ShapeDtypeStruct(shape, dtype)

    def scratch(shape):
        return pltpu.VMEM(shape, jnp.float32)

    row, long_row = array((1, lay.n_first)), array((1, lay.n_all))
    side, bias = array((lay.n_first, LANES)), scratch((lay.n_main, LANES))
    heads = array((lay.n_head, width), jnp.bfloat16)
    late_side, first_side = scratch((lay.n_late, LANES)), scratch((lay.n_first, LANES))
    sums, first_lane, lab_sub, heads_i = pair_call(
        inner_kernel, lay, (mine, early), (row, row, side, heads), (bias, first_side)
    )
    specs = vmem_specs(2) + (pl.BlockSpec(memory_space=pltpu.SMEM),) + vmem_specs(2)
    sums, first_other, unfit, _, _ = pair_call(
        cross_kernel,
        lay,
        (mine, other, early, early_j, heads_i, sums, first_lane),
        (row, row, array((1, 1), jnp.int32), side, heads),
        (bias, first_side),
        specs,
    )
    late = lay_out(late, home, (sums,))
    late_j = swap(late)
    late_sums, lane = pair_call(
        inner_late_kernel,
        lay,
        (mine, early, late, heads_i, first_lane),
        (long_row, long_row),
        (late_side, late_side),
        pairs=lay.n_late * (lay.n_all + lay.n_first),
    )
    (results,) = pair_call(
        cross_late_kernel,
        lay,
        (other, early, late, late_j, heads_i, first_lane, sums, first_other, lane, late_sums),
        (array((2 * n_owner, 1, capacity)),),
        (scratch(long_row.shape), late_side, late_side),
    )
    returned = lax.all_to_all(
        results, ("cl", "grp"), split_axis=0, concat_axis=0, tiled=True
    )
    return lax.cond(
        unfit[0, 0] == 0,
        lambda: fast_unpack(returned, pos).reshape(rows),
        lambda: general(embeddings, labels, owner_map),
    )


def solution(mesh):
    return jax.shard_map(
        body,
        mesh=mesh,
        in_specs=(P(("parts", "cl", "grp"), None), P(("parts", "cl", "grp")), P("parts")),
        out_specs=P(("parts", "cl", "grp")),
        check_vma=False,
    )
```

```python
import functools
import math

import jax
import jax.numpy as jnp
from jax import lax
from jax.experimental import pallas as pl
from jax.experimental.pallas import tpu as pltpu
from jax.sharding import PartitionSpec as P

SLOTS = 2048

temper = 0.2
neighbour_factor = 0.5
epsilon = 1e-06

LANES = 128
SCALE = math.log2(math.e) / temper
NEIGHBOUR = math.log2(neighbour_factor)
DEAD = -1e30
VMEM_LIMIT = 48 * 1024 * 1024
FAST_LIMIT = 16 * 1024 * 1024
WIDE = 512
INFO = 16


def column_of(row):
    pieces = []
    for start in range(0, row.shape[1], LANES):
        width = min(LANES, row.shape[1] - start)
        shape = (width, width)
        diagonal = lax.broadcasted_iota(jnp.int32, shape, 0) == lax.broadcasted_iota(
            jnp.int32, shape, 1
        )
        piece = jnp.broadcast_to(row[:, start : start + width], shape)
        pieces.append(jnp.sum(jnp.where(diagonal, piece, 0.0), axis=1, keepdims=True))
    return jnp.concatenate(pieces, axis=0)


def row_of(column):
    n = column.shape[0]
    diagonal = lax.broadcasted_iota(jnp.int32, (n, n), 0) == lax.broadcasted_iota(
        jnp.int32, (n, n), 1
    )
    return jnp.sum(jnp.where(diagonal, column, 0.0), axis=0, keepdims=True)


def pack_kernel(n_owner, capacity, x_ref, lab_ref, map_ref, out_ref, pos_ref, cnt_ref, unit, pos_row):
    rows = x_ref.shape[0]
    n_fine = map_ref.shape[1]
    per_owner = n_fine // n_owner
    owner_row = map_ref[...].astype(jnp.float32)
    fine_row = lax.broadcasted_iota(jnp.int32, (1, n_fine), 1).astype(jnp.float32)
    key_row = owner_row * n_fine + fine_row
    key_col = column_of(key_row)
    sorted_col = jnp.sum(jnp.where(key_row < key_col, 1.0, 0.0), axis=1, keepdims=True)
    lab = lab_ref[...].astype(jnp.float32)
    lab_row = jnp.concatenate([lab[b : b + 1, :] for b in range(lab.shape[0])], axis=1)
    fine_col = lax.broadcasted_iota(jnp.int32, (n_fine, rows), 0).astype(jnp.float32)
    fine_id = jnp.sum(jnp.where(fine_col == lab_row, sorted_col, 0.0), axis=0, keepdims=True)
    counts_col = jnp.sum(jnp.where(fine_col == fine_id, 1.0, 0.0), axis=1, keepdims=True)
    cnt_ref[...] = row_of(counts_col).astype(jnp.int32)
    coarse = jnp.floor((fine_id + 0.5) * (1.0 / per_owner))
    before = jnp.sum(
        jnp.where(fine_col < coarse * per_owner, counts_col, 0.0), axis=0, keepdims=True
    )
    index = lax.broadcasted_iota(jnp.int32, (1, rows), 1).astype(jnp.float32)
    row_key = fine_id * rows + index
    rank = jnp.zeros((1, rows), jnp.float32)
    for start in range(0, rows, LANES):
        other = column_of(row_key[:, start : start + LANES])
        rank = rank + jnp.sum(jnp.where(other < row_key, 1.0, 0.0), axis=0, keepdims=True)
    pos = (coarse * capacity + rank - before).astype(jnp.int32)
    pos_row[...] = pos
    pos_ref[...] = jnp.concatenate(
        [pos[:, start : start + LANES] for start in range(0, rows, LANES)], axis=0
    )
    x = x_ref[...].astype(jnp.float32)
    squares = jnp.sum(x * x, axis=1, keepdims=True)
    unit[...] = (x * lax.rsqrt(squares + epsilon)).astype(jnp.bfloat16)

    step = 256

    @pl.loop(0, out_ref.shape[0] // step)
    def _(block):
        slot = lax.broadcasted_iota(jnp.int32, (step, rows), 0) + block * step
        chosen = jnp.where(slot == pos_row[...], 1.0, 0.0).astype(jnp.bfloat16)
        packed = jnp.dot(chosen, unit[...], preferred_element_type=jnp.float32)
        out_ref[pl.ds(pl.multiple_of(block * step, step), step), :] = packed.astype(jnp.bfloat16)


def pack(embeddings, labels, owner_map, n_owner, capacity):
    rows, width = embeddings.shape
    n_fine = owner_map.shape[0]
    total = n_owner * capacity
    vmem = pl.BlockSpec(memory_space=pltpu.VMEM)
    return pl.pallas_call(
        functools.partial(pack_kernel, n_owner, capacity),
        out_shape=(
            jax.ShapeDtypeStruct((total, width), jnp.bfloat16),
            jax.ShapeDtypeStruct((rows // LANES, LANES), jnp.int32),
            jax.ShapeDtypeStruct((1, n_fine), jnp.int32),
        ),
        in_specs=[vmem] * 3,
        out_specs=(vmem, vmem, vmem),
        scratch_shapes=[pltpu.VMEM((rows, width), jnp.bfloat16), pltpu.VMEM((1, rows), jnp.int32)],
        compiler_params=pltpu.CompilerParams(vmem_limit_bytes=VMEM_LIMIT),
    )(embeddings, labels.reshape(rows // LANES, LANES), owner_map.reshape(1, n_fine))


def counts_kernel(n_owner, capacity, cnt_ref, mine_ref, other_ref, out_ref, lab_lane, lab_sub, bias):
    total = mine_ref.shape[0]
    per_owner = cnt_ref.shape[1] // n_owner
    me = lax.axis_index("cl")
    grp = lax.axis_index("grp")
    n_grp = lax.axis_size("grp")
    for member in range(2):
        for source in range(n_owner):
            line = source * n_grp + lax.rem(grp + member, n_grp)
            edges = []
            edge = jnp.int32(0)
            for f in range(per_owner):
                edge = edge + cnt_ref[line, me * per_owner + f]
                edges.append(edge)
            down = lax.broadcasted_iota(jnp.int32, (capacity, LANES), 0)
            label = jnp.zeros((capacity, LANES), jnp.int32)
            for edge in edges:
                label = label + jnp.where(down >= edge, 1, 0)
            start = (member * n_owner + source) * capacity
            lab_sub[start : start + capacity, :] = label
            bias[start : start + capacity, :] = jnp.where(
                label < per_owner, NEIGHBOUR - SCALE, DEAD
            )
            if member == 0:
                across = lax.broadcasted_iota(jnp.int32, (1, capacity), 1)
                label = jnp.zeros((1, capacity), jnp.int32)
                for edge in edges:
                    label = label + jnp.where(across >= edge, 1, 0)
                lab_lane[:, source * capacity : (source + 1) * capacity] = jnp.where(
                    label < per_owner, label, -1
                )
    wide, deep = min(512, total), min(256, total)

    @pl.loop(0, total // wide)
    def _(block):
        columns = pl.ds(pl.multiple_of(block * wide, wide), wide)
        rows_i = mine_ref[columns, :]
        label_i = lab_lane[:, columns]

        def add(ref, offset):
            def step(j, acc):
                start = pl.multiple_of(j * deep, deep)
                scores = lax.dot_general(
                    ref[pl.ds(start, deep), :],
                    rows_i,
                    (((1,), (1,)), ((), ())),
                    preferred_element_type=jnp.float32,
                )
                place = pl.ds(pl.multiple_of(start + offset, deep), deep)
                label_j = lab_sub[place, :]
                bias_j = bias[place, :]
                repeat = wide // LANES
                label_j = jnp.concatenate([label_j] * repeat, axis=1)
                bias_j = jnp.concatenate([bias_j] * repeat, axis=1)
                shift = jnp.where(label_j == label_i, -SCALE, bias_j)
                terms = jnp.exp2(scores * SCALE + shift)
                return acc + jnp.sum(terms.reshape(deep // 8, 8, wide), axis=0)

            return step

        acc = jnp.zeros((8, wide), jnp.float32)
        acc = lax.fori_loop(0, total // deep, add(mine_ref, 0), acc, unroll=2)
        acc = lax.fori_loop(0, total // deep, add(other_ref, total), acc, unroll=2)
        totals = jnp.sum(acc, axis=0, keepdims=True)
        out_ref[:, columns] = jnp.log(jnp.where(label_i >= 0, totals, 1.0))


def log_counts(counts, mine, other, n_owner, capacity):
    total = mine.shape[0]
    vmem = pl.BlockSpec(memory_space=pltpu.VMEM)
    return pl.pallas_call(
        functools.partial(counts_kernel, n_owner, capacity),
        out_shape=jax.ShapeDtypeStruct((1, total), jnp.float32),
        in_specs=[pl.BlockSpec(memory_space=pltpu.SMEM), vmem, vmem],
        out_specs=vmem,
        scratch_shapes=[
            pltpu.VMEM((1, total), jnp.int32),
            pltpu.VMEM((2 * total, LANES), jnp.int32),
            pltpu.VMEM((2 * total, LANES), jnp.float32),
        ],
        compiler_params=pltpu.CompilerParams(vmem_limit_bytes=VMEM_LIMIT),
    )(counts, mine, other)


def unpack_kernel(values_ref, pos_ref, out_ref):
    pos = pos_ref[...]
    lane = lax.rem(pos, LANES)
    line = lax.div(pos, LANES)
    out = jnp.zeros(pos.shape, jnp.float32)
    for r in range(values_ref.shape[0]):
        table = jnp.broadcast_to(values_ref[r : r + 1, :], pos.shape)
        found = jnp.take_along_axis(table, lane, axis=1)
        out = jnp.where(line == r, found, out)
    out_ref[...] = out


def unpack(values, pos):
    vmem = pl.BlockSpec(memory_space=pltpu.VMEM)
    return pl.pallas_call(
        unpack_kernel,
        out_shape=jax.ShapeDtypeStruct(pos.shape, jnp.float32),
        in_specs=[vmem, vmem],
        out_specs=vmem,
    )(values.reshape(-1, LANES), pos)


def swapped(x, first, second):
    return jnp.where(x == first, second, jnp.where(x == second, first, x))


def place_kernel(lay, x_hbm, lab_hbm, map_hbm, *refs):
    main_hbm, tail_ref, pos_ref, x_ref, lab_ref, map_ref, unit, main_ref, sems = refs
    n_owner, capacity, main, home = lay.n_owner, lay.capacity, lay.main, lay.home
    copies = [
        pltpu.make_async_copy(src, dst, sems.at[i])
        for i, (src, dst) in enumerate(((x_hbm, x_ref), (lab_hbm, lab_ref), (map_hbm, map_ref)))
    ]
    for copy in copies:
        copy.start()
    rows, width = x_ref.shape
    n_fine = map_ref.shape[1]
    per_owner = n_fine // n_owner
    copies[1].wait()
    copies[2].wait()
    owner_row = map_ref[...].astype(jnp.float32)
    fine_row = lax.broadcasted_iota(jnp.int32, (1, n_fine), 1).astype(jnp.float32)
    key_row = owner_row * n_fine + fine_row
    key_col = column_of(key_row)
    sorted_col = jnp.sum(jnp.where(key_row < key_col, 1.0, 0.0), axis=1, keepdims=True)
    lab = lab_ref[...].astype(jnp.float32)
    lab_row = jnp.concatenate([lab[b : b + 1, :] for b in range(lab.shape[0])], axis=1)
    fine_col = lax.broadcasted_iota(jnp.int32, (n_fine, rows), 0).astype(jnp.float32)
    fine_id = jnp.sum(jnp.where(fine_col == lab_row, sorted_col, 0.0), axis=0, keepdims=True)
    counts_col = jnp.sum(jnp.where(fine_col == fine_id, 1.0, 0.0), axis=1, keepdims=True)
    coarse = jnp.floor((fine_id + 0.5) * (1.0 / per_owner))
    first = coarse * per_owner
    before = jnp.sum(jnp.where(fine_col < first, counts_col, 0.0), axis=0, keepdims=True)
    upto = jnp.sum(jnp.where(fine_col < first + per_owner, counts_col, 0.0), axis=0, keepdims=True)
    full = jnp.min(
        jnp.where(upto - before == capacity, coarse, float(n_owner)), axis=1, keepdims=True
    )
    line = lax.broadcasted_iota(jnp.int32, (n_fine, LANES), 0)
    lane = lax.broadcasted_iota(jnp.int32, (n_fine, LANES), 1)
    inside = (line <= lane) & (lax.div(line, per_owner) == lax.div(lane, per_owner))
    running = jnp.sum(jnp.where(inside, counts_col, 0.0), axis=0, keepdims=True)
    info = jnp.where(lane[:1] < n_fine, running, full)
    index = lax.broadcasted_iota(jnp.int32, (1, rows), 1).astype(jnp.float32)
    row_key = fine_id * rows + index
    rank = jnp.zeros((1, rows), jnp.float32)
    for start in range(0, rows, LANES):
        other = column_of(row_key[:, start : start + LANES])
        rank = rank + jnp.sum(jnp.where(other < row_key, 1.0, 0.0), axis=0, keepdims=True)
    rank = (rank - before).astype(jnp.int32)
    place = swapped(coarse.astype(jnp.int32), full.astype(jnp.int32), home)
    table = place * capacity + rank
    pos_ref[...] = jnp.concatenate(
        [table[:, start : start + LANES] for start in range(0, rows, LANES)], axis=0
    )
    fits = rank < jnp.where(place == home, lay.head, main - 1)
    slot = jnp.where(fits, place * main + rank, -1)
    tail_slot = jnp.where(place == home, rank - lay.head, -1)
    copies[0].wait()
    x = x_ref[...].astype(jnp.float32)
    squares = jnp.sum(x * x, axis=1, keepdims=True)
    unit[...] = (x * lax.rsqrt(squares + epsilon)).astype(jnp.bfloat16)

    def chosen_rows(slot, start, count):
        here = lax.broadcasted_iota(jnp.int32, (count, rows), 0) + start
        chosen = jnp.where(here == slot, 1.0, 0.0).astype(jnp.bfloat16)
        return jnp.dot(chosen, unit[...], preferred_element_type=jnp.float32)

    count = 2 * main
    down = lax.broadcasted_iota(jnp.int32, (count, LANES), 0)
    is_info = lax.rem(down, main) == main - 1
    writes = []
    for i, start in enumerate(range(0, lay.n_main, count)):
        packed = chosen_rows(slot, start, count)
        place = slice(start, start + count)
        main_ref[place, LANES:] = packed[:, LANES:].astype(jnp.bfloat16)
        main_ref[place, :LANES] = jnp.where(is_info, info, packed[:, :LANES]).astype(jnp.bfloat16)
        writes.append(
            pltpu.make_async_copy(
                main_ref.at[pl.ds(start, count)], main_hbm.at[pl.ds(start, count)], sems.at[3 + i]
            )
        )
        writes[-1].start()
    tail_ref[...] = chosen_rows(tail_slot, 0, lay.rest).astype(jnp.bfloat16)
    for write in writes:
        write.wait()


def vmem_specs(count):
    return (pl.BlockSpec(memory_space=pltpu.VMEM),) * count


def place_rows(embeddings, labels, owner_map, lay):
    rows, width = embeddings.shape
    n_fine = owner_map.shape[0]
    lab_shape = (rows // LANES, LANES)
    anywhere = pl.BlockSpec(memory_space=pl.ANY)
    return pl.pallas_call(
        functools.partial(place_kernel, lay),
        out_shape=(
            jax.ShapeDtypeStruct((lay.n_main, width), jnp.bfloat16),
            jax.ShapeDtypeStruct((lay.rest, width), jnp.bfloat16),
            jax.ShapeDtypeStruct(lab_shape, jnp.int32),
        ),
        in_specs=[anywhere] * 3,
        out_specs=(anywhere,) + vmem_specs(2),
        scratch_shapes=[
            pltpu.VMEM((rows, width), jnp.bfloat16),
            pltpu.VMEM(lab_shape, jnp.int32),
            pltpu.VMEM((1, n_fine), jnp.int32),
            pltpu.VMEM((rows, width), jnp.bfloat16),
            pltpu.VMEM((lay.n_main, width), jnp.bfloat16),
            pltpu.SemaphoreType.DMA((3 + lay.n_owner // 2,)),
        ],
        compiler_params=pltpu.CompilerParams(vmem_limit_bytes=FAST_LIMIT),
    )(embeddings, labels.reshape(lab_shape), owner_map.reshape(1, n_fine))


def gate_kernel(*refs):
    pass


def after(rows, *there):
    return pl.pallas_call(
        gate_kernel,
        out_shape=jax.ShapeDtypeStruct(rows.shape, rows.dtype),
        in_specs=list(vmem_specs(1 + len(there))),
        out_specs=vmem_specs(1)[0],
        input_output_aliases={0: 0},
        compiler_params=pltpu.CompilerParams(vmem_limit_bytes=FAST_LIMIT),
    )(rows, *there)


def lay_out_kernel(n_arrays, home, *refs):
    chunks, out = refs[:n_arrays], refs[-1]

    def copy():
        start = 0
        for chunk in chunks:
            out[start : start + chunk.shape[0], :] = chunk[...]
            start += chunk.shape[0]

    if home is None:
        copy()
    else:
        pl.when(lax.axis_index("cl") == home)(copy)


def lay_out(chunks, home=None, waits=()):
    rows, width = sum(x.shape[0] for x in chunks), chunks[0].shape[1]
    return pl.pallas_call(
        functools.partial(lay_out_kernel, len(chunks), home),
        out_shape=jax.ShapeDtypeStruct((rows, width), jnp.bfloat16),
        in_specs=list(vmem_specs(len(chunks) + len(waits))),
        out_specs=vmem_specs(1)[0],
        compiler_params=pltpu.CompilerParams(vmem_limit_bytes=FAST_LIMIT),
    )(*chunks, *waits)


class Layout:
    early, late = (0, 1, 2, 3, 4, 5), (6, 7)

    def __init__(self, n_owner, n_fine, capacity, main, home):
        self.n_owner, self.n_fine, self.capacity = n_owner, n_fine, capacity
        self.main, self.home = main, home
        self.head = main - INFO
        self.rest = capacity - self.head
        self.per_owner = n_fine // n_owner
        self.n_main = n_owner * main
        self.n_head = n_owner * self.head
        self.n_early = len(self.early) * self.rest
        self.n_late = len(self.late) * self.rest
        self.n_first = self.n_head + self.n_early
        self.n_all = self.n_first + self.n_late


def info_line(lay, main_ref, source):
    end = (source + 1) * lay.main
    return main_ref[end - INFO : end, :LANES].astype(jnp.float32)[INFO - 1 :]


def lines_of(lay, main_ref):
    return [info_line(lay, main_ref, source) for source in range(lay.n_owner)]


def hot_of(lay, info):
    lane = lax.broadcasted_iota(jnp.int32, (1, LANES), 1)
    hot = jnp.max(jnp.where(lane == lay.n_fine, info, 0.0), axis=1, keepdims=True)
    return hot.astype(jnp.int32)


def write_labels(lay, infos, sources, first, count, at, lab_sub, bias):
    cluster = swapped(lax.axis_index("cl"), hot_of(lay, infos[0]), lay.home)
    lane = lax.broadcasted_iota(jnp.int32, (1, LANES), 1)
    is_edge = lax.div(lane, lay.per_owner) == cluster
    for i, source in enumerate(sources):
        edges = jnp.where(is_edge, infos[source], 2.0 * lay.capacity)
        slot = lax.broadcasted_iota(jnp.int32, (count, LANES), 0) + first
        label = jnp.where(slot.astype(jnp.float32) >= edges, 1.0, 0.0)
        label = jnp.broadcast_to(jnp.sum(label, axis=1, keepdims=True), (count, LANES))
        start = at + i * count
        lab_sub[start : start + count, :] = label
        if bias is not None:
            bias[start : start + count, :] = jnp.where(
                label < lay.per_owner, NEIGHBOUR - SCALE, DEAD
            )


def first_labels(lay, infos, lab_sub):
    write_labels(lay, infos, range(lay.n_owner), 0, lay.head, 0, lab_sub, None)
    write_labels(lay, infos, lay.early, lay.head, lay.rest, lay.n_head, lab_sub, None)


def late_labels(lay, infos, lab_sub):
    write_labels(lay, infos, lay.late, lay.head, lay.rest, 0, lab_sub, None)


def turn_labels(lay, lab_sub, count, lab_lane, at):
    for i in range(0, count, LANES):
        block = jnp.transpose(lab_sub[i : i + LANES, :])[:1]
        lab_lane[:, at + i : at + i + LANES] = jnp.where(block < lay.per_owner, block, -1.0)


def copy_head(lay, main_ref, rows):
    for source in range(lay.n_owner):
        rows[source * lay.head : (source + 1) * lay.head, :] = main_ref[
            source * lay.main : source * lay.main + lay.head, :
        ]


def pieces(count, parts):
    return [(i * (count // parts), count // parts) for i in range(parts)]


def stream(lanes, tiles, lab_lane, buffers, put):
    rows_i, count, at = lanes
    step = 32
    tiles = [
        (ref, s, d, lab_sub, bias, line + s, back)
        for ref, n, lab_sub, bias, line, parts, back in tiles
        for s, d in pieces(n, parts)
    ]

    def scores_to(buffer, tile, rows):
        ref, start, deep = tile[:3]
        buffer[:deep, : rows.shape[0]] = lax.dot_general(
            ref[start : start + deep, :],
            rows,
            (((1,), (1,)), ((), ())),
            preferred_element_type=jnp.float32,
        )

    def run(start, blocks, wide):
        repeat = wide // LANES

        def rows_of(block):
            return rows_i[pl.ds(pl.multiple_of(start + block * wide, LANES), wide), :]

        scores_to(buffers[0], tiles[0], rows_of(0))

        def one_block(block):
            here = rows_of(block)
            place = pl.ds(pl.multiple_of(at + start + block * wide, LANES), wide)
            label_i = lab_lane[:, place]
            acc = jnp.zeros((8, wide), jnp.float32)
            for i, (_, _, deep, lab_sub, bias, line, back) in enumerate(tiles):
                if i + 1 < len(tiles):
                    scores_to(buffers[(i + 1) % 2], tiles[i + 1], here)
                elif blocks > 1:

                    @pl.when(block + 1 < blocks)
                    def _():
                        scores_to(buffers[0], tiles[0], rows_of(block + 1))

                buffer = buffers[i % 2]
                for c in range(0, deep, step):
                    part = slice(line + c, line + c + step)
                    label_j = jnp.concatenate([lab_sub[part, :]] * repeat, axis=1)
                    if bias is None:
                        bias_j = NEIGHBOUR - SCALE
                    else:
                        bias_j = jnp.concatenate([bias[part, :]] * repeat, axis=1)
                    shift = jnp.where(label_j == label_i, -SCALE, bias_j)
                    terms = jnp.exp2(buffer[c : c + step, :wide] * SCALE + shift)
                    acc = acc + jnp.sum(terms.reshape(step // 8, 8, wide), axis=0)
                    if back is not None:
                        across = terms[:, :LANES]
                        for r in range(1, repeat):
                            across = across + terms[:, r * LANES : (r + 1) * LANES]
                        back[part, :] += across
            put(place, jnp.sum(acc, axis=0, keepdims=True))

        if blocks == 1:
            one_block(0)
        else:
            pl.loop(0, blocks)(one_block)

    if count >= WIDE:
        run(0, count // WIDE, WIDE)
    if count % WIDE:
        run(count - count % WIDE, 1, count % WIDE)


def turn_sums(back, count, sums, at):
    for i in range(0, count, LANES):
        block = jnp.transpose(back[i : i + LANES, :])
        sums[:, at + i : at + i + LANES] += jnp.sum(block, axis=0, keepdims=True)


def setter(ref):
    def put(place, values):
        ref[:, place] = values

    return put


def adder(ref):
    def put(place, values):
        ref[:, place] += values

    return put


def blocks_of(lay, rows, early):
    blocks = []
    for ref, count, at in ((rows, lay.n_head, 0), (early, lay.n_early, lay.n_head)):
        for start in range(0, count, WIDE):
            size = min(WIDE, count - start)
            blocks.append((ref.at[pl.ds(start, size)], size, at + start))
    return blocks


def inner_kernel(lay, mine, early, sums, lab_lane, lab_sub, rows, bias, back, buf_a, buf_b):
    is_home = lax.axis_index("cl") == lay.home
    infos = lines_of(lay, mine)
    buffers = (buf_a, buf_b)

    @pl.when(is_home)
    def _():
        copy_head(lay, mine, rows)
        first_labels(lay, infos, lab_sub)
        turn_labels(lay, lab_sub, lay.n_first, lab_lane, 0)
        back[...] = jnp.zeros(back.shape, jnp.float32)
        blocks = blocks_of(lay, rows, early)
        for i, (ref, size, at) in enumerate(blocks):
            tiles = [
                (ref_j, size_j, lab_sub, None, at_j, 2, None if at_j == at else back)
                for ref_j, size_j, at_j in blocks[i:]
            ]
            stream((ref, size, at), tiles, lab_lane, buffers, setter(sums))
        turn_sums(back, lay.n_first, sums, 0)

    @pl.when(jnp.logical_not(is_home))
    def _():
        write_labels(lay, infos, range(lay.n_owner), 0, lay.main, 0, lab_sub, bias)
        turn_labels(lay, lab_sub, lay.n_main, lab_lane, 0)
        tiles = [(mine, lay.n_main, lab_sub, bias, 0, 2, None)]
        stream((mine, lay.n_main, 0), tiles, lab_lane, buffers, setter(sums))


def half_blocks(ref_i, ref_j, lab_sub, line, back, at, lab_lane, buffers, put):
    half = ref_j.shape[0] // 2
    grp = lax.axis_index("grp")
    for h in range(2):
        start = pl.multiple_of((h ^ grp) * half, half)
        rows_j = ref_j.at[pl.ds(start, half)]
        sub = lab_sub.at[pl.ds(line + start, half)]
        backs = back.at[pl.ds(line + start, half)]
        lanes = (ref_i.at[pl.ds(h * half, half)], half, at + h * half)
        stream(lanes, [(rows_j, half, sub, None, 0, 1, backs)], lab_lane, buffers, put)


def cross_kernel(lay, mine, other, early, early_j, rows, sums, lab_lane, *refs):
    total, for_other, unfit_ref, lab_sub, rows_j, bias, back, buf_a, buf_b = refs
    is_home = lax.axis_index("cl") == lay.home
    infos = lines_of(lay, other)
    own = lines_of(lay, mine)
    hot = hot_of(lay, own[0])
    lane = lax.broadcasted_iota(jnp.int32, (1, LANES), 1)
    last = (lane < lay.n_fine) & (lax.rem(lane, lay.per_owner) == lay.per_owner - 1)
    last = last & (lax.div(lane, lay.per_owner) != hot)
    unfit = jnp.zeros((1, LANES), jnp.float32)
    for info in infos + own:
        wrong = last & (info >= lay.main)
        differs = (info != hot.astype(jnp.float32)) | (info >= lay.n_owner)
        wrong = wrong | ((lane == lay.n_fine) & differs)
        unfit = unfit + jnp.where(wrong, 1.0, 0.0)
    unfit_ref[0, 0] = jnp.max(unfit).astype(jnp.int32)
    total[...] = sums[...]
    buffers = (buf_a, buf_b)

    @pl.when(is_home)
    def _():
        copy_head(lay, other, rows_j)
        first_labels(lay, infos, lab_sub)
        back[...] = jnp.zeros(back.shape, jnp.float32)
        blocks_i = blocks_of(lay, rows, early)
        blocks_j = blocks_of(lay, rows_j, early_j)
        put, n = adder(total), len(blocks_i)

        def is_taken(i, j):
            step = (j - i) % n
            return 0 < 2 * step < n or (2 * step == n and i < j)

        for i, (ref, size, at) in enumerate(blocks_i):
            tiles = [
                (ref_j, size_j, lab_sub, None, at_j, 2, back)
                for j, (ref_j, size_j, at_j) in enumerate(blocks_j)
                if is_taken(i, j)
            ]
            if tiles:
                stream((ref, size, at), tiles, lab_lane, buffers, put)
            ref_j = blocks_j[i][0]
            half_blocks(ref, ref_j, lab_sub, at, back, at, lab_lane, buffers, put)
        for_other[...] = jnp.zeros(for_other.shape, jnp.float32)
        turn_sums(back, lay.n_first, for_other, 0)

    @pl.when(jnp.logical_not(is_home))
    def _():
        write_labels(lay, infos, range(lay.n_owner), 0, lay.main, 0, lab_sub, bias)
        tiles = [(other, lay.n_main, lab_sub, bias, 0, 2, None)]
        stream((mine, lay.n_main, 0), tiles, lab_lane, buffers, adder(total))


def late_pairs(lay, i_refs, late_j, late_sub, back, lab_lane, buffers, put):
    rows, early = i_refs
    lates = [(late_j, lay.n_late, late_sub, None, 0, 2, back)]
    stream((rows, lay.n_head, 0), lates, lab_lane, buffers, put)
    stream((early, lay.n_early, lay.n_head), lates, lab_lane, buffers, put)


def inner_late_kernel(lay, mine, early, late, rows, first_lane, *refs):
    sums, lab_lane, late_sub, back, buf_a, buf_b = refs

    @pl.when(lax.axis_index("cl") == lay.home)
    def _():
        late_labels(lay, lines_of(lay, mine), late_sub)
        lab_lane[:, : lay.n_first] = first_lane[...]
        turn_labels(lay, late_sub, lay.n_late, lab_lane, lay.n_first)
        buffers = (buf_a, buf_b)
        back[...] = jnp.zeros(back.shape, jnp.float32)
        put = setter(sums)
        late_pairs(lay, (rows, early), late, late_sub, back, lab_lane, buffers, put)
        tiles = [(late, lay.n_late, late_sub, None, 0, 2, None)]
        stream((late, lay.n_late, lay.n_first), tiles, lab_lane, buffers, put)
        turn_sums(back, lay.n_late, sums, lay.n_first)


def cross_late_kernel(lay, other, early, late, late_j, rows, first_lane, *refs):
    first_sums, first_other, lab_lane, sums, out_ref, total, late_sub, back, buf_a, buf_b = refs
    is_home = lax.axis_index("cl") == lay.home
    grp = lax.axis_index("grp")

    @pl.when(is_home)
    def _():
        infos = lines_of(lay, other)
        write_labels(lay, infos, lay.late, lay.head, lay.rest, 0, late_sub, None)
        total[...] = sums[...]
        total[:, : lay.n_first] += first_sums[...]
        back[...] = jnp.zeros(back.shape, jnp.float32)
        buffers, put = (buf_a, buf_b), adder(total)
        late_pairs(lay, (rows, early), late_j, late_sub, back, lab_lane, buffers, put)
        half_blocks(late, late_j, late_sub, 0, back, lay.n_first, lab_lane, buffers, put)

        def write(line, values):
            for source in range(lay.n_owner):
                start = source * lay.head
                out_ref[2 * source + line, :, : lay.head] = values[:, start : start + lay.head]
            for i, source in enumerate(lay.early + lay.late):
                start = lay.n_head + i * lay.rest
                out_ref[2 * source + line, :, lay.head :] = values[:, start : start + lay.rest]

        write(grp, total[...])
        total[:, : lay.n_first] = first_other[...]
        total[:, lay.n_first :] = jnp.zeros((1, lay.n_late), jnp.float32)
        turn_sums(back, lay.n_late, total, lay.n_first)
        write(1 - grp, total[...])

    @pl.when(jnp.logical_not(is_home))
    def _():
        out_ref[...] = jnp.zeros(out_ref.shape, jnp.float32)
        values = jnp.where(first_lane[...] >= 0, first_sums[...], 1.0)
        for source in range(lay.n_owner):
            start = source * lay.main
            out_ref[2 * source + grp, :, : lay.main] = values[:, start : start + lay.main]


def pair_call(kernel, lay, arrays, out_shape, scratch, out_specs=None, pairs=0):
    width = arrays[0].shape[1]
    buffer = pltpu.VMEM((lay.n_main // 2, WIDE), jnp.float32)
    return pl.pallas_call(
        functools.partial(kernel, lay),
        out_shape=out_shape,
        in_specs=list(vmem_specs(len(arrays))),
        out_specs=out_specs or vmem_specs(len(out_shape)),
        scratch_shapes=list(scratch) + [buffer, buffer],
        compiler_params=pltpu.CompilerParams(vmem_limit_bytes=FAST_LIMIT),
        cost_estimate=pl.CostEstimate(
            flops=2 * pairs * width, bytes_accessed=1, transcendentals=pairs
        ),
    )(*arrays)


def fast_unpack_kernel(values_ref, pos_ref, out_ref):
    pos = pos_ref[...]
    lane = lax.rem(pos, LANES)
    line = lax.div(pos, LANES)
    out = jnp.ones(pos.shape, jnp.float32)
    per = values_ref.shape[2] // LANES
    for r in range(values_ref.shape[0] // 2 * per):
        owner, part = r // per, slice(r % per * LANES, (r % per + 1) * LANES)
        table = values_ref[2 * owner, :, part] + values_ref[2 * owner + 1, :, part]
        found = jnp.take_along_axis(jnp.broadcast_to(table, pos.shape), lane, axis=1)
        out = jnp.where(line == r, found, out)
    out_ref[...] = jnp.log(out)


def fast_unpack(values, pos):
    vmem = pl.BlockSpec(memory_space=pltpu.VMEM)
    return pl.pallas_call(
        fast_unpack_kernel,
        out_shape=jax.ShapeDtypeStruct(pos.shape, jnp.float32),
        in_specs=[vmem, vmem],
        out_specs=vmem,
    )(values, pos)


def general(embeddings, labels, owner_map):
    n_owner = lax.axis_size("cl")
    capacity = SLOTS // n_owner
    rows, width = embeddings.shape
    packed, pos, counts = pack(embeddings, labels, owner_map, n_owner, capacity)
    counts = lax.all_gather(counts, ("cl", "grp"), tiled=True)
    mine = lax.all_to_all(
        packed.reshape(n_owner, capacity, width), "cl", split_axis=0, concat_axis=0, tiled=True
    ).reshape(SLOTS, width)
    other = lax.ppermute(mine, "grp", [(0, 1), (1, 0)])
    results = log_counts(counts, mine, other, n_owner, capacity)
    returned = lax.all_to_all(
        results.reshape(n_owner, capacity), "cl", split_axis=0, concat_axis=0, tiled=True
    )
    return unpack(returned.reshape(SLOTS), pos).reshape(rows)


def body(embeddings, labels, owner_map):
    n_owner = lax.axis_size("cl")
    capacity = SLOTS // n_owner
    rows, width = embeddings.shape
    n_fine = owner_map.shape[0]
    main = -(-(rows // n_owner * 9 // 8) // 16) * 16
    if n_owner != 8 or main >= capacity or n_fine >= LANES:
        return general(embeddings, labels, owner_map)
    home = 2
    lay = Layout(n_owner, n_fine, capacity, main, home)
    packed, extra, pos = place_rows(embeddings, labels, owner_map, lay)

    def hop(x, pairs):
        return lax.ppermute(x, "cl", pairs)

    def swap(x):
        return lax.ppermute(x, "grp", [(0, 1), (1, 0)])

    moved = hop(extra, [(6, 4), (7, 5)])
    early = [extra if s == home else hop(extra, [(s, home)]) for s in lay.early]
    early = lay_out(early, home)
    mine = lax.all_to_all(
        packed.reshape(n_owner, main, width), "cl", split_axis=0, concat_axis=0, tiled=True
    ).reshape(n_owner * main, width)
    mine = after(mine, early, moved)
    other, early_j = swap(mine), swap(early)
    late = [hop(moved, [(s, home)]) for s in (4, 5)]

    def array(shape, dtype=jnp.float32):
        return jax.ShapeDtypeStruct(shape, dtype)

    def scratch(shape):
        return pltpu.VMEM(shape, jnp.float32)

    row, long_row = array((1, lay.n_first)), array((1, lay.n_all))
    side, bias = array((lay.n_first, LANES)), scratch((lay.n_main, LANES))
    heads = array((lay.n_head, width), jnp.bfloat16)
    late_side, first_side = scratch((lay.n_late, LANES)), scratch((lay.n_first, LANES))
    sums, first_lane, lab_sub, heads_i = pair_call(
        inner_kernel, lay, (mine, early), (row, row, side, heads), (bias, first_side)
    )
    specs = vmem_specs(2) + (pl.BlockSpec(memory_space=pltpu.SMEM),) + vmem_specs(2)
    sums, first_other, unfit, _, _ = pair_call(
        cross_kernel,
        lay,
        (mine, other, early, early_j, heads_i, sums, first_lane),
        (row, row, array((1, 1), jnp.int32), side, heads),
        (bias, first_side),
        specs,
    )
    late = lay_out(late, home, (sums,))
    late_j = swap(late)
    late_sums, lane = pair_call(
        inner_late_kernel,
        lay,
        (mine, early, late, heads_i, first_lane),
        (long_row, long_row),
        (late_side, late_side),
        pairs=lay.n_late * (lay.n_all + lay.n_first),
    )
    (results,) = pair_call(
        cross_late_kernel,
        lay,
        (other, early, late, late_j, heads_i, first_lane, sums, first_other, lane, late_sums),
        (array((2 * n_owner, 1, capacity)),),
        (scratch(long_row.shape), late_side, late_side),
    )
    returned = lax.all_to_all(
        results, ("cl", "grp"), split_axis=0, concat_axis=0, tiled=True
    )
    return lax.cond(
        unfit[0, 0] == 0,
        lambda: fast_unpack(returned, pos).reshape(rows),
        lambda: general(embeddings, labels, owner_map),
    )


def solution(mesh):
    return jax.shard_map(
        body,
        mesh=mesh,
        in_specs=(P(("parts", "cl", "grp"), None), P(("parts", "cl", "grp")), P("parts")),
        out_specs=P(("parts", "cl", "grp")),
        check_vma=False,
    )
```

```python
import functools
import math

import jax
import jax.numpy as jnp
from jax import lax
from jax.experimental import pallas as pl
from jax.experimental.pallas import tpu as pltpu
from jax.sharding import PartitionSpec as P

SLOTS = 2048

temper = 0.2
neighbour_factor = 0.5
epsilon = 1e-06

LANES = 128
SCALE = math.log2(math.e) / temper
NEIGHBOUR = math.log2(neighbour_factor)
DEAD = -1e30
VMEM_LIMIT = 48 * 1024 * 1024
FAST_LIMIT = 16 * 1024 * 1024
WIDE = 512
INFO = 16


def column_of(row):
    pieces = []
    for start in range(0, row.shape[1], LANES):
        width = min(LANES, row.shape[1] - start)
        shape = (width, width)
        diagonal = lax.broadcasted_iota(jnp.int32, shape, 0) == lax.broadcasted_iota(
            jnp.int32, shape, 1
        )
        piece = jnp.broadcast_to(row[:, start : start + width], shape)
        pieces.append(jnp.sum(jnp.where(diagonal, piece, 0.0), axis=1, keepdims=True))
    return jnp.concatenate(pieces, axis=0)


def row_of(column):
    n = column.shape[0]
    diagonal = lax.broadcasted_iota(jnp.int32, (n, n), 0) == lax.broadcasted_iota(
        jnp.int32, (n, n), 1
    )
    return jnp.sum(jnp.where(diagonal, column, 0.0), axis=0, keepdims=True)


def pack_kernel(n_owner, capacity, x_ref, lab_ref, map_ref, out_ref, pos_ref, cnt_ref, unit, pos_row):
    rows = x_ref.shape[0]
    n_fine = map_ref.shape[1]
    per_owner = n_fine // n_owner
    owner_row = map_ref[...].astype(jnp.float32)
    fine_row = lax.broadcasted_iota(jnp.int32, (1, n_fine), 1).astype(jnp.float32)
    key_row = owner_row * n_fine + fine_row
    key_col = column_of(key_row)
    sorted_col = jnp.sum(jnp.where(key_row < key_col, 1.0, 0.0), axis=1, keepdims=True)
    lab = lab_ref[...].astype(jnp.float32)
    lab_row = jnp.concatenate([lab[b : b + 1, :] for b in range(lab.shape[0])], axis=1)
    fine_col = lax.broadcasted_iota(jnp.int32, (n_fine, rows), 0).astype(jnp.float32)
    fine_id = jnp.sum(jnp.where(fine_col == lab_row, sorted_col, 0.0), axis=0, keepdims=True)
    counts_col = jnp.sum(jnp.where(fine_col == fine_id, 1.0, 0.0), axis=1, keepdims=True)
    cnt_ref[...] = row_of(counts_col).astype(jnp.int32)
    coarse = jnp.floor((fine_id + 0.5) * (1.0 / per_owner))
    before = jnp.sum(
        jnp.where(fine_col < coarse * per_owner, counts_col, 0.0), axis=0, keepdims=True
    )
    index = lax.broadcasted_iota(jnp.int32, (1, rows), 1).astype(jnp.float32)
    row_key = fine_id * rows + index
    rank = jnp.zeros((1, rows), jnp.float32)
    for start in range(0, rows, LANES):
        other = column_of(row_key[:, start : start + LANES])
        rank = rank + jnp.sum(jnp.where(other < row_key, 1.0, 0.0), axis=0, keepdims=True)
    pos = (coarse * capacity + rank - before).astype(jnp.int32)
    pos_row[...] = pos
    pos_ref[...] = jnp.concatenate(
        [pos[:, start : start + LANES] for start in range(0, rows, LANES)], axis=0
    )
    x = x_ref[...].astype(jnp.float32)
    squares = jnp.sum(x * x, axis=1, keepdims=True)
    unit[...] = (x * lax.rsqrt(squares + epsilon)).astype(jnp.bfloat16)

    step = 256

    @pl.loop(0, out_ref.shape[0] // step)
    def _(block):
        slot = lax.broadcasted_iota(jnp.int32, (step, rows), 0) + block * step
        chosen = jnp.where(slot == pos_row[...], 1.0, 0.0).astype(jnp.bfloat16)
        packed = jnp.dot(chosen, unit[...], preferred_element_type=jnp.float32)
        out_ref[pl.ds(pl.multiple_of(block * step, step), step), :] = packed.astype(jnp.bfloat16)


def pack(embeddings, labels, owner_map, n_owner, capacity):
    rows, width = embeddings.shape
    n_fine = owner_map.shape[0]
    total = n_owner * capacity
    vmem = pl.BlockSpec(memory_space=pltpu.VMEM)
    return pl.pallas_call(
        functools.partial(pack_kernel, n_owner, capacity),
        out_shape=(
            jax.ShapeDtypeStruct((total, width), jnp.bfloat16),
            jax.ShapeDtypeStruct((rows // LANES, LANES), jnp.int32),
            jax.ShapeDtypeStruct((1, n_fine), jnp.int32),
        ),
        in_specs=[vmem] * 3,
        out_specs=(vmem, vmem, vmem),
        scratch_shapes=[pltpu.VMEM((rows, width), jnp.bfloat16), pltpu.VMEM((1, rows), jnp.int32)],
        compiler_params=pltpu.CompilerParams(vmem_limit_bytes=VMEM_LIMIT),
    )(embeddings, labels.reshape(rows // LANES, LANES), owner_map.reshape(1, n_fine))


def counts_kernel(n_owner, capacity, cnt_ref, mine_ref, other_ref, out_ref, lab_lane, lab_sub, bias):
    total = mine_ref.shape[0]
    per_owner = cnt_ref.shape[1] // n_owner
    me = lax.axis_index("cl")
    grp = lax.axis_index("grp")
    n_grp = lax.axis_size("grp")
    for member in range(2):
        for source in range(n_owner):
            line = source * n_grp + lax.rem(grp + member, n_grp)
            edges = []
            edge = jnp.int32(0)
            for f in range(per_owner):
                edge = edge + cnt_ref[line, me * per_owner + f]
                edges.append(edge)
            down = lax.broadcasted_iota(jnp.int32, (capacity, LANES), 0)
            label = jnp.zeros((capacity, LANES), jnp.int32)
            for edge in edges:
                label = label + jnp.where(down >= edge, 1, 0)
            start = (member * n_owner + source) * capacity
            lab_sub[start : start + capacity, :] = label
            bias[start : start + capacity, :] = jnp.where(
                label < per_owner, NEIGHBOUR - SCALE, DEAD
            )
            if member == 0:
                across = lax.broadcasted_iota(jnp.int32, (1, capacity), 1)
                label = jnp.zeros((1, capacity), jnp.int32)
                for edge in edges:
                    label = label + jnp.where(across >= edge, 1, 0)
                lab_lane[:, source * capacity : (source + 1) * capacity] = jnp.where(
                    label < per_owner, label, -1
                )
    wide, deep = min(512, total), min(256, total)

    @pl.loop(0, total // wide)
    def _(block):
        columns = pl.ds(pl.multiple_of(block * wide, wide), wide)
        rows_i = mine_ref[columns, :]
        label_i = lab_lane[:, columns]

        def add(ref, offset):
            def step(j, acc):
                start = pl.multiple_of(j * deep, deep)
                scores = lax.dot_general(
                    ref[pl.ds(start, deep), :],
                    rows_i,
                    (((1,), (1,)), ((), ())),
                    preferred_element_type=jnp.float32,
                )
                place = pl.ds(pl.multiple_of(start + offset, deep), deep)
                label_j = lab_sub[place, :]
                bias_j = bias[place, :]
                repeat = wide // LANES
                label_j = jnp.concatenate([label_j] * repeat, axis=1)
                bias_j = jnp.concatenate([bias_j] * repeat, axis=1)
                shift = jnp.where(label_j == label_i, -SCALE, bias_j)
                terms = jnp.exp2(scores * SCALE + shift)
                return acc + jnp.sum(terms.reshape(deep // 8, 8, wide), axis=0)

            return step

        acc = jnp.zeros((8, wide), jnp.float32)
        acc = lax.fori_loop(0, total // deep, add(mine_ref, 0), acc, unroll=2)
        acc = lax.fori_loop(0, total // deep, add(other_ref, total), acc, unroll=2)
        totals = jnp.sum(acc, axis=0, keepdims=True)
        out_ref[:, columns] = jnp.log(jnp.where(label_i >= 0, totals, 1.0))


def log_counts(counts, mine, other, n_owner, capacity):
    total = mine.shape[0]
    vmem = pl.BlockSpec(memory_space=pltpu.VMEM)
    return pl.pallas_call(
        functools.partial(counts_kernel, n_owner, capacity),
        out_shape=jax.ShapeDtypeStruct((1, total), jnp.float32),
        in_specs=[pl.BlockSpec(memory_space=pltpu.SMEM), vmem, vmem],
        out_specs=vmem,
        scratch_shapes=[
            pltpu.VMEM((1, total), jnp.int32),
            pltpu.VMEM((2 * total, LANES), jnp.int32),
            pltpu.VMEM((2 * total, LANES), jnp.float32),
        ],
        compiler_params=pltpu.CompilerParams(vmem_limit_bytes=VMEM_LIMIT),
    )(counts, mine, other)


def unpack_kernel(values_ref, pos_ref, out_ref):
    pos = pos_ref[...]
    lane = lax.rem(pos, LANES)
    line = lax.div(pos, LANES)
    out = jnp.zeros(pos.shape, jnp.float32)
    for r in range(values_ref.shape[0]):
        table = jnp.broadcast_to(values_ref[r : r + 1, :], pos.shape)
        found = jnp.take_along_axis(table, lane, axis=1)
        out = jnp.where(line == r, found, out)
    out_ref[...] = out


def unpack(values, pos):
    vmem = pl.BlockSpec(memory_space=pltpu.VMEM)
    return pl.pallas_call(
        unpack_kernel,
        out_shape=jax.ShapeDtypeStruct(pos.shape, jnp.float32),
        in_specs=[vmem, vmem],
        out_specs=vmem,
    )(values.reshape(-1, LANES), pos)


def swapped(x, first, second):
    return jnp.where(x == first, second, jnp.where(x == second, first, x))


def place_kernel(lay, x_hbm, lab_hbm, map_hbm, *refs):
    main_hbm, tail_ref, pos_ref, x_ref, lab_ref, map_ref, unit, main_ref, sems = refs
    n_owner, capacity, main, home = lay.n_owner, lay.capacity, lay.main, lay.home
    copies = [
        pltpu.make_async_copy(src, dst, sems.at[i])
        for i, (src, dst) in enumerate(((x_hbm, x_ref), (lab_hbm, lab_ref), (map_hbm, map_ref)))
    ]
    for copy in copies:
        copy.start()
    rows, width = x_ref.shape
    n_fine = map_ref.shape[1]
    per_owner = n_fine // n_owner
    copies[1].wait()
    copies[2].wait()
    owner_row = map_ref[...].astype(jnp.float32)
    fine_row = lax.broadcasted_iota(jnp.int32, (1, n_fine), 1).astype(jnp.float32)
    key_row = owner_row * n_fine + fine_row
    key_col = column_of(key_row)
    sorted_col = jnp.sum(jnp.where(key_row < key_col, 1.0, 0.0), axis=1, keepdims=True)
    lab = lab_ref[...].astype(jnp.float32)
    lab_row = jnp.concatenate([lab[b : b + 1, :] for b in range(lab.shape[0])], axis=1)
    fine_col = lax.broadcasted_iota(jnp.int32, (n_fine, rows), 0).astype(jnp.float32)
    fine_id = jnp.sum(jnp.where(fine_col == lab_row, sorted_col, 0.0), axis=0, keepdims=True)
    counts_col = jnp.sum(jnp.where(fine_col == fine_id, 1.0, 0.0), axis=1, keepdims=True)
    coarse = jnp.floor((fine_id + 0.5) * (1.0 / per_owner))
    first = coarse * per_owner
    before = jnp.sum(jnp.where(fine_col < first, counts_col, 0.0), axis=0, keepdims=True)
    upto = jnp.sum(jnp.where(fine_col < first + per_owner, counts_col, 0.0), axis=0, keepdims=True)
    full = jnp.min(
        jnp.where(upto - before == capacity, coarse, float(n_owner)), axis=1, keepdims=True
    )
    line = lax.broadcasted_iota(jnp.int32, (n_fine, LANES), 0)
    lane = lax.broadcasted_iota(jnp.int32, (n_fine, LANES), 1)
    inside = (line <= lane) & (lax.div(line, per_owner) == lax.div(lane, per_owner))
    running = jnp.sum(jnp.where(inside, counts_col, 0.0), axis=0, keepdims=True)
    info = jnp.where(lane[:1] < n_fine, running, full)
    index = lax.broadcasted_iota(jnp.int32, (1, rows), 1).astype(jnp.float32)
    row_key = fine_id * rows + index
    rank = jnp.zeros((1, rows), jnp.float32)
    for start in range(0, rows, LANES):
        other = column_of(row_key[:, start : start + LANES])
        rank = rank + jnp.sum(jnp.where(other < row_key, 1.0, 0.0), axis=0, keepdims=True)
    rank = (rank - before).astype(jnp.int32)
    place = swapped(coarse.astype(jnp.int32), full.astype(jnp.int32), home)
    table = place * capacity + rank
    pos_ref[...] = jnp.concatenate(
        [table[:, start : start + LANES] for start in range(0, rows, LANES)], axis=0
    )
    fits = rank < jnp.where(place == home, lay.head, main - 1)
    slot = jnp.where(fits, place * main + rank, -1)
    tail_slot = jnp.where(place == home, rank - lay.head, -1)
    copies[0].wait()
    x = x_ref[...].astype(jnp.float32)
    squares = jnp.sum(x * x, axis=1, keepdims=True)
    unit[...] = (x * lax.rsqrt(squares + epsilon)).astype(jnp.bfloat16)

    def chosen_rows(slot, start, count):
        here = lax.broadcasted_iota(jnp.int32, (count, rows), 0) + start
        chosen = jnp.where(here == slot, 1.0, 0.0).astype(jnp.bfloat16)
        return jnp.dot(chosen, unit[...], preferred_element_type=jnp.float32)

    count = 2 * main
    down = lax.broadcasted_iota(jnp.int32, (count, LANES), 0)
    is_info = lax.rem(down, main) == main - 1
    writes = []
    for i, start in enumerate(range(0, lay.n_main, count)):
        packed = chosen_rows(slot, start, count)
        place = slice(start, start + count)
        main_ref[place, LANES:] = packed[:, LANES:].astype(jnp.bfloat16)
        main_ref[place, :LANES] = jnp.where(is_info, info, packed[:, :LANES]).astype(jnp.bfloat16)
        writes.append(
            pltpu.make_async_copy(
                main_ref.at[pl.ds(start, count)], main_hbm.at[pl.ds(start, count)], sems.at[3 + i]
            )
        )
        writes[-1].start()
    tail_ref[...] = chosen_rows(tail_slot, 0, lay.rest).astype(jnp.bfloat16)
    for write in writes:
        write.wait()


def vmem_specs(count):
    return (pl.BlockSpec(memory_space=pltpu.VMEM),) * count


def place_rows(embeddings, labels, owner_map, lay):
    rows, width = embeddings.shape
    n_fine = owner_map.shape[0]
    lab_shape = (rows // LANES, LANES)
    anywhere = pl.BlockSpec(memory_space=pl.ANY)
    return pl.pallas_call(
        functools.partial(place_kernel, lay),
        out_shape=(
            jax.ShapeDtypeStruct((lay.n_main, width), jnp.bfloat16),
            jax.ShapeDtypeStruct((lay.rest, width), jnp.bfloat16),
            jax.ShapeDtypeStruct(lab_shape, jnp.int32),
        ),
        in_specs=[anywhere] * 3,
        out_specs=(anywhere,) + vmem_specs(2),
        scratch_shapes=[
            pltpu.VMEM((rows, width), jnp.bfloat16),
            pltpu.VMEM(lab_shape, jnp.int32),
            pltpu.VMEM((1, n_fine), jnp.int32),
            pltpu.VMEM((rows, width), jnp.bfloat16),
            pltpu.VMEM((lay.n_main, width), jnp.bfloat16),
            pltpu.SemaphoreType.DMA((3 + lay.n_owner // 2,)),
        ],
        compiler_params=pltpu.CompilerParams(vmem_limit_bytes=FAST_LIMIT),
    )(embeddings, labels.reshape(lab_shape), owner_map.reshape(1, n_fine))


def gate_kernel(*refs):
    pass


def after(rows, *there):
    return pl.pallas_call(
        gate_kernel,
        out_shape=jax.ShapeDtypeStruct(rows.shape, rows.dtype),
        in_specs=list(vmem_specs(1 + len(there))),
        out_specs=vmem_specs(1)[0],
        input_output_aliases={0: 0},
        compiler_params=pltpu.CompilerParams(vmem_limit_bytes=FAST_LIMIT),
    )(rows, *there)


def lay_out_kernel(n_arrays, home, *refs):
    chunks, out = refs[:n_arrays], refs[-1]

    def copy():
        start = 0
        for chunk in chunks:
            out[start : start + chunk.shape[0], :] = chunk[...]
            start += chunk.shape[0]

    if home is None:
        copy()
    else:
        pl.when(lax.axis_index("cl") == home)(copy)


def lay_out(chunks, home=None, waits=()):
    rows, width = sum(x.shape[0] for x in chunks), chunks[0].shape[1]
    return pl.pallas_call(
        functools.partial(lay_out_kernel, len(chunks), home),
        out_shape=jax.ShapeDtypeStruct((rows, width), jnp.bfloat16),
        in_specs=list(vmem_specs(len(chunks) + len(waits))),
        out_specs=vmem_specs(1)[0],
        compiler_params=pltpu.CompilerParams(vmem_limit_bytes=FAST_LIMIT),
    )(*chunks, *waits)


class Layout:
    early, late = (0, 1, 2, 3), (4, 6, 5, 7)

    def __init__(self, n_owner, n_fine, capacity, main, home):
        self.n_owner, self.n_fine, self.capacity = n_owner, n_fine, capacity
        self.main, self.home = main, home
        self.head = main - INFO
        self.rest = capacity - self.head
        self.per_owner = n_fine // n_owner
        self.n_main = n_owner * main
        self.n_head = n_owner * self.head
        self.n_early = len(self.early) * self.rest
        self.n_late = len(self.late) * self.rest
        self.n_first = self.n_head + self.n_early
        self.n_all = self.n_first + self.n_late


def info_line(lay, main_ref, source):
    end = (source + 1) * lay.main
    return main_ref[end - INFO : end, :LANES].astype(jnp.float32)[INFO - 1 :]


def lines_of(lay, main_ref):
    return [info_line(lay, main_ref, source) for source in range(lay.n_owner)]


def hot_of(lay, info):
    lane = lax.broadcasted_iota(jnp.int32, (1, LANES), 1)
    hot = jnp.max(jnp.where(lane == lay.n_fine, info, 0.0), axis=1, keepdims=True)
    return hot.astype(jnp.int32)


def write_labels(lay, infos, sources, first, count, at, lab_sub, bias):
    cluster = swapped(lax.axis_index("cl"), hot_of(lay, infos[0]), lay.home)
    lane = lax.broadcasted_iota(jnp.int32, (1, LANES), 1)
    is_edge = lax.div(lane, lay.per_owner) == cluster
    for i, source in enumerate(sources):
        edges = jnp.where(is_edge, infos[source], 2.0 * lay.capacity)
        slot = lax.broadcasted_iota(jnp.int32, (count, LANES), 0) + first
        label = jnp.where(slot.astype(jnp.float32) >= edges, 1.0, 0.0)
        label = jnp.broadcast_to(jnp.sum(label, axis=1, keepdims=True), (count, LANES))
        start = at + i * count
        lab_sub[start : start + count, :] = label
        if bias is not None:
            bias[start : start + count, :] = jnp.where(
                label < lay.per_owner, NEIGHBOUR - SCALE, DEAD
            )


def first_labels(lay, infos, lab_sub):
    write_labels(lay, infos, range(lay.n_owner), 0, lay.head, 0, lab_sub, None)
    write_labels(lay, infos, lay.early, lay.head, lay.rest, lay.n_head, lab_sub, None)


def late_labels(lay, infos, lab_sub):
    write_labels(lay, infos, lay.late, lay.head, lay.rest, 0, lab_sub, None)


def turn_labels(lay, lab_sub, count, lab_lane, at):
    for i in range(0, count, LANES):
        block = jnp.transpose(lab_sub[i : i + LANES, :])[:1]
        lab_lane[:, at + i : at + i + LANES] = jnp.where(block < lay.per_owner, block, -1.0)


def copy_head(lay, main_ref, rows):
    for source in range(lay.n_owner):
        rows[source * lay.head : (source + 1) * lay.head, :] = main_ref[
            source * lay.main : source * lay.main + lay.head, :
        ]


def pieces(count, parts):
    return [(i * (count // parts), count // parts) for i in range(parts)]


def stream(lanes, tiles, lab_lane, buffers, put):
    rows_i, count, at = lanes
    step = 32
    tiles = [
        (ref, s, d, lab_sub, bias, line + s, back)
        for ref, n, lab_sub, bias, line, parts, back in tiles
        for s, d in pieces(n, parts)
    ]

    def scores_to(buffer, tile, rows):
        ref, start, deep = tile[:3]
        buffer[:deep, : rows.shape[0]] = lax.dot_general(
            ref[start : start + deep, :],
            rows,
            (((1,), (1,)), ((), ())),
            preferred_element_type=jnp.float32,
        )

    def run(start, blocks, wide):
        repeat = wide // LANES

        def rows_of(block):
            return rows_i[pl.ds(pl.multiple_of(start + block * wide, LANES), wide), :]

        scores_to(buffers[0], tiles[0], rows_of(0))

        def one_block(block):
            here = rows_of(block)
            place = pl.ds(pl.multiple_of(at + start + block * wide, LANES), wide)
            label_i = lab_lane[:, place]
            acc = jnp.zeros((8, wide), jnp.float32)
            for i, (_, _, deep, lab_sub, bias, line, back) in enumerate(tiles):
                if i + 1 < len(tiles):
                    scores_to(buffers[(i + 1) % 2], tiles[i + 1], here)
                elif blocks > 1:

                    @pl.when(block + 1 < blocks)
                    def _():
                        scores_to(buffers[0], tiles[0], rows_of(block + 1))

                buffer = buffers[i % 2]
                for c in range(0, deep, step):
                    part = slice(line + c, line + c + step)
                    label_j = jnp.concatenate([lab_sub[part, :]] * repeat, axis=1)
                    if bias is None:
                        bias_j = NEIGHBOUR - SCALE
                    else:
                        bias_j = jnp.concatenate([bias[part, :]] * repeat, axis=1)
                    shift = jnp.where(label_j == label_i, -SCALE, bias_j)
                    terms = jnp.exp2(buffer[c : c + step, :wide] * SCALE + shift)
                    acc = acc + jnp.sum(terms.reshape(step // 8, 8, wide), axis=0)
                    if back is not None:
                        across = terms[:, :LANES]
                        for r in range(1, repeat):
                            across = across + terms[:, r * LANES : (r + 1) * LANES]
                        back[part, :] += across
            put(place, jnp.sum(acc, axis=0, keepdims=True))

        if blocks == 1:
            one_block(0)
        else:
            pl.loop(0, blocks)(one_block)

    if count >= WIDE:
        run(0, count // WIDE, WIDE)
    if count % WIDE:
        run(count - count % WIDE, 1, count % WIDE)


def turn_sums(back, count, sums, at):
    for i in range(0, count, LANES):
        block = jnp.transpose(back[i : i + LANES, :])
        sums[:, at + i : at + i + LANES] += jnp.sum(block, axis=0, keepdims=True)


def setter(ref):
    def put(place, values):
        ref[:, place] = values

    return put


def adder(ref):
    def put(place, values):
        ref[:, place] += values

    return put


def inner_kernel(lay, mine, early, sums, lab_lane, rows, lab_sub, bias, back, buf_a, buf_b):
    is_home = lax.axis_index("cl") == lay.home
    infos = lines_of(lay, mine)
    buffers = (buf_a, buf_b)

    @pl.when(is_home)
    def _():
        copy_head(lay, mine, rows)
        first_labels(lay, infos, lab_sub)
        turn_labels(lay, lab_sub, lay.n_first, lab_lane, 0)
        back[...] = jnp.zeros(back.shape, jnp.float32)
        size = lay.n_early
        blocks = [(rows.at[pl.ds(start, size)], start) for start in range(0, lay.n_head, size)]
        blocks.append((early, lay.n_head))
        for i, (ref, at) in enumerate(blocks):
            tiles = [
                (ref_j, size, lab_sub, None, at_j, 2, None if at_j == at else back)
                for ref_j, at_j in blocks[i:]
            ]
            stream((ref, size, at), tiles, lab_lane, buffers, setter(sums))
        turn_sums(back, lay.n_first, sums, 0)

    @pl.when(jnp.logical_not(is_home))
    def _():
        write_labels(lay, infos, range(lay.n_owner), 0, lay.main, 0, lab_sub, bias)
        turn_labels(lay, lab_sub, lay.n_main, lab_lane, 0)
        tiles = [(mine, lay.n_main, lab_sub, bias, 0, 2, None)]
        stream((mine, lay.n_main, 0), tiles, lab_lane, buffers, setter(sums))


def half_blocks(ref_i, ref_j, lab_sub, line, back, at, lab_lane, buffers, put):
    half = ref_j.shape[0] // 2
    grp = lax.axis_index("grp")
    for h in range(2):
        start = pl.multiple_of((h ^ grp) * half, half)
        rows_j = ref_j.at[pl.ds(start, half)]
        sub = lab_sub.at[pl.ds(line + start, half)]
        backs = back.at[pl.ds(line + start, half)]
        lanes = (ref_i.at[pl.ds(h * half, half)], half, at + h * half)
        stream(lanes, [(rows_j, half, sub, None, 0, 1, backs)], lab_lane, buffers, put)


def cross_kernel(lay, mine, other, early, early_j, rows, sums, lab_lane, *refs):
    total, for_other, unfit_ref, lab_sub, bias, back, rows_j, buf_a, buf_b = refs
    is_home = lax.axis_index("cl") == lay.home
    infos = lines_of(lay, other)
    own = lines_of(lay, mine)
    hot = hot_of(lay, own[0])
    lane = lax.broadcasted_iota(jnp.int32, (1, LANES), 1)
    last = (lane < lay.n_fine) & (lax.rem(lane, lay.per_owner) == lay.per_owner - 1)
    last = last & (lax.div(lane, lay.per_owner) != hot)
    unfit = jnp.zeros((1, LANES), jnp.float32)
    for info in infos + own:
        wrong = last & (info >= lay.main)
        differs = (info != hot.astype(jnp.float32)) | (info >= lay.n_owner)
        wrong = wrong | ((lane == lay.n_fine) & differs)
        unfit = unfit + jnp.where(wrong, 1.0, 0.0)
    unfit_ref[0, 0] = jnp.max(unfit).astype(jnp.int32)
    total[...] = sums[...]
    buffers = (buf_a, buf_b)

    @pl.when(is_home)
    def _():
        copy_head(lay, other, rows_j)
        first_labels(lay, infos, lab_sub)
        back[...] = jnp.zeros(back.shape, jnp.float32)
        size = lay.n_early
        blocks_i = [rows.at[pl.ds(start, size)] for start in range(0, lay.n_head, size)] + [early]
        blocks_j = [rows_j.at[pl.ds(start, size)] for start in range(0, lay.n_head, size)]
        blocks_j.append(early_j)
        put, n = adder(total), len(blocks_i)
        for i, ref in enumerate(blocks_i):
            tiles = [
                (blocks_j[j], size, lab_sub, None, j * size, 2, back)
                for j in ((i + step) % n for step in range(1, (n + 1) // 2))
            ]
            stream((ref, size, i * size), tiles, lab_lane, buffers, put)
            half_blocks(
                ref, blocks_j[i], lab_sub, i * size, back, i * size, lab_lane, buffers, put
            )
        for_other[...] = jnp.zeros(for_other.shape, jnp.float32)
        turn_sums(back, lay.n_first, for_other, 0)

    @pl.when(jnp.logical_not(is_home))
    def _():
        write_labels(lay, infos, range(lay.n_owner), 0, lay.main, 0, lab_sub, bias)
        tiles = [(other, lay.n_main, lab_sub, bias, 0, 2, None)]
        stream((mine, lay.n_main, 0), tiles, lab_lane, buffers, adder(total))


def late_pairs(lay, i_refs, late_j, late_sub, back, lab_lane, buffers, put):
    rows, early = i_refs
    lates = [(late_j, lay.n_late, late_sub, None, 0, 2, back)]
    stream((rows, lay.n_head, 0), lates, lab_lane, buffers, put)
    stream((early, lay.n_early, lay.n_head), lates, lab_lane, buffers, put)


def inner_late_kernel(lay, mine, early, late, rows, first_lane, *refs):
    sums, lab_lane, late_sub, back, buf_a, buf_b = refs

    @pl.when(lax.axis_index("cl") == lay.home)
    def _():
        late_labels(lay, lines_of(lay, mine), late_sub)
        lab_lane[:, : lay.n_first] = first_lane[...]
        turn_labels(lay, late_sub, lay.n_late, lab_lane, lay.n_first)
        buffers = (buf_a, buf_b)
        back[...] = jnp.zeros(back.shape, jnp.float32)
        put = setter(sums)
        late_pairs(lay, (rows, early), late, late_sub, back, lab_lane, buffers, put)
        tiles = [(late, lay.n_late, late_sub, None, 0, 2, None)]
        stream((late, lay.n_late, lay.n_first), tiles, lab_lane, buffers, put)
        turn_sums(back, lay.n_late, sums, lay.n_first)


def cross_late_kernel(lay, other, early, late, late_j, rows, first_lane, *refs):
    first_sums, first_other, lab_lane, sums, out_ref, total, late_sub, back, buf_a, buf_b = refs
    is_home = lax.axis_index("cl") == lay.home
    grp = lax.axis_index("grp")

    @pl.when(is_home)
    def _():
        infos = lines_of(lay, other)
        write_labels(lay, infos, lay.late, lay.head, lay.rest, 0, late_sub, None)
        total[...] = sums[...]
        total[:, : lay.n_first] += first_sums[...]
        back[...] = jnp.zeros(back.shape, jnp.float32)
        buffers, put = (buf_a, buf_b), adder(total)
        late_pairs(lay, (rows, early), late_j, late_sub, back, lab_lane, buffers, put)
        half_blocks(late, late_j, late_sub, 0, back, lay.n_first, lab_lane, buffers, put)

        def write(line, values):
            for source in range(lay.n_owner):
                start = source * lay.head
                out_ref[2 * source + line, :, : lay.head] = values[:, start : start + lay.head]
            for i, source in enumerate(lay.early + lay.late):
                start = lay.n_head + i * lay.rest
                out_ref[2 * source + line, :, lay.head :] = values[:, start : start + lay.rest]

        write(grp, total[...])
        total[:, : lay.n_first] = first_other[...]
        total[:, lay.n_first :] = jnp.zeros((1, lay.n_late), jnp.float32)
        turn_sums(back, lay.n_late, total, lay.n_first)
        write(1 - grp, total[...])

    @pl.when(jnp.logical_not(is_home))
    def _():
        out_ref[...] = jnp.zeros(out_ref.shape, jnp.float32)
        values = jnp.where(first_lane[...] >= 0, first_sums[...], 1.0)
        for source in range(lay.n_owner):
            start = source * lay.main
            out_ref[2 * source + grp, :, : lay.main] = values[:, start : start + lay.main]


def pair_call(kernel, lay, arrays, out_shape, scratch, out_specs=None, pairs=0):
    width = arrays[0].shape[1]
    buffer = pltpu.VMEM((lay.n_main // 2, WIDE), jnp.float32)
    return pl.pallas_call(
        functools.partial(kernel, lay),
        out_shape=out_shape,
        in_specs=list(vmem_specs(len(arrays))),
        out_specs=out_specs or vmem_specs(len(out_shape)),
        scratch_shapes=list(scratch) + [buffer, buffer],
        compiler_params=pltpu.CompilerParams(vmem_limit_bytes=FAST_LIMIT),
        cost_estimate=pl.CostEstimate(
            flops=2 * pairs * width, bytes_accessed=1, transcendentals=pairs
        ),
    )(*arrays)


def fast_unpack_kernel(values_ref, pos_ref, out_ref):
    pos = pos_ref[...]
    lane = lax.rem(pos, LANES)
    line = lax.div(pos, LANES)
    out = jnp.ones(pos.shape, jnp.float32)
    per = values_ref.shape[2] // LANES
    for r in range(values_ref.shape[0] // 2 * per):
        owner, part = r // per, slice(r % per * LANES, (r % per + 1) * LANES)
        table = values_ref[2 * owner, :, part] + values_ref[2 * owner + 1, :, part]
        found = jnp.take_along_axis(jnp.broadcast_to(table, pos.shape), lane, axis=1)
        out = jnp.where(line == r, found, out)
    out_ref[...] = jnp.log(out)


def fast_unpack(values, pos):
    vmem = pl.BlockSpec(memory_space=pltpu.VMEM)
    return pl.pallas_call(
        fast_unpack_kernel,
        out_shape=jax.ShapeDtypeStruct(pos.shape, jnp.float32),
        in_specs=[vmem, vmem],
        out_specs=vmem,
    )(values, pos)


def general(embeddings, labels, owner_map):
    n_owner = lax.axis_size("cl")
    capacity = SLOTS // n_owner
    rows, width = embeddings.shape
    packed, pos, counts = pack(embeddings, labels, owner_map, n_owner, capacity)
    counts = lax.all_gather(counts, ("cl", "grp"), tiled=True)
    mine = lax.all_to_all(
        packed.reshape(n_owner, capacity, width), "cl", split_axis=0, concat_axis=0, tiled=True
    ).reshape(SLOTS, width)
    other = lax.ppermute(mine, "grp", [(0, 1), (1, 0)])
    results = log_counts(counts, mine, other, n_owner, capacity)
    returned = lax.all_to_all(
        results.reshape(n_owner, capacity), "cl", split_axis=0, concat_axis=0, tiled=True
    )
    return unpack(returned.reshape(SLOTS), pos).reshape(rows)


def body(embeddings, labels, owner_map):
    n_owner = lax.axis_size("cl")
    capacity = SLOTS // n_owner
    rows, width = embeddings.shape
    n_fine = owner_map.shape[0]
    main = -(-(rows // n_owner * 9 // 8) // 16) * 16
    if n_owner != 8 or main >= capacity or n_fine >= LANES:
        return general(embeddings, labels, owner_map)
    home = 2
    lay = Layout(n_owner, n_fine, capacity, main, home)
    packed, extra, pos = place_rows(embeddings, labels, owner_map, lay)

    def hop(x, pairs):
        return lax.ppermute(x, "cl", pairs)

    def swap(x):
        return lax.ppermute(x, "grp", [(0, 1), (1, 0)])

    both = lay_out([extra, hop(extra, [(6, 4), (7, 5)])])
    early = [extra if s == home else hop(extra, [(s, home)]) for s in lay.early]
    early = lay_out(early, home)
    mine = lax.all_to_all(
        packed.reshape(n_owner, main, width), "cl", split_axis=0, concat_axis=0, tiled=True
    ).reshape(n_owner * main, width)
    mine = after(mine, early, both)
    other, early_j = swap(mine), swap(early)
    late = [hop(both, [(s, home)]) for s in (4, 5)]

    def array(shape, dtype=jnp.float32):
        return jax.ShapeDtypeStruct(shape, dtype)

    def scratch(shape):
        return pltpu.VMEM(shape, jnp.float32)

    row, long_row = array((1, lay.n_first)), array((1, lay.n_all))
    bias = scratch((lay.n_main, LANES))
    heads = array((lay.n_head, width), jnp.bfloat16)
    late_side, first_side = scratch((lay.n_late, LANES)), scratch((lay.n_first, LANES))
    sums, first_lane, heads_i = pair_call(
        inner_kernel, lay, (mine, early), (row, row, heads), (first_side, bias, first_side)
    )
    specs = vmem_specs(2) + (pl.BlockSpec(memory_space=pltpu.SMEM),)
    sums, first_other, unfit = pair_call(
        cross_kernel,
        lay,
        (mine, other, early, early_j, heads_i, sums, first_lane),
        (row, row, array((1, 1), jnp.int32)),
        (first_side, bias, first_side, pltpu.VMEM(heads.shape, heads.dtype)),
        specs,
    )
    late = lay_out(late, home, (sums,))
    late_j = swap(late)
    late_sums, lane = pair_call(
        inner_late_kernel,
        lay,
        (mine, early, late, heads_i, first_lane),
        (long_row, long_row),
        (late_side, late_side),
        pairs=lay.n_late * (lay.n_all + lay.n_first),
    )
    (results,) = pair_call(
        cross_late_kernel,
        lay,
        (other, early, late, late_j, heads_i, first_lane, sums, first_other, lane, late_sums),
        (array((2 * n_owner, 1, capacity)),),
        (scratch(long_row.shape), late_side, late_side),
    )
    returned = lax.all_to_all(
        results, ("cl", "grp"), split_axis=0, concat_axis=0, tiled=True
    )
    return lax.cond(
        unfit[0, 0] == 0,
        lambda: fast_unpack(returned, pos).reshape(rows),
        lambda: general(embeddings, labels, owner_map),
    )


def solution(mesh):
    return jax.shard_map(
        body,
        mesh=mesh,
        in_specs=(P(("parts", "cl", "grp"), None), P(("parts", "cl", "grp")), P("parts")),
        out_specs=P(("parts", "cl", "grp")),
        check_vma=False,
    )
```

```python
import functools
import math

import jax
import jax.numpy as jnp
from jax import lax
from jax.experimental import pallas as pl
from jax.experimental.pallas import tpu as pltpu
from jax.sharding import PartitionSpec as P

SLOTS = 2048

temper = 0.2
neighbour_factor = 0.5
epsilon = 1e-06

LANES = 128
SCALE = math.log2(math.e) / temper
NEIGHBOUR = math.log2(neighbour_factor)
DEAD = -1e30
VMEM_LIMIT = 48 * 1024 * 1024
FAST_LIMIT = 16 * 1024 * 1024
WIDE = 512
INFO = 16


def column_of(row):
    pieces = []
    for start in range(0, row.shape[1], LANES):
        width = min(LANES, row.shape[1] - start)
        shape = (width, width)
        diagonal = lax.broadcasted_iota(jnp.int32, shape, 0) == lax.broadcasted_iota(
            jnp.int32, shape, 1
        )
        piece = jnp.broadcast_to(row[:, start : start + width], shape)
        pieces.append(jnp.sum(jnp.where(diagonal, piece, 0.0), axis=1, keepdims=True))
    return jnp.concatenate(pieces, axis=0)


def row_of(column):
    n = column.shape[0]
    diagonal = lax.broadcasted_iota(jnp.int32, (n, n), 0) == lax.broadcasted_iota(
        jnp.int32, (n, n), 1
    )
    return jnp.sum(jnp.where(diagonal, column, 0.0), axis=0, keepdims=True)


def pack_kernel(n_owner, capacity, x_ref, lab_ref, map_ref, out_ref, pos_ref, cnt_ref, unit, pos_row):
    rows = x_ref.shape[0]
    n_fine = map_ref.shape[1]
    per_owner = n_fine // n_owner
    owner_row = map_ref[...].astype(jnp.float32)
    fine_row = lax.broadcasted_iota(jnp.int32, (1, n_fine), 1).astype(jnp.float32)
    key_row = owner_row * n_fine + fine_row
    key_col = column_of(key_row)
    sorted_col = jnp.sum(jnp.where(key_row < key_col, 1.0, 0.0), axis=1, keepdims=True)
    lab = lab_ref[...].astype(jnp.float32)
    lab_row = jnp.concatenate([lab[b : b + 1, :] for b in range(lab.shape[0])], axis=1)
    fine_col = lax.broadcasted_iota(jnp.int32, (n_fine, rows), 0).astype(jnp.float32)
    fine_id = jnp.sum(jnp.where(fine_col == lab_row, sorted_col, 0.0), axis=0, keepdims=True)
    counts_col = jnp.sum(jnp.where(fine_col == fine_id, 1.0, 0.0), axis=1, keepdims=True)
    cnt_ref[...] = row_of(counts_col).astype(jnp.int32)
    coarse = jnp.floor((fine_id + 0.5) * (1.0 / per_owner))
    before = jnp.sum(
        jnp.where(fine_col < coarse * per_owner, counts_col, 0.0), axis=0, keepdims=True
    )
    index = lax.broadcasted_iota(jnp.int32, (1, rows), 1).astype(jnp.float32)
    row_key = fine_id * rows + index
    rank = jnp.zeros((1, rows), jnp.float32)
    for start in range(0, rows, LANES):
        other = column_of(row_key[:, start : start + LANES])
        rank = rank + jnp.sum(jnp.where(other < row_key, 1.0, 0.0), axis=0, keepdims=True)
    pos = (coarse * capacity + rank - before).astype(jnp.int32)
    pos_row[...] = pos
    pos_ref[...] = jnp.concatenate(
        [pos[:, start : start + LANES] for start in range(0, rows, LANES)], axis=0
    )
    x = x_ref[...].astype(jnp.float32)
    squares = jnp.sum(x * x, axis=1, keepdims=True)
    unit[...] = (x * lax.rsqrt(squares + epsilon)).astype(jnp.bfloat16)

    step = 256

    @pl.loop(0, out_ref.shape[0] // step)
    def _(block):
        slot = lax.broadcasted_iota(jnp.int32, (step, rows), 0) + block * step
        chosen = jnp.where(slot == pos_row[...], 1.0, 0.0).astype(jnp.bfloat16)
        packed = jnp.dot(chosen, unit[...], preferred_element_type=jnp.float32)
        out_ref[pl.ds(pl.multiple_of(block * step, step), step), :] = packed.astype(jnp.bfloat16)


def pack(embeddings, labels, owner_map, n_owner, capacity):
    rows, width = embeddings.shape
    n_fine = owner_map.shape[0]
    total = n_owner * capacity
    vmem = pl.BlockSpec(memory_space=pltpu.VMEM)
    return pl.pallas_call(
        functools.partial(pack_kernel, n_owner, capacity),
        out_shape=(
            jax.ShapeDtypeStruct((total, width), jnp.bfloat16),
            jax.ShapeDtypeStruct((rows // LANES, LANES), jnp.int32),
            jax.ShapeDtypeStruct((1, n_fine), jnp.int32),
        ),
        in_specs=[vmem] * 3,
        out_specs=(vmem, vmem, vmem),
        scratch_shapes=[pltpu.VMEM((rows, width), jnp.bfloat16), pltpu.VMEM((1, rows), jnp.int32)],
        compiler_params=pltpu.CompilerParams(vmem_limit_bytes=VMEM_LIMIT),
    )(embeddings, labels.reshape(rows // LANES, LANES), owner_map.reshape(1, n_fine))


def counts_kernel(n_owner, capacity, cnt_ref, mine_ref, other_ref, out_ref, lab_lane, lab_sub, bias):
    total = mine_ref.shape[0]
    per_owner = cnt_ref.shape[1] // n_owner
    me = lax.axis_index("cl")
    grp = lax.axis_index("grp")
    n_grp = lax.axis_size("grp")
    for member in range(2):
        for source in range(n_owner):
            line = source * n_grp + lax.rem(grp + member, n_grp)
            edges = []
            edge = jnp.int32(0)
            for f in range(per_owner):
                edge = edge + cnt_ref[line, me * per_owner + f]
                edges.append(edge)
            down = lax.broadcasted_iota(jnp.int32, (capacity, LANES), 0)
            label = jnp.zeros((capacity, LANES), jnp.int32)
            for edge in edges:
                label = label + jnp.where(down >= edge, 1, 0)
            start = (member * n_owner + source) * capacity
            lab_sub[start : start + capacity, :] = label
            bias[start : start + capacity, :] = jnp.where(
                label < per_owner, NEIGHBOUR - SCALE, DEAD
            )
            if member == 0:
                across = lax.broadcasted_iota(jnp.int32, (1, capacity), 1)
                label = jnp.zeros((1, capacity), jnp.int32)
                for edge in edges:
                    label = label + jnp.where(across >= edge, 1, 0)
                lab_lane[:, source * capacity : (source + 1) * capacity] = jnp.where(
                    label < per_owner, label, -1
                )
    wide, deep = min(512, total), min(256, total)

    @pl.loop(0, total // wide)
    def _(block):
        columns = pl.ds(pl.multiple_of(block * wide, wide), wide)
        rows_i = mine_ref[columns, :]
        label_i = lab_lane[:, columns]

        def add(ref, offset):
            def step(j, acc):
                start = pl.multiple_of(j * deep, deep)
                scores = lax.dot_general(
                    ref[pl.ds(start, deep), :],
                    rows_i,
                    (((1,), (1,)), ((), ())),
                    preferred_element_type=jnp.float32,
                )
                place = pl.ds(pl.multiple_of(start + offset, deep), deep)
                label_j = lab_sub[place, :]
                bias_j = bias[place, :]
                repeat = wide // LANES
                label_j = jnp.concatenate([label_j] * repeat, axis=1)
                bias_j = jnp.concatenate([bias_j] * repeat, axis=1)
                shift = jnp.where(label_j == label_i, -SCALE, bias_j)
                terms = jnp.exp2(scores * SCALE + shift)
                return acc + jnp.sum(terms.reshape(deep // 8, 8, wide), axis=0)

            return step

        acc = jnp.zeros((8, wide), jnp.float32)
        acc = lax.fori_loop(0, total // deep, add(mine_ref, 0), acc, unroll=2)
        acc = lax.fori_loop(0, total // deep, add(other_ref, total), acc, unroll=2)
        totals = jnp.sum(acc, axis=0, keepdims=True)
        out_ref[:, columns] = jnp.log(jnp.where(label_i >= 0, totals, 1.0))


def log_counts(counts, mine, other, n_owner, capacity):
    total = mine.shape[0]
    vmem = pl.BlockSpec(memory_space=pltpu.VMEM)
    return pl.pallas_call(
        functools.partial(counts_kernel, n_owner, capacity),
        out_shape=jax.ShapeDtypeStruct((1, total), jnp.float32),
        in_specs=[pl.BlockSpec(memory_space=pltpu.SMEM), vmem, vmem],
        out_specs=vmem,
        scratch_shapes=[
            pltpu.VMEM((1, total), jnp.int32),
            pltpu.VMEM((2 * total, LANES), jnp.int32),
            pltpu.VMEM((2 * total, LANES), jnp.float32),
        ],
        compiler_params=pltpu.CompilerParams(vmem_limit_bytes=VMEM_LIMIT),
    )(counts, mine, other)


def unpack_kernel(values_ref, pos_ref, out_ref):
    pos = pos_ref[...]
    lane = lax.rem(pos, LANES)
    line = lax.div(pos, LANES)
    out = jnp.zeros(pos.shape, jnp.float32)
    for r in range(values_ref.shape[0]):
        table = jnp.broadcast_to(values_ref[r : r + 1, :], pos.shape)
        found = jnp.take_along_axis(table, lane, axis=1)
        out = jnp.where(line == r, found, out)
    out_ref[...] = out


def unpack(values, pos):
    vmem = pl.BlockSpec(memory_space=pltpu.VMEM)
    return pl.pallas_call(
        unpack_kernel,
        out_shape=jax.ShapeDtypeStruct(pos.shape, jnp.float32),
        in_specs=[vmem, vmem],
        out_specs=vmem,
    )(values.reshape(-1, LANES), pos)


def swapped(x, first, second):
    return jnp.where(x == first, second, jnp.where(x == second, first, x))


def place_kernel(lay, x_hbm, lab_hbm, map_hbm, *refs):
    main_hbm, tail_ref, pos_ref, x_ref, lab_ref, map_ref, unit, main_ref, sems = refs
    n_owner, capacity, main, home = lay.n_owner, lay.capacity, lay.main, lay.home
    copies = [
        pltpu.make_async_copy(src, dst, sems.at[i])
        for i, (src, dst) in enumerate(((x_hbm, x_ref), (lab_hbm, lab_ref), (map_hbm, map_ref)))
    ]
    for copy in copies:
        copy.start()
    rows, width = x_ref.shape
    n_fine = map_ref.shape[1]
    per_owner = n_fine // n_owner
    copies[1].wait()
    copies[2].wait()
    owner_row = map_ref[...].astype(jnp.float32)
    fine_row = lax.broadcasted_iota(jnp.int32, (1, n_fine), 1).astype(jnp.float32)
    key_row = owner_row * n_fine + fine_row
    key_col = column_of(key_row)
    sorted_col = jnp.sum(jnp.where(key_row < key_col, 1.0, 0.0), axis=1, keepdims=True)
    lab = lab_ref[...].astype(jnp.float32)
    lab_row = jnp.concatenate([lab[b : b + 1, :] for b in range(lab.shape[0])], axis=1)
    fine_col = lax.broadcasted_iota(jnp.int32, (n_fine, rows), 0).astype(jnp.float32)
    fine_id = jnp.sum(jnp.where(fine_col == lab_row, sorted_col, 0.0), axis=0, keepdims=True)
    counts_col = jnp.sum(jnp.where(fine_col == fine_id, 1.0, 0.0), axis=1, keepdims=True)
    coarse = jnp.floor((fine_id + 0.5) * (1.0 / per_owner))
    first = coarse * per_owner
    before = jnp.sum(jnp.where(fine_col < first, counts_col, 0.0), axis=0, keepdims=True)
    upto = jnp.sum(jnp.where(fine_col < first + per_owner, counts_col, 0.0), axis=0, keepdims=True)
    full = jnp.min(
        jnp.where(upto - before == capacity, coarse, float(n_owner)), axis=1, keepdims=True
    )
    line = lax.broadcasted_iota(jnp.int32, (n_fine, LANES), 0)
    lane = lax.broadcasted_iota(jnp.int32, (n_fine, LANES), 1)
    inside = (line <= lane) & (lax.div(line, per_owner) == lax.div(lane, per_owner))
    running = jnp.sum(jnp.where(inside, counts_col, 0.0), axis=0, keepdims=True)
    info = jnp.where(lane[:1] < n_fine, running, full)
    index = lax.broadcasted_iota(jnp.int32, (1, rows), 1).astype(jnp.float32)
    row_key = fine_id * rows + index
    rank = jnp.zeros((1, rows), jnp.float32)
    for start in range(0, rows, LANES):
        other = column_of(row_key[:, start : start + LANES])
        rank = rank + jnp.sum(jnp.where(other < row_key, 1.0, 0.0), axis=0, keepdims=True)
    rank = (rank - before).astype(jnp.int32)
    place = swapped(coarse.astype(jnp.int32), full.astype(jnp.int32), home)
    table = place * capacity + rank
    pos_ref[...] = jnp.concatenate(
        [table[:, start : start + LANES] for start in range(0, rows, LANES)], axis=0
    )
    fits = rank < jnp.where(place == home, lay.head, main - 1)
    slot = jnp.where(fits, place * main + rank, -1)
    tail_slot = jnp.where(place == home, rank - lay.head, -1)
    copies[0].wait()
    x = x_ref[...].astype(jnp.float32)
    squares = jnp.sum(x * x, axis=1, keepdims=True)
    unit[...] = (x * lax.rsqrt(squares + epsilon)).astype(jnp.bfloat16)

    def chosen_rows(slot, start, count):
        here = lax.broadcasted_iota(jnp.int32, (count, rows), 0) + start
        chosen = jnp.where(here == slot, 1.0, 0.0).astype(jnp.bfloat16)
        return jnp.dot(chosen, unit[...], preferred_element_type=jnp.float32)

    count = 2 * main
    down = lax.broadcasted_iota(jnp.int32, (count, LANES), 0)
    is_info = lax.rem(down, main) == main - 1
    writes = []
    for i, start in enumerate(range(0, lay.n_main, count)):
        packed = chosen_rows(slot, start, count)
        place = slice(start, start + count)
        main_ref[place, LANES:] = packed[:, LANES:].astype(jnp.bfloat16)
        main_ref[place, :LANES] = jnp.where(is_info, info, packed[:, :LANES]).astype(jnp.bfloat16)
        writes.append(
            pltpu.make_async_copy(
                main_ref.at[pl.ds(start, count)], main_hbm.at[pl.ds(start, count)], sems.at[3 + i]
            )
        )
        writes[-1].start()
    tail_ref[...] = chosen_rows(tail_slot, 0, lay.rest).astype(jnp.bfloat16)
    for write in writes:
        write.wait()


def vmem_specs(count):
    return (pl.BlockSpec(memory_space=pltpu.VMEM),) * count


def place_rows(embeddings, labels, owner_map, lay):
    rows, width = embeddings.shape
    n_fine = owner_map.shape[0]
    lab_shape = (rows // LANES, LANES)
    anywhere = pl.BlockSpec(memory_space=pl.ANY)
    return pl.pallas_call(
        functools.partial(place_kernel, lay),
        out_shape=(
            jax.ShapeDtypeStruct((lay.n_main, width), jnp.bfloat16),
            jax.ShapeDtypeStruct((lay.rest, width), jnp.bfloat16),
            jax.ShapeDtypeStruct(lab_shape, jnp.int32),
        ),
        in_specs=[anywhere] * 3,
        out_specs=(anywhere,) + vmem_specs(2),
        scratch_shapes=[
            pltpu.VMEM((rows, width), jnp.bfloat16),
            pltpu.VMEM(lab_shape, jnp.int32),
            pltpu.VMEM((1, n_fine), jnp.int32),
            pltpu.VMEM((rows, width), jnp.bfloat16),
            pltpu.VMEM((lay.n_main, width), jnp.bfloat16),
            pltpu.SemaphoreType.DMA((3 + lay.n_owner // 2,)),
        ],
        compiler_params=pltpu.CompilerParams(vmem_limit_bytes=FAST_LIMIT),
    )(embeddings, labels.reshape(lab_shape), owner_map.reshape(1, n_fine))


def gate_kernel(*refs):
    pass


def after(rows, *there):
    return pl.pallas_call(
        gate_kernel,
        out_shape=jax.ShapeDtypeStruct(rows.shape, rows.dtype),
        in_specs=list(vmem_specs(1 + len(there))),
        out_specs=vmem_specs(1)[0],
        input_output_aliases={0: 0},
        compiler_params=pltpu.CompilerParams(vmem_limit_bytes=FAST_LIMIT),
    )(rows, *there)


def lay_out_kernel(n_arrays, home, *refs):
    chunks, out = refs[:n_arrays], refs[-1]

    def copy():
        start = 0
        for chunk in chunks:
            out[start : start + chunk.shape[0], :] = chunk[...]
            start += chunk.shape[0]

    if home is None:
        copy()
    else:
        pl.when(lax.axis_index("cl") == home)(copy)


def lay_out(chunks, home=None, waits=()):
    rows, width = sum(x.shape[0] for x in chunks), chunks[0].shape[1]
    return pl.pallas_call(
        functools.partial(lay_out_kernel, len(chunks), home),
        out_shape=jax.ShapeDtypeStruct((rows, width), jnp.bfloat16),
        in_specs=list(vmem_specs(len(chunks) + len(waits))),
        out_specs=vmem_specs(1)[0],
        compiler_params=pltpu.CompilerParams(vmem_limit_bytes=FAST_LIMIT),
    )(*chunks, *waits)


class Layout:
    early, late = (0, 1, 2, 3), (4, 6, 5, 7)

    def __init__(self, n_owner, n_fine, capacity, main, home):
        self.n_owner, self.n_fine, self.capacity = n_owner, n_fine, capacity
        self.main, self.home = main, home
        self.head = main - INFO
        self.rest = capacity - self.head
        self.per_owner = n_fine // n_owner
        self.n_main = n_owner * main
        self.n_head = n_owner * self.head
        self.n_early = len(self.early) * self.rest
        self.n_late = len(self.late) * self.rest
        self.n_first = self.n_head + self.n_early
        self.n_all = self.n_first + self.n_late


def info_line(lay, main_ref, source):
    end = (source + 1) * lay.main
    return main_ref[end - INFO : end, :LANES].astype(jnp.float32)[INFO - 1 :]


def lines_of(lay, main_ref):
    return [info_line(lay, main_ref, source) for source in range(lay.n_owner)]


def hot_of(lay, info):
    lane = lax.broadcasted_iota(jnp.int32, (1, LANES), 1)
    hot = jnp.max(jnp.where(lane == lay.n_fine, info, 0.0), axis=1, keepdims=True)
    return hot.astype(jnp.int32)


def write_labels(lay, infos, sources, first, count, at, lab_sub, bias):
    cluster = swapped(lax.axis_index("cl"), hot_of(lay, infos[0]), lay.home)
    lane = lax.broadcasted_iota(jnp.int32, (1, LANES), 1)
    is_edge = lax.div(lane, lay.per_owner) == cluster
    for i, source in enumerate(sources):
        edges = jnp.where(is_edge, infos[source], 2.0 * lay.capacity)
        slot = lax.broadcasted_iota(jnp.int32, (count, LANES), 0) + first
        label = jnp.where(slot.astype(jnp.float32) >= edges, 1.0, 0.0)
        label = jnp.broadcast_to(jnp.sum(label, axis=1, keepdims=True), (count, LANES))
        start = at + i * count
        lab_sub[start : start + count, :] = label
        if bias is not None:
            bias[start : start + count, :] = jnp.where(
                label < lay.per_owner, NEIGHBOUR - SCALE, DEAD
            )


def first_labels(lay, infos, lab_sub):
    write_labels(lay, infos, range(lay.n_owner), 0, lay.head, 0, lab_sub, None)
    write_labels(lay, infos, lay.early, lay.head, lay.rest, lay.n_head, lab_sub, None)


def late_labels(lay, infos, lab_sub):
    write_labels(lay, infos, lay.late, lay.head, lay.rest, 0, lab_sub, None)


def turn_labels(lay, lab_sub, count, lab_lane, at):
    for i in range(0, count, LANES):
        block = jnp.transpose(lab_sub[i : i + LANES, :])[:1]
        lab_lane[:, at + i : at + i + LANES] = jnp.where(block < lay.per_owner, block, -1.0)


def copy_head(lay, main_ref, rows):
    for source in range(lay.n_owner):
        rows[source * lay.head : (source + 1) * lay.head, :] = main_ref[
            source * lay.main : source * lay.main + lay.head, :
        ]


def pieces(count, parts):
    return [(i * (count // parts), count // parts) for i in range(parts)]


def stream(lanes, tiles, lab_lane, buffers, put):
    rows_i, count, at = lanes
    step = 32
    tiles = [
        (ref, s, d, lab_sub, bias, line + s, back)
        for ref, n, lab_sub, bias, line, parts, back in tiles
        for s, d in pieces(n, parts)
    ]

    def scores_to(buffer, tile, rows):
        ref, start, deep = tile[:3]
        buffer[:deep, : rows.shape[0]] = lax.dot_general(
            ref[start : start + deep, :],
            rows,
            (((1,), (1,)), ((), ())),
            preferred_element_type=jnp.float32,
        )

    def run(start, blocks, wide):
        repeat = wide // LANES

        def rows_of(block):
            return rows_i[pl.ds(pl.multiple_of(start + block * wide, LANES), wide), :]

        scores_to(buffers[0], tiles[0], rows_of(0))

        def one_block(block):
            here = rows_of(block)
            place = pl.ds(pl.multiple_of(at + start + block * wide, LANES), wide)
            label_i = lab_lane[:, place]
            acc = jnp.zeros((8, wide), jnp.float32)
            for i, (_, _, deep, lab_sub, bias, line, back) in enumerate(tiles):
                if i + 1 < len(tiles):
                    scores_to(buffers[(i + 1) % 2], tiles[i + 1], here)
                elif blocks > 1:

                    @pl.when(block + 1 < blocks)
                    def _():
                        scores_to(buffers[0], tiles[0], rows_of(block + 1))

                buffer = buffers[i % 2]
                for c in range(0, deep, step):
                    part = slice(line + c, line + c + step)
                    label_j = jnp.concatenate([lab_sub[part, :]] * repeat, axis=1)
                    if bias is None:
                        bias_j = NEIGHBOUR - SCALE
                    else:
                        bias_j = jnp.concatenate([bias[part, :]] * repeat, axis=1)
                    shift = jnp.where(label_j == label_i, -SCALE, bias_j)
                    terms = jnp.exp2(buffer[c : c + step, :wide] * SCALE + shift)
                    acc = acc + jnp.sum(terms.reshape(step // 8, 8, wide), axis=0)
                    if back is not None:
                        across = terms[:, :LANES]
                        for r in range(1, repeat):
                            across = across + terms[:, r * LANES : (r + 1) * LANES]
                        back[part, :] += across
            put(place, jnp.sum(acc, axis=0, keepdims=True))

        if blocks == 1:
            one_block(0)
        else:
            pl.loop(0, blocks)(one_block)

    if count >= WIDE:
        run(0, count // WIDE, WIDE)
    if count % WIDE:
        run(count - count % WIDE, 1, count % WIDE)


def turn_sums(back, count, sums, at):
    for i in range(0, count, LANES):
        block = jnp.transpose(back[i : i + LANES, :])
        sums[:, at + i : at + i + LANES] += jnp.sum(block, axis=0, keepdims=True)


def setter(ref):
    def put(place, values):
        ref[:, place] = values

    return put


def adder(ref):
    def put(place, values):
        ref[:, place] += values

    return put


def inner_kernel(lay, mine, early, sums, lab_lane, rows, lab_sub, bias, back, buf_a, buf_b):
    is_home = lax.axis_index("cl") == lay.home
    infos = lines_of(lay, mine)
    buffers = (buf_a, buf_b)

    @pl.when(is_home)
    def _():
        copy_head(lay, mine, rows)
        first_labels(lay, infos, lab_sub)
        turn_labels(lay, lab_sub, lay.n_first, lab_lane, 0)
        back[...] = jnp.zeros(back.shape, jnp.float32)
        size = lay.n_early
        blocks = [(rows.at[pl.ds(start, size)], start) for start in range(0, lay.n_head, size)]
        blocks.append((early, lay.n_head))
        for i, (ref, at) in enumerate(blocks):
            tiles = [
                (ref_j, size, lab_sub, None, at_j, 2, None if at_j == at else back)
                for ref_j, at_j in blocks[i:]
            ]
            stream((ref, size, at), tiles, lab_lane, buffers, setter(sums))
        turn_sums(back, lay.n_first, sums, 0)

    @pl.when(jnp.logical_not(is_home))
    def _():
        write_labels(lay, infos, range(lay.n_owner), 0, lay.main, 0, lab_sub, bias)
        turn_labels(lay, lab_sub, lay.n_main, lab_lane, 0)
        tiles = [(mine, lay.n_main, lab_sub, bias, 0, 2, None)]
        stream((mine, lay.n_main, 0), tiles, lab_lane, buffers, setter(sums))


def half_blocks(ref_i, ref_j, lab_sub, line, back, at, lab_lane, buffers, put):
    half = ref_j.shape[0] // 2
    grp = lax.axis_index("grp")
    for h in range(2):
        start = pl.multiple_of((h ^ grp) * half, half)
        rows_j = ref_j.at[pl.ds(start, half)]
        sub = lab_sub.at[pl.ds(line + start, half)]
        backs = back.at[pl.ds(line + start, half)]
        lanes = (ref_i.at[pl.ds(h * half, half)], half, at + h * half)
        stream(lanes, [(rows_j, half, sub, None, 0, 1, backs)], lab_lane, buffers, put)


def cross_kernel(lay, mine, other, early, early_j, rows, sums, lab_lane, *refs):
    total, for_other, unfit_ref, late_sub, late_sub_j, long_lane = refs[:6]
    lab_sub, bias, back, rows_j, buf_a, buf_b = refs[6:]
    is_home = lax.axis_index("cl") == lay.home
    infos = lines_of(lay, other)
    own = lines_of(lay, mine)
    hot = hot_of(lay, own[0])
    lane = lax.broadcasted_iota(jnp.int32, (1, LANES), 1)
    last = (lane < lay.n_fine) & (lax.rem(lane, lay.per_owner) == lay.per_owner - 1)
    last = last & (lax.div(lane, lay.per_owner) != hot)
    unfit = jnp.zeros((1, LANES), jnp.float32)
    for info in infos + own:
        wrong = last & (info >= lay.main)
        differs = (info != hot.astype(jnp.float32)) | (info >= lay.n_owner)
        wrong = wrong | ((lane == lay.n_fine) & differs)
        unfit = unfit + jnp.where(wrong, 1.0, 0.0)
    unfit_ref[0, 0] = jnp.max(unfit).astype(jnp.int32)
    total[...] = sums[...]
    buffers = (buf_a, buf_b)

    @pl.when(is_home)
    def _():
        copy_head(lay, other, rows_j)
        first_labels(lay, infos, lab_sub)
        back[...] = jnp.zeros(back.shape, jnp.float32)
        size = lay.n_early
        blocks_i = [rows.at[pl.ds(start, size)] for start in range(0, lay.n_head, size)] + [early]
        blocks_j = [rows_j.at[pl.ds(start, size)] for start in range(0, lay.n_head, size)]
        blocks_j.append(early_j)
        put, n = adder(total), len(blocks_i)
        for i, ref in enumerate(blocks_i):
            tiles = [
                (blocks_j[j], size, lab_sub, None, j * size, 2, back)
                for j in ((i + step) % n for step in range(1, (n + 1) // 2))
            ]
            stream((ref, size, i * size), tiles, lab_lane, buffers, put)
            half_blocks(
                ref, blocks_j[i], lab_sub, i * size, back, i * size, lab_lane, buffers, put
            )
        write_labels(lay, own, lay.late, lay.head, lay.rest, 0, late_sub, None)
        write_labels(lay, infos, lay.late, lay.head, lay.rest, 0, late_sub_j, None)
        long_lane[:, : lay.n_first] = lab_lane[...]
        turn_labels(lay, late_sub, lay.n_late, long_lane, lay.n_first)
        for_other[...] = jnp.zeros(for_other.shape, jnp.float32)
        turn_sums(back, lay.n_first, for_other, 0)

    @pl.when(jnp.logical_not(is_home))
    def _():
        write_labels(lay, infos, range(lay.n_owner), 0, lay.main, 0, lab_sub, bias)
        tiles = [(other, lay.n_main, lab_sub, bias, 0, 2, None)]
        stream((mine, lay.n_main, 0), tiles, lab_lane, buffers, adder(total))


def late_pairs(lay, i_refs, late_j, late_sub, back, lab_lane, buffers, put):
    rows, early = i_refs
    lates = [(late_j, lay.n_late, late_sub, None, 0, 2, back)]
    stream((rows, lay.n_head, 0), lates, lab_lane, buffers, put)
    stream((early, lay.n_early, lay.n_head), lates, lab_lane, buffers, put)


def inner_late_kernel(lay, early, late, rows, late_sub, lab_lane, sums, back, buf_a, buf_b):
    @pl.when(lax.axis_index("cl") == lay.home)
    def _():
        buffers = (buf_a, buf_b)
        back[...] = jnp.zeros(back.shape, jnp.float32)
        put = setter(sums)
        late_pairs(lay, (rows, early), late, late_sub, back, lab_lane, buffers, put)
        tiles = [(late, lay.n_late, late_sub, None, 0, 2, None)]
        stream((late, lay.n_late, lay.n_first), tiles, lab_lane, buffers, put)
        turn_sums(back, lay.n_late, sums, lay.n_first)


def cross_late_kernel(lay, early, late, late_j, rows, late_sub, lab_lane, first_lane, *refs):
    first_sums, first_other, sums, out_ref, total, back, buf_a, buf_b = refs
    is_home = lax.axis_index("cl") == lay.home
    grp = lax.axis_index("grp")

    @pl.when(is_home)
    def _():
        total[...] = sums[...]
        total[:, : lay.n_first] += first_sums[...]
        back[...] = jnp.zeros(back.shape, jnp.float32)
        buffers, put = (buf_a, buf_b), adder(total)
        late_pairs(lay, (rows, early), late_j, late_sub, back, lab_lane, buffers, put)
        half_blocks(late, late_j, late_sub, 0, back, lay.n_first, lab_lane, buffers, put)

        def write(line, values):
            for source in range(lay.n_owner):
                start = source * lay.head
                out_ref[2 * source + line, :, : lay.head] = values[:, start : start + lay.head]
            for i, source in enumerate(lay.early + lay.late):
                start = lay.n_head + i * lay.rest
                out_ref[2 * source + line, :, lay.head :] = values[:, start : start + lay.rest]

        write(grp, total[...])
        total[:, : lay.n_first] = first_other[...]
        total[:, lay.n_first :] = jnp.zeros((1, lay.n_late), jnp.float32)
        turn_sums(back, lay.n_late, total, lay.n_first)
        write(1 - grp, total[...])

    @pl.when(jnp.logical_not(is_home))
    def _():
        out_ref[...] = jnp.zeros(out_ref.shape, jnp.float32)
        values = jnp.where(first_lane[...] >= 0, first_sums[...], 1.0)
        for source in range(lay.n_owner):
            start = source * lay.main
            out_ref[2 * source + grp, :, : lay.main] = values[:, start : start + lay.main]


def pair_call(kernel, lay, arrays, out_shape, scratch, out_specs=None, pairs=0):
    width = arrays[0].shape[1]
    buffer = pltpu.VMEM((lay.n_main // 2, WIDE), jnp.float32)
    return pl.pallas_call(
        functools.partial(kernel, lay),
        out_shape=out_shape,
        in_specs=list(vmem_specs(len(arrays))),
        out_specs=out_specs or vmem_specs(len(out_shape)),
        scratch_shapes=list(scratch) + [buffer, buffer],
        compiler_params=pltpu.CompilerParams(vmem_limit_bytes=FAST_LIMIT),
        cost_estimate=pl.CostEstimate(
            flops=2 * pairs * width, bytes_accessed=1, transcendentals=pairs
        ),
    )(*arrays)


def fast_unpack_kernel(values_ref, pos_ref, out_ref):
    pos = pos_ref[...]
    lane = lax.rem(pos, LANES)
    line = lax.div(pos, LANES)
    out = jnp.ones(pos.shape, jnp.float32)
    per = values_ref.shape[2] // LANES
    for r in range(values_ref.shape[0] // 2 * per):
        owner, part = r // per, slice(r % per * LANES, (r % per + 1) * LANES)
        table = values_ref[2 * owner, :, part] + values_ref[2 * owner + 1, :, part]
        found = jnp.take_along_axis(jnp.broadcast_to(table, pos.shape), lane, axis=1)
        out = jnp.where(line == r, found, out)
    out_ref[...] = jnp.log(out)


def fast_unpack(values, pos):
    vmem = pl.BlockSpec(memory_space=pltpu.VMEM)
    return pl.pallas_call(
        fast_unpack_kernel,
        out_shape=jax.ShapeDtypeStruct(pos.shape, jnp.float32),
        in_specs=[vmem, vmem],
        out_specs=vmem,
    )(values, pos)


def general(embeddings, labels, owner_map):
    n_owner = lax.axis_size("cl")
    capacity = SLOTS // n_owner
    rows, width = embeddings.shape
    packed, pos, counts = pack(embeddings, labels, owner_map, n_owner, capacity)
    counts = lax.all_gather(counts, ("cl", "grp"), tiled=True)
    mine = lax.all_to_all(
        packed.reshape(n_owner, capacity, width), "cl", split_axis=0, concat_axis=0, tiled=True
    ).reshape(SLOTS, width)
    other = lax.ppermute(mine, "grp", [(0, 1), (1, 0)])
    results = log_counts(counts, mine, other, n_owner, capacity)
    returned = lax.all_to_all(
        results.reshape(n_owner, capacity), "cl", split_axis=0, concat_axis=0, tiled=True
    )
    return unpack(returned.reshape(SLOTS), pos).reshape(rows)


def body(embeddings, labels, owner_map):
    n_owner = lax.axis_size("cl")
    capacity = SLOTS // n_owner
    rows, width = embeddings.shape
    n_fine = owner_map.shape[0]
    main = -(-(rows // n_owner * 9 // 8) // 16) * 16
    if n_owner != 8 or main >= capacity or n_fine >= LANES:
        return general(embeddings, labels, owner_map)
    home = 2
    lay = Layout(n_owner, n_fine, capacity, main, home)
    packed, extra, pos = place_rows(embeddings, labels, owner_map, lay)

    def hop(x, pairs):
        return lax.ppermute(x, "cl", pairs)

    def swap(x):
        return lax.ppermute(x, "grp", [(0, 1), (1, 0)])

    both = lay_out([extra, hop(extra, [(6, 4), (7, 5)])])
    early = [extra if s == home else hop(extra, [(s, home)]) for s in lay.early]
    early = lay_out(early, home)
    mine = lax.all_to_all(
        packed.reshape(n_owner, main, width), "cl", split_axis=0, concat_axis=0, tiled=True
    ).reshape(n_owner * main, width)
    mine = after(mine, early, both)
    other, early_j = swap(mine), swap(early)
    late = [hop(both, [(s, home)]) for s in (4, 5)]

    def array(shape, dtype=jnp.float32):
        return jax.ShapeDtypeStruct(shape, dtype)

    def scratch(shape):
        return pltpu.VMEM(shape, jnp.float32)

    row, long_row = array((1, lay.n_first)), array((1, lay.n_all))
    bias = scratch((lay.n_main, LANES))
    heads = array((lay.n_head, width), jnp.bfloat16)
    late_lines = array((lay.n_late, LANES))
    late_side, first_side = scratch((lay.n_late, LANES)), scratch((lay.n_first, LANES))
    sums, first_lane, heads_i = pair_call(
        inner_kernel, lay, (mine, early), (row, row, heads), (first_side, bias, first_side)
    )
    specs = vmem_specs(2) + (pl.BlockSpec(memory_space=pltpu.SMEM),) + vmem_specs(3)
    sums, first_other, unfit, late_sub, late_sub_j, lane = pair_call(
        cross_kernel,
        lay,
        (mine, other, early, early_j, heads_i, sums, first_lane),
        (row, row, array((1, 1), jnp.int32), late_lines, late_lines, long_row),
        (first_side, bias, first_side, pltpu.VMEM(heads.shape, heads.dtype)),
        specs,
    )
    late = lay_out(late, home, (sums,))
    late_j = swap(late)
    (late_sums,) = pair_call(
        inner_late_kernel,
        lay,
        (early, late, heads_i, late_sub, lane),
        (long_row,),
        (late_side,),
        pairs=lay.n_late * lay.n_all,
    )
    (results,) = pair_call(
        cross_late_kernel,
        lay,
        (early, late, late_j, heads_i, late_sub_j, lane, first_lane, sums, first_other, late_sums),
        (array((2 * n_owner, 1, capacity)),),
        (scratch(long_row.shape), late_side),
    )
    returned = lax.all_to_all(
        results, ("cl", "grp"), split_axis=0, concat_axis=0, tiled=True
    )
    return lax.cond(
        unfit[0, 0] == 0,
        lambda: fast_unpack(returned, pos).reshape(rows),
        lambda: general(embeddings, labels, owner_map),
    )


def solution(mesh):
    return jax.shard_map(
        body,
        mesh=mesh,
        in_specs=(P(("parts", "cl", "grp"), None), P(("parts", "cl", "grp")), P("parts")),
        out_specs=P(("parts", "cl", "grp")),
        check_vma=False,
    )
```

```python
import functools
import math

import jax
import jax.numpy as jnp
from jax import lax
from jax.experimental import pallas as pl
from jax.experimental.pallas import tpu as pltpu
from jax.sharding import PartitionSpec as P

SLOTS = 2048

temper = 0.2
neighbour_factor = 0.5
epsilon = 1e-06

LANES = 128
SCALE = math.log2(math.e) / temper
NEIGHBOUR = math.log2(neighbour_factor)
DEAD = -1e30
VMEM_LIMIT = 48 * 1024 * 1024
FAST_LIMIT = 16 * 1024 * 1024
WIDE = 512
INFO = 16


def column_of(row):
    pieces = []
    for start in range(0, row.shape[1], LANES):
        width = min(LANES, row.shape[1] - start)
        shape = (width, width)
        diagonal = lax.broadcasted_iota(jnp.int32, shape, 0) == lax.broadcasted_iota(
            jnp.int32, shape, 1
        )
        piece = jnp.broadcast_to(row[:, start : start + width], shape)
        pieces.append(jnp.sum(jnp.where(diagonal, piece, 0.0), axis=1, keepdims=True))
    return jnp.concatenate(pieces, axis=0)


def row_of(column):
    n = column.shape[0]
    diagonal = lax.broadcasted_iota(jnp.int32, (n, n), 0) == lax.broadcasted_iota(
        jnp.int32, (n, n), 1
    )
    return jnp.sum(jnp.where(diagonal, column, 0.0), axis=0, keepdims=True)


def pack_kernel(n_owner, capacity, x_ref, lab_ref, map_ref, out_ref, pos_ref, cnt_ref, unit, pos_row):
    rows = x_ref.shape[0]
    n_fine = map_ref.shape[1]
    per_owner = n_fine // n_owner
    owner_row = map_ref[...].astype(jnp.float32)
    fine_row = lax.broadcasted_iota(jnp.int32, (1, n_fine), 1).astype(jnp.float32)
    key_row = owner_row * n_fine + fine_row
    key_col = column_of(key_row)
    sorted_col = jnp.sum(jnp.where(key_row < key_col, 1.0, 0.0), axis=1, keepdims=True)
    lab = lab_ref[...].astype(jnp.float32)
    lab_row = jnp.concatenate([lab[b : b + 1, :] for b in range(lab.shape[0])], axis=1)
    fine_col = lax.broadcasted_iota(jnp.int32, (n_fine, rows), 0).astype(jnp.float32)
    fine_id = jnp.sum(jnp.where(fine_col == lab_row, sorted_col, 0.0), axis=0, keepdims=True)
    counts_col = jnp.sum(jnp.where(fine_col == fine_id, 1.0, 0.0), axis=1, keepdims=True)
    cnt_ref[...] = row_of(counts_col).astype(jnp.int32)
    coarse = jnp.floor((fine_id + 0.5) * (1.0 / per_owner))
    before = jnp.sum(
        jnp.where(fine_col < coarse * per_owner, counts_col, 0.0), axis=0, keepdims=True
    )
    index = lax.broadcasted_iota(jnp.int32, (1, rows), 1).astype(jnp.float32)
    row_key = fine_id * rows + index
    rank = jnp.zeros((1, rows), jnp.float32)
    for start in range(0, rows, LANES):
        other = column_of(row_key[:, start : start + LANES])
        rank = rank + jnp.sum(jnp.where(other < row_key, 1.0, 0.0), axis=0, keepdims=True)
    pos = (coarse * capacity + rank - before).astype(jnp.int32)
    pos_row[...] = pos
    pos_ref[...] = jnp.concatenate(
        [pos[:, start : start + LANES] for start in range(0, rows, LANES)], axis=0
    )
    x = x_ref[...].astype(jnp.float32)
    squares = jnp.sum(x * x, axis=1, keepdims=True)
    unit[...] = (x * lax.rsqrt(squares + epsilon)).astype(jnp.bfloat16)

    step = 256

    @pl.loop(0, out_ref.shape[0] // step)
    def _(block):
        slot = lax.broadcasted_iota(jnp.int32, (step, rows), 0) + block * step
        chosen = jnp.where(slot == pos_row[...], 1.0, 0.0).astype(jnp.bfloat16)
        packed = jnp.dot(chosen, unit[...], preferred_element_type=jnp.float32)
        out_ref[pl.ds(pl.multiple_of(block * step, step), step), :] = packed.astype(jnp.bfloat16)


def pack(embeddings, labels, owner_map, n_owner, capacity):
    rows, width = embeddings.shape
    n_fine = owner_map.shape[0]
    total = n_owner * capacity
    vmem = pl.BlockSpec(memory_space=pltpu.VMEM)
    return pl.pallas_call(
        functools.partial(pack_kernel, n_owner, capacity),
        out_shape=(
            jax.ShapeDtypeStruct((total, width), jnp.bfloat16),
            jax.ShapeDtypeStruct((rows // LANES, LANES), jnp.int32),
            jax.ShapeDtypeStruct((1, n_fine), jnp.int32),
        ),
        in_specs=[vmem] * 3,
        out_specs=(vmem, vmem, vmem),
        scratch_shapes=[pltpu.VMEM((rows, width), jnp.bfloat16), pltpu.VMEM((1, rows), jnp.int32)],
        compiler_params=pltpu.CompilerParams(vmem_limit_bytes=VMEM_LIMIT),
    )(embeddings, labels.reshape(rows // LANES, LANES), owner_map.reshape(1, n_fine))


def counts_kernel(n_owner, capacity, cnt_ref, mine_ref, other_ref, out_ref, lab_lane, lab_sub, bias):
    total = mine_ref.shape[0]
    per_owner = cnt_ref.shape[1] // n_owner
    me = lax.axis_index("cl")
    grp = lax.axis_index("grp")
    n_grp = lax.axis_size("grp")
    for member in range(2):
        for source in range(n_owner):
            line = source * n_grp + lax.rem(grp + member, n_grp)
            edges = []
            edge = jnp.int32(0)
            for f in range(per_owner):
                edge = edge + cnt_ref[line, me * per_owner + f]
                edges.append(edge)
            down = lax.broadcasted_iota(jnp.int32, (capacity, LANES), 0)
            label = jnp.zeros((capacity, LANES), jnp.int32)
            for edge in edges:
                label = label + jnp.where(down >= edge, 1, 0)
            start = (member * n_owner + source) * capacity
            lab_sub[start : start + capacity, :] = label
            bias[start : start + capacity, :] = jnp.where(
                label < per_owner, NEIGHBOUR - SCALE, DEAD
            )
            if member == 0:
                across = lax.broadcasted_iota(jnp.int32, (1, capacity), 1)
                label = jnp.zeros((1, capacity), jnp.int32)
                for edge in edges:
                    label = label + jnp.where(across >= edge, 1, 0)
                lab_lane[:, source * capacity : (source + 1) * capacity] = jnp.where(
                    label < per_owner, label, -1
                )
    wide, deep = min(512, total), min(256, total)

    @pl.loop(0, total // wide)
    def _(block):
        columns = pl.ds(pl.multiple_of(block * wide, wide), wide)
        rows_i = mine_ref[columns, :]
        label_i = lab_lane[:, columns]

        def add(ref, offset):
            def step(j, acc):
                start = pl.multiple_of(j * deep, deep)
                scores = lax.dot_general(
                    ref[pl.ds(start, deep), :],
                    rows_i,
                    (((1,), (1,)), ((), ())),
                    preferred_element_type=jnp.float32,
                )
                place = pl.ds(pl.multiple_of(start + offset, deep), deep)
                label_j = lab_sub[place, :]
                bias_j = bias[place, :]
                repeat = wide // LANES
                label_j = jnp.concatenate([label_j] * repeat, axis=1)
                bias_j = jnp.concatenate([bias_j] * repeat, axis=1)
                shift = jnp.where(label_j == label_i, -SCALE, bias_j)
                terms = jnp.exp2(scores * SCALE + shift)
                return acc + jnp.sum(terms.reshape(deep // 8, 8, wide), axis=0)

            return step

        acc = jnp.zeros((8, wide), jnp.float32)
        acc = lax.fori_loop(0, total // deep, add(mine_ref, 0), acc, unroll=2)
        acc = lax.fori_loop(0, total // deep, add(other_ref, total), acc, unroll=2)
        totals = jnp.sum(acc, axis=0, keepdims=True)
        out_ref[:, columns] = jnp.log(jnp.where(label_i >= 0, totals, 1.0))


def log_counts(counts, mine, other, n_owner, capacity):
    total = mine.shape[0]
    vmem = pl.BlockSpec(memory_space=pltpu.VMEM)
    return pl.pallas_call(
        functools.partial(counts_kernel, n_owner, capacity),
        out_shape=jax.ShapeDtypeStruct((1, total), jnp.float32),
        in_specs=[pl.BlockSpec(memory_space=pltpu.SMEM), vmem, vmem],
        out_specs=vmem,
        scratch_shapes=[
            pltpu.VMEM((1, total), jnp.int32),
            pltpu.VMEM((2 * total, LANES), jnp.int32),
            pltpu.VMEM((2 * total, LANES), jnp.float32),
        ],
        compiler_params=pltpu.CompilerParams(vmem_limit_bytes=VMEM_LIMIT),
    )(counts, mine, other)


def unpack_kernel(values_ref, pos_ref, out_ref):
    pos = pos_ref[...]
    lane = lax.rem(pos, LANES)
    line = lax.div(pos, LANES)
    out = jnp.zeros(pos.shape, jnp.float32)
    for r in range(values_ref.shape[0]):
        table = jnp.broadcast_to(values_ref[r : r + 1, :], pos.shape)
        found = jnp.take_along_axis(table, lane, axis=1)
        out = jnp.where(line == r, found, out)
    out_ref[...] = out


def unpack(values, pos):
    vmem = pl.BlockSpec(memory_space=pltpu.VMEM)
    return pl.pallas_call(
        unpack_kernel,
        out_shape=jax.ShapeDtypeStruct(pos.shape, jnp.float32),
        in_specs=[vmem, vmem],
        out_specs=vmem,
    )(values.reshape(-1, LANES), pos)


def swapped(x, first, second):
    return jnp.where(x == first, second, jnp.where(x == second, first, x))


def place_kernel(lay, x_hbm, lab_hbm, map_hbm, *refs):
    main_hbm, tail_ref, pos_ref, x_ref, lab_ref, map_ref, unit, main_ref, sems = refs
    n_owner, capacity, main, home = lay.n_owner, lay.capacity, lay.main, lay.home
    copies = [
        pltpu.make_async_copy(src, dst, sems.at[i])
        for i, (src, dst) in enumerate(((x_hbm, x_ref), (lab_hbm, lab_ref), (map_hbm, map_ref)))
    ]
    for copy in copies:
        copy.start()
    rows, width = x_ref.shape
    n_fine = map_ref.shape[1]
    per_owner = n_fine // n_owner
    copies[1].wait()
    copies[2].wait()
    owner_row = map_ref[...].astype(jnp.float32)
    fine_row = lax.broadcasted_iota(jnp.int32, (1, n_fine), 1).astype(jnp.float32)
    key_row = owner_row * n_fine + fine_row
    key_col = column_of(key_row)
    sorted_col = jnp.sum(jnp.where(key_row < key_col, 1.0, 0.0), axis=1, keepdims=True)
    lab = lab_ref[...].astype(jnp.float32)
    lab_row = jnp.concatenate([lab[b : b + 1, :] for b in range(lab.shape[0])], axis=1)
    fine_col = lax.broadcasted_iota(jnp.int32, (n_fine, rows), 0).astype(jnp.float32)
    fine_id = jnp.sum(jnp.where(fine_col == lab_row, sorted_col, 0.0), axis=0, keepdims=True)
    counts_col = jnp.sum(jnp.where(fine_col == fine_id, 1.0, 0.0), axis=1, keepdims=True)
    coarse = jnp.floor((fine_id + 0.5) * (1.0 / per_owner))
    first = coarse * per_owner
    before = jnp.sum(jnp.where(fine_col < first, counts_col, 0.0), axis=0, keepdims=True)
    upto = jnp.sum(jnp.where(fine_col < first + per_owner, counts_col, 0.0), axis=0, keepdims=True)
    full = jnp.min(
        jnp.where(upto - before == capacity, coarse, float(n_owner)), axis=1, keepdims=True
    )
    line = lax.broadcasted_iota(jnp.int32, (n_fine, LANES), 0)
    lane = lax.broadcasted_iota(jnp.int32, (n_fine, LANES), 1)
    inside = (line <= lane) & (lax.div(line, per_owner) == lax.div(lane, per_owner))
    running = jnp.sum(jnp.where(inside, counts_col, 0.0), axis=0, keepdims=True)
    info = jnp.where(lane[:1] < n_fine, running, full)
    index = lax.broadcasted_iota(jnp.int32, (1, rows), 1).astype(jnp.float32)
    row_key = fine_id * rows + index
    rank = jnp.zeros((1, rows), jnp.float32)
    for start in range(0, rows, LANES):
        other = column_of(row_key[:, start : start + LANES])
        rank = rank + jnp.sum(jnp.where(other < row_key, 1.0, 0.0), axis=0, keepdims=True)
    rank = (rank - before).astype(jnp.int32)
    place = swapped(coarse.astype(jnp.int32), full.astype(jnp.int32), home)
    table = place * capacity + rank
    pos_ref[...] = jnp.concatenate(
        [table[:, start : start + LANES] for start in range(0, rows, LANES)], axis=0
    )
    fits = rank < jnp.where(place == home, lay.head, main - 1)
    slot = jnp.where(
        fits,
        place * main + rank,
        jnp.where(place == home, lay.n_main + rank - lay.head, -1),
    )
    copies[0].wait()
    x = x_ref[...].astype(jnp.float32)
    squares = jnp.sum(x * x, axis=1, keepdims=True)
    unit[...] = (x * lax.rsqrt(squares + epsilon)).astype(jnp.bfloat16)

    def chosen_rows(slot, start, count):
        here = lax.broadcasted_iota(jnp.int32, (count, rows), 0) + start
        chosen = jnp.where(here == slot, 1.0, 0.0).astype(jnp.bfloat16)
        return jnp.dot(chosen, unit[...], preferred_element_type=jnp.float32)

    count = lay.n_main // 2
    down = lax.broadcasted_iota(jnp.int32, (count, LANES), 0)
    is_info = lax.rem(down, main) == main - 1
    writes = []
    for i, start in enumerate((0, count)):
        packed = chosen_rows(slot, start, count + i * lay.rest)
        place = slice(start, start + count)
        main_ref[place, LANES:] = packed[:count, LANES:].astype(jnp.bfloat16)
        first_lanes = jnp.where(is_info, info, packed[:count, :LANES])
        main_ref[place, :LANES] = first_lanes.astype(jnp.bfloat16)
        writes.append(
            pltpu.make_async_copy(
                main_ref.at[pl.ds(start, count)], main_hbm.at[pl.ds(start, count)], sems.at[3 + i]
            )
        )
        writes[-1].start()
    tail_ref[...] = packed[count:, :].astype(jnp.bfloat16)
    for write in writes:
        write.wait()


def vmem_specs(count):
    return (pl.BlockSpec(memory_space=pltpu.VMEM),) * count


def place_rows(embeddings, labels, owner_map, lay):
    rows, width = embeddings.shape
    n_fine = owner_map.shape[0]
    lab_shape = (rows // LANES, LANES)
    anywhere = pl.BlockSpec(memory_space=pl.ANY)
    return pl.pallas_call(
        functools.partial(place_kernel, lay),
        out_shape=(
            jax.ShapeDtypeStruct((lay.n_main, width), jnp.bfloat16),
            jax.ShapeDtypeStruct((lay.rest, width), jnp.bfloat16),
            jax.ShapeDtypeStruct(lab_shape, jnp.int32),
        ),
        in_specs=[anywhere] * 3,
        out_specs=(anywhere,) + vmem_specs(2),
        scratch_shapes=[
            pltpu.VMEM((rows, width), jnp.bfloat16),
            pltpu.VMEM(lab_shape, jnp.int32),
            pltpu.VMEM((1, n_fine), jnp.int32),
            pltpu.VMEM((rows, width), jnp.bfloat16),
            pltpu.VMEM((lay.n_main, width), jnp.bfloat16),
            pltpu.SemaphoreType.DMA((5,)),
        ],
        compiler_params=pltpu.CompilerParams(vmem_limit_bytes=FAST_LIMIT),
    )(embeddings, labels.reshape(lab_shape), owner_map.reshape(1, n_fine))


def gate_kernel(*refs):
    pass


def after(rows, *there):
    return pl.pallas_call(
        gate_kernel,
        out_shape=jax.ShapeDtypeStruct(rows.shape, rows.dtype),
        in_specs=list(vmem_specs(1 + len(there))),
        out_specs=vmem_specs(1)[0],
        input_output_aliases={0: 0},
        compiler_params=pltpu.CompilerParams(vmem_limit_bytes=FAST_LIMIT),
    )(rows, *there)


def lay_out_kernel(n_arrays, home, *refs):
    chunks, out = refs[:n_arrays], refs[-1]

    def copy():
        start = 0
        for chunk in chunks:
            out[start : start + chunk.shape[0], :] = chunk[...]
            start += chunk.shape[0]

    if home is None:
        copy()
    else:
        pl.when(lax.axis_index("cl") == home)(copy)


def lay_out(chunks, home=None, waits=()):
    rows, width = sum(x.shape[0] for x in chunks), chunks[0].shape[1]
    return pl.pallas_call(
        functools.partial(lay_out_kernel, len(chunks), home),
        out_shape=jax.ShapeDtypeStruct((rows, width), jnp.bfloat16),
        in_specs=list(vmem_specs(len(chunks) + len(waits))),
        out_specs=vmem_specs(1)[0],
        compiler_params=pltpu.CompilerParams(vmem_limit_bytes=FAST_LIMIT),
    )(*chunks, *waits)


class Layout:
    early, late = (0, 1, 2, 3), (5, 7, 4, 6)

    def __init__(self, n_owner, n_fine, capacity, main, home):
        self.n_owner, self.n_fine, self.capacity = n_owner, n_fine, capacity
        self.main, self.home = main, home
        self.head = main - INFO
        self.rest = capacity - self.head
        self.per_owner = n_fine // n_owner
        self.n_main = n_owner * main
        self.n_head = n_owner * self.head
        self.n_early = len(self.early) * self.rest
        self.n_late = len(self.late) * self.rest
        self.n_first = self.n_head + self.n_early
        self.n_all = self.n_first + self.n_late


def info_line(lay, main_ref, source):
    end = (source + 1) * lay.main
    return main_ref[end - INFO : end, :LANES].astype(jnp.float32)[INFO - 1 :]


def lines_of(lay, main_ref):
    return [info_line(lay, main_ref, source) for source in range(lay.n_owner)]


def hot_of(lay, info):
    lane = lax.broadcasted_iota(jnp.int32, (1, LANES), 1)
    hot = jnp.max(jnp.where(lane == lay.n_fine, info, 0.0), axis=1, keepdims=True)
    return hot.astype(jnp.int32)


def write_labels(lay, infos, sources, first, count, at, lab_sub, bias):
    cluster = swapped(lax.axis_index("cl"), hot_of(lay, infos[0]), lay.home)
    lane = lax.broadcasted_iota(jnp.int32, (1, LANES), 1)
    is_edge = lax.div(lane, lay.per_owner) == cluster
    for i, source in enumerate(sources):
        edges = jnp.where(is_edge, infos[source], 2.0 * lay.capacity)
        slot = lax.broadcasted_iota(jnp.int32, (count, LANES), 0) + first
        label = jnp.where(slot.astype(jnp.float32) >= edges, 1.0, 0.0)
        label = jnp.broadcast_to(jnp.sum(label, axis=1, keepdims=True), (count, LANES))
        start = at + i * count
        lab_sub[start : start + count, :] = label
        if bias is not None:
            bias[start : start + count, :] = jnp.where(
                label < lay.per_owner, NEIGHBOUR - SCALE, DEAD
            )


def first_labels(lay, infos, lab_sub):
    write_labels(lay, infos, range(lay.n_owner), 0, lay.head, 0, lab_sub, None)
    write_labels(lay, infos, lay.early, lay.head, lay.rest, lay.n_head, lab_sub, None)


def late_labels(lay, infos, lab_sub):
    write_labels(lay, infos, lay.late, lay.head, lay.rest, 0, lab_sub, None)


def turn_labels(lay, lab_sub, count, lab_lane, at):
    for i in range(0, count, LANES):
        block = jnp.transpose(lab_sub[i : i + LANES, :])[:1]
        lab_lane[:, at + i : at + i + LANES] = jnp.where(block < lay.per_owner, block, -1.0)


def copy_head(lay, main_ref, rows):
    for source in range(lay.n_owner):
        rows[source * lay.head : (source + 1) * lay.head, :] = main_ref[
            source * lay.main : source * lay.main + lay.head, :
        ]


def pieces(count, parts):
    return [(i * (count // parts), count // parts) for i in range(parts)]


def stream(lanes, tiles, lab_lane, buffers, put):
    rows_i, count, at = lanes
    step = 32
    tiles = [
        (ref, s, d, lab_sub, bias, line + s, back)
        for ref, n, lab_sub, bias, line, parts, back in tiles
        for s, d in pieces(n, parts)
    ]

    def scores_to(buffer, tile, rows):
        ref, start, deep = tile[:3]
        buffer[:deep, : rows.shape[0]] = lax.dot_general(
            ref[start : start + deep, :],
            rows,
            (((1,), (1,)), ((), ())),
            preferred_element_type=jnp.float32,
        )

    def run(start, blocks, wide):
        repeat = wide // LANES

        def rows_of(block):
            return rows_i[pl.ds(pl.multiple_of(start + block * wide, LANES), wide), :]

        scores_to(buffers[0], tiles[0], rows_of(0))

        def one_block(block):
            here = rows_of(block)
            place = pl.ds(pl.multiple_of(at + start + block * wide, LANES), wide)
            label_i = lab_lane[:, place]
            acc = jnp.zeros((8, wide), jnp.float32)
            for i, (_, _, deep, lab_sub, bias, line, back) in enumerate(tiles):
                if i + 1 < len(tiles):
                    scores_to(buffers[(i + 1) % 2], tiles[i + 1], here)
                elif blocks > 1:

                    @pl.when(block + 1 < blocks)
                    def _():
                        scores_to(buffers[0], tiles[0], rows_of(block + 1))

                buffer = buffers[i % 2]
                for c in range(0, deep, step):
                    part = slice(line + c, line + c + step)
                    label_j = jnp.concatenate([lab_sub[part, :]] * repeat, axis=1)
                    if bias is None:
                        bias_j = NEIGHBOUR - SCALE
                    else:
                        bias_j = jnp.concatenate([bias[part, :]] * repeat, axis=1)
                    shift = jnp.where(label_j == label_i, -SCALE, bias_j)
                    terms = jnp.exp2(buffer[c : c + step, :wide] * SCALE + shift)
                    acc = acc + jnp.sum(terms.reshape(step // 8, 8, wide), axis=0)
                    if back is not None:
                        across = terms[:, :LANES]
                        for r in range(1, repeat):
                            across = across + terms[:, r * LANES : (r + 1) * LANES]
                        back[part, :] += across
            put(place, jnp.sum(acc, axis=0, keepdims=True))

        if blocks == 1:
            one_block(0)
        else:
            pl.loop(0, blocks)(one_block)

    if count >= WIDE:
        run(0, count // WIDE, WIDE)
    if count % WIDE:
        run(count - count % WIDE, 1, count % WIDE)


def turn_sums(back, count, sums, at):
    for i in range(0, count, LANES):
        block = jnp.transpose(back[i : i + LANES, :])
        sums[:, at + i : at + i + LANES] += jnp.sum(block, axis=0, keepdims=True)


def setter(ref):
    def put(place, values):
        ref[:, place] = values

    return put


def adder(ref):
    def put(place, values):
        ref[:, place] += values

    return put


def inner_kernel(lay, mine, early, sums, lab_lane, rows, lab_sub, bias, back, buf_a, buf_b):
    is_home = lax.axis_index("cl") == lay.home
    infos = lines_of(lay, mine)
    buffers = (buf_a, buf_b)

    @pl.when(is_home)
    def _():
        copy_head(lay, mine, rows)
        first_labels(lay, infos, lab_sub)
        turn_labels(lay, lab_sub, lay.n_first, lab_lane, 0)
        back[...] = jnp.zeros(back.shape, jnp.float32)
        size = lay.n_early
        blocks = [(rows.at[pl.ds(start, size)], start) for start in range(0, lay.n_head, size)]
        blocks.append((early, lay.n_head))
        for i, (ref, at) in enumerate(blocks):
            tiles = [
                (ref_j, size, lab_sub, None, at_j, 2, None if at_j == at else back)
                for ref_j, at_j in blocks[i:]
            ]
            stream((ref, size, at), tiles, lab_lane, buffers, setter(sums))
        turn_sums(back, lay.n_first, sums, 0)

    @pl.when(jnp.logical_not(is_home))
    def _():
        write_labels(lay, infos, range(lay.n_owner), 0, lay.main, 0, lab_sub, bias)
        turn_labels(lay, lab_sub, lay.n_main, lab_lane, 0)
        tiles = [(mine, lay.n_main, lab_sub, bias, 0, 2, None)]
        stream((mine, lay.n_main, 0), tiles, lab_lane, buffers, setter(sums))


def half_blocks(ref_i, ref_j, lab_sub, line, back, at, lab_lane, buffers, put):
    half = ref_j.shape[0] // 2
    grp = lax.axis_index("grp")
    for h in range(2):
        start = pl.multiple_of((h ^ grp) * half, half)
        rows_j = ref_j.at[pl.ds(start, half)]
        sub = lab_sub.at[pl.ds(line + start, half)]
        backs = back.at[pl.ds(line + start, half)]
        lanes = (ref_i.at[pl.ds(h * half, half)], half, at + h * half)
        stream(lanes, [(rows_j, half, sub, None, 0, 1, backs)], lab_lane, buffers, put)


def cross_kernel(lay, mine, other, early, early_j, rows, sums, lab_lane, *refs):
    total, for_other, unfit_ref, late_sub, late_sub_j, long_lane = refs[:6]
    lab_sub, bias, back, rows_j, buf_a, buf_b = refs[6:]
    is_home = lax.axis_index("cl") == lay.home
    infos = lines_of(lay, other)
    own = lines_of(lay, mine)
    hot = hot_of(lay, own[0])
    lane = lax.broadcasted_iota(jnp.int32, (1, LANES), 1)
    last = (lane < lay.n_fine) & (lax.rem(lane, lay.per_owner) == lay.per_owner - 1)
    last = last & (lax.div(lane, lay.per_owner) != hot)
    unfit = jnp.zeros((1, LANES), jnp.float32)
    for info in infos + own:
        wrong = last & (info >= lay.main)
        differs = (info != hot.astype(jnp.float32)) | (info >= lay.n_owner)
        wrong = wrong | ((lane == lay.n_fine) & differs)
        unfit = unfit + jnp.where(wrong, 1.0, 0.0)
    unfit_ref[0, 0] = jnp.max(unfit).astype(jnp.int32)
    total[...] = sums[...]
    buffers = (buf_a, buf_b)

    @pl.when(is_home)
    def _():
        copy_head(lay, other, rows_j)
        first_labels(lay, infos, lab_sub)
        back[...] = jnp.zeros(back.shape, jnp.float32)
        size = lay.n_early
        blocks_i = [rows.at[pl.ds(start, size)] for start in range(0, lay.n_head, size)] + [early]
        blocks_j = [rows_j.at[pl.ds(start, size)] for start in range(0, lay.n_head, size)]
        blocks_j.append(early_j)
        put, n = adder(total), len(blocks_i)
        for i, ref in enumerate(blocks_i):
            tiles = [
                (blocks_j[j], size, lab_sub, None, j * size, 2, back)
                for j in ((i + step) % n for step in range(1, (n + 1) // 2))
            ]
            stream((ref, size, i * size), tiles, lab_lane, buffers, put)
            half_blocks(
                ref, blocks_j[i], lab_sub, i * size, back, i * size, lab_lane, buffers, put
            )
        write_labels(lay, own, lay.late, lay.head, lay.rest, 0, late_sub, None)
        write_labels(lay, infos, lay.late, lay.head, lay.rest, 0, late_sub_j, None)
        long_lane[:, : lay.n_first] = lab_lane[...]
        turn_labels(lay, late_sub, lay.n_late, long_lane, lay.n_first)
        for_other[...] = jnp.zeros(for_other.shape, jnp.float32)
        turn_sums(back, lay.n_first, for_other, 0)

    @pl.when(jnp.logical_not(is_home))
    def _():
        write_labels(lay, infos, range(lay.n_owner), 0, lay.main, 0, lab_sub, bias)
        tiles = [(other, lay.n_main, lab_sub, bias, 0, 2, None)]
        stream((mine, lay.n_main, 0), tiles, lab_lane, buffers, adder(total))


def late_pairs(lay, i_refs, late_j, late_sub, back, lab_lane, buffers, put):
    rows, early = i_refs
    lates = [(late_j, lay.n_late, late_sub, None, 0, 2, back)]
    stream((rows, lay.n_head, 0), lates, lab_lane, buffers, put)
    stream((early, lay.n_early, lay.n_head), lates, lab_lane, buffers, put)


def inner_late_kernel(lay, early, late, rows, late_sub, lab_lane, sums, back, buf_a, buf_b):
    @pl.when(lax.axis_index("cl") == lay.home)
    def _():
        buffers = (buf_a, buf_b)
        back[...] = jnp.zeros(back.shape, jnp.float32)
        put = setter(sums)
        late_pairs(lay, (rows, early), late, late_sub, back, lab_lane, buffers, put)
        tiles = [(late, lay.n_late, late_sub, None, 0, 2, None)]
        stream((late, lay.n_late, lay.n_first), tiles, lab_lane, buffers, put)
        turn_sums(back, lay.n_late, sums, lay.n_first)


def cross_late_kernel(lay, early, late, late_j, rows, late_sub, lab_lane, first_lane, *refs):
    first_sums, first_other, sums, out_ref, total, back, buf_a, buf_b = refs
    is_home = lax.axis_index("cl") == lay.home
    grp = lax.axis_index("grp")

    @pl.when(is_home)
    def _():
        total[...] = sums[...]
        total[:, : lay.n_first] += first_sums[...]
        back[...] = jnp.zeros(back.shape, jnp.float32)
        buffers, put = (buf_a, buf_b), adder(total)
        late_pairs(lay, (rows, early), late_j, late_sub, back, lab_lane, buffers, put)
        half_blocks(late, late_j, late_sub, 0, back, lay.n_first, lab_lane, buffers, put)

        def write(line, values):
            for source in range(lay.n_owner):
                start = source * lay.head
                out_ref[2 * source + line, :, : lay.head] = values[:, start : start + lay.head]
            for i, source in enumerate(lay.early + lay.late):
                start = lay.n_head + i * lay.rest
                out_ref[2 * source + line, :, lay.head :] = values[:, start : start + lay.rest]

        write(grp, total[...])
        total[:, : lay.n_first] = first_other[...]
        total[:, lay.n_first :] = jnp.zeros((1, lay.n_late), jnp.float32)
        turn_sums(back, lay.n_late, total, lay.n_first)
        write(1 - grp, total[...])

    @pl.when(jnp.logical_not(is_home))
    def _():
        out_ref[...] = jnp.zeros(out_ref.shape, jnp.float32)
        values = jnp.where(first_lane[...] >= 0, first_sums[...], 1.0)
        for source in range(lay.n_owner):
            start = source * lay.main
            out_ref[2 * source + grp, :, : lay.main] = values[:, start : start + lay.main]


def pair_call(kernel, lay, arrays, out_shape, scratch, out_specs=None, pairs=0):
    width = arrays[0].shape[1]
    buffer = pltpu.VMEM((lay.n_main // 2, WIDE), jnp.float32)
    return pl.pallas_call(
        functools.partial(kernel, lay),
        out_shape=out_shape,
        in_specs=list(vmem_specs(len(arrays))),
        out_specs=out_specs or vmem_specs(len(out_shape)),
        scratch_shapes=list(scratch) + [buffer, buffer],
        compiler_params=pltpu.CompilerParams(vmem_limit_bytes=FAST_LIMIT),
        cost_estimate=pl.CostEstimate(
            flops=2 * pairs * width, bytes_accessed=1, transcendentals=pairs
        ),
    )(*arrays)


def fast_unpack_kernel(values_ref, pos_ref, out_ref):
    pos = pos_ref[...]
    lane = lax.rem(pos, LANES)
    line = lax.div(pos, LANES)
    out = jnp.ones(pos.shape, jnp.float32)
    per = values_ref.shape[2] // LANES
    for r in range(values_ref.shape[0] // 2 * per):
        owner, part = r // per, slice(r % per * LANES, (r % per + 1) * LANES)
        table = values_ref[2 * owner, :, part] + values_ref[2 * owner + 1, :, part]
        found = jnp.take_along_axis(jnp.broadcast_to(table, pos.shape), lane, axis=1)
        out = jnp.where(line == r, found, out)
    out_ref[...] = jnp.log(out)


def fast_unpack(values, pos):
    vmem = pl.BlockSpec(memory_space=pltpu.VMEM)
    return pl.pallas_call(
        fast_unpack_kernel,
        out_shape=jax.ShapeDtypeStruct(pos.shape, jnp.float32),
        in_specs=[vmem, vmem],
        out_specs=vmem,
    )(values, pos)


def general(embeddings, labels, owner_map):
    n_owner = lax.axis_size("cl")
    capacity = SLOTS // n_owner
    rows, width = embeddings.shape
    packed, pos, counts = pack(embeddings, labels, owner_map, n_owner, capacity)
    counts = lax.all_gather(counts, ("cl", "grp"), tiled=True)
    mine = lax.all_to_all(
        packed.reshape(n_owner, capacity, width), "cl", split_axis=0, concat_axis=0, tiled=True
    ).reshape(SLOTS, width)
    other = lax.ppermute(mine, "grp", [(0, 1), (1, 0)])
    results = log_counts(counts, mine, other, n_owner, capacity)
    returned = lax.all_to_all(
        results.reshape(n_owner, capacity), "cl", split_axis=0, concat_axis=0, tiled=True
    )
    return unpack(returned.reshape(SLOTS), pos).reshape(rows)


def body(embeddings, labels, owner_map):
    n_owner = lax.axis_size("cl")
    capacity = SLOTS // n_owner
    rows, width = embeddings.shape
    n_fine = owner_map.shape[0]
    main = -(-(rows // n_owner * 9 // 8) // 16) * 16
    if n_owner != 8 or main >= capacity or n_fine >= LANES:
        return general(embeddings, labels, owner_map)
    home = 2
    lay = Layout(n_owner, n_fine, capacity, main, home)
    packed, extra, pos = place_rows(embeddings, labels, owner_map, lay)

    def hop(x, pairs):
        return lax.ppermute(x, "cl", pairs)

    def swap(x):
        return lax.ppermute(x, "grp", [(0, 1), (1, 0)])

    both = lay_out([extra, hop(extra, [(6, 4), (7, 5)])])
    early = [extra if s == home else hop(extra, [(s, home)]) for s in lay.early]
    early = lay_out(early, home)
    mine = lax.all_to_all(
        packed.reshape(n_owner, main, width), "cl", split_axis=0, concat_axis=0, tiled=True
    ).reshape(n_owner * main, width)
    mine = after(mine, early, both)
    other, early_j = swap(mine), swap(early)
    late = [hop(both, [(s, home)]) for s in (5, 4)]

    def array(shape, dtype=jnp.float32):
        return jax.ShapeDtypeStruct(shape, dtype)

    def scratch(shape):
        return pltpu.VMEM(shape, jnp.float32)

    row, long_row = array((1, lay.n_first)), array((1, lay.n_all))
    bias = scratch((lay.n_main, LANES))
    heads = array((lay.n_head, width), jnp.bfloat16)
    late_lines = array((lay.n_late, LANES))
    late_side, first_side = scratch((lay.n_late, LANES)), scratch((lay.n_first, LANES))
    sums, first_lane, heads_i = pair_call(
        inner_kernel, lay, (mine, early), (row, row, heads), (first_side, bias, first_side)
    )
    specs = vmem_specs(2) + (pl.BlockSpec(memory_space=pltpu.SMEM),) + vmem_specs(3)
    sums, first_other, unfit, late_sub, late_sub_j, lane = pair_call(
        cross_kernel,
        lay,
        (mine, other, early, early_j, heads_i, sums, first_lane),
        (row, row, array((1, 1), jnp.int32), late_lines, late_lines, long_row),
        (first_side, bias, first_side, pltpu.VMEM(heads.shape, heads.dtype)),
        specs,
    )
    late = lay_out(late, home, (sums,))
    late_j = swap(late)
    (late_sums,) = pair_call(
        inner_late_kernel,
        lay,
        (early, late, heads_i, late_sub, lane),
        (long_row,),
        (late_side,),
        pairs=lay.n_late * lay.n_all,
    )
    (results,) = pair_call(
        cross_late_kernel,
        lay,
        (early, late, late_j, heads_i, late_sub_j, lane, first_lane, sums, first_other, late_sums),
        (array((2 * n_owner, 1, capacity)),),
        (scratch(long_row.shape), late_side),
    )
    returned = lax.all_to_all(
        results, ("cl", "grp"), split_axis=0, concat_axis=0, tiled=True
    )
    return lax.cond(
        unfit[0, 0] == 0,
        lambda: fast_unpack(returned, pos).reshape(rows),
        lambda: general(embeddings, labels, owner_map),
    )


def solution(mesh):
    return jax.shard_map(
        body,
        mesh=mesh,
        in_specs=(P(("parts", "cl", "grp"), None), P(("parts", "cl", "grp")), P("parts")),
        out_specs=P(("parts", "cl", "grp")),
        check_vma=False,
    )
```

```python
import functools
import math

import jax
import jax.numpy as jnp
from jax import lax
from jax.experimental import pallas as pl
from jax.experimental.pallas import tpu as pltpu
from jax.sharding import PartitionSpec as P

SLOTS = 2048

temper = 0.2
neighbour_factor = 0.5
epsilon = 1e-06

LANES = 128
SCALE = math.log2(math.e) / temper
NEIGHBOUR = math.log2(neighbour_factor)
DEAD = -1e30
VMEM_LIMIT = 48 * 1024 * 1024
FAST_LIMIT = 16 * 1024 * 1024
WIDE = 512
INFO = 16


def column_of(row):
    pieces = []
    for start in range(0, row.shape[1], LANES):
        width = min(LANES, row.shape[1] - start)
        shape = (width, width)
        diagonal = lax.broadcasted_iota(jnp.int32, shape, 0) == lax.broadcasted_iota(
            jnp.int32, shape, 1
        )
        piece = jnp.broadcast_to(row[:, start : start + width], shape)
        pieces.append(jnp.sum(jnp.where(diagonal, piece, 0.0), axis=1, keepdims=True))
    return jnp.concatenate(pieces, axis=0)


def row_of(column):
    n = column.shape[0]
    diagonal = lax.broadcasted_iota(jnp.int32, (n, n), 0) == lax.broadcasted_iota(
        jnp.int32, (n, n), 1
    )
    return jnp.sum(jnp.where(diagonal, column, 0.0), axis=0, keepdims=True)


def pack_kernel(n_owner, capacity, x_ref, lab_ref, map_ref, out_ref, pos_ref, cnt_ref, unit, pos_row):
    rows = x_ref.shape[0]
    n_fine = map_ref.shape[1]
    per_owner = n_fine // n_owner
    owner_row = map_ref[...].astype(jnp.float32)
    fine_row = lax.broadcasted_iota(jnp.int32, (1, n_fine), 1).astype(jnp.float32)
    key_row = owner_row * n_fine + fine_row
    key_col = column_of(key_row)
    sorted_col = jnp.sum(jnp.where(key_row < key_col, 1.0, 0.0), axis=1, keepdims=True)
    lab = lab_ref[...].astype(jnp.float32)
    lab_row = jnp.concatenate([lab[b : b + 1, :] for b in range(lab.shape[0])], axis=1)
    fine_col = lax.broadcasted_iota(jnp.int32, (n_fine, rows), 0).astype(jnp.float32)
    fine_id = jnp.sum(jnp.where(fine_col == lab_row, sorted_col, 0.0), axis=0, keepdims=True)
    counts_col = jnp.sum(jnp.where(fine_col == fine_id, 1.0, 0.0), axis=1, keepdims=True)
    cnt_ref[...] = row_of(counts_col).astype(jnp.int32)
    coarse = jnp.floor((fine_id + 0.5) * (1.0 / per_owner))
    before = jnp.sum(
        jnp.where(fine_col < coarse * per_owner, counts_col, 0.0), axis=0, keepdims=True
    )
    index = lax.broadcasted_iota(jnp.int32, (1, rows), 1).astype(jnp.float32)
    row_key = fine_id * rows + index
    rank = jnp.zeros((1, rows), jnp.float32)
    for start in range(0, rows, LANES):
        other = column_of(row_key[:, start : start + LANES])
        rank = rank + jnp.sum(jnp.where(other < row_key, 1.0, 0.0), axis=0, keepdims=True)
    pos = (coarse * capacity + rank - before).astype(jnp.int32)
    pos_row[...] = pos
    pos_ref[...] = jnp.concatenate(
        [pos[:, start : start + LANES] for start in range(0, rows, LANES)], axis=0
    )
    x = x_ref[...].astype(jnp.float32)
    squares = jnp.sum(x * x, axis=1, keepdims=True)
    unit[...] = (x * lax.rsqrt(squares + epsilon)).astype(jnp.bfloat16)

    step = 256

    @pl.loop(0, out_ref.shape[0] // step)
    def _(block):
        slot = lax.broadcasted_iota(jnp.int32, (step, rows), 0) + block * step
        chosen = jnp.where(slot == pos_row[...], 1.0, 0.0).astype(jnp.bfloat16)
        packed = jnp.dot(chosen, unit[...], preferred_element_type=jnp.float32)
        out_ref[pl.ds(pl.multiple_of(block * step, step), step), :] = packed.astype(jnp.bfloat16)


def pack(embeddings, labels, owner_map, n_owner, capacity):
    rows, width = embeddings.shape
    n_fine = owner_map.shape[0]
    total = n_owner * capacity
    vmem = pl.BlockSpec(memory_space=pltpu.VMEM)
    return pl.pallas_call(
        functools.partial(pack_kernel, n_owner, capacity),
        out_shape=(
            jax.ShapeDtypeStruct((total, width), jnp.bfloat16),
            jax.ShapeDtypeStruct((rows // LANES, LANES), jnp.int32),
            jax.ShapeDtypeStruct((1, n_fine), jnp.int32),
        ),
        in_specs=[vmem] * 3,
        out_specs=(vmem, vmem, vmem),
        scratch_shapes=[pltpu.VMEM((rows, width), jnp.bfloat16), pltpu.VMEM((1, rows), jnp.int32)],
        compiler_params=pltpu.CompilerParams(vmem_limit_bytes=VMEM_LIMIT),
    )(embeddings, labels.reshape(rows // LANES, LANES), owner_map.reshape(1, n_fine))


def counts_kernel(n_owner, capacity, cnt_ref, mine_ref, other_ref, out_ref, lab_lane, lab_sub, bias):
    total = mine_ref.shape[0]
    per_owner = cnt_ref.shape[1] // n_owner
    me = lax.axis_index("cl")
    grp = lax.axis_index("grp")
    n_grp = lax.axis_size("grp")
    for member in range(2):
        for source in range(n_owner):
            line = source * n_grp + lax.rem(grp + member, n_grp)
            edges = []
            edge = jnp.int32(0)
            for f in range(per_owner):
                edge = edge + cnt_ref[line, me * per_owner + f]
                edges.append(edge)
            down = lax.broadcasted_iota(jnp.int32, (capacity, LANES), 0)
            label = jnp.zeros((capacity, LANES), jnp.int32)
            for edge in edges:
                label = label + jnp.where(down >= edge, 1, 0)
            start = (member * n_owner + source) * capacity
            lab_sub[start : start + capacity, :] = label
            bias[start : start + capacity, :] = jnp.where(
                label < per_owner, NEIGHBOUR - SCALE, DEAD
            )
            if member == 0:
                across = lax.broadcasted_iota(jnp.int32, (1, capacity), 1)
                label = jnp.zeros((1, capacity), jnp.int32)
                for edge in edges:
                    label = label + jnp.where(across >= edge, 1, 0)
                lab_lane[:, source * capacity : (source + 1) * capacity] = jnp.where(
                    label < per_owner, label, -1
                )
    wide, deep = min(512, total), min(256, total)

    @pl.loop(0, total // wide)
    def _(block):
        columns = pl.ds(pl.multiple_of(block * wide, wide), wide)
        rows_i = mine_ref[columns, :]
        label_i = lab_lane[:, columns]

        def add(ref, offset):
            def step(j, acc):
                start = pl.multiple_of(j * deep, deep)
                scores = lax.dot_general(
                    ref[pl.ds(start, deep), :],
                    rows_i,
                    (((1,), (1,)), ((), ())),
                    preferred_element_type=jnp.float32,
                )
                place = pl.ds(pl.multiple_of(start + offset, deep), deep)
                label_j = lab_sub[place, :]
                bias_j = bias[place, :]
                repeat = wide // LANES
                label_j = jnp.concatenate([label_j] * repeat, axis=1)
                bias_j = jnp.concatenate([bias_j] * repeat, axis=1)
                shift = jnp.where(label_j == label_i, -SCALE, bias_j)
                terms = jnp.exp2(scores * SCALE + shift)
                return acc + jnp.sum(terms.reshape(deep // 8, 8, wide), axis=0)

            return step

        acc = jnp.zeros((8, wide), jnp.float32)
        acc = lax.fori_loop(0, total // deep, add(mine_ref, 0), acc, unroll=2)
        acc = lax.fori_loop(0, total // deep, add(other_ref, total), acc, unroll=2)
        totals = jnp.sum(acc, axis=0, keepdims=True)
        out_ref[:, columns] = jnp.log(jnp.where(label_i >= 0, totals, 1.0))


def log_counts(counts, mine, other, n_owner, capacity):
    total = mine.shape[0]
    vmem = pl.BlockSpec(memory_space=pltpu.VMEM)
    return pl.pallas_call(
        functools.partial(counts_kernel, n_owner, capacity),
        out_shape=jax.ShapeDtypeStruct((1, total), jnp.float32),
        in_specs=[pl.BlockSpec(memory_space=pltpu.SMEM), vmem, vmem],
        out_specs=vmem,
        scratch_shapes=[
            pltpu.VMEM((1, total), jnp.int32),
            pltpu.VMEM((2 * total, LANES), jnp.int32),
            pltpu.VMEM((2 * total, LANES), jnp.float32),
        ],
        compiler_params=pltpu.CompilerParams(vmem_limit_bytes=VMEM_LIMIT),
    )(counts, mine, other)


def unpack_kernel(values_ref, pos_ref, out_ref):
    pos = pos_ref[...]
    lane = lax.rem(pos, LANES)
    line = lax.div(pos, LANES)
    out = jnp.zeros(pos.shape, jnp.float32)
    for r in range(values_ref.shape[0]):
        table = jnp.broadcast_to(values_ref[r : r + 1, :], pos.shape)
        found = jnp.take_along_axis(table, lane, axis=1)
        out = jnp.where(line == r, found, out)
    out_ref[...] = out


def unpack(values, pos):
    vmem = pl.BlockSpec(memory_space=pltpu.VMEM)
    return pl.pallas_call(
        unpack_kernel,
        out_shape=jax.ShapeDtypeStruct(pos.shape, jnp.float32),
        in_specs=[vmem, vmem],
        out_specs=vmem,
    )(values.reshape(-1, LANES), pos)


def swapped(x, first, second):
    return jnp.where(x == first, second, jnp.where(x == second, first, x))


def place_kernel(lay, x_hbm, lab_hbm, map_hbm, *refs):
    main_hbm, tail_ref, pos_ref, x_ref, lab_ref, map_ref, unit, main_ref, sems = refs
    n_owner, capacity, main, home = lay.n_owner, lay.capacity, lay.main, lay.home
    copies = [
        pltpu.make_async_copy(src, dst, sems.at[i])
        for i, (src, dst) in enumerate(((x_hbm, x_ref), (lab_hbm, lab_ref), (map_hbm, map_ref)))
    ]
    for copy in copies:
        copy.start()
    rows, width = x_ref.shape
    n_fine = map_ref.shape[1]
    per_owner = n_fine // n_owner
    for copy in copies:
        copy.wait()
    x = x_ref[...].astype(jnp.float32)
    squares = jnp.sum(x * x, axis=1, keepdims=True)
    unit[...] = (x * lax.rsqrt(squares + epsilon)).astype(jnp.bfloat16)
    owner_row = map_ref[...].astype(jnp.float32)
    fine_row = lax.broadcasted_iota(jnp.int32, (1, n_fine), 1).astype(jnp.float32)
    key_row = owner_row * n_fine + fine_row
    key_col = column_of(key_row)
    sorted_col = jnp.sum(jnp.where(key_row < key_col, 1.0, 0.0), axis=1, keepdims=True)
    lab = lab_ref[...].astype(jnp.float32)
    lab_row = jnp.concatenate([lab[b : b + 1, :] for b in range(lab.shape[0])], axis=1)
    fine_col = lax.broadcasted_iota(jnp.int32, (n_fine, rows), 0).astype(jnp.float32)
    fine_id = jnp.sum(jnp.where(fine_col == lab_row, sorted_col, 0.0), axis=0, keepdims=True)
    counts_col = jnp.sum(jnp.where(fine_col == fine_id, 1.0, 0.0), axis=1, keepdims=True)
    coarse = jnp.floor((fine_id + 0.5) * (1.0 / per_owner))
    first = coarse * per_owner
    before = jnp.sum(jnp.where(fine_col < first, counts_col, 0.0), axis=0, keepdims=True)
    upto = jnp.sum(jnp.where(fine_col < first + per_owner, counts_col, 0.0), axis=0, keepdims=True)
    full = jnp.min(
        jnp.where(upto - before == capacity, coarse, float(n_owner)), axis=1, keepdims=True
    )
    line = lax.broadcasted_iota(jnp.int32, (n_fine, LANES), 0)
    lane = lax.broadcasted_iota(jnp.int32, (n_fine, LANES), 1)
    inside = (line <= lane) & (lax.div(line, per_owner) == lax.div(lane, per_owner))
    running = jnp.sum(jnp.where(inside, counts_col, 0.0), axis=0, keepdims=True)
    info = jnp.where(lane[:1] < n_fine, running, full)
    index = lax.broadcasted_iota(jnp.int32, (1, rows), 1).astype(jnp.float32)
    row_key = fine_id * rows + index
    rank = jnp.zeros((1, rows), jnp.float32)
    for start in range(0, rows, LANES):
        other = column_of(row_key[:, start : start + LANES])
        rank = rank + jnp.sum(jnp.where(other < row_key, 1.0, 0.0), axis=0, keepdims=True)
    rank = (rank - before).astype(jnp.int32)
    place = swapped(coarse.astype(jnp.int32), full.astype(jnp.int32), home)
    table = place * capacity + rank
    pos_ref[...] = jnp.concatenate(
        [table[:, start : start + LANES] for start in range(0, rows, LANES)], axis=0
    )
    fits = rank < jnp.where(place == home, lay.head, main - 1)
    slot = jnp.where(fits, place * main + rank, -1)
    tail_slot = jnp.where(place == home, rank - lay.head, -1)

    def chosen_rows(slot, start, count):
        here = lax.broadcasted_iota(jnp.int32, (count, rows), 0) + start
        chosen = jnp.where(here == slot, 1.0, 0.0).astype(jnp.bfloat16)
        return jnp.dot(chosen, unit[...], preferred_element_type=jnp.float32)

    count = 2 * main
    down = lax.broadcasted_iota(jnp.int32, (count, LANES), 0)
    is_info = lax.rem(down, main) == main - 1
    writes = []
    for i, start in enumerate(range(0, lay.n_main, count)):
        packed = chosen_rows(slot, start, count)
        place = slice(start, start + count)
        main_ref[place, LANES:] = packed[:, LANES:].astype(jnp.bfloat16)
        main_ref[place, :LANES] = jnp.where(is_info, info, packed[:, :LANES]).astype(jnp.bfloat16)
        writes.append(
            pltpu.make_async_copy(
                main_ref.at[pl.ds(start, count)], main_hbm.at[pl.ds(start, count)], sems.at[3 + i]
            )
        )
        writes[-1].start()
    tail_ref[...] = chosen_rows(tail_slot, 0, lay.rest).astype(jnp.bfloat16)
    for write in writes:
        write.wait()


def vmem_specs(count):
    return (pl.BlockSpec(memory_space=pltpu.VMEM),) * count


def place_rows(embeddings, labels, owner_map, lay):
    rows, width = embeddings.shape
    n_fine = owner_map.shape[0]
    lab_shape = (rows // LANES, LANES)
    anywhere = pl.BlockSpec(memory_space=pl.ANY)
    return pl.pallas_call(
        functools.partial(place_kernel, lay),
        out_shape=(
            jax.ShapeDtypeStruct((lay.n_main, width), jnp.bfloat16),
            jax.ShapeDtypeStruct((lay.rest, width), jnp.bfloat16),
            jax.ShapeDtypeStruct(lab_shape, jnp.int32),
        ),
        in_specs=[anywhere] * 3,
        out_specs=(anywhere,) + vmem_specs(2),
        scratch_shapes=[
            pltpu.VMEM((rows, width), jnp.bfloat16),
            pltpu.VMEM(lab_shape, jnp.int32),
            pltpu.VMEM((1, n_fine), jnp.int32),
            pltpu.VMEM((rows, width), jnp.bfloat16),
            pltpu.VMEM((lay.n_main, width), jnp.bfloat16),
            pltpu.SemaphoreType.DMA((3 + lay.n_owner // 2,)),
        ],
        compiler_params=pltpu.CompilerParams(vmem_limit_bytes=FAST_LIMIT),
    )(embeddings, labels.reshape(lab_shape), owner_map.reshape(1, n_fine))


def gate_kernel(*refs):
    pass


def after(rows, *there):
    return pl.pallas_call(
        gate_kernel,
        out_shape=jax.ShapeDtypeStruct(rows.shape, rows.dtype),
        in_specs=list(vmem_specs(1 + len(there))),
        out_specs=vmem_specs(1)[0],
        input_output_aliases={0: 0},
        compiler_params=pltpu.CompilerParams(vmem_limit_bytes=FAST_LIMIT),
    )(rows, *there)


def lay_out_kernel(n_arrays, home, *refs):
    chunks, out = refs[:n_arrays], refs[-1]

    def copy():
        start = 0
        for chunk in chunks:
            out[start : start + chunk.shape[0], :] = chunk[...]
            start += chunk.shape[0]

    if home is None:
        copy()
    else:
        pl.when(lax.axis_index("cl") == home)(copy)


def lay_out(chunks, home=None, waits=()):
    rows, width = sum(x.shape[0] for x in chunks), chunks[0].shape[1]
    return pl.pallas_call(
        functools.partial(lay_out_kernel, len(chunks), home),
        out_shape=jax.ShapeDtypeStruct((rows, width), jnp.bfloat16),
        in_specs=list(vmem_specs(len(chunks) + len(waits))),
        out_specs=vmem_specs(1)[0],
        compiler_params=pltpu.CompilerParams(vmem_limit_bytes=FAST_LIMIT),
    )(*chunks, *waits)


class Layout:
    early, late = (0, 1, 2, 3), (5, 7, 4, 6)

    def __init__(self, n_owner, n_fine, capacity, main, home):
        self.n_owner, self.n_fine, self.capacity = n_owner, n_fine, capacity
        self.main, self.home = main, home
        self.head = main - INFO
        self.rest = capacity - self.head
        self.per_owner = n_fine // n_owner
        self.n_main = n_owner * main
        self.n_head = n_owner * self.head
        self.n_early = len(self.early) * self.rest
        self.n_late = len(self.late) * self.rest
        self.n_first = self.n_head + self.n_early
        self.n_all = self.n_first + self.n_late


def info_line(lay, main_ref, source):
    end = (source + 1) * lay.main
    return main_ref[end - INFO : end, :LANES].astype(jnp.float32)[INFO - 1 :]


def lines_of(lay, main_ref):
    return [info_line(lay, main_ref, source) for source in range(lay.n_owner)]


def hot_of(lay, info):
    lane = lax.broadcasted_iota(jnp.int32, (1, LANES), 1)
    hot = jnp.max(jnp.where(lane == lay.n_fine, info, 0.0), axis=1, keepdims=True)
    return hot.astype(jnp.int32)


def write_labels(lay, infos, sources, first, count, at, lab_sub, bias):
    cluster = swapped(lax.axis_index("cl"), hot_of(lay, infos[0]), lay.home)
    lane = lax.broadcasted_iota(jnp.int32, (1, LANES), 1)
    is_edge = lax.div(lane, lay.per_owner) == cluster
    for i, source in enumerate(sources):
        edges = jnp.where(is_edge, infos[source], 2.0 * lay.capacity)
        slot = lax.broadcasted_iota(jnp.int32, (count, LANES), 0) + first
        label = jnp.where(slot.astype(jnp.float32) >= edges, 1.0, 0.0)
        label = jnp.broadcast_to(jnp.sum(label, axis=1, keepdims=True), (count, LANES))
        start = at + i * count
        lab_sub[start : start + count, :] = label
        if bias is not None:
            bias[start : start + count, :] = jnp.where(
                label < lay.per_owner, NEIGHBOUR - SCALE, DEAD
            )


def first_labels(lay, infos, lab_sub):
    write_labels(lay, infos, range(lay.n_owner), 0, lay.head, 0, lab_sub, None)
    write_labels(lay, infos, lay.early, lay.head, lay.rest, lay.n_head, lab_sub, None)


def late_labels(lay, infos, lab_sub):
    write_labels(lay, infos, lay.late, lay.head, lay.rest, 0, lab_sub, None)


def turn_labels(lay, lab_sub, count, lab_lane, at):
    for i in range(0, count, LANES):
        block = jnp.transpose(lab_sub[i : i + LANES, :])[:1]
        lab_lane[:, at + i : at + i + LANES] = jnp.where(block < lay.per_owner, block, -1.0)


def copy_head(lay, main_ref, rows):
    for source in range(lay.n_owner):
        rows[source * lay.head : (source + 1) * lay.head, :] = main_ref[
            source * lay.main : source * lay.main + lay.head, :
        ]


def pieces(count, parts):
    return [(i * (count // parts), count // parts) for i in range(parts)]


def stream(lanes, tiles, lab_lane, buffers, put):
    rows_i, count, at = lanes
    step = 32
    tiles = [
        (ref, s, d, lab_sub, bias, line + s, back)
        for ref, n, lab_sub, bias, line, parts, back in tiles
        for s, d in pieces(n, parts)
    ]

    def scores_to(buffer, tile, rows):
        ref, start, deep = tile[:3]
        buffer[:deep, : rows.shape[0]] = lax.dot_general(
            ref[start : start + deep, :],
            rows,
            (((1,), (1,)), ((), ())),
            preferred_element_type=jnp.float32,
        )

    def run(start, blocks, wide):
        repeat = wide // LANES

        def rows_of(block):
            return rows_i[pl.ds(pl.multiple_of(start + block * wide, LANES), wide), :]

        scores_to(buffers[0], tiles[0], rows_of(0))

        def one_block(block):
            here = rows_of(block)
            place = pl.ds(pl.multiple_of(at + start + block * wide, LANES), wide)
            label_i = lab_lane[:, place]
            acc = jnp.zeros((8, wide), jnp.float32)
            for i, (_, _, deep, lab_sub, bias, line, back) in enumerate(tiles):
                if i + 1 < len(tiles):
                    scores_to(buffers[(i + 1) % 2], tiles[i + 1], here)
                elif blocks > 1:

                    @pl.when(block + 1 < blocks)
                    def _():
                        scores_to(buffers[0], tiles[0], rows_of(block + 1))

                buffer = buffers[i % 2]
                for c in range(0, deep, step):
                    part = slice(line + c, line + c + step)
                    label_j = jnp.concatenate([lab_sub[part, :]] * repeat, axis=1)
                    if bias is None:
                        bias_j = NEIGHBOUR - SCALE
                    else:
                        bias_j = jnp.concatenate([bias[part, :]] * repeat, axis=1)
                    shift = jnp.where(label_j == label_i, -SCALE, bias_j)
                    terms = jnp.exp2(buffer[c : c + step, :wide] * SCALE + shift)
                    acc = acc + jnp.sum(terms.reshape(step // 8, 8, wide), axis=0)
                    if back is not None:
                        across = terms[:, :LANES]
                        for r in range(1, repeat):
                            across = across + terms[:, r * LANES : (r + 1) * LANES]
                        back[part, :] += across
            put(place, jnp.sum(acc, axis=0, keepdims=True))

        if blocks == 1:
            one_block(0)
        else:
            pl.loop(0, blocks)(one_block)

    if count >= WIDE:
        run(0, count // WIDE, WIDE)
    if count % WIDE:
        run(count - count % WIDE, 1, count % WIDE)


def turn_sums(back, count, sums, at):
    for i in range(0, count, LANES):
        block = jnp.transpose(back[i : i + LANES, :])
        sums[:, at + i : at + i + LANES] += jnp.sum(block, axis=0, keepdims=True)


def setter(ref):
    def put(place, values):
        ref[:, place] = values

    return put


def adder(ref):
    def put(place, values):
        ref[:, place] += values

    return put


def inner_kernel(lay, mine, early, sums, lab_lane, rows, lab_sub, bias, back, buf_a, buf_b):
    is_home = lax.axis_index("cl") == lay.home
    infos = lines_of(lay, mine)
    buffers = (buf_a, buf_b)

    @pl.when(is_home)
    def _():
        copy_head(lay, mine, rows)
        first_labels(lay, infos, lab_sub)
        turn_labels(lay, lab_sub, lay.n_first, lab_lane, 0)
        back[...] = jnp.zeros(back.shape, jnp.float32)
        size = lay.n_early
        blocks = [(rows.at[pl.ds(start, size)], start) for start in range(0, lay.n_head, size)]
        blocks.append((early, lay.n_head))
        for i, (ref, at) in enumerate(blocks):
            tiles = [
                (ref_j, size, lab_sub, None, at_j, 2, None if at_j == at else back)
                for ref_j, at_j in blocks[i:]
            ]
            stream((ref, size, at), tiles, lab_lane, buffers, setter(sums))
        turn_sums(back, lay.n_first, sums, 0)

    @pl.when(jnp.logical_not(is_home))
    def _():
        write_labels(lay, infos, range(lay.n_owner), 0, lay.main, 0, lab_sub, bias)
        turn_labels(lay, lab_sub, lay.n_main, lab_lane, 0)
        tiles = [(mine, lay.n_main, lab_sub, bias, 0, 2, None)]
        stream((mine, lay.n_main, 0), tiles, lab_lane, buffers, setter(sums))


def half_blocks(ref_i, ref_j, lab_sub, line, back, at, lab_lane, buffers, put):
    half = ref_j.shape[0] // 2
    grp = lax.axis_index("grp")
    for h in range(2):
        start = pl.multiple_of((h ^ grp) * half, half)
        rows_j = ref_j.at[pl.ds(start, half)]
        sub = lab_sub.at[pl.ds(line + start, half)]
        backs = back.at[pl.ds(line + start, half)]
        lanes = (ref_i.at[pl.ds(h * half, half)], half, at + h * half)
        stream(lanes, [(rows_j, half, sub, None, 0, 1, backs)], lab_lane, buffers, put)


def cross_kernel(lay, mine, other, early, early_j, rows, sums, lab_lane, *refs):
    total, for_other, unfit_ref, late_sub, late_sub_j, long_lane = refs[:6]
    lab_sub, bias, back, rows_j, buf_a, buf_b = refs[6:]
    is_home = lax.axis_index("cl") == lay.home
    infos = lines_of(lay, other)
    own = lines_of(lay, mine)
    hot = hot_of(lay, own[0])
    lane = lax.broadcasted_iota(jnp.int32, (1, LANES), 1)
    last = (lane < lay.n_fine) & (lax.rem(lane, lay.per_owner) == lay.per_owner - 1)
    last = last & (lax.div(lane, lay.per_owner) != hot)
    unfit = jnp.zeros((1, LANES), jnp.float32)
    for info in infos + own:
        wrong = last & (info >= lay.main)
        differs = (info != hot.astype(jnp.float32)) | (info >= lay.n_owner)
        wrong = wrong | ((lane == lay.n_fine) & differs)
        unfit = unfit + jnp.where(wrong, 1.0, 0.0)
    unfit_ref[0, 0] = jnp.max(unfit).astype(jnp.int32)
    total[...] = sums[...]
    buffers = (buf_a, buf_b)

    @pl.when(is_home)
    def _():
        copy_head(lay, other, rows_j)
        first_labels(lay, infos, lab_sub)
        back[...] = jnp.zeros(back.shape, jnp.float32)
        size = lay.n_early
        blocks_i = [rows.at[pl.ds(start, size)] for start in range(0, lay.n_head, size)] + [early]
        blocks_j = [rows_j.at[pl.ds(start, size)] for start in range(0, lay.n_head, size)]
        blocks_j.append(early_j)
        put, n = adder(total), len(blocks_i)
        for i, ref in enumerate(blocks_i):
            tiles = [
                (blocks_j[j], size, lab_sub, None, j * size, 2, back)
                for j in ((i + step) % n for step in range(1, (n + 1) // 2))
            ]
            stream((ref, size, i * size), tiles, lab_lane, buffers, put)
            half_blocks(
                ref, blocks_j[i], lab_sub, i * size, back, i * size, lab_lane, buffers, put
            )
        write_labels(lay, own, lay.late, lay.head, lay.rest, 0, late_sub, None)
        write_labels(lay, infos, lay.late, lay.head, lay.rest, 0, late_sub_j, None)
        long_lane[:, : lay.n_first] = lab_lane[...]
        turn_labels(lay, late_sub, lay.n_late, long_lane, lay.n_first)
        for_other[...] = jnp.zeros(for_other.shape, jnp.float32)
        turn_sums(back, lay.n_first, for_other, 0)

    @pl.when(jnp.logical_not(is_home))
    def _():
        write_labels(lay, infos, range(lay.n_owner), 0, lay.main, 0, lab_sub, bias)
        tiles = [(other, lay.n_main, lab_sub, bias, 0, 2, None)]
        stream((mine, lay.n_main, 0), tiles, lab_lane, buffers, adder(total))


def late_pairs(lay, i_refs, late_j, late_sub, back, lab_lane, buffers, put):
    rows, early = i_refs
    lates = [(late_j, lay.n_late, late_sub, None, 0, 2, back)]
    stream((rows, lay.n_head, 0), lates, lab_lane, buffers, put)
    stream((early, lay.n_early, lay.n_head), lates, lab_lane, buffers, put)


def inner_late_kernel(lay, early, late, rows, late_sub, lab_lane, sums, back, buf_a, buf_b):
    @pl.when(lax.axis_index("cl") == lay.home)
    def _():
        buffers = (buf_a, buf_b)
        back[...] = jnp.zeros(back.shape, jnp.float32)
        put = setter(sums)
        late_pairs(lay, (rows, early), late, late_sub, back, lab_lane, buffers, put)
        tiles = [(late, lay.n_late, late_sub, None, 0, 2, None)]
        stream((late, lay.n_late, lay.n_first), tiles, lab_lane, buffers, put)
        turn_sums(back, lay.n_late, sums, lay.n_first)


def cross_late_kernel(lay, early, late, late_j, rows, late_sub, lab_lane, first_lane, *refs):
    first_sums, first_other, sums, out_ref, total, back, buf_a, buf_b = refs
    is_home = lax.axis_index("cl") == lay.home
    grp = lax.axis_index("grp")

    @pl.when(is_home)
    def _():
        total[...] = sums[...]
        total[:, : lay.n_first] += first_sums[...]
        back[...] = jnp.zeros(back.shape, jnp.float32)
        buffers, put = (buf_a, buf_b), adder(total)
        late_pairs(lay, (rows, early), late_j, late_sub, back, lab_lane, buffers, put)
        half_blocks(late, late_j, late_sub, 0, back, lay.n_first, lab_lane, buffers, put)

        def write(line, values):
            for source in range(lay.n_owner):
                start = source * lay.head
                out_ref[2 * source + line, :, : lay.head] = values[:, start : start + lay.head]
            for i, source in enumerate(lay.early + lay.late):
                start = lay.n_head + i * lay.rest
                out_ref[2 * source + line, :, lay.head :] = values[:, start : start + lay.rest]

        write(grp, total[...])
        total[:, : lay.n_first] = first_other[...]
        total[:, lay.n_first :] = jnp.zeros((1, lay.n_late), jnp.float32)
        turn_sums(back, lay.n_late, total, lay.n_first)
        write(1 - grp, total[...])

    @pl.when(jnp.logical_not(is_home))
    def _():
        out_ref[...] = jnp.zeros(out_ref.shape, jnp.float32)
        values = jnp.where(first_lane[...] >= 0, first_sums[...], 1.0)
        for source in range(lay.n_owner):
            start = source * lay.main
            out_ref[2 * source + grp, :, : lay.main] = values[:, start : start + lay.main]


def pair_call(kernel, lay, arrays, out_shape, scratch, out_specs=None, pairs=0):
    width = arrays[0].shape[1]
    buffer = pltpu.VMEM((lay.n_main // 2, WIDE), jnp.float32)
    return pl.pallas_call(
        functools.partial(kernel, lay),
        out_shape=out_shape,
        in_specs=list(vmem_specs(len(arrays))),
        out_specs=out_specs or vmem_specs(len(out_shape)),
        scratch_shapes=list(scratch) + [buffer, buffer],
        compiler_params=pltpu.CompilerParams(vmem_limit_bytes=FAST_LIMIT),
        cost_estimate=pl.CostEstimate(
            flops=2 * pairs * width, bytes_accessed=1, transcendentals=pairs
        ),
    )(*arrays)


def fast_unpack_kernel(values_ref, pos_ref, out_ref):
    pos = pos_ref[...]
    lane = lax.rem(pos, LANES)
    line = lax.div(pos, LANES)
    out = jnp.ones(pos.shape, jnp.float32)
    per = values_ref.shape[2] // LANES
    for r in range(values_ref.shape[0] // 2 * per):
        owner, part = r // per, slice(r % per * LANES, (r % per + 1) * LANES)
        table = values_ref[2 * owner, :, part] + values_ref[2 * owner + 1, :, part]
        found = jnp.take_along_axis(jnp.broadcast_to(table, pos.shape), lane, axis=1)
        out = jnp.where(line == r, found, out)
    out_ref[...] = jnp.log(out)


def fast_unpack(values, pos):
    vmem = pl.BlockSpec(memory_space=pltpu.VMEM)
    return pl.pallas_call(
        fast_unpack_kernel,
        out_shape=jax.ShapeDtypeStruct(pos.shape, jnp.float32),
        in_specs=[vmem, vmem],
        out_specs=vmem,
    )(values, pos)


def general(embeddings, labels, owner_map):
    n_owner = lax.axis_size("cl")
    capacity = SLOTS // n_owner
    rows, width = embeddings.shape
    packed, pos, counts = pack(embeddings, labels, owner_map, n_owner, capacity)
    counts = lax.all_gather(counts, ("cl", "grp"), tiled=True)
    mine = lax.all_to_all(
        packed.reshape(n_owner, capacity, width), "cl", split_axis=0, concat_axis=0, tiled=True
    ).reshape(SLOTS, width)
    other = lax.ppermute(mine, "grp", [(0, 1), (1, 0)])
    results = log_counts(counts, mine, other, n_owner, capacity)
    returned = lax.all_to_all(
        results.reshape(n_owner, capacity), "cl", split_axis=0, concat_axis=0, tiled=True
    )
    return unpack(returned.reshape(SLOTS), pos).reshape(rows)


def body(embeddings, labels, owner_map):
    n_owner = lax.axis_size("cl")
    capacity = SLOTS // n_owner
    rows, width = embeddings.shape
    n_fine = owner_map.shape[0]
    main = -(-(rows // n_owner * 9 // 8) // 16) * 16
    if n_owner != 8 or main >= capacity or n_fine >= LANES:
        return general(embeddings, labels, owner_map)
    home = 2
    lay = Layout(n_owner, n_fine, capacity, main, home)
    packed, extra, pos = place_rows(embeddings, labels, owner_map, lay)

    def hop(x, pairs):
        return lax.ppermute(x, "cl", pairs)

    def swap(x):
        return lax.ppermute(x, "grp", [(0, 1), (1, 0)])

    both = lay_out([extra, hop(extra, [(6, 4), (7, 5)])])
    early = [extra if s == home else hop(extra, [(s, home)]) for s in lay.early]
    early = lay_out(early, home)
    mine = lax.all_to_all(
        packed.reshape(n_owner, main, width), "cl", split_axis=0, concat_axis=0, tiled=True
    ).reshape(n_owner * main, width)
    mine = after(mine, early, both)
    other, early_j = swap(mine), swap(early)
    late = [hop(both, [(s, home)]) for s in (5, 4)]

    def array(shape, dtype=jnp.float32):
        return jax.ShapeDtypeStruct(shape, dtype)

    def scratch(shape):
        return pltpu.VMEM(shape, jnp.float32)

    row, long_row = array((1, lay.n_first)), array((1, lay.n_all))
    bias = scratch((lay.n_main, LANES))
    heads = array((lay.n_head, width), jnp.bfloat16)
    late_lines = array((lay.n_late, LANES))
    late_side, first_side = scratch((lay.n_late, LANES)), scratch((lay.n_first, LANES))
    sums, first_lane, heads_i = pair_call(
        inner_kernel, lay, (mine, early), (row, row, heads), (first_side, bias, first_side)
    )
    specs = vmem_specs(2) + (pl.BlockSpec(memory_space=pltpu.SMEM),) + vmem_specs(3)
    sums, first_other, unfit, late_sub, late_sub_j, lane = pair_call(
        cross_kernel,
        lay,
        (mine, other, early, early_j, heads_i, sums, first_lane),
        (row, row, array((1, 1), jnp.int32), late_lines, late_lines, long_row),
        (first_side, bias, first_side, pltpu.VMEM(heads.shape, heads.dtype)),
        specs,
    )
    late = lay_out(late, home, (sums,))
    late_j = swap(late)
    (late_sums,) = pair_call(
        inner_late_kernel,
        lay,
        (early, late, heads_i, late_sub, lane),
        (long_row,),
        (late_side,),
        pairs=lay.n_late * lay.n_all,
    )
    (results,) = pair_call(
        cross_late_kernel,
        lay,
        (early, late, late_j, heads_i, late_sub_j, lane, first_lane, sums, first_other, late_sums),
        (array((2 * n_owner, 1, capacity)),),
        (scratch(long_row.shape), late_side),
    )
    returned = lax.all_to_all(
        results, ("cl", "grp"), split_axis=0, concat_axis=0, tiled=True
    )
    return lax.cond(
        unfit[0, 0] == 0,
        lambda: fast_unpack(returned, pos).reshape(rows),
        lambda: general(embeddings, labels, owner_map),
    )


def solution(mesh):
    return jax.shard_map(
        body,
        mesh=mesh,
        in_specs=(P(("parts", "cl", "grp"), None), P(("parts", "cl", "grp")), P("parts")),
        out_specs=P(("parts", "cl", "grp")),
        check_vma=False,
    )
```

```python
import functools
import math

import jax
import jax.numpy as jnp
from jax import lax
from jax.experimental import pallas as pl
from jax.experimental.pallas import tpu as pltpu
from jax.sharding import PartitionSpec as P

SLOTS = 2048

temper = 0.2
neighbour_factor = 0.5
epsilon = 1e-06

LANES = 128
SCALE = math.log2(math.e) / temper
NEIGHBOUR = math.log2(neighbour_factor)
DEAD = -1e30
VMEM_LIMIT = 48 * 1024 * 1024
FAST_LIMIT = 16 * 1024 * 1024
WIDE = 512
INFO = 16


def column_of(row):
    pieces = []
    for start in range(0, row.shape[1], LANES):
        width = min(LANES, row.shape[1] - start)
        shape = (width, width)
        diagonal = lax.broadcasted_iota(jnp.int32, shape, 0) == lax.broadcasted_iota(
            jnp.int32, shape, 1
        )
        piece = jnp.broadcast_to(row[:, start : start + width], shape)
        pieces.append(jnp.sum(jnp.where(diagonal, piece, 0.0), axis=1, keepdims=True))
    return jnp.concatenate(pieces, axis=0)


def row_of(column):
    n = column.shape[0]
    diagonal = lax.broadcasted_iota(jnp.int32, (n, n), 0) == lax.broadcasted_iota(
        jnp.int32, (n, n), 1
    )
    return jnp.sum(jnp.where(diagonal, column, 0.0), axis=0, keepdims=True)


def pack_kernel(n_owner, capacity, x_ref, lab_ref, map_ref, out_ref, pos_ref, cnt_ref, unit, pos_row):
    rows = x_ref.shape[0]
    n_fine = map_ref.shape[1]
    per_owner = n_fine // n_owner
    owner_row = map_ref[...].astype(jnp.float32)
    fine_row = lax.broadcasted_iota(jnp.int32, (1, n_fine), 1).astype(jnp.float32)
    key_row = owner_row * n_fine + fine_row
    key_col = column_of(key_row)
    sorted_col = jnp.sum(jnp.where(key_row < key_col, 1.0, 0.0), axis=1, keepdims=True)
    lab = lab_ref[...].astype(jnp.float32)
    lab_row = jnp.concatenate([lab[b : b + 1, :] for b in range(lab.shape[0])], axis=1)
    fine_col = lax.broadcasted_iota(jnp.int32, (n_fine, rows), 0).astype(jnp.float32)
    fine_id = jnp.sum(jnp.where(fine_col == lab_row, sorted_col, 0.0), axis=0, keepdims=True)
    counts_col = jnp.sum(jnp.where(fine_col == fine_id, 1.0, 0.0), axis=1, keepdims=True)
    cnt_ref[...] = row_of(counts_col).astype(jnp.int32)
    coarse = jnp.floor((fine_id + 0.5) * (1.0 / per_owner))
    before = jnp.sum(
        jnp.where(fine_col < coarse * per_owner, counts_col, 0.0), axis=0, keepdims=True
    )
    index = lax.broadcasted_iota(jnp.int32, (1, rows), 1).astype(jnp.float32)
    row_key = fine_id * rows + index
    rank = jnp.zeros((1, rows), jnp.float32)
    for start in range(0, rows, LANES):
        other = column_of(row_key[:, start : start + LANES])
        rank = rank + jnp.sum(jnp.where(other < row_key, 1.0, 0.0), axis=0, keepdims=True)
    pos = (coarse * capacity + rank - before).astype(jnp.int32)
    pos_row[...] = pos
    pos_ref[...] = jnp.concatenate(
        [pos[:, start : start + LANES] for start in range(0, rows, LANES)], axis=0
    )
    x = x_ref[...].astype(jnp.float32)
    squares = jnp.sum(x * x, axis=1, keepdims=True)
    unit[...] = (x * lax.rsqrt(squares + epsilon)).astype(jnp.bfloat16)

    step = 256

    @pl.loop(0, out_ref.shape[0] // step)
    def _(block):
        slot = lax.broadcasted_iota(jnp.int32, (step, rows), 0) + block * step
        chosen = jnp.where(slot == pos_row[...], 1.0, 0.0).astype(jnp.bfloat16)
        packed = jnp.dot(chosen, unit[...], preferred_element_type=jnp.float32)
        out_ref[pl.ds(pl.multiple_of(block * step, step), step), :] = packed.astype(jnp.bfloat16)


def pack(embeddings, labels, owner_map, n_owner, capacity):
    rows, width = embeddings.shape
    n_fine = owner_map.shape[0]
    total = n_owner * capacity
    vmem = pl.BlockSpec(memory_space=pltpu.VMEM)
    return pl.pallas_call(
        functools.partial(pack_kernel, n_owner, capacity),
        out_shape=(
            jax.ShapeDtypeStruct((total, width), jnp.bfloat16),
            jax.ShapeDtypeStruct((rows // LANES, LANES), jnp.int32),
            jax.ShapeDtypeStruct((1, n_fine), jnp.int32),
        ),
        in_specs=[vmem] * 3,
        out_specs=(vmem, vmem, vmem),
        scratch_shapes=[pltpu.VMEM((rows, width), jnp.bfloat16), pltpu.VMEM((1, rows), jnp.int32)],
        compiler_params=pltpu.CompilerParams(vmem_limit_bytes=VMEM_LIMIT),
    )(embeddings, labels.reshape(rows // LANES, LANES), owner_map.reshape(1, n_fine))


def counts_kernel(n_owner, capacity, cnt_ref, mine_ref, other_ref, out_ref, lab_lane, lab_sub, bias):
    total = mine_ref.shape[0]
    per_owner = cnt_ref.shape[1] // n_owner
    me = lax.axis_index("cl")
    grp = lax.axis_index("grp")
    n_grp = lax.axis_size("grp")
    for member in range(2):
        for source in range(n_owner):
            line = source * n_grp + lax.rem(grp + member, n_grp)
            edges = []
            edge = jnp.int32(0)
            for f in range(per_owner):
                edge = edge + cnt_ref[line, me * per_owner + f]
                edges.append(edge)
            down = lax.broadcasted_iota(jnp.int32, (capacity, LANES), 0)
            label = jnp.zeros((capacity, LANES), jnp.int32)
            for edge in edges:
                label = label + jnp.where(down >= edge, 1, 0)
            start = (member * n_owner + source) * capacity
            lab_sub[start : start + capacity, :] = label
            bias[start : start + capacity, :] = jnp.where(
                label < per_owner, NEIGHBOUR - SCALE, DEAD
            )
            if member == 0:
                across = lax.broadcasted_iota(jnp.int32, (1, capacity), 1)
                label = jnp.zeros((1, capacity), jnp.int32)
                for edge in edges:
                    label = label + jnp.where(across >= edge, 1, 0)
                lab_lane[:, source * capacity : (source + 1) * capacity] = jnp.where(
                    label < per_owner, label, -1
                )
    wide, deep = min(512, total), min(256, total)

    @pl.loop(0, total // wide)
    def _(block):
        columns = pl.ds(pl.multiple_of(block * wide, wide), wide)
        rows_i = mine_ref[columns, :]
        label_i = lab_lane[:, columns]

        def add(ref, offset):
            def step(j, acc):
                start = pl.multiple_of(j * deep, deep)
                scores = lax.dot_general(
                    ref[pl.ds(start, deep), :],
                    rows_i,
                    (((1,), (1,)), ((), ())),
                    preferred_element_type=jnp.float32,
                )
                place = pl.ds(pl.multiple_of(start + offset, deep), deep)
                label_j = lab_sub[place, :]
                bias_j = bias[place, :]
                repeat = wide // LANES
                label_j = jnp.concatenate([label_j] * repeat, axis=1)
                bias_j = jnp.concatenate([bias_j] * repeat, axis=1)
                shift = jnp.where(label_j == label_i, -SCALE, bias_j)
                terms = jnp.exp2(scores * SCALE + shift)
                return acc + jnp.sum(terms.reshape(deep // 8, 8, wide), axis=0)

            return step

        acc = jnp.zeros((8, wide), jnp.float32)
        acc = lax.fori_loop(0, total // deep, add(mine_ref, 0), acc, unroll=2)
        acc = lax.fori_loop(0, total // deep, add(other_ref, total), acc, unroll=2)
        totals = jnp.sum(acc, axis=0, keepdims=True)
        out_ref[:, columns] = jnp.log(jnp.where(label_i >= 0, totals, 1.0))


def log_counts(counts, mine, other, n_owner, capacity):
    total = mine.shape[0]
    vmem = pl.BlockSpec(memory_space=pltpu.VMEM)
    return pl.pallas_call(
        functools.partial(counts_kernel, n_owner, capacity),
        out_shape=jax.ShapeDtypeStruct((1, total), jnp.float32),
        in_specs=[pl.BlockSpec(memory_space=pltpu.SMEM), vmem, vmem],
        out_specs=vmem,
        scratch_shapes=[
            pltpu.VMEM((1, total), jnp.int32),
            pltpu.VMEM((2 * total, LANES), jnp.int32),
            pltpu.VMEM((2 * total, LANES), jnp.float32),
        ],
        compiler_params=pltpu.CompilerParams(vmem_limit_bytes=VMEM_LIMIT),
    )(counts, mine, other)


def unpack_kernel(values_ref, pos_ref, out_ref):
    pos = pos_ref[...]
    lane = lax.rem(pos, LANES)
    line = lax.div(pos, LANES)
    out = jnp.zeros(pos.shape, jnp.float32)
    for r in range(values_ref.shape[0]):
        table = jnp.broadcast_to(values_ref[r : r + 1, :], pos.shape)
        found = jnp.take_along_axis(table, lane, axis=1)
        out = jnp.where(line == r, found, out)
    out_ref[...] = out


def unpack(values, pos):
    vmem = pl.BlockSpec(memory_space=pltpu.VMEM)
    return pl.pallas_call(
        unpack_kernel,
        out_shape=jax.ShapeDtypeStruct(pos.shape, jnp.float32),
        in_specs=[vmem, vmem],
        out_specs=vmem,
    )(values.reshape(-1, LANES), pos)


def swapped(x, first, second):
    return jnp.where(x == first, second, jnp.where(x == second, first, x))


def place_kernel(lay, x_hbm, lab_hbm, map_hbm, *refs):
    main_hbm, tail_ref, pos_ref, x_ref, lab_ref, map_ref, unit, main_ref, sems = refs
    n_owner, capacity, main, home = lay.n_owner, lay.capacity, lay.main, lay.home
    copies = [
        pltpu.make_async_copy(src, dst, sems.at[i])
        for i, (src, dst) in enumerate(((x_hbm, x_ref), (lab_hbm, lab_ref), (map_hbm, map_ref)))
    ]
    for copy in copies:
        copy.start()
    rows, width = x_ref.shape
    n_fine = map_ref.shape[1]
    per_owner = n_fine // n_owner
    copies[1].wait()
    copies[2].wait()
    owner_row = map_ref[...].astype(jnp.float32)
    fine_row = lax.broadcasted_iota(jnp.int32, (1, n_fine), 1).astype(jnp.float32)
    key_row = owner_row * n_fine + fine_row
    key_col = column_of(key_row)
    sorted_col = jnp.sum(jnp.where(key_row < key_col, 1.0, 0.0), axis=1, keepdims=True)
    lab = lab_ref[...].astype(jnp.float32)
    lab_row = jnp.concatenate([lab[b : b + 1, :] for b in range(lab.shape[0])], axis=1)
    fine_col = lax.broadcasted_iota(jnp.int32, (n_fine, rows), 0).astype(jnp.float32)
    fine_id = jnp.sum(jnp.where(fine_col == lab_row, sorted_col, 0.0), axis=0, keepdims=True)
    counts_col = jnp.sum(jnp.where(fine_col == fine_id, 1.0, 0.0), axis=1, keepdims=True)
    coarse = jnp.floor((fine_id + 0.5) * (1.0 / per_owner))
    first = coarse * per_owner
    before = jnp.sum(jnp.where(fine_col < first, counts_col, 0.0), axis=0, keepdims=True)
    upto = jnp.sum(jnp.where(fine_col < first + per_owner, counts_col, 0.0), axis=0, keepdims=True)
    full = jnp.min(
        jnp.where(upto - before == capacity, coarse, float(n_owner)), axis=1, keepdims=True
    )
    line = lax.broadcasted_iota(jnp.int32, (n_fine, LANES), 0)
    lane = lax.broadcasted_iota(jnp.int32, (n_fine, LANES), 1)
    inside = (line <= lane) & (lax.div(line, per_owner) == lax.div(lane, per_owner))
    running = jnp.sum(jnp.where(inside, counts_col, 0.0), axis=0, keepdims=True)
    info = jnp.where(lane[:1] < n_fine, running, full)
    index = lax.broadcasted_iota(jnp.int32, (1, rows), 1).astype(jnp.float32)
    row_key = fine_id * rows + index
    rank = jnp.zeros((1, rows), jnp.float32)
    for start in range(0, rows, LANES):
        other = column_of(row_key[:, start : start + LANES])
        rank = rank + jnp.sum(jnp.where(other < row_key, 1.0, 0.0), axis=0, keepdims=True)
    rank = (rank - before).astype(jnp.int32)
    place = swapped(coarse.astype(jnp.int32), full.astype(jnp.int32), home)
    table = place * capacity + rank
    pos_ref[...] = jnp.concatenate(
        [table[:, start : start + LANES] for start in range(0, rows, LANES)], axis=0
    )
    fits = rank < jnp.where(place == home, lay.head, main - 1)
    slot = jnp.where(fits, place * main + rank, -1)
    tail_slot = jnp.where(place == home, rank - lay.head, -1)
    copies[0].wait()
    x = x_ref[...].astype(jnp.float32)
    squares = jnp.sum(x * x, axis=1, keepdims=True)
    unit[...] = (x * lax.rsqrt(squares + epsilon)).astype(jnp.bfloat16)

    def chosen_rows(slot, start, count):
        here = lax.broadcasted_iota(jnp.int32, (count, rows), 0) + start
        chosen = jnp.where(here == slot, 1.0, 0.0).astype(jnp.bfloat16)
        return jnp.dot(chosen, unit[...], preferred_element_type=jnp.float32)

    count = 2 * main
    down = lax.broadcasted_iota(jnp.int32, (count, LANES), 0)
    is_info = lax.rem(down, main) == main - 1
    writes = []
    for i, start in enumerate(range(0, lay.n_main, count)):
        packed = chosen_rows(slot, start, count)
        place = slice(start, start + count)
        main_ref[place, LANES:] = packed[:, LANES:].astype(jnp.bfloat16)
        main_ref[place, :LANES] = jnp.where(is_info, info, packed[:, :LANES]).astype(jnp.bfloat16)
        writes.append(
            pltpu.make_async_copy(
                main_ref.at[pl.ds(start, count)], main_hbm.at[pl.ds(start, count)], sems.at[3 + i]
            )
        )
        writes[-1].start()
    tail_ref[...] = chosen_rows(tail_slot, 0, lay.rest).astype(jnp.bfloat16)
    for write in writes:
        write.wait()


def vmem_specs(count):
    return (pl.BlockSpec(memory_space=pltpu.VMEM),) * count


def place_rows(embeddings, labels, owner_map, lay):
    rows, width = embeddings.shape
    n_fine = owner_map.shape[0]
    lab_shape = (rows // LANES, LANES)
    anywhere = pl.BlockSpec(memory_space=pl.ANY)
    return pl.pallas_call(
        functools.partial(place_kernel, lay),
        out_shape=(
            jax.ShapeDtypeStruct((lay.n_main, width), jnp.bfloat16),
            jax.ShapeDtypeStruct((lay.rest, width), jnp.bfloat16),
            jax.ShapeDtypeStruct(lab_shape, jnp.int32),
        ),
        in_specs=[anywhere] * 3,
        out_specs=(anywhere,) + vmem_specs(2),
        scratch_shapes=[
            pltpu.VMEM((rows, width), jnp.bfloat16),
            pltpu.VMEM(lab_shape, jnp.int32),
            pltpu.VMEM((1, n_fine), jnp.int32),
            pltpu.VMEM((rows, width), jnp.bfloat16),
            pltpu.VMEM((lay.n_main, width), jnp.bfloat16),
            pltpu.SemaphoreType.DMA((3 + lay.n_owner // 2,)),
        ],
        compiler_params=pltpu.CompilerParams(vmem_limit_bytes=FAST_LIMIT),
    )(embeddings, labels.reshape(lab_shape), owner_map.reshape(1, n_fine))


def gate_kernel(*refs):
    pass


def after(rows, *there):
    return pl.pallas_call(
        gate_kernel,
        out_shape=jax.ShapeDtypeStruct(rows.shape, rows.dtype),
        in_specs=list(vmem_specs(1 + len(there))),
        out_specs=vmem_specs(1)[0],
        input_output_aliases={0: 0},
        compiler_params=pltpu.CompilerParams(vmem_limit_bytes=FAST_LIMIT),
    )(rows, *there)


def lay_out_kernel(n_arrays, home, *refs):
    chunks, out = refs[:n_arrays], refs[-1]

    def copy():
        start = 0
        for chunk in chunks:
            out[start : start + chunk.shape[0], :] = chunk[...]
            start += chunk.shape[0]

    if home is None:
        copy()
    else:
        pl.when(lax.axis_index("cl") == home)(copy)


def lay_out(chunks, home=None, waits=()):
    rows, width = sum(x.shape[0] for x in chunks), chunks[0].shape[1]
    return pl.pallas_call(
        functools.partial(lay_out_kernel, len(chunks), home),
        out_shape=jax.ShapeDtypeStruct((rows, width), jnp.bfloat16),
        in_specs=list(vmem_specs(len(chunks) + len(waits))),
        out_specs=vmem_specs(1)[0],
        compiler_params=pltpu.CompilerParams(vmem_limit_bytes=FAST_LIMIT),
    )(*chunks, *waits)


class Layout:
    early, late = (0, 1, 2, 3), (5, 4, 7, 6)

    def __init__(self, n_owner, n_fine, capacity, main, home):
        self.n_owner, self.n_fine, self.capacity = n_owner, n_fine, capacity
        self.main, self.home = main, home
        self.head = main - INFO
        self.rest = capacity - self.head
        self.per_owner = n_fine // n_owner
        self.n_main = n_owner * main
        self.n_head = n_owner * self.head
        self.n_early = len(self.early) * self.rest
        self.n_late = len(self.late) * self.rest
        self.n_first = self.n_head + self.n_early
        self.n_all = self.n_first + self.n_late


def info_line(lay, main_ref, source):
    end = (source + 1) * lay.main
    return main_ref[end - INFO : end, :LANES].astype(jnp.float32)[INFO - 1 :]


def lines_of(lay, main_ref):
    return [info_line(lay, main_ref, source) for source in range(lay.n_owner)]


def hot_of(lay, info):
    lane = lax.broadcasted_iota(jnp.int32, (1, LANES), 1)
    hot = jnp.max(jnp.where(lane == lay.n_fine, info, 0.0), axis=1, keepdims=True)
    return hot.astype(jnp.int32)


def write_labels(lay, infos, sources, first, count, at, lab_sub, bias):
    cluster = swapped(lax.axis_index("cl"), hot_of(lay, infos[0]), lay.home)
    lane = lax.broadcasted_iota(jnp.int32, (1, LANES), 1)
    is_edge = lax.div(lane, lay.per_owner) == cluster
    for i, source in enumerate(sources):
        edges = jnp.where(is_edge, infos[source], 2.0 * lay.capacity)
        slot = lax.broadcasted_iota(jnp.int32, (count, LANES), 0) + first
        label = jnp.where(slot.astype(jnp.float32) >= edges, 1.0, 0.0)
        label = jnp.broadcast_to(jnp.sum(label, axis=1, keepdims=True), (count, LANES))
        start = at + i * count
        lab_sub[start : start + count, :] = label
        if bias is not None:
            bias[start : start + count, :] = jnp.where(
                label < lay.per_owner, NEIGHBOUR - SCALE, DEAD
            )


def first_labels(lay, infos, lab_sub):
    write_labels(lay, infos, range(lay.n_owner), 0, lay.head, 0, lab_sub, None)
    write_labels(lay, infos, lay.early, lay.head, lay.rest, lay.n_head, lab_sub, None)


def late_labels(lay, infos, lab_sub):
    write_labels(lay, infos, lay.late, lay.head, lay.rest, 0, lab_sub, None)


def turn_labels(lay, lab_sub, count, lab_lane, at):
    for i in range(0, count, LANES):
        block = jnp.transpose(lab_sub[i : i + LANES, :])[:1]
        lab_lane[:, at + i : at + i + LANES] = jnp.where(block < lay.per_owner, block, -1.0)


def copy_head(lay, main_ref, rows):
    for source in range(lay.n_owner):
        rows[source * lay.head : (source + 1) * lay.head, :] = main_ref[
            source * lay.main : source * lay.main + lay.head, :
        ]


def pieces(count, parts):
    return [(i * (count // parts), count // parts) for i in range(parts)]


def stream(lanes, tiles, lab_lane, buffers, put):
    rows_i, count, at = lanes
    step = 32
    tiles = [
        (ref, s, d, lab_sub, bias, line + s, back)
        for ref, n, lab_sub, bias, line, parts, back in tiles
        for s, d in pieces(n, parts)
    ]

    def scores_to(buffer, tile, rows):
        ref, start, deep = tile[:3]
        buffer[:deep, : rows.shape[0]] = lax.dot_general(
            ref[start : start + deep, :],
            rows,
            (((1,), (1,)), ((), ())),
            preferred_element_type=jnp.float32,
        )

    def run(start, blocks, wide):
        repeat = wide // LANES

        def rows_of(block):
            return rows_i[pl.ds(pl.multiple_of(start + block * wide, LANES), wide), :]

        scores_to(buffers[0], tiles[0], rows_of(0))

        def one_block(block):
            here = rows_of(block)
            place = pl.ds(pl.multiple_of(at + start + block * wide, LANES), wide)
            label_i = lab_lane[:, place]
            acc = jnp.zeros((8, wide), jnp.float32)
            for i, (_, _, deep, lab_sub, bias, line, back) in enumerate(tiles):
                if i + 1 < len(tiles):
                    scores_to(buffers[(i + 1) % 2], tiles[i + 1], here)
                elif blocks > 1:

                    @pl.when(block + 1 < blocks)
                    def _():
                        scores_to(buffers[0], tiles[0], rows_of(block + 1))

                buffer = buffers[i % 2]
                for c in range(0, deep, step):
                    part = slice(line + c, line + c + step)
                    label_j = jnp.concatenate([lab_sub[part, :]] * repeat, axis=1)
                    if bias is None:
                        bias_j = NEIGHBOUR - SCALE
                    else:
                        bias_j = jnp.concatenate([bias[part, :]] * repeat, axis=1)
                    shift = jnp.where(label_j == label_i, -SCALE, bias_j)
                    terms = jnp.exp2(buffer[c : c + step, :wide] * SCALE + shift)
                    acc = acc + jnp.sum(terms.reshape(step // 8, 8, wide), axis=0)
                    if back is not None:
                        across = terms[:, :LANES]
                        for r in range(1, repeat):
                            across = across + terms[:, r * LANES : (r + 1) * LANES]
                        back[part, :] += across
            put(place, jnp.sum(acc, axis=0, keepdims=True))

        if blocks == 1:
            one_block(0)
        else:
            pl.loop(0, blocks)(one_block)

    if count >= WIDE:
        run(0, count // WIDE, WIDE)
    if count % WIDE:
        run(count - count % WIDE, 1, count % WIDE)


def turn_sums(back, count, sums, at):
    for i in range(0, count, LANES):
        block = jnp.transpose(back[i : i + LANES, :])
        sums[:, at + i : at + i + LANES] += jnp.sum(block, axis=0, keepdims=True)


def setter(ref):
    def put(place, values):
        ref[:, place] = values

    return put


def adder(ref):
    def put(place, values):
        ref[:, place] += values

    return put


def inner_kernel(lay, mine, early, sums, lab_lane, rows, lab_sub, bias, back, buf_a, buf_b):
    is_home = lax.axis_index("cl") == lay.home
    infos = lines_of(lay, mine)
    buffers = (buf_a, buf_b)

    @pl.when(is_home)
    def _():
        copy_head(lay, mine, rows)
        first_labels(lay, infos, lab_sub)
        turn_labels(lay, lab_sub, lay.n_first, lab_lane, 0)
        back[...] = jnp.zeros(back.shape, jnp.float32)
        size = lay.n_early
        blocks = [(rows.at[pl.ds(start, size)], start) for start in range(0, lay.n_head, size)]
        blocks.append((early, lay.n_head))
        for i, (ref, at) in enumerate(blocks):
            tiles = [
                (ref_j, size, lab_sub, None, at_j, 2, None if at_j == at else back)
                for ref_j, at_j in blocks[i:]
            ]
            stream((ref, size, at), tiles, lab_lane, buffers, setter(sums))
        turn_sums(back, lay.n_first, sums, 0)

    @pl.when(jnp.logical_not(is_home))
    def _():
        write_labels(lay, infos, range(lay.n_owner), 0, lay.main, 0, lab_sub, bias)
        turn_labels(lay, lab_sub, lay.n_main, lab_lane, 0)
        tiles = [(mine, lay.n_main, lab_sub, bias, 0, 2, None)]
        stream((mine, lay.n_main, 0), tiles, lab_lane, buffers, setter(sums))


def half_blocks(ref_i, ref_j, lab_sub, line, back, at, lab_lane, buffers, put):
    half = ref_j.shape[0] // 2
    grp = lax.axis_index("grp")
    for h in range(2):
        start = pl.multiple_of((h ^ grp) * half, half)
        rows_j = ref_j.at[pl.ds(start, half)]
        sub = lab_sub.at[pl.ds(line + start, half)]
        backs = back.at[pl.ds(line + start, half)]
        lanes = (ref_i.at[pl.ds(h * half, half)], half, at + h * half)
        stream(lanes, [(rows_j, half, sub, None, 0, 1, backs)], lab_lane, buffers, put)


def cross_kernel(lay, mine, other, early, early_j, rows, sums, lab_lane, *refs):
    total, for_other, unfit_ref, late_sub, late_sub_j, long_lane = refs[:6]
    lab_sub, bias, back, rows_j, buf_a, buf_b = refs[6:]
    is_home = lax.axis_index("cl") == lay.home
    infos = lines_of(lay, other)
    own = lines_of(lay, mine)
    hot = hot_of(lay, own[0])
    lane = lax.broadcasted_iota(jnp.int32, (1, LANES), 1)
    last = (lane < lay.n_fine) & (lax.rem(lane, lay.per_owner) == lay.per_owner - 1)
    last = last & (lax.div(lane, lay.per_owner) != hot)
    unfit = jnp.zeros((1, LANES), jnp.float32)
    for info in infos + own:
        wrong = last & (info >= lay.main)
        differs = (info != hot.astype(jnp.float32)) | (info >= lay.n_owner)
        wrong = wrong | ((lane == lay.n_fine) & differs)
        unfit = unfit + jnp.where(wrong, 1.0, 0.0)
    unfit_ref[0, 0] = jnp.max(unfit).astype(jnp.int32)
    total[...] = sums[...]
    buffers = (buf_a, buf_b)

    @pl.when(is_home)
    def _():
        copy_head(lay, other, rows_j)
        first_labels(lay, infos, lab_sub)
        back[...] = jnp.zeros(back.shape, jnp.float32)
        size = lay.n_early
        blocks_i = [rows.at[pl.ds(start, size)] for start in range(0, lay.n_head, size)] + [early]
        blocks_j = [rows_j.at[pl.ds(start, size)] for start in range(0, lay.n_head, size)]
        blocks_j.append(early_j)
        put, n = adder(total), len(blocks_i)
        for i, ref in enumerate(blocks_i):
            tiles = [
                (blocks_j[j], size, lab_sub, None, j * size, 2, back)
                for j in ((i + step) % n for step in range(1, (n + 1) // 2))
            ]
            stream((ref, size, i * size), tiles, lab_lane, buffers, put)
            half_blocks(
                ref, blocks_j[i], lab_sub, i * size, back, i * size, lab_lane, buffers, put
            )
        write_labels(lay, own, lay.late, lay.head, lay.rest, 0, late_sub, None)
        write_labels(lay, infos, lay.late, lay.head, lay.rest, 0, late_sub_j, None)
        long_lane[:, : lay.n_first] = lab_lane[...]
        turn_labels(lay, late_sub, lay.n_late, long_lane, lay.n_first)
        for_other[...] = jnp.zeros(for_other.shape, jnp.float32)
        turn_sums(back, lay.n_first, for_other, 0)

    @pl.when(jnp.logical_not(is_home))
    def _():
        write_labels(lay, infos, range(lay.n_owner), 0, lay.main, 0, lab_sub, bias)
        tiles = [(other, lay.n_main, lab_sub, bias, 0, 2, None)]
        stream((mine, lay.n_main, 0), tiles, lab_lane, buffers, adder(total))


def late_pairs(lay, i_refs, late_j, late_sub, back, lab_lane, buffers, put):
    rows, early = i_refs
    lates = [(late_j, lay.n_late, late_sub, None, 0, 2, back)]
    stream((rows, lay.n_head, 0), lates, lab_lane, buffers, put)
    stream((early, lay.n_early, lay.n_head), lates, lab_lane, buffers, put)


def inner_late_kernel(lay, early, late, rows, late_sub, lab_lane, sums, back, buf_a, buf_b):
    @pl.when(lax.axis_index("cl") == lay.home)
    def _():
        buffers = (buf_a, buf_b)
        back[...] = jnp.zeros(back.shape, jnp.float32)
        put = setter(sums)
        late_pairs(lay, (rows, early), late, late_sub, back, lab_lane, buffers, put)
        tiles = [(late, lay.n_late, late_sub, None, 0, 2, None)]
        stream((late, lay.n_late, lay.n_first), tiles, lab_lane, buffers, put)
        turn_sums(back, lay.n_late, sums, lay.n_first)


def cross_late_kernel(lay, early, late, late_j, rows, late_sub, lab_lane, first_lane, *refs):
    first_sums, first_other, sums, out_ref, total, back, buf_a, buf_b = refs
    is_home = lax.axis_index("cl") == lay.home
    grp = lax.axis_index("grp")

    @pl.when(is_home)
    def _():
        total[...] = sums[...]
        total[:, : lay.n_first] += first_sums[...]
        back[...] = jnp.zeros(back.shape, jnp.float32)
        buffers, put = (buf_a, buf_b), adder(total)
        late_pairs(lay, (rows, early), late_j, late_sub, back, lab_lane, buffers, put)
        half_blocks(late, late_j, late_sub, 0, back, lay.n_first, lab_lane, buffers, put)

        def write(line, values):
            for source in range(lay.n_owner):
                start = source * lay.head
                out_ref[2 * source + line, :, : lay.head] = values[:, start : start + lay.head]
            for i, source in enumerate(lay.early + lay.late):
                start = lay.n_head + i * lay.rest
                out_ref[2 * source + line, :, lay.head :] = values[:, start : start + lay.rest]

        write(grp, total[...])
        total[:, : lay.n_first] = first_other[...]
        total[:, lay.n_first :] = jnp.zeros((1, lay.n_late), jnp.float32)
        turn_sums(back, lay.n_late, total, lay.n_first)
        write(1 - grp, total[...])

    @pl.when(jnp.logical_not(is_home))
    def _():
        out_ref[...] = jnp.zeros(out_ref.shape, jnp.float32)
        values = jnp.where(first_lane[...] >= 0, first_sums[...], 1.0)
        for source in range(lay.n_owner):
            start = source * lay.main
            out_ref[2 * source + grp, :, : lay.main] = values[:, start : start + lay.main]


def pair_call(kernel, lay, arrays, out_shape, scratch, out_specs=None, pairs=0):
    width = arrays[0].shape[1]
    buffer = pltpu.VMEM((lay.n_main // 2, WIDE), jnp.float32)
    return pl.pallas_call(
        functools.partial(kernel, lay),
        out_shape=out_shape,
        in_specs=list(vmem_specs(len(arrays))),
        out_specs=out_specs or vmem_specs(len(out_shape)),
        scratch_shapes=list(scratch) + [buffer, buffer],
        compiler_params=pltpu.CompilerParams(vmem_limit_bytes=FAST_LIMIT),
        cost_estimate=pl.CostEstimate(
            flops=2 * pairs * width, bytes_accessed=1, transcendentals=pairs
        ),
    )(*arrays)


def fast_unpack_kernel(values_ref, pos_ref, out_ref):
    pos = pos_ref[...]
    lane = lax.rem(pos, LANES)
    line = lax.div(pos, LANES)
    out = jnp.ones(pos.shape, jnp.float32)
    per = values_ref.shape[2] // LANES
    for r in range(values_ref.shape[0] // 2 * per):
        owner, part = r // per, slice(r % per * LANES, (r % per + 1) * LANES)
        table = values_ref[2 * owner, :, part] + values_ref[2 * owner + 1, :, part]
        found = jnp.take_along_axis(jnp.broadcast_to(table, pos.shape), lane, axis=1)
        out = jnp.where(line == r, found, out)
    out_ref[...] = jnp.log(out)


def fast_unpack(values, pos):
    vmem = pl.BlockSpec(memory_space=pltpu.VMEM)
    return pl.pallas_call(
        fast_unpack_kernel,
        out_shape=jax.ShapeDtypeStruct(pos.shape, jnp.float32),
        in_specs=[vmem, vmem],
        out_specs=vmem,
    )(values, pos)


def general(embeddings, labels, owner_map):
    n_owner = lax.axis_size("cl")
    capacity = SLOTS // n_owner
    rows, width = embeddings.shape
    packed, pos, counts = pack(embeddings, labels, owner_map, n_owner, capacity)
    counts = lax.all_gather(counts, ("cl", "grp"), tiled=True)
    mine = lax.all_to_all(
        packed.reshape(n_owner, capacity, width), "cl", split_axis=0, concat_axis=0, tiled=True
    ).reshape(SLOTS, width)
    other = lax.ppermute(mine, "grp", [(0, 1), (1, 0)])
    results = log_counts(counts, mine, other, n_owner, capacity)
    returned = lax.all_to_all(
        results.reshape(n_owner, capacity), "cl", split_axis=0, concat_axis=0, tiled=True
    )
    return unpack(returned.reshape(SLOTS), pos).reshape(rows)


def body(embeddings, labels, owner_map):
    n_owner = lax.axis_size("cl")
    capacity = SLOTS // n_owner
    rows, width = embeddings.shape
    n_fine = owner_map.shape[0]
    main = -(-(rows // n_owner * 9 // 8) // 16) * 16
    if n_owner != 8 or main >= capacity or n_fine >= LANES:
        return general(embeddings, labels, owner_map)
    home = 2
    lay = Layout(n_owner, n_fine, capacity, main, home)
    packed, extra, pos = place_rows(embeddings, labels, owner_map, lay)

    def hop(x, pairs):
        return lax.ppermute(x, "cl", pairs)

    def swap(x):
        return lax.ppermute(x, "grp", [(0, 1), (1, 0)])

    arrived = {s: extra if s == home else hop(extra, [(s, home)]) for s in (0, 1, 2, 3, 5, 4)}
    early = lay_out([arrived[s] for s in lay.early], home)
    mine = lax.all_to_all(
        packed.reshape(n_owner, main, width), "cl", split_axis=0, concat_axis=0, tiled=True
    ).reshape(n_owner * main, width)
    mine = after(mine, early)
    other = swap(mine)
    early_j = swap(lay_out([early], home, (arrived[5], arrived[4])))
    late = [arrived[5], arrived[4]] + [hop(extra, [(s, home)]) for s in (7, 6)]

    def array(shape, dtype=jnp.float32):
        return jax.ShapeDtypeStruct(shape, dtype)

    def scratch(shape):
        return pltpu.VMEM(shape, jnp.float32)

    row, long_row = array((1, lay.n_first)), array((1, lay.n_all))
    bias = scratch((lay.n_main, LANES))
    heads = array((lay.n_head, width), jnp.bfloat16)
    late_lines = array((lay.n_late, LANES))
    late_side, first_side = scratch((lay.n_late, LANES)), scratch((lay.n_first, LANES))
    sums, first_lane, heads_i = pair_call(
        inner_kernel, lay, (mine, early), (row, row, heads), (first_side, bias, first_side)
    )
    specs = vmem_specs(2) + (pl.BlockSpec(memory_space=pltpu.SMEM),) + vmem_specs(3)
    sums, first_other, unfit, late_sub, late_sub_j, lane = pair_call(
        cross_kernel,
        lay,
        (mine, other, early, early_j, heads_i, sums, first_lane),
        (row, row, array((1, 1), jnp.int32), late_lines, late_lines, long_row),
        (first_side, bias, first_side, pltpu.VMEM(heads.shape, heads.dtype)),
        specs,
    )
    late = lay_out(late, home, (sums,))
    late_j = swap(late)
    (late_sums,) = pair_call(
        inner_late_kernel,
        lay,
        (early, late, heads_i, late_sub, lane),
        (long_row,),
        (late_side,),
        pairs=lay.n_late * lay.n_all,
    )
    (results,) = pair_call(
        cross_late_kernel,
        lay,
        (early, late, late_j, heads_i, late_sub_j, lane, first_lane, sums, first_other, late_sums),
        (array((2 * n_owner, 1, capacity)),),
        (scratch(long_row.shape), late_side),
    )
    returned = lax.all_to_all(
        results, ("cl", "grp"), split_axis=0, concat_axis=0, tiled=True
    )
    return lax.cond(
        unfit[0, 0] == 0,
        lambda: fast_unpack(returned, pos).reshape(rows),
        lambda: general(embeddings, labels, owner_map),
    )


def solution(mesh):
    return jax.shard_map(
        body,
        mesh=mesh,
        in_specs=(P(("parts", "cl", "grp"), None), P(("parts", "cl", "grp")), P("parts")),
        out_specs=P(("parts", "cl", "grp")),
        check_vma=False,
    )
```

```python
import functools
import math

import jax
import jax.numpy as jnp
from jax import lax
from jax.experimental import pallas as pl
from jax.experimental.pallas import tpu as pltpu
from jax.sharding import PartitionSpec as P

SLOTS = 2048

temper = 0.2
neighbour_factor = 0.5
epsilon = 1e-06

LANES = 128
SCALE = math.log2(math.e) / temper
NEIGHBOUR = math.log2(neighbour_factor)
DEAD = -1e30
VMEM_LIMIT = 48 * 1024 * 1024
FAST_LIMIT = 16 * 1024 * 1024
WIDE = 512
INFO = 16


def column_of(row):
    pieces = []
    for start in range(0, row.shape[1], LANES):
        width = min(LANES, row.shape[1] - start)
        shape = (width, width)
        diagonal = lax.broadcasted_iota(jnp.int32, shape, 0) == lax.broadcasted_iota(
            jnp.int32, shape, 1
        )
        piece = jnp.broadcast_to(row[:, start : start + width], shape)
        pieces.append(jnp.sum(jnp.where(diagonal, piece, 0.0), axis=1, keepdims=True))
    return jnp.concatenate(pieces, axis=0)


def row_of(column):
    n = column.shape[0]
    diagonal = lax.broadcasted_iota(jnp.int32, (n, n), 0) == lax.broadcasted_iota(
        jnp.int32, (n, n), 1
    )
    return jnp.sum(jnp.where(diagonal, column, 0.0), axis=0, keepdims=True)


def pack_kernel(n_owner, capacity, x_ref, lab_ref, map_ref, out_ref, pos_ref, cnt_ref, unit, pos_row):
    rows = x_ref.shape[0]
    n_fine = map_ref.shape[1]
    per_owner = n_fine // n_owner
    owner_row = map_ref[...].astype(jnp.float32)
    fine_row = lax.broadcasted_iota(jnp.int32, (1, n_fine), 1).astype(jnp.float32)
    key_row = owner_row * n_fine + fine_row
    key_col = column_of(key_row)
    sorted_col = jnp.sum(jnp.where(key_row < key_col, 1.0, 0.0), axis=1, keepdims=True)
    lab = lab_ref[...].astype(jnp.float32)
    lab_row = jnp.concatenate([lab[b : b + 1, :] for b in range(lab.shape[0])], axis=1)
    fine_col = lax.broadcasted_iota(jnp.int32, (n_fine, rows), 0).astype(jnp.float32)
    fine_id = jnp.sum(jnp.where(fine_col == lab_row, sorted_col, 0.0), axis=0, keepdims=True)
    counts_col = jnp.sum(jnp.where(fine_col == fine_id, 1.0, 0.0), axis=1, keepdims=True)
    cnt_ref[...] = row_of(counts_col).astype(jnp.int32)
    coarse = jnp.floor((fine_id + 0.5) * (1.0 / per_owner))
    before = jnp.sum(
        jnp.where(fine_col < coarse * per_owner, counts_col, 0.0), axis=0, keepdims=True
    )
    index = lax.broadcasted_iota(jnp.int32, (1, rows), 1).astype(jnp.float32)
    row_key = fine_id * rows + index
    rank = jnp.zeros((1, rows), jnp.float32)
    for start in range(0, rows, LANES):
        other = column_of(row_key[:, start : start + LANES])
        rank = rank + jnp.sum(jnp.where(other < row_key, 1.0, 0.0), axis=0, keepdims=True)
    pos = (coarse * capacity + rank - before).astype(jnp.int32)
    pos_row[...] = pos
    pos_ref[...] = jnp.concatenate(
        [pos[:, start : start + LANES] for start in range(0, rows, LANES)], axis=0
    )
    x = x_ref[...].astype(jnp.float32)
    squares = jnp.sum(x * x, axis=1, keepdims=True)
    unit[...] = (x * lax.rsqrt(squares + epsilon)).astype(jnp.bfloat16)

    step = 256

    @pl.loop(0, out_ref.shape[0] // step)
    def _(block):
        slot = lax.broadcasted_iota(jnp.int32, (step, rows), 0) + block * step
        chosen = jnp.where(slot == pos_row[...], 1.0, 0.0).astype(jnp.bfloat16)
        packed = jnp.dot(chosen, unit[...], preferred_element_type=jnp.float32)
        out_ref[pl.ds(pl.multiple_of(block * step, step), step), :] = packed.astype(jnp.bfloat16)


def pack(embeddings, labels, owner_map, n_owner, capacity):
    rows, width = embeddings.shape
    n_fine = owner_map.shape[0]
    total = n_owner * capacity
    vmem = pl.BlockSpec(memory_space=pltpu.VMEM)
    return pl.pallas_call(
        functools.partial(pack_kernel, n_owner, capacity),
        out_shape=(
            jax.ShapeDtypeStruct((total, width), jnp.bfloat16),
            jax.ShapeDtypeStruct((rows // LANES, LANES), jnp.int32),
            jax.ShapeDtypeStruct((1, n_fine), jnp.int32),
        ),
        in_specs=[vmem] * 3,
        out_specs=(vmem, vmem, vmem),
        scratch_shapes=[pltpu.VMEM((rows, width), jnp.bfloat16), pltpu.VMEM((1, rows), jnp.int32)],
        compiler_params=pltpu.CompilerParams(vmem_limit_bytes=VMEM_LIMIT),
    )(embeddings, labels.reshape(rows // LANES, LANES), owner_map.reshape(1, n_fine))


def counts_kernel(n_owner, capacity, cnt_ref, mine_ref, other_ref, out_ref, lab_lane, lab_sub, bias):
    total = mine_ref.shape[0]
    per_owner = cnt_ref.shape[1] // n_owner
    me = lax.axis_index("cl")
    grp = lax.axis_index("grp")
    n_grp = lax.axis_size("grp")
    for member in range(2):
        for source in range(n_owner):
            line = source * n_grp + lax.rem(grp + member, n_grp)
            edges = []
            edge = jnp.int32(0)
            for f in range(per_owner):
                edge = edge + cnt_ref[line, me * per_owner + f]
                edges.append(edge)
            down = lax.broadcasted_iota(jnp.int32, (capacity, LANES), 0)
            label = jnp.zeros((capacity, LANES), jnp.int32)
            for edge in edges:
                label = label + jnp.where(down >= edge, 1, 0)
            start = (member * n_owner + source) * capacity
            lab_sub[start : start + capacity, :] = label
            bias[start : start + capacity, :] = jnp.where(
                label < per_owner, NEIGHBOUR - SCALE, DEAD
            )
            if member == 0:
                across = lax.broadcasted_iota(jnp.int32, (1, capacity), 1)
                label = jnp.zeros((1, capacity), jnp.int32)
                for edge in edges:
                    label = label + jnp.where(across >= edge, 1, 0)
                lab_lane[:, source * capacity : (source + 1) * capacity] = jnp.where(
                    label < per_owner, label, -1
                )
    wide, deep = min(512, total), min(256, total)

    @pl.loop(0, total // wide)
    def _(block):
        columns = pl.ds(pl.multiple_of(block * wide, wide), wide)
        rows_i = mine_ref[columns, :]
        label_i = lab_lane[:, columns]

        def add(ref, offset):
            def step(j, acc):
                start = pl.multiple_of(j * deep, deep)
                scores = lax.dot_general(
                    ref[pl.ds(start, deep), :],
                    rows_i,
                    (((1,), (1,)), ((), ())),
                    preferred_element_type=jnp.float32,
                )
                place = pl.ds(pl.multiple_of(start + offset, deep), deep)
                label_j = lab_sub[place, :]
                bias_j = bias[place, :]
                repeat = wide // LANES
                label_j = jnp.concatenate([label_j] * repeat, axis=1)
                bias_j = jnp.concatenate([bias_j] * repeat, axis=1)
                shift = jnp.where(label_j == label_i, -SCALE, bias_j)
                terms = jnp.exp2(scores * SCALE + shift)
                return acc + jnp.sum(terms.reshape(deep // 8, 8, wide), axis=0)

            return step

        acc = jnp.zeros((8, wide), jnp.float32)
        acc = lax.fori_loop(0, total // deep, add(mine_ref, 0), acc, unroll=2)
        acc = lax.fori_loop(0, total // deep, add(other_ref, total), acc, unroll=2)
        totals = jnp.sum(acc, axis=0, keepdims=True)
        out_ref[:, columns] = jnp.log(jnp.where(label_i >= 0, totals, 1.0))


def log_counts(counts, mine, other, n_owner, capacity):
    total = mine.shape[0]
    vmem = pl.BlockSpec(memory_space=pltpu.VMEM)
    return pl.pallas_call(
        functools.partial(counts_kernel, n_owner, capacity),
        out_shape=jax.ShapeDtypeStruct((1, total), jnp.float32),
        in_specs=[pl.BlockSpec(memory_space=pltpu.SMEM), vmem, vmem],
        out_specs=vmem,
        scratch_shapes=[
            pltpu.VMEM((1, total), jnp.int32),
            pltpu.VMEM((2 * total, LANES), jnp.int32),
            pltpu.VMEM((2 * total, LANES), jnp.float32),
        ],
        compiler_params=pltpu.CompilerParams(vmem_limit_bytes=VMEM_LIMIT),
    )(counts, mine, other)


def unpack_kernel(values_ref, pos_ref, out_ref):
    pos = pos_ref[...]
    lane = lax.rem(pos, LANES)
    line = lax.div(pos, LANES)
    out = jnp.zeros(pos.shape, jnp.float32)
    for r in range(values_ref.shape[0]):
        table = jnp.broadcast_to(values_ref[r : r + 1, :], pos.shape)
        found = jnp.take_along_axis(table, lane, axis=1)
        out = jnp.where(line == r, found, out)
    out_ref[...] = out


def unpack(values, pos):
    vmem = pl.BlockSpec(memory_space=pltpu.VMEM)
    return pl.pallas_call(
        unpack_kernel,
        out_shape=jax.ShapeDtypeStruct(pos.shape, jnp.float32),
        in_specs=[vmem, vmem],
        out_specs=vmem,
    )(values.reshape(-1, LANES), pos)


def swapped(x, first, second):
    return jnp.where(x == first, second, jnp.where(x == second, first, x))


def place_kernel(lay, x_hbm, lab_hbm, map_hbm, *refs):
    main_hbm, tail_ref, pos_ref, x_ref, lab_ref, map_ref, unit, main_ref, sems = refs
    n_owner, capacity, main, home = lay.n_owner, lay.capacity, lay.main, lay.home
    copies = [
        pltpu.make_async_copy(src, dst, sems.at[i])
        for i, (src, dst) in enumerate(((x_hbm, x_ref), (lab_hbm, lab_ref), (map_hbm, map_ref)))
    ]
    for copy in copies:
        copy.start()
    rows, width = x_ref.shape
    n_fine = map_ref.shape[1]
    per_owner = n_fine // n_owner
    copies[1].wait()
    copies[2].wait()
    owner_row = map_ref[...].astype(jnp.float32)
    fine_row = lax.broadcasted_iota(jnp.int32, (1, n_fine), 1).astype(jnp.float32)
    key_row = owner_row * n_fine + fine_row
    key_col = column_of(key_row)
    sorted_col = jnp.sum(jnp.where(key_row < key_col, 1.0, 0.0), axis=1, keepdims=True)
    lab = lab_ref[...].astype(jnp.float32)
    lab_row = jnp.concatenate([lab[b : b + 1, :] for b in range(lab.shape[0])], axis=1)
    fine_col = lax.broadcasted_iota(jnp.int32, (n_fine, rows), 0).astype(jnp.float32)
    fine_id = jnp.sum(jnp.where(fine_col == lab_row, sorted_col, 0.0), axis=0, keepdims=True)
    counts_col = jnp.sum(jnp.where(fine_col == fine_id, 1.0, 0.0), axis=1, keepdims=True)
    coarse = jnp.floor((fine_id + 0.5) * (1.0 / per_owner))
    first = coarse * per_owner
    before = jnp.sum(jnp.where(fine_col < first, counts_col, 0.0), axis=0, keepdims=True)
    upto = jnp.sum(jnp.where(fine_col < first + per_owner, counts_col, 0.0), axis=0, keepdims=True)
    full = jnp.min(
        jnp.where(upto - before == capacity, coarse, float(n_owner)), axis=1, keepdims=True
    )
    line = lax.broadcasted_iota(jnp.int32, (n_fine, LANES), 0)
    lane = lax.broadcasted_iota(jnp.int32, (n_fine, LANES), 1)
    inside = (line <= lane) & (lax.div(line, per_owner) == lax.div(lane, per_owner))
    running = jnp.sum(jnp.where(inside, counts_col, 0.0), axis=0, keepdims=True)
    info = jnp.where(lane[:1] < n_fine, running, full)
    index = lax.broadcasted_iota(jnp.int32, (1, rows), 1).astype(jnp.float32)
    row_key = fine_id * rows + index
    rank = jnp.zeros((1, rows), jnp.float32)
    for start in range(0, rows, LANES):
        other = column_of(row_key[:, start : start + LANES])
        rank = rank + jnp.sum(jnp.where(other < row_key, 1.0, 0.0), axis=0, keepdims=True)
    rank = (rank - before).astype(jnp.int32)
    place = swapped(coarse.astype(jnp.int32), full.astype(jnp.int32), home)
    table = place * capacity + rank
    pos_ref[...] = jnp.concatenate(
        [table[:, start : start + LANES] for start in range(0, rows, LANES)], axis=0
    )
    fits = rank < jnp.where(place == home, lay.head, main - 1)
    slot = jnp.where(fits, place * main + rank, -1)
    tail_slot = jnp.where(place == home, rank - lay.head, -1)
    copies[0].wait()
    x = x_ref[...].astype(jnp.float32)
    squares = jnp.sum(x * x, axis=1, keepdims=True)
    unit[...] = (x * lax.rsqrt(squares + epsilon)).astype(jnp.bfloat16)

    def chosen_rows(slot, start, count):
        here = lax.broadcasted_iota(jnp.int32, (count, rows), 0) + start
        chosen = jnp.where(here == slot, 1.0, 0.0).astype(jnp.bfloat16)
        return jnp.dot(chosen, unit[...], preferred_element_type=jnp.float32)

    count = 2 * main
    down = lax.broadcasted_iota(jnp.int32, (count, LANES), 0)
    is_info = lax.rem(down, main) == main - 1
    writes = []
    for i, start in enumerate(range(0, lay.n_main, count)):
        packed = chosen_rows(slot, start, count)
        place = slice(start, start + count)
        main_ref[place, LANES:] = packed[:, LANES:].astype(jnp.bfloat16)
        main_ref[place, :LANES] = jnp.where(is_info, info, packed[:, :LANES]).astype(jnp.bfloat16)
        writes.append(
            pltpu.make_async_copy(
                main_ref.at[pl.ds(start, count)], main_hbm.at[pl.ds(start, count)], sems.at[3 + i]
            )
        )
        writes[-1].start()
    tail_ref[...] = chosen_rows(tail_slot, 0, lay.rest).astype(jnp.bfloat16)
    for write in writes:
        write.wait()


def vmem_specs(count):
    return (pl.BlockSpec(memory_space=pltpu.VMEM),) * count


def place_rows(embeddings, labels, owner_map, lay):
    rows, width = embeddings.shape
    n_fine = owner_map.shape[0]
    lab_shape = (rows // LANES, LANES)
    anywhere = pl.BlockSpec(memory_space=pl.ANY)
    return pl.pallas_call(
        functools.partial(place_kernel, lay),
        out_shape=(
            jax.ShapeDtypeStruct((lay.n_main, width), jnp.bfloat16),
            jax.ShapeDtypeStruct((lay.rest, width), jnp.bfloat16),
            jax.ShapeDtypeStruct(lab_shape, jnp.int32),
        ),
        in_specs=[anywhere] * 3,
        out_specs=(anywhere,) + vmem_specs(2),
        scratch_shapes=[
            pltpu.VMEM((rows, width), jnp.bfloat16),
            pltpu.VMEM(lab_shape, jnp.int32),
            pltpu.VMEM((1, n_fine), jnp.int32),
            pltpu.VMEM((rows, width), jnp.bfloat16),
            pltpu.VMEM((lay.n_main, width), jnp.bfloat16),
            pltpu.SemaphoreType.DMA((3 + lay.n_owner // 2,)),
        ],
        compiler_params=pltpu.CompilerParams(vmem_limit_bytes=FAST_LIMIT),
    )(embeddings, labels.reshape(lab_shape), owner_map.reshape(1, n_fine))


def gate_kernel(*refs):
    pass


def after(rows, *there):
    return pl.pallas_call(
        gate_kernel,
        out_shape=jax.ShapeDtypeStruct(rows.shape, rows.dtype),
        in_specs=list(vmem_specs(1 + len(there))),
        out_specs=vmem_specs(1)[0],
        input_output_aliases={0: 0},
        compiler_params=pltpu.CompilerParams(vmem_limit_bytes=FAST_LIMIT),
    )(rows, *there)


def lay_out_kernel(n_arrays, home, *refs):
    chunks, out = refs[:n_arrays], refs[-1]

    def copy():
        start = 0
        for chunk in chunks:
            out[start : start + chunk.shape[0], :] = chunk[...]
            start += chunk.shape[0]

    if home is None:
        copy()
    else:
        pl.when(lax.axis_index("cl") == home)(copy)


def lay_out(chunks, home=None, waits=()):
    rows, width = sum(x.shape[0] for x in chunks), chunks[0].shape[1]
    return pl.pallas_call(
        functools.partial(lay_out_kernel, len(chunks), home),
        out_shape=jax.ShapeDtypeStruct((rows, width), jnp.bfloat16),
        in_specs=list(vmem_specs(len(chunks) + len(waits))),
        out_specs=vmem_specs(1)[0],
        compiler_params=pltpu.CompilerParams(vmem_limit_bytes=FAST_LIMIT),
    )(*chunks, *waits)


class Layout:
    early, late = (0, 1, 2, 3), (5, 7, 4, 6)

    def __init__(self, n_owner, n_fine, capacity, main, home):
        self.n_owner, self.n_fine, self.capacity = n_owner, n_fine, capacity
        self.main, self.home = main, home
        self.head = main - INFO
        self.rest = capacity - self.head
        self.per_owner = n_fine // n_owner
        self.n_main = n_owner * main
        self.n_head = n_owner * self.head
        self.n_early = len(self.early) * self.rest
        self.n_late = len(self.late) * self.rest
        self.n_first = self.n_head + self.n_early
        self.n_all = self.n_first + self.n_late


def info_line(lay, main_ref, source):
    end = (source + 1) * lay.main
    return main_ref[end - INFO : end, :LANES].astype(jnp.float32)[INFO - 1 :]


def lines_of(lay, main_ref):
    return [info_line(lay, main_ref, source) for source in range(lay.n_owner)]


def hot_of(lay, info):
    lane = lax.broadcasted_iota(jnp.int32, (1, LANES), 1)
    hot = jnp.max(jnp.where(lane == lay.n_fine, info, 0.0), axis=1, keepdims=True)
    return hot.astype(jnp.int32)


def write_labels(lay, infos, sources, first, count, at, lab_sub, bias):
    cluster = swapped(lax.axis_index("cl"), hot_of(lay, infos[0]), lay.home)
    lane = lax.broadcasted_iota(jnp.int32, (1, LANES), 1)
    is_edge = lax.div(lane, lay.per_owner) == cluster
    for i, source in enumerate(sources):
        edges = jnp.where(is_edge, infos[source], 2.0 * lay.capacity)
        slot = lax.broadcasted_iota(jnp.int32, (count, LANES), 0) + first
        label = jnp.where(slot.astype(jnp.float32) >= edges, 1.0, 0.0)
        label = jnp.broadcast_to(jnp.sum(label, axis=1, keepdims=True), (count, LANES))
        start = at + i * count
        lab_sub[start : start + count, :] = label
        if bias is not None:
            bias[start : start + count, :] = jnp.where(
                label < lay.per_owner, NEIGHBOUR - SCALE, DEAD
            )


def first_labels(lay, infos, lab_sub):
    write_labels(lay, infos, range(lay.n_owner), 0, lay.head, 0, lab_sub, None)
    write_labels(lay, infos, lay.early, lay.head, lay.rest, lay.n_head, lab_sub, None)


def late_labels(lay, infos, lab_sub):
    write_labels(lay, infos, lay.late, lay.head, lay.rest, 0, lab_sub, None)


def turn_labels(lay, lab_sub, count, lab_lane, at):
    for i in range(0, count, LANES):
        block = jnp.transpose(lab_sub[i : i + LANES, :])[:1]
        lab_lane[:, at + i : at + i + LANES] = jnp.where(block < lay.per_owner, block, -1.0)


def copy_head(lay, main_ref, rows):
    for source in range(lay.n_owner):
        rows[source * lay.head : (source + 1) * lay.head, :] = main_ref[
            source * lay.main : source * lay.main + lay.head, :
        ]


def pieces(count, parts):
    return [(i * (count // parts), count // parts) for i in range(parts)]


def stream(lanes, tiles, lab_lane, buffers, put):
    rows_i, count, at = lanes
    step = 32
    tiles = [
        (ref, s, d, lab_sub, bias, line + s, back)
        for ref, n, lab_sub, bias, line, parts, back in tiles
        for s, d in pieces(n, parts)
    ]

    def scores_to(buffer, tile, rows):
        ref, start, deep = tile[:3]
        buffer[:deep, : rows.shape[0]] = lax.dot_general(
            ref[start : start + deep, :],
            rows,
            (((1,), (1,)), ((), ())),
            preferred_element_type=jnp.float32,
        )

    def run(start, blocks, wide):
        repeat = wide // LANES

        def rows_of(block):
            return rows_i[pl.ds(pl.multiple_of(start + block * wide, LANES), wide), :]

        scores_to(buffers[0], tiles[0], rows_of(0))

        def one_block(block):
            here = rows_of(block)
            place = pl.ds(pl.multiple_of(at + start + block * wide, LANES), wide)
            label_i = lab_lane[:, place]
            acc = jnp.zeros((8, wide), jnp.float32)
            for i, (_, _, deep, lab_sub, bias, line, back) in enumerate(tiles):
                if i + 1 < len(tiles):
                    scores_to(buffers[(i + 1) % 2], tiles[i + 1], here)
                elif blocks > 1:

                    @pl.when(block + 1 < blocks)
                    def _():
                        scores_to(buffers[0], tiles[0], rows_of(block + 1))

                buffer = buffers[i % 2]
                for c in range(0, deep, step):
                    part = slice(line + c, line + c + step)
                    label_j = jnp.concatenate([lab_sub[part, :]] * repeat, axis=1)
                    if bias is None:
                        bias_j = NEIGHBOUR - SCALE
                    else:
                        bias_j = jnp.concatenate([bias[part, :]] * repeat, axis=1)
                    shift = jnp.where(label_j == label_i, -SCALE, bias_j)
                    terms = jnp.exp2(buffer[c : c + step, :wide] * SCALE + shift)
                    acc = acc + jnp.sum(terms.reshape(step // 8, 8, wide), axis=0)
                    if back is not None:
                        across = terms[:, :LANES]
                        for r in range(1, repeat):
                            across = across + terms[:, r * LANES : (r + 1) * LANES]
                        back[part, :] += across
            put(place, jnp.sum(acc, axis=0, keepdims=True))

        if blocks == 1:
            one_block(0)
        else:
            pl.loop(0, blocks)(one_block)

    if count >= WIDE:
        run(0, count // WIDE, WIDE)
    if count % WIDE:
        run(count - count % WIDE, 1, count % WIDE)


def turn_sums(back, count, sums, at):
    for i in range(0, count, LANES):
        block = jnp.transpose(back[i : i + LANES, :])
        sums[:, at + i : at + i + LANES] += jnp.sum(block, axis=0, keepdims=True)


def setter(ref):
    def put(place, values):
        ref[:, place] = values

    return put


def adder(ref):
    def put(place, values):
        ref[:, place] += values

    return put


def inner_kernel(lay, mine, early, sums, lab_lane, lab_sub, rows, bias, back, buf_a, buf_b):
    is_home = lax.axis_index("cl") == lay.home
    infos = lines_of(lay, mine)
    buffers = (buf_a, buf_b)

    @pl.when(is_home)
    def _():
        copy_head(lay, mine, rows)
        first_labels(lay, infos, lab_sub)
        turn_labels(lay, lab_sub, lay.n_first, lab_lane, 0)
        back[...] = jnp.zeros(back.shape, jnp.float32)
        size = lay.n_early
        blocks = [(rows.at[pl.ds(start, size)], start) for start in range(0, lay.n_head, size)]
        blocks.append((early, lay.n_head))
        for i, (ref, at) in enumerate(blocks):
            tiles = [
                (ref_j, size, lab_sub, None, at_j, 2, None if at_j == at else back)
                for ref_j, at_j in blocks[i:]
            ]
            stream((ref, size, at), tiles, lab_lane, buffers, setter(sums))
        turn_sums(back, lay.n_first, sums, 0)

    @pl.when(jnp.logical_not(is_home))
    def _():
        write_labels(lay, infos, range(lay.n_owner), 0, lay.main, 0, lab_sub, bias)
        turn_labels(lay, lab_sub, lay.n_main, lab_lane, 0)
        tiles = [(mine, lay.n_main, lab_sub, bias, 0, 2, None)]
        stream((mine, lay.n_main, 0), tiles, lab_lane, buffers, setter(sums))


def half_blocks(ref_i, ref_j, lab_sub, line, back, at, lab_lane, buffers, put):
    half = ref_j.shape[0] // 2
    grp = lax.axis_index("grp")
    for h in range(2):
        start = pl.multiple_of((h ^ grp) * half, half)
        rows_j = ref_j.at[pl.ds(start, half)]
        sub = lab_sub.at[pl.ds(line + start, half)]
        backs = back.at[pl.ds(line + start, half)]
        lanes = (ref_i.at[pl.ds(h * half, half)], half, at + h * half)
        stream(lanes, [(rows_j, half, sub, None, 0, 1, backs)], lab_lane, buffers, put)


def cross_kernel(lay, mine, other, early, early_j, rows, sums, lab_lane, *refs):
    total, for_other, unfit_ref, late_sub, late_sub_j, long_lane, late_lane_j = refs[:7]
    lab_sub, bias, back, rows_j, buf_a, buf_b = refs[7:]
    is_home = lax.axis_index("cl") == lay.home
    infos = lines_of(lay, other)
    own = lines_of(lay, mine)
    hot = hot_of(lay, own[0])
    lane = lax.broadcasted_iota(jnp.int32, (1, LANES), 1)
    last = (lane < lay.n_fine) & (lax.rem(lane, lay.per_owner) == lay.per_owner - 1)
    last = last & (lax.div(lane, lay.per_owner) != hot)
    unfit = jnp.zeros((1, LANES), jnp.float32)
    for info in infos + own:
        wrong = last & (info >= lay.main)
        differs = (info != hot.astype(jnp.float32)) | (info >= lay.n_owner)
        wrong = wrong | ((lane == lay.n_fine) & differs)
        unfit = unfit + jnp.where(wrong, 1.0, 0.0)
    unfit_ref[0, 0] = jnp.max(unfit).astype(jnp.int32)
    total[...] = sums[...]
    buffers = (buf_a, buf_b)

    @pl.when(is_home)
    def _():
        copy_head(lay, other, rows_j)
        first_labels(lay, infos, lab_sub)
        back[...] = jnp.zeros(back.shape, jnp.float32)
        size = lay.n_early
        blocks_i = [rows.at[pl.ds(start, size)] for start in range(0, lay.n_head, size)] + [early]
        blocks_j = [rows_j.at[pl.ds(start, size)] for start in range(0, lay.n_head, size)]
        blocks_j.append(early_j)
        put, n = adder(total), len(blocks_i)
        for i, ref in enumerate(blocks_i):
            tiles = [
                (blocks_j[j], size, lab_sub, None, j * size, 2, back)
                for j in ((i + step) % n for step in range(1, (n + 1) // 2))
            ]
            stream((ref, size, i * size), tiles, lab_lane, buffers, put)
            half_blocks(
                ref, blocks_j[i], lab_sub, i * size, back, i * size, lab_lane, buffers, put
            )
        write_labels(lay, own, lay.late, lay.head, lay.rest, 0, late_sub, None)
        write_labels(lay, infos, lay.late, lay.head, lay.rest, 0, late_sub_j, None)
        long_lane[:, : lay.n_first] = lab_lane[...]
        turn_labels(lay, late_sub, lay.n_late, long_lane, lay.n_first)
        turn_labels(lay, late_sub_j, lay.n_late, late_lane_j, 0)
        for_other[...] = jnp.zeros(for_other.shape, jnp.float32)
        turn_sums(back, lay.n_first, for_other, 0)

    @pl.when(jnp.logical_not(is_home))
    def _():
        write_labels(lay, infos, range(lay.n_owner), 0, lay.main, 0, lab_sub, bias)
        tiles = [(other, lay.n_main, lab_sub, bias, 0, 2, None)]
        stream((mine, lay.n_main, 0), tiles, lab_lane, buffers, adder(total))


def first_tiles(lay, rows, early, lab_sub, back):
    return [
        (rows, lay.n_head, lab_sub, None, 0, 4, back),
        (early, lay.n_early, lab_sub, None, lay.n_head, 2, back),
    ]


def inner_late_kernel(lay, early, late, rows, lab_sub, late_sub, lab_lane, sums, *refs):
    back, buf_a, buf_b = refs

    @pl.when(lax.axis_index("cl") == lay.home)
    def _():
        back[...] = jnp.zeros(back.shape, jnp.float32)
        sums[:, : lay.n_first] = jnp.zeros((1, lay.n_first), jnp.float32)
        tiles = first_tiles(lay, rows, early, lab_sub, back)
        tiles.append((late, lay.n_late, late_sub, None, 0, 2, None))
        lanes = (late, lay.n_late, lay.n_first)
        stream(lanes, tiles, lab_lane, (buf_a, buf_b), setter(sums))
        turn_sums(back, lay.n_first, sums, 0)


def cross_late_kernel(lay, early, late, late_j, rows, lab_sub, late_sub, lab_lane, *refs):
    late_lane, first_lane, first_sums, first_other, sums, out_ref = refs[:6]
    total, late_other, back, late_back, buf_a, buf_b = refs[6:]
    is_home = lax.axis_index("cl") == lay.home
    grp = lax.axis_index("grp")

    @pl.when(is_home)
    def _():
        total[...] = sums[...]
        total[:, : lay.n_first] += first_sums[...]
        back[...] = jnp.zeros(back.shape, jnp.float32)
        late_back[...] = jnp.zeros(late_back.shape, jnp.float32)
        buffers = (buf_a, buf_b)
        tiles = first_tiles(lay, rows, early, lab_sub, back)
        stream((late_j, lay.n_late, 0), tiles, late_lane, buffers, setter(late_other))
        turn_sums(back, lay.n_first, total, 0)
        put = adder(total)
        half_blocks(late, late_j, late_sub, 0, late_back, lay.n_first, lab_lane, buffers, put)
        turn_sums(late_back, lay.n_late, late_other, 0)

        def write(line, values):
            for source in range(lay.n_owner):
                start = source * lay.head
                out_ref[2 * source + line, :, : lay.head] = values[:, start : start + lay.head]
            for i, source in enumerate(lay.early + lay.late):
                start = lay.n_head + i * lay.rest
                out_ref[2 * source + line, :, lay.head :] = values[:, start : start + lay.rest]

        write(grp, total[...])
        total[:, : lay.n_first] = first_other[...]
        total[:, lay.n_first :] = late_other[...]
        write(1 - grp, total[...])

    @pl.when(jnp.logical_not(is_home))
    def _():
        out_ref[...] = jnp.zeros(out_ref.shape, jnp.float32)
        values = jnp.where(first_lane[...] >= 0, first_sums[...], 1.0)
        for source in range(lay.n_owner):
            start = source * lay.main
            out_ref[2 * source + grp, :, : lay.main] = values[:, start : start + lay.main]


def pair_call(kernel, lay, arrays, out_shape, scratch, out_specs=None, pairs=0):
    width = arrays[0].shape[1]
    buffer = pltpu.VMEM((lay.n_main // 2, WIDE), jnp.float32)
    return pl.pallas_call(
        functools.partial(kernel, lay),
        out_shape=out_shape,
        in_specs=list(vmem_specs(len(arrays))),
        out_specs=out_specs or vmem_specs(len(out_shape)),
        scratch_shapes=list(scratch) + [buffer, buffer],
        compiler_params=pltpu.CompilerParams(vmem_limit_bytes=FAST_LIMIT),
        cost_estimate=pl.CostEstimate(
            flops=2 * pairs * width, bytes_accessed=1, transcendentals=pairs
        ),
    )(*arrays)


def fast_unpack_kernel(values_ref, pos_ref, out_ref):
    pos = pos_ref[...]
    lane = lax.rem(pos, LANES)
    line = lax.div(pos, LANES)
    out = jnp.ones(pos.shape, jnp.float32)
    per = values_ref.shape[2] // LANES
    for r in range(values_ref.shape[0] // 2 * per):
        owner, part = r // per, slice(r % per * LANES, (r % per + 1) * LANES)
        table = values_ref[2 * owner, :, part] + values_ref[2 * owner + 1, :, part]
        found = jnp.take_along_axis(jnp.broadcast_to(table, pos.shape), lane, axis=1)
        out = jnp.where(line == r, found, out)
    out_ref[...] = jnp.log(out)


def fast_unpack(values, pos):
    vmem = pl.BlockSpec(memory_space=pltpu.VMEM)
    return pl.pallas_call(
        fast_unpack_kernel,
        out_shape=jax.ShapeDtypeStruct(pos.shape, jnp.float32),
        in_specs=[vmem, vmem],
        out_specs=vmem,
    )(values, pos)


def general(embeddings, labels, owner_map):
    n_owner = lax.axis_size("cl")
    capacity = SLOTS // n_owner
    rows, width = embeddings.shape
    packed, pos, counts = pack(embeddings, labels, owner_map, n_owner, capacity)
    counts = lax.all_gather(counts, ("cl", "grp"), tiled=True)
    mine = lax.all_to_all(
        packed.reshape(n_owner, capacity, width), "cl", split_axis=0, concat_axis=0, tiled=True
    ).reshape(SLOTS, width)
    other = lax.ppermute(mine, "grp", [(0, 1), (1, 0)])
    results = log_counts(counts, mine, other, n_owner, capacity)
    returned = lax.all_to_all(
        results.reshape(n_owner, capacity), "cl", split_axis=0, concat_axis=0, tiled=True
    )
    return unpack(returned.reshape(SLOTS), pos).reshape(rows)


def body(embeddings, labels, owner_map):
    n_owner = lax.axis_size("cl")
    capacity = SLOTS // n_owner
    rows, width = embeddings.shape
    n_fine = owner_map.shape[0]
    main = -(-(rows // n_owner * 9 // 8) // 16) * 16
    if n_owner != 8 or main >= capacity or n_fine >= LANES:
        return general(embeddings, labels, owner_map)
    home = 2
    lay = Layout(n_owner, n_fine, capacity, main, home)
    packed, extra, pos = place_rows(embeddings, labels, owner_map, lay)

    def hop(x, pairs):
        return lax.ppermute(x, "cl", pairs)

    def swap(x):
        return lax.ppermute(x, "grp", [(0, 1), (1, 0)])

    both = lay_out([extra, hop(extra, [(6, 4), (7, 5)])])
    early = [extra if s == home else hop(extra, [(s, home)]) for s in lay.early]
    early = lay_out(early, home)
    mine = lax.all_to_all(
        packed.reshape(n_owner, main, width), "cl", split_axis=0, concat_axis=0, tiled=True
    ).reshape(n_owner * main, width)
    mine = after(mine, early, both)
    other, early_j = swap(mine), swap(early)
    late = [hop(both, [(s, home)]) for s in (5, 4)]

    def array(shape, dtype=jnp.float32):
        return jax.ShapeDtypeStruct(shape, dtype)

    def scratch(shape):
        return pltpu.VMEM(shape, jnp.float32)

    row, long_row = array((1, lay.n_first)), array((1, lay.n_all))
    bias = scratch((lay.n_main, LANES))
    heads = array((lay.n_head, width), jnp.bfloat16)
    late_lines, first_lines = array((lay.n_late, LANES)), array((lay.n_first, LANES))
    late_row = array((1, lay.n_late))
    late_side, first_side = scratch((lay.n_late, LANES)), scratch((lay.n_first, LANES))
    sums, first_lane, lab_sub, heads_i = pair_call(
        inner_kernel, lay, (mine, early), (row, row, first_lines, heads), (bias, first_side)
    )
    specs = vmem_specs(2) + (pl.BlockSpec(memory_space=pltpu.SMEM),) + vmem_specs(4)
    sums, first_other, unfit, late_sub, late_sub_j, lane, lane_j = pair_call(
        cross_kernel,
        lay,
        (mine, other, early, early_j, heads_i, sums, first_lane),
        (row, row, array((1, 1), jnp.int32), late_lines, late_lines, long_row, late_row),
        (first_side, bias, first_side, pltpu.VMEM(heads.shape, heads.dtype)),
        specs,
    )
    late = lay_out(late, home, (sums,))
    late_j = swap(late)
    (late_sums,) = pair_call(
        inner_late_kernel,
        lay,
        (early, late, heads_i, lab_sub, late_sub, lane),
        (long_row,),
        (first_side,),
        pairs=lay.n_late * lay.n_all,
    )
    (results,) = pair_call(
        cross_late_kernel,
        lay,
        (
            *(early, late, late_j, heads_i, lab_sub, late_sub_j, lane, lane_j),
            *(first_lane, sums, first_other, late_sums),
        ),
        (array((2 * n_owner, 1, capacity)),),
        (scratch(long_row.shape), scratch(late_row.shape), first_side, late_side),
    )
    returned = lax.all_to_all(
        results, ("cl", "grp"), split_axis=0, concat_axis=0, tiled=True
    )
    return lax.cond(
        unfit[0, 0] == 0,
        lambda: fast_unpack(returned, pos).reshape(rows),
        lambda: general(embeddings, labels, owner_map),
    )


def solution(mesh):
    return jax.shard_map(
        body,
        mesh=mesh,
        in_specs=(P(("parts", "cl", "grp"), None), P(("parts", "cl", "grp")), P("parts")),
        out_specs=P(("parts", "cl", "grp")),
        check_vma=False,
    )
```

```python
import functools
import math

import jax
import jax.numpy as jnp
from jax import lax
from jax.experimental import pallas as pl
from jax.experimental.pallas import tpu as pltpu
from jax.sharding import PartitionSpec as P

SLOTS = 2048

temper = 0.2
neighbour_factor = 0.5
epsilon = 1e-06

LANES = 128
SCALE = math.log2(math.e) / temper
NEIGHBOUR = math.log2(neighbour_factor)
DEAD = -1e30
VMEM_LIMIT = 48 * 1024 * 1024
FAST_LIMIT = 16 * 1024 * 1024
WIDE = 512
INFO = 16


def column_of(row):
    pieces = []
    for start in range(0, row.shape[1], LANES):
        width = min(LANES, row.shape[1] - start)
        shape = (width, width)
        diagonal = lax.broadcasted_iota(jnp.int32, shape, 0) == lax.broadcasted_iota(
            jnp.int32, shape, 1
        )
        piece = jnp.broadcast_to(row[:, start : start + width], shape)
        pieces.append(jnp.sum(jnp.where(diagonal, piece, 0.0), axis=1, keepdims=True))
    return jnp.concatenate(pieces, axis=0)


def row_of(column):
    n = column.shape[0]
    diagonal = lax.broadcasted_iota(jnp.int32, (n, n), 0) == lax.broadcasted_iota(
        jnp.int32, (n, n), 1
    )
    return jnp.sum(jnp.where(diagonal, column, 0.0), axis=0, keepdims=True)


def pack_kernel(n_owner, capacity, x_ref, lab_ref, map_ref, out_ref, pos_ref, cnt_ref, unit, pos_row):
    rows = x_ref.shape[0]
    n_fine = map_ref.shape[1]
    per_owner = n_fine // n_owner
    owner_row = map_ref[...].astype(jnp.float32)
    fine_row = lax.broadcasted_iota(jnp.int32, (1, n_fine), 1).astype(jnp.float32)
    key_row = owner_row * n_fine + fine_row
    key_col = column_of(key_row)
    sorted_col = jnp.sum(jnp.where(key_row < key_col, 1.0, 0.0), axis=1, keepdims=True)
    lab = lab_ref[...].astype(jnp.float32)
    lab_row = jnp.concatenate([lab[b : b + 1, :] for b in range(lab.shape[0])], axis=1)
    fine_col = lax.broadcasted_iota(jnp.int32, (n_fine, rows), 0).astype(jnp.float32)
    fine_id = jnp.sum(jnp.where(fine_col == lab_row, sorted_col, 0.0), axis=0, keepdims=True)
    counts_col = jnp.sum(jnp.where(fine_col == fine_id, 1.0, 0.0), axis=1, keepdims=True)
    cnt_ref[...] = row_of(counts_col).astype(jnp.int32)
    coarse = jnp.floor((fine_id + 0.5) * (1.0 / per_owner))
    before = jnp.sum(
        jnp.where(fine_col < coarse * per_owner, counts_col, 0.0), axis=0, keepdims=True
    )
    index = lax.broadcasted_iota(jnp.int32, (1, rows), 1).astype(jnp.float32)
    row_key = fine_id * rows + index
    rank = jnp.zeros((1, rows), jnp.float32)
    for start in range(0, rows, LANES):
        other = column_of(row_key[:, start : start + LANES])
        rank = rank + jnp.sum(jnp.where(other < row_key, 1.0, 0.0), axis=0, keepdims=True)
    pos = (coarse * capacity + rank - before).astype(jnp.int32)
    pos_row[...] = pos
    pos_ref[...] = jnp.concatenate(
        [pos[:, start : start + LANES] for start in range(0, rows, LANES)], axis=0
    )
    x = x_ref[...].astype(jnp.float32)
    squares = jnp.sum(x * x, axis=1, keepdims=True)
    unit[...] = (x * lax.rsqrt(squares + epsilon)).astype(jnp.bfloat16)

    step = 256

    @pl.loop(0, out_ref.shape[0] // step)
    def _(block):
        slot = lax.broadcasted_iota(jnp.int32, (step, rows), 0) + block * step
        chosen = jnp.where(slot == pos_row[...], 1.0, 0.0).astype(jnp.bfloat16)
        packed = jnp.dot(chosen, unit[...], preferred_element_type=jnp.float32)
        out_ref[pl.ds(pl.multiple_of(block * step, step), step), :] = packed.astype(jnp.bfloat16)


def pack(embeddings, labels, owner_map, n_owner, capacity):
    rows, width = embeddings.shape
    n_fine = owner_map.shape[0]
    total = n_owner * capacity
    vmem = pl.BlockSpec(memory_space=pltpu.VMEM)
    return pl.pallas_call(
        functools.partial(pack_kernel, n_owner, capacity),
        out_shape=(
            jax.ShapeDtypeStruct((total, width), jnp.bfloat16),
            jax.ShapeDtypeStruct((rows // LANES, LANES), jnp.int32),
            jax.ShapeDtypeStruct((1, n_fine), jnp.int32),
        ),
        in_specs=[vmem] * 3,
        out_specs=(vmem, vmem, vmem),
        scratch_shapes=[pltpu.VMEM((rows, width), jnp.bfloat16), pltpu.VMEM((1, rows), jnp.int32)],
        compiler_params=pltpu.CompilerParams(vmem_limit_bytes=VMEM_LIMIT),
    )(embeddings, labels.reshape(rows // LANES, LANES), owner_map.reshape(1, n_fine))


def counts_kernel(n_owner, capacity, cnt_ref, mine_ref, other_ref, out_ref, lab_lane, lab_sub, bias):
    total = mine_ref.shape[0]
    per_owner = cnt_ref.shape[1] // n_owner
    me = lax.axis_index("cl")
    grp = lax.axis_index("grp")
    n_grp = lax.axis_size("grp")
    for member in range(2):
        for source in range(n_owner):
            line = source * n_grp + lax.rem(grp + member, n_grp)
            edges = []
            edge = jnp.int32(0)
            for f in range(per_owner):
                edge = edge + cnt_ref[line, me * per_owner + f]
                edges.append(edge)
            down = lax.broadcasted_iota(jnp.int32, (capacity, LANES), 0)
            label = jnp.zeros((capacity, LANES), jnp.int32)
            for edge in edges:
                label = label + jnp.where(down >= edge, 1, 0)
            start = (member * n_owner + source) * capacity
            lab_sub[start : start + capacity, :] = label
            bias[start : start + capacity, :] = jnp.where(
                label < per_owner, NEIGHBOUR - SCALE, DEAD
            )
            if member == 0:
                across = lax.broadcasted_iota(jnp.int32, (1, capacity), 1)
                label = jnp.zeros((1, capacity), jnp.int32)
                for edge in edges:
                    label = label + jnp.where(across >= edge, 1, 0)
                lab_lane[:, source * capacity : (source + 1) * capacity] = jnp.where(
                    label < per_owner, label, -1
                )
    wide, deep = min(512, total), min(256, total)

    @pl.loop(0, total // wide)
    def _(block):
        columns = pl.ds(pl.multiple_of(block * wide, wide), wide)
        rows_i = mine_ref[columns, :]
        label_i = lab_lane[:, columns]

        def add(ref, offset):
            def step(j, acc):
                start = pl.multiple_of(j * deep, deep)
                scores = lax.dot_general(
                    ref[pl.ds(start, deep), :],
                    rows_i,
                    (((1,), (1,)), ((), ())),
                    preferred_element_type=jnp.float32,
                )
                place = pl.ds(pl.multiple_of(start + offset, deep), deep)
                label_j = lab_sub[place, :]
                bias_j = bias[place, :]
                repeat = wide // LANES
                label_j = jnp.concatenate([label_j] * repeat, axis=1)
                bias_j = jnp.concatenate([bias_j] * repeat, axis=1)
                shift = jnp.where(label_j == label_i, -SCALE, bias_j)
                terms = jnp.exp2(scores * SCALE + shift)
                return acc + jnp.sum(terms.reshape(deep // 8, 8, wide), axis=0)

            return step

        acc = jnp.zeros((8, wide), jnp.float32)
        acc = lax.fori_loop(0, total // deep, add(mine_ref, 0), acc, unroll=2)
        acc = lax.fori_loop(0, total // deep, add(other_ref, total), acc, unroll=2)
        totals = jnp.sum(acc, axis=0, keepdims=True)
        out_ref[:, columns] = jnp.log(jnp.where(label_i >= 0, totals, 1.0))


def log_counts(counts, mine, other, n_owner, capacity):
    total = mine.shape[0]
    vmem = pl.BlockSpec(memory_space=pltpu.VMEM)
    return pl.pallas_call(
        functools.partial(counts_kernel, n_owner, capacity),
        out_shape=jax.ShapeDtypeStruct((1, total), jnp.float32),
        in_specs=[pl.BlockSpec(memory_space=pltpu.SMEM), vmem, vmem],
        out_specs=vmem,
        scratch_shapes=[
            pltpu.VMEM((1, total), jnp.int32),
            pltpu.VMEM((2 * total, LANES), jnp.int32),
            pltpu.VMEM((2 * total, LANES), jnp.float32),
        ],
        compiler_params=pltpu.CompilerParams(vmem_limit_bytes=VMEM_LIMIT),
    )(counts, mine, other)


def unpack_kernel(values_ref, pos_ref, out_ref):
    pos = pos_ref[...]
    lane = lax.rem(pos, LANES)
    line = lax.div(pos, LANES)
    out = jnp.zeros(pos.shape, jnp.float32)
    for r in range(values_ref.shape[0]):
        table = jnp.broadcast_to(values_ref[r : r + 1, :], pos.shape)
        found = jnp.take_along_axis(table, lane, axis=1)
        out = jnp.where(line == r, found, out)
    out_ref[...] = out


def unpack(values, pos):
    vmem = pl.BlockSpec(memory_space=pltpu.VMEM)
    return pl.pallas_call(
        unpack_kernel,
        out_shape=jax.ShapeDtypeStruct(pos.shape, jnp.float32),
        in_specs=[vmem, vmem],
        out_specs=vmem,
    )(values.reshape(-1, LANES), pos)


def swapped(x, first, second):
    return jnp.where(x == first, second, jnp.where(x == second, first, x))


def place_kernel(lay, x_hbm, lab_hbm, map_hbm, *refs):
    main_hbm, tail_ref, pos_ref, x_ref, lab_ref, map_ref, unit, main_ref, sems = refs
    n_owner, capacity, main, home = lay.n_owner, lay.capacity, lay.main, lay.home
    copies = [
        pltpu.make_async_copy(src, dst, sems.at[i])
        for i, (src, dst) in enumerate(((x_hbm, x_ref), (lab_hbm, lab_ref), (map_hbm, map_ref)))
    ]
    for copy in copies:
        copy.start()
    rows, width = x_ref.shape
    n_fine = map_ref.shape[1]
    per_owner = n_fine // n_owner
    copies[1].wait()
    copies[2].wait()
    owner_row = map_ref[...].astype(jnp.float32)
    fine_row = lax.broadcasted_iota(jnp.int32, (1, n_fine), 1).astype(jnp.float32)
    key_row = owner_row * n_fine + fine_row
    key_col = column_of(key_row)
    sorted_col = jnp.sum(jnp.where(key_row < key_col, 1.0, 0.0), axis=1, keepdims=True)
    lab = lab_ref[...].astype(jnp.float32)
    lab_row = jnp.concatenate([lab[b : b + 1, :] for b in range(lab.shape[0])], axis=1)
    fine_col = lax.broadcasted_iota(jnp.int32, (n_fine, rows), 0).astype(jnp.float32)
    fine_id = jnp.sum(jnp.where(fine_col == lab_row, sorted_col, 0.0), axis=0, keepdims=True)
    counts_col = jnp.sum(jnp.where(fine_col == fine_id, 1.0, 0.0), axis=1, keepdims=True)
    coarse = jnp.floor((fine_id + 0.5) * (1.0 / per_owner))
    first = coarse * per_owner
    before = jnp.sum(jnp.where(fine_col < first, counts_col, 0.0), axis=0, keepdims=True)
    upto = jnp.sum(jnp.where(fine_col < first + per_owner, counts_col, 0.0), axis=0, keepdims=True)
    full = jnp.min(
        jnp.where(upto - before == capacity, coarse, float(n_owner)), axis=1, keepdims=True
    )
    line = lax.broadcasted_iota(jnp.int32, (n_fine, LANES), 0)
    lane = lax.broadcasted_iota(jnp.int32, (n_fine, LANES), 1)
    inside = (line <= lane) & (lax.div(line, per_owner) == lax.div(lane, per_owner))
    running = jnp.sum(jnp.where(inside, counts_col, 0.0), axis=0, keepdims=True)
    info = jnp.where(lane[:1] < n_fine, running, full)
    index = lax.broadcasted_iota(jnp.int32, (1, rows), 1).astype(jnp.float32)
    row_key = fine_id * rows + index
    rank = jnp.zeros((1, rows), jnp.float32)
    for start in range(0, rows, LANES):
        other = column_of(row_key[:, start : start + LANES])
        rank = rank + jnp.sum(jnp.where(other < row_key, 1.0, 0.0), axis=0, keepdims=True)
    rank = (rank - before).astype(jnp.int32)
    place = swapped(coarse.astype(jnp.int32), full.astype(jnp.int32), home)
    table = place * capacity + rank
    pos_ref[...] = jnp.concatenate(
        [table[:, start : start + LANES] for start in range(0, rows, LANES)], axis=0
    )
    fits = rank < jnp.where(place == home, lay.head, main - 1)
    slot = jnp.where(fits, place * main + rank, -1)
    tail_slot = jnp.where(place == home, rank - lay.head, -1)
    copies[0].wait()
    x = x_ref[...].astype(jnp.float32)
    squares = jnp.sum(x * x, axis=1, keepdims=True)
    unit[...] = (x * lax.rsqrt(squares + epsilon)).astype(jnp.bfloat16)

    def chosen_rows(slot, start, count):
        here = lax.broadcasted_iota(jnp.int32, (count, rows), 0) + start
        chosen = jnp.where(here == slot, 1.0, 0.0).astype(jnp.bfloat16)
        return jnp.dot(chosen, unit[...], preferred_element_type=jnp.float32)

    count = 2 * main
    down = lax.broadcasted_iota(jnp.int32, (count, LANES), 0)
    is_info = lax.rem(down, main) == main - 1
    writes = []
    for i, start in enumerate(range(0, lay.n_main, count)):
        packed = chosen_rows(slot, start, count)
        place = slice(start, start + count)
        main_ref[place, LANES:] = packed[:, LANES:].astype(jnp.bfloat16)
        main_ref[place, :LANES] = jnp.where(is_info, info, packed[:, :LANES]).astype(jnp.bfloat16)
        writes.append(
            pltpu.make_async_copy(
                main_ref.at[pl.ds(start, count)], main_hbm.at[pl.ds(start, count)], sems.at[3 + i]
            )
        )
        writes[-1].start()
    tail_ref[...] = chosen_rows(tail_slot, 0, lay.rest).astype(jnp.bfloat16)
    for write in writes:
        write.wait()


def vmem_specs(count):
    return (pl.BlockSpec(memory_space=pltpu.VMEM),) * count


def place_rows(embeddings, labels, owner_map, lay):
    rows, width = embeddings.shape
    n_fine = owner_map.shape[0]
    lab_shape = (rows // LANES, LANES)
    anywhere = pl.BlockSpec(memory_space=pl.ANY)
    return pl.pallas_call(
        functools.partial(place_kernel, lay),
        out_shape=(
            jax.ShapeDtypeStruct((lay.n_main, width), jnp.bfloat16),
            jax.ShapeDtypeStruct((lay.rest, width), jnp.bfloat16),
            jax.ShapeDtypeStruct(lab_shape, jnp.int32),
        ),
        in_specs=[anywhere] * 3,
        out_specs=(anywhere,) + vmem_specs(2),
        scratch_shapes=[
            pltpu.VMEM((rows, width), jnp.bfloat16),
            pltpu.VMEM(lab_shape, jnp.int32),
            pltpu.VMEM((1, n_fine), jnp.int32),
            pltpu.VMEM((rows, width), jnp.bfloat16),
            pltpu.VMEM((lay.n_main, width), jnp.bfloat16),
            pltpu.SemaphoreType.DMA((3 + lay.n_owner // 2,)),
        ],
        compiler_params=pltpu.CompilerParams(vmem_limit_bytes=FAST_LIMIT),
    )(embeddings, labels.reshape(lab_shape), owner_map.reshape(1, n_fine))


def gate_kernel(*refs):
    pass


def after(rows, *there):
    return pl.pallas_call(
        gate_kernel,
        out_shape=jax.ShapeDtypeStruct(rows.shape, rows.dtype),
        in_specs=list(vmem_specs(1 + len(there))),
        out_specs=vmem_specs(1)[0],
        input_output_aliases={0: 0},
        compiler_params=pltpu.CompilerParams(vmem_limit_bytes=FAST_LIMIT),
    )(rows, *there)


def lay_out_kernel(n_arrays, home, *refs):
    chunks, out = refs[:n_arrays], refs[-1]

    def copy():
        start = 0
        for chunk in chunks:
            out[start : start + chunk.shape[0], :] = chunk[...]
            start += chunk.shape[0]

    if home is None:
        copy()
    else:
        pl.when(lax.axis_index("cl") == home)(copy)


def lay_out(chunks, home=None, waits=()):
    rows, width = sum(x.shape[0] for x in chunks), chunks[0].shape[1]
    return pl.pallas_call(
        functools.partial(lay_out_kernel, len(chunks), home),
        out_shape=jax.ShapeDtypeStruct((rows, width), jnp.bfloat16),
        in_specs=list(vmem_specs(len(chunks) + len(waits))),
        out_specs=vmem_specs(1)[0],
        compiler_params=pltpu.CompilerParams(vmem_limit_bytes=FAST_LIMIT),
    )(*chunks, *waits)


class Layout:
    early, late = (0, 1, 2, 3), (5, 7, 4, 6)

    def __init__(self, n_owner, n_fine, capacity, main, home):
        self.n_owner, self.n_fine, self.capacity = n_owner, n_fine, capacity
        self.main, self.home = main, home
        self.head = main - INFO
        self.rest = capacity - self.head
        self.per_owner = n_fine // n_owner
        self.n_main = n_owner * main
        self.n_head = n_owner * self.head
        self.n_early = len(self.early) * self.rest
        self.n_late = len(self.late) * self.rest
        self.n_first = self.n_head + self.n_early
        self.n_all = self.n_first + self.n_late


def info_line(lay, main_ref, source):
    end = (source + 1) * lay.main
    return main_ref[end - INFO : end, :LANES].astype(jnp.float32)[INFO - 1 :]


def lines_of(lay, main_ref):
    return [info_line(lay, main_ref, source) for source in range(lay.n_owner)]


def hot_of(lay, info):
    lane = lax.broadcasted_iota(jnp.int32, (1, LANES), 1)
    hot = jnp.max(jnp.where(lane == lay.n_fine, info, 0.0), axis=1, keepdims=True)
    return hot.astype(jnp.int32)


def write_labels(lay, infos, sources, first, count, at, lab_sub, bias):
    cluster = swapped(lax.axis_index("cl"), hot_of(lay, infos[0]), lay.home)
    lane = lax.broadcasted_iota(jnp.int32, (1, LANES), 1)
    is_edge = lax.div(lane, lay.per_owner) == cluster
    for i, source in enumerate(sources):
        edges = jnp.where(is_edge, infos[source], 2.0 * lay.capacity)
        slot = lax.broadcasted_iota(jnp.int32, (count, LANES), 0) + first
        label = jnp.where(slot.astype(jnp.float32) >= edges, 1.0, 0.0)
        label = jnp.broadcast_to(jnp.sum(label, axis=1, keepdims=True), (count, LANES))
        start = at + i * count
        lab_sub[start : start + count, :] = label
        if bias is not None:
            bias[start : start + count, :] = jnp.where(
                label < lay.per_owner, NEIGHBOUR - SCALE, DEAD
            )


def first_labels(lay, infos, lab_sub):
    write_labels(lay, infos, range(lay.n_owner), 0, lay.head, 0, lab_sub, None)
    write_labels(lay, infos, lay.early, lay.head, lay.rest, lay.n_head, lab_sub, None)


def late_labels(lay, infos, lab_sub):
    write_labels(lay, infos, lay.late, lay.head, lay.rest, 0, lab_sub, None)


def turn_labels(lay, lab_sub, count, lab_lane, at):
    for i in range(0, count, LANES):
        block = jnp.transpose(lab_sub[i : i + LANES, :])[:1]
        lab_lane[:, at + i : at + i + LANES] = jnp.where(block < lay.per_owner, block, -1.0)


def copy_head(lay, main_ref, rows):
    for source in range(lay.n_owner):
        rows[source * lay.head : (source + 1) * lay.head, :] = main_ref[
            source * lay.main : source * lay.main + lay.head, :
        ]


def pieces(count, parts):
    return [(i * (count // parts), count // parts) for i in range(parts)]


def stream(lanes, tiles, lab_lane, buffers, put):
    rows_i, count, at = lanes
    step = 32
    tiles = [
        (ref, s, d, lab_sub, bias, line + s, back)
        for ref, n, lab_sub, bias, line, parts, back in tiles
        for s, d in pieces(n, parts)
    ]

    def scores_to(buffer, tile, rows):
        ref, start, deep = tile[:3]
        buffer[:deep, : rows.shape[0]] = lax.dot_general(
            ref[start : start + deep, :],
            rows,
            (((1,), (1,)), ((), ())),
            preferred_element_type=jnp.float32,
        )

    def run(start, blocks, wide):
        repeat = wide // LANES

        def rows_of(block):
            return rows_i[pl.ds(pl.multiple_of(start + block * wide, LANES), wide), :]

        scores_to(buffers[0], tiles[0], rows_of(0))

        def one_block(block):
            here = rows_of(block)
            place = pl.ds(pl.multiple_of(at + start + block * wide, LANES), wide)
            label_i = lab_lane[:, place]
            acc = jnp.zeros((8, wide), jnp.float32)
            for i, (_, _, deep, lab_sub, bias, line, back) in enumerate(tiles):
                if i + 1 < len(tiles):
                    scores_to(buffers[(i + 1) % 2], tiles[i + 1], here)
                elif blocks > 1:

                    @pl.when(block + 1 < blocks)
                    def _():
                        scores_to(buffers[0], tiles[0], rows_of(block + 1))

                buffer = buffers[i % 2]
                for c in range(0, deep, step):
                    part = slice(line + c, line + c + step)
                    label_j = jnp.concatenate([lab_sub[part, :]] * repeat, axis=1)
                    if bias is None:
                        bias_j = NEIGHBOUR - SCALE
                    else:
                        bias_j = jnp.concatenate([bias[part, :]] * repeat, axis=1)
                    shift = jnp.where(label_j == label_i, -SCALE, bias_j)
                    terms = jnp.exp2(buffer[c : c + step, :wide] * SCALE + shift)
                    acc = acc + jnp.sum(terms.reshape(step // 8, 8, wide), axis=0)
                    if back is not None:
                        across = terms[:, :LANES]
                        for r in range(1, repeat):
                            across = across + terms[:, r * LANES : (r + 1) * LANES]
                        back[part, :] += across
            put(place, jnp.sum(acc, axis=0, keepdims=True))

        if blocks == 1:
            one_block(0)
        else:
            pl.loop(0, blocks)(one_block)

    if count >= WIDE:
        run(0, count // WIDE, WIDE)
    if count % WIDE:
        run(count - count % WIDE, 1, count % WIDE)


def turn_sums(back, count, sums, at):
    for i in range(0, count, LANES):
        block = jnp.transpose(back[i : i + LANES, :])
        sums[:, at + i : at + i + LANES] += jnp.sum(block, axis=0, keepdims=True)


def setter(ref):
    def put(place, values):
        ref[:, place] = values

    return put


def adder(ref):
    def put(place, values):
        ref[:, place] += values

    return put


def inner_kernel(lay, mine, early, sums, lab_lane, lab_sub, rows, bias, back, buf_a, buf_b):
    is_home = lax.axis_index("cl") == lay.home
    infos = lines_of(lay, mine)
    buffers = (buf_a, buf_b)

    @pl.when(is_home)
    def _():
        copy_head(lay, mine, rows)
        first_labels(lay, infos, lab_sub)
        turn_labels(lay, lab_sub, lay.n_first, lab_lane, 0)
        back[...] = jnp.zeros(back.shape, jnp.float32)
        size = lay.n_early
        blocks = [(rows.at[pl.ds(start, size)], start) for start in range(0, lay.n_head, size)]
        blocks.append((early, lay.n_head))
        for i, (ref, at) in enumerate(blocks):
            tiles = [
                (ref_j, size, lab_sub, None, at_j, 2, None if at_j == at else back)
                for ref_j, at_j in blocks[i:]
            ]
            stream((ref, size, at), tiles, lab_lane, buffers, setter(sums))
        turn_sums(back, lay.n_first, sums, 0)

    @pl.when(jnp.logical_not(is_home))
    def _():
        write_labels(lay, infos, range(lay.n_owner), 0, lay.main, 0, lab_sub, bias)
        turn_labels(lay, lab_sub, lay.n_main, lab_lane, 0)
        tiles = [(mine, lay.n_main, lab_sub, bias, 0, 2, None)]
        stream((mine, lay.n_main, 0), tiles, lab_lane, buffers, setter(sums))


def half_blocks(ref_i, ref_j, lab_sub, line, back, at, lab_lane, buffers, put):
    half = ref_j.shape[0] // 2
    grp = lax.axis_index("grp")
    for h in range(2):
        start = pl.multiple_of((h ^ grp) * half, half)
        rows_j = ref_j.at[pl.ds(start, half)]
        sub = lab_sub.at[pl.ds(line + start, half)]
        backs = back.at[pl.ds(line + start, half)]
        lanes = (ref_i.at[pl.ds(h * half, half)], half, at + h * half)
        stream(lanes, [(rows_j, half, sub, None, 0, 1, backs)], lab_lane, buffers, put)


def cross_kernel(lay, mine, other, early, early_j, rows, sums, lab_lane, *refs):
    total, for_other, unfit_ref, late_sub, late_sub_j, long_lane, late_lane_j = refs[:7]
    lab_sub, bias, back, rows_j, buf_a, buf_b = refs[7:]
    is_home = lax.axis_index("cl") == lay.home
    infos = lines_of(lay, other)
    own = lines_of(lay, mine)
    hot = hot_of(lay, own[0])
    lane = lax.broadcasted_iota(jnp.int32, (1, LANES), 1)
    last = (lane < lay.n_fine) & (lax.rem(lane, lay.per_owner) == lay.per_owner - 1)
    last = last & (lax.div(lane, lay.per_owner) != hot)
    unfit = jnp.zeros((1, LANES), jnp.float32)
    for info in infos + own:
        wrong = last & (info >= lay.main)
        differs = (info != hot.astype(jnp.float32)) | (info >= lay.n_owner)
        wrong = wrong | ((lane == lay.n_fine) & differs)
        unfit = unfit + jnp.where(wrong, 1.0, 0.0)
    unfit_ref[0, 0] = jnp.max(unfit).astype(jnp.int32)
    total[...] = sums[...]
    buffers = (buf_a, buf_b)

    @pl.when(is_home)
    def _():
        copy_head(lay, other, rows_j)
        first_labels(lay, infos, lab_sub)
        back[...] = jnp.zeros(back.shape, jnp.float32)
        size = lay.n_early
        blocks_i = [rows.at[pl.ds(start, size)] for start in range(0, lay.n_head, size)] + [early]
        blocks_j = [rows_j.at[pl.ds(start, size)] for start in range(0, lay.n_head, size)]
        blocks_j.append(early_j)
        put, n = adder(total), len(blocks_i)
        for i, ref in enumerate(blocks_i):
            tiles = [
                (blocks_j[j], size, lab_sub, None, j * size, 2, back)
                for j in ((i + step) % n for step in range(1, (n + 1) // 2))
            ]
            stream((ref, size, i * size), tiles, lab_lane, buffers, put)
            half_blocks(
                ref, blocks_j[i], lab_sub, i * size, back, i * size, lab_lane, buffers, put
            )
        write_labels(lay, own, lay.late, lay.head, lay.rest, 0, late_sub, None)
        write_labels(lay, infos, lay.late, lay.head, lay.rest, 0, late_sub_j, None)
        long_lane[:, : lay.n_first] = lab_lane[...]
        turn_labels(lay, late_sub, lay.n_late, long_lane, lay.n_first)
        turn_labels(lay, late_sub_j, lay.n_late, late_lane_j, 0)
        for_other[...] = jnp.zeros(for_other.shape, jnp.float32)
        turn_sums(back, lay.n_first, for_other, 0)

    @pl.when(jnp.logical_not(is_home))
    def _():
        write_labels(lay, infos, range(lay.n_owner), 0, lay.main, 0, lab_sub, bias)
        tiles = [(other, lay.n_main, lab_sub, bias, 0, 2, None)]
        stream((mine, lay.n_main, 0), tiles, lab_lane, buffers, adder(total))


def first_tiles(lay, rows, early, lab_sub, back):
    return [
        (rows, lay.n_head, lab_sub, None, 0, 4, back),
        (early, lay.n_early, lab_sub, None, lay.n_head, 2, back),
    ]


def inner_late_kernel(lay, early, late, rows, lab_sub, late_sub, lab_lane, sums, *refs):
    back, buf_a, buf_b = refs

    @pl.when(lax.axis_index("cl") == lay.home)
    def _():
        back[...] = jnp.zeros(back.shape, jnp.float32)
        sums[:, : lay.n_first] = jnp.zeros((1, lay.n_first), jnp.float32)
        tiles = first_tiles(lay, rows, early, lab_sub, back)
        tiles.append((late, lay.n_late, late_sub, None, 0, 2, None))
        lanes = (late, lay.n_late, lay.n_first)
        stream(lanes, tiles, lab_lane, (buf_a, buf_b), setter(sums))
        turn_sums(back, lay.n_first, sums, 0)


def cross_late_kernel(lay, early, late, late_j, rows, lab_sub, late_sub, lab_lane, *refs):
    late_lane, first_lane, first_sums, first_other, sums, out_ref = refs[:6]
    total, late_other, back, late_back, buf_a, buf_b = refs[6:]
    is_home = lax.axis_index("cl") == lay.home
    grp = lax.axis_index("grp")

    @pl.when(is_home)
    def _():
        total[...] = sums[...]
        total[:, : lay.n_first] += first_sums[...]
        back[...] = jnp.zeros(back.shape, jnp.float32)
        late_back[...] = jnp.zeros(late_back.shape, jnp.float32)
        buffers = (buf_a, buf_b)
        tiles = first_tiles(lay, rows, early, lab_sub, back)
        stream((late_j, lay.n_late, 0), tiles, late_lane, buffers, setter(late_other))
        turn_sums(back, lay.n_first, total, 0)
        put = adder(total)
        half_blocks(late, late_j, late_sub, 0, late_back, lay.n_first, lab_lane, buffers, put)
        turn_sums(late_back, lay.n_late, late_other, 0)

        def write(line, values):
            for source in range(lay.n_owner):
                start = source * lay.head
                out_ref[2 * source + line, :, : lay.head] = values[:, start : start + lay.head]
            for i, source in enumerate(lay.early + lay.late):
                start = lay.n_head + i * lay.rest
                out_ref[2 * source + line, :, lay.head :] = values[:, start : start + lay.rest]

        write(grp, total[...])
        total[:, : lay.n_first] = first_other[...]
        total[:, lay.n_first :] = late_other[...]
        write(1 - grp, total[...])

    @pl.when(jnp.logical_not(is_home))
    def _():
        out_ref[...] = jnp.zeros(out_ref.shape, jnp.float32)
        values = jnp.where(first_lane[...] >= 0, first_sums[...], 1.0)
        for source in range(lay.n_owner):
            start = source * lay.main
            out_ref[2 * source + grp, :, : lay.main] = values[:, start : start + lay.main]


def pair_call(kernel, lay, arrays, out_shape, scratch, out_specs=None, pairs=0):
    width = arrays[0].shape[1]
    buffer = pltpu.VMEM((lay.n_main // 2, WIDE), jnp.float32)
    return pl.pallas_call(
        functools.partial(kernel, lay),
        out_shape=out_shape,
        in_specs=list(vmem_specs(len(arrays))),
        out_specs=out_specs or vmem_specs(len(out_shape)),
        scratch_shapes=list(scratch) + [buffer, buffer],
        compiler_params=pltpu.CompilerParams(vmem_limit_bytes=FAST_LIMIT),
        cost_estimate=pl.CostEstimate(
            flops=2 * pairs * width, bytes_accessed=1, transcendentals=pairs
        ),
    )(*arrays)


def fast_unpack_kernel(values_ref, pos_ref, out_ref):
    pos = pos_ref[...]
    lane = lax.rem(pos, LANES)
    line = lax.div(pos, LANES)
    out = jnp.ones(pos.shape, jnp.float32)
    per = values_ref.shape[2] // LANES
    for r in range(values_ref.shape[0] // 2 * per):
        owner, part = r // per, slice(r % per * LANES, (r % per + 1) * LANES)
        table = values_ref[2 * owner, :, part] + values_ref[2 * owner + 1, :, part]
        found = jnp.take_along_axis(jnp.broadcast_to(table, pos.shape), lane, axis=1)
        out = jnp.where(line == r, found, out)
    out_ref[...] = jnp.log(out)


def fast_unpack(values, pos):
    vmem = pl.BlockSpec(memory_space=pltpu.VMEM)
    return pl.pallas_call(
        fast_unpack_kernel,
        out_shape=jax.ShapeDtypeStruct(pos.shape, jnp.float32),
        in_specs=[vmem, vmem],
        out_specs=vmem,
    )(values, pos)


def general(embeddings, labels, owner_map):
    n_owner = lax.axis_size("cl")
    capacity = SLOTS // n_owner
    rows, width = embeddings.shape
    packed, pos, counts = pack(embeddings, labels, owner_map, n_owner, capacity)
    counts = lax.all_gather(counts, ("cl", "grp"), tiled=True)
    mine = lax.all_to_all(
        packed.reshape(n_owner, capacity, width), "cl", split_axis=0, concat_axis=0, tiled=True
    ).reshape(SLOTS, width)
    other = lax.ppermute(mine, "grp", [(0, 1), (1, 0)])
    results = log_counts(counts, mine, other, n_owner, capacity)
    returned = lax.all_to_all(
        results.reshape(n_owner, capacity), "cl", split_axis=0, concat_axis=0, tiled=True
    )
    return unpack(returned.reshape(SLOTS), pos).reshape(rows)


def body(embeddings, labels, owner_map):
    n_owner = lax.axis_size("cl")
    capacity = SLOTS // n_owner
    rows, width = embeddings.shape
    n_fine = owner_map.shape[0]
    main = -(-(rows // n_owner * 9 // 8) // 16) * 16
    if n_owner != 8 or main >= capacity or n_fine >= LANES:
        return general(embeddings, labels, owner_map)
    home = 2
    lay = Layout(n_owner, n_fine, capacity, main, home)
    packed, extra, pos = place_rows(embeddings, labels, owner_map, lay)

    def hop(x, pairs):
        return lax.ppermute(x, "cl", pairs)

    def swap(x):
        return lax.ppermute(x, "grp", [(0, 1), (1, 0)])

    both = lay_out([extra, hop(extra, [(6, 4), (7, 5)])])
    early = [extra if s == home else hop(extra, [(s, home)]) for s in lay.early]
    early = lay_out(early, home)
    mine = lax.all_to_all(
        packed.reshape(n_owner, main, width), "cl", split_axis=0, concat_axis=0, tiled=True
    ).reshape(n_owner * main, width)
    mine = after(mine, early, both)
    other = swap(mine)
    late = [hop(both, [(s, home)]) for s in (5, 4)]

    def array(shape, dtype=jnp.float32):
        return jax.ShapeDtypeStruct(shape, dtype)

    def scratch(shape):
        return pltpu.VMEM(shape, jnp.float32)

    row, long_row = array((1, lay.n_first)), array((1, lay.n_all))
    bias = scratch((lay.n_main, LANES))
    heads = array((lay.n_head, width), jnp.bfloat16)
    late_lines, first_lines = array((lay.n_late, LANES)), array((lay.n_first, LANES))
    late_row = array((1, lay.n_late))
    late_side, first_side = scratch((lay.n_late, LANES)), scratch((lay.n_first, LANES))
    sums, first_lane, lab_sub, heads_i = pair_call(
        inner_kernel, lay, (mine, early), (row, row, first_lines, heads), (bias, first_side)
    )
    early_j = swap(lay_out([early], home, (sums,)))
    specs = vmem_specs(2) + (pl.BlockSpec(memory_space=pltpu.SMEM),) + vmem_specs(4)
    sums, first_other, unfit, late_sub, late_sub_j, lane, lane_j = pair_call(
        cross_kernel,
        lay,
        (mine, other, early, early_j, heads_i, sums, first_lane),
        (row, row, array((1, 1), jnp.int32), late_lines, late_lines, long_row, late_row),
        (first_side, bias, first_side, pltpu.VMEM(heads.shape, heads.dtype)),
        specs,
    )
    late = lay_out(late, home, (sums,))
    late_j = swap(late)
    (late_sums,) = pair_call(
        inner_late_kernel,
        lay,
        (early, late, heads_i, lab_sub, late_sub, lane),
        (long_row,),
        (first_side,),
        pairs=lay.n_late * lay.n_all,
    )
    (results,) = pair_call(
        cross_late_kernel,
        lay,
        (
            *(early, late, late_j, heads_i, lab_sub, late_sub_j, lane, lane_j),
            *(first_lane, sums, first_other, late_sums),
        ),
        (array((2 * n_owner, 1, capacity)),),
        (scratch(long_row.shape), scratch(late_row.shape), first_side, late_side),
    )
    returned = lax.all_to_all(
        results, ("cl", "grp"), split_axis=0, concat_axis=0, tiled=True
    )
    return lax.cond(
        unfit[0, 0] == 0,
        lambda: fast_unpack(returned, pos).reshape(rows),
        lambda: general(embeddings, labels, owner_map),
    )


def solution(mesh):
    return jax.shard_map(
        body,
        mesh=mesh,
        in_specs=(P(("parts", "cl", "grp"), None), P(("parts", "cl", "grp")), P("parts")),
        out_specs=P(("parts", "cl", "grp")),
        check_vma=False,
    )
```

```python
import functools
import math

import jax
import jax.numpy as jnp
from jax import lax
from jax.experimental import pallas as pl
from jax.experimental.pallas import tpu as pltpu
from jax.sharding import PartitionSpec as P

SLOTS = 2048

temper = 0.2
neighbour_factor = 0.5
epsilon = 1e-06

LANES = 128
SCALE = math.log2(math.e) / temper
NEIGHBOUR = math.log2(neighbour_factor)
DEAD = -1e30
VMEM_LIMIT = 48 * 1024 * 1024
FAST_LIMIT = 16 * 1024 * 1024
WIDE = 512
INFO = 16


def column_of(row):
    pieces = []
    for start in range(0, row.shape[1], LANES):
        width = min(LANES, row.shape[1] - start)
        shape = (width, width)
        diagonal = lax.broadcasted_iota(jnp.int32, shape, 0) == lax.broadcasted_iota(
            jnp.int32, shape, 1
        )
        piece = jnp.broadcast_to(row[:, start : start + width], shape)
        pieces.append(jnp.sum(jnp.where(diagonal, piece, 0.0), axis=1, keepdims=True))
    return jnp.concatenate(pieces, axis=0)


def row_of(column):
    n = column.shape[0]
    diagonal = lax.broadcasted_iota(jnp.int32, (n, n), 0) == lax.broadcasted_iota(
        jnp.int32, (n, n), 1
    )
    return jnp.sum(jnp.where(diagonal, column, 0.0), axis=0, keepdims=True)


def pack_kernel(n_owner, capacity, x_ref, lab_ref, map_ref, out_ref, pos_ref, cnt_ref, unit, pos_row):
    rows = x_ref.shape[0]
    n_fine = map_ref.shape[1]
    per_owner = n_fine // n_owner
    owner_row = map_ref[...].astype(jnp.float32)
    fine_row = lax.broadcasted_iota(jnp.int32, (1, n_fine), 1).astype(jnp.float32)
    key_row = owner_row * n_fine + fine_row
    key_col = column_of(key_row)
    sorted_col = jnp.sum(jnp.where(key_row < key_col, 1.0, 0.0), axis=1, keepdims=True)
    lab = lab_ref[...].astype(jnp.float32)
    lab_row = jnp.concatenate([lab[b : b + 1, :] for b in range(lab.shape[0])], axis=1)
    fine_col = lax.broadcasted_iota(jnp.int32, (n_fine, rows), 0).astype(jnp.float32)
    fine_id = jnp.sum(jnp.where(fine_col == lab_row, sorted_col, 0.0), axis=0, keepdims=True)
    counts_col = jnp.sum(jnp.where(fine_col == fine_id, 1.0, 0.0), axis=1, keepdims=True)
    cnt_ref[...] = row_of(counts_col).astype(jnp.int32)
    coarse = jnp.floor((fine_id + 0.5) * (1.0 / per_owner))
    before = jnp.sum(
        jnp.where(fine_col < coarse * per_owner, counts_col, 0.0), axis=0, keepdims=True
    )
    index = lax.broadcasted_iota(jnp.int32, (1, rows), 1).astype(jnp.float32)
    row_key = fine_id * rows + index
    rank = jnp.zeros((1, rows), jnp.float32)
    for start in range(0, rows, LANES):
        other = column_of(row_key[:, start : start + LANES])
        rank = rank + jnp.sum(jnp.where(other < row_key, 1.0, 0.0), axis=0, keepdims=True)
    pos = (coarse * capacity + rank - before).astype(jnp.int32)
    pos_row[...] = pos
    pos_ref[...] = jnp.concatenate(
        [pos[:, start : start + LANES] for start in range(0, rows, LANES)], axis=0
    )
    x = x_ref[...].astype(jnp.float32)
    squares = jnp.sum(x * x, axis=1, keepdims=True)
    unit[...] = (x * lax.rsqrt(squares + epsilon)).astype(jnp.bfloat16)

    step = 256

    @pl.loop(0, out_ref.shape[0] // step)
    def _(block):
        slot = lax.broadcasted_iota(jnp.int32, (step, rows), 0) + block * step
        chosen = jnp.where(slot == pos_row[...], 1.0, 0.0).astype(jnp.bfloat16)
        packed = jnp.dot(chosen, unit[...], preferred_element_type=jnp.float32)
        out_ref[pl.ds(pl.multiple_of(block * step, step), step), :] = packed.astype(jnp.bfloat16)


def pack(embeddings, labels, owner_map, n_owner, capacity):
    rows, width = embeddings.shape
    n_fine = owner_map.shape[0]
    total = n_owner * capacity
    vmem = pl.BlockSpec(memory_space=pltpu.VMEM)
    return pl.pallas_call(
        functools.partial(pack_kernel, n_owner, capacity),
        out_shape=(
            jax.ShapeDtypeStruct((total, width), jnp.bfloat16),
            jax.ShapeDtypeStruct((rows // LANES, LANES), jnp.int32),
            jax.ShapeDtypeStruct((1, n_fine), jnp.int32),
        ),
        in_specs=[vmem] * 3,
        out_specs=(vmem, vmem, vmem),
        scratch_shapes=[pltpu.VMEM((rows, width), jnp.bfloat16), pltpu.VMEM((1, rows), jnp.int32)],
        compiler_params=pltpu.CompilerParams(vmem_limit_bytes=VMEM_LIMIT),
    )(embeddings, labels.reshape(rows // LANES, LANES), owner_map.reshape(1, n_fine))


def counts_kernel(n_owner, capacity, cnt_ref, mine_ref, other_ref, out_ref, lab_lane, lab_sub, bias):
    total = mine_ref.shape[0]
    per_owner = cnt_ref.shape[1] // n_owner
    me = lax.axis_index("cl")
    grp = lax.axis_index("grp")
    n_grp = lax.axis_size("grp")
    for member in range(2):
        for source in range(n_owner):
            line = source * n_grp + lax.rem(grp + member, n_grp)
            edges = []
            edge = jnp.int32(0)
            for f in range(per_owner):
                edge = edge + cnt_ref[line, me * per_owner + f]
                edges.append(edge)
            down = lax.broadcasted_iota(jnp.int32, (capacity, LANES), 0)
            label = jnp.zeros((capacity, LANES), jnp.int32)
            for edge in edges:
                label = label + jnp.where(down >= edge, 1, 0)
            start = (member * n_owner + source) * capacity
            lab_sub[start : start + capacity, :] = label
            bias[start : start + capacity, :] = jnp.where(
                label < per_owner, NEIGHBOUR - SCALE, DEAD
            )
            if member == 0:
                across = lax.broadcasted_iota(jnp.int32, (1, capacity), 1)
                label = jnp.zeros((1, capacity), jnp.int32)
                for edge in edges:
                    label = label + jnp.where(across >= edge, 1, 0)
                lab_lane[:, source * capacity : (source + 1) * capacity] = jnp.where(
                    label < per_owner, label, -1
                )
    wide, deep = min(512, total), min(256, total)

    @pl.loop(0, total // wide)
    def _(block):
        columns = pl.ds(pl.multiple_of(block * wide, wide), wide)
        rows_i = mine_ref[columns, :]
        label_i = lab_lane[:, columns]

        def add(ref, offset):
            def step(j, acc):
                start = pl.multiple_of(j * deep, deep)
                scores = lax.dot_general(
                    ref[pl.ds(start, deep), :],
                    rows_i,
                    (((1,), (1,)), ((), ())),
                    preferred_element_type=jnp.float32,
                )
                place = pl.ds(pl.multiple_of(start + offset, deep), deep)
                label_j = lab_sub[place, :]
                bias_j = bias[place, :]
                repeat = wide // LANES
                label_j = jnp.concatenate([label_j] * repeat, axis=1)
                bias_j = jnp.concatenate([bias_j] * repeat, axis=1)
                shift = jnp.where(label_j == label_i, -SCALE, bias_j)
                terms = jnp.exp2(scores * SCALE + shift)
                return acc + jnp.sum(terms.reshape(deep // 8, 8, wide), axis=0)

            return step

        acc = jnp.zeros((8, wide), jnp.float32)
        acc = lax.fori_loop(0, total // deep, add(mine_ref, 0), acc, unroll=2)
        acc = lax.fori_loop(0, total // deep, add(other_ref, total), acc, unroll=2)
        totals = jnp.sum(acc, axis=0, keepdims=True)
        out_ref[:, columns] = jnp.log(jnp.where(label_i >= 0, totals, 1.0))


def log_counts(counts, mine, other, n_owner, capacity):
    total = mine.shape[0]
    vmem = pl.BlockSpec(memory_space=pltpu.VMEM)
    return pl.pallas_call(
        functools.partial(counts_kernel, n_owner, capacity),
        out_shape=jax.ShapeDtypeStruct((1, total), jnp.float32),
        in_specs=[pl.BlockSpec(memory_space=pltpu.SMEM), vmem, vmem],
        out_specs=vmem,
        scratch_shapes=[
            pltpu.VMEM((1, total), jnp.int32),
            pltpu.VMEM((2 * total, LANES), jnp.int32),
            pltpu.VMEM((2 * total, LANES), jnp.float32),
        ],
        compiler_params=pltpu.CompilerParams(vmem_limit_bytes=VMEM_LIMIT),
    )(counts, mine, other)


def unpack_kernel(values_ref, pos_ref, out_ref):
    pos = pos_ref[...]
    lane = lax.rem(pos, LANES)
    line = lax.div(pos, LANES)
    out = jnp.zeros(pos.shape, jnp.float32)
    for r in range(values_ref.shape[0]):
        table = jnp.broadcast_to(values_ref[r : r + 1, :], pos.shape)
        found = jnp.take_along_axis(table, lane, axis=1)
        out = jnp.where(line == r, found, out)
    out_ref[...] = out


def unpack(values, pos):
    vmem = pl.BlockSpec(memory_space=pltpu.VMEM)
    return pl.pallas_call(
        unpack_kernel,
        out_shape=jax.ShapeDtypeStruct(pos.shape, jnp.float32),
        in_specs=[vmem, vmem],
        out_specs=vmem,
    )(values.reshape(-1, LANES), pos)


def swapped(x, first, second):
    return jnp.where(x == first, second, jnp.where(x == second, first, x))


def place_kernel(lay, x_hbm, lab_hbm, map_hbm, *refs):
    main_hbm, unit, tail_slot_ref, pos_ref, x_ref, lab_ref, map_ref, main_ref, sems = refs
    n_owner, capacity, main, home = lay.n_owner, lay.capacity, lay.main, lay.home
    copies = [
        pltpu.make_async_copy(src, dst, sems.at[i])
        for i, (src, dst) in enumerate(((x_hbm, x_ref), (lab_hbm, lab_ref), (map_hbm, map_ref)))
    ]
    for copy in copies:
        copy.start()
    rows, width = x_ref.shape
    n_fine = map_ref.shape[1]
    per_owner = n_fine // n_owner
    copies[1].wait()
    copies[2].wait()
    owner_row = map_ref[...].astype(jnp.float32)
    fine_row = lax.broadcasted_iota(jnp.int32, (1, n_fine), 1).astype(jnp.float32)
    key_row = owner_row * n_fine + fine_row
    key_col = column_of(key_row)
    sorted_col = jnp.sum(jnp.where(key_row < key_col, 1.0, 0.0), axis=1, keepdims=True)
    lab = lab_ref[...].astype(jnp.float32)
    lab_row = jnp.concatenate([lab[b : b + 1, :] for b in range(lab.shape[0])], axis=1)
    fine_col = lax.broadcasted_iota(jnp.int32, (n_fine, rows), 0).astype(jnp.float32)
    fine_id = jnp.sum(jnp.where(fine_col == lab_row, sorted_col, 0.0), axis=0, keepdims=True)
    counts_col = jnp.sum(jnp.where(fine_col == fine_id, 1.0, 0.0), axis=1, keepdims=True)
    coarse = jnp.floor((fine_id + 0.5) * (1.0 / per_owner))
    first = coarse * per_owner
    before = jnp.sum(jnp.where(fine_col < first, counts_col, 0.0), axis=0, keepdims=True)
    upto = jnp.sum(jnp.where(fine_col < first + per_owner, counts_col, 0.0), axis=0, keepdims=True)
    full = jnp.min(
        jnp.where(upto - before == capacity, coarse, float(n_owner)), axis=1, keepdims=True
    )
    line = lax.broadcasted_iota(jnp.int32, (n_fine, LANES), 0)
    lane = lax.broadcasted_iota(jnp.int32, (n_fine, LANES), 1)
    inside = (line <= lane) & (lax.div(line, per_owner) == lax.div(lane, per_owner))
    running = jnp.sum(jnp.where(inside, counts_col, 0.0), axis=0, keepdims=True)
    info = jnp.where(lane[:1] < n_fine, running, full)
    index = lax.broadcasted_iota(jnp.int32, (1, rows), 1).astype(jnp.float32)
    row_key = fine_id * rows + index
    rank = jnp.zeros((1, rows), jnp.float32)
    for start in range(0, rows, LANES):
        other = column_of(row_key[:, start : start + LANES])
        rank = rank + jnp.sum(jnp.where(other < row_key, 1.0, 0.0), axis=0, keepdims=True)
    rank = (rank - before).astype(jnp.int32)
    place = swapped(coarse.astype(jnp.int32), full.astype(jnp.int32), home)
    table = place * capacity + rank
    pos_ref[...] = jnp.concatenate(
        [table[:, start : start + LANES] for start in range(0, rows, LANES)], axis=0
    )
    fits = rank < jnp.where(place == home, lay.head, main - 1)
    slot = jnp.where(fits, place * main + rank, -1)
    tail_slot_ref[...] = jnp.where(place == home, rank - lay.head, -1)
    copies[0].wait()
    x = x_ref[...].astype(jnp.float32)
    squares = jnp.sum(x * x, axis=1, keepdims=True)
    unit[...] = (x * lax.rsqrt(squares + epsilon)).astype(jnp.bfloat16)

    count = 2 * main
    down = lax.broadcasted_iota(jnp.int32, (count, LANES), 0)
    is_info = lax.rem(down, main) == main - 1
    writes = []
    for i, start in enumerate(range(0, lay.n_main, count)):
        packed = chosen_rows(unit, slot, start, count)
        place = slice(start, start + count)
        main_ref[place, LANES:] = packed[:, LANES:].astype(jnp.bfloat16)
        main_ref[place, :LANES] = jnp.where(is_info, info, packed[:, :LANES]).astype(jnp.bfloat16)
        writes.append(
            pltpu.make_async_copy(
                main_ref.at[pl.ds(start, count)], main_hbm.at[pl.ds(start, count)], sems.at[3 + i]
            )
        )
        writes[-1].start()
    for write in writes:
        write.wait()


def chosen_rows(unit, slot, start, count):
    here = lax.broadcasted_iota(jnp.int32, (count, unit.shape[0]), 0) + start
    chosen = jnp.where(here == slot, 1.0, 0.0).astype(jnp.bfloat16)
    return jnp.dot(chosen, unit[...], preferred_element_type=jnp.float32)


def tail_kernel(unit, slot_ref, out_ref):
    out_ref[...] = chosen_rows(unit, slot_ref[...], 0, out_ref.shape[0]).astype(jnp.bfloat16)


def tail_rows(unit, slot, lay):
    return pl.pallas_call(
        tail_kernel,
        out_shape=jax.ShapeDtypeStruct((lay.rest, unit.shape[1]), jnp.bfloat16),
        in_specs=list(vmem_specs(2)),
        out_specs=vmem_specs(1)[0],
        compiler_params=pltpu.CompilerParams(vmem_limit_bytes=FAST_LIMIT),
    )(unit, slot)


def vmem_specs(count):
    return (pl.BlockSpec(memory_space=pltpu.VMEM),) * count


def place_rows(embeddings, labels, owner_map, lay):
    rows, width = embeddings.shape
    n_fine = owner_map.shape[0]
    lab_shape = (rows // LANES, LANES)
    anywhere = pl.BlockSpec(memory_space=pl.ANY)
    return pl.pallas_call(
        functools.partial(place_kernel, lay),
        out_shape=(
            jax.ShapeDtypeStruct((lay.n_main, width), jnp.bfloat16),
            jax.ShapeDtypeStruct((rows, width), jnp.bfloat16),
            jax.ShapeDtypeStruct((1, rows), jnp.int32),
            jax.ShapeDtypeStruct(lab_shape, jnp.int32),
        ),
        in_specs=[anywhere] * 3,
        out_specs=(anywhere,) + vmem_specs(3),
        scratch_shapes=[
            pltpu.VMEM((rows, width), jnp.bfloat16),
            pltpu.VMEM(lab_shape, jnp.int32),
            pltpu.VMEM((1, n_fine), jnp.int32),
            pltpu.VMEM((lay.n_main, width), jnp.bfloat16),
            pltpu.SemaphoreType.DMA((3 + lay.n_owner // 2,)),
        ],
        compiler_params=pltpu.CompilerParams(vmem_limit_bytes=FAST_LIMIT),
    )(embeddings, labels.reshape(lab_shape), owner_map.reshape(1, n_fine))


def gate_kernel(*refs):
    pass


def after(rows, *there):
    return pl.pallas_call(
        gate_kernel,
        out_shape=jax.ShapeDtypeStruct(rows.shape, rows.dtype),
        in_specs=list(vmem_specs(1 + len(there))),
        out_specs=vmem_specs(1)[0],
        input_output_aliases={0: 0},
        compiler_params=pltpu.CompilerParams(vmem_limit_bytes=FAST_LIMIT),
    )(rows, *there)


def lay_out_kernel(n_arrays, home, *refs):
    chunks, out = refs[:n_arrays], refs[-1]

    def copy():
        start = 0
        for chunk in chunks:
            out[start : start + chunk.shape[0], :] = chunk[...]
            start += chunk.shape[0]

    if home is None:
        copy()
    else:
        pl.when(lax.axis_index("cl") == home)(copy)


def lay_out(chunks, home=None, waits=()):
    rows, width = sum(x.shape[0] for x in chunks), chunks[0].shape[1]
    return pl.pallas_call(
        functools.partial(lay_out_kernel, len(chunks), home),
        out_shape=jax.ShapeDtypeStruct((rows, width), jnp.bfloat16),
        in_specs=list(vmem_specs(len(chunks) + len(waits))),
        out_specs=vmem_specs(1)[0],
        compiler_params=pltpu.CompilerParams(vmem_limit_bytes=FAST_LIMIT),
    )(*chunks, *waits)


class Layout:
    early, late = (0, 1, 2, 3), (5, 7, 4, 6)

    def __init__(self, n_owner, n_fine, capacity, main, home):
        self.n_owner, self.n_fine, self.capacity = n_owner, n_fine, capacity
        self.main, self.home = main, home
        self.head = main - INFO
        self.rest = capacity - self.head
        self.per_owner = n_fine // n_owner
        self.n_main = n_owner * main
        self.n_head = n_owner * self.head
        self.n_early = len(self.early) * self.rest
        self.n_late = len(self.late) * self.rest
        self.n_first = self.n_head + self.n_early
        self.n_all = self.n_first + self.n_late


def info_line(lay, main_ref, source):
    end = (source + 1) * lay.main
    return main_ref[end - INFO : end, :LANES].astype(jnp.float32)[INFO - 1 :]


def lines_of(lay, main_ref):
    return [info_line(lay, main_ref, source) for source in range(lay.n_owner)]


def hot_of(lay, info):
    lane = lax.broadcasted_iota(jnp.int32, (1, LANES), 1)
    hot = jnp.max(jnp.where(lane == lay.n_fine, info, 0.0), axis=1, keepdims=True)
    return hot.astype(jnp.int32)


def write_labels(lay, infos, sources, first, count, at, lab_sub, bias):
    cluster = swapped(lax.axis_index("cl"), hot_of(lay, infos[0]), lay.home)
    lane = lax.broadcasted_iota(jnp.int32, (1, LANES), 1)
    is_edge = lax.div(lane, lay.per_owner) == cluster
    for i, source in enumerate(sources):
        edges = jnp.where(is_edge, infos[source], 2.0 * lay.capacity)
        slot = lax.broadcasted_iota(jnp.int32, (count, LANES), 0) + first
        label = jnp.where(slot.astype(jnp.float32) >= edges, 1.0, 0.0)
        label = jnp.broadcast_to(jnp.sum(label, axis=1, keepdims=True), (count, LANES))
        start = at + i * count
        lab_sub[start : start + count, :] = label
        if bias is not None:
            bias[start : start + count, :] = jnp.where(
                label < lay.per_owner, NEIGHBOUR - SCALE, DEAD
            )


def first_labels(lay, infos, lab_sub):
    write_labels(lay, infos, range(lay.n_owner), 0, lay.head, 0, lab_sub, None)
    write_labels(lay, infos, lay.early, lay.head, lay.rest, lay.n_head, lab_sub, None)


def late_labels(lay, infos, lab_sub):
    write_labels(lay, infos, lay.late, lay.head, lay.rest, 0, lab_sub, None)


def turn_labels(lay, lab_sub, count, lab_lane, at):
    for i in range(0, count, LANES):
        block = jnp.transpose(lab_sub[i : i + LANES, :])[:1]
        lab_lane[:, at + i : at + i + LANES] = jnp.where(block < lay.per_owner, block, -1.0)


def copy_head(lay, main_ref, rows):
    for source in range(lay.n_owner):
        rows[source * lay.head : (source + 1) * lay.head, :] = main_ref[
            source * lay.main : source * lay.main + lay.head, :
        ]


def pieces(count, parts):
    return [(i * (count // parts), count // parts) for i in range(parts)]


def stream(lanes, tiles, lab_lane, buffers, put, one_way=None):
    rows_i, count, at = lanes
    step = 32
    tiles = [
        (ref, s, d, lab_sub, bias, line + s, back)
        for ref, n, lab_sub, bias, line, parts, back in tiles
        for s, d in pieces(n, parts)
    ]

    def scores_to(buffer, tile, rows):
        ref, start, deep = tile[:3]
        buffer[:deep, : rows.shape[0]] = lax.dot_general(
            ref[start : start + deep, :],
            rows,
            (((1,), (1,)), ((), ())),
            preferred_element_type=jnp.float32,
        )

    def run(start, blocks, wide):
        repeat = wide // LANES

        def rows_of(block):
            return rows_i[pl.ds(pl.multiple_of(start + block * wide, LANES), wide), :]

        scores_to(buffers[0], tiles[0], rows_of(0))

        def one_block(block):
            here = rows_of(block)
            place = pl.ds(pl.multiple_of(at + start + block * wide, LANES), wide)
            label_i = lab_lane[:, place]
            acc = jnp.zeros((8, wide), jnp.float32)
            for i, (_, _, deep, lab_sub, bias, line, back) in enumerate(tiles):
                if i + 1 < len(tiles):
                    scores_to(buffers[(i + 1) % 2], tiles[i + 1], here)
                elif blocks > 1:

                    @pl.when(block + 1 < blocks)
                    def _():
                        scores_to(buffers[0], tiles[0], rows_of(block + 1))

                buffer = buffers[i % 2]
                for c in range(0, deep, step):
                    part = slice(line + c, line + c + step)
                    label_j = jnp.concatenate([lab_sub[part, :]] * repeat, axis=1)
                    if bias is None:
                        bias_j = NEIGHBOUR - SCALE
                    else:
                        bias_j = jnp.concatenate([bias[part, :]] * repeat, axis=1)
                    shift = jnp.where(label_j == label_i, -SCALE, bias_j)
                    terms = jnp.exp2(buffer[c : c + step, :wide] * SCALE + shift)
                    if one_way is None or back is not one_way:
                        acc = acc + jnp.sum(terms.reshape(step // 8, 8, wide), axis=0)
                    if back is not None:
                        across = terms[:, :LANES]
                        for r in range(1, repeat):
                            across = across + terms[:, r * LANES : (r + 1) * LANES]
                        back[part, :] += across
            put(place, jnp.sum(acc, axis=0, keepdims=True))

        if blocks == 1:
            one_block(0)
        else:
            pl.loop(0, blocks)(one_block)

    if count >= WIDE:
        run(0, count // WIDE, WIDE)
    if count % WIDE:
        run(count - count % WIDE, 1, count % WIDE)


def turn_sums(back, count, sums, at):
    for i in range(0, count, LANES):
        block = jnp.transpose(back[i : i + LANES, :])
        sums[:, at + i : at + i + LANES] += jnp.sum(block, axis=0, keepdims=True)


def setter(ref):
    def put(place, values):
        ref[:, place] = values

    return put


def adder(ref):
    def put(place, values):
        ref[:, place] += values

    return put


def inner_kernel(lay, mine, early, sums, lab_lane, lab_sub, rows, bias, back, buf_a, buf_b):
    is_home = lax.axis_index("cl") == lay.home
    infos = lines_of(lay, mine)
    buffers = (buf_a, buf_b)

    @pl.when(is_home)
    def _():
        copy_head(lay, mine, rows)
        first_labels(lay, infos, lab_sub)
        turn_labels(lay, lab_sub, lay.n_first, lab_lane, 0)
        back[...] = jnp.zeros(back.shape, jnp.float32)
        size = lay.n_early
        blocks = [(rows.at[pl.ds(start, size)], start) for start in range(0, lay.n_head, size)]
        blocks.append((early, lay.n_head))
        for i, (ref, at) in enumerate(blocks):
            tiles = [
                (ref_j, size, lab_sub, None, at_j, 2, None if at_j == at else back)
                for ref_j, at_j in blocks[i:]
            ]
            stream((ref, size, at), tiles, lab_lane, buffers, setter(sums))
        turn_sums(back, lay.n_first, sums, 0)

    @pl.when(jnp.logical_not(is_home))
    def _():
        write_labels(lay, infos, range(lay.n_owner), 0, lay.main, 0, lab_sub, bias)
        turn_labels(lay, lab_sub, lay.n_main, lab_lane, 0)
        tiles = [(mine, lay.n_main, lab_sub, bias, 0, 2, None)]
        stream((mine, lay.n_main, 0), tiles, lab_lane, buffers, setter(sums))


def half_blocks(ref_i, ref_j, lab_sub, line, back, at, lab_lane, buffers, put):
    half = ref_j.shape[0] // 2
    grp = lax.axis_index("grp")
    for h in range(2):
        start = pl.multiple_of((h ^ grp) * half, half)
        rows_j = ref_j.at[pl.ds(start, half)]
        sub = lab_sub.at[pl.ds(line + start, half)]
        backs = back.at[pl.ds(line + start, half)]
        lanes = (ref_i.at[pl.ds(h * half, half)], half, at + h * half)
        stream(lanes, [(rows_j, half, sub, None, 0, 1, backs)], lab_lane, buffers, put)


def cross_kernel(lay, mine, other, early, early_j, rows, sums, lab_lane, *refs):
    total, for_other, unfit_ref, late_sub, long_lane, late_lane_j = refs[:6]
    lab_sub, bias, back, rows_j, late_sub_j, buf_a, buf_b = refs[6:]
    is_home = lax.axis_index("cl") == lay.home
    infos = lines_of(lay, other)
    own = lines_of(lay, mine)
    hot = hot_of(lay, own[0])
    lane = lax.broadcasted_iota(jnp.int32, (1, LANES), 1)
    last = (lane < lay.n_fine) & (lax.rem(lane, lay.per_owner) == lay.per_owner - 1)
    last = last & (lax.div(lane, lay.per_owner) != hot)
    unfit = jnp.zeros((1, LANES), jnp.float32)
    for info in infos + own:
        wrong = last & (info >= lay.main)
        differs = (info != hot.astype(jnp.float32)) | (info >= lay.n_owner)
        wrong = wrong | ((lane == lay.n_fine) & differs)
        unfit = unfit + jnp.where(wrong, 1.0, 0.0)
    unfit_ref[0, 0] = jnp.max(unfit).astype(jnp.int32)
    total[...] = sums[...]
    buffers = (buf_a, buf_b)

    @pl.when(is_home)
    def _():
        copy_head(lay, other, rows_j)
        first_labels(lay, infos, lab_sub)
        back[...] = jnp.zeros(back.shape, jnp.float32)
        size = lay.n_early
        blocks_i = [rows.at[pl.ds(start, size)] for start in range(0, lay.n_head, size)] + [early]
        blocks_j = [rows_j.at[pl.ds(start, size)] for start in range(0, lay.n_head, size)]
        blocks_j.append(early_j)
        put, n = adder(total), len(blocks_i)
        for i, ref in enumerate(blocks_i):
            tiles = [
                (blocks_j[j], size, lab_sub, None, j * size, 2, back)
                for j in ((i + step) % n for step in range(1, (n + 1) // 2))
            ]
            stream((ref, size, i * size), tiles, lab_lane, buffers, put)
            half_blocks(
                ref, blocks_j[i], lab_sub, i * size, back, i * size, lab_lane, buffers, put
            )
        write_labels(lay, own, lay.late, lay.head, lay.rest, 0, late_sub, None)
        write_labels(lay, infos, lay.late, lay.head, lay.rest, 0, late_sub_j, None)
        long_lane[:, : lay.n_first] = lab_lane[...]
        turn_labels(lay, late_sub, lay.n_late, long_lane, lay.n_first)
        turn_labels(lay, late_sub_j, lay.n_late, late_lane_j, 0)
        for_other[...] = jnp.zeros(for_other.shape, jnp.float32)
        turn_sums(back, lay.n_first, for_other, 0)

    @pl.when(jnp.logical_not(is_home))
    def _():
        write_labels(lay, infos, range(lay.n_owner), 0, lay.main, 0, lab_sub, bias)
        tiles = [(other, lay.n_main, lab_sub, bias, 0, 2, None)]
        stream((mine, lay.n_main, 0), tiles, lab_lane, buffers, adder(total))


def first_tiles(lay, rows, early, lab_sub, back):
    return [
        (rows, lay.n_head, lab_sub, None, 0, 4, back),
        (early, lay.n_early, lab_sub, None, lay.n_head, 2, back),
    ]


def inner_late_kernel(lay, early, late, rows, lab_sub, late_sub, lab_lane, sums, *refs):
    back, buf_a, buf_b = refs

    @pl.when(lax.axis_index("cl") == lay.home)
    def _():
        back[...] = jnp.zeros(back.shape, jnp.float32)
        sums[:, : lay.n_first] = jnp.zeros((1, lay.n_first), jnp.float32)
        tiles = first_tiles(lay, rows, early, lab_sub, back)
        tiles.append((late, lay.n_late, late_sub, None, 0, 2, None))
        lanes = (late, lay.n_late, lay.n_first)
        stream(lanes, tiles, lab_lane, (buf_a, buf_b), setter(sums))
        turn_sums(back, lay.n_first, sums, 0)


def cross_late_kernel(lay, early, late, late_j, rows, lab_sub, late_sub, late_lane, *refs):
    first_lane, first_sums, first_other, sums, out_ref = refs[:5]
    total, late_other, back, late_back, buf_a, buf_b = refs[5:]
    is_home = lax.axis_index("cl") == lay.home
    grp = lax.axis_index("grp")

    @pl.when(is_home)
    def _():
        total[...] = sums[...]
        total[:, : lay.n_first] += first_sums[...]
        back[...] = jnp.zeros(back.shape, jnp.float32)
        late_back[...] = jnp.zeros(late_back.shape, jnp.float32)
        buffers = (buf_a, buf_b)
        tiles = first_tiles(lay, rows, early, lab_sub, back)
        tiles.append((late, lay.n_late, late_sub, None, 0, 2, late_back))
        lanes, put = (late_j, lay.n_late, 0), setter(late_other)
        stream(lanes, tiles, late_lane, buffers, put, one_way=late_back)
        turn_sums(back, lay.n_first, total, 0)
        turn_sums(late_back, lay.n_late, total, lay.n_first)

        def write(line, values):
            for source in range(lay.n_owner):
                start = source * lay.head
                out_ref[2 * source + line, :, : lay.head] = values[:, start : start + lay.head]
            for i, source in enumerate(lay.early + lay.late):
                start = lay.n_head + i * lay.rest
                out_ref[2 * source + line, :, lay.head :] = values[:, start : start + lay.rest]

        write(grp, total[...])
        total[:, : lay.n_first] = first_other[...]
        total[:, lay.n_first :] = late_other[...]
        write(1 - grp, total[...])

    @pl.when(jnp.logical_not(is_home))
    def _():
        out_ref[...] = jnp.zeros(out_ref.shape, jnp.float32)
        values = jnp.where(first_lane[...] >= 0, first_sums[...], 1.0)
        for source in range(lay.n_owner):
            start = source * lay.main
            out_ref[2 * source + grp, :, : lay.main] = values[:, start : start + lay.main]


def pair_call(kernel, lay, arrays, out_shape, scratch, out_specs=None, pairs=0):
    width = arrays[0].shape[1]
    buffer = pltpu.VMEM((lay.n_main // 2, WIDE), jnp.float32)
    return pl.pallas_call(
        functools.partial(kernel, lay),
        out_shape=out_shape,
        in_specs=list(vmem_specs(len(arrays))),
        out_specs=out_specs or vmem_specs(len(out_shape)),
        scratch_shapes=list(scratch) + [buffer, buffer],
        compiler_params=pltpu.CompilerParams(vmem_limit_bytes=FAST_LIMIT),
        cost_estimate=pl.CostEstimate(
            flops=2 * pairs * width, bytes_accessed=1, transcendentals=pairs
        ),
    )(*arrays)


def fast_unpack_kernel(values_ref, pos_ref, out_ref):
    pos = pos_ref[...]
    lane = lax.rem(pos, LANES)
    line = lax.div(pos, LANES)
    out = jnp.ones(pos.shape, jnp.float32)
    per = values_ref.shape[2] // LANES
    for r in range(values_ref.shape[0] // 2 * per):
        owner, part = r // per, slice(r % per * LANES, (r % per + 1) * LANES)
        table = values_ref[2 * owner, :, part] + values_ref[2 * owner + 1, :, part]
        found = jnp.take_along_axis(jnp.broadcast_to(table, pos.shape), lane, axis=1)
        out = jnp.where(line == r, found, out)
    out_ref[...] = jnp.log(out)


def fast_unpack(values, pos):
    vmem = pl.BlockSpec(memory_space=pltpu.VMEM)
    return pl.pallas_call(
        fast_unpack_kernel,
        out_shape=jax.ShapeDtypeStruct(pos.shape, jnp.float32),
        in_specs=[vmem, vmem],
        out_specs=vmem,
    )(values, pos)


def general(embeddings, labels, owner_map):
    n_owner = lax.axis_size("cl")
    capacity = SLOTS // n_owner
    rows, width = embeddings.shape
    packed, pos, counts = pack(embeddings, labels, owner_map, n_owner, capacity)
    counts = lax.all_gather(counts, ("cl", "grp"), tiled=True)
    mine = lax.all_to_all(
        packed.reshape(n_owner, capacity, width), "cl", split_axis=0, concat_axis=0, tiled=True
    ).reshape(SLOTS, width)
    other = lax.ppermute(mine, "grp", [(0, 1), (1, 0)])
    results = log_counts(counts, mine, other, n_owner, capacity)
    returned = lax.all_to_all(
        results.reshape(n_owner, capacity), "cl", split_axis=0, concat_axis=0, tiled=True
    )
    return unpack(returned.reshape(SLOTS), pos).reshape(rows)


def body(embeddings, labels, owner_map):
    n_owner = lax.axis_size("cl")
    capacity = SLOTS // n_owner
    rows, width = embeddings.shape
    n_fine = owner_map.shape[0]
    main = -(-(rows // n_owner * 9 // 8) // 16) * 16
    if n_owner != 8 or main >= capacity or n_fine >= LANES:
        return general(embeddings, labels, owner_map)
    home = 2
    lay = Layout(n_owner, n_fine, capacity, main, home)
    packed, unit, tail_slot, pos = place_rows(embeddings, labels, owner_map, lay)
    extra = tail_rows(unit, tail_slot, lay)

    def hop(x, pairs):
        return lax.ppermute(x, "cl", pairs)

    def swap(x):
        return lax.ppermute(x, "grp", [(0, 1), (1, 0)])

    both = lay_out([extra, hop(extra, [(6, 4), (7, 5)])])
    early = [extra if s == home else hop(extra, [(s, home)]) for s in lay.early]
    early = lay_out(early, home)
    mine = lax.all_to_all(
        packed.reshape(n_owner, main, width), "cl", split_axis=0, concat_axis=0, tiled=True
    ).reshape(n_owner * main, width)
    mine = after(mine, early, both)
    other, early_j = swap(mine), swap(early)
    late = [hop(both, [(s, home)]) for s in (5, 4)]

    def array(shape, dtype=jnp.float32):
        return jax.ShapeDtypeStruct(shape, dtype)

    def scratch(shape):
        return pltpu.VMEM(shape, jnp.float32)

    row, long_row = array((1, lay.n_first)), array((1, lay.n_all))
    bias = scratch((lay.n_main, LANES))
    heads = array((lay.n_head, width), jnp.bfloat16)
    late_lines, first_lines = array((lay.n_late, LANES)), array((lay.n_first, LANES))
    late_row = array((1, lay.n_late))
    late_side, first_side = scratch((lay.n_late, LANES)), scratch((lay.n_first, LANES))
    sums, first_lane, lab_sub, heads_i = pair_call(
        inner_kernel, lay, (mine, early), (row, row, first_lines, heads), (bias, first_side)
    )
    specs = vmem_specs(2) + (pl.BlockSpec(memory_space=pltpu.SMEM),) + vmem_specs(3)
    sums, first_other, unfit, late_sub, lane, lane_j = pair_call(
        cross_kernel,
        lay,
        (mine, other, early, early_j, heads_i, sums, first_lane),
        (row, row, array((1, 1), jnp.int32), late_lines, long_row, late_row),
        (first_side, bias, first_side, pltpu.VMEM(heads.shape, heads.dtype), late_side),
        specs,
    )
    late = lay_out(late, home, (sums,))
    late_j = swap(late)
    (late_sums,) = pair_call(
        inner_late_kernel,
        lay,
        (early, late, heads_i, lab_sub, late_sub, lane),
        (long_row,),
        (first_side,),
        pairs=lay.n_late * lay.n_all,
    )
    (results,) = pair_call(
        cross_late_kernel,
        lay,
        (
            *(early, late, late_j, heads_i, lab_sub, late_sub, lane_j),
            *(first_lane, sums, first_other, late_sums),
        ),
        (array((2 * n_owner, 1, capacity)),),
        (scratch(long_row.shape), scratch(late_row.shape), first_side, late_side),
    )
    returned = lax.all_to_all(
        results, ("cl", "grp"), split_axis=0, concat_axis=0, tiled=True
    )
    return lax.cond(
        unfit[0, 0] == 0,
        lambda: fast_unpack(returned, pos).reshape(rows),
        lambda: general(embeddings, labels, owner_map),
    )


def solution(mesh):
    return jax.shard_map(
        body,
        mesh=mesh,
        in_specs=(P(("parts", "cl", "grp"), None), P(("parts", "cl", "grp")), P("parts")),
        out_specs=P(("parts", "cl", "grp")),
        check_vma=False,
    )
```

```python
import functools
import math

import jax
import jax.numpy as jnp
from jax import lax
from jax.experimental import pallas as pl
from jax.experimental.pallas import tpu as pltpu
from jax.sharding import PartitionSpec as P

SLOTS = 2048

temper = 0.2
neighbour_factor = 0.5
epsilon = 1e-06

LANES = 128
SCALE = math.log2(math.e) / temper
NEIGHBOUR = math.log2(neighbour_factor)
DEAD = -1e30
VMEM_LIMIT = 48 * 1024 * 1024
FAST_LIMIT = 16 * 1024 * 1024
WIDE = 512
INFO = 16


def column_of(row):
    pieces = []
    for start in range(0, row.shape[1], LANES):
        width = min(LANES, row.shape[1] - start)
        shape = (width, width)
        diagonal = lax.broadcasted_iota(jnp.int32, shape, 0) == lax.broadcasted_iota(
            jnp.int32, shape, 1
        )
        piece = jnp.broadcast_to(row[:, start : start + width], shape)
        pieces.append(jnp.sum(jnp.where(diagonal, piece, 0.0), axis=1, keepdims=True))
    return jnp.concatenate(pieces, axis=0)


def row_of(column):
    n = column.shape[0]
    diagonal = lax.broadcasted_iota(jnp.int32, (n, n), 0) == lax.broadcasted_iota(
        jnp.int32, (n, n), 1
    )
    return jnp.sum(jnp.where(diagonal, column, 0.0), axis=0, keepdims=True)


def pack_kernel(n_owner, capacity, x_ref, lab_ref, map_ref, out_ref, pos_ref, cnt_ref, unit, pos_row):
    rows = x_ref.shape[0]
    n_fine = map_ref.shape[1]
    per_owner = n_fine // n_owner
    owner_row = map_ref[...].astype(jnp.float32)
    fine_row = lax.broadcasted_iota(jnp.int32, (1, n_fine), 1).astype(jnp.float32)
    key_row = owner_row * n_fine + fine_row
    key_col = column_of(key_row)
    sorted_col = jnp.sum(jnp.where(key_row < key_col, 1.0, 0.0), axis=1, keepdims=True)
    lab = lab_ref[...].astype(jnp.float32)
    lab_row = jnp.concatenate([lab[b : b + 1, :] for b in range(lab.shape[0])], axis=1)
    fine_col = lax.broadcasted_iota(jnp.int32, (n_fine, rows), 0).astype(jnp.float32)
    fine_id = jnp.sum(jnp.where(fine_col == lab_row, sorted_col, 0.0), axis=0, keepdims=True)
    counts_col = jnp.sum(jnp.where(fine_col == fine_id, 1.0, 0.0), axis=1, keepdims=True)
    cnt_ref[...] = row_of(counts_col).astype(jnp.int32)
    coarse = jnp.floor((fine_id + 0.5) * (1.0 / per_owner))
    before = jnp.sum(
        jnp.where(fine_col < coarse * per_owner, counts_col, 0.0), axis=0, keepdims=True
    )
    index = lax.broadcasted_iota(jnp.int32, (1, rows), 1).astype(jnp.float32)
    row_key = fine_id * rows + index
    rank = jnp.zeros((1, rows), jnp.float32)
    for start in range(0, rows, LANES):
        other = column_of(row_key[:, start : start + LANES])
        rank = rank + jnp.sum(jnp.where(other < row_key, 1.0, 0.0), axis=0, keepdims=True)
    pos = (coarse * capacity + rank - before).astype(jnp.int32)
    pos_row[...] = pos
    pos_ref[...] = jnp.concatenate(
        [pos[:, start : start + LANES] for start in range(0, rows, LANES)], axis=0
    )
    x = x_ref[...].astype(jnp.float32)
    squares = jnp.sum(x * x, axis=1, keepdims=True)
    unit[...] = (x * lax.rsqrt(squares + epsilon)).astype(jnp.bfloat16)

    step = 256

    @pl.loop(0, out_ref.shape[0] // step)
    def _(block):
        slot = lax.broadcasted_iota(jnp.int32, (step, rows), 0) + block * step
        chosen = jnp.where(slot == pos_row[...], 1.0, 0.0).astype(jnp.bfloat16)
        packed = jnp.dot(chosen, unit[...], preferred_element_type=jnp.float32)
        out_ref[pl.ds(pl.multiple_of(block * step, step), step), :] = packed.astype(jnp.bfloat16)


def pack(embeddings, labels, owner_map, n_owner, capacity):
    rows, width = embeddings.shape
    n_fine = owner_map.shape[0]
    total = n_owner * capacity
    vmem = pl.BlockSpec(memory_space=pltpu.VMEM)
    return pl.pallas_call(
        functools.partial(pack_kernel, n_owner, capacity),
        out_shape=(
            jax.ShapeDtypeStruct((total, width), jnp.bfloat16),
            jax.ShapeDtypeStruct((rows // LANES, LANES), jnp.int32),
            jax.ShapeDtypeStruct((1, n_fine), jnp.int32),
        ),
        in_specs=[vmem] * 3,
        out_specs=(vmem, vmem, vmem),
        scratch_shapes=[pltpu.VMEM((rows, width), jnp.bfloat16), pltpu.VMEM((1, rows), jnp.int32)],
        compiler_params=pltpu.CompilerParams(vmem_limit_bytes=VMEM_LIMIT),
    )(embeddings, labels.reshape(rows // LANES, LANES), owner_map.reshape(1, n_fine))


def counts_kernel(n_owner, capacity, cnt_ref, mine_ref, other_ref, out_ref, lab_lane, lab_sub, bias):
    total = mine_ref.shape[0]
    per_owner = cnt_ref.shape[1] // n_owner
    me = lax.axis_index("cl")
    grp = lax.axis_index("grp")
    n_grp = lax.axis_size("grp")
    for member in range(2):
        for source in range(n_owner):
            line = source * n_grp + lax.rem(grp + member, n_grp)
            edges = []
            edge = jnp.int32(0)
            for f in range(per_owner):
                edge = edge + cnt_ref[line, me * per_owner + f]
                edges.append(edge)
            down = lax.broadcasted_iota(jnp.int32, (capacity, LANES), 0)
            label = jnp.zeros((capacity, LANES), jnp.int32)
            for edge in edges:
                label = label + jnp.where(down >= edge, 1, 0)
            start = (member * n_owner + source) * capacity
            lab_sub[start : start + capacity, :] = label
            bias[start : start + capacity, :] = jnp.where(
                label < per_owner, NEIGHBOUR - SCALE, DEAD
            )
            if member == 0:
                across = lax.broadcasted_iota(jnp.int32, (1, capacity), 1)
                label = jnp.zeros((1, capacity), jnp.int32)
                for edge in edges:
                    label = label + jnp.where(across >= edge, 1, 0)
                lab_lane[:, source * capacity : (source + 1) * capacity] = jnp.where(
                    label < per_owner, label, -1
                )
    wide, deep = min(512, total), min(256, total)

    @pl.loop(0, total // wide)
    def _(block):
        columns = pl.ds(pl.multiple_of(block * wide, wide), wide)
        rows_i = mine_ref[columns, :]
        label_i = lab_lane[:, columns]

        def add(ref, offset):
            def step(j, acc):
                start = pl.multiple_of(j * deep, deep)
                scores = lax.dot_general(
                    ref[pl.ds(start, deep), :],
                    rows_i,
                    (((1,), (1,)), ((), ())),
                    preferred_element_type=jnp.float32,
                )
                place = pl.ds(pl.multiple_of(start + offset, deep), deep)
                label_j = lab_sub[place, :]
                bias_j = bias[place, :]
                repeat = wide // LANES
                label_j = jnp.concatenate([label_j] * repeat, axis=1)
                bias_j = jnp.concatenate([bias_j] * repeat, axis=1)
                shift = jnp.where(label_j == label_i, -SCALE, bias_j)
                terms = jnp.exp2(scores * SCALE + shift)
                return acc + jnp.sum(terms.reshape(deep // 8, 8, wide), axis=0)

            return step

        acc = jnp.zeros((8, wide), jnp.float32)
        acc = lax.fori_loop(0, total // deep, add(mine_ref, 0), acc, unroll=2)
        acc = lax.fori_loop(0, total // deep, add(other_ref, total), acc, unroll=2)
        totals = jnp.sum(acc, axis=0, keepdims=True)
        out_ref[:, columns] = jnp.log(jnp.where(label_i >= 0, totals, 1.0))


def log_counts(counts, mine, other, n_owner, capacity):
    total = mine.shape[0]
    vmem = pl.BlockSpec(memory_space=pltpu.VMEM)
    return pl.pallas_call(
        functools.partial(counts_kernel, n_owner, capacity),
        out_shape=jax.ShapeDtypeStruct((1, total), jnp.float32),
        in_specs=[pl.BlockSpec(memory_space=pltpu.SMEM), vmem, vmem],
        out_specs=vmem,
        scratch_shapes=[
            pltpu.VMEM((1, total), jnp.int32),
            pltpu.VMEM((2 * total, LANES), jnp.int32),
            pltpu.VMEM((2 * total, LANES), jnp.float32),
        ],
        compiler_params=pltpu.CompilerParams(vmem_limit_bytes=VMEM_LIMIT),
    )(counts, mine, other)


def unpack_kernel(values_ref, pos_ref, out_ref):
    pos = pos_ref[...]
    lane = lax.rem(pos, LANES)
    line = lax.div(pos, LANES)
    out = jnp.zeros(pos.shape, jnp.float32)
    for r in range(values_ref.shape[0]):
        table = jnp.broadcast_to(values_ref[r : r + 1, :], pos.shape)
        found = jnp.take_along_axis(table, lane, axis=1)
        out = jnp.where(line == r, found, out)
    out_ref[...] = out


def unpack(values, pos):
    vmem = pl.BlockSpec(memory_space=pltpu.VMEM)
    return pl.pallas_call(
        unpack_kernel,
        out_shape=jax.ShapeDtypeStruct(pos.shape, jnp.float32),
        in_specs=[vmem, vmem],
        out_specs=vmem,
    )(values.reshape(-1, LANES), pos)


def swapped(x, first, second):
    return jnp.where(x == first, second, jnp.where(x == second, first, x))


def place_kernel(lay, x_hbm, lab_hbm, map_hbm, *refs):
    main_hbm, tail_ref, pos_ref, x_ref, lab_ref, map_ref, unit, main_ref, sems = refs
    n_owner, capacity, main, home = lay.n_owner, lay.capacity, lay.main, lay.home
    copies = [
        pltpu.make_async_copy(src, dst, sems.at[i])
        for i, (src, dst) in enumerate(((x_hbm, x_ref), (lab_hbm, lab_ref), (map_hbm, map_ref)))
    ]
    for copy in copies:
        copy.start()
    rows, width = x_ref.shape
    n_fine = map_ref.shape[1]
    per_owner = n_fine // n_owner
    copies[1].wait()
    copies[2].wait()
    owner_row = map_ref[...].astype(jnp.float32)
    fine_row = lax.broadcasted_iota(jnp.int32, (1, n_fine), 1).astype(jnp.float32)
    key_row = owner_row * n_fine + fine_row
    key_col = column_of(key_row)
    sorted_col = jnp.sum(jnp.where(key_row < key_col, 1.0, 0.0), axis=1, keepdims=True)
    lab = lab_ref[...].astype(jnp.float32)
    lab_row = jnp.concatenate([lab[b : b + 1, :] for b in range(lab.shape[0])], axis=1)
    fine_col = lax.broadcasted_iota(jnp.int32, (n_fine, rows), 0).astype(jnp.float32)
    fine_id = jnp.sum(jnp.where(fine_col == lab_row, sorted_col, 0.0), axis=0, keepdims=True)
    counts_col = jnp.sum(jnp.where(fine_col == fine_id, 1.0, 0.0), axis=1, keepdims=True)
    coarse = jnp.floor((fine_id + 0.5) * (1.0 / per_owner))
    first = coarse * per_owner
    before = jnp.sum(jnp.where(fine_col < first, counts_col, 0.0), axis=0, keepdims=True)
    upto = jnp.sum(jnp.where(fine_col < first + per_owner, counts_col, 0.0), axis=0, keepdims=True)
    full = jnp.min(
        jnp.where(upto - before == capacity, coarse, float(n_owner)), axis=1, keepdims=True
    )
    line = lax.broadcasted_iota(jnp.int32, (n_fine, LANES), 0)
    lane = lax.broadcasted_iota(jnp.int32, (n_fine, LANES), 1)
    inside = (line <= lane) & (lax.div(line, per_owner) == lax.div(lane, per_owner))
    running = jnp.sum(jnp.where(inside, counts_col, 0.0), axis=0, keepdims=True)
    info = jnp.where(lane[:1] < n_fine, running, full)
    index = lax.broadcasted_iota(jnp.int32, (1, rows), 1).astype(jnp.float32)
    row_key = fine_id * rows + index
    rank = jnp.zeros((1, rows), jnp.float32)
    for start in range(0, rows, LANES):
        other = column_of(row_key[:, start : start + LANES])
        rank = rank + jnp.sum(jnp.where(other < row_key, 1.0, 0.0), axis=0, keepdims=True)
    rank = (rank - before).astype(jnp.int32)
    place = swapped(coarse.astype(jnp.int32), full.astype(jnp.int32), home)
    table = place * capacity + rank
    pos_ref[...] = jnp.concatenate(
        [table[:, start : start + LANES] for start in range(0, rows, LANES)], axis=0
    )
    fits = rank < jnp.where(place == home, lay.head, main - 1)
    slot = jnp.where(fits, place * main + rank, -1)
    tail_slot = jnp.where(place == home, rank - lay.head, -1)
    copies[0].wait()
    x = x_ref[...].astype(jnp.float32)
    squares = jnp.sum(x * x, axis=1, keepdims=True)
    unit[...] = (x * lax.rsqrt(squares + epsilon)).astype(jnp.bfloat16)

    def chosen_rows(slot, start, count):
        here = lax.broadcasted_iota(jnp.int32, (count, rows), 0) + start
        chosen = jnp.where(here == slot, 1.0, 0.0).astype(jnp.bfloat16)
        return jnp.dot(chosen, unit[...], preferred_element_type=jnp.float32)

    count = 2 * main
    down = lax.broadcasted_iota(jnp.int32, (count, LANES), 0)
    is_info = lax.rem(down, main) == main - 1
    writes = []
    for i, start in enumerate(range(0, lay.n_main, count)):
        packed = chosen_rows(slot, start, count)
        place = slice(start, start + count)
        main_ref[place, LANES:] = packed[:, LANES:].astype(jnp.bfloat16)
        main_ref[place, :LANES] = jnp.where(is_info, info, packed[:, :LANES]).astype(jnp.bfloat16)
        writes.append(
            pltpu.make_async_copy(
                main_ref.at[pl.ds(start, count)], main_hbm.at[pl.ds(start, count)], sems.at[3 + i]
            )
        )
        writes[-1].start()
    tail_ref[...] = chosen_rows(tail_slot, 0, lay.rest).astype(jnp.bfloat16)
    for write in writes:
        write.wait()


def vmem_specs(count):
    return (pl.BlockSpec(memory_space=pltpu.VMEM),) * count


def place_rows(embeddings, labels, owner_map, lay):
    rows, width = embeddings.shape
    n_fine = owner_map.shape[0]
    lab_shape = (rows // LANES, LANES)
    anywhere = pl.BlockSpec(memory_space=pl.ANY)
    return pl.pallas_call(
        functools.partial(place_kernel, lay),
        out_shape=(
            jax.ShapeDtypeStruct((lay.n_main, width), jnp.bfloat16),
            jax.ShapeDtypeStruct((lay.rest, width), jnp.bfloat16),
            jax.ShapeDtypeStruct(lab_shape, jnp.int32),
        ),
        in_specs=[anywhere] * 3,
        out_specs=(anywhere,) + vmem_specs(2),
        scratch_shapes=[
            pltpu.VMEM((rows, width), jnp.bfloat16),
            pltpu.VMEM(lab_shape, jnp.int32),
            pltpu.VMEM((1, n_fine), jnp.int32),
            pltpu.VMEM((rows, width), jnp.bfloat16),
            pltpu.VMEM((lay.n_main, width), jnp.bfloat16),
            pltpu.SemaphoreType.DMA((3 + lay.n_owner // 2,)),
        ],
        compiler_params=pltpu.CompilerParams(vmem_limit_bytes=FAST_LIMIT),
    )(embeddings, labels.reshape(lab_shape), owner_map.reshape(1, n_fine))


def gate_kernel(*refs):
    pass


def after(rows, *there):
    return pl.pallas_call(
        gate_kernel,
        out_shape=jax.ShapeDtypeStruct(rows.shape, rows.dtype),
        in_specs=list(vmem_specs(1 + len(there))),
        out_specs=vmem_specs(1)[0],
        input_output_aliases={0: 0},
        compiler_params=pltpu.CompilerParams(vmem_limit_bytes=FAST_LIMIT),
    )(rows, *there)


def lay_out_kernel(n_arrays, home, *refs):
    chunks, out = refs[:n_arrays], refs[-1]

    def copy():
        start = 0
        for chunk in chunks:
            out[start : start + chunk.shape[0], :] = chunk[...]
            start += chunk.shape[0]

    if home is None:
        copy()
    else:
        pl.when(lax.axis_index("cl") == home)(copy)


def lay_out(chunks, home=None, waits=()):
    rows, width = sum(x.shape[0] for x in chunks), chunks[0].shape[1]
    return pl.pallas_call(
        functools.partial(lay_out_kernel, len(chunks), home),
        out_shape=jax.ShapeDtypeStruct((rows, width), jnp.bfloat16),
        in_specs=list(vmem_specs(len(chunks) + len(waits))),
        out_specs=vmem_specs(1)[0],
        compiler_params=pltpu.CompilerParams(vmem_limit_bytes=FAST_LIMIT),
    )(*chunks, *waits)


class Layout:
    early, late = (0, 1, 2, 3), (5, 7, 4, 6)

    def __init__(self, n_owner, n_fine, capacity, main, home):
        self.n_owner, self.n_fine, self.capacity = n_owner, n_fine, capacity
        self.main, self.home = main, home
        self.head = main - INFO
        self.rest = capacity - self.head
        self.per_owner = n_fine // n_owner
        self.n_main = n_owner * main
        self.n_head = n_owner * self.head
        self.n_early = len(self.early) * self.rest
        self.n_late = len(self.late) * self.rest
        self.n_first = self.n_head + self.n_early
        self.n_all = self.n_first + self.n_late


def info_line(lay, main_ref, source):
    end = (source + 1) * lay.main
    return main_ref[end - INFO : end, :LANES].astype(jnp.float32)[INFO - 1 :]


def lines_of(lay, main_ref):
    return [info_line(lay, main_ref, source) for source in range(lay.n_owner)]


def hot_of(lay, info):
    lane = lax.broadcasted_iota(jnp.int32, (1, LANES), 1)
    hot = jnp.max(jnp.where(lane == lay.n_fine, info, 0.0), axis=1, keepdims=True)
    return hot.astype(jnp.int32)


def write_labels(lay, infos, sources, first, count, at, lab_sub, bias):
    cluster = swapped(lax.axis_index("cl"), hot_of(lay, infos[0]), lay.home)
    lane = lax.broadcasted_iota(jnp.int32, (1, LANES), 1)
    is_edge = lax.div(lane, lay.per_owner) == cluster
    for i, source in enumerate(sources):
        edges = jnp.where(is_edge, infos[source], 2.0 * lay.capacity)
        slot = lax.broadcasted_iota(jnp.int32, (count, LANES), 0) + first
        label = jnp.where(slot.astype(jnp.float32) >= edges, 1.0, 0.0)
        label = jnp.broadcast_to(jnp.sum(label, axis=1, keepdims=True), (count, LANES))
        start = at + i * count
        lab_sub[start : start + count, :] = label
        if bias is not None:
            bias[start : start + count, :] = jnp.where(
                label < lay.per_owner, NEIGHBOUR - SCALE, DEAD
            )


def first_labels(lay, infos, lab_sub):
    write_labels(lay, infos, range(lay.n_owner), 0, lay.head, 0, lab_sub, None)
    write_labels(lay, infos, lay.early, lay.head, lay.rest, lay.n_head, lab_sub, None)


def late_labels(lay, infos, lab_sub):
    write_labels(lay, infos, lay.late, lay.head, lay.rest, 0, lab_sub, None)


def turn_labels(lay, lab_sub, count, lab_lane, at):
    for i in range(0, count, LANES):
        block = jnp.transpose(lab_sub[i : i + LANES, :])[:1]
        lab_lane[:, at + i : at + i + LANES] = jnp.where(block < lay.per_owner, block, -1.0)


def copy_head(lay, main_ref, rows):
    for source in range(lay.n_owner):
        rows[source * lay.head : (source + 1) * lay.head, :] = main_ref[
            source * lay.main : source * lay.main + lay.head, :
        ]


def pieces(count, parts):
    return [(i * (count // parts), count // parts) for i in range(parts)]


def stream(lanes, tiles, lab_lane, buffers, put):
    rows_i, count, at = lanes
    step = 16
    tiles = [
        (ref, s, d, lab_sub, bias, line + s, back)
        for ref, n, lab_sub, bias, line, parts, back in tiles
        for s, d in pieces(n, parts)
    ]

    def scores_to(buffer, tile, rows):
        ref, start, deep = tile[:3]
        buffer[:deep, : rows.shape[0]] = lax.dot_general(
            ref[start : start + deep, :],
            rows,
            (((1,), (1,)), ((), ())),
            preferred_element_type=jnp.float32,
        )

    def run(start, blocks, wide):
        repeat = wide // LANES

        def rows_of(block):
            return rows_i[pl.ds(pl.multiple_of(start + block * wide, LANES), wide), :]

        scores_to(buffers[0], tiles[0], rows_of(0))

        def one_block(block):
            here = rows_of(block)
            place = pl.ds(pl.multiple_of(at + start + block * wide, LANES), wide)
            label_i = lab_lane[:, place]
            acc = jnp.zeros((8, wide), jnp.float32)
            for i, (_, _, deep, lab_sub, bias, line, back) in enumerate(tiles):
                if i + 1 < len(tiles):
                    scores_to(buffers[(i + 1) % 2], tiles[i + 1], here)
                elif blocks > 1:

                    @pl.when(block + 1 < blocks)
                    def _():
                        scores_to(buffers[0], tiles[0], rows_of(block + 1))

                buffer = buffers[i % 2]
                for c in range(0, deep, step):
                    part = slice(line + c, line + c + step)
                    label_j = jnp.concatenate([lab_sub[part, :]] * repeat, axis=1)
                    if bias is None:
                        bias_j = NEIGHBOUR - SCALE
                    else:
                        bias_j = jnp.concatenate([bias[part, :]] * repeat, axis=1)
                    shift = jnp.where(label_j == label_i, -SCALE, bias_j)
                    terms = jnp.exp2(buffer[c : c + step, :wide] * SCALE + shift)
                    acc = acc + jnp.sum(terms.reshape(step // 8, 8, wide), axis=0)
                    if back is not None:
                        across = terms[:, :LANES]
                        for r in range(1, repeat):
                            across = across + terms[:, r * LANES : (r + 1) * LANES]
                        back[part, :] += across
            put(place, jnp.sum(acc, axis=0, keepdims=True))

        if blocks == 1:
            one_block(0)
        else:
            pl.loop(0, blocks)(one_block)

    if count >= WIDE:
        run(0, count // WIDE, WIDE)
    if count % WIDE:
        run(count - count % WIDE, 1, count % WIDE)


def turn_sums(back, count, sums, at):
    for i in range(0, count, LANES):
        block = jnp.transpose(back[i : i + LANES, :])
        sums[:, at + i : at + i + LANES] += jnp.sum(block, axis=0, keepdims=True)


def setter(ref):
    def put(place, values):
        ref[:, place] = values

    return put


def adder(ref):
    def put(place, values):
        ref[:, place] += values

    return put


def inner_kernel(lay, mine, early, sums, lab_lane, lab_sub, rows, bias, back, buf_a, buf_b):
    is_home = lax.axis_index("cl") == lay.home
    infos = lines_of(lay, mine)
    buffers = (buf_a, buf_b)

    @pl.when(is_home)
    def _():
        copy_head(lay, mine, rows)
        first_labels(lay, infos, lab_sub)
        turn_labels(lay, lab_sub, lay.n_first, lab_lane, 0)
        back[...] = jnp.zeros(back.shape, jnp.float32)
        size = lay.n_early
        blocks = [(rows.at[pl.ds(start, size)], start) for start in range(0, lay.n_head, size)]
        blocks.append((early, lay.n_head))
        for i, (ref, at) in enumerate(blocks):
            tiles = [
                (ref_j, size, lab_sub, None, at_j, 2, None if at_j == at else back)
                for ref_j, at_j in blocks[i:]
            ]
            stream((ref, size, at), tiles, lab_lane, buffers, setter(sums))
        turn_sums(back, lay.n_first, sums, 0)

    @pl.when(jnp.logical_not(is_home))
    def _():
        write_labels(lay, infos, range(lay.n_owner), 0, lay.main, 0, lab_sub, bias)
        turn_labels(lay, lab_sub, lay.n_main, lab_lane, 0)
        tiles = [(mine, lay.n_main, lab_sub, bias, 0, 2, None)]
        stream((mine, lay.n_main, 0), tiles, lab_lane, buffers, setter(sums))


def half_blocks(ref_i, ref_j, lab_sub, line, back, at, lab_lane, buffers, put):
    half = ref_j.shape[0] // 2
    grp = lax.axis_index("grp")
    for h in range(2):
        start = pl.multiple_of((h ^ grp) * half, half)
        rows_j = ref_j.at[pl.ds(start, half)]
        sub = lab_sub.at[pl.ds(line + start, half)]
        backs = back.at[pl.ds(line + start, half)]
        lanes = (ref_i.at[pl.ds(h * half, half)], half, at + h * half)
        stream(lanes, [(rows_j, half, sub, None, 0, 1, backs)], lab_lane, buffers, put)


def cross_kernel(lay, mine, other, early, early_j, rows, sums, lab_lane, *refs):
    total, for_other, unfit_ref, late_sub, late_sub_j, long_lane, late_lane_j = refs[:7]
    lab_sub, bias, back, rows_j, buf_a, buf_b = refs[7:]
    is_home = lax.axis_index("cl") == lay.home
    infos = lines_of(lay, other)
    own = lines_of(lay, mine)
    hot = hot_of(lay, own[0])
    lane = lax.broadcasted_iota(jnp.int32, (1, LANES), 1)
    last = (lane < lay.n_fine) & (lax.rem(lane, lay.per_owner) == lay.per_owner - 1)
    last = last & (lax.div(lane, lay.per_owner) != hot)
    unfit = jnp.zeros((1, LANES), jnp.float32)
    for info in infos + own:
        wrong = last & (info >= lay.main)
        differs = (info != hot.astype(jnp.float32)) | (info >= lay.n_owner)
        wrong = wrong | ((lane == lay.n_fine) & differs)
        unfit = unfit + jnp.where(wrong, 1.0, 0.0)
    unfit_ref[0, 0] = jnp.max(unfit).astype(jnp.int32)
    total[...] = sums[...]
    buffers = (buf_a, buf_b)

    @pl.when(is_home)
    def _():
        copy_head(lay, other, rows_j)
        first_labels(lay, infos, lab_sub)
        back[...] = jnp.zeros(back.shape, jnp.float32)
        size = lay.n_early
        blocks_i = [rows.at[pl.ds(start, size)] for start in range(0, lay.n_head, size)] + [early]
        blocks_j = [rows_j.at[pl.ds(start, size)] for start in range(0, lay.n_head, size)]
        blocks_j.append(early_j)
        put, n = adder(total), len(blocks_i)
        for i, ref in enumerate(blocks_i):
            tiles = [
                (blocks_j[j], size, lab_sub, None, j * size, 2, back)
                for j in ((i + step) % n for step in range(1, (n + 1) // 2))
            ]
            stream((ref, size, i * size), tiles, lab_lane, buffers, put)
            half_blocks(
                ref, blocks_j[i], lab_sub, i * size, back, i * size, lab_lane, buffers, put
            )
        write_labels(lay, own, lay.late, lay.head, lay.rest, 0, late_sub, None)
        write_labels(lay, infos, lay.late, lay.head, lay.rest, 0, late_sub_j, None)
        long_lane[:, : lay.n_first] = lab_lane[...]
        turn_labels(lay, late_sub, lay.n_late, long_lane, lay.n_first)
        turn_labels(lay, late_sub_j, lay.n_late, late_lane_j, 0)
        for_other[...] = jnp.zeros(for_other.shape, jnp.float32)
        turn_sums(back, lay.n_first, for_other, 0)

    @pl.when(jnp.logical_not(is_home))
    def _():
        write_labels(lay, infos, range(lay.n_owner), 0, lay.main, 0, lab_sub, bias)
        tiles = [(other, lay.n_main, lab_sub, bias, 0, 2, None)]
        stream((mine, lay.n_main, 0), tiles, lab_lane, buffers, adder(total))


def first_tiles(lay, rows, early, lab_sub, back):
    return [
        (rows, lay.n_head, lab_sub, None, 0, 4, back),
        (early, lay.n_early, lab_sub, None, lay.n_head, 2, back),
    ]


def inner_late_kernel(lay, early, late, rows, lab_sub, late_sub, lab_lane, sums, *refs):
    back, buf_a, buf_b = refs

    @pl.when(lax.axis_index("cl") == lay.home)
    def _():
        back[...] = jnp.zeros(back.shape, jnp.float32)
        sums[:, : lay.n_first] = jnp.zeros((1, lay.n_first), jnp.float32)
        tiles = first_tiles(lay, rows, early, lab_sub, back)
        tiles.append((late, lay.n_late, late_sub, None, 0, 2, None))
        lanes = (late, lay.n_late, lay.n_first)
        stream(lanes, tiles, lab_lane, (buf_a, buf_b), setter(sums))
        turn_sums(back, lay.n_first, sums, 0)


def cross_late_kernel(lay, early, late, late_j, rows, lab_sub, late_sub, lab_lane, *refs):
    late_lane, first_lane, first_sums, first_other, sums, out_ref = refs[:6]
    total, late_other, back, late_back, buf_a, buf_b = refs[6:]
    is_home = lax.axis_index("cl") == lay.home
    grp = lax.axis_index("grp")

    @pl.when(is_home)
    def _():
        total[...] = sums[...]
        total[:, : lay.n_first] += first_sums[...]
        back[...] = jnp.zeros(back.shape, jnp.float32)
        late_back[...] = jnp.zeros(late_back.shape, jnp.float32)
        buffers = (buf_a, buf_b)
        tiles = first_tiles(lay, rows, early, lab_sub, back)
        stream((late_j, lay.n_late, 0), tiles, late_lane, buffers, setter(late_other))
        turn_sums(back, lay.n_first, total, 0)
        put = adder(total)
        half_blocks(late, late_j, late_sub, 0, late_back, lay.n_first, lab_lane, buffers, put)
        turn_sums(late_back, lay.n_late, late_other, 0)

        def write(line, values):
            for source in range(lay.n_owner):
                start = source * lay.head
                out_ref[2 * source + line, :, : lay.head] = values[:, start : start + lay.head]
            for i, source in enumerate(lay.early + lay.late):
                start = lay.n_head + i * lay.rest
                out_ref[2 * source + line, :, lay.head :] = values[:, start : start + lay.rest]

        write(grp, total[...])
        total[:, : lay.n_first] = first_other[...]
        total[:, lay.n_first :] = late_other[...]
        write(1 - grp, total[...])

    @pl.when(jnp.logical_not(is_home))
    def _():
        out_ref[...] = jnp.zeros(out_ref.shape, jnp.float32)
        values = jnp.where(first_lane[...] >= 0, first_sums[...], 1.0)
        for source in range(lay.n_owner):
            start = source * lay.main
            out_ref[2 * source + grp, :, : lay.main] = values[:, start : start + lay.main]


def pair_call(kernel, lay, arrays, out_shape, scratch, out_specs=None, pairs=0):
    width = arrays[0].shape[1]
    buffer = pltpu.VMEM((lay.n_main // 2, WIDE), jnp.float32)
    return pl.pallas_call(
        functools.partial(kernel, lay),
        out_shape=out_shape,
        in_specs=list(vmem_specs(len(arrays))),
        out_specs=out_specs or vmem_specs(len(out_shape)),
        scratch_shapes=list(scratch) + [buffer, buffer],
        compiler_params=pltpu.CompilerParams(vmem_limit_bytes=FAST_LIMIT),
        cost_estimate=pl.CostEstimate(
            flops=2 * pairs * width, bytes_accessed=1, transcendentals=pairs
        ),
    )(*arrays)


def fast_unpack_kernel(values_ref, pos_ref, out_ref):
    pos = pos_ref[...]
    lane = lax.rem(pos, LANES)
    line = lax.div(pos, LANES)
    out = jnp.ones(pos.shape, jnp.float32)
    per = values_ref.shape[2] // LANES
    for r in range(values_ref.shape[0] // 2 * per):
        owner, part = r // per, slice(r % per * LANES, (r % per + 1) * LANES)
        table = values_ref[2 * owner, :, part] + values_ref[2 * owner + 1, :, part]
        found = jnp.take_along_axis(jnp.broadcast_to(table, pos.shape), lane, axis=1)
        out = jnp.where(line == r, found, out)
    out_ref[...] = jnp.log(out)


def fast_unpack(values, pos):
    vmem = pl.BlockSpec(memory_space=pltpu.VMEM)
    return pl.pallas_call(
        fast_unpack_kernel,
        out_shape=jax.ShapeDtypeStruct(pos.shape, jnp.float32),
        in_specs=[vmem, vmem],
        out_specs=vmem,
    )(values, pos)


def general(embeddings, labels, owner_map):
    n_owner = lax.axis_size("cl")
    capacity = SLOTS // n_owner
    rows, width = embeddings.shape
    packed, pos, counts = pack(embeddings, labels, owner_map, n_owner, capacity)
    counts = lax.all_gather(counts, ("cl", "grp"), tiled=True)
    mine = lax.all_to_all(
        packed.reshape(n_owner, capacity, width), "cl", split_axis=0, concat_axis=0, tiled=True
    ).reshape(SLOTS, width)
    other = lax.ppermute(mine, "grp", [(0, 1), (1, 0)])
    results = log_counts(counts, mine, other, n_owner, capacity)
    returned = lax.all_to_all(
        results.reshape(n_owner, capacity), "cl", split_axis=0, concat_axis=0, tiled=True
    )
    return unpack(returned.reshape(SLOTS), pos).reshape(rows)


def body(embeddings, labels, owner_map):
    n_owner = lax.axis_size("cl")
    capacity = SLOTS // n_owner
    rows, width = embeddings.shape
    n_fine = owner_map.shape[0]
    main = -(-(rows // n_owner * 9 // 8) // 16) * 16
    if n_owner != 8 or main >= capacity or n_fine >= LANES:
        return general(embeddings, labels, owner_map)
    home = 2
    lay = Layout(n_owner, n_fine, capacity, main, home)
    packed, extra, pos = place_rows(embeddings, labels, owner_map, lay)

    def hop(x, pairs):
        return lax.ppermute(x, "cl", pairs)

    def swap(x):
        return lax.ppermute(x, "grp", [(0, 1), (1, 0)])

    both = lay_out([extra, hop(extra, [(6, 4), (7, 5)])])
    early = [extra if s == home else hop(extra, [(s, home)]) for s in lay.early]
    early = lay_out(early, home)
    mine = lax.all_to_all(
        packed.reshape(n_owner, main, width), "cl", split_axis=0, concat_axis=0, tiled=True
    ).reshape(n_owner * main, width)
    mine = after(mine, early, both)
    other, early_j = swap(mine), swap(early)
    late = [hop(both, [(s, home)]) for s in (5, 4)]

    def array(shape, dtype=jnp.float32):
        return jax.ShapeDtypeStruct(shape, dtype)

    def scratch(shape):
        return pltpu.VMEM(shape, jnp.float32)

    row, long_row = array((1, lay.n_first)), array((1, lay.n_all))
    bias = scratch((lay.n_main, LANES))
    heads = array((lay.n_head, width), jnp.bfloat16)
    late_lines, first_lines = array((lay.n_late, LANES)), array((lay.n_first, LANES))
    late_row = array((1, lay.n_late))
    late_side, first_side = scratch((lay.n_late, LANES)), scratch((lay.n_first, LANES))
    sums, first_lane, lab_sub, heads_i = pair_call(
        inner_kernel, lay, (mine, early), (row, row, first_lines, heads), (bias, first_side)
    )
    specs = vmem_specs(2) + (pl.BlockSpec(memory_space=pltpu.SMEM),) + vmem_specs(4)
    sums, first_other, unfit, late_sub, late_sub_j, lane, lane_j = pair_call(
        cross_kernel,
        lay,
        (mine, other, early, early_j, heads_i, sums, first_lane),
        (row, row, array((1, 1), jnp.int32), late_lines, late_lines, long_row, late_row),
        (first_side, bias, first_side, pltpu.VMEM(heads.shape, heads.dtype)),
        specs,
    )
    late = lay_out(late, home, (sums,))
    late_j = swap(late)
    (late_sums,) = pair_call(
        inner_late_kernel,
        lay,
        (early, late, heads_i, lab_sub, late_sub, lane),
        (long_row,),
        (first_side,),
        pairs=lay.n_late * lay.n_all,
    )
    (results,) = pair_call(
        cross_late_kernel,
        lay,
        (
            *(early, late, late_j, heads_i, lab_sub, late_sub_j, lane, lane_j),
            *(first_lane, sums, first_other, late_sums),
        ),
        (array((2 * n_owner, 1, capacity)),),
        (scratch(long_row.shape), scratch(late_row.shape), first_side, late_side),
    )
    returned = lax.all_to_all(
        results, ("cl", "grp"), split_axis=0, concat_axis=0, tiled=True
    )
    return lax.cond(
        unfit[0, 0] == 0,
        lambda: fast_unpack(returned, pos).reshape(rows),
        lambda: general(embeddings, labels, owner_map),
    )


def solution(mesh):
    return jax.shard_map(
        body,
        mesh=mesh,
        in_specs=(P(("parts", "cl", "grp"), None), P(("parts", "cl", "grp")), P("parts")),
        out_specs=P(("parts", "cl", "grp")),
        check_vma=False,
    )
```

```python
import functools
import math

import jax
import jax.numpy as jnp
from jax import lax
from jax.experimental import pallas as pl
from jax.experimental.pallas import tpu as pltpu
from jax.sharding import PartitionSpec as P

SLOTS = 2048

temper = 0.2
neighbour_factor = 0.5
epsilon = 1e-06

LANES = 128
SCALE = math.log2(math.e) / temper
NEIGHBOUR = math.log2(neighbour_factor)
DEAD = -1e30
VMEM_LIMIT = 48 * 1024 * 1024
FAST_LIMIT = 16 * 1024 * 1024
WIDE = 512
INFO = 16


def column_of(row):
    pieces = []
    for start in range(0, row.shape[1], LANES):
        width = min(LANES, row.shape[1] - start)
        shape = (width, width)
        diagonal = lax.broadcasted_iota(jnp.int32, shape, 0) == lax.broadcasted_iota(
            jnp.int32, shape, 1
        )
        piece = jnp.broadcast_to(row[:, start : start + width], shape)
        pieces.append(jnp.sum(jnp.where(diagonal, piece, 0.0), axis=1, keepdims=True))
    return jnp.concatenate(pieces, axis=0)


def row_of(column):
    n = column.shape[0]
    diagonal = lax.broadcasted_iota(jnp.int32, (n, n), 0) == lax.broadcasted_iota(
        jnp.int32, (n, n), 1
    )
    return jnp.sum(jnp.where(diagonal, column, 0.0), axis=0, keepdims=True)


def pack_kernel(n_owner, capacity, x_ref, lab_ref, map_ref, out_ref, pos_ref, cnt_ref, unit, pos_row):
    rows = x_ref.shape[0]
    n_fine = map_ref.shape[1]
    per_owner = n_fine // n_owner
    owner_row = map_ref[...].astype(jnp.float32)
    fine_row = lax.broadcasted_iota(jnp.int32, (1, n_fine), 1).astype(jnp.float32)
    key_row = owner_row * n_fine + fine_row
    key_col = column_of(key_row)
    sorted_col = jnp.sum(jnp.where(key_row < key_col, 1.0, 0.0), axis=1, keepdims=True)
    lab = lab_ref[...].astype(jnp.float32)
    lab_row = jnp.concatenate([lab[b : b + 1, :] for b in range(lab.shape[0])], axis=1)
    fine_col = lax.broadcasted_iota(jnp.int32, (n_fine, rows), 0).astype(jnp.float32)
    fine_id = jnp.sum(jnp.where(fine_col == lab_row, sorted_col, 0.0), axis=0, keepdims=True)
    counts_col = jnp.sum(jnp.where(fine_col == fine_id, 1.0, 0.0), axis=1, keepdims=True)
    cnt_ref[...] = row_of(counts_col).astype(jnp.int32)
    coarse = jnp.floor((fine_id + 0.5) * (1.0 / per_owner))
    before = jnp.sum(
        jnp.where(fine_col < coarse * per_owner, counts_col, 0.0), axis=0, keepdims=True
    )
    index = lax.broadcasted_iota(jnp.int32, (1, rows), 1).astype(jnp.float32)
    row_key = fine_id * rows + index
    rank = jnp.zeros((1, rows), jnp.float32)
    for start in range(0, rows, LANES):
        other = column_of(row_key[:, start : start + LANES])
        rank = rank + jnp.sum(jnp.where(other < row_key, 1.0, 0.0), axis=0, keepdims=True)
    pos = (coarse * capacity + rank - before).astype(jnp.int32)
    pos_row[...] = pos
    pos_ref[...] = jnp.concatenate(
        [pos[:, start : start + LANES] for start in range(0, rows, LANES)], axis=0
    )
    x = x_ref[...].astype(jnp.float32)
    squares = jnp.sum(x * x, axis=1, keepdims=True)
    unit[...] = (x * lax.rsqrt(squares + epsilon)).astype(jnp.bfloat16)

    step = 256

    @pl.loop(0, out_ref.shape[0] // step)
    def _(block):
        slot = lax.broadcasted_iota(jnp.int32, (step, rows), 0) + block * step
        chosen = jnp.where(slot == pos_row[...], 1.0, 0.0).astype(jnp.bfloat16)
        packed = jnp.dot(chosen, unit[...], preferred_element_type=jnp.float32)
        out_ref[pl.ds(pl.multiple_of(block * step, step), step), :] = packed.astype(jnp.bfloat16)


def pack(embeddings, labels, owner_map, n_owner, capacity):
    rows, width = embeddings.shape
    n_fine = owner_map.shape[0]
    total = n_owner * capacity
    vmem = pl.BlockSpec(memory_space=pltpu.VMEM)
    return pl.pallas_call(
        functools.partial(pack_kernel, n_owner, capacity),
        out_shape=(
            jax.ShapeDtypeStruct((total, width), jnp.bfloat16),
            jax.ShapeDtypeStruct((rows // LANES, LANES), jnp.int32),
            jax.ShapeDtypeStruct((1, n_fine), jnp.int32),
        ),
        in_specs=[vmem] * 3,
        out_specs=(vmem, vmem, vmem),
        scratch_shapes=[pltpu.VMEM((rows, width), jnp.bfloat16), pltpu.VMEM((1, rows), jnp.int32)],
        compiler_params=pltpu.CompilerParams(vmem_limit_bytes=VMEM_LIMIT),
    )(embeddings, labels.reshape(rows // LANES, LANES), owner_map.reshape(1, n_fine))


def counts_kernel(n_owner, capacity, cnt_ref, mine_ref, other_ref, out_ref, lab_lane, lab_sub, bias):
    total = mine_ref.shape[0]
    per_owner = cnt_ref.shape[1] // n_owner
    me = lax.axis_index("cl")
    grp = lax.axis_index("grp")
    n_grp = lax.axis_size("grp")
    for member in range(2):
        for source in range(n_owner):
            line = source * n_grp + lax.rem(grp + member, n_grp)
            edges = []
            edge = jnp.int32(0)
            for f in range(per_owner):
                edge = edge + cnt_ref[line, me * per_owner + f]
                edges.append(edge)
            down = lax.broadcasted_iota(jnp.int32, (capacity, LANES), 0)
            label = jnp.zeros((capacity, LANES), jnp.int32)
            for edge in edges:
                label = label + jnp.where(down >= edge, 1, 0)
            start = (member * n_owner + source) * capacity
            lab_sub[start : start + capacity, :] = label
            bias[start : start + capacity, :] = jnp.where(
                label < per_owner, NEIGHBOUR - SCALE, DEAD
            )
            if member == 0:
                across = lax.broadcasted_iota(jnp.int32, (1, capacity), 1)
                label = jnp.zeros((1, capacity), jnp.int32)
                for edge in edges:
                    label = label + jnp.where(across >= edge, 1, 0)
                lab_lane[:, source * capacity : (source + 1) * capacity] = jnp.where(
                    label < per_owner, label, -1
                )
    wide, deep = min(512, total), min(256, total)

    @pl.loop(0, total // wide)
    def _(block):
        columns = pl.ds(pl.multiple_of(block * wide, wide), wide)
        rows_i = mine_ref[columns, :]
        label_i = lab_lane[:, columns]

        def add(ref, offset):
            def step(j, acc):
                start = pl.multiple_of(j * deep, deep)
                scores = lax.dot_general(
                    ref[pl.ds(start, deep), :],
                    rows_i,
                    (((1,), (1,)), ((), ())),
                    preferred_element_type=jnp.float32,
                )
                place = pl.ds(pl.multiple_of(start + offset, deep), deep)
                label_j = lab_sub[place, :]
                bias_j = bias[place, :]
                repeat = wide // LANES
                label_j = jnp.concatenate([label_j] * repeat, axis=1)
                bias_j = jnp.concatenate([bias_j] * repeat, axis=1)
                shift = jnp.where(label_j == label_i, -SCALE, bias_j)
                terms = jnp.exp2(scores * SCALE + shift)
                return acc + jnp.sum(terms.reshape(deep // 8, 8, wide), axis=0)

            return step

        acc = jnp.zeros((8, wide), jnp.float32)
        acc = lax.fori_loop(0, total // deep, add(mine_ref, 0), acc, unroll=2)
        acc = lax.fori_loop(0, total // deep, add(other_ref, total), acc, unroll=2)
        totals = jnp.sum(acc, axis=0, keepdims=True)
        out_ref[:, columns] = jnp.log(jnp.where(label_i >= 0, totals, 1.0))


def log_counts(counts, mine, other, n_owner, capacity):
    total = mine.shape[0]
    vmem = pl.BlockSpec(memory_space=pltpu.VMEM)
    return pl.pallas_call(
        functools.partial(counts_kernel, n_owner, capacity),
        out_shape=jax.ShapeDtypeStruct((1, total), jnp.float32),
        in_specs=[pl.BlockSpec(memory_space=pltpu.SMEM), vmem, vmem],
        out_specs=vmem,
        scratch_shapes=[
            pltpu.VMEM((1, total), jnp.int32),
            pltpu.VMEM((2 * total, LANES), jnp.int32),
            pltpu.VMEM((2 * total, LANES), jnp.float32),
        ],
        compiler_params=pltpu.CompilerParams(vmem_limit_bytes=VMEM_LIMIT),
    )(counts, mine, other)


def unpack_kernel(values_ref, pos_ref, out_ref):
    pos = pos_ref[...]
    lane = lax.rem(pos, LANES)
    line = lax.div(pos, LANES)
    out = jnp.zeros(pos.shape, jnp.float32)
    for r in range(values_ref.shape[0]):
        table = jnp.broadcast_to(values_ref[r : r + 1, :], pos.shape)
        found = jnp.take_along_axis(table, lane, axis=1)
        out = jnp.where(line == r, found, out)
    out_ref[...] = out


def unpack(values, pos):
    vmem = pl.BlockSpec(memory_space=pltpu.VMEM)
    return pl.pallas_call(
        unpack_kernel,
        out_shape=jax.ShapeDtypeStruct(pos.shape, jnp.float32),
        in_specs=[vmem, vmem],
        out_specs=vmem,
    )(values.reshape(-1, LANES), pos)


def swapped(x, first, second):
    return jnp.where(x == first, second, jnp.where(x == second, first, x))


def place_kernel(lay, x_hbm, lab_hbm, map_hbm, *refs):
    main_hbm, tail_ref, pos_ref, x_ref, lab_ref, map_ref, unit, main_ref, sems = refs
    n_owner, capacity, main, home = lay.n_owner, lay.capacity, lay.main, lay.home
    copies = [
        pltpu.make_async_copy(src, dst, sems.at[i])
        for i, (src, dst) in enumerate(((x_hbm, x_ref), (lab_hbm, lab_ref), (map_hbm, map_ref)))
    ]
    for copy in copies:
        copy.start()
    rows, width = x_ref.shape
    n_fine = map_ref.shape[1]
    per_owner = n_fine // n_owner
    copies[1].wait()
    copies[2].wait()
    owner_row = map_ref[...].astype(jnp.float32)
    fine_row = lax.broadcasted_iota(jnp.int32, (1, n_fine), 1).astype(jnp.float32)
    key_row = owner_row * n_fine + fine_row
    key_col = column_of(key_row)
    sorted_col = jnp.sum(jnp.where(key_row < key_col, 1.0, 0.0), axis=1, keepdims=True)
    lab = lab_ref[...].astype(jnp.float32)
    lab_row = jnp.concatenate([lab[b : b + 1, :] for b in range(lab.shape[0])], axis=1)
    fine_col = lax.broadcasted_iota(jnp.int32, (n_fine, rows), 0).astype(jnp.float32)
    fine_id = jnp.sum(jnp.where(fine_col == lab_row, sorted_col, 0.0), axis=0, keepdims=True)
    counts_col = jnp.sum(jnp.where(fine_col == fine_id, 1.0, 0.0), axis=1, keepdims=True)
    coarse = jnp.floor((fine_id + 0.5) * (1.0 / per_owner))
    first = coarse * per_owner
    before = jnp.sum(jnp.where(fine_col < first, counts_col, 0.0), axis=0, keepdims=True)
    upto = jnp.sum(jnp.where(fine_col < first + per_owner, counts_col, 0.0), axis=0, keepdims=True)
    full = jnp.min(
        jnp.where(upto - before == capacity, coarse, float(n_owner)), axis=1, keepdims=True
    )
    line = lax.broadcasted_iota(jnp.int32, (n_fine, LANES), 0)
    lane = lax.broadcasted_iota(jnp.int32, (n_fine, LANES), 1)
    inside = (line <= lane) & (lax.div(line, per_owner) == lax.div(lane, per_owner))
    running = jnp.sum(jnp.where(inside, counts_col, 0.0), axis=0, keepdims=True)
    info = jnp.where(lane[:1] < n_fine, running, full)
    index = lax.broadcasted_iota(jnp.int32, (1, rows), 1).astype(jnp.float32)
    row_key = fine_id * rows + index
    rank = jnp.zeros((1, rows), jnp.float32)
    for start in range(0, rows, LANES):
        other = column_of(row_key[:, start : start + LANES])
        rank = rank + jnp.sum(jnp.where(other < row_key, 1.0, 0.0), axis=0, keepdims=True)
    rank = (rank - before).astype(jnp.int32)
    place = swapped(coarse.astype(jnp.int32), full.astype(jnp.int32), home)
    table = place * capacity + rank
    pos_ref[...] = jnp.concatenate(
        [table[:, start : start + LANES] for start in range(0, rows, LANES)], axis=0
    )
    fits = rank < jnp.where(place == home, lay.head, main - 1)
    slot = jnp.where(fits, place * main + rank, -1)
    tail_slot = jnp.where(place == home, rank - lay.head, -1)
    copies[0].wait()
    x = x_ref[...].astype(jnp.float32)
    squares = jnp.sum(x * x, axis=1, keepdims=True)
    unit[...] = (x * lax.rsqrt(squares + epsilon)).astype(jnp.bfloat16)

    def chosen_rows(slot, start, count):
        here = lax.broadcasted_iota(jnp.int32, (count, rows), 0) + start
        chosen = jnp.where(here == slot, 1.0, 0.0).astype(jnp.bfloat16)
        return jnp.dot(chosen, unit[...], preferred_element_type=jnp.float32)

    count = 2 * main
    down = lax.broadcasted_iota(jnp.int32, (count, LANES), 0)
    is_info = lax.rem(down, main) == main - 1
    writes = []
    for i, start in enumerate(range(0, lay.n_main, count)):
        packed = chosen_rows(slot, start, count)
        place = slice(start, start + count)
        main_ref[place, LANES:] = packed[:, LANES:].astype(jnp.bfloat16)
        main_ref[place, :LANES] = jnp.where(is_info, info, packed[:, :LANES]).astype(jnp.bfloat16)
        writes.append(
            pltpu.make_async_copy(
                main_ref.at[pl.ds(start, count)], main_hbm.at[pl.ds(start, count)], sems.at[3 + i]
            )
        )
        writes[-1].start()
    tail_ref[...] = chosen_rows(tail_slot, 0, lay.rest).astype(jnp.bfloat16)
    for write in writes:
        write.wait()


def vmem_specs(count):
    return (pl.BlockSpec(memory_space=pltpu.VMEM),) * count


def place_rows(embeddings, labels, owner_map, lay):
    rows, width = embeddings.shape
    n_fine = owner_map.shape[0]
    lab_shape = (rows // LANES, LANES)
    anywhere = pl.BlockSpec(memory_space=pl.ANY)
    return pl.pallas_call(
        functools.partial(place_kernel, lay),
        out_shape=(
            jax.ShapeDtypeStruct((lay.n_main, width), jnp.bfloat16),
            jax.ShapeDtypeStruct((lay.rest, width), jnp.bfloat16),
            jax.ShapeDtypeStruct(lab_shape, jnp.int32),
        ),
        in_specs=[anywhere] * 3,
        out_specs=(anywhere,) + vmem_specs(2),
        scratch_shapes=[
            pltpu.VMEM((rows, width), jnp.bfloat16),
            pltpu.VMEM(lab_shape, jnp.int32),
            pltpu.VMEM((1, n_fine), jnp.int32),
            pltpu.VMEM((rows, width), jnp.bfloat16),
            pltpu.VMEM((lay.n_main, width), jnp.bfloat16),
            pltpu.SemaphoreType.DMA((3 + lay.n_owner // 2,)),
        ],
        compiler_params=pltpu.CompilerParams(vmem_limit_bytes=FAST_LIMIT),
    )(embeddings, labels.reshape(lab_shape), owner_map.reshape(1, n_fine))


def gate_kernel(*refs):
    pass


def after(rows, *there):
    return pl.pallas_call(
        gate_kernel,
        out_shape=jax.ShapeDtypeStruct(rows.shape, rows.dtype),
        in_specs=list(vmem_specs(1 + len(there))),
        out_specs=vmem_specs(1)[0],
        input_output_aliases={0: 0},
        compiler_params=pltpu.CompilerParams(vmem_limit_bytes=FAST_LIMIT),
    )(rows, *there)


def lay_out_kernel(n_arrays, home, *refs):
    chunks, out = refs[:n_arrays], refs[-1]

    def copy():
        start = 0
        for chunk in chunks:
            out[start : start + chunk.shape[0], :] = chunk[...]
            start += chunk.shape[0]

    if home is None:
        copy()
    else:
        pl.when(lax.axis_index("cl") == home)(copy)


def lay_out(chunks, home=None, waits=()):
    rows, width = sum(x.shape[0] for x in chunks), chunks[0].shape[1]
    return pl.pallas_call(
        functools.partial(lay_out_kernel, len(chunks), home),
        out_shape=jax.ShapeDtypeStruct((rows, width), jnp.bfloat16),
        in_specs=list(vmem_specs(len(chunks) + len(waits))),
        out_specs=vmem_specs(1)[0],
        compiler_params=pltpu.CompilerParams(vmem_limit_bytes=FAST_LIMIT),
    )(*chunks, *waits)


class Layout:
    early, late = (0, 1, 2, 3), (5, 7, 4, 6)

    def __init__(self, n_owner, n_fine, capacity, main, home):
        self.n_owner, self.n_fine, self.capacity = n_owner, n_fine, capacity
        self.main, self.home = main, home
        self.head = main - INFO
        self.rest = capacity - self.head
        self.per_owner = n_fine // n_owner
        self.n_main = n_owner * main
        self.n_head = n_owner * self.head
        self.n_early = len(self.early) * self.rest
        self.n_late = len(self.late) * self.rest
        self.n_first = self.n_head + self.n_early
        self.n_all = self.n_first + self.n_late


def info_line(lay, main_ref, source):
    end = (source + 1) * lay.main
    return main_ref[end - INFO : end, :LANES].astype(jnp.float32)[INFO - 1 :]


def lines_of(lay, main_ref):
    return [info_line(lay, main_ref, source) for source in range(lay.n_owner)]


def hot_of(lay, info):
    lane = lax.broadcasted_iota(jnp.int32, (1, LANES), 1)
    hot = jnp.max(jnp.where(lane == lay.n_fine, info, 0.0), axis=1, keepdims=True)
    return hot.astype(jnp.int32)


def write_labels(lay, infos, sources, first, count, at, lab_sub, bias):
    cluster = swapped(lax.axis_index("cl"), hot_of(lay, infos[0]), lay.home)
    lane = lax.broadcasted_iota(jnp.int32, (1, LANES), 1)
    is_edge = lax.div(lane, lay.per_owner) == cluster
    for i, source in enumerate(sources):
        edges = jnp.where(is_edge, infos[source], 2.0 * lay.capacity)
        slot = lax.broadcasted_iota(jnp.int32, (count, LANES), 0) + first
        label = jnp.where(slot.astype(jnp.float32) >= edges, 1.0, 0.0)
        label = jnp.broadcast_to(jnp.sum(label, axis=1, keepdims=True), (count, LANES))
        start = at + i * count
        lab_sub[start : start + count, :] = label
        if bias is not None:
            bias[start : start + count, :] = jnp.where(
                label < lay.per_owner, NEIGHBOUR - SCALE, DEAD
            )


def first_labels(lay, infos, lab_sub):
    write_labels(lay, infos, range(lay.n_owner), 0, lay.head, 0, lab_sub, None)
    write_labels(lay, infos, lay.early, lay.head, lay.rest, lay.n_head, lab_sub, None)


def late_labels(lay, infos, lab_sub):
    write_labels(lay, infos, lay.late, lay.head, lay.rest, 0, lab_sub, None)


def turn_labels(lay, lab_sub, count, lab_lane, at):
    for i in range(0, count, LANES):
        block = jnp.transpose(lab_sub[i : i + LANES, :])[:1]
        lab_lane[:, at + i : at + i + LANES] = jnp.where(block < lay.per_owner, block, -1.0)


def copy_head(lay, main_ref, rows):
    for source in range(lay.n_owner):
        rows[source * lay.head : (source + 1) * lay.head, :] = main_ref[
            source * lay.main : source * lay.main + lay.head, :
        ]


def pieces(count, parts):
    return [(i * (count // parts), count // parts) for i in range(parts)]


def stream(lanes, tiles, lab_lane, buffers, put):
    rows_i, count, at = lanes
    step = 16
    tiles = [
        (ref, s, d, lab_sub, bias, line + s, back)
        for ref, n, lab_sub, bias, line, parts, back in tiles
        for s, d in pieces(n, parts)
    ]

    def scores_to(buffer, tile, rows):
        ref, start, deep = tile[:3]
        buffer[:deep, : rows.shape[0]] = lax.dot_general(
            ref[start : start + deep, :],
            rows,
            (((1,), (1,)), ((), ())),
            preferred_element_type=jnp.float32,
        )

    def run(start, blocks, wide):
        repeat = wide // LANES

        def rows_of(block):
            return rows_i[pl.ds(pl.multiple_of(start + block * wide, LANES), wide), :]

        scores_to(buffers[0], tiles[0], rows_of(0))

        def one_block(block):
            here = rows_of(block)
            place = pl.ds(pl.multiple_of(at + start + block * wide, LANES), wide)
            label_i = lab_lane[:, place]
            acc = jnp.zeros((8, wide), jnp.float32)
            for i, (_, _, deep, lab_sub, bias, line, back) in enumerate(tiles):
                if i + 1 < len(tiles):
                    scores_to(buffers[(i + 1) % 2], tiles[i + 1], here)
                elif blocks > 1:

                    @pl.when(block + 1 < blocks)
                    def _():
                        scores_to(buffers[0], tiles[0], rows_of(block + 1))

                buffer = buffers[i % 2]
                for c in range(0, deep, step):
                    part = slice(line + c, line + c + step)
                    label_j = jnp.concatenate([lab_sub[part, :]] * repeat, axis=1)
                    if bias is None:
                        bias_j = NEIGHBOUR - SCALE
                    else:
                        bias_j = jnp.concatenate([bias[part, :]] * repeat, axis=1)
                    shift = jnp.where(label_j == label_i, -SCALE, bias_j)
                    terms = jnp.exp2(buffer[c : c + step, :wide] * SCALE + shift)
                    acc = acc + jnp.sum(terms.reshape(step // 8, 8, wide), axis=0)
                    if back is not None:
                        across = terms[:, :LANES]
                        for r in range(1, repeat):
                            across = across + terms[:, r * LANES : (r + 1) * LANES]
                        back[part, :] += across
            put(place, jnp.sum(acc, axis=0, keepdims=True))

        if blocks == 1:
            one_block(0)
        else:
            pl.loop(0, blocks)(one_block)

    if count >= WIDE:
        run(0, count // WIDE, WIDE)
    if count % WIDE:
        run(count - count % WIDE, 1, count % WIDE)


def turn_sums(back, count, sums, at):
    for i in range(0, count, LANES):
        block = jnp.transpose(back[i : i + LANES, :])
        sums[:, at + i : at + i + LANES] += jnp.sum(block, axis=0, keepdims=True)


def setter(ref):
    def put(place, values):
        ref[:, place] = values

    return put


def adder(ref):
    def put(place, values):
        ref[:, place] += values

    return put


def inner_kernel(lay, mine, early, sums, lab_lane, lab_sub, rows, bias, back, buf_a, buf_b):
    is_home = lax.axis_index("cl") == lay.home
    infos = lines_of(lay, mine)
    buffers = (buf_a, buf_b)

    @pl.when(is_home)
    def _():
        copy_head(lay, mine, rows)
        first_labels(lay, infos, lab_sub)
        turn_labels(lay, lab_sub, lay.n_first, lab_lane, 0)
        back[...] = jnp.zeros(back.shape, jnp.float32)
        size = lay.n_early
        blocks = [(rows.at[pl.ds(start, size)], start) for start in range(0, lay.n_head, size)]
        blocks.append((early, lay.n_head))
        for i, (ref, at) in enumerate(blocks):
            tiles = [
                (ref_j, size, lab_sub, None, at_j, 2, None if at_j == at else back)
                for ref_j, at_j in blocks[i:]
            ]
            stream((ref, size, at), tiles, lab_lane, buffers, setter(sums))
        turn_sums(back, lay.n_first, sums, 0)

    @pl.when(jnp.logical_not(is_home))
    def _():
        write_labels(lay, infos, range(lay.n_owner), 0, lay.main, 0, lab_sub, bias)
        turn_labels(lay, lab_sub, lay.n_main, lab_lane, 0)
        tiles = [(mine, lay.n_main, lab_sub, bias, 0, 2, None)]
        stream((mine, lay.n_main, 0), tiles, lab_lane, buffers, setter(sums))


def half_blocks(ref_i, ref_j, lab_sub, line, back, at, lab_lane, buffers, put):
    half = ref_j.shape[0] // 2
    grp = lax.axis_index("grp")
    for h in range(2):
        start = pl.multiple_of((h ^ grp) * half, half)
        rows_j = ref_j.at[pl.ds(start, half)]
        sub = lab_sub.at[pl.ds(line + start, half)]
        backs = back.at[pl.ds(line + start, half)]
        lanes = (ref_i.at[pl.ds(h * half, half)], half, at + h * half)
        stream(lanes, [(rows_j, half, sub, None, 0, 1, backs)], lab_lane, buffers, put)


def cross_kernel(lay, mine, other, early, early_j, rows, sums, lab_lane, *refs):
    total, for_other, unfit_ref, late_sub, late_sub_j, long_lane, late_lane_j = refs[:7]
    lab_sub, bias, back, rows_j, buf_a, buf_b = refs[7:]
    is_home = lax.axis_index("cl") == lay.home
    infos = lines_of(lay, other)
    own = lines_of(lay, mine)
    hot = hot_of(lay, own[0])
    lane = lax.broadcasted_iota(jnp.int32, (1, LANES), 1)
    last = (lane < lay.n_fine) & (lax.rem(lane, lay.per_owner) == lay.per_owner - 1)
    last = last & (lax.div(lane, lay.per_owner) != hot)
    unfit = jnp.zeros((1, LANES), jnp.float32)
    for info in infos + own:
        wrong = last & (info >= lay.main)
        differs = (info != hot.astype(jnp.float32)) | (info >= lay.n_owner)
        wrong = wrong | ((lane == lay.n_fine) & differs)
        unfit = unfit + jnp.where(wrong, 1.0, 0.0)
    unfit_ref[0, 0] = jnp.max(unfit).astype(jnp.int32)
    total[...] = sums[...]
    buffers = (buf_a, buf_b)

    @pl.when(is_home)
    def _():
        copy_head(lay, other, rows_j)
        first_labels(lay, infos, lab_sub)
        back[...] = jnp.zeros(back.shape, jnp.float32)
        size = lay.n_early
        blocks_i = [rows.at[pl.ds(start, size)] for start in range(0, lay.n_head, size)] + [early]
        blocks_j = [rows_j.at[pl.ds(start, size)] for start in range(0, lay.n_head, size)]
        blocks_j.append(early_j)
        put, n = adder(total), len(blocks_i)
        for i, ref in enumerate(blocks_i):
            tiles = [
                (blocks_j[j], size, lab_sub, None, j * size, 2, back)
                for j in ((i + step) % n for step in range(1, (n + 1) // 2))
            ]
            stream((ref, size, i * size), tiles, lab_lane, buffers, put)
            half_blocks(
                ref, blocks_j[i], lab_sub, i * size, back, i * size, lab_lane, buffers, put
            )
        write_labels(lay, own, lay.late, lay.head, lay.rest, 0, late_sub, None)
        write_labels(lay, infos, lay.late, lay.head, lay.rest, 0, late_sub_j, None)
        long_lane[:, : lay.n_first] = lab_lane[...]
        turn_labels(lay, late_sub, lay.n_late, long_lane, lay.n_first)
        turn_labels(lay, late_sub_j, lay.n_late, late_lane_j, 0)
        for_other[...] = jnp.zeros(for_other.shape, jnp.float32)
        turn_sums(back, lay.n_first, for_other, 0)

    @pl.when(jnp.logical_not(is_home))
    def _():
        write_labels(lay, infos, range(lay.n_owner), 0, lay.main, 0, lab_sub, bias)
        tiles = [(other, lay.n_main, lab_sub, bias, 0, 2, None)]
        stream((mine, lay.n_main, 0), tiles, lab_lane, buffers, adder(total))


def first_tiles(lay, rows, early, lab_sub, back, size):
    return [
        (rows, lay.n_head, lab_sub, None, 0, lay.n_head // size, back),
        (early, lay.n_early, lab_sub, None, lay.n_head, lay.n_early // size, back),
    ]


def inner_late_kernel(lay, early, late, rows, lab_sub, late_sub, lab_lane, sums, *refs):
    back, buf_a, buf_b = refs

    @pl.when(lax.axis_index("cl") == lay.home)
    def _():
        back[...] = jnp.zeros(back.shape, jnp.float32)
        sums[:, : lay.n_first] = jnp.zeros((1, lay.n_first), jnp.float32)
        tiles = first_tiles(lay, rows, early, lab_sub, back, 512)
        tiles.append((late, lay.n_late, late_sub, None, 0, 1, None))
        lanes = (late, lay.n_late, lay.n_first)
        stream(lanes, tiles, lab_lane, (buf_a, buf_b), setter(sums))
        turn_sums(back, lay.n_first, sums, 0)


def cross_late_kernel(lay, early, late, late_j, rows, lab_sub, late_sub, lab_lane, *refs):
    late_lane, first_lane, first_sums, first_other, sums, out_ref = refs[:6]
    total, late_other, back, late_back, buf_a, buf_b = refs[6:]
    is_home = lax.axis_index("cl") == lay.home
    grp = lax.axis_index("grp")

    @pl.when(is_home)
    def _():
        total[...] = sums[...]
        total[:, : lay.n_first] += first_sums[...]
        back[...] = jnp.zeros(back.shape, jnp.float32)
        late_back[...] = jnp.zeros(late_back.shape, jnp.float32)
        buffers = (buf_a, buf_b)
        tiles = first_tiles(lay, rows, early, lab_sub, back, 128)
        stream((late_j, lay.n_late, 0), tiles, late_lane, buffers, setter(late_other))
        turn_sums(back, lay.n_first, total, 0)
        put = adder(total)
        half_blocks(late, late_j, late_sub, 0, late_back, lay.n_first, lab_lane, buffers, put)
        turn_sums(late_back, lay.n_late, late_other, 0)

        def write(line, values):
            for source in range(lay.n_owner):
                start = source * lay.head
                out_ref[2 * source + line, :, : lay.head] = values[:, start : start + lay.head]
            for i, source in enumerate(lay.early + lay.late):
                start = lay.n_head + i * lay.rest
                out_ref[2 * source + line, :, lay.head :] = values[:, start : start + lay.rest]

        write(grp, total[...])
        total[:, : lay.n_first] = first_other[...]
        total[:, lay.n_first :] = late_other[...]
        write(1 - grp, total[...])

    @pl.when(jnp.logical_not(is_home))
    def _():
        out_ref[...] = jnp.zeros(out_ref.shape, jnp.float32)
        values = jnp.where(first_lane[...] >= 0, first_sums[...], 1.0)
        for source in range(lay.n_owner):
            start = source * lay.main
            out_ref[2 * source + grp, :, : lay.main] = values[:, start : start + lay.main]


def pair_call(kernel, lay, arrays, out_shape, scratch, out_specs=None, pairs=0):
    width = arrays[0].shape[1]
    buffer = pltpu.VMEM((lay.n_main // 2, WIDE), jnp.float32)
    return pl.pallas_call(
        functools.partial(kernel, lay),
        out_shape=out_shape,
        in_specs=list(vmem_specs(len(arrays))),
        out_specs=out_specs or vmem_specs(len(out_shape)),
        scratch_shapes=list(scratch) + [buffer, buffer],
        compiler_params=pltpu.CompilerParams(vmem_limit_bytes=FAST_LIMIT),
        cost_estimate=pl.CostEstimate(
            flops=2 * pairs * width, bytes_accessed=1, transcendentals=pairs
        ),
    )(*arrays)


def fast_unpack_kernel(values_ref, pos_ref, out_ref):
    pos = pos_ref[...]
    lane = lax.rem(pos, LANES)
    line = lax.div(pos, LANES)
    out = jnp.ones(pos.shape, jnp.float32)
    per = values_ref.shape[2] // LANES
    for r in range(values_ref.shape[0] // 2 * per):
        owner, part = r // per, slice(r % per * LANES, (r % per + 1) * LANES)
        table = values_ref[2 * owner, :, part] + values_ref[2 * owner + 1, :, part]
        found = jnp.take_along_axis(jnp.broadcast_to(table, pos.shape), lane, axis=1)
        out = jnp.where(line == r, found, out)
    out_ref[...] = jnp.log(out)


def fast_unpack(values, pos):
    vmem = pl.BlockSpec(memory_space=pltpu.VMEM)
    return pl.pallas_call(
        fast_unpack_kernel,
        out_shape=jax.ShapeDtypeStruct(pos.shape, jnp.float32),
        in_specs=[vmem, vmem],
        out_specs=vmem,
    )(values, pos)


def general(embeddings, labels, owner_map):
    n_owner = lax.axis_size("cl")
    capacity = SLOTS // n_owner
    rows, width = embeddings.shape
    packed, pos, counts = pack(embeddings, labels, owner_map, n_owner, capacity)
    counts = lax.all_gather(counts, ("cl", "grp"), tiled=True)
    mine = lax.all_to_all(
        packed.reshape(n_owner, capacity, width), "cl", split_axis=0, concat_axis=0, tiled=True
    ).reshape(SLOTS, width)
    other = lax.ppermute(mine, "grp", [(0, 1), (1, 0)])
    results = log_counts(counts, mine, other, n_owner, capacity)
    returned = lax.all_to_all(
        results.reshape(n_owner, capacity), "cl", split_axis=0, concat_axis=0, tiled=True
    )
    return unpack(returned.reshape(SLOTS), pos).reshape(rows)


def body(embeddings, labels, owner_map):
    n_owner = lax.axis_size("cl")
    capacity = SLOTS // n_owner
    rows, width = embeddings.shape
    n_fine = owner_map.shape[0]
    main = -(-(rows // n_owner * 9 // 8) // 16) * 16
    if n_owner != 8 or main >= capacity or n_fine >= LANES:
        return general(embeddings, labels, owner_map)
    home = 2
    lay = Layout(n_owner, n_fine, capacity, main, home)
    packed, extra, pos = place_rows(embeddings, labels, owner_map, lay)

    def hop(x, pairs):
        return lax.ppermute(x, "cl", pairs)

    def swap(x):
        return lax.ppermute(x, "grp", [(0, 1), (1, 0)])

    both = lay_out([extra, hop(extra, [(6, 4), (7, 5)])])
    early = [extra if s == home else hop(extra, [(s, home)]) for s in lay.early]
    early = lay_out(early, home)
    mine = lax.all_to_all(
        packed.reshape(n_owner, main, width), "cl", split_axis=0, concat_axis=0, tiled=True
    ).reshape(n_owner * main, width)
    mine = after(mine, early, both)
    other, early_j = swap(mine), swap(early)
    late = [hop(both, [(s, home)]) for s in (5, 4)]

    def array(shape, dtype=jnp.float32):
        return jax.ShapeDtypeStruct(shape, dtype)

    def scratch(shape):
        return pltpu.VMEM(shape, jnp.float32)

    row, long_row = array((1, lay.n_first)), array((1, lay.n_all))
    bias = scratch((lay.n_main, LANES))
    heads = array((lay.n_head, width), jnp.bfloat16)
    late_lines, first_lines = array((lay.n_late, LANES)), array((lay.n_first, LANES))
    late_row = array((1, lay.n_late))
    late_side, first_side = scratch((lay.n_late, LANES)), scratch((lay.n_first, LANES))
    sums, first_lane, lab_sub, heads_i = pair_call(
        inner_kernel, lay, (mine, early), (row, row, first_lines, heads), (bias, first_side)
    )
    specs = vmem_specs(2) + (pl.BlockSpec(memory_space=pltpu.SMEM),) + vmem_specs(4)
    sums, first_other, unfit, late_sub, late_sub_j, lane, lane_j = pair_call(
        cross_kernel,
        lay,
        (mine, other, early, early_j, heads_i, sums, first_lane),
        (row, row, array((1, 1), jnp.int32), late_lines, late_lines, long_row, late_row),
        (first_side, bias, first_side, pltpu.VMEM(heads.shape, heads.dtype)),
        specs,
    )
    late = lay_out(late, home, (sums,))
    late_j = swap(late)
    (late_sums,) = pair_call(
        inner_late_kernel,
        lay,
        (early, late, heads_i, lab_sub, late_sub, lane),
        (long_row,),
        (first_side,),
        pairs=lay.n_late * lay.n_all,
    )
    (results,) = pair_call(
        cross_late_kernel,
        lay,
        (
            *(early, late, late_j, heads_i, lab_sub, late_sub_j, lane, lane_j),
            *(first_lane, sums, first_other, late_sums),
        ),
        (array((2 * n_owner, 1, capacity)),),
        (scratch(long_row.shape), scratch(late_row.shape), first_side, late_side),
    )
    returned = lax.all_to_all(
        results, ("cl", "grp"), split_axis=0, concat_axis=0, tiled=True
    )
    return lax.cond(
        unfit[0, 0] == 0,
        lambda: fast_unpack(returned, pos).reshape(rows),
        lambda: general(embeddings, labels, owner_map),
    )


def solution(mesh):
    return jax.shard_map(
        body,
        mesh=mesh,
        in_specs=(P(("parts", "cl", "grp"), None), P(("parts", "cl", "grp")), P("parts")),
        out_specs=P(("parts", "cl", "grp")),
        check_vma=False,
    )
```

```python
import functools
import math

import jax
import jax.numpy as jnp
from jax import lax
from jax.experimental import pallas as pl
from jax.experimental.pallas import tpu as pltpu
from jax.sharding import PartitionSpec as P

SLOTS = 2048

temper = 0.2
neighbour_factor = 0.5
epsilon = 1e-06

LANES = 128
SCALE = math.log2(math.e) / temper
NEIGHBOUR = math.log2(neighbour_factor)
DEAD = -1e30
VMEM_LIMIT = 48 * 1024 * 1024
FAST_LIMIT = 16 * 1024 * 1024
WIDE = 512
INFO = 16


def column_of(row):
    pieces = []
    for start in range(0, row.shape[1], LANES):
        width = min(LANES, row.shape[1] - start)
        shape = (width, width)
        diagonal = lax.broadcasted_iota(jnp.int32, shape, 0) == lax.broadcasted_iota(
            jnp.int32, shape, 1
        )
        piece = jnp.broadcast_to(row[:, start : start + width], shape)
        pieces.append(jnp.sum(jnp.where(diagonal, piece, 0.0), axis=1, keepdims=True))
    return jnp.concatenate(pieces, axis=0)


def row_of(column):
    n = column.shape[0]
    diagonal = lax.broadcasted_iota(jnp.int32, (n, n), 0) == lax.broadcasted_iota(
        jnp.int32, (n, n), 1
    )
    return jnp.sum(jnp.where(diagonal, column, 0.0), axis=0, keepdims=True)


def pack_kernel(n_owner, capacity, x_ref, lab_ref, map_ref, out_ref, pos_ref, cnt_ref, unit, pos_row):
    rows = x_ref.shape[0]
    n_fine = map_ref.shape[1]
    per_owner = n_fine // n_owner
    owner_row = map_ref[...].astype(jnp.float32)
    fine_row = lax.broadcasted_iota(jnp.int32, (1, n_fine), 1).astype(jnp.float32)
    key_row = owner_row * n_fine + fine_row
    key_col = column_of(key_row)
    sorted_col = jnp.sum(jnp.where(key_row < key_col, 1.0, 0.0), axis=1, keepdims=True)
    lab = lab_ref[...].astype(jnp.float32)
    lab_row = jnp.concatenate([lab[b : b + 1, :] for b in range(lab.shape[0])], axis=1)
    fine_col = lax.broadcasted_iota(jnp.int32, (n_fine, rows), 0).astype(jnp.float32)
    fine_id = jnp.sum(jnp.where(fine_col == lab_row, sorted_col, 0.0), axis=0, keepdims=True)
    counts_col = jnp.sum(jnp.where(fine_col == fine_id, 1.0, 0.0), axis=1, keepdims=True)
    cnt_ref[...] = row_of(counts_col).astype(jnp.int32)
    coarse = jnp.floor((fine_id + 0.5) * (1.0 / per_owner))
    before = jnp.sum(
        jnp.where(fine_col < coarse * per_owner, counts_col, 0.0), axis=0, keepdims=True
    )
    index = lax.broadcasted_iota(jnp.int32, (1, rows), 1).astype(jnp.float32)
    row_key = fine_id * rows + index
    rank = jnp.zeros((1, rows), jnp.float32)
    for start in range(0, rows, LANES):
        other = column_of(row_key[:, start : start + LANES])
        rank = rank + jnp.sum(jnp.where(other < row_key, 1.0, 0.0), axis=0, keepdims=True)
    pos = (coarse * capacity + rank - before).astype(jnp.int32)
    pos_row[...] = pos
    pos_ref[...] = jnp.concatenate(
        [pos[:, start : start + LANES] for start in range(0, rows, LANES)], axis=0
    )
    x = x_ref[...].astype(jnp.float32)
    squares = jnp.sum(x * x, axis=1, keepdims=True)
    unit[...] = (x * lax.rsqrt(squares + epsilon)).astype(jnp.bfloat16)

    step = 256

    @pl.loop(0, out_ref.shape[0] // step)
    def _(block):
        slot = lax.broadcasted_iota(jnp.int32, (step, rows), 0) + block * step
        chosen = jnp.where(slot == pos_row[...], 1.0, 0.0).astype(jnp.bfloat16)
        packed = jnp.dot(chosen, unit[...], preferred_element_type=jnp.float32)
        out_ref[pl.ds(pl.multiple_of(block * step, step), step), :] = packed.astype(jnp.bfloat16)


def pack(embeddings, labels, owner_map, n_owner, capacity):
    rows, width = embeddings.shape
    n_fine = owner_map.shape[0]
    total = n_owner * capacity
    vmem = pl.BlockSpec(memory_space=pltpu.VMEM)
    return pl.pallas_call(
        functools.partial(pack_kernel, n_owner, capacity),
        out_shape=(
            jax.ShapeDtypeStruct((total, width), jnp.bfloat16),
            jax.ShapeDtypeStruct((rows // LANES, LANES), jnp.int32),
            jax.ShapeDtypeStruct((1, n_fine), jnp.int32),
        ),
        in_specs=[vmem] * 3,
        out_specs=(vmem, vmem, vmem),
        scratch_shapes=[pltpu.VMEM((rows, width), jnp.bfloat16), pltpu.VMEM((1, rows), jnp.int32)],
        compiler_params=pltpu.CompilerParams(vmem_limit_bytes=VMEM_LIMIT),
    )(embeddings, labels.reshape(rows // LANES, LANES), owner_map.reshape(1, n_fine))


def counts_kernel(n_owner, capacity, cnt_ref, mine_ref, other_ref, out_ref, lab_lane, lab_sub, bias):
    total = mine_ref.shape[0]
    per_owner = cnt_ref.shape[1] // n_owner
    me = lax.axis_index("cl")
    grp = lax.axis_index("grp")
    n_grp = lax.axis_size("grp")
    for member in range(2):
        for source in range(n_owner):
            line = source * n_grp + lax.rem(grp + member, n_grp)
            edges = []
            edge = jnp.int32(0)
            for f in range(per_owner):
                edge = edge + cnt_ref[line, me * per_owner + f]
                edges.append(edge)
            down = lax.broadcasted_iota(jnp.int32, (capacity, LANES), 0)
            label = jnp.zeros((capacity, LANES), jnp.int32)
            for edge in edges:
                label = label + jnp.where(down >= edge, 1, 0)
            start = (member * n_owner + source) * capacity
            lab_sub[start : start + capacity, :] = label
            bias[start : start + capacity, :] = jnp.where(
                label < per_owner, NEIGHBOUR - SCALE, DEAD
            )
            if member == 0:
                across = lax.broadcasted_iota(jnp.int32, (1, capacity), 1)
                label = jnp.zeros((1, capacity), jnp.int32)
                for edge in edges:
                    label = label + jnp.where(across >= edge, 1, 0)
                lab_lane[:, source * capacity : (source + 1) * capacity] = jnp.where(
                    label < per_owner, label, -1
                )
    wide, deep = min(512, total), min(256, total)

    @pl.loop(0, total // wide)
    def _(block):
        columns = pl.ds(pl.multiple_of(block * wide, wide), wide)
        rows_i = mine_ref[columns, :]
        label_i = lab_lane[:, columns]

        def add(ref, offset):
            def step(j, acc):
                start = pl.multiple_of(j * deep, deep)
                scores = lax.dot_general(
                    ref[pl.ds(start, deep), :],
                    rows_i,
                    (((1,), (1,)), ((), ())),
                    preferred_element_type=jnp.float32,
                )
                place = pl.ds(pl.multiple_of(start + offset, deep), deep)
                label_j = lab_sub[place, :]
                bias_j = bias[place, :]
                repeat = wide // LANES
                label_j = jnp.concatenate([label_j] * repeat, axis=1)
                bias_j = jnp.concatenate([bias_j] * repeat, axis=1)
                shift = jnp.where(label_j == label_i, -SCALE, bias_j)
                terms = jnp.exp2(scores * SCALE + shift)
                return acc + jnp.sum(terms.reshape(deep // 8, 8, wide), axis=0)

            return step

        acc = jnp.zeros((8, wide), jnp.float32)
        acc = lax.fori_loop(0, total // deep, add(mine_ref, 0), acc, unroll=2)
        acc = lax.fori_loop(0, total // deep, add(other_ref, total), acc, unroll=2)
        totals = jnp.sum(acc, axis=0, keepdims=True)
        out_ref[:, columns] = jnp.log(jnp.where(label_i >= 0, totals, 1.0))


def log_counts(counts, mine, other, n_owner, capacity):
    total = mine.shape[0]
    vmem = pl.BlockSpec(memory_space=pltpu.VMEM)
    return pl.pallas_call(
        functools.partial(counts_kernel, n_owner, capacity),
        out_shape=jax.ShapeDtypeStruct((1, total), jnp.float32),
        in_specs=[pl.BlockSpec(memory_space=pltpu.SMEM), vmem, vmem],
        out_specs=vmem,
        scratch_shapes=[
            pltpu.VMEM((1, total), jnp.int32),
            pltpu.VMEM((2 * total, LANES), jnp.int32),
            pltpu.VMEM((2 * total, LANES), jnp.float32),
        ],
        compiler_params=pltpu.CompilerParams(vmem_limit_bytes=VMEM_LIMIT),
    )(counts, mine, other)


def unpack_kernel(values_ref, pos_ref, out_ref):
    pos = pos_ref[...]
    lane = lax.rem(pos, LANES)
    line = lax.div(pos, LANES)
    out = jnp.zeros(pos.shape, jnp.float32)
    for r in range(values_ref.shape[0]):
        table = jnp.broadcast_to(values_ref[r : r + 1, :], pos.shape)
        found = jnp.take_along_axis(table, lane, axis=1)
        out = jnp.where(line == r, found, out)
    out_ref[...] = out


def unpack(values, pos):
    vmem = pl.BlockSpec(memory_space=pltpu.VMEM)
    return pl.pallas_call(
        unpack_kernel,
        out_shape=jax.ShapeDtypeStruct(pos.shape, jnp.float32),
        in_specs=[vmem, vmem],
        out_specs=vmem,
    )(values.reshape(-1, LANES), pos)


def swapped(x, first, second):
    return jnp.where(x == first, second, jnp.where(x == second, first, x))


def place_kernel(lay, x_hbm, lab_hbm, map_hbm, *refs):
    main_hbm, tail_ref, pos_ref, x_ref, lab_ref, map_ref, unit, main_ref, sems = refs
    n_owner, capacity, main, home = lay.n_owner, lay.capacity, lay.main, lay.home
    copies = [
        pltpu.make_async_copy(src, dst, sems.at[i])
        for i, (src, dst) in enumerate(((x_hbm, x_ref), (lab_hbm, lab_ref), (map_hbm, map_ref)))
    ]
    for copy in copies:
        copy.start()
    rows, width = x_ref.shape
    n_fine = map_ref.shape[1]
    per_owner = n_fine // n_owner
    copies[1].wait()
    copies[2].wait()
    owner_row = map_ref[...].astype(jnp.float32)
    fine_row = lax.broadcasted_iota(jnp.int32, (1, n_fine), 1).astype(jnp.float32)
    key_row = owner_row * n_fine + fine_row
    key_col = column_of(key_row)
    sorted_col = jnp.sum(jnp.where(key_row < key_col, 1.0, 0.0), axis=1, keepdims=True)
    lab = lab_ref[...].astype(jnp.float32)
    lab_row = jnp.concatenate([lab[b : b + 1, :] for b in range(lab.shape[0])], axis=1)
    fine_col = lax.broadcasted_iota(jnp.int32, (n_fine, rows), 0).astype(jnp.float32)
    fine_id = jnp.sum(jnp.where(fine_col == lab_row, sorted_col, 0.0), axis=0, keepdims=True)
    counts_col = jnp.sum(jnp.where(fine_col == fine_id, 1.0, 0.0), axis=1, keepdims=True)
    coarse = jnp.floor((fine_id + 0.5) * (1.0 / per_owner))
    first = coarse * per_owner
    before = jnp.sum(jnp.where(fine_col < first, counts_col, 0.0), axis=0, keepdims=True)
    upto = jnp.sum(jnp.where(fine_col < first + per_owner, counts_col, 0.0), axis=0, keepdims=True)
    full = jnp.min(
        jnp.where(upto - before == capacity, coarse, float(n_owner)), axis=1, keepdims=True
    )
    line = lax.broadcasted_iota(jnp.int32, (n_fine, LANES), 0)
    lane = lax.broadcasted_iota(jnp.int32, (n_fine, LANES), 1)
    inside = (line <= lane) & (lax.div(line, per_owner) == lax.div(lane, per_owner))
    running = jnp.sum(jnp.where(inside, counts_col, 0.0), axis=0, keepdims=True)
    info = jnp.where(lane[:1] < n_fine, running, full)
    index = lax.broadcasted_iota(jnp.int32, (1, rows), 1).astype(jnp.float32)
    row_key = fine_id * rows + index
    rank = jnp.zeros((1, rows), jnp.float32)
    for start in range(0, rows, LANES):
        other = column_of(row_key[:, start : start + LANES])
        rank = rank + jnp.sum(jnp.where(other < row_key, 1.0, 0.0), axis=0, keepdims=True)
    rank = (rank - before).astype(jnp.int32)
    place = swapped(coarse.astype(jnp.int32), full.astype(jnp.int32), home)
    table = place * capacity + rank
    pos_ref[...] = jnp.concatenate(
        [table[:, start : start + LANES] for start in range(0, rows, LANES)], axis=0
    )
    fits = rank < jnp.where(place == home, lay.head, main - 1)
    slot = jnp.where(fits, place * main + rank, -1)
    tail_slot = jnp.where(place == home, rank - lay.head, -1)
    copies[0].wait()
    x = x_ref[...].astype(jnp.float32)
    squares = jnp.sum(x * x, axis=1, keepdims=True)
    unit[...] = (x * lax.rsqrt(squares + epsilon)).astype(jnp.bfloat16)

    def chosen_rows(slot, start, count):
        here = lax.broadcasted_iota(jnp.int32, (count, rows), 0) + start
        chosen = jnp.where(here == slot, 1.0, 0.0).astype(jnp.bfloat16)
        return jnp.dot(chosen, unit[...], preferred_element_type=jnp.float32)

    count = 2 * main
    down = lax.broadcasted_iota(jnp.int32, (count, LANES), 0)
    is_info = lax.rem(down, main) == main - 1
    writes = []
    for i, start in enumerate(range(0, lay.n_main, count)):
        packed = chosen_rows(slot, start, count)
        place = slice(start, start + count)
        main_ref[place, LANES:] = packed[:, LANES:].astype(jnp.bfloat16)
        main_ref[place, :LANES] = jnp.where(is_info, info, packed[:, :LANES]).astype(jnp.bfloat16)
        writes.append(
            pltpu.make_async_copy(
                main_ref.at[pl.ds(start, count)], main_hbm.at[pl.ds(start, count)], sems.at[3 + i]
            )
        )
        writes[-1].start()
    tail_ref[...] = chosen_rows(tail_slot, 0, lay.rest).astype(jnp.bfloat16)
    for write in writes:
        write.wait()


def vmem_specs(count):
    return (pl.BlockSpec(memory_space=pltpu.VMEM),) * count


def place_rows(embeddings, labels, owner_map, lay):
    rows, width = embeddings.shape
    n_fine = owner_map.shape[0]
    lab_shape = (rows // LANES, LANES)
    anywhere = pl.BlockSpec(memory_space=pl.ANY)
    return pl.pallas_call(
        functools.partial(place_kernel, lay),
        out_shape=(
            jax.ShapeDtypeStruct((lay.n_main, width), jnp.bfloat16),
            jax.ShapeDtypeStruct((lay.rest, width), jnp.bfloat16),
            jax.ShapeDtypeStruct(lab_shape, jnp.int32),
        ),
        in_specs=[anywhere] * 3,
        out_specs=(anywhere,) + vmem_specs(2),
        scratch_shapes=[
            pltpu.VMEM((rows, width), jnp.bfloat16),
            pltpu.VMEM(lab_shape, jnp.int32),
            pltpu.VMEM((1, n_fine), jnp.int32),
            pltpu.VMEM((rows, width), jnp.bfloat16),
            pltpu.VMEM((lay.n_main, width), jnp.bfloat16),
            pltpu.SemaphoreType.DMA((3 + lay.n_owner // 2,)),
        ],
        compiler_params=pltpu.CompilerParams(vmem_limit_bytes=FAST_LIMIT),
    )(embeddings, labels.reshape(lab_shape), owner_map.reshape(1, n_fine))


def gate_kernel(*refs):
    pass


def after(rows, *there):
    return pl.pallas_call(
        gate_kernel,
        out_shape=jax.ShapeDtypeStruct(rows.shape, rows.dtype),
        in_specs=list(vmem_specs(1 + len(there))),
        out_specs=vmem_specs(1)[0],
        input_output_aliases={0: 0},
        compiler_params=pltpu.CompilerParams(vmem_limit_bytes=FAST_LIMIT),
    )(rows, *there)


def lay_out_kernel(n_arrays, home, *refs):
    chunks, out = refs[:n_arrays], refs[-1]

    def copy():
        start = 0
        for chunk in chunks:
            out[start : start + chunk.shape[0], :] = chunk[...]
            start += chunk.shape[0]

    if home is None:
        copy()
    else:
        pl.when(lax.axis_index("cl") == home)(copy)


def lay_out(chunks, home=None, waits=()):
    rows, width = sum(x.shape[0] for x in chunks), chunks[0].shape[1]
    return pl.pallas_call(
        functools.partial(lay_out_kernel, len(chunks), home),
        out_shape=jax.ShapeDtypeStruct((rows, width), jnp.bfloat16),
        in_specs=list(vmem_specs(len(chunks) + len(waits))),
        out_specs=vmem_specs(1)[0],
        compiler_params=pltpu.CompilerParams(vmem_limit_bytes=FAST_LIMIT),
    )(*chunks, *waits)


class Layout:
    early, late = (0, 1, 2, 3), (5, 7, 4, 6)

    def __init__(self, n_owner, n_fine, capacity, main, home):
        self.n_owner, self.n_fine, self.capacity = n_owner, n_fine, capacity
        self.main, self.home = main, home
        self.head = main - INFO
        self.rest = capacity - self.head
        self.per_owner = n_fine // n_owner
        self.n_main = n_owner * main
        self.n_head = n_owner * self.head
        self.n_early = len(self.early) * self.rest
        self.n_late = len(self.late) * self.rest
        self.n_first = self.n_head + self.n_early
        self.n_all = self.n_first + self.n_late


def info_line(lay, main_ref, source):
    end = (source + 1) * lay.main
    return main_ref[end - INFO : end, :LANES].astype(jnp.float32)[INFO - 1 :]


def lines_of(lay, main_ref):
    return [info_line(lay, main_ref, source) for source in range(lay.n_owner)]


def hot_of(lay, info):
    lane = lax.broadcasted_iota(jnp.int32, (1, LANES), 1)
    hot = jnp.max(jnp.where(lane == lay.n_fine, info, 0.0), axis=1, keepdims=True)
    return hot.astype(jnp.int32)


def write_labels(lay, infos, sources, first, count, at, lab_sub, bias):
    cluster = swapped(lax.axis_index("cl"), hot_of(lay, infos[0]), lay.home)
    lane = lax.broadcasted_iota(jnp.int32, (1, LANES), 1)
    is_edge = lax.div(lane, lay.per_owner) == cluster
    for i, source in enumerate(sources):
        edges = jnp.where(is_edge, infos[source], 2.0 * lay.capacity)
        slot = lax.broadcasted_iota(jnp.int32, (count, LANES), 0) + first
        label = jnp.where(slot.astype(jnp.float32) >= edges, 1.0, 0.0)
        label = jnp.broadcast_to(jnp.sum(label, axis=1, keepdims=True), (count, LANES))
        start = at + i * count
        lab_sub[start : start + count, :] = label
        if bias is not None:
            bias[start : start + count, :] = jnp.where(
                label < lay.per_owner, NEIGHBOUR - SCALE, DEAD
            )


def first_labels(lay, infos, lab_sub):
    write_labels(lay, infos, range(lay.n_owner), 0, lay.head, 0, lab_sub, None)
    write_labels(lay, infos, lay.early, lay.head, lay.rest, lay.n_head, lab_sub, None)


def late_labels(lay, infos, lab_sub):
    write_labels(lay, infos, lay.late, lay.head, lay.rest, 0, lab_sub, None)


def turn_labels(lay, lab_sub, count, lab_lane, at):
    for i in range(0, count, LANES):
        block = jnp.transpose(lab_sub[i : i + LANES, :])[:1]
        lab_lane[:, at + i : at + i + LANES] = jnp.where(block < lay.per_owner, block, -1.0)


def copy_head(lay, main_ref, rows):
    for source in range(lay.n_owner):
        rows[source * lay.head : (source + 1) * lay.head, :] = main_ref[
            source * lay.main : source * lay.main + lay.head, :
        ]


def pieces(count, parts):
    return [(i * (count // parts), count // parts) for i in range(parts)]


def stream(lanes, tiles, lab_lane, buffers, put):
    rows_i, count, at = lanes
    step = 16
    tiles = [
        (ref, s, d, lab_sub, bias, line + s, back)
        for ref, n, lab_sub, bias, line, parts, back in tiles
        for s, d in pieces(n, parts)
    ]

    def scores_to(buffer, tile, rows):
        ref, start, deep = tile[:3]
        buffer[:deep, : rows.shape[0]] = lax.dot_general(
            ref[start : start + deep, :],
            rows,
            (((1,), (1,)), ((), ())),
            preferred_element_type=jnp.float32,
        )

    def run(start, blocks, wide):
        repeat = wide // LANES

        def rows_of(block):
            return rows_i[pl.ds(pl.multiple_of(start + block * wide, LANES), wide), :]

        scores_to(buffers[0], tiles[0], rows_of(0))

        def one_block(block):
            here = rows_of(block)
            place = pl.ds(pl.multiple_of(at + start + block * wide, LANES), wide)
            label_i = lab_lane[:, place]
            acc = jnp.zeros((8, wide), jnp.float32)
            for i, (_, _, deep, lab_sub, bias, line, back) in enumerate(tiles):
                if i + 1 < len(tiles):
                    scores_to(buffers[(i + 1) % 2], tiles[i + 1], here)
                elif blocks > 1:

                    @pl.when(block + 1 < blocks)
                    def _():
                        scores_to(buffers[0], tiles[0], rows_of(block + 1))

                buffer = buffers[i % 2]
                for c in range(0, deep, step):
                    part = slice(line + c, line + c + step)
                    label_j = jnp.concatenate([lab_sub[part, :]] * repeat, axis=1)
                    if bias is None:
                        bias_j = NEIGHBOUR - SCALE
                    else:
                        bias_j = jnp.concatenate([bias[part, :]] * repeat, axis=1)
                    shift = jnp.where(label_j == label_i, -SCALE, bias_j)
                    terms = jnp.exp2(buffer[c : c + step, :wide] * SCALE + shift)
                    acc = acc + jnp.sum(terms.reshape(step // 8, 8, wide), axis=0)
                    if back is not None:
                        across = terms[:, :LANES]
                        for r in range(1, repeat):
                            across = across + terms[:, r * LANES : (r + 1) * LANES]
                        back[part, :] += across
            put(place, jnp.sum(acc, axis=0, keepdims=True))

        if blocks == 1:
            one_block(0)
        else:
            pl.loop(0, blocks)(one_block)

    if count >= WIDE:
        run(0, count // WIDE, WIDE)
    if count % WIDE:
        run(count - count % WIDE, 1, count % WIDE)


def turn_sums(back, count, sums, at):
    for i in range(0, count, LANES):
        block = jnp.transpose(back[i : i + LANES, :])
        sums[:, at + i : at + i + LANES] += jnp.sum(block, axis=0, keepdims=True)


def setter(ref):
    def put(place, values):
        ref[:, place] = values

    return put


def adder(ref):
    def put(place, values):
        ref[:, place] += values

    return put


def inner_kernel(lay, mine, early, sums, lab_lane, lab_sub, rows, bias, back, buf_a, buf_b):
    is_home = lax.axis_index("cl") == lay.home
    infos = lines_of(lay, mine)
    buffers = (buf_a, buf_b)

    @pl.when(is_home)
    def _():
        copy_head(lay, mine, rows)
        first_labels(lay, infos, lab_sub)
        turn_labels(lay, lab_sub, lay.n_first, lab_lane, 0)
        back[...] = jnp.zeros(back.shape, jnp.float32)
        size = lay.n_early
        blocks = [(rows.at[pl.ds(start, size)], start) for start in range(0, lay.n_head, size)]
        blocks.append((early, lay.n_head))
        for i, (ref, at) in enumerate(blocks):
            tiles = [
                (ref_j, size, lab_sub, None, at_j, 2, None if at_j == at else back)
                for ref_j, at_j in blocks[i:]
            ]
            stream((ref, size, at), tiles, lab_lane, buffers, setter(sums))
        turn_sums(back, lay.n_first, sums, 0)

    @pl.when(jnp.logical_not(is_home))
    def _():
        write_labels(lay, infos, range(lay.n_owner), 0, lay.main, 0, lab_sub, bias)
        turn_labels(lay, lab_sub, lay.n_main, lab_lane, 0)
        tiles = [(mine, lay.n_main, lab_sub, bias, 0, 2, None)]
        stream((mine, lay.n_main, 0), tiles, lab_lane, buffers, setter(sums))


def half_blocks(ref_i, ref_j, lab_sub, line, back, at, lab_lane, buffers, put):
    half = ref_j.shape[0] // 2
    grp = lax.axis_index("grp")
    for h in range(2):
        start = pl.multiple_of((h ^ grp) * half, half)
        rows_j = ref_j.at[pl.ds(start, half)]
        sub = lab_sub.at[pl.ds(line + start, half)]
        backs = back.at[pl.ds(line + start, half)]
        lanes = (ref_i.at[pl.ds(h * half, half)], half, at + h * half)
        stream(lanes, [(rows_j, half, sub, None, 0, 1, backs)], lab_lane, buffers, put)


def cross_kernel(lay, mine, other, early, early_j, rows, sums, lab_lane, *refs):
    total, for_other, unfit_ref, late_sub, late_sub_j, long_lane, late_lane_j = refs[:7]
    lab_sub, bias, back, rows_j, buf_a, buf_b = refs[7:]
    is_home = lax.axis_index("cl") == lay.home
    infos = lines_of(lay, other)
    own = lines_of(lay, mine)
    hot = hot_of(lay, own[0])
    lane = lax.broadcasted_iota(jnp.int32, (1, LANES), 1)
    last = (lane < lay.n_fine) & (lax.rem(lane, lay.per_owner) == lay.per_owner - 1)
    last = last & (lax.div(lane, lay.per_owner) != hot)
    unfit = jnp.zeros((1, LANES), jnp.float32)
    for info in infos + own:
        wrong = last & (info >= lay.main)
        differs = (info != hot.astype(jnp.float32)) | (info >= lay.n_owner)
        wrong = wrong | ((lane == lay.n_fine) & differs)
        unfit = unfit + jnp.where(wrong, 1.0, 0.0)
    unfit_ref[0, 0] = jnp.max(unfit).astype(jnp.int32)
    total[...] = sums[...]
    buffers = (buf_a, buf_b)

    @pl.when(is_home)
    def _():
        copy_head(lay, other, rows_j)
        first_labels(lay, infos, lab_sub)
        back[...] = jnp.zeros(back.shape, jnp.float32)
        size = lay.n_early
        blocks_i = [rows.at[pl.ds(start, size)] for start in range(0, lay.n_head, size)] + [early]
        blocks_j = [rows_j.at[pl.ds(start, size)] for start in range(0, lay.n_head, size)]
        blocks_j.append(early_j)
        put, n = adder(total), len(blocks_i)
        for i, ref in enumerate(blocks_i):
            tiles = [
                (blocks_j[j], size, lab_sub, None, j * size, 2, back)
                for j in ((i + step) % n for step in range(1, (n + 1) // 2))
            ]
            stream((ref, size, i * size), tiles, lab_lane, buffers, put)
            half_blocks(
                ref, blocks_j[i], lab_sub, i * size, back, i * size, lab_lane, buffers, put
            )
        write_labels(lay, own, lay.late, lay.head, lay.rest, 0, late_sub, None)
        write_labels(lay, infos, lay.late, lay.head, lay.rest, 0, late_sub_j, None)
        long_lane[:, : lay.n_first] = lab_lane[...]
        turn_labels(lay, late_sub, lay.n_late, long_lane, lay.n_first)
        turn_labels(lay, late_sub_j, lay.n_late, late_lane_j, 0)
        for_other[...] = jnp.zeros(for_other.shape, jnp.float32)
        turn_sums(back, lay.n_first, for_other, 0)

    @pl.when(jnp.logical_not(is_home))
    def _():
        write_labels(lay, infos, range(lay.n_owner), 0, lay.main, 0, lab_sub, bias)
        tiles = [(other, lay.n_main, lab_sub, bias, 0, 2, None)]
        stream((mine, lay.n_main, 0), tiles, lab_lane, buffers, adder(total))


def first_tiles(lay, rows, early, lab_sub, back, size):
    return [
        (rows, lay.n_head, lab_sub, None, 0, lay.n_head // size, back),
        (early, lay.n_early, lab_sub, None, lay.n_head, lay.n_early // size, back),
    ]


def inner_late_kernel(lay, early, late, rows, lab_sub, late_sub, lab_lane, sums, *refs):
    back, buf_a, buf_b = refs

    @pl.when(lax.axis_index("cl") == lay.home)
    def _():
        back[...] = jnp.zeros(back.shape, jnp.float32)
        sums[:, : lay.n_first] = jnp.zeros((1, lay.n_first), jnp.float32)
        tiles = first_tiles(lay, rows, early, lab_sub, back, 512)
        tiles.append((late, lay.n_late, late_sub, None, 0, 1, None))
        lanes = (late, lay.n_late, lay.n_first)
        stream(lanes, tiles, lab_lane, (buf_a, buf_b), setter(sums))
        turn_sums(back, lay.n_first, sums, 0)


def cross_late_kernel(lay, early, late, late_j, rows, lab_sub, late_sub, lab_lane, *refs):
    late_lane, first_lane, first_sums, first_other, sums, out_ref = refs[:6]
    total, late_other, back, late_back, buf_a, buf_b = refs[6:]
    is_home = lax.axis_index("cl") == lay.home
    grp = lax.axis_index("grp")

    @pl.when(is_home)
    def _():
        total[...] = sums[...]
        total[:, : lay.n_first] += first_sums[...]
        back[...] = jnp.zeros(back.shape, jnp.float32)
        late_back[...] = jnp.zeros(late_back.shape, jnp.float32)
        buffers = (buf_a, buf_b)
        tiles = first_tiles(lay, rows, early, lab_sub, back, 512)
        stream((late_j, lay.n_late, 0), tiles, late_lane, buffers, setter(late_other))
        turn_sums(back, lay.n_first, total, 0)
        put = adder(total)
        half_blocks(late, late_j, late_sub, 0, late_back, lay.n_first, lab_lane, buffers, put)
        turn_sums(late_back, lay.n_late, late_other, 0)

        def write(line, values):
            for source in range(lay.n_owner):
                start = source * lay.head
                out_ref[2 * source + line, :, : lay.head] = values[:, start : start + lay.head]
            for i, source in enumerate(lay.early + lay.late):
                start = lay.n_head + i * lay.rest
                out_ref[2 * source + line, :, lay.head :] = values[:, start : start + lay.rest]

        write(grp, total[...])
        total[:, : lay.n_first] = first_other[...]
        total[:, lay.n_first :] = late_other[...]
        write(1 - grp, total[...])

    @pl.when(jnp.logical_not(is_home))
    def _():
        out_ref[...] = jnp.zeros(out_ref.shape, jnp.float32)
        values = jnp.where(first_lane[...] >= 0, first_sums[...], 1.0)
        for source in range(lay.n_owner):
            start = source * lay.main
            out_ref[2 * source + grp, :, : lay.main] = values[:, start : start + lay.main]


def pair_call(kernel, lay, arrays, out_shape, scratch, out_specs=None, pairs=0):
    width = arrays[0].shape[1]
    buffer = pltpu.VMEM((lay.n_main // 2, WIDE), jnp.float32)
    return pl.pallas_call(
        functools.partial(kernel, lay),
        out_shape=out_shape,
        in_specs=list(vmem_specs(len(arrays))),
        out_specs=out_specs or vmem_specs(len(out_shape)),
        scratch_shapes=list(scratch) + [buffer, buffer],
        compiler_params=pltpu.CompilerParams(vmem_limit_bytes=FAST_LIMIT),
        cost_estimate=pl.CostEstimate(
            flops=2 * pairs * width, bytes_accessed=1, transcendentals=pairs
        ),
    )(*arrays)


def fast_unpack_kernel(values_ref, pos_ref, out_ref):
    pos = pos_ref[...]
    lane = lax.rem(pos, LANES)
    line = lax.div(pos, LANES)
    out = jnp.ones(pos.shape, jnp.float32)
    per = values_ref.shape[2] // LANES
    for r in range(values_ref.shape[0] // 2 * per):
        owner, part = r // per, slice(r % per * LANES, (r % per + 1) * LANES)
        table = values_ref[2 * owner, :, part] + values_ref[2 * owner + 1, :, part]
        found = jnp.take_along_axis(jnp.broadcast_to(table, pos.shape), lane, axis=1)
        out = jnp.where(line == r, found, out)
    out_ref[...] = jnp.log(out)


def fast_unpack(values, pos):
    vmem = pl.BlockSpec(memory_space=pltpu.VMEM)
    return pl.pallas_call(
        fast_unpack_kernel,
        out_shape=jax.ShapeDtypeStruct(pos.shape, jnp.float32),
        in_specs=[vmem, vmem],
        out_specs=vmem,
    )(values, pos)


def general(embeddings, labels, owner_map):
    n_owner = lax.axis_size("cl")
    capacity = SLOTS // n_owner
    rows, width = embeddings.shape
    packed, pos, counts = pack(embeddings, labels, owner_map, n_owner, capacity)
    counts = lax.all_gather(counts, ("cl", "grp"), tiled=True)
    mine = lax.all_to_all(
        packed.reshape(n_owner, capacity, width), "cl", split_axis=0, concat_axis=0, tiled=True
    ).reshape(SLOTS, width)
    other = lax.ppermute(mine, "grp", [(0, 1), (1, 0)])
    results = log_counts(counts, mine, other, n_owner, capacity)
    returned = lax.all_to_all(
        results.reshape(n_owner, capacity), "cl", split_axis=0, concat_axis=0, tiled=True
    )
    return unpack(returned.reshape(SLOTS), pos).reshape(rows)


def body(embeddings, labels, owner_map):
    n_owner = lax.axis_size("cl")
    capacity = SLOTS // n_owner
    rows, width = embeddings.shape
    n_fine = owner_map.shape[0]
    main = -(-(rows // n_owner * 9 // 8) // 16) * 16
    if n_owner != 8 or main >= capacity or n_fine >= LANES:
        return general(embeddings, labels, owner_map)
    home = 2
    lay = Layout(n_owner, n_fine, capacity, main, home)
    packed, extra, pos = place_rows(embeddings, labels, owner_map, lay)

    def hop(x, pairs):
        return lax.ppermute(x, "cl", pairs)

    def swap(x):
        return lax.ppermute(x, "grp", [(0, 1), (1, 0)])

    both = lay_out([extra, hop(extra, [(6, 4), (7, 5)])])
    early = [extra if s == home else hop(extra, [(s, home)]) for s in lay.early]
    early = lay_out(early, home)
    mine = lax.all_to_all(
        packed.reshape(n_owner, main, width), "cl", split_axis=0, concat_axis=0, tiled=True
    ).reshape(n_owner * main, width)
    mine = after(mine, early, both)
    other, early_j = swap(mine), swap(early)
    late = [hop(both, [(s, home)]) for s in (5, 4)]

    def array(shape, dtype=jnp.float32):
        return jax.ShapeDtypeStruct(shape, dtype)

    def scratch(shape):
        return pltpu.VMEM(shape, jnp.float32)

    row, long_row = array((1, lay.n_first)), array((1, lay.n_all))
    bias = scratch((lay.n_main, LANES))
    heads = array((lay.n_head, width), jnp.bfloat16)
    late_lines, first_lines = array((lay.n_late, LANES)), array((lay.n_first, LANES))
    late_row = array((1, lay.n_late))
    late_side, first_side = scratch((lay.n_late, LANES)), scratch((lay.n_first, LANES))
    sums, first_lane, lab_sub, heads_i = pair_call(
        inner_kernel, lay, (mine, early), (row, row, first_lines, heads), (bias, first_side)
    )
    specs = vmem_specs(2) + (pl.BlockSpec(memory_space=pltpu.SMEM),) + vmem_specs(4)
    sums, first_other, unfit, late_sub, late_sub_j, lane, lane_j = pair_call(
        cross_kernel,
        lay,
        (mine, other, early, early_j, heads_i, sums, first_lane),
        (row, row, array((1, 1), jnp.int32), late_lines, late_lines, long_row, late_row),
        (first_side, bias, first_side, pltpu.VMEM(heads.shape, heads.dtype)),
        specs,
    )
    late = lay_out(late, home, (sums,))
    late_j = swap(late)
    (late_sums,) = pair_call(
        inner_late_kernel,
        lay,
        (early, late, heads_i, lab_sub, late_sub, lane),
        (long_row,),
        (first_side,),
        pairs=lay.n_late * lay.n_all,
    )
    (results,) = pair_call(
        cross_late_kernel,
        lay,
        (
            *(early, late, late_j, heads_i, lab_sub, late_sub_j, lane, lane_j),
            *(first_lane, sums, first_other, late_sums),
        ),
        (array((2 * n_owner, 1, capacity)),),
        (scratch(long_row.shape), scratch(late_row.shape), first_side, late_side),
    )
    returned = lax.all_to_all(
        results, ("cl", "grp"), split_axis=0, concat_axis=0, tiled=True
    )
    return lax.cond(
        unfit[0, 0] == 0,
        lambda: fast_unpack(returned, pos).reshape(rows),
        lambda: general(embeddings, labels, owner_map),
    )


def solution(mesh):
    return jax.shard_map(
        body,
        mesh=mesh,
        in_specs=(P(("parts", "cl", "grp"), None), P(("parts", "cl", "grp")), P("parts")),
        out_specs=P(("parts", "cl", "grp")),
        check_vma=False,
    )
```

```python
import functools
import math

import jax
import jax.numpy as jnp
from jax import lax
from jax.experimental import pallas as pl
from jax.experimental.pallas import tpu as pltpu
from jax.sharding import PartitionSpec as P

SLOTS = 2048

temper = 0.2
neighbour_factor = 0.5
epsilon = 1e-06

LANES = 128
SCALE = math.log2(math.e) / temper
NEIGHBOUR = math.log2(neighbour_factor)
DEAD = -1e30
VMEM_LIMIT = 48 * 1024 * 1024
FAST_LIMIT = 16 * 1024 * 1024
WIDE = 512
INFO = 16


def column_of(row):
    pieces = []
    for start in range(0, row.shape[1], LANES):
        width = min(LANES, row.shape[1] - start)
        shape = (width, width)
        diagonal = lax.broadcasted_iota(jnp.int32, shape, 0) == lax.broadcasted_iota(
            jnp.int32, shape, 1
        )
        piece = jnp.broadcast_to(row[:, start : start + width], shape)
        pieces.append(jnp.sum(jnp.where(diagonal, piece, 0.0), axis=1, keepdims=True))
    return jnp.concatenate(pieces, axis=0)


def row_of(column):
    n = column.shape[0]
    diagonal = lax.broadcasted_iota(jnp.int32, (n, n), 0) == lax.broadcasted_iota(
        jnp.int32, (n, n), 1
    )
    return jnp.sum(jnp.where(diagonal, column, 0.0), axis=0, keepdims=True)


def pack_kernel(n_owner, capacity, x_ref, lab_ref, map_ref, out_ref, pos_ref, cnt_ref, unit, pos_row):
    rows = x_ref.shape[0]
    n_fine = map_ref.shape[1]
    per_owner = n_fine // n_owner
    owner_row = map_ref[...].astype(jnp.float32)
    fine_row = lax.broadcasted_iota(jnp.int32, (1, n_fine), 1).astype(jnp.float32)
    key_row = owner_row * n_fine + fine_row
    key_col = column_of(key_row)
    sorted_col = jnp.sum(jnp.where(key_row < key_col, 1.0, 0.0), axis=1, keepdims=True)
    lab = lab_ref[...].astype(jnp.float32)
    lab_row = jnp.concatenate([lab[b : b + 1, :] for b in range(lab.shape[0])], axis=1)
    fine_col = lax.broadcasted_iota(jnp.int32, (n_fine, rows), 0).astype(jnp.float32)
    fine_id = jnp.sum(jnp.where(fine_col == lab_row, sorted_col, 0.0), axis=0, keepdims=True)
    counts_col = jnp.sum(jnp.where(fine_col == fine_id, 1.0, 0.0), axis=1, keepdims=True)
    cnt_ref[...] = row_of(counts_col).astype(jnp.int32)
    coarse = jnp.floor((fine_id + 0.5) * (1.0 / per_owner))
    before = jnp.sum(
        jnp.where(fine_col < coarse * per_owner, counts_col, 0.0), axis=0, keepdims=True
    )
    index = lax.broadcasted_iota(jnp.int32, (1, rows), 1).astype(jnp.float32)
    row_key = fine_id * rows + index
    rank = jnp.zeros((1, rows), jnp.float32)
    for start in range(0, rows, LANES):
        other = column_of(row_key[:, start : start + LANES])
        rank = rank + jnp.sum(jnp.where(other < row_key, 1.0, 0.0), axis=0, keepdims=True)
    pos = (coarse * capacity + rank - before).astype(jnp.int32)
    pos_row[...] = pos
    pos_ref[...] = jnp.concatenate(
        [pos[:, start : start + LANES] for start in range(0, rows, LANES)], axis=0
    )
    x = x_ref[...].astype(jnp.float32)
    squares = jnp.sum(x * x, axis=1, keepdims=True)
    unit[...] = (x * lax.rsqrt(squares + epsilon)).astype(jnp.bfloat16)

    step = 256

    @pl.loop(0, out_ref.shape[0] // step)
    def _(block):
        slot = lax.broadcasted_iota(jnp.int32, (step, rows), 0) + block * step
        chosen = jnp.where(slot == pos_row[...], 1.0, 0.0).astype(jnp.bfloat16)
        packed = jnp.dot(chosen, unit[...], preferred_element_type=jnp.float32)
        out_ref[pl.ds(pl.multiple_of(block * step, step), step), :] = packed.astype(jnp.bfloat16)


def pack(embeddings, labels, owner_map, n_owner, capacity):
    rows, width = embeddings.shape
    n_fine = owner_map.shape[0]
    total = n_owner * capacity
    vmem = pl.BlockSpec(memory_space=pltpu.VMEM)
    return pl.pallas_call(
        functools.partial(pack_kernel, n_owner, capacity),
        out_shape=(
            jax.ShapeDtypeStruct((total, width), jnp.bfloat16),
            jax.ShapeDtypeStruct((rows // LANES, LANES), jnp.int32),
            jax.ShapeDtypeStruct((1, n_fine), jnp.int32),
        ),
        in_specs=[vmem] * 3,
        out_specs=(vmem, vmem, vmem),
        scratch_shapes=[pltpu.VMEM((rows, width), jnp.bfloat16), pltpu.VMEM((1, rows), jnp.int32)],
        compiler_params=pltpu.CompilerParams(vmem_limit_bytes=VMEM_LIMIT),
    )(embeddings, labels.reshape(rows // LANES, LANES), owner_map.reshape(1, n_fine))


def counts_kernel(n_owner, capacity, cnt_ref, mine_ref, other_ref, out_ref, lab_lane, lab_sub, bias):
    total = mine_ref.shape[0]
    per_owner = cnt_ref.shape[1] // n_owner
    me = lax.axis_index("cl")
    grp = lax.axis_index("grp")
    n_grp = lax.axis_size("grp")
    for member in range(2):
        for source in range(n_owner):
            line = source * n_grp + lax.rem(grp + member, n_grp)
            edges = []
            edge = jnp.int32(0)
            for f in range(per_owner):
                edge = edge + cnt_ref[line, me * per_owner + f]
                edges.append(edge)
            down = lax.broadcasted_iota(jnp.int32, (capacity, LANES), 0)
            label = jnp.zeros((capacity, LANES), jnp.int32)
            for edge in edges:
                label = label + jnp.where(down >= edge, 1, 0)
            start = (member * n_owner + source) * capacity
            lab_sub[start : start + capacity, :] = label
            bias[start : start + capacity, :] = jnp.where(
                label < per_owner, NEIGHBOUR - SCALE, DEAD
            )
            if member == 0:
                across = lax.broadcasted_iota(jnp.int32, (1, capacity), 1)
                label = jnp.zeros((1, capacity), jnp.int32)
                for edge in edges:
                    label = label + jnp.where(across >= edge, 1, 0)
                lab_lane[:, source * capacity : (source + 1) * capacity] = jnp.where(
                    label < per_owner, label, -1
                )
    wide, deep = min(512, total), min(256, total)

    @pl.loop(0, total // wide)
    def _(block):
        columns = pl.ds(pl.multiple_of(block * wide, wide), wide)
        rows_i = mine_ref[columns, :]
        label_i = lab_lane[:, columns]

        def add(ref, offset):
            def step(j, acc):
                start = pl.multiple_of(j * deep, deep)
                scores = lax.dot_general(
                    ref[pl.ds(start, deep), :],
                    rows_i,
                    (((1,), (1,)), ((), ())),
                    preferred_element_type=jnp.float32,
                )
                place = pl.ds(pl.multiple_of(start + offset, deep), deep)
                label_j = lab_sub[place, :]
                bias_j = bias[place, :]
                repeat = wide // LANES
                label_j = jnp.concatenate([label_j] * repeat, axis=1)
                bias_j = jnp.concatenate([bias_j] * repeat, axis=1)
                shift = jnp.where(label_j == label_i, -SCALE, bias_j)
                terms = jnp.exp2(scores * SCALE + shift)
                return acc + jnp.sum(terms.reshape(deep // 8, 8, wide), axis=0)

            return step

        acc = jnp.zeros((8, wide), jnp.float32)
        acc = lax.fori_loop(0, total // deep, add(mine_ref, 0), acc, unroll=2)
        acc = lax.fori_loop(0, total // deep, add(other_ref, total), acc, unroll=2)
        totals = jnp.sum(acc, axis=0, keepdims=True)
        out_ref[:, columns] = jnp.log(jnp.where(label_i >= 0, totals, 1.0))


def log_counts(counts, mine, other, n_owner, capacity):
    total = mine.shape[0]
    vmem = pl.BlockSpec(memory_space=pltpu.VMEM)
    return pl.pallas_call(
        functools.partial(counts_kernel, n_owner, capacity),
        out_shape=jax.ShapeDtypeStruct((1, total), jnp.float32),
        in_specs=[pl.BlockSpec(memory_space=pltpu.SMEM), vmem, vmem],
        out_specs=vmem,
        scratch_shapes=[
            pltpu.VMEM((1, total), jnp.int32),
            pltpu.VMEM((2 * total, LANES), jnp.int32),
            pltpu.VMEM((2 * total, LANES), jnp.float32),
        ],
        compiler_params=pltpu.CompilerParams(vmem_limit_bytes=VMEM_LIMIT),
    )(counts, mine, other)


def unpack_kernel(values_ref, pos_ref, out_ref):
    pos = pos_ref[...]
    lane = lax.rem(pos, LANES)
    line = lax.div(pos, LANES)
    out = jnp.zeros(pos.shape, jnp.float32)
    for r in range(values_ref.shape[0]):
        table = jnp.broadcast_to(values_ref[r : r + 1, :], pos.shape)
        found = jnp.take_along_axis(table, lane, axis=1)
        out = jnp.where(line == r, found, out)
    out_ref[...] = out


def unpack(values, pos):
    vmem = pl.BlockSpec(memory_space=pltpu.VMEM)
    return pl.pallas_call(
        unpack_kernel,
        out_shape=jax.ShapeDtypeStruct(pos.shape, jnp.float32),
        in_specs=[vmem, vmem],
        out_specs=vmem,
    )(values.reshape(-1, LANES), pos)


def swapped(x, first, second):
    return jnp.where(x == first, second, jnp.where(x == second, first, x))


def place_kernel(lay, x_hbm, lab_hbm, map_hbm, *refs):
    main_hbm, tail_ref, pos_ref, x_ref, lab_ref, map_ref, unit, main_ref, sems = refs
    n_owner, capacity, main, home = lay.n_owner, lay.capacity, lay.main, lay.home
    copies = [
        pltpu.make_async_copy(src, dst, sems.at[i])
        for i, (src, dst) in enumerate(((x_hbm, x_ref), (lab_hbm, lab_ref), (map_hbm, map_ref)))
    ]
    for copy in copies:
        copy.start()
    rows, width = x_ref.shape
    n_fine = map_ref.shape[1]
    per_owner = n_fine // n_owner
    copies[1].wait()
    copies[2].wait()
    owner_row = map_ref[...].astype(jnp.float32)
    fine_row = lax.broadcasted_iota(jnp.int32, (1, n_fine), 1).astype(jnp.float32)
    key_row = owner_row * n_fine + fine_row
    key_col = column_of(key_row)
    sorted_col = jnp.sum(jnp.where(key_row < key_col, 1.0, 0.0), axis=1, keepdims=True)
    lab = lab_ref[...].astype(jnp.float32)
    lab_row = jnp.concatenate([lab[b : b + 1, :] for b in range(lab.shape[0])], axis=1)
    fine_col = lax.broadcasted_iota(jnp.int32, (n_fine, rows), 0).astype(jnp.float32)
    fine_id = jnp.sum(jnp.where(fine_col == lab_row, sorted_col, 0.0), axis=0, keepdims=True)
    counts_col = jnp.sum(jnp.where(fine_col == fine_id, 1.0, 0.0), axis=1, keepdims=True)
    coarse = jnp.floor((fine_id + 0.5) * (1.0 / per_owner))
    first = coarse * per_owner
    before = jnp.sum(jnp.where(fine_col < first, counts_col, 0.0), axis=0, keepdims=True)
    upto = jnp.sum(jnp.where(fine_col < first + per_owner, counts_col, 0.0), axis=0, keepdims=True)
    full = jnp.min(
        jnp.where(upto - before == capacity, coarse, float(n_owner)), axis=1, keepdims=True
    )
    line = lax.broadcasted_iota(jnp.int32, (n_fine, LANES), 0)
    lane = lax.broadcasted_iota(jnp.int32, (n_fine, LANES), 1)
    inside = (line <= lane) & (lax.div(line, per_owner) == lax.div(lane, per_owner))
    running = jnp.sum(jnp.where(inside, counts_col, 0.0), axis=0, keepdims=True)
    info = jnp.where(lane[:1] < n_fine, running, full)
    index = lax.broadcasted_iota(jnp.int32, (1, rows), 1).astype(jnp.float32)
    row_key = fine_id * rows + index
    rank = jnp.zeros((1, rows), jnp.float32)
    for start in range(0, rows, LANES):
        other = column_of(row_key[:, start : start + LANES])
        rank = rank + jnp.sum(jnp.where(other < row_key, 1.0, 0.0), axis=0, keepdims=True)
    rank = (rank - before).astype(jnp.int32)
    place = swapped(coarse.astype(jnp.int32), full.astype(jnp.int32), home)
    table = place * capacity + rank
    pos_ref[...] = jnp.concatenate(
        [table[:, start : start + LANES] for start in range(0, rows, LANES)], axis=0
    )
    fits = rank < jnp.where(place == home, lay.head, main - 1)
    slot = jnp.where(fits, place * main + rank, -1)
    tail_slot = jnp.where(place == home, rank - lay.head, -1)
    copies[0].wait()
    x = x_ref[...].astype(jnp.float32)
    squares = jnp.sum(x * x, axis=1, keepdims=True)
    unit[...] = (x * lax.rsqrt(squares + epsilon)).astype(jnp.bfloat16)

    def chosen_rows(slot, start, count):
        here = lax.broadcasted_iota(jnp.int32, (count, rows), 0) + start
        chosen = jnp.where(here == slot, 1.0, 0.0).astype(jnp.bfloat16)
        return jnp.dot(chosen, unit[...], preferred_element_type=jnp.float32)

    count = 2 * main
    down = lax.broadcasted_iota(jnp.int32, (count, LANES), 0)
    is_info = lax.rem(down, main) == main - 1
    writes = []
    for i, start in enumerate(range(0, lay.n_main, count)):
        packed = chosen_rows(slot, start, count)
        place = slice(start, start + count)
        main_ref[place, LANES:] = packed[:, LANES:].astype(jnp.bfloat16)
        main_ref[place, :LANES] = jnp.where(is_info, info, packed[:, :LANES]).astype(jnp.bfloat16)
        writes.append(
            pltpu.make_async_copy(
                main_ref.at[pl.ds(start, count)], main_hbm.at[pl.ds(start, count)], sems.at[3 + i]
            )
        )
        writes[-1].start()
    tail_ref[...] = chosen_rows(tail_slot, 0, lay.rest).astype(jnp.bfloat16)
    for write in writes:
        write.wait()


def vmem_specs(count):
    return (pl.BlockSpec(memory_space=pltpu.VMEM),) * count


def place_rows(embeddings, labels, owner_map, lay):
    rows, width = embeddings.shape
    n_fine = owner_map.shape[0]
    lab_shape = (rows // LANES, LANES)
    anywhere = pl.BlockSpec(memory_space=pl.ANY)
    return pl.pallas_call(
        functools.partial(place_kernel, lay),
        out_shape=(
            jax.ShapeDtypeStruct((lay.n_main, width), jnp.bfloat16),
            jax.ShapeDtypeStruct((lay.rest, width), jnp.bfloat16),
            jax.ShapeDtypeStruct(lab_shape, jnp.int32),
        ),
        in_specs=[anywhere] * 3,
        out_specs=(anywhere,) + vmem_specs(2),
        scratch_shapes=[
            pltpu.VMEM((rows, width), jnp.bfloat16),
            pltpu.VMEM(lab_shape, jnp.int32),
            pltpu.VMEM((1, n_fine), jnp.int32),
            pltpu.VMEM((rows, width), jnp.bfloat16),
            pltpu.VMEM((lay.n_main, width), jnp.bfloat16),
            pltpu.SemaphoreType.DMA((3 + lay.n_owner // 2,)),
        ],
        compiler_params=pltpu.CompilerParams(vmem_limit_bytes=FAST_LIMIT),
    )(embeddings, labels.reshape(lab_shape), owner_map.reshape(1, n_fine))


def gate_kernel(*refs):
    pass


def after(rows, *there):
    return pl.pallas_call(
        gate_kernel,
        out_shape=jax.ShapeDtypeStruct(rows.shape, rows.dtype),
        in_specs=list(vmem_specs(1 + len(there))),
        out_specs=vmem_specs(1)[0],
        input_output_aliases={0: 0},
        compiler_params=pltpu.CompilerParams(vmem_limit_bytes=FAST_LIMIT),
    )(rows, *there)


def lay_out_kernel(n_arrays, home, *refs):
    chunks, out = refs[:n_arrays], refs[-1]

    def copy():
        start = 0
        for chunk in chunks:
            out[start : start + chunk.shape[0], :] = chunk[...]
            start += chunk.shape[0]

    if home is None:
        copy()
    else:
        pl.when(lax.axis_index("cl") == home)(copy)


def lay_out(chunks, home=None, waits=()):
    rows, width = sum(x.shape[0] for x in chunks), chunks[0].shape[1]
    return pl.pallas_call(
        functools.partial(lay_out_kernel, len(chunks), home),
        out_shape=jax.ShapeDtypeStruct((rows, width), jnp.bfloat16),
        in_specs=list(vmem_specs(len(chunks) + len(waits))),
        out_specs=vmem_specs(1)[0],
        compiler_params=pltpu.CompilerParams(vmem_limit_bytes=FAST_LIMIT),
    )(*chunks, *waits)


class Layout:
    early, late = (0, 1, 2, 3), (5, 7, 4, 6)

    def __init__(self, n_owner, n_fine, capacity, main, home):
        self.n_owner, self.n_fine, self.capacity = n_owner, n_fine, capacity
        self.main, self.home = main, home
        self.head = main - INFO
        self.rest = capacity - self.head
        self.per_owner = n_fine // n_owner
        self.n_main = n_owner * main
        self.n_head = n_owner * self.head
        self.n_early = len(self.early) * self.rest
        self.n_late = len(self.late) * self.rest
        self.n_first = self.n_head + self.n_early
        self.n_all = self.n_first + self.n_late


def info_line(lay, main_ref, source):
    end = (source + 1) * lay.main
    return main_ref[end - INFO : end, :LANES].astype(jnp.float32)[INFO - 1 :]


def lines_of(lay, main_ref):
    return [info_line(lay, main_ref, source) for source in range(lay.n_owner)]


def hot_of(lay, info):
    lane = lax.broadcasted_iota(jnp.int32, (1, LANES), 1)
    hot = jnp.max(jnp.where(lane == lay.n_fine, info, 0.0), axis=1, keepdims=True)
    return hot.astype(jnp.int32)


def write_labels(lay, infos, sources, first, count, at, lab_sub, bias):
    cluster = swapped(lax.axis_index("cl"), hot_of(lay, infos[0]), lay.home)
    lane = lax.broadcasted_iota(jnp.int32, (1, LANES), 1)
    is_edge = lax.div(lane, lay.per_owner) == cluster
    for i, source in enumerate(sources):
        edges = jnp.where(is_edge, infos[source], 2.0 * lay.capacity)
        slot = lax.broadcasted_iota(jnp.int32, (count, LANES), 0) + first
        label = jnp.where(slot.astype(jnp.float32) >= edges, 1.0, 0.0)
        label = jnp.broadcast_to(jnp.sum(label, axis=1, keepdims=True), (count, LANES))
        start = at + i * count
        lab_sub[start : start + count, :] = label
        if bias is not None:
            bias[start : start + count, :] = jnp.where(
                label < lay.per_owner, NEIGHBOUR - SCALE, DEAD
            )


def first_labels(lay, infos, lab_sub):
    write_labels(lay, infos, range(lay.n_owner), 0, lay.head, 0, lab_sub, None)
    write_labels(lay, infos, lay.early, lay.head, lay.rest, lay.n_head, lab_sub, None)


def late_labels(lay, infos, lab_sub):
    write_labels(lay, infos, lay.late, lay.head, lay.rest, 0, lab_sub, None)


def turn_labels(lay, lab_sub, count, lab_lane, at):
    for i in range(0, count, LANES):
        block = jnp.transpose(lab_sub[i : i + LANES, :])[:1]
        lab_lane[:, at + i : at + i + LANES] = jnp.where(block < lay.per_owner, block, -1.0)


def copy_head(lay, main_ref, rows):
    for source in range(lay.n_owner):
        rows[source * lay.head : (source + 1) * lay.head, :] = main_ref[
            source * lay.main : source * lay.main + lay.head, :
        ]


def pieces(count, parts):
    return [(i * (count // parts), count // parts) for i in range(parts)]


def stream(lanes, tiles, lab_lane, buffers, put):
    rows_i, count, at = lanes
    step = 16
    tiles = [
        (ref, s, d, lab_sub, bias, line + s, back)
        for ref, n, lab_sub, bias, line, parts, back in tiles
        for s, d in pieces(n, parts)
    ]

    def scores_to(buffer, tile, rows):
        ref, start, deep = tile[:3]
        buffer[:deep, : rows.shape[0]] = lax.dot_general(
            ref[start : start + deep, :],
            rows,
            (((1,), (1,)), ((), ())),
            preferred_element_type=jnp.float32,
        )

    def run(start, blocks, wide):
        repeat = wide // LANES

        def rows_of(block):
            return rows_i[pl.ds(pl.multiple_of(start + block * wide, LANES), wide), :]

        scores_to(buffers[0], tiles[0], rows_of(0))

        def one_block(block):
            here = rows_of(block)
            place = pl.ds(pl.multiple_of(at + start + block * wide, LANES), wide)
            label_i = lab_lane[:, place]
            acc = jnp.zeros((8, wide), jnp.float32)
            for i, (_, _, deep, lab_sub, bias, line, back) in enumerate(tiles):
                if i + 1 < len(tiles):
                    scores_to(buffers[(i + 1) % 2], tiles[i + 1], here)
                elif blocks > 1:

                    @pl.when(block + 1 < blocks)
                    def _():
                        scores_to(buffers[0], tiles[0], rows_of(block + 1))

                buffer = buffers[i % 2]
                for c in range(0, deep, step):
                    part = slice(line + c, line + c + step)
                    label_j = jnp.concatenate([lab_sub[part, :]] * repeat, axis=1)
                    if bias is None:
                        bias_j = NEIGHBOUR - SCALE
                    else:
                        bias_j = jnp.concatenate([bias[part, :]] * repeat, axis=1)
                    shift = jnp.where(label_j == label_i, -SCALE, bias_j)
                    terms = jnp.exp2(buffer[c : c + step, :wide] * SCALE + shift)
                    acc = acc + jnp.sum(terms.reshape(step // 8, 8, wide), axis=0)
                    if back is not None:
                        across = terms[:, :LANES]
                        for r in range(1, repeat):
                            across = across + terms[:, r * LANES : (r + 1) * LANES]
                        back[part, :] += across
            put(place, jnp.sum(acc, axis=0, keepdims=True))

        if blocks == 1:
            one_block(0)
        else:
            pl.loop(0, blocks)(one_block)

    if count >= WIDE:
        run(0, count // WIDE, WIDE)
    if count % WIDE:
        run(count - count % WIDE, 1, count % WIDE)


def turn_sums(back, count, sums, at):
    for i in range(0, count, LANES):
        block = jnp.transpose(back[i : i + LANES, :])
        sums[:, at + i : at + i + LANES] += jnp.sum(block, axis=0, keepdims=True)


def setter(ref):
    def put(place, values):
        ref[:, place] = values

    return put


def adder(ref):
    def put(place, values):
        ref[:, place] += values

    return put


def inner_kernel(lay, mine, early, sums, lab_lane, lab_sub, rows, bias, back, buf_a, buf_b):
    is_home = lax.axis_index("cl") == lay.home
    infos = lines_of(lay, mine)
    buffers = (buf_a, buf_b)

    @pl.when(is_home)
    def _():
        copy_head(lay, mine, rows)
        first_labels(lay, infos, lab_sub)
        turn_labels(lay, lab_sub, lay.n_first, lab_lane, 0)
        back[...] = jnp.zeros(back.shape, jnp.float32)
        size = lay.n_early
        blocks = [(rows.at[pl.ds(start, size)], start) for start in range(0, lay.n_head, size)]
        blocks.append((early, lay.n_head))
        for i, (ref, at) in enumerate(blocks):
            tiles = [
                (ref_j, size, lab_sub, None, at_j, 2, None if at_j == at else back)
                for ref_j, at_j in blocks[i:]
            ]
            stream((ref, size, at), tiles, lab_lane, buffers, setter(sums))
        turn_sums(back, lay.n_first, sums, 0)

    @pl.when(jnp.logical_not(is_home))
    def _():
        write_labels(lay, infos, range(lay.n_owner), 0, lay.main, 0, lab_sub, bias)
        turn_labels(lay, lab_sub, lay.n_main, lab_lane, 0)
        tiles = [(mine, lay.n_main, lab_sub, bias, 0, 2, None)]
        stream((mine, lay.n_main, 0), tiles, lab_lane, buffers, setter(sums))


def half_blocks(ref_i, ref_j, lab_sub, line, back, at, lab_lane, buffers, put):
    half = ref_j.shape[0] // 2
    grp = lax.axis_index("grp")
    for h in range(2):
        start = pl.multiple_of((h ^ grp) * half, half)
        rows_j = ref_j.at[pl.ds(start, half)]
        sub = lab_sub.at[pl.ds(line + start, half)]
        backs = back.at[pl.ds(line + start, half)]
        lanes = (ref_i.at[pl.ds(h * half, half)], half, at + h * half)
        stream(lanes, [(rows_j, half, sub, None, 0, 1, backs)], lab_lane, buffers, put)


def cross_kernel(lay, mine, other, early, early_j, rows, sums, lab_lane, *refs):
    total, for_other, unfit_ref, late_sub, late_sub_j, long_lane, late_lane_j = refs[:7]
    lab_sub, bias, back, rows_j, buf_a, buf_b = refs[7:]
    is_home = lax.axis_index("cl") == lay.home
    infos = lines_of(lay, other)
    own = lines_of(lay, mine)
    hot = hot_of(lay, own[0])
    lane = lax.broadcasted_iota(jnp.int32, (1, LANES), 1)
    last = (lane < lay.n_fine) & (lax.rem(lane, lay.per_owner) == lay.per_owner - 1)
    last = last & (lax.div(lane, lay.per_owner) != hot)
    unfit = jnp.zeros((1, LANES), jnp.float32)
    for info in infos + own:
        wrong = last & (info >= lay.main)
        differs = (info != hot.astype(jnp.float32)) | (info >= lay.n_owner)
        wrong = wrong | ((lane == lay.n_fine) & differs)
        unfit = unfit + jnp.where(wrong, 1.0, 0.0)
    unfit_ref[0, 0] = jnp.max(unfit).astype(jnp.int32)
    total[...] = sums[...]
    buffers = (buf_a, buf_b)

    @pl.when(is_home)
    def _():
        copy_head(lay, other, rows_j)
        first_labels(lay, infos, lab_sub)
        back[...] = jnp.zeros(back.shape, jnp.float32)
        size = lay.n_early
        blocks_i = [rows.at[pl.ds(start, size)] for start in range(0, lay.n_head, size)] + [early]
        blocks_j = [rows_j.at[pl.ds(start, size)] for start in range(0, lay.n_head, size)]
        blocks_j.append(early_j)
        put, n = adder(total), len(blocks_i)
        for i, ref in enumerate(blocks_i):
            tiles = [
                (blocks_j[j], size, lab_sub, None, j * size, 2, back)
                for j in ((i + step) % n for step in range(1, (n + 1) // 2))
            ]
            stream((ref, size, i * size), tiles, lab_lane, buffers, put)
            half_blocks(
                ref, blocks_j[i], lab_sub, i * size, back, i * size, lab_lane, buffers, put
            )
        write_labels(lay, own, lay.late, lay.head, lay.rest, 0, late_sub, None)
        write_labels(lay, infos, lay.late, lay.head, lay.rest, 0, late_sub_j, None)
        long_lane[:, : lay.n_first] = lab_lane[...]
        turn_labels(lay, late_sub, lay.n_late, long_lane, lay.n_first)
        turn_labels(lay, late_sub_j, lay.n_late, late_lane_j, 0)
        for_other[...] = jnp.zeros(for_other.shape, jnp.float32)
        turn_sums(back, lay.n_first, for_other, 0)

    @pl.when(jnp.logical_not(is_home))
    def _():
        write_labels(lay, infos, range(lay.n_owner), 0, lay.main, 0, lab_sub, bias)
        tiles = [(other, lay.n_main, lab_sub, bias, 0, 2, None)]
        stream((mine, lay.n_main, 0), tiles, lab_lane, buffers, adder(total))


def first_tiles(lay, rows, early, lab_sub, back):
    return [
        (rows, lay.n_head, lab_sub, None, 0, 4, back),
        (early, lay.n_early, lab_sub, None, lay.n_head, 2, back),
    ]


def inner_late_kernel(lay, early, late, rows, lab_sub, late_sub, lab_lane, sums, *refs):
    back, buf_a, buf_b = refs

    @pl.when(lax.axis_index("cl") == lay.home)
    def _():
        back[...] = jnp.zeros(back.shape, jnp.float32)
        sums[:, : lay.n_first] = jnp.zeros((1, lay.n_first), jnp.float32)
        tiles = first_tiles(lay, rows, early, lab_sub, back)
        tiles.append((late, lay.n_late, late_sub, None, 0, 2, None))
        lanes = (late, lay.n_late, lay.n_first)
        stream(lanes, tiles, lab_lane, (buf_a, buf_b), setter(sums))
        turn_sums(back, lay.n_first, sums, 0)


def cross_late_kernel(lay, early, late, late_j, rows, lab_sub, late_sub, lab_lane, *refs):
    late_lane, first_lane, first_sums, first_other, sums, out_ref = refs[:6]
    total, late_other, back, late_back, buf_a, buf_b = refs[6:]
    is_home = lax.axis_index("cl") == lay.home
    grp = lax.axis_index("grp")

    @pl.when(is_home)
    def _():
        total[...] = sums[...]
        total[:, : lay.n_first] += first_sums[...]
        back[...] = jnp.zeros(back.shape, jnp.float32)
        late_back[...] = jnp.zeros(late_back.shape, jnp.float32)
        buffers = (buf_a, buf_b)
        tiles = first_tiles(lay, rows, early, lab_sub, back)
        stream((late_j, lay.n_late, 0), tiles, late_lane, buffers, setter(late_other))
        turn_sums(back, lay.n_first, total, 0)
        put = adder(total)
        half_blocks(late, late_j, late_sub, 0, late_back, lay.n_first, lab_lane, buffers, put)
        turn_sums(late_back, lay.n_late, late_other, 0)

        def write(line, values):
            for source in range(lay.n_owner):
                start = source * lay.head
                out_ref[2 * source + line, :, : lay.head] = values[:, start : start + lay.head]
            for i, source in enumerate(lay.early + lay.late):
                start = lay.n_head + i * lay.rest
                out_ref[2 * source + line, :, lay.head :] = values[:, start : start + lay.rest]

        write(grp, total[...])
        total[:, : lay.n_first] = first_other[...]
        total[:, lay.n_first :] = late_other[...]
        write(1 - grp, total[...])

    @pl.when(jnp.logical_not(is_home))
    def _():
        out_ref[...] = jnp.zeros(out_ref.shape, jnp.float32)
        values = jnp.where(first_lane[...] >= 0, first_sums[...], 1.0)
        for source in range(lay.n_owner):
            start = source * lay.main
            out_ref[2 * source + grp, :, : lay.main] = values[:, start : start + lay.main]


def pair_call(kernel, lay, arrays, out_shape, scratch, out_specs=None, pairs=0):
    width = arrays[0].shape[1]
    buffer = pltpu.VMEM((lay.n_main // 2, WIDE), jnp.float32)
    return pl.pallas_call(
        functools.partial(kernel, lay),
        out_shape=out_shape,
        in_specs=list(vmem_specs(len(arrays))),
        out_specs=out_specs or vmem_specs(len(out_shape)),
        scratch_shapes=list(scratch) + [buffer, buffer],
        compiler_params=pltpu.CompilerParams(vmem_limit_bytes=FAST_LIMIT),
        cost_estimate=pl.CostEstimate(
            flops=2 * pairs * width, bytes_accessed=1, transcendentals=pairs
        ),
    )(*arrays)


def fast_unpack_kernel(values_ref, pos_ref, out_ref):
    pos = pos_ref[...]
    lane = lax.rem(pos, LANES)
    line = lax.div(pos, LANES)
    out = jnp.ones(pos.shape, jnp.float32)
    per = values_ref.shape[2] // LANES
    for r in range(values_ref.shape[0] // 2 * per):
        owner, part = r // per, slice(r % per * LANES, (r % per + 1) * LANES)
        table = values_ref[2 * owner, :, part] + values_ref[2 * owner + 1, :, part]
        found = jnp.take_along_axis(jnp.broadcast_to(table, pos.shape), lane, axis=1)
        out = jnp.where(line == r, found, out)
    out_ref[...] = jnp.log(out)


def fast_unpack(values, pos):
    vmem = pl.BlockSpec(memory_space=pltpu.VMEM)
    return pl.pallas_call(
        fast_unpack_kernel,
        out_shape=jax.ShapeDtypeStruct(pos.shape, jnp.float32),
        in_specs=[vmem, vmem],
        out_specs=vmem,
    )(values, pos)


def general(embeddings, labels, owner_map):
    n_owner = lax.axis_size("cl")
    capacity = SLOTS // n_owner
    rows, width = embeddings.shape
    packed, pos, counts = pack(embeddings, labels, owner_map, n_owner, capacity)
    counts = lax.all_gather(counts, ("cl", "grp"), tiled=True)
    mine = lax.all_to_all(
        packed.reshape(n_owner, capacity, width), "cl", split_axis=0, concat_axis=0, tiled=True
    ).reshape(SLOTS, width)
    other = lax.ppermute(mine, "grp", [(0, 1), (1, 0)])
    results = log_counts(counts, mine, other, n_owner, capacity)
    returned = lax.all_to_all(
        results.reshape(n_owner, capacity), "cl", split_axis=0, concat_axis=0, tiled=True
    )
    return unpack(returned.reshape(SLOTS), pos).reshape(rows)


def body(embeddings, labels, owner_map):
    n_owner = lax.axis_size("cl")
    capacity = SLOTS // n_owner
    rows, width = embeddings.shape
    n_fine = owner_map.shape[0]
    main = -(-(rows // n_owner * 9 // 8) // 16) * 16
    if n_owner != 8 or main >= capacity or n_fine >= LANES:
        return general(embeddings, labels, owner_map)
    home = 2
    lay = Layout(n_owner, n_fine, capacity, main, home)
    packed, extra, pos = place_rows(embeddings, labels, owner_map, lay)

    def hop(x, pairs):
        return lax.ppermute(x, "cl", pairs)

    def swap(x):
        return lax.ppermute(x, "grp", [(0, 1), (1, 0)])

    both = lay_out([extra, hop(extra, [(6, 4), (7, 5)])])
    early = [extra if s == home else hop(extra, [(s, home)]) for s in lay.early]
    early = lay_out(early, home)
    mine = lax.all_to_all(
        packed.reshape(n_owner, main, width), "cl", split_axis=0, concat_axis=0, tiled=True
    ).reshape(n_owner * main, width)
    mine = after(mine, early, both)
    other, early_j = swap(mine), swap(early)
    late = [hop(both, [(s, home)]) for s in (5, 4)]

    def array(shape, dtype=jnp.float32):
        return jax.ShapeDtypeStruct(shape, dtype)

    def scratch(shape):
        return pltpu.VMEM(shape, jnp.float32)

    row, long_row = array((1, lay.n_first)), array((1, lay.n_all))
    bias = scratch((lay.n_main, LANES))
    heads = array((lay.n_head, width), jnp.bfloat16)
    late_lines, first_lines = array((lay.n_late, LANES)), array((lay.n_first, LANES))
    late_row = array((1, lay.n_late))
    late_side, first_side = scratch((lay.n_late, LANES)), scratch((lay.n_first, LANES))
    sums, first_lane, lab_sub, heads_i = pair_call(
        inner_kernel, lay, (mine, early), (row, row, first_lines, heads), (bias, first_side)
    )
    specs = vmem_specs(2) + (pl.BlockSpec(memory_space=pltpu.SMEM),) + vmem_specs(4)
    sums, first_other, unfit, late_sub, late_sub_j, lane, lane_j = pair_call(
        cross_kernel,
        lay,
        (mine, other, early, early_j, heads_i, sums, first_lane),
        (row, row, array((1, 1), jnp.int32), late_lines, late_lines, long_row, late_row),
        (first_side, bias, first_side, pltpu.VMEM(heads.shape, heads.dtype)),
        specs,
    )
    late = lay_out(late, home, (sums,))
    late_j = swap(late)
    (late_sums,) = pair_call(
        inner_late_kernel,
        lay,
        (early, late, heads_i, lab_sub, late_sub, lane),
        (long_row,),
        (first_side,),
        pairs=lay.n_late * lay.n_all,
    )
    (results,) = pair_call(
        cross_late_kernel,
        lay,
        (
            *(early, late, late_j, heads_i, lab_sub, late_sub_j, lane, lane_j),
            *(first_lane, sums, first_other, late_sums),
        ),
        (array((2 * n_owner, 1, capacity)),),
        (scratch(long_row.shape), scratch(late_row.shape), first_side, late_side),
    )
    returned = lax.all_to_all(
        results, ("cl", "grp"), split_axis=0, concat_axis=0, tiled=True
    )
    result = fast_unpack(returned, pos).reshape(rows)
    return lax.cond(
        unfit[0, 0] == 0,
        lambda: result,
        lambda: general(embeddings, labels, owner_map),
    )


def solution(mesh):
    return jax.shard_map(
        body,
        mesh=mesh,
        in_specs=(P(("parts", "cl", "grp"), None), P(("parts", "cl", "grp")), P("parts")),
        out_specs=P(("parts", "cl", "grp")),
        check_vma=False,
    )
```
